32 devices in a mesh: ctx: 8 (over z, x), wt: 4 (over y, core).
Axes of the slice: x: 2, y: 2, z: 4, core: 2. Of those that a mesh axis runs over, the one named last changes fastest.
Arguments:
- tokens: bfloat16 [4, 1024, 768], P('wt', 'ctx'), may hold values from -6 to 6
- cotangent: bfloat16 [4, 1024, 768], P('wt', 'ctx'), may hold values from -6 to 6
- gain_attention: bfloat16 [768], P('wt'), may hold values from 0.5 to 1.5
- query_weight: bfloat16 [768, 768], P('wt'), may hold values from -0.21875 to 0.21875
- key_weight: bfloat16 [768, 768], P('wt'), may hold values from -0.21875 to 0.21875
- value_weight: bfloat16 [768, 768], P('wt'), may hold values from -0.21875 to 0.21875
- output_weight: bfloat16 [768, 768], P('wt'), may hold values from -0.875 to 0.875
- gain_mixer: bfloat16 [768], P('wt'), may hold values from 0.5 to 1.5
- router_weight: bfloat16 [768, 8], P('wt'), may hold values from -0.21875 to 0.21875
- shared_gate: bfloat16 [768, 2048], P('wt'), may hold values from -0.21875 to 0.21875
- shared_up: bfloat16 [768, 2048], P('wt'), may hold values from -0.21875 to 0.21875
- shared_down: bfloat16 [2048, 768], P('wt'), may hold values from -0.1875 to 0.1875
- expert_gate: bfloat16 [768, 16384], P('wt', 'ctx'), may hold values from -0.21875 to 0.21875
- expert_up: bfloat16 [768, 16384], P('wt', 'ctx'), may hold values from -0.21875 to 0.21875
- expert_down: bfloat16 [768, 16384], P('wt', 'ctx'), may hold values from -0.25 to 0.25
- routes: int32 [4, 1024, 2], P('wt', 'ctx'), may hold values from 0 to 7, all different within a row
- slot_order: int32 [4, 8, 256], P('wt', 'ctx'), may hold values from 0 to 255, each once within a row
- block_deal: int32 [8], replicated, may hold values from 0 to 7, each once
Outputs:
- output: bfloat16 [4, 1024, 768], P('wt', 'ctx')
- input_gradient: float32 [4, 1024, 768], P('wt', 'ctx')
- gain_attention_gradient: float32 [768], P('wt')
- query_gradient: float32 [768, 768], P('wt')
- key_gradient: float32 [768, 768], P('wt')
- value_gradient: float32 [768, 768], P('wt')
- output_weight_gradient: float32 [768, 768], P('wt')
- gain_mixer_gradient: float32 [768], P('wt')
- router_gradient: float32 [768, 8], P('wt')
- shared_gate_gradient: float32 [768, 2048], P('wt')
- shared_up_gradient: float32 [768, 2048], P('wt')
- shared_down_gradient: float32 [2048, 768], P('wt')
- expert_gate_gradient: float32 [768, 16384], P('wt', 'ctx')
- expert_up_gradient: float32 [768, 16384], P('wt', 'ctx')
- expert_down_gradient: float32 [768, 16384], P('wt', 'ctx')
The draws below stay inside these ranges and needn't reach their ends.
Inputs may be any that keep to these rules, and one draw needn't show every extreme that they name: `routes`: each token names 2 different experts. `slot_order`: each row lists every pair index of a device once. `block_deal`: each rank's number appears once.
All inputs are finite; a program needn't handle non-finite values.
Results may differ from the reference program's by a relative error of at most 0.02.
Values may be sent and summed in bfloat16 or wider, within the bound.
A program may use at most 320 MiB of HBM per device.

```python
import jax
import jax.numpy as jnp
from jax import lax

D = 768
HEADS = 12
HD = 64
H = 2048
FS = 2048
TOP = 2
BLK = 256
UNIT = 64
TOK_DEV = 128
SEQ_LEN = 1024
SEQS = 4
EXPERTS = 8
PAIRS = 256
CAP = 40
N_CTX = 8


def shard_levels(key, dims, shards, smallest, high):
    loudness = 1.0
    for position, blocks in shards:
        steps = jax.random.uniform(jax.random.fold_in(jax.random.fold_in(key, 6), position), (blocks,), jnp.float32, smallest / len(shards), high / len(shards))
        loudness = loudness * jnp.repeat(jnp.exp(steps), dims[position] // blocks).reshape((-1,) + (1,) * (len(dims) - 1 - position))
    return loudness


def picks_of(stream_key, rows, number_of, top, lift):
    sequence = jax.random.permutation(jax.random.fold_in(stream_key, 1), number_of)
    pull = sequence
    for power in range(3):
        pull = pull * pull // number_of
    pull = pull * lift // number_of
    lots = jax.random.randint(jax.random.fold_in(stream_key, 2), (rows, number_of), 0, 4096) + pull
    fixed_rows = jax.random.permutation(jax.random.fold_in(stream_key, 3), rows)[jnp.arange(number_of) % rows]
    lots = jnp.where(jnp.arange(rows)[:, None] == fixed_rows[None, :], 1 << 14, lots)
    priority = lots * number_of + jnp.arange(number_of)
    return lax.top_k(priority.astype(jnp.int32), top)[1].astype(jnp.int32)


def gaussian(rng, dims, scale, bound, cuts=(), held_as=jnp.bfloat16):
    entries = jax.random.normal(rng, dims, jnp.float32) * scale
    if len(cuts) > 0:
        entries = shard_levels(rng, dims, cuts, -0.22, 0.18) * entries
    return jnp.clip(entries, min=-bound, max=bound).astype(held_as)


def setup_inputs(seed: int = 0) -> dict:
    key_list = jax.random.split(jax.random.key(seed), 19)
    return {
        "tokens": gaussian(key_list[0], (SEQS, SEQ_LEN, D), 1.0, 6.0, ((0, 4), (1, 8))),
        "cotangent": gaussian(key_list[1], (SEQS, SEQ_LEN, D), 1.0, 6.0, ((0, 4), (1, 8))),
        "gain_attention": jnp.clip(1.0 + 0.1 * jax.random.normal(key_list[2], (D,), jnp.float32), 0.5, 1.5).astype(jnp.bfloat16),
        "query_weight": gaussian(key_list[3], (D, D), D ** -0.5, 0.21875, ((0, 4),)),
        "key_weight": gaussian(key_list[4], (D, D), D ** -0.5, 0.21875, ((0, 4),)),
        "value_weight": gaussian(key_list[5], (D, D), D ** -0.5, 0.21875, ((0, 4),)),
        "output_weight": gaussian(key_list[6], (D, D), (D // 16) ** -0.5, 0.875, ((0, 4),)),
        "gain_mixer": jnp.clip(1.0 + 0.1 * jax.random.normal(key_list[7], (D,), jnp.float32), 0.5, 1.5).astype(jnp.bfloat16),
        "router_weight": gaussian(key_list[8], (D, EXPERTS), D ** -0.5, 0.21875, ((0, 4),)),
        "shared_gate": gaussian(key_list[9], (D, FS), D ** -0.5, 0.21875, ((0, 4),)),
        "shared_up": gaussian(key_list[10], (D, FS), D ** -0.5, 0.21875, ((0, 4),)),
        "shared_down": gaussian(key_list[11], (FS, D), (FS // 2) ** -0.5, 0.1875, ((0, 4),)),
        "expert_gate": gaussian(key_list[12], (D, EXPERTS * H), D ** -0.5, 0.21875, ((0, 4), (1, 8))),
        "expert_up": gaussian(key_list[13], (D, EXPERTS * H), D ** -0.5, 0.21875, ((0, 4), (1, 8))),
        "expert_down": gaussian(key_list[14], (D, EXPERTS * H), (H // 4) ** -0.5, 0.25, ((0, 4), (1, 8))),
        "routes": picks_of(key_list[15], SEQS * SEQ_LEN, EXPERTS, TOP, 2048).reshape((SEQS, SEQ_LEN, TOP)),
        "slot_order": jax.vmap(lambda own: jax.random.permutation(own, PAIRS))(jax.random.split(key_list[16], SEQS * N_CTX)).reshape((SEQS, N_CTX, PAIRS)).astype(jnp.int32),
        "block_deal": jax.random.permutation(key_list[17], N_CTX).astype(jnp.int32),
    }


EPS = 1e-06
HIGH = lax.Precision.HIGHEST

@jax.custom_vjp
def low(v):
    return lax.optimization_barrier(v.astype(jnp.bfloat16)).astype(jnp.float32)

@jax.custom_vjp
def low_back(v):
    return v

def low_keep(v):
    return (low(v), None)

def low_pass(kept, grad):
    return (grad,)

def back_keep(v):
    return (v, None)

def back_low(kept, grad):
    return (low(grad),)
low.defvjp(low_keep, low_pass)
low_back.defvjp(back_keep, back_low)

def product(left, right):
    return jnp.dot(left, right, precision=HIGH, preferred_element_type=jnp.float32)

def rms_norm(values, gain):
    return values * lax.rsqrt(lax.optimization_barrier(jnp.mean(values * values, axis=-1, keepdims=True)) + EPS) * gain

def positions(block_deal):
    row_index = jnp.arange(SEQ_LEN, dtype=jnp.int32)
    owner_rank = row_index // TOK_DEV
    inner_row = row_index % TOK_DEV
    paired = block_deal[owner_rank]
    unit_index = jnp.where(inner_row < UNIT, paired, 2 * N_CTX - 1 - paired)
    return unit_index * UNIT + inner_row % UNIT

def rotate(values, place):
    half_size = HD // 2
    frequency = 10000.0 ** (-jnp.arange(half_size, dtype=jnp.float32) / half_size)
    angles = place.astype(jnp.float32)[:, None] * frequency[None, :]
    cosine = jnp.cos(angles)[:, None, :]
    sine_part = jnp.sin(angles)[:, None, :]
    shaped = values.reshape(values.shape[0], HEADS, 2, half_size)
    first_half = shaped[:, :, 0, :]
    second_half = shaped[:, :, 1, :]
    turned = jnp.stack([first_half * cosine - second_half * sine_part, second_half * cosine + first_half * sine_part], axis=2)
    return turned.reshape(values.shape)

def attention(query_rot, key_rot, value_rot, place):
    block_rows = min(512, SEQ_LEN)
    scale_factor = HD ** (-0.5)
    key_heads = key_rot.reshape(SEQ_LEN, HEADS, HD)
    value_heads = value_rot.reshape(SEQ_LEN, HEADS, HD)
    key_block = place // BLK

    def one_block(inputs):
        query_rows, query_place = inputs
        scores = jnp.einsum('qhd,khd->hqk', query_rows.reshape(block_rows, HEADS, HD), key_heads, precision=HIGH)
        scores = low_back(scores) * scale_factor
        allowed = key_block[None, None, :] <= (query_place // BLK)[None, :, None]
        scores = jnp.where(allowed, scores, -1e+30)
        largest = lax.optimization_barrier(jnp.max(scores, axis=2, keepdims=True))
        raised = jnp.where(allowed, jnp.exp(scores - largest), 0.0)
        attention_weights = low(raised / lax.optimization_barrier(jnp.sum(raised, axis=2, keepdims=True)))
        mixed = jnp.einsum('hqk,khd->qhd', attention_weights, value_heads, precision=HIGH)
        return mixed.reshape(block_rows, HEADS * HD)
    blocks = (query_rot.reshape(SEQ_LEN // block_rows, block_rows, HEADS * HD), place.reshape(SEQ_LEN // block_rows, block_rows))
    return lax.map(jax.checkpoint(one_block), blocks).reshape(SEQ_LEN, HEADS * HD)

def assign_slots(route, order):
    expert_ids = route.reshape(PAIRS)
    ordered = expert_ids[order]
    onehot = (ordered[:, None] == jnp.arange(EXPERTS, dtype=jnp.int32)[None, :]).astype(jnp.int32)
    before = jnp.cumsum(onehot, axis=0) - onehot
    slot_turn = lax.optimization_barrier(jnp.sum(before * onehot, axis=1))
    slot_index = jnp.zeros((PAIRS,), jnp.int32).at[order].set(slot_turn)
    kept_pairs = slot_index < CAP
    target = jnp.where(kept_pairs, expert_ids * CAP + slot_index, EXPERTS * CAP)
    slot_table = jnp.full((EXPERTS * CAP,), PAIRS, jnp.int32).at[target].set(jnp.arange(PAIRS, dtype=jnp.int32), mode='drop')
    return (target, kept_pairs, slot_table)

def pick_rows(rows_here, picked):
    return rows_here[picked]

def apply_expert(inputs):
    rows_in, gate_weight, up_weight, down_weight = inputs
    gate_part = low_back(product(rows_in, gate_weight))
    up_projection_part = low_back(product(rows_in, up_weight))
    hidden = low(jax.nn.silu(gate_part) * up_projection_part)
    return low_back(jnp.dot(hidden, down_weight.T, precision=HIGH, preferred_element_type=jnp.float32))

def layer(params, inputs, route, order, place):
    gain_one, query_weight, key_weight, value_weight, output_weight, gain_two, router_weight, shared_gate, shared_up, shared_down, expert_gate, expert_up, expert_down = params
    normed = low(rms_norm(inputs, gain_one))
    query_rot = low(rotate(low_back(product(normed, query_weight)), place))
    key_rot = low(rotate(low_back(product(normed, key_weight)), place))
    value_rot = low(low_back(product(normed, value_weight)))
    mixed = low(low_back(attention(query_rot, key_rot, value_rot, place)))
    second = inputs + low_back(product(mixed, output_weight))
    mixer = low(rms_norm(second, gain_two))
    logits = product(mixer, router_weight)
    target, kept_pairs, slot_table = jax.vmap(assign_slots)(route.reshape(N_CTX, TOK_DEV, TOP), order)
    per_rank = mixer.reshape(N_CTX, TOK_DEV, D)
    valid = slot_table < PAIRS
    source = jnp.minimum(slot_table, PAIRS - 1) // TOP
    dispatched = jnp.where(valid[:, :, None], jax.vmap(pick_rows)(per_rank, source), 0.0)
    by_expert = dispatched.reshape(N_CTX, EXPERTS, CAP, D).transpose(1, 0, 2, 3).reshape(EXPERTS, N_CTX * CAP, D)
    gate_stack = expert_gate.reshape(D, EXPERTS, H).transpose(1, 0, 2)
    up_stack = expert_up.reshape(D, EXPERTS, H).transpose(1, 0, 2)
    down_stack = expert_down.reshape(D, EXPERTS, H).transpose(1, 0, 2)
    expert_out = lax.map(jax.checkpoint(apply_expert), (by_expert, gate_stack, up_stack, down_stack))
    returned = expert_out.reshape(EXPERTS, N_CTX, CAP, D).transpose(1, 0, 2, 3).reshape(N_CTX, EXPERTS * CAP, D)
    pair_out = jax.vmap(pick_rows)(returned, jnp.minimum(target, EXPERTS * CAP - 1))
    pair_out = jnp.where(kept_pairs[:, :, None], pair_out, 0.0).reshape(SEQ_LEN, TOP, D)
    chosen = jnp.take_along_axis(logits, route, axis=1)
    gates = jax.nn.softmax(chosen, axis=1)
    mixture = lax.optimization_barrier(jnp.sum(gates[:, :, None] * pair_out, axis=1))
    shared_hidden = low(jax.nn.silu(low_back(product(mixer, shared_gate))) * low_back(product(mixer, shared_up)))
    shared_out = low_back(product(shared_hidden, shared_down))
    return second + mixture + shared_out

def reference(tokens, cotangent, gain_attention, query_weight, key_weight, value_weight, output_weight, gain_mixer, router_weight, shared_gate, shared_up, shared_down, expert_gate, expert_up, expert_down, routes, slot_order, block_deal):
    params = (gain_attention.astype(jnp.float32), query_weight.astype(jnp.float32), key_weight.astype(jnp.float32), value_weight.astype(jnp.float32), output_weight.astype(jnp.float32), gain_mixer.astype(jnp.float32), router_weight.astype(jnp.float32), shared_gate.astype(jnp.float32), shared_up.astype(jnp.float32), shared_down.astype(jnp.float32), expert_gate.astype(jnp.float32), expert_up.astype(jnp.float32), expert_down.astype(jnp.float32))
    place = positions(block_deal)
    inputs = tokens.astype(jnp.float32)

    def forward(weights_all, inputs_all):

        def one_sequence(items):
            return layer(weights_all, items[0], items[1], items[2], place)
        return lax.map(jax.checkpoint(one_sequence), (inputs_all, routes, slot_order))
    result, pullback = jax.vjp(forward, params, inputs)
    grads, input_grad = pullback(cotangent.astype(jnp.float32))
    return (result.astype(jnp.bfloat16), input_grad, grads[0], grads[1], grads[2], grads[3], grads[4], grads[5], grads[6], grads[7], grads[8], grads[9], grads[10], grads[11], grads[12])
```

```python
import jax
import jax.numpy as jnp
from jax import lax
from jax.experimental import pallas as pl
from jax.experimental.pallas import tpu as pltpu
from jax.sharding import PartitionSpec as P

HD = 64
BLK = 256


EPS = 1e-06
KEY_ROWS = 512
HIGH = lax.Precision.HIGHEST
MASKED = -1e30


MESH = pl.DeviceIdType.MESH
VMEM = pltpu.VMEM
BF = jnp.bfloat16
F32 = jnp.float32
PAIR = 2 * HD


class Spot:
    def __init__(self, line_size):
        self.k = lax.axis_index("ctx")
        self.w = lax.axis_index("wt")
        self.z, self.x = lax.div(self.k, 2), lax.rem(self.k, 2)
        self.y, self.c = lax.div(self.w, 2), lax.rem(self.w, 2)
        self.far = lax.div(self.z, 2)
        self.mid = self.z + self.far * (3 - 2 * self.z)
        step = 1 - 2 * self.far
        self.core = (self.k, 2 * self.y + 1 - self.c)
        self.across = (self.k, 2 * (1 - self.y) + self.c)
        self.corner = (self.k, 2 * (1 - self.y) + 1 - self.c)
        self.column = (2 * self.z + 1 - self.x, self.w)
        self.inner = (2 * (self.z + step) + self.x, self.w)
        self.outer = (2 * (self.z - step) + self.x, self.w)

    def plane(self, step):
        mirrored = (self.mid, 1 - self.mid, 2, 3)[step]
        return mirrored + self.far * (3 - 2 * mirrored)


class Sems:
    def __init__(self, ref):
        self.ref, self.used = ref, 0

    def new(self):
        self.used += 1
        return self.ref.at[self.used - 1]


def remote(src, dst, send, recv, to):
    return pltpu.make_async_remote_copy(
        src_ref=src, dst_ref=dst, send_sem=send, recv_sem=recv, device_id=to, device_id_type=MESH
    )


def greet(devices, middle=None):
    barrier = pltpu.get_barrier_semaphore()
    for to in devices:
        pl.semaphore_signal(barrier, inc=1, device_id=to, device_id_type=MESH)
    if middle is None:
        pl.semaphore_wait(barrier, len(devices))
        return

    @pl.when(middle[0] == 1)
    def _():
        pl.semaphore_signal(barrier, inc=1, device_id=middle[1], device_id_type=MESH)

    pl.semaphore_wait(barrier, len(devices) + middle[0])


class Gather:
    def __init__(self, spot, src, dst, sems):
        self.spot, self.dst, self.sems = spot, dst, sems
        self.rows = src.shape[0]
        here = self.block(spot.w)
        self.local = pltpu.make_async_copy(src, here, sems.new())
        self.to_core = remote(src, here, sems.new(), sems.new(), spot.core)
        self.to_across = remote(src, here, sems.new(), sems.new(), spot.across)
        for copy in (self.to_across, self.to_core, self.local):
            copy.start()

    def block(self, w):
        return self.dst.at[pl.ds(pl.multiple_of(self.rows * w, 64), self.rows)]

    def forward(self):
        self.to_across.wait_recv()
        part = self.block(self.spot.across[1])
        self.onward = remote(part, part, self.sems.new(), self.sems.new(), self.spot.core)
        self.onward.start()

    def finish(self):
        self.local.wait()
        self.to_core.wait_recv()
        self.onward.wait_recv()

    def drain(self):
        self.to_core.wait_send()
        self.to_across.wait_send()
        self.onward.wait_send()


class Spread:
    def __init__(self, spot, pick, place, sems, local=True):
        self.copies = []
        for to in (spot.across, spot.corner, spot.core):
            self.copies.append(remote(pick(to[1]), place(spot.w), sems.new(), sems.new(), to))
        self.local = None
        if local:
            self.local = pltpu.make_async_copy(pick(spot.w), place(spot.w), sems.new())
        for copy in self.copies:
            copy.start()
        if local:
            self.local.start()

    def finish(self):
        for copy in self.copies:
            copy.wait_recv()
        if self.local is not None:
            self.local.wait()

    def drain(self):
        for copy in self.copies:
            copy.wait_send()


def nt(left, right):
    return lax.dot_general(left, right, (((1,), (1,)), ((), ())), preferred_element_type=F32)


def nn(left, right):
    return jnp.dot(left, right, preferred_element_type=F32)


def tn(left, right):
    return lax.dot_general(left, right, (((0,), (0,)), ((), ())), preferred_element_type=F32)


def turn(values, cosine, sine):
    wide = values.shape[1]
    lane = lax.broadcasted_iota(jnp.int32, values.shape, 1)
    first = lax.rem(lane, HD) < HD // 2
    swapped = jnp.where(
        first, pltpu.roll(values, wide - HD // 2, 1), pltpu.roll(values, HD // 2, 1)
    )
    copies = wide // PAIR
    cosine = jnp.concatenate([cosine] * copies, axis=1)
    sine = jnp.concatenate([sine] * copies, axis=1)
    return values * cosine + swapped * sine


def stack_pair(values):
    lane = lax.broadcasted_iota(jnp.int32, values.shape, 1)
    none = jnp.zeros_like(values)
    return jnp.concatenate(
        [jnp.where(lane < HD, values, none), jnp.where(lane < HD, none, values)], axis=0
    )


def unstack_pair(values):
    rows = values.shape[0] // 2
    lane = lax.broadcasted_iota(jnp.int32, (rows, PAIR), 1)
    return jnp.where(lane < HD, values[:rows], values[rows:])


class Ring:
    def __init__(self, spot, blocks, recv, send):
        self.spot, self.blocks, self.recv, self.send = spot, blocks, recv, send
        self.used = 0
        self.sent, self.sent_mid = [], []

    def copy(self, slot, to):
        self.used += 1
        return remote(
            self.blocks.at[slot],
            self.blocks.at[slot],
            self.send.at[self.used - 1],
            self.recv.at[slot],
            to,
        )

    def arrived(self, slot):
        remote(
            self.blocks.at[slot],
            self.blocks.at[slot],
            self.send.at[0],
            self.recv.at[slot],
            self.spot.column,
        ).wait_recv()

    def start(self):
        spot = self.spot
        own = self.copy(spot.k, spot.inner)
        side = self.copy(spot.k, spot.column)
        back = self.copy(spot.k, spot.outer)
        own.start()

        @pl.when(spot.mid == 1)
        def _():
            back.start()

        side.start()
        self.sent += [own, side]
        self.sent_mid += [back]

    def step(self, number):
        spot = self.spot
        plane = spot.plane(number)
        if number > 0:
            slot = 2 * plane + spot.x
            self.arrived(slot)
            along = self.copy(slot, spot.inner if number == 1 else spot.outer)

            @pl.when(spot.mid == 1)
            def _():
                along.start()

            side = self.copy(slot, spot.column)
            side.start()
            self.sent += [side]
            self.sent_mid += [along]
        return plane

    def other(self, plane):
        self.arrived(2 * plane + 1 - self.spot.x)

    def drain(self):
        for copy in self.sent:
            copy.wait_send()

        @pl.when(self.spot.mid == 1)
        def _():
            for copy in self.sent_mid:
                copy.wait_send()


def forward_kernel(
    tok, pack, cosr, sinr, kb, qb, cot, wq, wk, wv, wo, sg, su, eg, eu,
    q_out, kv_out, mixed_out, lse_out, second_out, mixer_out, normed_out, pack_out,
    wfull_out, sg_out, su_out, eg_out, eu_out, cot_out,
    wbuf, kv, packs, top, low, acc, sem, kv_recv, kv_send,
):
    spot = Spot(4)
    sems = Sems(sem)
    rows = tok.shape[0]
    width = tok.shape[1]
    pairs = width // PAIR
    greet((spot.core, spot.across, spot.corner, spot.column, spot.inner), (spot.mid, spot.outer))
    params = Spread(spot, lambda w: pack, lambda w: packs.at[w], sems)
    key_w = Gather(spot, wk, wbuf.at[1], sems)
    value_w = Gather(spot, wv, wbuf.at[2], sems)
    query_w = Gather(spot, wq, wbuf.at[0], sems)
    inputs = tok[...].astype(F32)
    scale = lax.rsqrt(jnp.mean(inputs * inputs, axis=-1, keepdims=True) + EPS)
    scaled = inputs * scale
    params.finish()
    pack_all = packs[0] + packs[1] + packs[2] + packs[3]
    pack_out[...] = pack_all
    normed = (scaled * pack_all[0:1]).astype(BF)
    normed_out[...] = normed
    cosine, sine = cosr[...], sinr[...]
    key_w.forward()
    value_w.forward()
    key_w.finish()
    kv[spot.k, :, 0:width] = turn(nn(normed, wbuf[1]), cosine, sine).astype(BF)
    value_w.finish()
    kv[spot.k, :, width : 2 * width] = nn(normed, wbuf[2]).astype(BF)
    ring = Ring(spot, kv, kv_recv, kv_send)
    ring.start()
    query_w.forward()
    out_w = Gather(spot, wo, wbuf.at[3], sems)
    sg_w = Spread(
        spot,
        lambda w: sg.at[:, pl.ds(pl.multiple_of(512 * w, 512), 512)],
        lambda w: sg_out.at[pl.ds(pl.multiple_of(192 * w, 64), 192)],
        sems,
    )
    su_w = Spread(
        spot,
        lambda w: su.at[:, pl.ds(pl.multiple_of(512 * w, 512), 512)],
        lambda w: su_out.at[pl.ds(pl.multiple_of(192 * w, 64), 192)],
        sems,
    )
    cot_w = Spread(spot, lambda w: cot, lambda w: cot_out.at[w], sems)
    gate_w = Gather(spot, eg, eg_out, sems)
    up_w = Gather(spot, eu, eu_out, sems)
    query_w.finish()
    query = turn(nn(normed, wbuf[0]), cosine, sine).astype(BF) * jnp.asarray(HD**-0.5, BF)
    for j in range(pairs):
        q_out[j] = stack_pair(query[:, PAIR * j : PAIR * (j + 1)])
    top[...] = jnp.full_like(top, MASKED)
    low[...] = jnp.zeros_like(low)
    acc[...] = jnp.zeros_like(acc)
    q_block = qb[...]

    def chunk(plane):
        k_block = kb[:, pl.ds(pl.multiple_of(2 * rows * plane, 2 * rows), 2 * rows)]
        allowed = k_block <= q_block

        def one_pair(j, carry):
            lane = pl.multiple_of(PAIR * j, PAIR)
            key = kv[pl.ds(2 * plane, 2), :, pl.ds(lane, PAIR)].reshape(2 * rows, PAIR)
            value = kv[pl.ds(2 * plane, 2), :, pl.ds(width + lane, PAIR)].reshape(2 * rows, PAIR)
            scores = jnp.where(allowed, nt(q_out[j], key), MASKED)
            old = top[j]
            new = jnp.maximum(old, jnp.max(scores, axis=1, keepdims=True))
            raised = jnp.where(allowed, jnp.exp(scores - new[:, 0:1]), 0.0)
            factor = jnp.exp(old - new)
            top[j] = new
            low[j] = low[j] * factor + jnp.sum(raised, axis=1, keepdims=True)
            acc[j] = acc[j] * factor + nn(raised.astype(BF), value)
            return carry

        lax.fori_loop(0, pairs, one_pair, 0)

    for number in range(4):
        plane = ring.step(number)
        ring.other(plane)
        chunk(plane)
    saves = [pltpu.make_async_copy(kv, kv_out, sems.new())]
    saves[0].start()
    out_w.forward()
    for j in range(pairs):
        mixed_out[:, PAIR * j : PAIR * (j + 1)] = unstack_pair(acc[j] / low[j])
        lse_out[j] = top[j] + jnp.log(low[j])
    out_w.finish()
    saves.append(pltpu.make_async_copy(wbuf, wfull_out, sems.new()))
    saves[1].start()
    second = inputs + nn(mixed_out[...].astype(BF), wbuf[3])
    second_out[...] = second
    scale_two = lax.rsqrt(jnp.mean(second * second, axis=-1, keepdims=True) + EPS)
    mixer_out[...] = (second * scale_two * pack_all[1:2]).astype(BF)
    gate_w.forward()
    up_w.forward()
    for part in (sg_w, su_w, cot_w, gate_w, up_w):
        part.finish()
    for part in (params, key_w, value_w, query_w, out_w, sg_w, su_w, cot_w, gate_w, up_w, ring):
        part.drain()
    for copy in saves:
        copy.wait()


def run_forward(tok, pack, cosr, sinr, kb, qb, cot, wq, wk, wv, wo, sg, su, eg, eu):
    rows, width = tok.shape
    pairs = width // PAIR
    ranks = 8
    any_, vm = pl.BlockSpec(memory_space=pl.ANY), pl.BlockSpec(memory_space=VMEM)
    shape = jax.ShapeDtypeStruct
    hidden = eg.shape[1]
    part = sg.shape[1] // 4
    return pl.pallas_call(
        forward_kernel,
        out_shape=(
            shape((pairs, 2 * rows, PAIR), BF),
            shape((ranks, rows, 2 * width), BF),
            shape((rows, width), F32),
            shape((pairs, 2 * rows, PAIR), F32),
            shape((rows, width), F32),
            shape((rows, width), BF),
            shape((rows, width), BF),
            shape(pack.shape, F32),
            shape((4, width, width), BF),
            shape((width, part), BF),
            shape((width, part), BF),
            shape((width, hidden), BF),
            shape((width, hidden), BF),
            shape((4, rows, width), BF),
        ),
        in_specs=[vm] * 6 + [any_] * 9,
        out_specs=(vm, any_, vm, vm, vm, vm, vm, vm, any_, any_, any_, any_, any_, any_),
        scratch_shapes=[
            VMEM((4, width, width), BF),
            VMEM((ranks, rows, 2 * width), BF),
            VMEM((4,) + pack.shape, F32),
            VMEM((pairs, 2 * rows, PAIR), F32),
            VMEM((pairs, 2 * rows, PAIR), F32),
            VMEM((pairs, 2 * rows, PAIR), F32),
            pltpu.SemaphoreType.DMA((96,)),
            pltpu.SemaphoreType.DMA((ranks,)),
            pltpu.SemaphoreType.DMA((16,)),
        ],
        compiler_params=pltpu.CompilerParams(
            collective_id=1, has_side_effects=True, vmem_limit_bytes=48 * 2**20
        ),
    )(tok, pack, cosr, sinr, kb, qb, cot, wq, wk, wv, wo, sg, su, eg, eu)


def angles_of(block_deal, rows_dev):
    here = places(lax.axis_index("ctx") * rows_dev, rows_dev, block_deal, rows_dev)
    half_size = HD // 2
    frequency = 10000.0 ** (-jnp.arange(half_size, dtype=F32) / half_size)
    angles = here.astype(F32)[:, None] * frequency[None, :]
    cosine, sine = jnp.cos(angles), jnp.sin(angles)
    cosr = jnp.concatenate([cosine] * 4, axis=1)
    sinr = jnp.concatenate([-sine, sine, -sine, sine], axis=1)
    return here, cosr, sinr


def pack_params(gain_one, gain_two, router):
    width = 4 * gain_one.shape[0]
    shard = jnp.concatenate(
        [gain_one[None], gain_two[None], router.T, jnp.zeros((6, gain_one.shape[0]), BF)], axis=0
    ).astype(F32)
    start = lax.axis_index("wt") * gain_one.shape[0]
    return lax.dynamic_update_slice(jnp.zeros((16, width), F32), shard, (0, start))


def contract_product(left, right, left_dim, right_dim):
    return lax.dot_general(
        left, right, (((left_dim,), (right_dim,)), ((), ())), preferred_element_type=jnp.float32
    )


def contract_exact(left, right, left_dim, right_dim):
    return lax.dot_general(
        left,
        right,
        (((left_dim,), (right_dim,)), ((), ())),
        precision=HIGH,
        preferred_element_type=jnp.float32,
    )


def rms_norm(values, gain):
    norm_scale = lax.rsqrt(jnp.mean(values * values, axis=-1, keepdims=True) + EPS)
    return (values * norm_scale * gain, norm_scale)


def rms_back(values, norm_scale, gain, upstream):
    weighted = upstream * gain
    inner_mean = jnp.mean(weighted * values, axis=-1, keepdims=True)
    through = norm_scale * weighted - values * norm_scale * norm_scale * norm_scale * inner_mean
    return (through, jnp.sum(upstream * values * norm_scale, axis=0))


def silu_parts(gate_part):
    sigmoid = jax.nn.sigmoid(gate_part)
    return (gate_part * sigmoid, sigmoid * (1.0 + gate_part * (1.0 - sigmoid)))


def rotate(values, place, sign):
    half_size = HD // 2
    frequency = 10000.0 ** (-jnp.arange(half_size, dtype=jnp.float32) / half_size)
    angles = place.astype(jnp.float32)[:, None] * frequency[None, :]
    cosine = jnp.cos(angles)[:, None, :]
    sine_part = sign * jnp.sin(angles)[:, None, :]
    shaped = values.reshape(values.shape[0], values.shape[1] // HD, 2, half_size)
    first_half = shaped[:, :, 0, :]
    second_half = shaped[:, :, 1, :]
    turned = jnp.stack(
        [
            first_half * cosine - second_half * sine_part,
            second_half * cosine + first_half * sine_part,
        ],
        axis=2,
    )
    return turned.reshape(values.shape)


def places(first_row, row_count, block_deal, rows_dev):
    row_index = first_row + jnp.arange(row_count, dtype=jnp.int32)
    owner_rank = row_index // rows_dev
    inner_row = row_index % rows_dev
    ranks = block_deal.shape[0]
    matches = owner_rank[:, None] == jnp.arange(ranks, dtype=jnp.int32)[None, :]
    paired = jnp.sum(jnp.where(matches, block_deal[None, :], 0), axis=1)
    piece_size = rows_dev // 2
    unit_index = jnp.where(inner_row < piece_size, paired, 2 * ranks - 1 - paired)
    return unit_index * piece_size + inner_row % piece_size


def score_block(query_side, key_rows, key_place):
    query3, query_block = query_side
    key3 = key_rows.reshape(key_rows.shape[0], -1, HD)
    raw_scores = jnp.einsum("qhd,khd->hqk", query3, key3, preferred_element_type=jnp.float32)
    allowed = (key_place // BLK)[None, None, :] <= query_block[None, :, None]
    return (jnp.where(allowed, raw_scores * HD ** (-0.5), MASKED), allowed)


def absorb(running, key_rows, value_rows, key_place, query_side):
    largest, denom, accum = running
    scores, allowed = score_block(query_side, key_rows, key_place)
    new_largest = jnp.maximum(largest, jnp.max(scores, axis=2))
    factor = jnp.exp(largest - new_largest)
    raised = jnp.where(allowed, jnp.exp(scores - new_largest[:, :, None]), 0.0)
    denom = denom * factor + jnp.sum(raised, axis=2)
    value3 = value_rows.reshape(value_rows.shape[0], -1, HD)
    accum = accum * factor.T[:, :, None] + jnp.einsum(
        "hqk,khd->qhd", raised.astype(jnp.bfloat16), value3, preferred_element_type=jnp.float32
    )
    return (new_largest, denom, accum)


def fold_keys(running, key_piece, query_side, block_deal, rows_dev):
    key_all, value_all = key_piece
    row_count = key_all.shape[0]
    block_size = KEY_ROWS

    def key_step(current, offset):
        key_rows = lax.dynamic_slice_in_dim(key_all, offset, block_size, 0)
        value_rows = lax.dynamic_slice_in_dim(value_all, offset, block_size, 0)
        key_place = places(offset, block_size, block_deal, rows_dev)
        return (absorb(current, key_rows, value_rows, key_place, query_side), None)

    offsets = jnp.arange(row_count // block_size, dtype=jnp.int32) * block_size
    running, unused = lax.scan(key_step, running, offsets)
    return running


def differentiate(query_side, log_total, delta, grad_out3, key_rows, value_rows, key_place):
    scores, allowed = score_block(query_side, key_rows, key_place)
    probs_full = jnp.where(allowed, jnp.exp(scores - log_total[:, :, None]), 0.0)
    value3 = value_rows.reshape(value_rows.shape[0], -1, HD)
    grad_probs = jnp.einsum("qhd,khd->hqk", grad_out3, value3, preferred_element_type=jnp.float32)
    grad_scores = (probs_full * (grad_probs - delta[:, :, None]) * HD ** (-0.5)).astype(
        jnp.bfloat16
    )
    return (probs_full, grad_scores)


def assign_slots(route, order, experts, capacity):
    pair_count = order.shape[0]
    expert_ids = route.reshape(pair_count)
    ordered = expert_ids[order]
    onehot = (ordered[:, None] == jnp.arange(experts, dtype=jnp.int32)[None, :]).astype(jnp.int32)
    before = jnp.cumsum(onehot, axis=0) - onehot
    slot_turn = jnp.sum(before * onehot, axis=1)
    slot_index = jnp.zeros((pair_count,), jnp.int32).at[order].set(slot_turn)
    kept_pairs = slot_index < capacity
    target = jnp.where(kept_pairs, expert_ids * capacity + slot_index, experts * capacity)
    slot_table = (
        jnp.full((experts * capacity,), pair_count, jnp.int32)
        .at[target]
        .set(jnp.arange(pair_count, dtype=jnp.int32), mode="drop")
    )
    return (target, kept_pairs, slot_table)


def body(
    tokens,
    cotangent,
    gain_attention,
    query_weight,
    key_weight,
    value_weight,
    output_weight,
    gain_mixer,
    router_weight,
    shared_gate,
    shared_up,
    shared_down,
    expert_gate,
    expert_up,
    expert_down,
    routes,
    slot_order,
    block_deal,
):
    rows_dev = tokens.shape[1]
    width = tokens.shape[2]
    ranks = lax.axis_size("ctx")
    (
        gain_one,
        query_full,
        key_full,
        value_full,
        output_full,
        gain_two,
        router_full,
        sgate_full,
        sup_full,
        sdown_full,
        expert_gate_whole,
        expert_up_whole,
        edown_full,
    ) = (
        lax.all_gather(gain_attention, "wt", axis=0, tiled=True),
        lax.all_gather(query_weight, "wt", axis=0, tiled=True),
        lax.all_gather(key_weight, "wt", axis=0, tiled=True),
        lax.all_gather(value_weight, "wt", axis=0, tiled=True),
        lax.all_gather(output_weight, "wt", axis=0, tiled=True),
        lax.all_gather(gain_mixer, "wt", axis=0, tiled=True),
        lax.all_gather(router_weight, "wt", axis=0, tiled=True),
        lax.all_gather(shared_gate, "wt", axis=0, tiled=True),
        lax.all_gather(shared_up, "wt", axis=0, tiled=True),
        lax.all_gather(shared_down, "wt", axis=0, tiled=True),
        lax.all_gather(expert_gate, "wt", axis=0, tiled=True),
        lax.all_gather(expert_up, "wt", axis=0, tiled=True),
        lax.all_gather(expert_down, "wt", axis=0, tiled=True),
    )
    gain_first = gain_one.astype(jnp.float32)
    gain_second = gain_two.astype(jnp.float32)
    heads = width // HD
    inputs = tokens[0].astype(jnp.float32)
    here = places(lax.axis_index("ctx") * rows_dev, rows_dev, block_deal, rows_dev)
    query_side_block = here // BLK
    normed_f, scale_one = rms_norm(inputs, gain_first)
    normed = normed_f.astype(jnp.bfloat16)
    query_rot = rotate(
        jnp.dot(normed, query_full, preferred_element_type=jnp.float32), here, 1.0
    ).astype(jnp.bfloat16)
    key_rot = rotate(
        jnp.dot(normed, key_full, preferred_element_type=jnp.float32), here, 1.0
    ).astype(jnp.bfloat16)
    value_low = jnp.dot(normed, value_full, preferred_element_type=jnp.float32).astype(jnp.bfloat16)
    query3 = query_rot.reshape(rows_dev, heads, HD)
    query_side = (query3, query_side_block)
    start_state = (
        jnp.full((heads, rows_dev), MASKED, jnp.float32),
        jnp.zeros((heads, rows_dev), jnp.float32),
        jnp.zeros((rows_dev, heads, HD), jnp.float32),
    )
    largest, denom, accum = fold_keys(
        start_state,
        (
            lax.all_gather(key_rot, "ctx", axis=0, tiled=True),
            lax.all_gather(value_low, "ctx", axis=0, tiled=True),
        ),
        query_side,
        block_deal,
        rows_dev,
    )
    mixed3 = accum / denom.T[:, :, None]
    log_total = largest + jnp.log(denom)
    mixed_low = mixed3.reshape(rows_dev, width).astype(jnp.bfloat16)
    second = inputs + jnp.dot(mixed_low, output_full, preferred_element_type=jnp.float32)
    mixer_f, scale_two = rms_norm(second, gain_second)
    mixer = mixer_f.astype(jnp.bfloat16)
    experts = router_full.shape[1]
    logits = jnp.dot(mixer, router_full, preferred_element_type=jnp.float32)
    route = routes[0]
    top_count = route.shape[1]
    pair_count = rows_dev * top_count
    capacity = (5 * pair_count + 4 * experts - 1) // (4 * experts)
    split_count = ranks // experts
    expert_match = route[:, :, None] == jnp.arange(experts, dtype=jnp.int32)[None, None, :]
    chosen = jnp.sum(jnp.where(expert_match, logits[:, None, :], 0.0), axis=2)
    gates = jax.nn.softmax(chosen, axis=1)
    target, kept_pairs, slot_table = assign_slots(route, slot_order[0, 0], experts, capacity)
    valid = slot_table < pair_count
    pair_pick = jnp.minimum(slot_table, pair_count - 1)
    target_pick = jnp.minimum(target, experts * capacity - 1)
    send_rows = jnp.where(
        valid[:, None], mixer[pair_pick // top_count], jnp.zeros((), jnp.bfloat16)
    )
    send_rows = jnp.broadcast_to(
        send_rows.reshape(experts, 1, capacity, width), (experts, split_count, capacity, width)
    ).reshape(ranks, capacity, width)
    received = lax.all_to_all(send_rows, "ctx", split_axis=0, concat_axis=0, tiled=True)
    slot_count = received.shape[1]
    flattened_input = received.reshape(ranks * slot_count, width)
    gate_part = jnp.dot(flattened_input, expert_gate_whole, preferred_element_type=jnp.float32)
    up_projection_part = jnp.dot(
        flattened_input, expert_up_whole, preferred_element_type=jnp.float32
    )
    activated, unused = silu_parts(gate_part)
    hidden = (activated * up_projection_part).astype(jnp.bfloat16)
    partial_value = contract_product(hidden, edown_full, 1, 1).reshape(ranks, slot_count, width)
    back = lax.all_to_all(
        partial_value.astype(jnp.bfloat16), "ctx", split_axis=0, concat_axis=0, tiled=True
    ).astype(partial_value.dtype)
    expert_gate_part = gate_part.reshape(ranks, slot_count, -1)
    expert_up_part = up_projection_part.reshape(ranks, slot_count, -1)
    combined = jnp.sum(back.reshape(experts, split_count, capacity, width), axis=1).reshape(
        experts * capacity, width
    )
    pair_out = jnp.where(kept_pairs[:, None], combined[target_pick], 0.0).reshape(
        rows_dev, top_count, width
    )
    mixture = jnp.sum(gates[:, :, None] * pair_out, axis=1)
    sgate_part = jnp.dot(mixer, sgate_full, preferred_element_type=jnp.float32)
    sup_part = jnp.dot(mixer, sup_full, preferred_element_type=jnp.float32)
    shared_act, shared_slope = silu_parts(sgate_part)
    shared_hidden = (shared_act * sup_part).astype(jnp.bfloat16)
    shared_out = jnp.dot(shared_hidden, sdown_full, preferred_element_type=jnp.float32)
    result = (second + mixture + shared_out).astype(jnp.bfloat16)
    grad_final = cotangent[0].astype(jnp.float32)
    grad_low = grad_final.astype(jnp.bfloat16)
    sdown_grad = contract_product(shared_hidden, grad_low, 0, 0)
    grad_shared_hidden = contract_product(grad_low, sdown_full, 1, 1)
    grad_sgate = (grad_shared_hidden * sup_part * shared_slope).astype(jnp.bfloat16)
    grad_sup = (grad_shared_hidden * shared_act).astype(jnp.bfloat16)
    sgate_grad = contract_product(mixer, grad_sgate, 0, 0)
    sup_grad = contract_product(mixer, grad_sup, 0, 0)
    grad_mixer = contract_product(grad_sgate, sgate_full, 1, 1) + contract_product(
        grad_sup, sup_full, 1, 1
    )
    pair_grad = (
        (gates[:, :, None] * grad_final[:, None, :]).reshape(pair_count, width).astype(jnp.bfloat16)
    )
    grad_gates = jnp.sum(grad_final[:, None, :] * pair_out, axis=2)
    send_grad = jnp.where(valid[:, None], pair_grad[pair_pick], jnp.zeros((), jnp.bfloat16))
    send_grad = jnp.broadcast_to(
        send_grad.reshape(experts, 1, capacity, width), (experts, split_count, capacity, width)
    ).reshape(ranks, capacity, width)
    recv_grad = lax.all_to_all(send_grad, "ctx", split_axis=0, concat_axis=0, tiled=True)
    flattened_input = received.reshape(ranks * capacity, width)
    flat_grad = recv_grad.reshape(ranks * capacity, width)
    gate_flat = expert_gate_part.reshape(ranks * capacity, -1)
    up_flat = expert_up_part.reshape(ranks * capacity, -1)
    expert_activation, expert_slope = silu_parts(gate_flat)
    expert_hidden = (expert_activation * up_flat).astype(jnp.bfloat16)
    edown_grad = contract_product(flat_grad, expert_hidden, 0, 0)
    expert_hidden_grad = jnp.dot(flat_grad, edown_full, preferred_element_type=jnp.float32)
    expert_gate_grad_rows = (expert_hidden_grad * up_flat * expert_slope).astype(jnp.bfloat16)
    expert_up_grad_rows = (expert_hidden_grad * expert_activation).astype(jnp.bfloat16)
    egate_grad = contract_product(flattened_input, expert_gate_grad_rows, 0, 0)
    expert_up_weight_grad = contract_product(flattened_input, expert_up_grad_rows, 0, 0)
    input_back = (
        contract_product(expert_gate_grad_rows, expert_gate_whole, 1, 1)
        + contract_product(expert_up_grad_rows, expert_up_whole, 1, 1)
    ).reshape(ranks, capacity, width)
    back_grad = lax.all_to_all(
        input_back.astype(jnp.bfloat16), "ctx", split_axis=0, concat_axis=0, tiled=True
    ).astype(input_back.dtype)
    merged = jnp.sum(back_grad.reshape(experts, split_count, capacity, width), axis=1).reshape(
        experts * capacity, width
    )
    pair_back = jnp.where(kept_pairs[:, None], merged[target_pick], 0.0).reshape(
        rows_dev, top_count, width
    )
    grad_mixer = grad_mixer + jnp.sum(pair_back, axis=1)
    grad_chosen = gates * (grad_gates - jnp.sum(gates * grad_gates, axis=1, keepdims=True))
    grad_logits = jnp.sum(jnp.where(expert_match, grad_chosen[:, :, None], 0.0), axis=1)
    router_grad = contract_exact(mixer.astype(jnp.float32), grad_logits, 0, 0)
    grad_mixer = grad_mixer + contract_exact(grad_logits, router_full.astype(jnp.float32), 1, 1)
    through_two, gain_two_grad = rms_back(second, scale_two, gain_second, grad_mixer)
    grad_second = grad_final + through_two
    grad_attention = grad_second.astype(jnp.bfloat16)
    output_grad = contract_product(mixed_low, grad_attention, 0, 0)
    grad_mixed = contract_product(grad_attention, output_full, 1, 1).astype(jnp.bfloat16)
    grad_out3 = grad_mixed.reshape(rows_dev, heads, HD)
    delta = jnp.sum(grad_out3.astype(jnp.float32) * mixed3, axis=2).T
    all_keys, all_values = (
        lax.all_gather(key_rot, "ctx", axis=0, tiled=True),
        lax.all_gather(value_low, "ctx", axis=0, tiled=True),
    )
    total_rows = all_keys.shape[0]
    block_size = KEY_ROWS

    def query_step(grad_sum, offset):
        key_rows = lax.dynamic_slice_in_dim(all_keys, offset, block_size, 0)
        value_rows = lax.dynamic_slice_in_dim(all_values, offset, block_size, 0)
        key_place = places(offset, block_size, block_deal, rows_dev)
        unused, grad_scores = differentiate(
            query_side, log_total, delta, grad_out3, key_rows, value_rows, key_place
        )
        key3 = key_rows.reshape(block_size, heads, HD)
        return (
            grad_sum
            + jnp.einsum("hqk,khd->qhd", grad_scores, key3, preferred_element_type=jnp.float32),
            None,
        )

    offsets = jnp.arange(total_rows // block_size, dtype=jnp.int32) * block_size
    grad_query3, unused = lax.scan(
        query_step, jnp.zeros((rows_dev, heads, HD), jnp.float32), offsets
    )
    inner_size = KEY_ROWS

    def one_part(offset):
        key_rows = lax.dynamic_slice_in_dim(all_keys, offset, inner_size, 0)
        value_rows = lax.dynamic_slice_in_dim(all_values, offset, inner_size, 0)
        key_place = places(offset, inner_size, block_deal, rows_dev)
        probs_full, grad_scores = differentiate(
            query_side, log_total, delta, grad_out3, key_rows, value_rows, key_place
        )
        grad_value_rows = jnp.einsum(
            "hqk,qhd->khd",
            probs_full.astype(jnp.bfloat16),
            grad_out3,
            preferred_element_type=jnp.float32,
        )
        grad_key_rows = jnp.einsum(
            "hqk,qhd->khd", grad_scores, query3, preferred_element_type=jnp.float32
        )
        return jnp.concatenate(
            [grad_key_rows.reshape(inner_size, width), grad_value_rows.reshape(inner_size, width)],
            axis=1,
        )

    parts = lax.map(
        one_part,
        jnp.arange(lax.axis_size("ctx") * rows_dev // inner_size, dtype=jnp.int32) * inner_size,
    )
    key_value_grad = lax.psum_scatter(
        parts.reshape(lax.axis_size("ctx") * rows_dev, 2 * width),
        "ctx",
        scatter_dimension=0,
        tiled=True,
    )
    grad_key_pre = rotate(key_value_grad[:, :width], here, -1.0).astype(jnp.bfloat16)
    grad_value_low = key_value_grad[:, width:].astype(jnp.bfloat16)
    grad_query_pre = rotate(grad_query3.reshape(rows_dev, width), here, -1.0).astype(jnp.bfloat16)
    query_grad = contract_product(normed, grad_query_pre, 0, 0)
    key_grad = contract_product(normed, grad_key_pre, 0, 0)
    value_grad = contract_product(normed, grad_value_low, 0, 0)
    grad_normed = (
        contract_product(grad_query_pre, query_full, 1, 1)
        + contract_product(grad_key_pre, key_full, 1, 1)
        + contract_product(grad_value_low, value_full, 1, 1)
    )
    through_one, gain_one_grad = rms_back(inputs, scale_one, gain_first, grad_normed)
    grad_input = grad_second + through_one
    (
        gain_one_share,
        query_share,
        key_share,
        value_share,
        output_share,
        gain_two_share,
        router_share,
        sgate_share,
        sup_share,
        sdown_share,
        egate_share,
        expert_up_portion,
        edown_share,
    ) = (
        lax.psum_scatter(
            gain_one_grad.astype(jnp.bfloat16), "wt", scatter_dimension=0, tiled=True
        ).astype(jnp.float32),
        lax.psum_scatter(
            query_grad.astype(jnp.bfloat16), "wt", scatter_dimension=0, tiled=True
        ).astype(jnp.float32),
        lax.psum_scatter(
            key_grad.astype(jnp.bfloat16), "wt", scatter_dimension=0, tiled=True
        ).astype(jnp.float32),
        lax.psum_scatter(
            value_grad.astype(jnp.bfloat16), "wt", scatter_dimension=0, tiled=True
        ).astype(jnp.float32),
        lax.psum_scatter(
            output_grad.astype(jnp.bfloat16), "wt", scatter_dimension=0, tiled=True
        ).astype(jnp.float32),
        lax.psum_scatter(
            gain_two_grad.astype(jnp.bfloat16), "wt", scatter_dimension=0, tiled=True
        ).astype(jnp.float32),
        lax.psum_scatter(
            router_grad.astype(jnp.bfloat16), "wt", scatter_dimension=0, tiled=True
        ).astype(jnp.float32),
        lax.psum_scatter(
            sgate_grad.astype(jnp.bfloat16), "wt", scatter_dimension=0, tiled=True
        ).astype(jnp.float32),
        lax.psum_scatter(
            sup_grad.astype(jnp.bfloat16), "wt", scatter_dimension=0, tiled=True
        ).astype(jnp.float32),
        lax.psum_scatter(
            sdown_grad.astype(jnp.bfloat16), "wt", scatter_dimension=0, tiled=True
        ).astype(jnp.float32),
        lax.psum_scatter(
            egate_grad.astype(jnp.bfloat16), "wt", scatter_dimension=0, tiled=True
        ).astype(jnp.float32),
        lax.psum_scatter(
            expert_up_weight_grad.astype(jnp.bfloat16), "wt", scatter_dimension=0, tiled=True
        ).astype(jnp.float32),
        lax.psum_scatter(
            edown_grad.astype(jnp.bfloat16), "wt", scatter_dimension=0, tiled=True
        ).astype(jnp.float32),
    )
    (
        gain_one_sum,
        query_sum,
        key_sum,
        value_sum,
        output_sum,
        gain_two_sum,
        router_sum,
        sgate_sum,
        sup_sum,
        sdown_sum,
    ) = lax.psum(
        (
            gain_one_share,
            query_share,
            key_share,
            value_share,
            output_share,
            gain_two_share,
            router_share,
            sgate_share,
            sup_share,
            sdown_share,
        ),
        "ctx",
    )
    return (
        result[None],
        grad_input[None],
        gain_one_sum,
        query_sum,
        key_sum,
        value_sum,
        output_sum,
        gain_two_sum,
        router_sum,
        sgate_sum,
        sup_sum,
        sdown_sum,
        egate_share,
        expert_up_portion,
        edown_share,
    )


def fast_body(
    tokens,
    cotangent,
    gain_attention,
    query_weight,
    key_weight,
    value_weight,
    output_weight,
    gain_mixer,
    router_weight,
    shared_gate,
    shared_up,
    shared_down,
    expert_gate,
    expert_up,
    expert_down,
    routes,
    slot_order,
    block_deal,
):
    rows_dev = tokens.shape[1]
    width = tokens.shape[2]
    ranks = lax.axis_size("ctx")
    heads = width // HD
    inputs = tokens[0].astype(jnp.float32)
    here, cosr, sinr = angles_of(block_deal, rows_dev)
    query_side_block = here // BLK
    kb = (places(0, ranks * rows_dev, block_deal, rows_dev) // BLK)[None, :]
    qb = jnp.concatenate([query_side_block, query_side_block])[:, None]
    pack = pack_params(gain_attention, gain_mixer, router_weight)
    (q_st, kv_all, mixed_f, lse, second, mixer, normed, pack_all, wfull, sg_sl, su_sl, expert_gate_whole, expert_up_whole, cot4) = run_forward(
        tokens[0], pack, cosr, sinr, kb, qb, cotangent[0], query_weight, key_weight, value_weight, output_weight, shared_gate, shared_up, expert_gate, expert_up)
    gain_first, gain_second = pack_all[0], pack_all[1]
    router_full = pack_all[2:10].T.astype(jnp.bfloat16)
    query_full, key_full, value_full, output_full = wfull[0], wfull[1], wfull[2], wfull[3]
    sgate_full = lax.all_gather(shared_gate, "wt", axis=0, tiled=True)
    sup_full = lax.all_gather(shared_up, "wt", axis=0, tiled=True)
    sdown_full = lax.all_gather(shared_down, "wt", axis=0, tiled=True)
    edown_full = lax.all_gather(expert_down, "wt", axis=0, tiled=True)
    query_rot = (8.0 * (q_st[:, :rows_dev] + q_st[:, rows_dev:])).astype(jnp.bfloat16).transpose(1, 0, 2).reshape(rows_dev, width)
    query3 = query_rot.reshape(rows_dev, heads, HD)
    query_side = (query3, query_side_block)
    log_total = lse[:, :, 0].reshape(heads, rows_dev)
    mixed3 = mixed_f.reshape(rows_dev, heads, HD)
    scale_one = lax.rsqrt(jnp.mean(inputs * inputs, axis=-1, keepdims=True) + EPS)
    scale_two = lax.rsqrt(jnp.mean(second * second, axis=-1, keepdims=True) + EPS)
    key_rot = kv_all[lax.axis_index("ctx"), :, :width]
    mixed_low = mixed3.reshape(rows_dev, width).astype(jnp.bfloat16)
    experts = router_full.shape[1]
    logits = jnp.dot(mixer, router_full, preferred_element_type=jnp.float32)
    route = routes[0]
    top_count = route.shape[1]
    pair_count = rows_dev * top_count
    capacity = (5 * pair_count + 4 * experts - 1) // (4 * experts)
    split_count = ranks // experts
    expert_match = route[:, :, None] == jnp.arange(experts, dtype=jnp.int32)[None, None, :]
    chosen = jnp.sum(jnp.where(expert_match, logits[:, None, :], 0.0), axis=2)
    gates = jax.nn.softmax(chosen, axis=1)
    target, kept_pairs, slot_table = assign_slots(route, slot_order[0, 0], experts, capacity)
    valid = slot_table < pair_count
    pair_pick = jnp.minimum(slot_table, pair_count - 1)
    target_pick = jnp.minimum(target, experts * capacity - 1)
    send_rows = jnp.where(
        valid[:, None], mixer[pair_pick // top_count], jnp.zeros((), jnp.bfloat16)
    )
    send_rows = jnp.broadcast_to(
        send_rows.reshape(experts, 1, capacity, width), (experts, split_count, capacity, width)
    ).reshape(ranks, capacity, width)
    received = lax.all_to_all(send_rows, "ctx", split_axis=0, concat_axis=0, tiled=True)
    slot_count = received.shape[1]
    flattened_input = received.reshape(ranks * slot_count, width)
    gate_part = jnp.dot(flattened_input, expert_gate_whole, preferred_element_type=jnp.float32)
    up_projection_part = jnp.dot(
        flattened_input, expert_up_whole, preferred_element_type=jnp.float32
    )
    activated, unused = silu_parts(gate_part)
    hidden = (activated * up_projection_part).astype(jnp.bfloat16)
    partial_value = contract_product(hidden, edown_full, 1, 1).reshape(ranks, slot_count, width)
    back = lax.all_to_all(
        partial_value.astype(jnp.bfloat16), "ctx", split_axis=0, concat_axis=0, tiled=True
    ).astype(partial_value.dtype)
    expert_gate_part = gate_part.reshape(ranks, slot_count, -1)
    expert_up_part = up_projection_part.reshape(ranks, slot_count, -1)
    combined = jnp.sum(back.reshape(experts, split_count, capacity, width), axis=1).reshape(
        experts * capacity, width
    )
    pair_out = jnp.where(kept_pairs[:, None], combined[target_pick], 0.0).reshape(
        rows_dev, top_count, width
    )
    mixture = jnp.sum(gates[:, :, None] * pair_out, axis=1)
    sgate_part = jnp.dot(mixer, sgate_full, preferred_element_type=jnp.float32)
    sup_part = jnp.dot(mixer, sup_full, preferred_element_type=jnp.float32)
    shared_act, shared_slope = silu_parts(sgate_part)
    shared_hidden = (shared_act * sup_part).astype(jnp.bfloat16)
    shared_out = jnp.dot(shared_hidden, sdown_full, preferred_element_type=jnp.float32)
    result = (second + mixture + shared_out).astype(jnp.bfloat16)
    grad_final = cotangent[0].astype(jnp.float32)
    grad_low = grad_final.astype(jnp.bfloat16)
    sdown_grad = contract_product(shared_hidden, grad_low, 0, 0)
    grad_shared_hidden = contract_product(grad_low, sdown_full, 1, 1)
    grad_sgate = (grad_shared_hidden * sup_part * shared_slope).astype(jnp.bfloat16)
    grad_sup = (grad_shared_hidden * shared_act).astype(jnp.bfloat16)
    sgate_grad = contract_product(mixer, grad_sgate, 0, 0)
    sup_grad = contract_product(mixer, grad_sup, 0, 0)
    grad_mixer = contract_product(grad_sgate, sgate_full, 1, 1) + contract_product(
        grad_sup, sup_full, 1, 1
    )
    pair_grad = (
        (gates[:, :, None] * grad_final[:, None, :]).reshape(pair_count, width).astype(jnp.bfloat16)
    )
    grad_gates = jnp.sum(grad_final[:, None, :] * pair_out, axis=2)
    send_grad = jnp.where(valid[:, None], pair_grad[pair_pick], jnp.zeros((), jnp.bfloat16))
    send_grad = jnp.broadcast_to(
        send_grad.reshape(experts, 1, capacity, width), (experts, split_count, capacity, width)
    ).reshape(ranks, capacity, width)
    recv_grad = lax.all_to_all(send_grad, "ctx", split_axis=0, concat_axis=0, tiled=True)
    flattened_input = received.reshape(ranks * capacity, width)
    flat_grad = recv_grad.reshape(ranks * capacity, width)
    gate_flat = expert_gate_part.reshape(ranks * capacity, -1)
    up_flat = expert_up_part.reshape(ranks * capacity, -1)
    expert_activation, expert_slope = silu_parts(gate_flat)
    expert_hidden = (expert_activation * up_flat).astype(jnp.bfloat16)
    edown_grad = contract_product(flat_grad, expert_hidden, 0, 0)
    expert_hidden_grad = jnp.dot(flat_grad, edown_full, preferred_element_type=jnp.float32)
    expert_gate_grad_rows = (expert_hidden_grad * up_flat * expert_slope).astype(jnp.bfloat16)
    expert_up_grad_rows = (expert_hidden_grad * expert_activation).astype(jnp.bfloat16)
    egate_grad = contract_product(flattened_input, expert_gate_grad_rows, 0, 0)
    expert_up_weight_grad = contract_product(flattened_input, expert_up_grad_rows, 0, 0)
    input_back = (
        contract_product(expert_gate_grad_rows, expert_gate_whole, 1, 1)
        + contract_product(expert_up_grad_rows, expert_up_whole, 1, 1)
    ).reshape(ranks, capacity, width)
    back_grad = lax.all_to_all(
        input_back.astype(jnp.bfloat16), "ctx", split_axis=0, concat_axis=0, tiled=True
    ).astype(input_back.dtype)
    merged = jnp.sum(back_grad.reshape(experts, split_count, capacity, width), axis=1).reshape(
        experts * capacity, width
    )
    pair_back = jnp.where(kept_pairs[:, None], merged[target_pick], 0.0).reshape(
        rows_dev, top_count, width
    )
    grad_mixer = grad_mixer + jnp.sum(pair_back, axis=1)
    grad_chosen = gates * (grad_gates - jnp.sum(gates * grad_gates, axis=1, keepdims=True))
    grad_logits = jnp.sum(jnp.where(expert_match, grad_chosen[:, :, None], 0.0), axis=1)
    router_grad = contract_exact(mixer.astype(jnp.float32), grad_logits, 0, 0)
    grad_mixer = grad_mixer + contract_exact(grad_logits, router_full.astype(jnp.float32), 1, 1)
    through_two, gain_two_grad = rms_back(second, scale_two, gain_second, grad_mixer)
    grad_second = grad_final + through_two
    grad_attention = grad_second.astype(jnp.bfloat16)
    output_grad = contract_product(mixed_low, grad_attention, 0, 0)
    grad_mixed = contract_product(grad_attention, output_full, 1, 1).astype(jnp.bfloat16)
    grad_out3 = grad_mixed.reshape(rows_dev, heads, HD)
    delta = jnp.sum(grad_out3.astype(jnp.float32) * mixed3, axis=2).T
    all_keys, all_values = (
        kv_all[:, :, :width].reshape(ranks * rows_dev, width),
        kv_all[:, :, width:].reshape(ranks * rows_dev, width),
    )
    total_rows = all_keys.shape[0]
    block_size = KEY_ROWS

    def query_step(grad_sum, offset):
        key_rows = lax.dynamic_slice_in_dim(all_keys, offset, block_size, 0)
        value_rows = lax.dynamic_slice_in_dim(all_values, offset, block_size, 0)
        key_place = places(offset, block_size, block_deal, rows_dev)
        unused, grad_scores = differentiate(
            query_side, log_total, delta, grad_out3, key_rows, value_rows, key_place
        )
        key3 = key_rows.reshape(block_size, heads, HD)
        return (
            grad_sum
            + jnp.einsum("hqk,khd->qhd", grad_scores, key3, preferred_element_type=jnp.float32),
            None,
        )

    offsets = jnp.arange(total_rows // block_size, dtype=jnp.int32) * block_size
    grad_query3, unused = lax.scan(
        query_step, jnp.zeros((rows_dev, heads, HD), jnp.float32), offsets
    )
    inner_size = KEY_ROWS

    def one_part(offset):
        key_rows = lax.dynamic_slice_in_dim(all_keys, offset, inner_size, 0)
        value_rows = lax.dynamic_slice_in_dim(all_values, offset, inner_size, 0)
        key_place = places(offset, inner_size, block_deal, rows_dev)
        probs_full, grad_scores = differentiate(
            query_side, log_total, delta, grad_out3, key_rows, value_rows, key_place
        )
        grad_value_rows = jnp.einsum(
            "hqk,qhd->khd",
            probs_full.astype(jnp.bfloat16),
            grad_out3,
            preferred_element_type=jnp.float32,
        )
        grad_key_rows = jnp.einsum(
            "hqk,qhd->khd", grad_scores, query3, preferred_element_type=jnp.float32
        )
        return jnp.concatenate(
            [grad_key_rows.reshape(inner_size, width), grad_value_rows.reshape(inner_size, width)],
            axis=1,
        )

    parts = lax.map(
        one_part,
        jnp.arange(lax.axis_size("ctx") * rows_dev // inner_size, dtype=jnp.int32) * inner_size,
    )
    key_value_grad = lax.psum_scatter(
        parts.reshape(lax.axis_size("ctx") * rows_dev, 2 * width),
        "ctx",
        scatter_dimension=0,
        tiled=True,
    )
    grad_key_pre = rotate(key_value_grad[:, :width], here, -1.0).astype(jnp.bfloat16)
    grad_value_low = key_value_grad[:, width:].astype(jnp.bfloat16)
    grad_query_pre = rotate(grad_query3.reshape(rows_dev, width), here, -1.0).astype(jnp.bfloat16)
    query_grad = contract_product(normed, grad_query_pre, 0, 0)
    key_grad = contract_product(normed, grad_key_pre, 0, 0)
    value_grad = contract_product(normed, grad_value_low, 0, 0)
    grad_normed = (
        contract_product(grad_query_pre, query_full, 1, 1)
        + contract_product(grad_key_pre, key_full, 1, 1)
        + contract_product(grad_value_low, value_full, 1, 1)
    )
    through_one, gain_one_grad = rms_back(inputs, scale_one, gain_first, grad_normed)
    grad_input = grad_second + through_one
    (
        gain_one_share,
        query_share,
        key_share,
        value_share,
        output_share,
        gain_two_share,
        router_share,
        sgate_share,
        sup_share,
        sdown_share,
        egate_share,
        expert_up_portion,
        edown_share,
    ) = (
        lax.psum_scatter(
            gain_one_grad.astype(jnp.bfloat16), "wt", scatter_dimension=0, tiled=True
        ).astype(jnp.float32),
        lax.psum_scatter(
            query_grad.astype(jnp.bfloat16), "wt", scatter_dimension=0, tiled=True
        ).astype(jnp.float32),
        lax.psum_scatter(
            key_grad.astype(jnp.bfloat16), "wt", scatter_dimension=0, tiled=True
        ).astype(jnp.float32),
        lax.psum_scatter(
            value_grad.astype(jnp.bfloat16), "wt", scatter_dimension=0, tiled=True
        ).astype(jnp.float32),
        lax.psum_scatter(
            output_grad.astype(jnp.bfloat16), "wt", scatter_dimension=0, tiled=True
        ).astype(jnp.float32),
        lax.psum_scatter(
            gain_two_grad.astype(jnp.bfloat16), "wt", scatter_dimension=0, tiled=True
        ).astype(jnp.float32),
        lax.psum_scatter(
            router_grad.astype(jnp.bfloat16), "wt", scatter_dimension=0, tiled=True
        ).astype(jnp.float32),
        lax.psum_scatter(
            sgate_grad.astype(jnp.bfloat16), "wt", scatter_dimension=0, tiled=True
        ).astype(jnp.float32),
        lax.psum_scatter(
            sup_grad.astype(jnp.bfloat16), "wt", scatter_dimension=0, tiled=True
        ).astype(jnp.float32),
        lax.psum_scatter(
            sdown_grad.astype(jnp.bfloat16), "wt", scatter_dimension=0, tiled=True
        ).astype(jnp.float32),
        lax.psum_scatter(
            egate_grad.astype(jnp.bfloat16), "wt", scatter_dimension=0, tiled=True
        ).astype(jnp.float32),
        lax.psum_scatter(
            expert_up_weight_grad.astype(jnp.bfloat16), "wt", scatter_dimension=0, tiled=True
        ).astype(jnp.float32),
        lax.psum_scatter(
            edown_grad.astype(jnp.bfloat16), "wt", scatter_dimension=0, tiled=True
        ).astype(jnp.float32),
    )
    (
        gain_one_sum,
        query_sum,
        key_sum,
        value_sum,
        output_sum,
        gain_two_sum,
        router_sum,
        sgate_sum,
        sup_sum,
        sdown_sum,
    ) = lax.psum(
        (
            gain_one_share,
            query_share,
            key_share,
            value_share,
            output_share,
            gain_two_share,
            router_share,
            sgate_share,
            sup_share,
            sdown_share,
        ),
        "ctx",
    )
    return (
        result[None],
        grad_input[None],
        gain_one_sum,
        query_sum,
        key_sum,
        value_sum,
        output_sum,
        gain_two_sum,
        router_sum,
        sgate_sum,
        sup_sum,
        sdown_sum,
        egate_share,
        expert_up_portion,
        edown_share,
    )


def solution(mesh):
    in_specs = (
        P("wt", "ctx", None),
        P("wt", "ctx", None),
        P("wt"),
        P("wt", None),
        P("wt", None),
        P("wt", None),
        P("wt", None),
        P("wt"),
        P("wt", None),
        P("wt", None),
        P("wt", None),
        P("wt", None),
        P("wt", "ctx"),
        P("wt", "ctx"),
        P("wt", "ctx"),
        P("wt", "ctx", None),
        P("wt", "ctx", None),
        P(),
    )
    out_specs = (
        P("wt", "ctx", None),
        P("wt", "ctx", None),
        P("wt"),
        P("wt", None),
        P("wt", None),
        P("wt", None),
        P("wt", None),
        P("wt"),
        P("wt", None),
        P("wt", None),
        P("wt", None),
        P("wt", None),
        P("wt", "ctx"),
        P("wt", "ctx"),
        P("wt", "ctx"),
    )
    chosen = fast_body if (mesh.shape["ctx"], mesh.shape["wt"]) == (8, 4) else body
    return jax.shard_map(chosen, mesh=mesh, in_specs=in_specs, out_specs=out_specs, check_vma=False)
```

```python
import jax
import jax.numpy as jnp
from jax import lax
from jax.experimental import pallas as pl
from jax.experimental.pallas import tpu as pltpu
from jax.sharding import PartitionSpec as P

HD = 64
BLK = 256


EPS = 1e-06
KEY_ROWS = 512
HIGH = lax.Precision.HIGHEST
MASKED = -1e30


MESH = pl.DeviceIdType.MESH
VMEM = pltpu.VMEM
BF = jnp.bfloat16
F32 = jnp.float32
PAIR = 2 * HD


class Spot:
    def __init__(self, line_size):
        self.k = lax.axis_index("ctx")
        self.w = lax.axis_index("wt")
        self.z, self.x = lax.div(self.k, 2), lax.rem(self.k, 2)
        self.y, self.c = lax.div(self.w, 2), lax.rem(self.w, 2)
        self.far = lax.div(self.z, 2)
        self.mid = self.z + self.far * (3 - 2 * self.z)
        step = 1 - 2 * self.far
        self.core = (self.k, 2 * self.y + 1 - self.c)
        self.across = (self.k, 2 * (1 - self.y) + self.c)
        self.corner = (self.k, 2 * (1 - self.y) + 1 - self.c)
        self.column = (2 * self.z + 1 - self.x, self.w)
        self.inner = (2 * (self.z + step) + self.x, self.w)
        self.outer = (2 * (self.z - step) + self.x, self.w)

    def plane(self, step):
        mirrored = (self.mid, 1 - self.mid, 2, 3)[step]
        return mirrored + self.far * (3 - 2 * mirrored)


class Sems:
    def __init__(self, ref):
        self.ref, self.used = ref, 0

    def new(self):
        self.used += 1
        return self.ref.at[self.used - 1]


def remote(src, dst, send, recv, to):
    return pltpu.make_async_remote_copy(
        src_ref=src, dst_ref=dst, send_sem=send, recv_sem=recv, device_id=to, device_id_type=MESH
    )


def greet(devices, middle=None):
    barrier = pltpu.get_barrier_semaphore()
    for to in devices:
        pl.semaphore_signal(barrier, inc=1, device_id=to, device_id_type=MESH)
    if middle is None:
        pl.semaphore_wait(barrier, len(devices))
        return

    @pl.when(middle[0] == 1)
    def _():
        pl.semaphore_signal(barrier, inc=1, device_id=middle[1], device_id_type=MESH)

    pl.semaphore_wait(barrier, len(devices) + middle[0])


class Gather:
    def __init__(self, spot, src, dst, sems):
        self.spot, self.dst, self.sems = spot, dst, sems
        self.rows = src.shape[0]
        here = self.block(spot.w)
        self.local = pltpu.make_async_copy(src, here, sems.new())
        self.to_core = remote(src, here, sems.new(), sems.new(), spot.core)
        self.to_across = remote(src, here, sems.new(), sems.new(), spot.across)
        for copy in (self.to_across, self.to_core, self.local):
            copy.start()

    def block(self, w):
        return self.dst.at[pl.ds(pl.multiple_of(self.rows * w, 64), self.rows)]

    def forward(self):
        self.to_across.wait_recv()
        part = self.block(self.spot.across[1])
        self.onward = remote(part, part, self.sems.new(), self.sems.new(), self.spot.core)
        self.onward.start()

    def finish(self):
        self.local.wait()
        self.to_core.wait_recv()
        self.onward.wait_recv()

    def drain(self):
        self.to_core.wait_send()
        self.to_across.wait_send()
        self.onward.wait_send()


class Spread:
    def __init__(self, spot, pick, place, sems, local=True):
        self.copies = []
        for to in (spot.across, spot.corner, spot.core):
            self.copies.append(remote(pick(to[1]), place(spot.w), sems.new(), sems.new(), to))
        self.local = None
        if local:
            self.local = pltpu.make_async_copy(pick(spot.w), place(spot.w), sems.new())
        for copy in self.copies:
            copy.start()
        if local:
            self.local.start()

    def finish(self):
        for copy in self.copies:
            copy.wait_recv()
        if self.local is not None:
            self.local.wait()

    def drain(self):
        for copy in self.copies:
            copy.wait_send()


def nt(left, right):
    return lax.dot_general(left, right, (((1,), (1,)), ((), ())), preferred_element_type=F32)


def nn(left, right):
    return jnp.dot(left, right, preferred_element_type=F32)


def tn(left, right):
    return lax.dot_general(left, right, (((0,), (0,)), ((), ())), preferred_element_type=F32)


def turn(values, cosine, sine):
    wide = values.shape[1]
    lane = lax.broadcasted_iota(jnp.int32, values.shape, 1)
    first = lax.rem(lane, HD) < HD // 2
    swapped = jnp.where(
        first, pltpu.roll(values, wide - HD // 2, 1), pltpu.roll(values, HD // 2, 1)
    )
    copies = wide // PAIR
    cosine = jnp.concatenate([cosine] * copies, axis=1)
    sine = jnp.concatenate([sine] * copies, axis=1)
    return values * cosine + swapped * sine


def stack_pair(values):
    lane = lax.broadcasted_iota(jnp.int32, values.shape, 1)
    none = jnp.zeros_like(values)
    return jnp.concatenate(
        [jnp.where(lane < HD, values, none), jnp.where(lane < HD, none, values)], axis=0
    )


def unstack_pair(values):
    rows = values.shape[0] // 2
    lane = lax.broadcasted_iota(jnp.int32, (rows, PAIR), 1)
    return jnp.where(lane < HD, values[:rows], values[rows:])


class Ring:
    def __init__(self, spot, blocks, recv, send):
        self.spot, self.blocks, self.recv, self.send = spot, blocks, recv, send
        self.used = 0
        self.sent, self.sent_mid = [], []

    def copy(self, slot, to):
        self.used += 1
        return remote(
            self.blocks.at[slot],
            self.blocks.at[slot],
            self.send.at[self.used - 1],
            self.recv.at[slot],
            to,
        )

    def arrived(self, slot):
        remote(
            self.blocks.at[slot],
            self.blocks.at[slot],
            self.send.at[0],
            self.recv.at[slot],
            self.spot.column,
        ).wait_recv()

    def start(self):
        spot = self.spot
        own = self.copy(spot.k, spot.inner)
        side = self.copy(spot.k, spot.column)
        back = self.copy(spot.k, spot.outer)
        own.start()

        @pl.when(spot.mid == 1)
        def _():
            back.start()

        side.start()
        self.sent += [own, side]
        self.sent_mid += [back]

    def step(self, number):
        spot = self.spot
        plane = spot.plane(number)
        if number > 0:
            slot = 2 * plane + spot.x
            self.arrived(slot)
            along = self.copy(slot, spot.inner if number == 1 else spot.outer)

            @pl.when(spot.mid == 1)
            def _():
                along.start()

            side = self.copy(slot, spot.column)
            side.start()
            self.sent += [side]
            self.sent_mid += [along]
        return plane

    def other(self, plane):
        self.arrived(2 * plane + 1 - self.spot.x)

    def drain(self):
        for copy in self.sent:
            copy.wait_send()

        @pl.when(self.spot.mid == 1)
        def _():
            for copy in self.sent_mid:
                copy.wait_send()


def forward_kernel(
    tok, pack, cosr, sinr, kb, qb, cot, wq, wk, wv, wo, sg, su, eg, eu,
    q_out, kv_out, mixed_out, lse_out, second_out, mixer_out, normed_out, pack_out,
    wfull_out, sg_out, su_out, eg_out, eu_out, cot_out,
    wbuf, kv, packs, top, low, acc, sem, kv_recv, kv_send,
):
    spot = Spot(4)
    sems = Sems(sem)
    rows = tok.shape[0]
    width = tok.shape[1]
    pairs = width // PAIR
    greet((spot.core, spot.across, spot.corner, spot.column, spot.inner), (spot.mid, spot.outer))
    params = Spread(spot, lambda w: pack, lambda w: packs.at[w], sems)
    key_w = Gather(spot, wk, wbuf.at[1], sems)
    value_w = Gather(spot, wv, wbuf.at[2], sems)
    query_w = Gather(spot, wq, wbuf.at[0], sems)
    inputs = tok[...].astype(F32)
    scale = lax.rsqrt(jnp.mean(inputs * inputs, axis=-1, keepdims=True) + EPS)
    scaled = inputs * scale
    params.finish()
    pack_all = packs[0] + packs[1] + packs[2] + packs[3]
    pack_out[...] = pack_all
    normed = (scaled * pack_all[0:1]).astype(BF)
    normed_out[...] = normed
    cosine, sine = cosr[...], sinr[...]
    key_w.forward()
    value_w.forward()
    key_w.finish()
    kv[spot.k, :, 0:width] = turn(nn(normed, wbuf[1]), cosine, sine).astype(BF)
    value_w.finish()
    kv[spot.k, :, width : 2 * width] = nn(normed, wbuf[2]).astype(BF)
    ring = Ring(spot, kv, kv_recv, kv_send)
    ring.start()
    query_w.forward()
    out_w = Gather(spot, wo, wbuf.at[3], sems)
    sg_w = Spread(
        spot,
        lambda w: sg.at[:, pl.ds(pl.multiple_of(512 * w, 512), 512)],
        lambda w: sg_out.at[pl.ds(pl.multiple_of(192 * w, 64), 192)],
        sems,
    )
    su_w = Spread(
        spot,
        lambda w: su.at[:, pl.ds(pl.multiple_of(512 * w, 512), 512)],
        lambda w: su_out.at[pl.ds(pl.multiple_of(192 * w, 64), 192)],
        sems,
    )
    cot_w = Spread(spot, lambda w: cot, lambda w: cot_out.at[w], sems)
    gate_w = Gather(spot, eg, eg_out, sems)
    up_w = Gather(spot, eu, eu_out, sems)
    query_w.finish()
    query = turn(nn(normed, wbuf[0]), cosine, sine).astype(BF) * jnp.asarray(HD**-0.5, BF)
    for j in range(pairs):
        q_out[j] = stack_pair(query[:, PAIR * j : PAIR * (j + 1)])
    top[...] = jnp.full_like(top, MASKED)
    low[...] = jnp.zeros_like(low)
    acc[...] = jnp.zeros_like(acc)
    q_block = qb[...]

    def chunk(plane):
        k_block = kb[:, pl.ds(pl.multiple_of(2 * rows * plane, 2 * rows), 2 * rows)]
        allowed = k_block <= q_block

        def one_pair(j, carry):
            lane = pl.multiple_of(PAIR * j, PAIR)
            key = kv[pl.ds(2 * plane, 2), :, pl.ds(lane, PAIR)].reshape(2 * rows, PAIR)
            value = kv[pl.ds(2 * plane, 2), :, pl.ds(width + lane, PAIR)].reshape(2 * rows, PAIR)
            scores = jnp.where(allowed, nt(q_out[j], key), MASKED)
            old = top[j]
            new = jnp.maximum(old, jnp.max(scores, axis=1, keepdims=True))
            raised = jnp.where(allowed, jnp.exp(scores - new[:, 0:1]), 0.0)
            factor = jnp.exp(old - new)
            top[j] = new
            low[j] = low[j] * factor + jnp.sum(raised, axis=1, keepdims=True)
            acc[j] = acc[j] * factor + nn(raised.astype(BF), value)
            return carry

        lax.fori_loop(0, pairs, one_pair, 0)

    for number in range(4):
        plane = ring.step(number)
        ring.other(plane)
        chunk(plane)
    saves = [pltpu.make_async_copy(kv, kv_out, sems.new())]
    saves[0].start()
    out_w.forward()
    for j in range(pairs):
        mixed_out[:, PAIR * j : PAIR * (j + 1)] = unstack_pair(acc[j] / low[j])
        lse_out[j] = top[j] + jnp.log(low[j])
    out_w.finish()
    saves.append(pltpu.make_async_copy(wbuf, wfull_out, sems.new()))
    saves[1].start()
    second = inputs + nn(mixed_out[...].astype(BF), wbuf[3])
    second_out[...] = second
    scale_two = lax.rsqrt(jnp.mean(second * second, axis=-1, keepdims=True) + EPS)
    mixer_out[...] = (second * scale_two * pack_all[1:2]).astype(BF)
    gate_w.forward()
    up_w.forward()
    for part in (sg_w, su_w, cot_w, gate_w, up_w):
        part.finish()
    for part in (params, key_w, value_w, query_w, out_w, sg_w, su_w, cot_w, gate_w, up_w, ring):
        part.drain()
    for copy in saves:
        copy.wait()


def run_forward(tok, pack, cosr, sinr, kb, qb, cot, wq, wk, wv, wo, sg, su, eg, eu):
    rows, width = tok.shape
    pairs = width // PAIR
    ranks = 8
    any_, vm = pl.BlockSpec(memory_space=pl.ANY), pl.BlockSpec(memory_space=VMEM)
    shape = jax.ShapeDtypeStruct
    hidden = eg.shape[1]
    part = sg.shape[1] // 4
    return pl.pallas_call(
        forward_kernel,
        out_shape=(
            shape((pairs, 2 * rows, PAIR), BF),
            shape((ranks, rows, 2 * width), BF),
            shape((rows, width), F32),
            shape((pairs, 2 * rows, PAIR), F32),
            shape((rows, width), F32),
            shape((rows, width), BF),
            shape((rows, width), BF),
            shape(pack.shape, F32),
            shape((4, width, width), BF),
            shape((width, part), BF),
            shape((width, part), BF),
            shape((width, hidden), BF),
            shape((width, hidden), BF),
            shape((4, rows, width), BF),
        ),
        in_specs=[vm] * 6 + [any_] * 9,
        out_specs=(vm, any_, vm, vm, vm, vm, vm, vm, any_, any_, any_, any_, any_, any_),
        scratch_shapes=[
            VMEM((4, width, width), BF),
            VMEM((ranks, rows, 2 * width), BF),
            VMEM((4,) + pack.shape, F32),
            VMEM((pairs, 2 * rows, PAIR), F32),
            VMEM((pairs, 2 * rows, PAIR), F32),
            VMEM((pairs, 2 * rows, PAIR), F32),
            pltpu.SemaphoreType.DMA((96,)),
            pltpu.SemaphoreType.DMA((ranks,)),
            pltpu.SemaphoreType.DMA((16,)),
        ],
        compiler_params=pltpu.CompilerParams(
            collective_id=1, has_side_effects=True, vmem_limit_bytes=48 * 2**20
        ),
    )(tok, pack, cosr, sinr, kb, qb, cot, wq, wk, wv, wo, sg, su, eg, eu)


def angles_of(block_deal, rows_dev):
    here = places(lax.axis_index("ctx") * rows_dev, rows_dev, block_deal, rows_dev)
    half_size = HD // 2
    frequency = 10000.0 ** (-jnp.arange(half_size, dtype=F32) / half_size)
    angles = here.astype(F32)[:, None] * frequency[None, :]
    cosine, sine = jnp.cos(angles), jnp.sin(angles)
    cosr = jnp.concatenate([cosine] * 4, axis=1)
    sinr = jnp.concatenate([-sine, sine, -sine, sine], axis=1)
    return here, cosr, sinr


def pack_params(gain_one, gain_two, router):
    width = 4 * gain_one.shape[0]
    shard = jnp.concatenate(
        [gain_one[None], gain_two[None], router.T, jnp.zeros((6, gain_one.shape[0]), BF)], axis=0
    ).astype(F32)
    start = lax.axis_index("wt") * gain_one.shape[0]
    return lax.dynamic_update_slice(jnp.zeros((16, width), F32), shard, (0, start))


def swish(values):
    sigmoid = 1.0 / (1.0 + jnp.exp(-values))
    return values * sigmoid, sigmoid * (1.0 + values * (1.0 - sigmoid))


class Exchange:
    def __init__(self, spot, out, back, send, recv):
        self.spot, self.out, self.back = spot, out, back
        self.send, self.recv, self.ranks = send, recv, out.shape[0]
        self.copies = []

    def start(self):
        spot = self.spot
        for offset in range(1, self.ranks):
            peer = lax.rem(spot.k + offset, self.ranks)
            self.copies.append(
                remote(
                    self.out.at[peer],
                    self.back.at[spot.k],
                    self.send.at[offset],
                    self.recv.at[spot.k],
                    (peer, spot.w),
                )
            )
            self.copies[-1].start()
        self.back[spot.k] = self.out[spot.k]

    def finish(self):
        spot = self.spot
        for offset in range(1, self.ranks):
            peer = lax.rem(spot.k + offset, self.ranks)
            remote(
                self.out.at[peer],
                self.back.at[peer],
                self.send.at[offset],
                self.recv.at[peer],
                (peer, spot.w),
            ).wait_recv()

    def drain(self):
        for copy in self.copies:
            copy.wait_send()


def fold_rows(values, ref):
    ranks = ref.shape[0]
    slots = values.shape[0] // ranks
    for e in range(ranks):
        part = values[slots * e : slots * (e + 1)]
        tiles = [part[:, 128 * t : 128 * (t + 1)] for t in range(values.shape[1] // 128)]
        ref[e] = jnp.concatenate(tiles, axis=0).astype(BF)


def unfold_rows(ref, slots):
    parts = []
    for e in range(ref.shape[0]):
        part = ref[e].astype(F32)
        tiles = [part[slots * t : slots * (t + 1)] for t in range(part.shape[0] // slots)]
        parts.append(jnp.concatenate(tiles, axis=1))
    return jnp.concatenate(parts, axis=0).astype(BF)


def split_three(values):
    high = values.astype(BF)
    rest = values - high.astype(F32)
    middle = rest.astype(BF)
    return high, middle, (rest - middle.astype(F32)).astype(BF)


def slot_maps(e_row, e_col, o_row, o_col, slots, experts):
    pairs = e_row.shape[1]
    down = lax.broadcasted_iota(jnp.int32, (pairs, pairs), 0)
    along = lax.broadcasted_iota(jnp.int32, (pairs, pairs), 1)
    turn_row = jnp.sum(jnp.where(o_col == along, down.astype(F32), 0.0), axis=0, keepdims=True)
    turn_col = jnp.sum(jnp.where(o_row == down, along.astype(F32), 0.0), axis=1, keepdims=True)
    same = e_col == e_row
    slot_row = jnp.sum(
        jnp.where(same & (turn_col < turn_row), 1.0, 0.0), axis=0, keepdims=True
    ).astype(jnp.int32)
    slot_col = jnp.sum(
        jnp.where(same & (turn_row < turn_col), 1.0, 0.0), axis=1, keepdims=True
    ).astype(jnp.int32)
    target_row = jnp.where(slot_row < slots, e_row * slots + slot_row, -1)
    target_col = jnp.where(slot_col < slots, e_col * slots + slot_col, -1)
    total = experts * slots
    place = lax.broadcasted_iota(jnp.int32, (total, pairs), 0)
    to_slots = jnp.where(place == target_row, 1.0, 0.0).astype(BF)
    place = lax.broadcasted_iota(jnp.int32, (pairs, total), 1)
    to_pairs = jnp.where(place == target_col, 1.0, 0.0).astype(BF)
    return to_slots, to_pairs


def experts_kernel(
    second_ref, mixer_ref, pack_ref, cot_ref, route_ref, e_row, e_col, o_row, o_col,
    sd_ref, sg_ref, su_ref, cot4_ref, eg_ref, eu_ref, ed_ref,
    result_out, grad_second_out, pack_grad_out, dsg_out, dsu_out, dsd_out,
    dg_out, du_out, dd_out,
    wg, wu, wd, m4, sh_send, sh_recv, gm_send, gm_recv,
    xs, xr, gs, gr, os, orr, bs, br, x_s, g_s, sum_s,
    gate_s, up_s, hid_s, dgate_s, dup_s, sem, a2a_send, a2a_recv,
):
    spot = Spot(4)
    sems = Sems(sem)
    rows, width = mixer_ref.shape
    ranks = xs.shape[0]
    slots = xs.shape[1] * 128 // width
    hidden = wg.shape[1]
    loads = [
        pltpu.make_async_copy(eg_ref, wg, sems.new()),
        pltpu.make_async_copy(eu_ref, wu, sems.new()),
    ]
    for copy in loads:
        copy.start()
    others = [(lax.rem(spot.k + o, ranks), spot.w) for o in range(1, ranks)]
    greet([spot.core, spot.across, spot.corner] + others)
    mixer = mixer_ref[...]
    to_slots, to_pairs = slot_maps(
        e_row[...], e_col[...], o_row[...], o_col[...], slots, ranks
    )
    fold_rows(nn(to_slots[:, :rows] + to_slots[:, rows:], mixer), xs)
    rows_out = Exchange(spot, xs, xr, a2a_send.at[0], a2a_recv.at[0])
    rows_out.start()
    mixers = Spread(spot, lambda w: mixer_ref, lambda w: m4.at[w], sems)
    down_w = Gather(spot, ed_ref, wd, sems)
    pack = pack_ref[...]
    router = pack[2:16].astype(BF)
    router = jnp.concatenate([router, jnp.zeros((2, width), BF)], axis=0)
    logits = nt(mixer, router)
    lane = lax.broadcasted_iota(jnp.int32, logits.shape, 1)
    matches = [lane == route_ref[:, j : j + 1] for j in range(2)]
    chosen = [jnp.sum(jnp.where(m, logits, 0.0), axis=1, keepdims=True) for m in matches]
    largest = jnp.maximum(chosen[0], chosen[1])
    raised = [jnp.exp(c - largest) for c in chosen]
    gates = [r / (raised[0] + raised[1]) for r in raised]
    grad = cot_ref[...].astype(F32)
    pair_grad = jnp.concatenate([(g * grad).astype(BF) for g in gates], axis=0)
    fold_rows(nn(to_slots, pair_grad), gs)
    grads_out = Exchange(spot, gs, gr, a2a_send.at[1], a2a_recv.at[1])
    grads_out.start()

    mixers.finish()
    rows_all = m4[...].reshape(4 * rows, width)
    grad_all = cot4_ref[...].reshape(4 * rows, width)
    gate_part, up_part = nn(rows_all, sg_ref[...]), nn(rows_all, su_ref[...])
    act, slope = swish(gate_part)
    shared_hidden = (act * up_part).astype(BF)
    sh_send[...] = nn(shared_hidden, sd_ref[...]).astype(BF).reshape(4, rows, width)
    shared_out = Spread(spot, lambda w: sh_send.at[w], lambda w: sh_recv.at[w], sems)
    hid_grad = nt(grad_all, sd_ref[...])
    grad_gate = (hid_grad * up_part * slope).astype(BF)
    grad_up = (hid_grad * act).astype(BF)
    back = nt(grad_gate, sg_ref[...]) + nt(grad_up, su_ref[...])
    gm_send[...] = back.astype(BF).reshape(4, rows, width)
    shared_back = Spread(spot, lambda w: gm_send.at[w], lambda w: gm_recv.at[w], sems)
    down_w.forward()
    for copy in loads:
        copy.wait()

    rows_out.finish()
    x_s[...] = unfold_rows(xr, slots)
    block = 512

    def parts(i):
        return pl.ds(pl.multiple_of(block * i, block), block)

    def up_step(i, carry):
        at = parts(i)
        gate = nn(x_s[...], wg[:, at])
        up = nn(x_s[...], wu[:, at])
        act, slope = swish(gate)
        hid_s[:, at] = (act * up).astype(BF)
        gate_s[:, at] = up * slope
        up_s[:, at] = act
        return carry

    lax.fori_loop(0, hidden // block, up_step, 0)
    down_w.finish()
    sum_s[...] = nt(hid_s[...], wd[...])
    fold_rows(sum_s[...], os)
    outs = Exchange(spot, os, orr, a2a_send.at[2], a2a_recv.at[2])
    outs.start()
    grads_out.finish()
    g_s[...] = unfold_rows(gr, slots)

    def down_step(i, carry):
        at = parts(i)
        grad_hidden = nn(g_s[...], wd[:, at])
        dgate_s[:, at] = (grad_hidden * gate_s[:, at]).astype(BF)
        dup_s[:, at] = (grad_hidden * up_s[:, at]).astype(BF)
        return carry

    lax.fori_loop(0, hidden // block, down_step, 0)
    sum_s[...] = nt(dgate_s[...], wg[...]) + nt(dup_s[...], wu[...])
    fold_rows(sum_s[...], bs)
    backs = Exchange(spot, bs, br, a2a_send.at[3], a2a_recv.at[3])
    backs.start()

    down_w.drain()

    def grad_step(i, carry):
        at = parts(i)
        wg[:, at] = tn(x_s[...], dgate_s[:, at]).astype(BF)
        wu[:, at] = tn(x_s[...], dup_s[:, at]).astype(BF)
        wd[:, at] = tn(g_s[...], hid_s[:, at]).astype(BF)
        return carry

    lax.fori_loop(0, hidden // block, grad_step, 0)
    saves = [
        pltpu.make_async_copy(src, dst, sems.new())
        for src, dst in ((wg, dg_out), (wu, du_out), (wd, dd_out))
    ]
    for copy in saves:
        copy.start()
    dsg_out[...] = tn(rows_all, grad_gate).astype(BF)
    dsu_out[...] = tn(rows_all, grad_up).astype(BF)
    dsd_out[...] = tn(shared_hidden, grad_all).astype(BF)

    second = second_ref[...]
    shared_out.finish()
    total = second
    for w in range(4):
        total = total + sh_recv[w].astype(F32)
    outs.finish()
    pair_out = nn(to_pairs, unfold_rows(orr, slots))
    pair_out = [pair_out[:rows], pair_out[rows:]]
    result_out[...] = (total + gates[0] * pair_out[0] + gates[1] * pair_out[1]).astype(BF)
    grad_gates = [jnp.sum(grad * p, axis=1, keepdims=True) for p in pair_out]
    inner = gates[0] * grad_gates[0] + gates[1] * grad_gates[1]
    grad_logits = jnp.zeros_like(logits)
    for j in range(2):
        grad_logits += jnp.where(matches[j], gates[j] * (grad_gates[j] - inner), 0.0)
    pieces = split_three(grad_logits)
    router_grad = sum(tn(piece, mixer) for piece in pieces)
    grad_mixer = sum(nn(piece, router) for piece in pieces)
    shared_back.finish()
    for w in range(4):
        grad_mixer = grad_mixer + gm_recv[w].astype(F32)
    backs.finish()
    grad_mixer = grad_mixer + nn(to_pairs[:rows] + to_pairs[rows:], unfold_rows(br, slots))
    scale = lax.rsqrt(jnp.mean(second * second, axis=-1, keepdims=True) + EPS)
    weighted = grad_mixer * pack[1:2]
    mean = jnp.mean(weighted * second, axis=-1, keepdims=True)
    grad_second_out[...] = grad + scale * weighted - second * (scale * scale * scale * mean)
    gain_grad = jnp.sum(grad_mixer * second * scale, axis=0, keepdims=True)
    pack_grad_out[...] = jnp.concatenate(
        [jnp.zeros_like(gain_grad), gain_grad, router_grad[:14]], axis=0
    )
    for part in (rows_out, grads_out, outs, backs, mixers, shared_out, shared_back):
        part.drain()
    for copy in saves:
        copy.wait()


def run_experts(
    second, mixer, pack, cot, route, e_row, e_col, o_row, o_col, sd, sg, su, cot4, eg, eu, ed
):
    rows, width = mixer.shape
    ranks, slots = 8, 40
    hidden = eg.shape[1]
    part = sg.shape[1]
    total = ranks * slots
    folded = (ranks, slots * width // 128, 128)
    any_, vm = pl.BlockSpec(memory_space=pl.ANY), pl.BlockSpec(memory_space=VMEM)
    shape = jax.ShapeDtypeStruct
    return pl.pallas_call(
        experts_kernel,
        out_shape=(
            shape((rows, width), BF),
            shape((rows, width), F32),
            shape(pack.shape, F32),
            shape((width, part), BF),
            shape((width, part), BF),
            shape((part, width), BF),
            shape((width, hidden), BF),
            shape((width, hidden), BF),
            shape((width, hidden), BF),
        ),
        in_specs=[vm] * 13 + [any_] * 3,
        out_specs=tuple([vm] * 6 + [any_] * 3),
        scratch_shapes=[
            VMEM((width, hidden), BF),
            VMEM((width, hidden), BF),
            VMEM((width, hidden), BF),
            VMEM((4, rows, width), BF),
            VMEM((4, rows, width), BF),
            VMEM((4, rows, width), BF),
            VMEM((4, rows, width), BF),
            VMEM((4, rows, width), BF),
            VMEM(folded, BF),
            VMEM(folded, BF),
            VMEM(folded, BF),
            VMEM(folded, BF),
            VMEM(folded, BF),
            VMEM(folded, BF),
            VMEM(folded, BF),
            VMEM(folded, BF),
            VMEM((total, width), BF),
            VMEM((total, width), BF),
            VMEM((total, width), F32),
            VMEM((total, hidden), F32),
            VMEM((total, hidden), F32),
            VMEM((total, hidden), BF),
            VMEM((total, hidden), BF),
            VMEM((total, hidden), BF),
            pltpu.SemaphoreType.DMA((48,)),
            pltpu.SemaphoreType.DMA((4, ranks)),
            pltpu.SemaphoreType.DMA((4, ranks)),
        ],
        compiler_params=pltpu.CompilerParams(
            collective_id=2, has_side_effects=True, vmem_limit_bytes=56 * 2**20
        ),
    )(second, mixer, pack, cot, route, e_row, e_col, o_row, o_col, sd, sg, su, cot4, eg, eu, ed)


def contract_product(left, right, left_dim, right_dim):
    return lax.dot_general(
        left, right, (((left_dim,), (right_dim,)), ((), ())), preferred_element_type=jnp.float32
    )


def contract_exact(left, right, left_dim, right_dim):
    return lax.dot_general(
        left,
        right,
        (((left_dim,), (right_dim,)), ((), ())),
        precision=HIGH,
        preferred_element_type=jnp.float32,
    )


def rms_norm(values, gain):
    norm_scale = lax.rsqrt(jnp.mean(values * values, axis=-1, keepdims=True) + EPS)
    return (values * norm_scale * gain, norm_scale)


def rms_back(values, norm_scale, gain, upstream):
    weighted = upstream * gain
    inner_mean = jnp.mean(weighted * values, axis=-1, keepdims=True)
    through = norm_scale * weighted - values * norm_scale * norm_scale * norm_scale * inner_mean
    return (through, jnp.sum(upstream * values * norm_scale, axis=0))


def silu_parts(gate_part):
    sigmoid = jax.nn.sigmoid(gate_part)
    return (gate_part * sigmoid, sigmoid * (1.0 + gate_part * (1.0 - sigmoid)))


def rotate(values, place, sign):
    half_size = HD // 2
    frequency = 10000.0 ** (-jnp.arange(half_size, dtype=jnp.float32) / half_size)
    angles = place.astype(jnp.float32)[:, None] * frequency[None, :]
    cosine = jnp.cos(angles)[:, None, :]
    sine_part = sign * jnp.sin(angles)[:, None, :]
    shaped = values.reshape(values.shape[0], values.shape[1] // HD, 2, half_size)
    first_half = shaped[:, :, 0, :]
    second_half = shaped[:, :, 1, :]
    turned = jnp.stack(
        [
            first_half * cosine - second_half * sine_part,
            second_half * cosine + first_half * sine_part,
        ],
        axis=2,
    )
    return turned.reshape(values.shape)


def places(first_row, row_count, block_deal, rows_dev):
    row_index = first_row + jnp.arange(row_count, dtype=jnp.int32)
    owner_rank = row_index // rows_dev
    inner_row = row_index % rows_dev
    ranks = block_deal.shape[0]
    matches = owner_rank[:, None] == jnp.arange(ranks, dtype=jnp.int32)[None, :]
    paired = jnp.sum(jnp.where(matches, block_deal[None, :], 0), axis=1)
    piece_size = rows_dev // 2
    unit_index = jnp.where(inner_row < piece_size, paired, 2 * ranks - 1 - paired)
    return unit_index * piece_size + inner_row % piece_size


def score_block(query_side, key_rows, key_place):
    query3, query_block = query_side
    key3 = key_rows.reshape(key_rows.shape[0], -1, HD)
    raw_scores = jnp.einsum("qhd,khd->hqk", query3, key3, preferred_element_type=jnp.float32)
    allowed = (key_place // BLK)[None, None, :] <= query_block[None, :, None]
    return (jnp.where(allowed, raw_scores * HD ** (-0.5), MASKED), allowed)


def absorb(running, key_rows, value_rows, key_place, query_side):
    largest, denom, accum = running
    scores, allowed = score_block(query_side, key_rows, key_place)
    new_largest = jnp.maximum(largest, jnp.max(scores, axis=2))
    factor = jnp.exp(largest - new_largest)
    raised = jnp.where(allowed, jnp.exp(scores - new_largest[:, :, None]), 0.0)
    denom = denom * factor + jnp.sum(raised, axis=2)
    value3 = value_rows.reshape(value_rows.shape[0], -1, HD)
    accum = accum * factor.T[:, :, None] + jnp.einsum(
        "hqk,khd->qhd", raised.astype(jnp.bfloat16), value3, preferred_element_type=jnp.float32
    )
    return (new_largest, denom, accum)


def fold_keys(running, key_piece, query_side, block_deal, rows_dev):
    key_all, value_all = key_piece
    row_count = key_all.shape[0]
    block_size = KEY_ROWS

    def key_step(current, offset):
        key_rows = lax.dynamic_slice_in_dim(key_all, offset, block_size, 0)
        value_rows = lax.dynamic_slice_in_dim(value_all, offset, block_size, 0)
        key_place = places(offset, block_size, block_deal, rows_dev)
        return (absorb(current, key_rows, value_rows, key_place, query_side), None)

    offsets = jnp.arange(row_count // block_size, dtype=jnp.int32) * block_size
    running, unused = lax.scan(key_step, running, offsets)
    return running


def differentiate(query_side, log_total, delta, grad_out3, key_rows, value_rows, key_place):
    scores, allowed = score_block(query_side, key_rows, key_place)
    probs_full = jnp.where(allowed, jnp.exp(scores - log_total[:, :, None]), 0.0)
    value3 = value_rows.reshape(value_rows.shape[0], -1, HD)
    grad_probs = jnp.einsum("qhd,khd->hqk", grad_out3, value3, preferred_element_type=jnp.float32)
    grad_scores = (probs_full * (grad_probs - delta[:, :, None]) * HD ** (-0.5)).astype(
        jnp.bfloat16
    )
    return (probs_full, grad_scores)


def assign_slots(route, order, experts, capacity):
    pair_count = order.shape[0]
    expert_ids = route.reshape(pair_count)
    ordered = expert_ids[order]
    onehot = (ordered[:, None] == jnp.arange(experts, dtype=jnp.int32)[None, :]).astype(jnp.int32)
    before = jnp.cumsum(onehot, axis=0) - onehot
    slot_turn = jnp.sum(before * onehot, axis=1)
    slot_index = jnp.zeros((pair_count,), jnp.int32).at[order].set(slot_turn)
    kept_pairs = slot_index < capacity
    target = jnp.where(kept_pairs, expert_ids * capacity + slot_index, experts * capacity)
    slot_table = (
        jnp.full((experts * capacity,), pair_count, jnp.int32)
        .at[target]
        .set(jnp.arange(pair_count, dtype=jnp.int32), mode="drop")
    )
    return (target, kept_pairs, slot_table)


def body(
    tokens,
    cotangent,
    gain_attention,
    query_weight,
    key_weight,
    value_weight,
    output_weight,
    gain_mixer,
    router_weight,
    shared_gate,
    shared_up,
    shared_down,
    expert_gate,
    expert_up,
    expert_down,
    routes,
    slot_order,
    block_deal,
):
    rows_dev = tokens.shape[1]
    width = tokens.shape[2]
    ranks = lax.axis_size("ctx")
    (
        gain_one,
        query_full,
        key_full,
        value_full,
        output_full,
        gain_two,
        router_full,
        sgate_full,
        sup_full,
        sdown_full,
        expert_gate_whole,
        expert_up_whole,
        edown_full,
    ) = (
        lax.all_gather(gain_attention, "wt", axis=0, tiled=True),
        lax.all_gather(query_weight, "wt", axis=0, tiled=True),
        lax.all_gather(key_weight, "wt", axis=0, tiled=True),
        lax.all_gather(value_weight, "wt", axis=0, tiled=True),
        lax.all_gather(output_weight, "wt", axis=0, tiled=True),
        lax.all_gather(gain_mixer, "wt", axis=0, tiled=True),
        lax.all_gather(router_weight, "wt", axis=0, tiled=True),
        lax.all_gather(shared_gate, "wt", axis=0, tiled=True),
        lax.all_gather(shared_up, "wt", axis=0, tiled=True),
        lax.all_gather(shared_down, "wt", axis=0, tiled=True),
        lax.all_gather(expert_gate, "wt", axis=0, tiled=True),
        lax.all_gather(expert_up, "wt", axis=0, tiled=True),
        lax.all_gather(expert_down, "wt", axis=0, tiled=True),
    )
    gain_first = gain_one.astype(jnp.float32)
    gain_second = gain_two.astype(jnp.float32)
    heads = width // HD
    inputs = tokens[0].astype(jnp.float32)
    here = places(lax.axis_index("ctx") * rows_dev, rows_dev, block_deal, rows_dev)
    query_side_block = here // BLK
    normed_f, scale_one = rms_norm(inputs, gain_first)
    normed = normed_f.astype(jnp.bfloat16)
    query_rot = rotate(
        jnp.dot(normed, query_full, preferred_element_type=jnp.float32), here, 1.0
    ).astype(jnp.bfloat16)
    key_rot = rotate(
        jnp.dot(normed, key_full, preferred_element_type=jnp.float32), here, 1.0
    ).astype(jnp.bfloat16)
    value_low = jnp.dot(normed, value_full, preferred_element_type=jnp.float32).astype(jnp.bfloat16)
    query3 = query_rot.reshape(rows_dev, heads, HD)
    query_side = (query3, query_side_block)
    start_state = (
        jnp.full((heads, rows_dev), MASKED, jnp.float32),
        jnp.zeros((heads, rows_dev), jnp.float32),
        jnp.zeros((rows_dev, heads, HD), jnp.float32),
    )
    largest, denom, accum = fold_keys(
        start_state,
        (
            lax.all_gather(key_rot, "ctx", axis=0, tiled=True),
            lax.all_gather(value_low, "ctx", axis=0, tiled=True),
        ),
        query_side,
        block_deal,
        rows_dev,
    )
    mixed3 = accum / denom.T[:, :, None]
    log_total = largest + jnp.log(denom)
    mixed_low = mixed3.reshape(rows_dev, width).astype(jnp.bfloat16)
    second = inputs + jnp.dot(mixed_low, output_full, preferred_element_type=jnp.float32)
    mixer_f, scale_two = rms_norm(second, gain_second)
    mixer = mixer_f.astype(jnp.bfloat16)
    experts = router_full.shape[1]
    logits = jnp.dot(mixer, router_full, preferred_element_type=jnp.float32)
    route = routes[0]
    top_count = route.shape[1]
    pair_count = rows_dev * top_count
    capacity = (5 * pair_count + 4 * experts - 1) // (4 * experts)
    split_count = ranks // experts
    expert_match = route[:, :, None] == jnp.arange(experts, dtype=jnp.int32)[None, None, :]
    chosen = jnp.sum(jnp.where(expert_match, logits[:, None, :], 0.0), axis=2)
    gates = jax.nn.softmax(chosen, axis=1)
    target, kept_pairs, slot_table = assign_slots(route, slot_order[0, 0], experts, capacity)
    valid = slot_table < pair_count
    pair_pick = jnp.minimum(slot_table, pair_count - 1)
    target_pick = jnp.minimum(target, experts * capacity - 1)
    send_rows = jnp.where(
        valid[:, None], mixer[pair_pick // top_count], jnp.zeros((), jnp.bfloat16)
    )
    send_rows = jnp.broadcast_to(
        send_rows.reshape(experts, 1, capacity, width), (experts, split_count, capacity, width)
    ).reshape(ranks, capacity, width)
    received = lax.all_to_all(send_rows, "ctx", split_axis=0, concat_axis=0, tiled=True)
    slot_count = received.shape[1]
    flattened_input = received.reshape(ranks * slot_count, width)
    gate_part = jnp.dot(flattened_input, expert_gate_whole, preferred_element_type=jnp.float32)
    up_projection_part = jnp.dot(
        flattened_input, expert_up_whole, preferred_element_type=jnp.float32
    )
    activated, unused = silu_parts(gate_part)
    hidden = (activated * up_projection_part).astype(jnp.bfloat16)
    partial_value = contract_product(hidden, edown_full, 1, 1).reshape(ranks, slot_count, width)
    back = lax.all_to_all(
        partial_value.astype(jnp.bfloat16), "ctx", split_axis=0, concat_axis=0, tiled=True
    ).astype(partial_value.dtype)
    expert_gate_part = gate_part.reshape(ranks, slot_count, -1)
    expert_up_part = up_projection_part.reshape(ranks, slot_count, -1)
    combined = jnp.sum(back.reshape(experts, split_count, capacity, width), axis=1).reshape(
        experts * capacity, width
    )
    pair_out = jnp.where(kept_pairs[:, None], combined[target_pick], 0.0).reshape(
        rows_dev, top_count, width
    )
    mixture = jnp.sum(gates[:, :, None] * pair_out, axis=1)
    sgate_part = jnp.dot(mixer, sgate_full, preferred_element_type=jnp.float32)
    sup_part = jnp.dot(mixer, sup_full, preferred_element_type=jnp.float32)
    shared_act, shared_slope = silu_parts(sgate_part)
    shared_hidden = (shared_act * sup_part).astype(jnp.bfloat16)
    shared_out = jnp.dot(shared_hidden, sdown_full, preferred_element_type=jnp.float32)
    result = (second + mixture + shared_out).astype(jnp.bfloat16)
    grad_final = cotangent[0].astype(jnp.float32)
    grad_low = grad_final.astype(jnp.bfloat16)
    sdown_grad = contract_product(shared_hidden, grad_low, 0, 0)
    grad_shared_hidden = contract_product(grad_low, sdown_full, 1, 1)
    grad_sgate = (grad_shared_hidden * sup_part * shared_slope).astype(jnp.bfloat16)
    grad_sup = (grad_shared_hidden * shared_act).astype(jnp.bfloat16)
    sgate_grad = contract_product(mixer, grad_sgate, 0, 0)
    sup_grad = contract_product(mixer, grad_sup, 0, 0)
    grad_mixer = contract_product(grad_sgate, sgate_full, 1, 1) + contract_product(
        grad_sup, sup_full, 1, 1
    )
    pair_grad = (
        (gates[:, :, None] * grad_final[:, None, :]).reshape(pair_count, width).astype(jnp.bfloat16)
    )
    grad_gates = jnp.sum(grad_final[:, None, :] * pair_out, axis=2)
    send_grad = jnp.where(valid[:, None], pair_grad[pair_pick], jnp.zeros((), jnp.bfloat16))
    send_grad = jnp.broadcast_to(
        send_grad.reshape(experts, 1, capacity, width), (experts, split_count, capacity, width)
    ).reshape(ranks, capacity, width)
    recv_grad = lax.all_to_all(send_grad, "ctx", split_axis=0, concat_axis=0, tiled=True)
    flattened_input = received.reshape(ranks * capacity, width)
    flat_grad = recv_grad.reshape(ranks * capacity, width)
    gate_flat = expert_gate_part.reshape(ranks * capacity, -1)
    up_flat = expert_up_part.reshape(ranks * capacity, -1)
    expert_activation, expert_slope = silu_parts(gate_flat)
    expert_hidden = (expert_activation * up_flat).astype(jnp.bfloat16)
    edown_grad = contract_product(flat_grad, expert_hidden, 0, 0)
    expert_hidden_grad = jnp.dot(flat_grad, edown_full, preferred_element_type=jnp.float32)
    expert_gate_grad_rows = (expert_hidden_grad * up_flat * expert_slope).astype(jnp.bfloat16)
    expert_up_grad_rows = (expert_hidden_grad * expert_activation).astype(jnp.bfloat16)
    egate_grad = contract_product(flattened_input, expert_gate_grad_rows, 0, 0)
    expert_up_weight_grad = contract_product(flattened_input, expert_up_grad_rows, 0, 0)
    input_back = (
        contract_product(expert_gate_grad_rows, expert_gate_whole, 1, 1)
        + contract_product(expert_up_grad_rows, expert_up_whole, 1, 1)
    ).reshape(ranks, capacity, width)
    back_grad = lax.all_to_all(
        input_back.astype(jnp.bfloat16), "ctx", split_axis=0, concat_axis=0, tiled=True
    ).astype(input_back.dtype)
    merged = jnp.sum(back_grad.reshape(experts, split_count, capacity, width), axis=1).reshape(
        experts * capacity, width
    )
    pair_back = jnp.where(kept_pairs[:, None], merged[target_pick], 0.0).reshape(
        rows_dev, top_count, width
    )
    grad_mixer = grad_mixer + jnp.sum(pair_back, axis=1)
    grad_chosen = gates * (grad_gates - jnp.sum(gates * grad_gates, axis=1, keepdims=True))
    grad_logits = jnp.sum(jnp.where(expert_match, grad_chosen[:, :, None], 0.0), axis=1)
    router_grad = contract_exact(mixer.astype(jnp.float32), grad_logits, 0, 0)
    grad_mixer = grad_mixer + contract_exact(grad_logits, router_full.astype(jnp.float32), 1, 1)
    through_two, gain_two_grad = rms_back(second, scale_two, gain_second, grad_mixer)
    grad_second = grad_final + through_two
    grad_attention = grad_second.astype(jnp.bfloat16)
    output_grad = contract_product(mixed_low, grad_attention, 0, 0)
    grad_mixed = contract_product(grad_attention, output_full, 1, 1).astype(jnp.bfloat16)
    grad_out3 = grad_mixed.reshape(rows_dev, heads, HD)
    delta = jnp.sum(grad_out3.astype(jnp.float32) * mixed3, axis=2).T
    all_keys, all_values = (
        lax.all_gather(key_rot, "ctx", axis=0, tiled=True),
        lax.all_gather(value_low, "ctx", axis=0, tiled=True),
    )
    total_rows = all_keys.shape[0]
    block_size = KEY_ROWS

    def query_step(grad_sum, offset):
        key_rows = lax.dynamic_slice_in_dim(all_keys, offset, block_size, 0)
        value_rows = lax.dynamic_slice_in_dim(all_values, offset, block_size, 0)
        key_place = places(offset, block_size, block_deal, rows_dev)
        unused, grad_scores = differentiate(
            query_side, log_total, delta, grad_out3, key_rows, value_rows, key_place
        )
        key3 = key_rows.reshape(block_size, heads, HD)
        return (
            grad_sum
            + jnp.einsum("hqk,khd->qhd", grad_scores, key3, preferred_element_type=jnp.float32),
            None,
        )

    offsets = jnp.arange(total_rows // block_size, dtype=jnp.int32) * block_size
    grad_query3, unused = lax.scan(
        query_step, jnp.zeros((rows_dev, heads, HD), jnp.float32), offsets
    )
    inner_size = KEY_ROWS

    def one_part(offset):
        key_rows = lax.dynamic_slice_in_dim(all_keys, offset, inner_size, 0)
        value_rows = lax.dynamic_slice_in_dim(all_values, offset, inner_size, 0)
        key_place = places(offset, inner_size, block_deal, rows_dev)
        probs_full, grad_scores = differentiate(
            query_side, log_total, delta, grad_out3, key_rows, value_rows, key_place
        )
        grad_value_rows = jnp.einsum(
            "hqk,qhd->khd",
            probs_full.astype(jnp.bfloat16),
            grad_out3,
            preferred_element_type=jnp.float32,
        )
        grad_key_rows = jnp.einsum(
            "hqk,qhd->khd", grad_scores, query3, preferred_element_type=jnp.float32
        )
        return jnp.concatenate(
            [grad_key_rows.reshape(inner_size, width), grad_value_rows.reshape(inner_size, width)],
            axis=1,
        )

    parts = lax.map(
        one_part,
        jnp.arange(lax.axis_size("ctx") * rows_dev // inner_size, dtype=jnp.int32) * inner_size,
    )
    key_value_grad = lax.psum_scatter(
        parts.reshape(lax.axis_size("ctx") * rows_dev, 2 * width),
        "ctx",
        scatter_dimension=0,
        tiled=True,
    )
    grad_key_pre = rotate(key_value_grad[:, :width], here, -1.0).astype(jnp.bfloat16)
    grad_value_low = key_value_grad[:, width:].astype(jnp.bfloat16)
    grad_query_pre = rotate(grad_query3.reshape(rows_dev, width), here, -1.0).astype(jnp.bfloat16)
    query_grad = contract_product(normed, grad_query_pre, 0, 0)
    key_grad = contract_product(normed, grad_key_pre, 0, 0)
    value_grad = contract_product(normed, grad_value_low, 0, 0)
    grad_normed = (
        contract_product(grad_query_pre, query_full, 1, 1)
        + contract_product(grad_key_pre, key_full, 1, 1)
        + contract_product(grad_value_low, value_full, 1, 1)
    )
    through_one, gain_one_grad = rms_back(inputs, scale_one, gain_first, grad_normed)
    grad_input = grad_second + through_one
    (
        gain_one_share,
        query_share,
        key_share,
        value_share,
        output_share,
        gain_two_share,
        router_share,
        sgate_share,
        sup_share,
        sdown_share,
        egate_share,
        expert_up_portion,
        edown_share,
    ) = (
        lax.psum_scatter(
            gain_one_grad.astype(jnp.bfloat16), "wt", scatter_dimension=0, tiled=True
        ).astype(jnp.float32),
        lax.psum_scatter(
            query_grad.astype(jnp.bfloat16), "wt", scatter_dimension=0, tiled=True
        ).astype(jnp.float32),
        lax.psum_scatter(
            key_grad.astype(jnp.bfloat16), "wt", scatter_dimension=0, tiled=True
        ).astype(jnp.float32),
        lax.psum_scatter(
            value_grad.astype(jnp.bfloat16), "wt", scatter_dimension=0, tiled=True
        ).astype(jnp.float32),
        lax.psum_scatter(
            output_grad.astype(jnp.bfloat16), "wt", scatter_dimension=0, tiled=True
        ).astype(jnp.float32),
        lax.psum_scatter(
            gain_two_grad.astype(jnp.bfloat16), "wt", scatter_dimension=0, tiled=True
        ).astype(jnp.float32),
        lax.psum_scatter(
            router_grad.astype(jnp.bfloat16), "wt", scatter_dimension=0, tiled=True
        ).astype(jnp.float32),
        lax.psum_scatter(
            sgate_grad.astype(jnp.bfloat16), "wt", scatter_dimension=0, tiled=True
        ).astype(jnp.float32),
        lax.psum_scatter(
            sup_grad.astype(jnp.bfloat16), "wt", scatter_dimension=0, tiled=True
        ).astype(jnp.float32),
        lax.psum_scatter(
            sdown_grad.astype(jnp.bfloat16), "wt", scatter_dimension=0, tiled=True
        ).astype(jnp.float32),
        lax.psum_scatter(
            egate_grad.astype(jnp.bfloat16), "wt", scatter_dimension=0, tiled=True
        ).astype(jnp.float32),
        lax.psum_scatter(
            expert_up_weight_grad.astype(jnp.bfloat16), "wt", scatter_dimension=0, tiled=True
        ).astype(jnp.float32),
        lax.psum_scatter(
            edown_grad.astype(jnp.bfloat16), "wt", scatter_dimension=0, tiled=True
        ).astype(jnp.float32),
    )
    (
        gain_one_sum,
        query_sum,
        key_sum,
        value_sum,
        output_sum,
        gain_two_sum,
        router_sum,
        sgate_sum,
        sup_sum,
        sdown_sum,
    ) = lax.psum(
        (
            gain_one_share,
            query_share,
            key_share,
            value_share,
            output_share,
            gain_two_share,
            router_share,
            sgate_share,
            sup_share,
            sdown_share,
        ),
        "ctx",
    )
    return (
        result[None],
        grad_input[None],
        gain_one_sum,
        query_sum,
        key_sum,
        value_sum,
        output_sum,
        gain_two_sum,
        router_sum,
        sgate_sum,
        sup_sum,
        sdown_sum,
        egate_share,
        expert_up_portion,
        edown_share,
    )


def fast_body(
    tokens,
    cotangent,
    gain_attention,
    query_weight,
    key_weight,
    value_weight,
    output_weight,
    gain_mixer,
    router_weight,
    shared_gate,
    shared_up,
    shared_down,
    expert_gate,
    expert_up,
    expert_down,
    routes,
    slot_order,
    block_deal,
):
    rows_dev = tokens.shape[1]
    width = tokens.shape[2]
    ranks = lax.axis_size("ctx")
    heads = width // HD
    inputs = tokens[0].astype(jnp.float32)
    here, cosr, sinr = angles_of(block_deal, rows_dev)
    query_side_block = here // BLK
    kb = (places(0, ranks * rows_dev, block_deal, rows_dev) // BLK)[None, :]
    qb = jnp.concatenate([query_side_block, query_side_block])[:, None]
    pack = pack_params(gain_attention, gain_mixer, router_weight)
    (q_st, kv_all, mixed_f, lse, second, mixer, normed, pack_all, wfull, sg_sl, su_sl, eg_full, eu_full, cot4) = run_forward(
        tokens[0], pack, cosr, sinr, kb, qb, cotangent[0], query_weight, key_weight, value_weight, output_weight, shared_gate, shared_up, expert_gate, expert_up)
    gain_first, gain_second = pack_all[0], pack_all[1]
    query_full, key_full, value_full, output_full = wfull[0], wfull[1], wfull[2], wfull[3]
    route = routes[0]
    top_count = route.shape[1]
    by_choice = route.T.reshape(1, rows_dev * top_count)
    turns = slot_order[0, 0]
    turns = lax.rem(turns, top_count) * rows_dev + lax.div(turns, top_count)
    (result, grad_second, pack_grad, dsg, dsu, dsd, egate_grad, expert_up_weight_grad, edown_grad) = run_experts(
        second, mixer, pack_all, cotangent[0], route, by_choice, by_choice.reshape(-1, 1), turns[None, :], turns[:, None],
        shared_down, sg_sl, su_sl, cot4, eg_full, eu_full, expert_down)
    query_rot = (8.0 * (q_st[:, :rows_dev] + q_st[:, rows_dev:])).astype(jnp.bfloat16).transpose(1, 0, 2).reshape(rows_dev, width)
    query3 = query_rot.reshape(rows_dev, heads, HD)
    query_side = (query3, query_side_block)
    log_total = lse[:, :, 0].reshape(heads, rows_dev)
    mixed3 = mixed_f.reshape(rows_dev, heads, HD)
    scale_one = lax.rsqrt(jnp.mean(inputs * inputs, axis=-1, keepdims=True) + EPS)
    gain_two_grad = pack_grad[1]
    router_grad = pack_grad[2:10].T
    sgate_grad, sup_grad, sdown_grad = dsg, dsu, dsd
    mixed_low = mixed3.reshape(rows_dev, width).astype(jnp.bfloat16)
    grad_attention = grad_second.astype(jnp.bfloat16)
    output_grad = contract_product(mixed_low, grad_attention, 0, 0)
    grad_mixed = contract_product(grad_attention, output_full, 1, 1).astype(jnp.bfloat16)
    grad_out3 = grad_mixed.reshape(rows_dev, heads, HD)
    delta = jnp.sum(grad_out3.astype(jnp.float32) * mixed3, axis=2).T
    all_keys, all_values = (
        kv_all[:, :, :width].reshape(ranks * rows_dev, width),
        kv_all[:, :, width:].reshape(ranks * rows_dev, width),
    )
    total_rows = all_keys.shape[0]
    block_size = KEY_ROWS

    def query_step(grad_sum, offset):
        key_rows = lax.dynamic_slice_in_dim(all_keys, offset, block_size, 0)
        value_rows = lax.dynamic_slice_in_dim(all_values, offset, block_size, 0)
        key_place = places(offset, block_size, block_deal, rows_dev)
        unused, grad_scores = differentiate(
            query_side, log_total, delta, grad_out3, key_rows, value_rows, key_place
        )
        key3 = key_rows.reshape(block_size, heads, HD)
        return (
            grad_sum
            + jnp.einsum("hqk,khd->qhd", grad_scores, key3, preferred_element_type=jnp.float32),
            None,
        )

    offsets = jnp.arange(total_rows // block_size, dtype=jnp.int32) * block_size
    grad_query3, unused = lax.scan(
        query_step, jnp.zeros((rows_dev, heads, HD), jnp.float32), offsets
    )
    inner_size = KEY_ROWS

    def one_part(offset):
        key_rows = lax.dynamic_slice_in_dim(all_keys, offset, inner_size, 0)
        value_rows = lax.dynamic_slice_in_dim(all_values, offset, inner_size, 0)
        key_place = places(offset, inner_size, block_deal, rows_dev)
        probs_full, grad_scores = differentiate(
            query_side, log_total, delta, grad_out3, key_rows, value_rows, key_place
        )
        grad_value_rows = jnp.einsum(
            "hqk,qhd->khd",
            probs_full.astype(jnp.bfloat16),
            grad_out3,
            preferred_element_type=jnp.float32,
        )
        grad_key_rows = jnp.einsum(
            "hqk,qhd->khd", grad_scores, query3, preferred_element_type=jnp.float32
        )
        return jnp.concatenate(
            [grad_key_rows.reshape(inner_size, width), grad_value_rows.reshape(inner_size, width)],
            axis=1,
        )

    parts = lax.map(
        one_part,
        jnp.arange(lax.axis_size("ctx") * rows_dev // inner_size, dtype=jnp.int32) * inner_size,
    )
    key_value_grad = lax.psum_scatter(
        parts.reshape(lax.axis_size("ctx") * rows_dev, 2 * width),
        "ctx",
        scatter_dimension=0,
        tiled=True,
    )
    grad_key_pre = rotate(key_value_grad[:, :width], here, -1.0).astype(jnp.bfloat16)
    grad_value_low = key_value_grad[:, width:].astype(jnp.bfloat16)
    grad_query_pre = rotate(grad_query3.reshape(rows_dev, width), here, -1.0).astype(jnp.bfloat16)
    query_grad = contract_product(normed, grad_query_pre, 0, 0)
    key_grad = contract_product(normed, grad_key_pre, 0, 0)
    value_grad = contract_product(normed, grad_value_low, 0, 0)
    grad_normed = (
        contract_product(grad_query_pre, query_full, 1, 1)
        + contract_product(grad_key_pre, key_full, 1, 1)
        + contract_product(grad_value_low, value_full, 1, 1)
    )
    through_one, gain_one_grad = rms_back(inputs, scale_one, gain_first, grad_normed)
    grad_input = grad_second + through_one
    (
        gain_one_share,
        query_share,
        key_share,
        value_share,
        output_share,
        gain_two_share,
        router_share,
        sgate_share,
        sup_share,
        sdown_share,
        egate_share,
        expert_up_portion,
        edown_share,
    ) = (
        lax.psum_scatter(
            gain_one_grad.astype(jnp.bfloat16), "wt", scatter_dimension=0, tiled=True
        ).astype(jnp.float32),
        lax.psum_scatter(
            query_grad.astype(jnp.bfloat16), "wt", scatter_dimension=0, tiled=True
        ).astype(jnp.float32),
        lax.psum_scatter(
            key_grad.astype(jnp.bfloat16), "wt", scatter_dimension=0, tiled=True
        ).astype(jnp.float32),
        lax.psum_scatter(
            value_grad.astype(jnp.bfloat16), "wt", scatter_dimension=0, tiled=True
        ).astype(jnp.float32),
        lax.psum_scatter(
            output_grad.astype(jnp.bfloat16), "wt", scatter_dimension=0, tiled=True
        ).astype(jnp.float32),
        lax.psum_scatter(
            gain_two_grad.astype(jnp.bfloat16), "wt", scatter_dimension=0, tiled=True
        ).astype(jnp.float32),
        lax.psum_scatter(
            router_grad.astype(jnp.bfloat16), "wt", scatter_dimension=0, tiled=True
        ).astype(jnp.float32),
        lax.all_to_all(sgate_grad, "wt", split_axis=0, concat_axis=1, tiled=True).astype(jnp.float32),
        lax.all_to_all(sup_grad, "wt", split_axis=0, concat_axis=1, tiled=True).astype(jnp.float32),
        sdown_grad.astype(jnp.float32),
        lax.psum_scatter(
            egate_grad.astype(jnp.bfloat16), "wt", scatter_dimension=0, tiled=True
        ).astype(jnp.float32),
        lax.psum_scatter(
            expert_up_weight_grad.astype(jnp.bfloat16), "wt", scatter_dimension=0, tiled=True
        ).astype(jnp.float32),
        lax.psum_scatter(
            edown_grad.astype(jnp.bfloat16), "wt", scatter_dimension=0, tiled=True
        ).astype(jnp.float32),
    )
    (
        gain_one_sum,
        query_sum,
        key_sum,
        value_sum,
        output_sum,
        gain_two_sum,
        router_sum,
        sgate_sum,
        sup_sum,
        sdown_sum,
    ) = lax.psum(
        (
            gain_one_share,
            query_share,
            key_share,
            value_share,
            output_share,
            gain_two_share,
            router_share,
            sgate_share,
            sup_share,
            sdown_share,
        ),
        "ctx",
    )
    return (
        result[None],
        grad_input[None],
        gain_one_sum,
        query_sum,
        key_sum,
        value_sum,
        output_sum,
        gain_two_sum,
        router_sum,
        sgate_sum,
        sup_sum,
        sdown_sum,
        egate_share,
        expert_up_portion,
        edown_share,
    )


def solution(mesh):
    in_specs = (
        P("wt", "ctx", None),
        P("wt", "ctx", None),
        P("wt"),
        P("wt", None),
        P("wt", None),
        P("wt", None),
        P("wt", None),
        P("wt"),
        P("wt", None),
        P("wt", None),
        P("wt", None),
        P("wt", None),
        P("wt", "ctx"),
        P("wt", "ctx"),
        P("wt", "ctx"),
        P("wt", "ctx", None),
        P("wt", "ctx", None),
        P(),
    )
    out_specs = (
        P("wt", "ctx", None),
        P("wt", "ctx", None),
        P("wt"),
        P("wt", None),
        P("wt", None),
        P("wt", None),
        P("wt", None),
        P("wt"),
        P("wt", None),
        P("wt", None),
        P("wt", None),
        P("wt", None),
        P("wt", "ctx"),
        P("wt", "ctx"),
        P("wt", "ctx"),
    )
    chosen = fast_body if (mesh.shape["ctx"], mesh.shape["wt"]) == (8, 4) else body
    return jax.shard_map(chosen, mesh=mesh, in_specs=in_specs, out_specs=out_specs, check_vma=False)
```

```python
import jax
import jax.numpy as jnp
from jax import lax
from jax.experimental import pallas as pl
from jax.experimental.pallas import tpu as pltpu
from jax.sharding import PartitionSpec as P

HD = 64
BLK = 256


EPS = 1e-06
KEY_ROWS = 512
HIGH = lax.Precision.HIGHEST
MASKED = -1e30


MESH = pl.DeviceIdType.MESH
VMEM = pltpu.VMEM
BF = jnp.bfloat16
F32 = jnp.float32
PAIR = 2 * HD


class Spot:
    def __init__(self, line_size):
        self.k = lax.axis_index("ctx")
        self.w = lax.axis_index("wt")
        self.z, self.x = lax.div(self.k, 2), lax.rem(self.k, 2)
        self.y, self.c = lax.div(self.w, 2), lax.rem(self.w, 2)
        self.far = lax.div(self.z, 2)
        self.mid = self.z + self.far * (3 - 2 * self.z)
        step = 1 - 2 * self.far
        self.core = (self.k, 2 * self.y + 1 - self.c)
        self.across = (self.k, 2 * (1 - self.y) + self.c)
        self.corner = (self.k, 2 * (1 - self.y) + 1 - self.c)
        self.column = (2 * self.z + 1 - self.x, self.w)
        self.inner = (2 * (self.z + step) + self.x, self.w)
        self.outer = (2 * (self.z - step) + self.x, self.w)

    def plane(self, step):
        mirrored = (self.mid, 1 - self.mid, 2, 3)[step]
        return mirrored + self.far * (3 - 2 * mirrored)


class Sems:
    def __init__(self, ref):
        self.ref, self.used = ref, 0

    def new(self):
        self.used += 1
        return self.ref.at[self.used - 1]


def remote(src, dst, send, recv, to):
    return pltpu.make_async_remote_copy(
        src_ref=src, dst_ref=dst, send_sem=send, recv_sem=recv, device_id=to, device_id_type=MESH
    )


def greet(devices, middle=None):
    barrier = pltpu.get_barrier_semaphore()
    for to in devices:
        pl.semaphore_signal(barrier, inc=1, device_id=to, device_id_type=MESH)
    if middle is None:
        pl.semaphore_wait(barrier, len(devices))
        return

    @pl.when(middle[0] == 1)
    def _():
        pl.semaphore_signal(barrier, inc=1, device_id=middle[1], device_id_type=MESH)

    pl.semaphore_wait(barrier, len(devices) + middle[0])


class Gather:
    def __init__(self, spot, src, dst, sems):
        self.spot, self.dst, self.sems = spot, dst, sems
        self.rows = src.shape[0]
        here = self.block(spot.w)
        self.local = pltpu.make_async_copy(src, here, sems.new())
        self.to_core = remote(src, here, sems.new(), sems.new(), spot.core)
        self.to_across = remote(src, here, sems.new(), sems.new(), spot.across)
        for copy in (self.to_across, self.to_core, self.local):
            copy.start()

    def block(self, w):
        return self.dst.at[pl.ds(pl.multiple_of(self.rows * w, 64), self.rows)]

    def forward(self):
        self.to_across.wait_recv()
        part = self.block(self.spot.across[1])
        self.onward = remote(part, part, self.sems.new(), self.sems.new(), self.spot.core)
        self.onward.start()

    def finish(self):
        self.local.wait()
        self.to_core.wait_recv()
        self.onward.wait_recv()

    def drain(self):
        self.to_core.wait_send()
        self.to_across.wait_send()
        self.onward.wait_send()


class Spread:
    def __init__(self, spot, pick, place, sems, local=True):
        self.copies = []
        for to in (spot.across, spot.corner, spot.core):
            self.copies.append(remote(pick(to[1]), place(spot.w), sems.new(), sems.new(), to))
        self.local = None
        if local:
            self.local = pltpu.make_async_copy(pick(spot.w), place(spot.w), sems.new())
        for copy in self.copies:
            copy.start()
        if local:
            self.local.start()

    def finish(self):
        for copy in self.copies:
            copy.wait_recv()
        if self.local is not None:
            self.local.wait()

    def drain(self):
        for copy in self.copies:
            copy.wait_send()


def nt(left, right):
    return lax.dot_general(left, right, (((1,), (1,)), ((), ())), preferred_element_type=F32)


def nn(left, right):
    return jnp.dot(left, right, preferred_element_type=F32)


def tn(left, right):
    return lax.dot_general(left, right, (((0,), (0,)), ((), ())), preferred_element_type=F32)


def turn(values, cosine, sine):
    wide = values.shape[1]
    lane = lax.broadcasted_iota(jnp.int32, values.shape, 1)
    first = lax.rem(lane, HD) < HD // 2
    swapped = jnp.where(
        first, pltpu.roll(values, wide - HD // 2, 1), pltpu.roll(values, HD // 2, 1)
    )
    copies = wide // PAIR
    cosine = jnp.concatenate([cosine] * copies, axis=1)
    sine = jnp.concatenate([sine] * copies, axis=1)
    return values * cosine + swapped * sine


def stack_pair(values):
    lane = lax.broadcasted_iota(jnp.int32, values.shape, 1)
    none = jnp.zeros_like(values)
    return jnp.concatenate(
        [jnp.where(lane < HD, values, none), jnp.where(lane < HD, none, values)], axis=0
    )


def unstack_pair(values):
    rows = values.shape[0] // 2
    lane = lax.broadcasted_iota(jnp.int32, (rows, PAIR), 1)
    return jnp.where(lane < HD, values[:rows], values[rows:])


class Ring:
    def __init__(self, spot, blocks, recv, send):
        self.spot, self.blocks, self.recv, self.send = spot, blocks, recv, send
        self.used = 0
        self.sent, self.sent_mid = [], []

    def copy(self, slot, to):
        self.used += 1
        return remote(
            self.blocks.at[slot],
            self.blocks.at[slot],
            self.send.at[self.used - 1],
            self.recv.at[slot],
            to,
        )

    def arrived(self, slot):
        remote(
            self.blocks.at[slot],
            self.blocks.at[slot],
            self.send.at[0],
            self.recv.at[slot],
            self.spot.column,
        ).wait_recv()

    def start(self):
        spot = self.spot
        own = self.copy(spot.k, spot.inner)
        side = self.copy(spot.k, spot.column)
        back = self.copy(spot.k, spot.outer)
        own.start()

        @pl.when(spot.mid == 1)
        def _():
            back.start()

        side.start()
        self.sent += [own, side]
        self.sent_mid += [back]

    def step(self, number):
        spot = self.spot
        plane = spot.plane(number)
        if number > 0:
            slot = 2 * plane + spot.x
            self.arrived(slot)
            along = self.copy(slot, spot.inner if number == 1 else spot.outer)

            @pl.when(spot.mid == 1)
            def _():
                along.start()

            side = self.copy(slot, spot.column)
            side.start()
            self.sent += [side]
            self.sent_mid += [along]
        return plane

    def other(self, plane):
        self.arrived(2 * plane + 1 - self.spot.x)

    def drain(self):
        for copy in self.sent:
            copy.wait_send()

        @pl.when(self.spot.mid == 1)
        def _():
            for copy in self.sent_mid:
                copy.wait_send()


def forward_kernel(
    tok, pack, cosr, sinr, kb, qb, cot, wq, wk, wv, wo, sg, su, eg, eu,
    q_out, kv_out, mixed_out, lse_out, second_out, mixer_out, normed_out, pack_out,
    wfull_out, sg_out, su_out, eg_out, eu_out, cot_out,
    wbuf, kv, packs, top, low, acc, sem, kv_recv, kv_send,
):
    spot = Spot(4)
    sems = Sems(sem)
    rows = tok.shape[0]
    width = tok.shape[1]
    pairs = width // PAIR
    greet((spot.core, spot.across, spot.corner, spot.column, spot.inner), (spot.mid, spot.outer))
    params = Spread(spot, lambda w: pack, lambda w: packs.at[w], sems)
    key_w = Gather(spot, wk, wbuf.at[1], sems)
    value_w = Gather(spot, wv, wbuf.at[2], sems)
    query_w = Gather(spot, wq, wbuf.at[0], sems)
    inputs = tok[...].astype(F32)
    scale = lax.rsqrt(jnp.mean(inputs * inputs, axis=-1, keepdims=True) + EPS)
    scaled = inputs * scale
    params.finish()
    pack_all = packs[0] + packs[1] + packs[2] + packs[3]
    pack_out[...] = pack_all
    normed = (scaled * pack_all[0:1]).astype(BF)
    normed_out[...] = normed
    cosine, sine = cosr[...], sinr[...]
    key_w.forward()
    value_w.forward()
    key_w.finish()
    kv[spot.k, :, 0:width] = turn(nn(normed, wbuf[1]), cosine, sine).astype(BF)
    value_w.finish()
    kv[spot.k, :, width : 2 * width] = nn(normed, wbuf[2]).astype(BF)
    ring = Ring(spot, kv, kv_recv, kv_send)
    ring.start()
    query_w.forward()
    out_w = Gather(spot, wo, wbuf.at[3], sems)
    sg_w = Spread(
        spot,
        lambda w: sg.at[:, pl.ds(pl.multiple_of(512 * w, 512), 512)],
        lambda w: sg_out.at[pl.ds(pl.multiple_of(192 * w, 64), 192)],
        sems,
    )
    su_w = Spread(
        spot,
        lambda w: su.at[:, pl.ds(pl.multiple_of(512 * w, 512), 512)],
        lambda w: su_out.at[pl.ds(pl.multiple_of(192 * w, 64), 192)],
        sems,
    )
    cot_w = Spread(spot, lambda w: cot, lambda w: cot_out.at[w], sems)
    gate_w = Gather(spot, eg, eg_out, sems)
    up_w = Gather(spot, eu, eu_out, sems)
    query_w.finish()
    query = turn(nn(normed, wbuf[0]), cosine, sine).astype(BF) * jnp.asarray(HD**-0.5, BF)
    for j in range(pairs):
        q_out[j] = stack_pair(query[:, PAIR * j : PAIR * (j + 1)])
    top[...] = jnp.full_like(top, MASKED)
    low[...] = jnp.zeros_like(low)
    acc[...] = jnp.zeros_like(acc)
    q_block = qb[...]

    def chunk(plane):
        k_block = kb[:, pl.ds(pl.multiple_of(2 * rows * plane, 2 * rows), 2 * rows)]
        allowed = k_block <= q_block

        def one_pair(j, carry):
            lane = pl.multiple_of(PAIR * j, PAIR)
            key = kv[pl.ds(2 * plane, 2), :, pl.ds(lane, PAIR)].reshape(2 * rows, PAIR)
            value = kv[pl.ds(2 * plane, 2), :, pl.ds(width + lane, PAIR)].reshape(2 * rows, PAIR)
            scores = jnp.where(allowed, nt(q_out[j], key), MASKED)
            old = top[j]
            new = jnp.maximum(old, jnp.max(scores, axis=1, keepdims=True))
            raised = jnp.where(allowed, jnp.exp(scores - new[:, 0:1]), 0.0)
            factor = jnp.exp(old - new)
            top[j] = new
            low[j] = low[j] * factor + jnp.sum(raised, axis=1, keepdims=True)
            acc[j] = acc[j] * factor + nn(raised.astype(BF), value)
            return carry

        lax.fori_loop(0, pairs, one_pair, 0)

    for number in range(4):
        plane = ring.step(number)
        ring.other(plane)
        chunk(plane)
    saves = [pltpu.make_async_copy(kv, kv_out, sems.new())]
    saves[0].start()
    out_w.forward()
    for j in range(pairs):
        mixed_out[:, PAIR * j : PAIR * (j + 1)] = unstack_pair(acc[j] / low[j])
        lse_out[j] = top[j] + jnp.log(low[j])
    out_w.finish()
    saves.append(pltpu.make_async_copy(wbuf, wfull_out, sems.new()))
    saves[1].start()
    second = inputs + nn(mixed_out[...].astype(BF), wbuf[3])
    second_out[...] = second
    scale_two = lax.rsqrt(jnp.mean(second * second, axis=-1, keepdims=True) + EPS)
    mixer_out[...] = (second * scale_two * pack_all[1:2]).astype(BF)
    gate_w.forward()
    up_w.forward()
    for part in (sg_w, su_w, cot_w, gate_w, up_w):
        part.finish()
    for part in (params, key_w, value_w, query_w, out_w, sg_w, su_w, cot_w, gate_w, up_w, ring):
        part.drain()
    for copy in saves:
        copy.wait()


def run_forward(tok, pack, cosr, sinr, kb, qb, cot, wq, wk, wv, wo, sg, su, eg, eu):
    rows, width = tok.shape
    pairs = width // PAIR
    ranks = 8
    any_, vm = pl.BlockSpec(memory_space=pl.ANY), pl.BlockSpec(memory_space=VMEM)
    shape = jax.ShapeDtypeStruct
    hidden = eg.shape[1]
    part = sg.shape[1] // 4
    return pl.pallas_call(
        forward_kernel,
        out_shape=(
            shape((pairs, 2 * rows, PAIR), BF),
            shape((ranks, rows, 2 * width), BF),
            shape((rows, width), F32),
            shape((pairs, 2 * rows, PAIR), F32),
            shape((rows, width), F32),
            shape((rows, width), BF),
            shape((rows, width), BF),
            shape(pack.shape, F32),
            shape((4, width, width), BF),
            shape((width, part), BF),
            shape((width, part), BF),
            shape((width, hidden), BF),
            shape((width, hidden), BF),
            shape((4, rows, width), BF),
        ),
        in_specs=[vm] * 6 + [any_] * 9,
        out_specs=(vm, any_, vm, vm, vm, vm, vm, vm, any_, any_, any_, any_, any_, any_),
        scratch_shapes=[
            VMEM((4, width, width), BF),
            VMEM((ranks, rows, 2 * width), BF),
            VMEM((4,) + pack.shape, F32),
            VMEM((pairs, 2 * rows, PAIR), F32),
            VMEM((pairs, 2 * rows, PAIR), F32),
            VMEM((pairs, 2 * rows, PAIR), F32),
            pltpu.SemaphoreType.DMA((96,)),
            pltpu.SemaphoreType.DMA((ranks,)),
            pltpu.SemaphoreType.DMA((16,)),
        ],
        compiler_params=pltpu.CompilerParams(
            collective_id=1, has_side_effects=True, vmem_limit_bytes=48 * 2**20
        ),
    )(tok, pack, cosr, sinr, kb, qb, cot, wq, wk, wv, wo, sg, su, eg, eu)


def angles_of(block_deal, rows_dev):
    here = places(lax.axis_index("ctx") * rows_dev, rows_dev, block_deal, rows_dev)
    half_size = HD // 2
    frequency = 10000.0 ** (-jnp.arange(half_size, dtype=F32) / half_size)
    angles = here.astype(F32)[:, None] * frequency[None, :]
    cosine, sine = jnp.cos(angles), jnp.sin(angles)
    cosr = jnp.concatenate([cosine] * 4, axis=1)
    sinr = jnp.concatenate([-sine, sine, -sine, sine], axis=1)
    return here, cosr, sinr


def pack_params(gain_one, gain_two, router):
    width = 4 * gain_one.shape[0]
    shard = jnp.concatenate(
        [gain_one[None], gain_two[None], router.T, jnp.zeros((6, gain_one.shape[0]), BF)], axis=0
    ).astype(F32)
    start = lax.axis_index("wt") * gain_one.shape[0]
    return lax.dynamic_update_slice(jnp.zeros((16, width), F32), shard, (0, start))


def swish(values):
    sigmoid = 1.0 / (1.0 + jnp.exp(-values))
    return values * sigmoid, sigmoid * (1.0 + values * (1.0 - sigmoid))


class Exchange:
    def __init__(self, spot, out, back, send, recv):
        self.spot, self.out, self.back = spot, out, back
        self.send, self.recv, self.ranks = send, recv, out.shape[0]
        self.copies = []

    def start(self):
        spot = self.spot
        for offset in range(1, self.ranks):
            peer = lax.rem(spot.k + offset, self.ranks)
            self.copies.append(
                remote(
                    self.out.at[peer],
                    self.back.at[spot.k],
                    self.send.at[offset],
                    self.recv.at[spot.k],
                    (peer, spot.w),
                )
            )
            self.copies[-1].start()
        self.back[spot.k] = self.out[spot.k]

    def finish(self):
        spot = self.spot
        for offset in range(1, self.ranks):
            peer = lax.rem(spot.k + offset, self.ranks)
            remote(
                self.out.at[peer],
                self.back.at[peer],
                self.send.at[offset],
                self.recv.at[peer],
                (peer, spot.w),
            ).wait_recv()

    def drain(self):
        for copy in self.copies:
            copy.wait_send()


def fold_rows(values, ref):
    ranks = ref.shape[0]
    slots = values.shape[0] // ranks
    for e in range(ranks):
        part = values[slots * e : slots * (e + 1)]
        tiles = [part[:, 128 * t : 128 * (t + 1)] for t in range(values.shape[1] // 128)]
        ref[e] = jnp.concatenate(tiles, axis=0).astype(BF)


def unfold_rows(ref, slots):
    parts = []
    for e in range(ref.shape[0]):
        part = ref[e].astype(F32)
        tiles = [part[slots * t : slots * (t + 1)] for t in range(part.shape[0] // slots)]
        parts.append(jnp.concatenate(tiles, axis=1))
    return jnp.concatenate(parts, axis=0).astype(BF)


def split_three(values):
    high = values.astype(BF)
    rest = values - high.astype(F32)
    middle = rest.astype(BF)
    return high, middle, (rest - middle.astype(F32)).astype(BF)


def slot_maps(e_row, e_col, o_row, o_col, slots, experts):
    pairs = e_row.shape[1]
    down = lax.broadcasted_iota(jnp.int32, (pairs, pairs), 0)
    along = lax.broadcasted_iota(jnp.int32, (pairs, pairs), 1)
    turn_row = jnp.sum(jnp.where(o_col == along, down.astype(F32), 0.0), axis=0, keepdims=True)
    turn_col = jnp.sum(jnp.where(o_row == down, along.astype(F32), 0.0), axis=1, keepdims=True)
    same = e_col == e_row
    slot_row = jnp.sum(
        jnp.where(same & (turn_col < turn_row), 1.0, 0.0), axis=0, keepdims=True
    ).astype(jnp.int32)
    slot_col = jnp.sum(
        jnp.where(same & (turn_row < turn_col), 1.0, 0.0), axis=1, keepdims=True
    ).astype(jnp.int32)
    target_row = jnp.where(slot_row < slots, e_row * slots + slot_row, -1)
    target_col = jnp.where(slot_col < slots, e_col * slots + slot_col, -1)
    total = experts * slots
    place = lax.broadcasted_iota(jnp.int32, (total, pairs), 0)
    to_slots = jnp.where(place == target_row, 1.0, 0.0).astype(BF)
    place = lax.broadcasted_iota(jnp.int32, (pairs, total), 1)
    to_pairs = jnp.where(place == target_col, 1.0, 0.0).astype(BF)
    return to_slots, to_pairs


def experts_kernel(
    second_ref, mixer_ref, pack_ref, cot_ref, route_ref, e_row, e_col, o_row, o_col,
    sd_ref, sg_ref, su_ref, cot4_ref, eg_ref, eu_ref, ed_ref,
    result_out, grad_second_out, pack_grad_out, dsh_out,
    dg_out, du_out, dd_out,
    wg, wu, wd, m4, sh_send, sh_recv, gm_send, gm_recv,
    xs, xr, gs, gr, os, orr, bs, br, x_s, g_s, sum_s,
    gate_s, up_s, hid_s, dgate_s, dup_s, dsh, dsh_x, sem, a2a_send, a2a_recv, sem_sh,
):
    spot = Spot(4)
    sems = Sems(sem)
    rows, width = mixer_ref.shape
    ranks = xs.shape[0]
    slots = xs.shape[1] * 128 // width
    hidden = wg.shape[1]
    loads = [
        pltpu.make_async_copy(eg_ref, wg, sems.new()),
        pltpu.make_async_copy(eu_ref, wu, sems.new()),
    ]
    for copy in loads:
        copy.start()
    others = [(lax.rem(spot.k + o, ranks), spot.w) for o in range(1, ranks)]
    greet([spot.core, spot.across, spot.corner] + others)
    mixer = mixer_ref[...]
    to_slots, to_pairs = slot_maps(
        e_row[...], e_col[...], o_row[...], o_col[...], slots, ranks
    )
    fold_rows(nn(to_slots[:, :rows] + to_slots[:, rows:], mixer), xs)
    rows_out = Exchange(spot, xs, xr, a2a_send.at[0], a2a_recv.at[0])
    rows_out.start()
    mixers = Spread(spot, lambda w: mixer_ref, lambda w: m4.at[w], sems)
    down_w = Gather(spot, ed_ref, wd, sems)
    pack = pack_ref[...]
    router = pack[2:16].astype(BF)
    router = jnp.concatenate([router, jnp.zeros((2, width), BF)], axis=0)
    logits = nt(mixer, router)
    lane = lax.broadcasted_iota(jnp.int32, logits.shape, 1)
    matches = [lane == route_ref[:, j : j + 1] for j in range(2)]
    chosen = [jnp.sum(jnp.where(m, logits, 0.0), axis=1, keepdims=True) for m in matches]
    largest = jnp.maximum(chosen[0], chosen[1])
    raised = [jnp.exp(c - largest) for c in chosen]
    gates = [r / (raised[0] + raised[1]) for r in raised]
    grad = cot_ref[...].astype(F32)
    pair_grad = jnp.concatenate([(g * grad).astype(BF) for g in gates], axis=0)
    fold_rows(nn(to_slots, pair_grad), gs)
    grads_out = Exchange(spot, gs, gr, a2a_send.at[1], a2a_recv.at[1])
    grads_out.start()

    mixers.finish()
    rows_all = m4[...].reshape(4 * rows, width)
    grad_all = cot4_ref[...].reshape(4 * rows, width)
    gate_part, up_part = nn(rows_all, sg_ref[...]), nn(rows_all, su_ref[...])
    act, slope = swish(gate_part)
    shared_hidden = (act * up_part).astype(BF)
    sh_send[...] = nn(shared_hidden, sd_ref[...]).astype(BF).reshape(4, rows, width)
    shared_out = Spread(spot, lambda w: sh_send.at[w], lambda w: sh_recv.at[w], sems)
    hid_grad = nt(grad_all, sd_ref[...])
    grad_gate = (hid_grad * up_part * slope).astype(BF)
    grad_up = (hid_grad * act).astype(BF)
    back = nt(grad_gate, sg_ref[...]) + nt(grad_up, su_ref[...])
    gm_send[...] = back.astype(BF).reshape(4, rows, width)
    shared_back = Spread(spot, lambda w: gm_send.at[w], lambda w: gm_recv.at[w], sems)
    shard = width // 4
    half = shard // 2
    for at, values in ((0, tn(rows_all, grad_gate)), (half, tn(rows_all, grad_up))):
        values = values.astype(BF)
        for r in range(ranks):
            top, left = half * (r // 4), 128 * (r % 4)
            for w in range(4):
                dsh[r, shard * w + at : shard * w + at + half] = values[
                    shard * w + top : shard * w + top + half, left : left + 128
                ]
    values = tn(shared_hidden, grad_all).astype(BF)
    deep = values.shape[0] // ranks
    for r in range(ranks):
        for t in range(width // 128):
            dsh[r, width + deep * t : width + deep * (t + 1)] = values[
                deep * r : deep * (r + 1), 128 * t : 128 * (t + 1)
            ]
    shared_grad = Reduce(spot, dsh, dsh_x, None, None, sem_sh)
    for number in (3, 2, 1, 0):
        shared_grad.side(number)
    down_w.forward()
    for copy in loads:
        copy.wait()

    rows_out.finish()
    x_s[...] = unfold_rows(xr, slots)
    block = 512

    def parts(i):
        return pl.ds(pl.multiple_of(block * i, block), block)

    def up_step(i, carry):
        at = parts(i)
        gate = nn(x_s[...], wg[:, at])
        up = nn(x_s[...], wu[:, at])
        act, slope = swish(gate)
        hid_s[:, at] = (act * up).astype(BF)
        gate_s[:, at] = up * slope
        up_s[:, at] = act
        return carry

    lax.fori_loop(0, hidden // block, up_step, 0)
    down_w.finish()
    sum_s[...] = nt(hid_s[...], wd[...])
    fold_rows(sum_s[...], os)
    outs = Exchange(spot, os, orr, a2a_send.at[2], a2a_recv.at[2])
    outs.start()
    grads_out.finish()
    g_s[...] = unfold_rows(gr, slots)

    def down_step(i, carry):
        at = parts(i)
        grad_hidden = nn(g_s[...], wd[:, at])
        dgate_s[:, at] = (grad_hidden * gate_s[:, at]).astype(BF)
        dup_s[:, at] = (grad_hidden * up_s[:, at]).astype(BF)
        return carry

    lax.fori_loop(0, hidden // block, down_step, 0)
    sum_s[...] = nt(dgate_s[...], wg[...]) + nt(dup_s[...], wu[...])
    fold_rows(sum_s[...], bs)
    backs = Exchange(spot, bs, br, a2a_send.at[3], a2a_recv.at[3])
    backs.start()

    down_w.drain()

    def grad_step(i, carry):
        at = parts(i)
        wg[:, at] = tn(x_s[...], dgate_s[:, at]).astype(BF)
        wu[:, at] = tn(x_s[...], dup_s[:, at]).astype(BF)
        wd[:, at] = tn(g_s[...], hid_s[:, at]).astype(BF)
        return carry

    lax.fori_loop(0, hidden // block, grad_step, 0)
    saves = [
        pltpu.make_async_copy(src, dst, sems.new())
        for src, dst in ((wg, dg_out), (wu, du_out), (wd, dd_out))
    ]
    for copy in saves:
        copy.start()

    for number in (3, 2, 1, 0):
        shared_grad.meet(number)
        plane = spot.plane(number)
        dsh_out[plane] = dsh[2 * plane + spot.x]

    second = second_ref[...]
    shared_out.finish()
    total = second
    for w in range(4):
        total = total + sh_recv[w].astype(F32)
    outs.finish()
    pair_out = nn(to_pairs, unfold_rows(orr, slots))
    pair_out = [pair_out[:rows], pair_out[rows:]]
    result_out[...] = (total + gates[0] * pair_out[0] + gates[1] * pair_out[1]).astype(BF)
    grad_gates = [jnp.sum(grad * p, axis=1, keepdims=True) for p in pair_out]
    inner = gates[0] * grad_gates[0] + gates[1] * grad_gates[1]
    grad_logits = jnp.zeros_like(logits)
    for j in range(2):
        grad_logits += jnp.where(matches[j], gates[j] * (grad_gates[j] - inner), 0.0)
    pieces = split_three(grad_logits)
    router_grad = sum(tn(piece, mixer) for piece in pieces)
    grad_mixer = sum(nn(piece, router) for piece in pieces)
    shared_back.finish()
    for w in range(4):
        grad_mixer = grad_mixer + gm_recv[w].astype(F32)
    backs.finish()
    grad_mixer = grad_mixer + nn(to_pairs[:rows] + to_pairs[rows:], unfold_rows(br, slots))
    scale = lax.rsqrt(jnp.mean(second * second, axis=-1, keepdims=True) + EPS)
    weighted = grad_mixer * pack[1:2]
    mean = jnp.mean(weighted * second, axis=-1, keepdims=True)
    grad_second_out[...] = grad + scale * weighted - second * (scale * scale * scale * mean)
    gain_grad = jnp.sum(grad_mixer * second * scale, axis=0, keepdims=True)
    pack_grad_out[...] = jnp.concatenate(
        [jnp.zeros_like(gain_grad), gain_grad, router_grad[:14]], axis=0
    )
    for part in (rows_out, grads_out, outs, backs, mixers, shared_out, shared_back):
        part.drain()
    for copy in shared_grad.sent:
        copy.wait_send()
    for copy in saves:
        copy.wait()


def run_experts(
    second, mixer, pack, cot, route, e_row, e_col, o_row, o_col, sd, sg, su, cot4, eg, eu, ed
):
    rows, width = mixer.shape
    ranks, slots = 8, 40
    hidden = eg.shape[1]
    part = sg.shape[1]
    total = ranks * slots
    tall = width + part * width // (128 * ranks)
    folded = (ranks, slots * width // 128, 128)
    any_, vm = pl.BlockSpec(memory_space=pl.ANY), pl.BlockSpec(memory_space=VMEM)
    shape = jax.ShapeDtypeStruct
    return pl.pallas_call(
        experts_kernel,
        out_shape=(
            shape((rows, width), BF),
            shape((rows, width), F32),
            shape(pack.shape, F32),
            shape((4, tall, 128), BF),
            shape((width, hidden), BF),
            shape((width, hidden), BF),
            shape((width, hidden), BF),
        ),
        in_specs=[vm] * 13 + [any_] * 3,
        out_specs=tuple([vm] * 4 + [any_] * 3),
        scratch_shapes=[
            VMEM((width, hidden), BF),
            VMEM((width, hidden), BF),
            VMEM((width, hidden), BF),
            VMEM((4, rows, width), BF),
            VMEM((4, rows, width), BF),
            VMEM((4, rows, width), BF),
            VMEM((4, rows, width), BF),
            VMEM((4, rows, width), BF),
            VMEM(folded, BF),
            VMEM(folded, BF),
            VMEM(folded, BF),
            VMEM(folded, BF),
            VMEM(folded, BF),
            VMEM(folded, BF),
            VMEM(folded, BF),
            VMEM(folded, BF),
            VMEM((total, width), BF),
            VMEM((total, width), BF),
            VMEM((total, width), F32),
            VMEM((total, hidden), F32),
            VMEM((total, hidden), F32),
            VMEM((total, hidden), BF),
            VMEM((total, hidden), BF),
            VMEM((total, hidden), BF),
            VMEM((ranks, tall, 128), BF),
            VMEM((4, tall, 128), BF),
            pltpu.SemaphoreType.DMA((48,)),
            pltpu.SemaphoreType.DMA((4, ranks)),
            pltpu.SemaphoreType.DMA((4, ranks)),
            pltpu.SemaphoreType.DMA((5, 4)),
        ],
        compiler_params=pltpu.CompilerParams(
            collective_id=2, has_side_effects=True, vmem_limit_bytes=56 * 2**20
        ),
    )(second, mixer, pack, cot, route, e_row, e_col, o_row, o_col, sd, sg, su, cot4, eg, eu, ed)


class Reduce:
    def __init__(self, spot, part, sides, zo, zi, sems, folded=False):
        self.spot, self.part, self.sides, self.zo, self.zi = spot, part, sides, zo, zi
        self.x_send, self.x_recv, self.z_send, self.zo_recv, self.zi_recv = (
            sems.at[i] for i in range(5)
        )
        self.folded = folded
        self.sent, self.sent_end, self.sent_mid = [], [], []

    def own(self, plane):
        return self.part.at[plane if self.folded else 2 * plane + self.spot.x]

    def wait(self, land, recv, plane):
        remote(
            land.at[plane], land.at[plane], self.z_send.at[plane], recv.at[plane], self.spot.column
        ).wait_recv()

    def side(self, number):
        spot = self.spot
        plane = spot.plane(number)
        copy = remote(
            self.part.at[2 * plane + 1 - spot.x],
            self.sides.at[plane],
            self.x_send.at[plane],
            self.x_recv.at[plane],
            spot.column,
        )
        copy.start()
        self.sent.append(copy)

    def meet(self, number):
        plane = self.spot.plane(number)
        self.wait(self.sides, self.x_recv, plane)
        own = self.own(plane)
        own[...] = (own[...].astype(F32) + self.sides[plane].astype(F32)).astype(BF)

    def launch(self, number):
        plane = self.spot.plane(number)
        copy = remote(
            self.own(plane),
            self.zo.at[plane],
            self.z_send.at[plane],
            self.zo_recv.at[plane],
            self.spot.inner,
        )

        @pl.when(self.spot.mid == 0)
        def _():
            copy.start()

        self.sent_end.append(copy)

    def relay(self, number):
        plane = self.spot.plane(number)
        land, recv = (self.zi, self.zi_recv) if number == 1 else (self.zo, self.zo_recv)
        own = self.own(plane)
        copy = remote(
            own,
            self.zi.at[plane],
            self.z_send.at[plane],
            self.zi_recv.at[plane],
            self.spot.outer if number == 1 else self.spot.inner,
        )

        @pl.when(self.spot.mid == 1)
        def _():
            self.wait(land, recv, plane)
            own[...] = (own[...].astype(F32) + land[plane].astype(F32)).astype(BF)
            copy.start()

        self.sent_mid.append(copy)

    def last(self, result):
        plane = self.spot.plane(0)
        self.wait(self.zi, self.zi_recv, plane)
        result[...] = self.own(plane)[...].astype(F32) + self.zi[plane].astype(F32)

        @pl.when(self.spot.mid == 1)
        def _():
            self.wait(self.zo, self.zo_recv, plane)
            result[...] += self.zo[plane].astype(F32)

    def drain(self):
        for copy in self.sent:
            copy.wait_send()

        @pl.when(self.spot.mid == 0)
        def _():
            for copy in self.sent_end:
                copy.wait_send()

        @pl.when(self.spot.mid == 1)
        def _():
            for copy in self.sent_mid:
                copy.wait_send()


def backward_kernel(
    grad_second_ref, tok, pack_ref, pack_grad_ref, normed_ref, mixed_ref, q_ref, lse_ref,
    cosr, sinr, kb, qb, dsh_ref, kv_ref, wfull_ref, dg_ref, du_ref, dd_ref,
    grad_input_out, pack_out, att1_out, att2_out, sh_out, keep_out, other_out,
    wbuf, kv, kvb, kv_x, kv_zo, kv_zi, kv_sum, gst, delta_s, dq,
    ga, ga4, gq, gq4, gkv, gkv4, n_t, m_t, n_all, m_all, pk, pk4,
    a1, a1_x, a1_zo, a1_zi, a1_sum, a2, a2_x, a2_zo, a2_zi, a2_sum, r1, r2,
    sh, sh_zo, sh_zi, sh_sum, sh_chunk, sh_land, r3, po, cb,
    sem, sem_kv, sem_a1, sem_a2, sem_sh, ring_recv, ring_send,
):
    spot = Spot(4)
    sems = Sems(sem)
    rows, width = tok.shape
    pairs = width // PAIR
    shard = width // 4
    loads = [pltpu.make_async_copy(wfull_ref.at[i], wbuf.at[i], sems.new()) for i in (3, 0, 1, 2)]
    loads.insert(1, pltpu.make_async_copy(kv_ref, kv, sems.new()))
    loads.append(pltpu.make_async_copy(dsh_ref, sh, sems.new()))
    for copy in loads:
        copy.start()
    grads = (dg_ref, du_ref, dd_ref)

    def block(ref, w):
        return ref.at[pl.ds(pl.multiple_of(shard * w, 64), shard)]

    mine = []
    for a in range(3):
        for row in range(2):
            mine.append(
                pltpu.make_async_copy(block(grads[a], 2 * row + spot.c), po.at[a, row], sems.new())
            )
            mine[-1].start()
    greet((spot.core, spot.across, spot.corner, spot.column, spot.inner), (spot.mid, spot.outer))
    grad_second = grad_second_ref[...]
    ga[...] = grad_second.astype(BF)
    grads_w = Spread(spot, lambda w: ga, lambda w: ga4.at[w], sems)
    swaps = []
    for a in range(3):
        for row in range(2):
            swaps.append(
                remote(
                    block(grads[a], 2 * row + 1 - spot.c),
                    cb.at[a, row],
                    sems.new(),
                    sems.new(),
                    spot.core,
                )
            )
            swaps[-1].start()
    loads[-1].wait()
    shared = Reduce(spot, sh, None, sh_zo, sh_zi, sem_sh, folded=True)
    for number in (3, 2, 1):
        shared.launch(number)
    mixed = mixed_ref[...]
    n_t[...] = normed_ref[...].T
    m_t[...] = mixed.astype(BF).T

    def columns(ref):
        return lambda w: ref.at[:, pl.ds(pl.multiple_of(rows * w, 128), rows)]

    normed_w = Spread(spot, lambda w: block(n_t, w), columns(n_all), sems)
    mixed_w = Spread(spot, lambda w: block(m_t, w), columns(m_all), sems)
    loads[0].wait()
    grad_mixed = nt(ga[...], wbuf[3]).astype(BF)
    product = grad_mixed.astype(F32) * mixed
    for j in range(pairs):
        lanes = slice(PAIR * j, PAIR * (j + 1))
        gst[j] = stack_pair(grad_mixed[:, lanes])
        delta_s[j] = jnp.broadcast_to(
            jnp.sum(stack_pair(product[:, lanes]), axis=1, keepdims=True), (2 * rows, PAIR)
        )
    dq[...] = jnp.zeros_like(dq)
    loads[1].wait()
    q_block = qb[...]

    def chunk(number):
        plane = spot.plane(number)
        k_block = kb[:, pl.ds(pl.multiple_of(2 * rows * plane, 2 * rows), 2 * rows)]
        allowed = k_block <= q_block

        def one_pair(j, carry):
            lane = pl.multiple_of(PAIR * j, PAIR)
            both = pl.ds(2 * plane, 2)
            key = kv[both, :, pl.ds(lane, PAIR)].reshape(2 * rows, PAIR)
            value = kv[both, :, pl.ds(width + lane, PAIR)].reshape(2 * rows, PAIR)
            query, grad = q_ref[j], gst[j]
            scores = nt(query, key)
            probs = jnp.where(allowed, jnp.exp(scores - lse_ref[j][:, 0:1]), 0.0)
            inner = nt(grad, value) - delta_s[j][:, 0:1]
            grad_scores = (probs * inner * HD**-0.5).astype(BF)
            dq[j] += nn(grad_scores, key)
            grad_key = tn(grad_scores, query) * HD**0.5
            grad_value = tn(probs.astype(BF), grad)
            kvb[both, :, pl.ds(lane, PAIR)] = grad_key.astype(BF).reshape(2, rows, PAIR)
            kvb[both, :, pl.ds(width + lane, PAIR)] = grad_value.astype(BF).reshape(2, rows, PAIR)
            return carry

        lax.fori_loop(0, pairs, one_pair, 0)

    kv_grad = Reduce(spot, kvb, kv_x, kv_zo, kv_zi, sem_kv)
    chunk(3)
    kv_grad.side(3)

    for copy in mine:
        copy.wait()
    across = []
    for a in range(3):
        for row in range(2):
            swaps[2 * a + row].wait_recv()

        def add(i, carry):
            at = pl.ds(pl.multiple_of(16 * i, 16), 16)
            for row in range(2):
                total = po[a, row, at].astype(F32) + cb[a, row, at].astype(F32)
                po[a, row, at] = total.astype(BF)
            return carry

        lax.fori_loop(0, shard // 16, add, 0)
        across.append(
            remote(po.at[a, 1 - spot.y], other_out.at[a], sems.new(), sems.new(), spot.across)
        )
        across[-1].start()
    keeps = [
        pltpu.make_async_copy(po.at[a, spot.y], keep_out.at[a], sems.new()) for a in range(3)
    ]
    for copy in keeps:
        copy.start()

    shared.relay(3)
    chunk(2)
    kv_grad.side(2)
    kv_grad.meet(3)
    kv_grad.launch(3)
    shared.relay(2)
    chunk(1)
    kv_grad.side(1)
    kv_grad.meet(2)
    kv_grad.launch(2)
    kv_grad.relay(3)
    shared.relay(1)
    chunk(0)
    kv_grad.side(0)
    cosine, sine = cosr[...], sinr[...]
    gq[...] = turn(
        jnp.concatenate([unstack_pair(dq[j]) for j in range(pairs)], axis=1), cosine, -sine
    ).astype(BF)
    query_w = Spread(spot, lambda w: gq, lambda w: gq4.at[w], sems)
    shared.last(sh_sum)
    sh_chunk[...] = sh_sum[...].astype(BF)
    part = 2 * shard // 2

    def piece(w):
        return sh_chunk.at[pl.ds(pl.multiple_of(part * w, 64), part)]

    def place(w):
        return r3.at[spot.k, pl.ds(pl.multiple_of(part * w, 64), part)]

    shared_w = Spread(spot, piece, place, sems)
    rest = sh_chunk.shape[0] - 4 * part
    r3[spot.k, pl.ds(4 * part, rest)] = sh_chunk[pl.ds(4 * part, rest)]
    kv_grad.meet(1)
    kv_grad.launch(1)
    kv_grad.relay(2)
    for part_w in (grads_w, normed_w, mixed_w):
        part_w.finish()
    out_grad = nn(m_all[...], ga4[...].reshape(4 * rows, width))
    kv_grad.meet(0)
    kv_grad.relay(1)
    query_w.finish()
    query_grad = nn(n_all[...], gq4[...].reshape(4 * rows, width))
    half = jnp.concatenate([out_grad, query_grad], axis=0).astype(BF)
    a1[...] = half.reshape(a1.shape)
    first = Reduce(spot, a1, a1_x, a1_zo, a1_zi, sem_a1)
    for number in (3, 2, 1, 0):
        first.side(number)
    shared_w.finish()
    ring3 = Ring(spot, r3, ring_recv.at[2], ring_send.at[2])
    ring3.start()
    kv_grad.last(kv_sum)
    gkv[:, 0:width] = turn(kv_sum[:, 0:width], cosine, -sine).astype(BF)
    gkv[:, width : 2 * width] = kv_sum[:, width : 2 * width].astype(BF)
    kv_w = Spread(spot, lambda w: gkv, lambda w: gkv4.at[w], sems)
    for copy in loads[2:5]:
        copy.wait()
    grad_normed = nt(gq[...], wbuf[0]) + nt(gkv[:, 0:width], wbuf[1])
    grad_normed = grad_normed + nt(gkv[:, width : 2 * width], wbuf[2])
    inputs = tok[...].astype(F32)
    scale = lax.rsqrt(jnp.mean(inputs * inputs, axis=-1, keepdims=True) + EPS)
    weighted = grad_normed * pack_ref[0:1]
    mean = jnp.mean(weighted * inputs, axis=-1, keepdims=True)
    grad_input_out[...] = (
        grad_second + scale * weighted - inputs * (scale * scale * scale * mean)
    )
    gain_grad = jnp.sum(grad_normed * inputs * scale, axis=0, keepdims=True)
    pk[...] = jnp.concatenate([gain_grad, pack_grad_ref[1:16]], axis=0)
    pack_w = Spread(spot, lambda w: pk, lambda w: pk4.at[w], sems)
    for number in (3, 2, 1):
        first.meet(number)
        first.launch(number)
    first.meet(0)
    first.relay(3)
    ring3.step(1)
    first.relay(2)
    first.relay(1)
    kv_w.finish()
    pack_w.finish()
    grad_kv = gkv4[...].reshape(4 * rows, 2 * width)
    both = nn(n_all[...], grad_kv)
    both = jnp.concatenate([both[:, 0:width], both[:, width : 2 * width]], axis=0).astype(BF)
    size = both.shape[0] // 8
    extra = (pk4[0] + pk4[1] + pk4[2] + pk4[3]).astype(BF)
    for r in range(8):
        a2[r, 0:size] = both[size * r : size * (r + 1)]
        a2[r, size : size + 16] = extra
    second = Reduce(spot, a2, a2_x, a2_zo, a2_zi, sem_a2)
    for number in (3, 2, 1, 0):
        second.side(number)
    first.last(a1_sum)
    r1[spot.k] = a1_sum[...].astype(BF)
    ring1 = Ring(spot, r1, ring_recv.at[0], ring_send.at[0])
    ring1.start()
    for number in (3, 2, 1):
        second.meet(number)
        second.launch(number)
    second.meet(0)
    ring3.step(2)
    second.relay(3)
    second.relay(2)
    second.relay(1)
    ring3.step(3)
    ring1.step(1)
    second.last(a2_sum)
    r2[spot.k] = a2_sum[0:size].astype(BF)
    ring2 = Ring(spot, r2, ring_recv.at[1], ring_send.at[1])
    ring2.start()
    pack_out[...] = a2_sum[size : size + 16]
    for number in (2, 3):
        ring1.step(number)
    for number in (1, 2, 3):
        ring2.step(number)
    for ring in (ring3, ring1, ring2):
        for number in range(4):
            ring.other(spot.plane(number))
    saves = [
        pltpu.make_async_copy(src, dst, sems.new())
        for src, dst in ((r3, sh_out), (r1, att1_out), (r2, att2_out))
    ]
    for copy in saves:
        copy.start()
    for copy in across:
        copy.wait_recv()
    for copy in swaps + across:
        copy.wait_send()
    for part_w in (grads_w, normed_w, mixed_w, query_w, shared_w, kv_w, pack_w):
        part_w.drain()
    for part_w in (shared, kv_grad, first, second, ring1, ring2, ring3):
        part_w.drain()
    for copy in saves + keeps:
        copy.wait()


def run_backward(
    grad_second, tok, pack, pack_grad, normed, mixed, q, lse, cosr, sinr, kb, qb, dsh, kv, wfull,
    dg, du, dd,
):
    rows, width = tok.shape
    pairs = width // PAIR
    ranks = 8
    shard, hidden = width // 4, dg.shape[1]
    size = 2 * shard // ranks
    tall = dsh.shape[1]
    any_, vm = pl.BlockSpec(memory_space=pl.ANY), pl.BlockSpec(memory_space=VMEM)
    shape = jax.ShapeDtypeStruct

    def low(*dims):
        return VMEM(dims, BF)

    def full(*dims):
        return VMEM(dims, F32)

    dma = pltpu.SemaphoreType.DMA
    return pl.pallas_call(
        backward_kernel,
        out_shape=(
            shape((rows, width), F32),
            shape(pack.shape, F32),
            shape((ranks, size, width), BF),
            shape((ranks, size, width), BF),
            shape((ranks, tall, 128), BF),
            shape((3, shard, hidden), BF),
            shape((3, shard, hidden), BF),
        ),
        in_specs=[vm] * 12 + [any_] * 6,
        out_specs=(vm, vm, any_, any_, any_, any_, any_),
        scratch_shapes=[
            low(4, width, width),
            low(ranks, rows, 2 * width),
            low(ranks, rows, 2 * width),
            low(4, rows, 2 * width),
            low(4, rows, 2 * width),
            low(4, rows, 2 * width),
            full(rows, 2 * width),
            low(pairs, 2 * rows, PAIR),
            full(pairs, 2 * rows, PAIR),
            full(pairs, 2 * rows, PAIR),
            low(rows, width),
            low(4, rows, width),
            low(rows, width),
            low(4, rows, width),
            low(rows, 2 * width),
            low(4, rows, 2 * width),
            low(width, rows),
            low(width, rows),
            low(shard, 4 * rows),
            low(shard, 4 * rows),
            full(16, width),
            full(4, 16, width),
            low(ranks, size, width),
            low(4, size, width),
            low(4, size, width),
            low(4, size, width),
            full(size, width),
            low(ranks, size + 16, width),
            low(4, size + 16, width),
            low(4, size + 16, width),
            low(4, size + 16, width),
            full(size + 16, width),
            low(ranks, size, width),
            low(ranks, size, width),
            low(4, tall, 128),
            low(4, tall, 128),
            low(4, tall, 128),
            full(tall, 128),
            low(tall, 128),
            low(16, 128),
            low(ranks, tall, 128),
            low(3, 2, shard, hidden),
            low(3, 2, shard, hidden),
            dma((112,)),
            dma((5, 4)),
            dma((5, 4)),
            dma((5, 4)),
            dma((5, 4)),
            dma((3, ranks)),
            dma((3, 16)),
        ],
        compiler_params=pltpu.CompilerParams(
            collective_id=3, has_side_effects=True, vmem_limit_bytes=58 * 2**20
        ),
    )(
        grad_second, tok, pack, pack_grad, normed, mixed, q, lse, cosr, sinr, kb, qb, dsh, kv,
        wfull, dg, du, dd,
    )


def contract_product(left, right, left_dim, right_dim):
    return lax.dot_general(
        left, right, (((left_dim,), (right_dim,)), ((), ())), preferred_element_type=jnp.float32
    )


def contract_exact(left, right, left_dim, right_dim):
    return lax.dot_general(
        left,
        right,
        (((left_dim,), (right_dim,)), ((), ())),
        precision=HIGH,
        preferred_element_type=jnp.float32,
    )


def rms_norm(values, gain):
    norm_scale = lax.rsqrt(jnp.mean(values * values, axis=-1, keepdims=True) + EPS)
    return (values * norm_scale * gain, norm_scale)


def rms_back(values, norm_scale, gain, upstream):
    weighted = upstream * gain
    inner_mean = jnp.mean(weighted * values, axis=-1, keepdims=True)
    through = norm_scale * weighted - values * norm_scale * norm_scale * norm_scale * inner_mean
    return (through, jnp.sum(upstream * values * norm_scale, axis=0))


def silu_parts(gate_part):
    sigmoid = jax.nn.sigmoid(gate_part)
    return (gate_part * sigmoid, sigmoid * (1.0 + gate_part * (1.0 - sigmoid)))


def rotate(values, place, sign):
    half_size = HD // 2
    frequency = 10000.0 ** (-jnp.arange(half_size, dtype=jnp.float32) / half_size)
    angles = place.astype(jnp.float32)[:, None] * frequency[None, :]
    cosine = jnp.cos(angles)[:, None, :]
    sine_part = sign * jnp.sin(angles)[:, None, :]
    shaped = values.reshape(values.shape[0], values.shape[1] // HD, 2, half_size)
    first_half = shaped[:, :, 0, :]
    second_half = shaped[:, :, 1, :]
    turned = jnp.stack(
        [
            first_half * cosine - second_half * sine_part,
            second_half * cosine + first_half * sine_part,
        ],
        axis=2,
    )
    return turned.reshape(values.shape)


def places(first_row, row_count, block_deal, rows_dev):
    row_index = first_row + jnp.arange(row_count, dtype=jnp.int32)
    owner_rank = row_index // rows_dev
    inner_row = row_index % rows_dev
    ranks = block_deal.shape[0]
    matches = owner_rank[:, None] == jnp.arange(ranks, dtype=jnp.int32)[None, :]
    paired = jnp.sum(jnp.where(matches, block_deal[None, :], 0), axis=1)
    piece_size = rows_dev // 2
    unit_index = jnp.where(inner_row < piece_size, paired, 2 * ranks - 1 - paired)
    return unit_index * piece_size + inner_row % piece_size


def score_block(query_side, key_rows, key_place):
    query3, query_block = query_side
    key3 = key_rows.reshape(key_rows.shape[0], -1, HD)
    raw_scores = jnp.einsum("qhd,khd->hqk", query3, key3, preferred_element_type=jnp.float32)
    allowed = (key_place // BLK)[None, None, :] <= query_block[None, :, None]
    return (jnp.where(allowed, raw_scores * HD ** (-0.5), MASKED), allowed)


def absorb(running, key_rows, value_rows, key_place, query_side):
    largest, denom, accum = running
    scores, allowed = score_block(query_side, key_rows, key_place)
    new_largest = jnp.maximum(largest, jnp.max(scores, axis=2))
    factor = jnp.exp(largest - new_largest)
    raised = jnp.where(allowed, jnp.exp(scores - new_largest[:, :, None]), 0.0)
    denom = denom * factor + jnp.sum(raised, axis=2)
    value3 = value_rows.reshape(value_rows.shape[0], -1, HD)
    accum = accum * factor.T[:, :, None] + jnp.einsum(
        "hqk,khd->qhd", raised.astype(jnp.bfloat16), value3, preferred_element_type=jnp.float32
    )
    return (new_largest, denom, accum)


def fold_keys(running, key_piece, query_side, block_deal, rows_dev):
    key_all, value_all = key_piece
    row_count = key_all.shape[0]
    block_size = KEY_ROWS

    def key_step(current, offset):
        key_rows = lax.dynamic_slice_in_dim(key_all, offset, block_size, 0)
        value_rows = lax.dynamic_slice_in_dim(value_all, offset, block_size, 0)
        key_place = places(offset, block_size, block_deal, rows_dev)
        return (absorb(current, key_rows, value_rows, key_place, query_side), None)

    offsets = jnp.arange(row_count // block_size, dtype=jnp.int32) * block_size
    running, unused = lax.scan(key_step, running, offsets)
    return running


def differentiate(query_side, log_total, delta, grad_out3, key_rows, value_rows, key_place):
    scores, allowed = score_block(query_side, key_rows, key_place)
    probs_full = jnp.where(allowed, jnp.exp(scores - log_total[:, :, None]), 0.0)
    value3 = value_rows.reshape(value_rows.shape[0], -1, HD)
    grad_probs = jnp.einsum("qhd,khd->hqk", grad_out3, value3, preferred_element_type=jnp.float32)
    grad_scores = (probs_full * (grad_probs - delta[:, :, None]) * HD ** (-0.5)).astype(
        jnp.bfloat16
    )
    return (probs_full, grad_scores)


def assign_slots(route, order, experts, capacity):
    pair_count = order.shape[0]
    expert_ids = route.reshape(pair_count)
    ordered = expert_ids[order]
    onehot = (ordered[:, None] == jnp.arange(experts, dtype=jnp.int32)[None, :]).astype(jnp.int32)
    before = jnp.cumsum(onehot, axis=0) - onehot
    slot_turn = jnp.sum(before * onehot, axis=1)
    slot_index = jnp.zeros((pair_count,), jnp.int32).at[order].set(slot_turn)
    kept_pairs = slot_index < capacity
    target = jnp.where(kept_pairs, expert_ids * capacity + slot_index, experts * capacity)
    slot_table = (
        jnp.full((experts * capacity,), pair_count, jnp.int32)
        .at[target]
        .set(jnp.arange(pair_count, dtype=jnp.int32), mode="drop")
    )
    return (target, kept_pairs, slot_table)


def body(
    tokens,
    cotangent,
    gain_attention,
    query_weight,
    key_weight,
    value_weight,
    output_weight,
    gain_mixer,
    router_weight,
    shared_gate,
    shared_up,
    shared_down,
    expert_gate,
    expert_up,
    expert_down,
    routes,
    slot_order,
    block_deal,
):
    rows_dev = tokens.shape[1]
    width = tokens.shape[2]
    ranks = lax.axis_size("ctx")
    (
        gain_one,
        query_full,
        key_full,
        value_full,
        output_full,
        gain_two,
        router_full,
        sgate_full,
        sup_full,
        sdown_full,
        expert_gate_whole,
        expert_up_whole,
        edown_full,
    ) = (
        lax.all_gather(gain_attention, "wt", axis=0, tiled=True),
        lax.all_gather(query_weight, "wt", axis=0, tiled=True),
        lax.all_gather(key_weight, "wt", axis=0, tiled=True),
        lax.all_gather(value_weight, "wt", axis=0, tiled=True),
        lax.all_gather(output_weight, "wt", axis=0, tiled=True),
        lax.all_gather(gain_mixer, "wt", axis=0, tiled=True),
        lax.all_gather(router_weight, "wt", axis=0, tiled=True),
        lax.all_gather(shared_gate, "wt", axis=0, tiled=True),
        lax.all_gather(shared_up, "wt", axis=0, tiled=True),
        lax.all_gather(shared_down, "wt", axis=0, tiled=True),
        lax.all_gather(expert_gate, "wt", axis=0, tiled=True),
        lax.all_gather(expert_up, "wt", axis=0, tiled=True),
        lax.all_gather(expert_down, "wt", axis=0, tiled=True),
    )
    gain_first = gain_one.astype(jnp.float32)
    gain_second = gain_two.astype(jnp.float32)
    heads = width // HD
    inputs = tokens[0].astype(jnp.float32)
    here = places(lax.axis_index("ctx") * rows_dev, rows_dev, block_deal, rows_dev)
    query_side_block = here // BLK
    normed_f, scale_one = rms_norm(inputs, gain_first)
    normed = normed_f.astype(jnp.bfloat16)
    query_rot = rotate(
        jnp.dot(normed, query_full, preferred_element_type=jnp.float32), here, 1.0
    ).astype(jnp.bfloat16)
    key_rot = rotate(
        jnp.dot(normed, key_full, preferred_element_type=jnp.float32), here, 1.0
    ).astype(jnp.bfloat16)
    value_low = jnp.dot(normed, value_full, preferred_element_type=jnp.float32).astype(jnp.bfloat16)
    query3 = query_rot.reshape(rows_dev, heads, HD)
    query_side = (query3, query_side_block)
    start_state = (
        jnp.full((heads, rows_dev), MASKED, jnp.float32),
        jnp.zeros((heads, rows_dev), jnp.float32),
        jnp.zeros((rows_dev, heads, HD), jnp.float32),
    )
    largest, denom, accum = fold_keys(
        start_state,
        (
            lax.all_gather(key_rot, "ctx", axis=0, tiled=True),
            lax.all_gather(value_low, "ctx", axis=0, tiled=True),
        ),
        query_side,
        block_deal,
        rows_dev,
    )
    mixed3 = accum / denom.T[:, :, None]
    log_total = largest + jnp.log(denom)
    mixed_low = mixed3.reshape(rows_dev, width).astype(jnp.bfloat16)
    second = inputs + jnp.dot(mixed_low, output_full, preferred_element_type=jnp.float32)
    mixer_f, scale_two = rms_norm(second, gain_second)
    mixer = mixer_f.astype(jnp.bfloat16)
    experts = router_full.shape[1]
    logits = jnp.dot(mixer, router_full, preferred_element_type=jnp.float32)
    route = routes[0]
    top_count = route.shape[1]
    pair_count = rows_dev * top_count
    capacity = (5 * pair_count + 4 * experts - 1) // (4 * experts)
    split_count = ranks // experts
    expert_match = route[:, :, None] == jnp.arange(experts, dtype=jnp.int32)[None, None, :]
    chosen = jnp.sum(jnp.where(expert_match, logits[:, None, :], 0.0), axis=2)
    gates = jax.nn.softmax(chosen, axis=1)
    target, kept_pairs, slot_table = assign_slots(route, slot_order[0, 0], experts, capacity)
    valid = slot_table < pair_count
    pair_pick = jnp.minimum(slot_table, pair_count - 1)
    target_pick = jnp.minimum(target, experts * capacity - 1)
    send_rows = jnp.where(
        valid[:, None], mixer[pair_pick // top_count], jnp.zeros((), jnp.bfloat16)
    )
    send_rows = jnp.broadcast_to(
        send_rows.reshape(experts, 1, capacity, width), (experts, split_count, capacity, width)
    ).reshape(ranks, capacity, width)
    received = lax.all_to_all(send_rows, "ctx", split_axis=0, concat_axis=0, tiled=True)
    slot_count = received.shape[1]
    flattened_input = received.reshape(ranks * slot_count, width)
    gate_part = jnp.dot(flattened_input, expert_gate_whole, preferred_element_type=jnp.float32)
    up_projection_part = jnp.dot(
        flattened_input, expert_up_whole, preferred_element_type=jnp.float32
    )
    activated, unused = silu_parts(gate_part)
    hidden = (activated * up_projection_part).astype(jnp.bfloat16)
    partial_value = contract_product(hidden, edown_full, 1, 1).reshape(ranks, slot_count, width)
    back = lax.all_to_all(
        partial_value.astype(jnp.bfloat16), "ctx", split_axis=0, concat_axis=0, tiled=True
    ).astype(partial_value.dtype)
    expert_gate_part = gate_part.reshape(ranks, slot_count, -1)
    expert_up_part = up_projection_part.reshape(ranks, slot_count, -1)
    combined = jnp.sum(back.reshape(experts, split_count, capacity, width), axis=1).reshape(
        experts * capacity, width
    )
    pair_out = jnp.where(kept_pairs[:, None], combined[target_pick], 0.0).reshape(
        rows_dev, top_count, width
    )
    mixture = jnp.sum(gates[:, :, None] * pair_out, axis=1)
    sgate_part = jnp.dot(mixer, sgate_full, preferred_element_type=jnp.float32)
    sup_part = jnp.dot(mixer, sup_full, preferred_element_type=jnp.float32)
    shared_act, shared_slope = silu_parts(sgate_part)
    shared_hidden = (shared_act * sup_part).astype(jnp.bfloat16)
    shared_out = jnp.dot(shared_hidden, sdown_full, preferred_element_type=jnp.float32)
    result = (second + mixture + shared_out).astype(jnp.bfloat16)
    grad_final = cotangent[0].astype(jnp.float32)
    grad_low = grad_final.astype(jnp.bfloat16)
    sdown_grad = contract_product(shared_hidden, grad_low, 0, 0)
    grad_shared_hidden = contract_product(grad_low, sdown_full, 1, 1)
    grad_sgate = (grad_shared_hidden * sup_part * shared_slope).astype(jnp.bfloat16)
    grad_sup = (grad_shared_hidden * shared_act).astype(jnp.bfloat16)
    sgate_grad = contract_product(mixer, grad_sgate, 0, 0)
    sup_grad = contract_product(mixer, grad_sup, 0, 0)
    grad_mixer = contract_product(grad_sgate, sgate_full, 1, 1) + contract_product(
        grad_sup, sup_full, 1, 1
    )
    pair_grad = (
        (gates[:, :, None] * grad_final[:, None, :]).reshape(pair_count, width).astype(jnp.bfloat16)
    )
    grad_gates = jnp.sum(grad_final[:, None, :] * pair_out, axis=2)
    send_grad = jnp.where(valid[:, None], pair_grad[pair_pick], jnp.zeros((), jnp.bfloat16))
    send_grad = jnp.broadcast_to(
        send_grad.reshape(experts, 1, capacity, width), (experts, split_count, capacity, width)
    ).reshape(ranks, capacity, width)
    recv_grad = lax.all_to_all(send_grad, "ctx", split_axis=0, concat_axis=0, tiled=True)
    flattened_input = received.reshape(ranks * capacity, width)
    flat_grad = recv_grad.reshape(ranks * capacity, width)
    gate_flat = expert_gate_part.reshape(ranks * capacity, -1)
    up_flat = expert_up_part.reshape(ranks * capacity, -1)
    expert_activation, expert_slope = silu_parts(gate_flat)
    expert_hidden = (expert_activation * up_flat).astype(jnp.bfloat16)
    edown_grad = contract_product(flat_grad, expert_hidden, 0, 0)
    expert_hidden_grad = jnp.dot(flat_grad, edown_full, preferred_element_type=jnp.float32)
    expert_gate_grad_rows = (expert_hidden_grad * up_flat * expert_slope).astype(jnp.bfloat16)
    expert_up_grad_rows = (expert_hidden_grad * expert_activation).astype(jnp.bfloat16)
    egate_grad = contract_product(flattened_input, expert_gate_grad_rows, 0, 0)
    expert_up_weight_grad = contract_product(flattened_input, expert_up_grad_rows, 0, 0)
    input_back = (
        contract_product(expert_gate_grad_rows, expert_gate_whole, 1, 1)
        + contract_product(expert_up_grad_rows, expert_up_whole, 1, 1)
    ).reshape(ranks, capacity, width)
    back_grad = lax.all_to_all(
        input_back.astype(jnp.bfloat16), "ctx", split_axis=0, concat_axis=0, tiled=True
    ).astype(input_back.dtype)
    merged = jnp.sum(back_grad.reshape(experts, split_count, capacity, width), axis=1).reshape(
        experts * capacity, width
    )
    pair_back = jnp.where(kept_pairs[:, None], merged[target_pick], 0.0).reshape(
        rows_dev, top_count, width
    )
    grad_mixer = grad_mixer + jnp.sum(pair_back, axis=1)
    grad_chosen = gates * (grad_gates - jnp.sum(gates * grad_gates, axis=1, keepdims=True))
    grad_logits = jnp.sum(jnp.where(expert_match, grad_chosen[:, :, None], 0.0), axis=1)
    router_grad = contract_exact(mixer.astype(jnp.float32), grad_logits, 0, 0)
    grad_mixer = grad_mixer + contract_exact(grad_logits, router_full.astype(jnp.float32), 1, 1)
    through_two, gain_two_grad = rms_back(second, scale_two, gain_second, grad_mixer)
    grad_second = grad_final + through_two
    grad_attention = grad_second.astype(jnp.bfloat16)
    output_grad = contract_product(mixed_low, grad_attention, 0, 0)
    grad_mixed = contract_product(grad_attention, output_full, 1, 1).astype(jnp.bfloat16)
    grad_out3 = grad_mixed.reshape(rows_dev, heads, HD)
    delta = jnp.sum(grad_out3.astype(jnp.float32) * mixed3, axis=2).T
    all_keys, all_values = (
        lax.all_gather(key_rot, "ctx", axis=0, tiled=True),
        lax.all_gather(value_low, "ctx", axis=0, tiled=True),
    )
    total_rows = all_keys.shape[0]
    block_size = KEY_ROWS

    def query_step(grad_sum, offset):
        key_rows = lax.dynamic_slice_in_dim(all_keys, offset, block_size, 0)
        value_rows = lax.dynamic_slice_in_dim(all_values, offset, block_size, 0)
        key_place = places(offset, block_size, block_deal, rows_dev)
        unused, grad_scores = differentiate(
            query_side, log_total, delta, grad_out3, key_rows, value_rows, key_place
        )
        key3 = key_rows.reshape(block_size, heads, HD)
        return (
            grad_sum
            + jnp.einsum("hqk,khd->qhd", grad_scores, key3, preferred_element_type=jnp.float32),
            None,
        )

    offsets = jnp.arange(total_rows // block_size, dtype=jnp.int32) * block_size
    grad_query3, unused = lax.scan(
        query_step, jnp.zeros((rows_dev, heads, HD), jnp.float32), offsets
    )
    inner_size = KEY_ROWS

    def one_part(offset):
        key_rows = lax.dynamic_slice_in_dim(all_keys, offset, inner_size, 0)
        value_rows = lax.dynamic_slice_in_dim(all_values, offset, inner_size, 0)
        key_place = places(offset, inner_size, block_deal, rows_dev)
        probs_full, grad_scores = differentiate(
            query_side, log_total, delta, grad_out3, key_rows, value_rows, key_place
        )
        grad_value_rows = jnp.einsum(
            "hqk,qhd->khd",
            probs_full.astype(jnp.bfloat16),
            grad_out3,
            preferred_element_type=jnp.float32,
        )
        grad_key_rows = jnp.einsum(
            "hqk,qhd->khd", grad_scores, query3, preferred_element_type=jnp.float32
        )
        return jnp.concatenate(
            [grad_key_rows.reshape(inner_size, width), grad_value_rows.reshape(inner_size, width)],
            axis=1,
        )

    parts = lax.map(
        one_part,
        jnp.arange(lax.axis_size("ctx") * rows_dev // inner_size, dtype=jnp.int32) * inner_size,
    )
    key_value_grad = lax.psum_scatter(
        parts.reshape(lax.axis_size("ctx") * rows_dev, 2 * width),
        "ctx",
        scatter_dimension=0,
        tiled=True,
    )
    grad_key_pre = rotate(key_value_grad[:, :width], here, -1.0).astype(jnp.bfloat16)
    grad_value_low = key_value_grad[:, width:].astype(jnp.bfloat16)
    grad_query_pre = rotate(grad_query3.reshape(rows_dev, width), here, -1.0).astype(jnp.bfloat16)
    query_grad = contract_product(normed, grad_query_pre, 0, 0)
    key_grad = contract_product(normed, grad_key_pre, 0, 0)
    value_grad = contract_product(normed, grad_value_low, 0, 0)
    grad_normed = (
        contract_product(grad_query_pre, query_full, 1, 1)
        + contract_product(grad_key_pre, key_full, 1, 1)
        + contract_product(grad_value_low, value_full, 1, 1)
    )
    through_one, gain_one_grad = rms_back(inputs, scale_one, gain_first, grad_normed)
    grad_input = grad_second + through_one
    (
        gain_one_share,
        query_share,
        key_share,
        value_share,
        output_share,
        gain_two_share,
        router_share,
        sgate_share,
        sup_share,
        sdown_share,
        egate_share,
        expert_up_portion,
        edown_share,
    ) = (
        lax.psum_scatter(
            gain_one_grad.astype(jnp.bfloat16), "wt", scatter_dimension=0, tiled=True
        ).astype(jnp.float32),
        lax.psum_scatter(
            query_grad.astype(jnp.bfloat16), "wt", scatter_dimension=0, tiled=True
        ).astype(jnp.float32),
        lax.psum_scatter(
            key_grad.astype(jnp.bfloat16), "wt", scatter_dimension=0, tiled=True
        ).astype(jnp.float32),
        lax.psum_scatter(
            value_grad.astype(jnp.bfloat16), "wt", scatter_dimension=0, tiled=True
        ).astype(jnp.float32),
        lax.psum_scatter(
            output_grad.astype(jnp.bfloat16), "wt", scatter_dimension=0, tiled=True
        ).astype(jnp.float32),
        lax.psum_scatter(
            gain_two_grad.astype(jnp.bfloat16), "wt", scatter_dimension=0, tiled=True
        ).astype(jnp.float32),
        lax.psum_scatter(
            router_grad.astype(jnp.bfloat16), "wt", scatter_dimension=0, tiled=True
        ).astype(jnp.float32),
        lax.psum_scatter(
            sgate_grad.astype(jnp.bfloat16), "wt", scatter_dimension=0, tiled=True
        ).astype(jnp.float32),
        lax.psum_scatter(
            sup_grad.astype(jnp.bfloat16), "wt", scatter_dimension=0, tiled=True
        ).astype(jnp.float32),
        lax.psum_scatter(
            sdown_grad.astype(jnp.bfloat16), "wt", scatter_dimension=0, tiled=True
        ).astype(jnp.float32),
        lax.psum_scatter(
            egate_grad.astype(jnp.bfloat16), "wt", scatter_dimension=0, tiled=True
        ).astype(jnp.float32),
        lax.psum_scatter(
            expert_up_weight_grad.astype(jnp.bfloat16), "wt", scatter_dimension=0, tiled=True
        ).astype(jnp.float32),
        lax.psum_scatter(
            edown_grad.astype(jnp.bfloat16), "wt", scatter_dimension=0, tiled=True
        ).astype(jnp.float32),
    )
    (
        gain_one_sum,
        query_sum,
        key_sum,
        value_sum,
        output_sum,
        gain_two_sum,
        router_sum,
        sgate_sum,
        sup_sum,
        sdown_sum,
    ) = lax.psum(
        (
            gain_one_share,
            query_share,
            key_share,
            value_share,
            output_share,
            gain_two_share,
            router_share,
            sgate_share,
            sup_share,
            sdown_share,
        ),
        "ctx",
    )
    return (
        result[None],
        grad_input[None],
        gain_one_sum,
        query_sum,
        key_sum,
        value_sum,
        output_sum,
        gain_two_sum,
        router_sum,
        sgate_sum,
        sup_sum,
        sdown_sum,
        egate_share,
        expert_up_portion,
        edown_share,
    )


def fast_body(
    tokens,
    cotangent,
    gain_attention,
    query_weight,
    key_weight,
    value_weight,
    output_weight,
    gain_mixer,
    router_weight,
    shared_gate,
    shared_up,
    shared_down,
    expert_gate,
    expert_up,
    expert_down,
    routes,
    slot_order,
    block_deal,
):
    rows_dev, width = tokens.shape[1:]
    ranks = lax.axis_size("ctx")
    shard = width // 4
    here, cosr, sinr = angles_of(block_deal, rows_dev)
    kb = (places(0, ranks * rows_dev, block_deal, rows_dev) // BLK)[None, :]
    qb = jnp.concatenate([here // BLK] * 2)[:, None]
    pack = pack_params(gain_attention, gain_mixer, router_weight)
    (
        q_st, kv_all, mixed, lse, second, mixer, normed, pack_all, wfull, sg_part, su_part,
        eg_full, eu_full, cot4,
    ) = run_forward(
        tokens[0], pack, cosr, sinr, kb, qb, cotangent[0], query_weight, key_weight,
        value_weight, output_weight, shared_gate, shared_up, expert_gate, expert_up,
    )
    route = routes[0]
    top_count = route.shape[1]
    by_choice = route.T.reshape(1, rows_dev * top_count)
    turns = slot_order[0, 0]
    turns = lax.rem(turns, top_count) * rows_dev + lax.div(turns, top_count)
    result, grad_second, pack_grad, dsh, dg, du, dd = run_experts(
        second, mixer, pack_all, cotangent[0], route, by_choice, by_choice.reshape(-1, 1),
        turns[None, :], turns[:, None], shared_down, sg_part, su_part, cot4, eg_full, eu_full,
        expert_down,
    )
    grad_input, pack_sum, att1, att2, sh, keep, other = run_backward(
        grad_second, tokens[0], pack_all, pack_grad, normed, mixed, q_st, lse, cosr, sinr, kb, qb,
        dsh, kv_all, wfull, dg, du, dd,
    )
    att1 = att1.reshape(2 * shard, width).astype(F32)
    att2 = att2.reshape(2 * shard, width).astype(F32)
    mine = lax.dynamic_slice(
        pack_sum, (0, lax.axis_index("wt") * shard), (pack_sum.shape[0], shard)
    )
    both = sh[:, :width].reshape(2, 4, 4, 2, shard // 2, 128)
    both = both.transpose(3, 0, 4, 2, 1, 5).reshape(2, shard, shared_gate.shape[1]).astype(F32)
    down = sh[:, width:].reshape(ranks, width // 128, -1, 128).transpose(0, 2, 1, 3)
    down = down.reshape(shared_down.shape).astype(F32)
    sums = [keep[a].astype(F32) + other[a].astype(F32) for a in range(3)]
    return (
        result[None],
        grad_input[None],
        mine[0],
        att1[shard:],
        att2[:shard],
        att2[shard:],
        att1[:shard],
        mine[1],
        mine[2 : 2 + router_weight.shape[1]].T,
        both[0],
        both[1],
        down,
        sums[0],
        sums[1],
        sums[2],
    )


def solution(mesh):
    in_specs = (
        P("wt", "ctx", None),
        P("wt", "ctx", None),
        P("wt"),
        P("wt", None),
        P("wt", None),
        P("wt", None),
        P("wt", None),
        P("wt"),
        P("wt", None),
        P("wt", None),
        P("wt", None),
        P("wt", None),
        P("wt", "ctx"),
        P("wt", "ctx"),
        P("wt", "ctx"),
        P("wt", "ctx", None),
        P("wt", "ctx", None),
        P(),
    )
    out_specs = (
        P("wt", "ctx", None),
        P("wt", "ctx", None),
        P("wt"),
        P("wt", None),
        P("wt", None),
        P("wt", None),
        P("wt", None),
        P("wt"),
        P("wt", None),
        P("wt", None),
        P("wt", None),
        P("wt", None),
        P("wt", "ctx"),
        P("wt", "ctx"),
        P("wt", "ctx"),
    )
    chosen = fast_body if (mesh.shape["ctx"], mesh.shape["wt"]) == (8, 4) else body
    return jax.shard_map(chosen, mesh=mesh, in_specs=in_specs, out_specs=out_specs, check_vma=False)
```

```python
import jax
import jax.numpy as jnp
from jax import lax
from jax.experimental import pallas as pl
from jax.experimental.pallas import tpu as pltpu
from jax.sharding import PartitionSpec as P

HD = 64
BLK = 256


EPS = 1e-06
KEY_ROWS = 512
HIGH = lax.Precision.HIGHEST
MASKED = -1e30


MESH = pl.DeviceIdType.MESH
VMEM = pltpu.VMEM
BF = jnp.bfloat16
F32 = jnp.float32
PAIR = 2 * HD
VMEM_BYTES = 63 * 2**20


class Spot:
    def __init__(self, line_size):
        self.k = lax.axis_index("ctx")
        self.w = lax.axis_index("wt")
        self.z, self.x = lax.div(self.k, 2), lax.rem(self.k, 2)
        self.y, self.c = lax.div(self.w, 2), lax.rem(self.w, 2)
        self.far = lax.div(self.z, 2)
        self.mid = self.z + self.far * (3 - 2 * self.z)
        step = 1 - 2 * self.far
        self.core = (self.k, 2 * self.y + 1 - self.c)
        self.across = (self.k, 2 * (1 - self.y) + self.c)
        self.corner = (self.k, 2 * (1 - self.y) + 1 - self.c)
        self.column = (2 * self.z + 1 - self.x, self.w)
        self.inner = (2 * (self.z + step) + self.x, self.w)
        self.outer = (2 * (self.z - step) + self.x, self.w)

    def plane(self, step):
        mirrored = (self.mid, 1 - self.mid, 2, 3)[step]
        return mirrored + self.far * (3 - 2 * mirrored)


class Sems:
    def __init__(self, ref):
        self.ref, self.used = ref, 0

    def new(self):
        self.used += 1
        return self.ref.at[self.used - 1]


def remote(src, dst, send, recv, to):
    return pltpu.make_async_remote_copy(
        src_ref=src, dst_ref=dst, send_sem=send, recv_sem=recv, device_id=to, device_id_type=MESH
    )


def greet(devices, middle=None):
    barrier = pltpu.get_barrier_semaphore()
    for to in devices:
        pl.semaphore_signal(barrier, inc=1, device_id=to, device_id_type=MESH)
    if middle is None:
        pl.semaphore_wait(barrier, len(devices))
        return

    @pl.when(middle[0] == 1)
    def _():
        pl.semaphore_signal(barrier, inc=1, device_id=middle[1], device_id_type=MESH)

    pl.semaphore_wait(barrier, len(devices) + middle[0])


class Gather:
    def __init__(self, spot, src, dst, sems):
        self.spot, self.dst, self.sems = spot, dst, sems
        self.rows = src.shape[0]
        here = self.block(spot.w)
        self.local = pltpu.make_async_copy(src, here, sems.new())
        self.to_core = remote(src, here, sems.new(), sems.new(), spot.core)
        self.to_across = remote(src, here, sems.new(), sems.new(), spot.across)
        for copy in (self.to_across, self.to_core, self.local):
            copy.start()

    def block(self, w):
        return self.dst.at[pl.ds(pl.multiple_of(self.rows * w, 64), self.rows)]

    def forward(self):
        self.to_across.wait_recv()
        part = self.block(self.spot.across[1])
        self.onward = remote(part, part, self.sems.new(), self.sems.new(), self.spot.core)
        self.onward.start()

    def finish(self):
        self.local.wait()
        self.to_core.wait_recv()
        self.onward.wait_recv()

    def drain(self):
        self.to_core.wait_send()
        self.to_across.wait_send()
        self.onward.wait_send()


class Share:
    def __init__(self, spot, src, dst, sems):
        self.spot, self.dst, self.sems = spot, dst, sems
        self.rows = src.shape[0]
        self.half = self.rows // 2
        here = self.block(spot.w)
        half = pl.ds(pl.multiple_of(self.half * spot.x, 32), self.half)
        self.local = pltpu.make_async_copy(src, here, sems.new())
        self.to_core = remote(src, here, sems.new(), sems.new(), spot.core)
        self.to_across = remote(
            src.at[half], self.part(spot.w, spot.x), sems.new(), sems.new(), spot.across
        )
        for copy in (self.to_across, self.to_core, self.local):
            copy.start()

    def block(self, w):
        return self.dst.at[pl.ds(pl.multiple_of(self.rows * w, 64), self.rows)]

    def part(self, w, x):
        return self.dst.at[pl.ds(pl.multiple_of(self.rows * w + self.half * x, 32), self.half)]

    def forward(self):
        spot = self.spot
        self.to_across.wait_recv()
        part = self.part(spot.across[1], spot.x)
        self.aside = remote(part, part, self.sems.new(), self.sems.new(), spot.column)
        self.onward = remote(part, part, self.sems.new(), self.sems.new(), spot.core)
        self.aside.start()
        self.onward.start()

    def second(self):
        self.aside.wait_recv()
        part = self.part(self.spot.across[1], 1 - self.spot.x)
        self.rest = remote(part, part, self.sems.new(), self.sems.new(), self.spot.core)
        self.rest.start()

    def finish(self):
        self.local.wait()
        self.to_core.wait_recv()
        self.onward.wait_recv()
        self.rest.wait_recv()

    def drain(self):
        for copy in (self.to_core, self.to_across, self.aside, self.onward, self.rest):
            copy.wait_send()


class Spread:
    def __init__(self, spot, pick, place, sems, local=True):
        self.copies = []
        for to in (spot.across, spot.corner, spot.core):
            self.copies.append(remote(pick(to[1]), place(spot.w), sems.new(), sems.new(), to))
        self.local = None
        if local:
            self.local = pltpu.make_async_copy(pick(spot.w), place(spot.w), sems.new())
        for copy in self.copies:
            copy.start()
        if local:
            self.local.start()

    def finish(self):
        for copy in self.copies:
            copy.wait_recv()
        if self.local is not None:
            self.local.wait()

    def drain(self):
        for copy in self.copies:
            copy.wait_send()


def nt(left, right):
    return lax.dot_general(left, right, (((1,), (1,)), ((), ())), preferred_element_type=F32)


def nn(left, right):
    return jnp.dot(left, right, preferred_element_type=F32)


def tn(left, right):
    return lax.dot_general(left, right, (((0,), (0,)), ((), ())), preferred_element_type=F32)


def turn(values, cosine, sine):
    wide = values.shape[1]
    lane = lax.broadcasted_iota(jnp.int32, values.shape, 1)
    first = lax.rem(lane, HD) < HD // 2
    swapped = jnp.where(
        first, pltpu.roll(values, wide - HD // 2, 1), pltpu.roll(values, HD // 2, 1)
    )
    copies = wide // PAIR
    cosine = jnp.concatenate([cosine] * copies, axis=1)
    sine = jnp.concatenate([sine] * copies, axis=1)
    return values * cosine + swapped * sine


def stack_pair(values):
    lane = lax.broadcasted_iota(jnp.int32, values.shape, 1)
    none = jnp.zeros_like(values)
    return jnp.concatenate(
        [jnp.where(lane < HD, values, none), jnp.where(lane < HD, none, values)], axis=0
    )


def unstack_pair(values):
    rows = values.shape[0] // 2
    lane = lax.broadcasted_iota(jnp.int32, (rows, PAIR), 1)
    return jnp.where(lane < HD, values[:rows], values[rows:])


class Ring:
    def __init__(self, spot, blocks, recv, send, parts=1):
        self.spot, self.blocks, self.recv, self.send, self.parts = spot, blocks, recv, send, parts
        self.ranks = blocks.shape[0]
        self.used = 0
        self.sent, self.sent_mid = [], []

    def piece(self, slot, part):
        rows = self.blocks.shape[1] // self.parts
        return self.blocks.at[slot, pl.ds(rows * part, rows)]

    def copy(self, slot, part, to):
        self.used += 1
        return remote(
            self.piece(slot, part),
            self.piece(slot, part),
            self.send.at[self.used - 1],
            self.recv.at[slot + self.ranks * part],
            to,
        )

    def arrived(self, slot, part):
        remote(
            self.piece(slot, part),
            self.piece(slot, part),
            self.send.at[0],
            self.recv.at[slot + self.ranks * part],
            self.spot.column,
        ).wait_recv()

    def start(self):
        spot = self.spot
        for part in range(self.parts):
            own = self.copy(spot.k, part, spot.inner)
            side = self.copy(spot.k, part, spot.column)
            back = self.copy(spot.k, part, spot.outer)
            own.start()
            self.middle(back)
            side.start()
            self.sent += [own, side]
            self.sent_mid += [back]

    def middle(self, copy):
        @pl.when(self.spot.mid == 1)
        def _():
            copy.start()

    def step(self, number):
        spot = self.spot
        slot = 2 * spot.plane(number) + spot.x
        for part in range(self.parts):
            self.arrived(slot, part)
            along = self.copy(slot, part, spot.inner if number == 1 else spot.outer)
            self.middle(along)
            side = self.copy(slot, part, spot.column)
            side.start()
            self.sent += [side]
            self.sent_mid += [along]

    def other(self, number):
        for part in range(self.parts):
            self.arrived(2 * self.spot.plane(number) + 1 - self.spot.x, part)

    def drain(self):
        for copy in self.sent:
            copy.wait_send()

        @pl.when(self.spot.mid == 1)
        def _():
            for copy in self.sent_mid:
                copy.wait_send()


class Reduce:
    def __init__(self, spot, part, sides, zo, zi, sems, folded=False, parts=1):
        self.spot, self.part, self.sides, self.zo, self.zi = spot, part, sides, zo, zi
        self.x_send, self.x_recv, self.z_send, self.zo_recv, self.zi_recv = (
            sems.at[i] for i in range(5)
        )
        self.folded, self.parts = folded, parts
        self.rows = part.shape[1] // parts
        self.sent, self.sent_end, self.sent_mid = [], [], []

    def cut(self, ref, index, h):
        return ref.at[index, pl.ds(self.rows * h, self.rows)]

    def own(self, plane, h):
        return self.cut(self.part, plane if self.folded else 2 * plane + self.spot.x, h)

    def wait(self, land, recv, plane, h):
        piece = self.cut(land, plane, h)
        at = plane + 4 * h
        remote(piece, piece, self.z_send.at[at], recv.at[at], self.spot.column).wait_recv()

    def side(self, number):
        spot = self.spot
        plane = spot.plane(number)
        for h in range(self.parts):
            at = plane + 4 * h
            copy = remote(
                self.cut(self.part, 2 * plane + 1 - spot.x, h),
                self.cut(self.sides, plane, h),
                self.x_send.at[at],
                self.x_recv.at[at],
                spot.column,
            )
            copy.start()
            self.sent.append(copy)

    def add(self, ref, land):
        ref[...] = (ref[...].astype(F32) + land[...].astype(F32)).astype(BF)

    def meet(self, number):
        plane = self.spot.plane(number)
        for h in range(self.parts):
            self.wait(self.sides, self.x_recv, plane, h)
            self.add(self.own(plane, h), self.cut(self.sides, plane, h))
            if number > 0 and self.zo is not None:
                self.launch_part(number, h)

    def launch(self, number):
        for h in range(self.parts):
            self.launch_part(number, h)

    def launch_part(self, number, h):
        plane = self.spot.plane(number)
        at = plane + 4 * h
        copy = remote(
            self.own(plane, h),
            self.cut(self.zo, plane, h),
            self.z_send.at[at],
            self.zo_recv.at[at],
            self.spot.inner,
        )

        @pl.when(self.spot.mid == 0)
        def _():
            copy.start()

        self.sent_end.append(copy)

    def relay(self, number):
        plane = self.spot.plane(number)
        land, recv = (self.zi, self.zi_recv) if number == 1 else (self.zo, self.zo_recv)
        copies = []
        for h in range(self.parts):
            at = plane + 4 * h
            copies.append(
                remote(
                    self.own(plane, h),
                    self.cut(self.zi, plane, h),
                    self.z_send.at[at],
                    self.zi_recv.at[at],
                    self.spot.outer if number == 1 else self.spot.inner,
                )
            )

        @pl.when(self.spot.mid == 1)
        def _():
            for h, copy in enumerate(copies):
                self.wait(land, recv, plane, h)
                self.add(self.own(plane, h), self.cut(land, plane, h))
                copy.start()

        self.sent_mid += copies

    def last(self, result):
        plane = self.spot.plane(0)
        for h in range(self.parts):
            self.wait(self.zi, self.zi_recv, plane, h)
            rows = pl.ds(self.rows * h, self.rows)
            total = self.own(plane, h)[...].astype(F32)
            result[rows] = total + self.cut(self.zi, plane, h)[...].astype(F32)

        @pl.when(self.spot.mid == 1)
        def _():
            for h in range(self.parts):
                self.wait(self.zo, self.zo_recv, plane, h)
                rows = pl.ds(self.rows * h, self.rows)
                result[rows] += self.cut(self.zo, plane, h)[...].astype(F32)

    def drain(self):
        for copy in self.sent:
            copy.wait_send()

        @pl.when(self.spot.mid == 0)
        def _():
            for copy in self.sent_end:
                copy.wait_send()

        @pl.when(self.spot.mid == 1)
        def _():
            for copy in self.sent_mid:
                copy.wait_send()


def swish(values):
    sigmoid = 1.0 / (1.0 + jnp.exp(-values))
    return values * sigmoid, sigmoid * (1.0 + values * (1.0 - sigmoid))


class Exchange:
    def __init__(self, spot, out, back, send, recv):
        self.spot, self.out, self.back = spot, out, back
        self.send, self.recv, self.ranks = send, recv, out.shape[0]
        self.copies = []

    def start(self):
        spot = self.spot
        for offset in range(1, self.ranks):
            peer = lax.rem(spot.k + offset, self.ranks)
            self.copies.append(
                remote(
                    self.out.at[peer],
                    self.back.at[spot.k],
                    self.send.at[offset],
                    self.recv.at[spot.k],
                    (peer, spot.w),
                )
            )
            self.copies[-1].start()
        self.back[spot.k] = self.out[spot.k]

    def finish(self):
        spot = self.spot
        for offset in range(1, self.ranks):
            peer = lax.rem(spot.k + offset, self.ranks)
            remote(
                self.out.at[peer],
                self.back.at[peer],
                self.send.at[offset],
                self.recv.at[peer],
                (peer, spot.w),
            ).wait_recv()

    def drain(self):
        for copy in self.copies:
            copy.wait_send()


def fold_rows(values, ref):
    ranks = ref.shape[0]
    slots = values.shape[0] // ranks
    for e in range(ranks):
        part = values[slots * e : slots * (e + 1)]
        tiles = [part[:, 128 * t : 128 * (t + 1)] for t in range(values.shape[1] // 128)]
        ref[e] = jnp.concatenate(tiles, axis=0).astype(BF)


def unfold_rows(ref, slots):
    parts = []
    for e in range(ref.shape[0]):
        part = ref[e].astype(F32)
        tiles = [part[slots * t : slots * (t + 1)] for t in range(part.shape[0] // slots)]
        parts.append(jnp.concatenate(tiles, axis=1))
    return jnp.concatenate(parts, axis=0).astype(BF)


def split_three(values):
    high = values.astype(BF)
    rest = values - high.astype(F32)
    middle = rest.astype(BF)
    return high, middle, (rest - middle.astype(F32)).astype(BF)


def diagonal(values, axis):
    size = max(values.shape)
    down = lax.broadcasted_iota(jnp.int32, (size, size), 0)
    along = lax.broadcasted_iota(jnp.int32, (size, size), 1)
    return jnp.sum(
        jnp.where(down == along, values.astype(F32), 0.0), axis=axis, keepdims=True
    ).astype(jnp.int32)


def slot_maps(routes, order, slots, experts):
    rows, top = routes.shape
    pairs = rows * top
    columns = [routes[:, j : j + 1] for j in range(top)]
    e_col = jnp.concatenate(columns, axis=0)
    e_row = jnp.concatenate([diagonal(column, 0) for column in columns], axis=1)
    o_row = lax.rem(order, top) * rows + lax.div(order, top)
    o_col = diagonal(o_row, 1)
    down = lax.broadcasted_iota(jnp.int32, (pairs, pairs), 0)
    along = lax.broadcasted_iota(jnp.int32, (pairs, pairs), 1)
    turn_row = jnp.sum(jnp.where(o_col == along, down.astype(F32), 0.0), axis=0, keepdims=True)
    turn_col = jnp.sum(jnp.where(o_row == down, along.astype(F32), 0.0), axis=1, keepdims=True)
    same = e_col == e_row
    slot_row = jnp.sum(
        jnp.where(same & (turn_col < turn_row), 1.0, 0.0), axis=0, keepdims=True
    ).astype(jnp.int32)
    slot_col = jnp.sum(
        jnp.where(same & (turn_row < turn_col), 1.0, 0.0), axis=1, keepdims=True
    ).astype(jnp.int32)
    target_row = jnp.where(slot_row < slots, e_row * slots + slot_row, -1)
    target_col = jnp.where(slot_col < slots, e_col * slots + slot_col, -1)
    total = experts * slots
    place = lax.broadcasted_iota(jnp.int32, (total, pairs), 0)
    to_slots = jnp.where(place == target_row, 1.0, 0.0).astype(BF)
    place = lax.broadcasted_iota(jnp.int32, (pairs, total), 1)
    to_pairs = jnp.where(place == target_col, 1.0, 0.0).astype(BF)
    return to_slots, to_pairs


def forward_kernel(
    tok, pack, cosr, sinr, kb, qb, cot, routes, order, sd,
    wq, wk, wv, wo, sg, su, eg, eu, ed,
    q_out, mixed_out, lse_out, normed_out, pack_out, result_out, grad_second_out, pack_grad_out,
    dsh_out, kv_out, wfull_out, keep_out, give_out, other_out,
    wbuf, kv, packs, top, low, acc, sg_all, su_all, wg, wu, wd, mix, m4, cot4,
    sh_send, sh_recv, gm_send, gm_recv, xs, xr, gs, gr, os, orr, bs, br,
    x_s, g_s, sum_s, gate_s, up_s, hid_s, dgate_s, dup_s, dsh, dsh_x, slot_s, pair_s, cb,
    sem, kv_recv, kv_send, a2a_send, a2a_recv, sem_sh,
):
    spot = Spot(4)
    sems = Sems(sem)
    rows, width = tok.shape
    pairs = width // PAIR
    ranks = xs.shape[0]
    slots = xs.shape[1] * 128 // width
    hidden = wg.shape[1]
    shard = width // 4
    part = sg_all.shape[1]
    peers = [(lax.rem(spot.k + o, ranks), spot.w) for o in range(1, ranks)]
    greet([spot.core, spot.across, spot.corner] + peers)
    params = Spread(spot, lambda w: pack, lambda w: packs.at[w], sems)
    key_w = Share(spot, wk, wbuf.at[1], sems)
    value_w = Share(spot, wv, wbuf.at[2], sems)
    query_w = Share(spot, wq, wbuf.at[0], sems)
    inputs = tok[...].astype(F32)
    scale = lax.rsqrt(jnp.mean(inputs * inputs, axis=-1, keepdims=True) + EPS)
    scaled = inputs * scale
    params.finish()
    pack_all = packs[0] + packs[1] + packs[2] + packs[3]
    pack_out[...] = pack_all
    normed = (scaled * pack_all[0:1]).astype(BF)
    normed_out[...] = normed
    cosine, sine = cosr[...], sinr[...]
    key_w.forward()
    to_slots, to_pairs = slot_maps(routes[...], order[...], slots, ranks)
    slot_s[...] = to_slots
    pair_s[...] = to_pairs
    value_w.forward()
    key_w.second()
    query_w.forward()
    key_w.finish()
    kv[spot.k, :, 0:width] = turn(nn(normed, wbuf[1]), cosine, sine).astype(BF)
    value_w.second()
    value_w.finish()
    kv[spot.k, :, width : 2 * width] = nn(normed, wbuf[2]).astype(BF)
    ring = Ring(spot, kv, kv_recv, kv_send, parts=2)
    ring.start()
    query_w.second()
    out_w = Gather(spot, wo, wbuf.at[3], sems)

    def columns(ref):
        return lambda w: ref.at[:, pl.ds(pl.multiple_of(part * w, part), part)]

    def stripe(ref):
        return lambda w: ref.at[pl.ds(pl.multiple_of(shard * w, 64), shard)]

    gate_w = Gather(spot, eg, wg, sems)
    query_w.finish()
    query = turn(nn(normed, wbuf[0]), cosine, sine).astype(BF) * jnp.asarray(HD**-0.5, BF)
    for j in range(pairs):
        q_out[j] = stack_pair(query[:, PAIR * j : PAIR * (j + 1)])
    top[...] = jnp.full_like(top, MASKED)
    low[...] = jnp.zeros_like(low)
    acc[...] = jnp.zeros_like(acc)
    q_block = qb[...]

    def chunk(plane):
        k_block = kb[:, pl.ds(pl.multiple_of(2 * rows * plane, 2 * rows), 2 * rows)]
        allowed = k_block <= q_block

        def one_pair(j, carry):
            lane = pl.multiple_of(PAIR * j, PAIR)
            key = kv[pl.ds(2 * plane, 2), :, pl.ds(lane, PAIR)].reshape(2 * rows, PAIR)
            value = kv[pl.ds(2 * plane, 2), :, pl.ds(width + lane, PAIR)].reshape(2 * rows, PAIR)
            scores = jnp.where(allowed, nt(q_out[j], key), MASKED)
            old = top[j]
            new = jnp.maximum(old, jnp.max(scores, axis=1, keepdims=True))
            raised = jnp.where(allowed, jnp.exp(scores - new[:, 0:1]), 0.0)
            factor = jnp.exp(old - new)
            top[j] = new
            low[j] = low[j] * factor + jnp.sum(raised, axis=1, keepdims=True)
            acc[j] = acc[j] * factor + nn(raised.astype(BF), value)
            return carry

        lax.fori_loop(0, pairs, one_pair, 0)

    ring.step(1)
    ring.step(2)
    sg_w = Spread(spot, columns(sg), stripe(sg_all), sems)
    su_w = Spread(spot, columns(su), stripe(su_all), sems)
    cot_w = Spread(spot, lambda w: cot, lambda w: cot4.at[w], sems)
    ring.other(0)
    chunk(spot.plane(0))
    ring.step(3)
    ring.other(1)
    chunk(spot.plane(1))
    out_w.forward()
    gate_w.forward()
    up_w = Gather(spot, eu, wu, sems)
    ring.other(2)
    chunk(spot.plane(2))
    ring.other(3)
    chunk(spot.plane(3))
    saves = [pltpu.make_async_copy(kv, kv_out, sems.new())]
    saves[0].start()
    for j in range(pairs):
        mixed_out[:, PAIR * j : PAIR * (j + 1)] = unstack_pair(acc[j] / low[j])
        lse_out[j] = top[j] + jnp.log(low[j])
    out_w.finish()
    saves.append(pltpu.make_async_copy(wbuf, wfull_out, sems.new()))
    saves[1].start()
    second = inputs + nn(mixed_out[...].astype(BF), wbuf[3])
    scale = lax.rsqrt(jnp.mean(second * second, axis=-1, keepdims=True) + EPS)
    mixer = (second * scale * pack_all[1:2]).astype(BF)
    mix[...] = mixer

    mixers = Spread(spot, lambda w: mix, lambda w: m4.at[w], sems)
    fold_rows(nn(slot_s[:, :rows] + slot_s[:, rows:], mixer), xs)
    rows_out = Exchange(spot, xs, xr, a2a_send.at[0], a2a_recv.at[0])
    rows_out.start()
    router = pack_all[2:16].astype(BF)
    router = jnp.concatenate([router, jnp.zeros((2, width), BF)], axis=0)
    logits = nt(mixer, router)
    lane = lax.broadcasted_iota(jnp.int32, logits.shape, 1)
    matches = [lane == routes[:, j : j + 1] for j in range(2)]
    chosen = [jnp.sum(jnp.where(m, logits, 0.0), axis=1, keepdims=True) for m in matches]
    largest = jnp.maximum(chosen[0], chosen[1])
    raised = [jnp.exp(c - largest) for c in chosen]
    gates = [r / (raised[0] + raised[1]) for r in raised]
    grad = cot[...].astype(F32)
    pair_grad = jnp.concatenate([(g * grad).astype(BF) for g in gates], axis=0)
    fold_rows(nn(slot_s[...], pair_grad), gs)
    grads_out = Exchange(spot, gs, gr, a2a_send.at[1], a2a_recv.at[1])
    grads_out.start()
    up_w.forward()
    down_w = Gather(spot, ed, wd, sems)

    for part_w in (sg_w, su_w, cot_w, mixers):
        part_w.finish()
    rows_all = m4[...].reshape(4 * rows, width)
    grad_all = cot4[...].reshape(4 * rows, width)
    gate_part, up_part = nn(rows_all, sg_all[...]), nn(rows_all, su_all[...])
    act, slope = swish(gate_part)
    shared_hidden = (act * up_part).astype(BF)
    sh_send[...] = nn(shared_hidden, sd[...]).astype(BF).reshape(4, rows, width)
    shared_out = Spread(spot, lambda w: sh_send.at[w], lambda w: sh_recv.at[w], sems)
    hid_grad = nt(grad_all, sd[...])
    grad_gate = (hid_grad * up_part * slope).astype(BF)
    grad_up = (hid_grad * act).astype(BF)
    back = nt(grad_gate, sg_all[...]) + nt(grad_up, su_all[...])
    gm_send[...] = back.astype(BF).reshape(4, rows, width)
    shared_back = Spread(spot, lambda w: gm_send.at[w], lambda w: gm_recv.at[w], sems)
    half = shard // 2
    for at, values in ((0, tn(rows_all, grad_gate)), (half, tn(rows_all, grad_up))):
        values = values.astype(BF)
        for r in range(ranks):
            down, left = half * (r // 4), 128 * (r % 4)
            for w in range(4):
                dsh[r, shard * w + at : shard * w + at + half] = values[
                    shard * w + down : shard * w + down + half, left : left + 128
                ]
    values = tn(shared_hidden, grad_all).astype(BF)
    deep = values.shape[0] // ranks
    for r in range(ranks):
        for t in range(width // 128):
            dsh[r, width + deep * t : width + deep * (t + 1)] = values[
                deep * r : deep * (r + 1), 128 * t : 128 * (t + 1)
            ]
    shared_grad = Reduce(spot, dsh, dsh_x, None, None, sem_sh)
    for number in (3, 2, 1, 0):
        shared_grad.side(number)

    for part_w in (gate_w, up_w):
        part_w.finish()
    rows_out.finish()
    x_s[...] = unfold_rows(xr, slots)
    block = 512

    def parts(i):
        return pl.ds(pl.multiple_of(block * i, block), block)

    def up_step(i, carry):
        at = parts(i)
        gate = nn(x_s[...], wg[:, at])
        up = nn(x_s[...], wu[:, at])
        act, slope = swish(gate)
        hid_s[:, at] = (act * up).astype(BF)
        gate_s[:, at] = up * slope
        up_s[:, at] = act
        return carry

    lax.fori_loop(0, hidden // block, up_step, 0)
    grads_out.finish()
    g_s[...] = unfold_rows(gr, slots)
    down_w.forward()
    down_w.finish()

    def down_step(i, carry):
        at = parts(i)
        grad_hidden = nn(g_s[...], wd[:, at])
        dgate_s[:, at] = (grad_hidden * gate_s[:, at]).astype(BF)
        dup_s[:, at] = (grad_hidden * up_s[:, at]).astype(BF)
        return carry

    lax.fori_loop(0, hidden // block, down_step, 0)
    sum_s[...] = nt(dgate_s[...], wg[...]) + nt(dup_s[...], wu[...])
    fold_rows(sum_s[...], bs)
    backs = Exchange(spot, bs, br, a2a_send.at[3], a2a_recv.at[3])
    backs.start()
    sum_s[...] = nt(hid_s[...], wd[...])
    fold_rows(sum_s[...], os)
    outs = Exchange(spot, os, orr, a2a_send.at[2], a2a_recv.at[2])
    outs.start()

    for part_w in (gate_w, up_w, down_w):
        part_w.drain()
    swaps = []
    for a, (ref, left, right) in enumerate(
        ((wg, x_s, dgate_s), (wu, x_s, dup_s), (wd, g_s, hid_s))
    ):

        def grad_step(i, carry, ref=ref, left=left, right=right):
            at = parts(i)
            ref[:, at] = tn(left[...], right[:, at]).astype(BF)
            return carry

        lax.fori_loop(0, hidden // block, grad_step, 0)
        for row in range(2):
            src = ref.at[pl.ds(pl.multiple_of(shard * (2 * row + 1 - spot.c), 64), shard)]
            swaps.append(remote(src, cb.at[a, row], sems.new(), sems.new(), spot.core))
            swaps[-1].start()
    across = []
    for a, ref in enumerate((wg, wu, wd)):
        for row in range(2):
            swaps[2 * a + row].wait_recv()

        def add(i, carry, a=a, ref=ref):
            for row in range(2):
                at = pl.ds(pl.multiple_of(shard * (2 * row + spot.c) + 16 * i, 16), 16)
                own = ref[at].astype(F32)
                ref[at] = (own + cb[a, row, pl.ds(16 * i, 16)].astype(F32)).astype(BF)
            return carry

        lax.fori_loop(0, shard // 16, add, 0)
        give = ref.at[pl.ds(pl.multiple_of(shard * spot.across[1], 64), shard)]
        keep = ref.at[pl.ds(pl.multiple_of(shard * spot.w, 64), shard)]
        saves.append(pltpu.make_async_copy(keep, keep_out.at[a], sems.new()))
        saves[-1].start()
        if a == 0:
            across.append(remote(give, other_out, sems.new(), sems.new(), spot.across))
            across[-1].start()
        else:
            saves.append(pltpu.make_async_copy(give, give_out.at[a - 1], sems.new()))
            saves[-1].start()
    for number in (3, 2, 1, 0):
        shared_grad.meet(number)
        plane = spot.plane(number)
        dsh_out[plane] = dsh[2 * plane + spot.x]

    shared_out.finish()
    total = second
    for w in range(4):
        total = total + sh_recv[w].astype(F32)
    shared_back.finish()
    grad_mixer = gm_recv[0].astype(F32)
    for w in range(1, 4):
        grad_mixer = grad_mixer + gm_recv[w].astype(F32)
    outs.finish()
    pair_out = nn(pair_s[...], unfold_rows(orr, slots))
    pair_out = [pair_out[:rows], pair_out[rows:]]
    result_out[...] = (total + gates[0] * pair_out[0] + gates[1] * pair_out[1]).astype(BF)
    grad_gates = [jnp.sum(grad * p, axis=1, keepdims=True) for p in pair_out]
    inner = gates[0] * grad_gates[0] + gates[1] * grad_gates[1]
    grad_logits = jnp.zeros_like(logits)
    for j in range(2):
        grad_logits += jnp.where(matches[j], gates[j] * (grad_gates[j] - inner), 0.0)
    pieces = split_three(grad_logits)
    router_grad = sum(tn(piece, mixer) for piece in pieces)
    grad_mixer = grad_mixer + sum(nn(piece, router) for piece in pieces)
    backs.finish()
    grad_mixer = grad_mixer + nn(pair_s[:rows] + pair_s[rows:], unfold_rows(br, slots))
    weighted = grad_mixer * pack_all[1:2]
    mean = jnp.mean(weighted * second, axis=-1, keepdims=True)
    grad_second_out[...] = grad + scale * weighted - second * (scale * scale * scale * mean)
    gain_grad = jnp.sum(grad_mixer * second * scale, axis=0, keepdims=True)
    pack_grad_out[...] = jnp.concatenate(
        [jnp.zeros_like(gain_grad), gain_grad, router_grad[:14]], axis=0
    )
    for copy in across:
        copy.wait_recv()
    for part_w in (params, key_w, value_w, query_w, out_w, sg_w, su_w, cot_w, ring, mixers):
        part_w.drain()
    for part_w in (rows_out, grads_out, outs, backs, shared_out, shared_back):
        part_w.drain()
    for copy in shared_grad.sent + swaps + across:
        copy.wait_send()
    for copy in saves:
        copy.wait()


def run_forward(
    tok, pack, cosr, sinr, kb, qb, cot, routes, order, sd, wq, wk, wv, wo, sg, su, eg, eu, ed
):
    rows, width = tok.shape
    pairs = width // PAIR
    ranks, slots = 8, 40
    hidden = eg.shape[1]
    part = sg.shape[1] // 4
    shard = width // 4
    total = ranks * slots
    tall = width + part * width // (128 * ranks)
    any_, vm = pl.BlockSpec(memory_space=pl.ANY), pl.BlockSpec(memory_space=VMEM)
    shape = jax.ShapeDtypeStruct

    def low(*dims):
        return VMEM(dims, BF)

    def full(*dims):
        return VMEM(dims, F32)

    dma = pltpu.SemaphoreType.DMA
    folded = low(ranks, slots * width // 128, 128)
    return pl.pallas_call(
        forward_kernel,
        out_shape=(
            shape((pairs, 2 * rows, PAIR), BF),
            shape((rows, width), F32),
            shape((pairs, 2 * rows, PAIR), F32),
            shape((rows, width), BF),
            shape(pack.shape, F32),
            shape((rows, width), BF),
            shape((rows, width), F32),
            shape(pack.shape, F32),
            shape((4, tall, 128), BF),
            shape((ranks, rows, 2 * width), BF),
            shape((4, width, width), BF),
            shape((3, shard, hidden), BF),
            shape((2, shard, hidden), BF),
            shape((shard, hidden), BF),
        ),
        in_specs=[vm] * 10 + [any_] * 9,
        out_specs=tuple([vm] * 9 + [any_] * 5),
        scratch_shapes=[
            low(4, width, width),
            low(ranks, rows, 2 * width),
            full(4, *pack.shape),
            full(pairs, 2 * rows, PAIR),
            full(pairs, 2 * rows, PAIR),
            full(pairs, 2 * rows, PAIR),
            low(width, part),
            low(width, part),
            low(width, hidden),
            low(width, hidden),
            low(width, hidden),
            low(rows, width),
            low(4, rows, width),
            low(4, rows, width),
            low(4, rows, width),
            low(4, rows, width),
            low(4, rows, width),
            low(4, rows, width),
            *[folded] * 8,
            low(total, width),
            low(total, width),
            full(total, width),
            full(total, hidden),
            full(total, hidden),
            low(total, hidden),
            low(total, hidden),
            low(total, hidden),
            low(ranks, tall, 128),
            low(4, tall, 128),
            low(total, 2 * rows),
            low(2 * rows, total),
            low(3, 2, shard, hidden),
            dma((144,)),
            dma((2 * ranks,)),
            dma((32,)),
            dma((4, ranks)),
            dma((4, ranks)),
            dma((5, 8)),
        ],
        compiler_params=pltpu.CompilerParams(
            collective_id=1, has_side_effects=True, vmem_limit_bytes=VMEM_BYTES
        ),
    )(tok, pack, cosr, sinr, kb, qb, cot, routes, order, sd, wq, wk, wv, wo, sg, su, eg, eu, ed)


def backward_kernel(
    grad_second_ref, tok, pack_ref, pack_grad_ref, normed_ref, mixed_ref, q_ref, lse_ref,
    cosr, sinr, kb, qb, dsh_ref, kv_ref, wfull_ref, give_ref,
    grad_input_out, pack_out, att1_out, att2_out, sh_out, other_out,
    wbuf, kv, kvb, kv_x, kv_zo, kv_zi, kv_sum, gst, delta_s, dq,
    ga, ga4, gq, gq4, gkv, gkv4, n_t, m_t, n_all, m_all, pk, pk4,
    a1, a1_x, a1_zo, a1_zi, a1_sum, a2, a2_x, a2_zo, a2_zi, a2_sum, r1, r2,
    sh, sh_zo, sh_zi, sh_sum, sh_chunk, r3,
    sem, sem_kv, sem_a1, sem_a2, sem_sh, ring_recv, ring_send,
):
    spot = Spot(4)
    sems = Sems(sem)
    rows, width = tok.shape
    pairs = width // PAIR
    shard = width // 4
    loads = [pltpu.make_async_copy(wfull_ref.at[i], wbuf.at[i], sems.new()) for i in (3, 0, 1, 2)]
    loads.insert(1, pltpu.make_async_copy(kv_ref, kv, sems.new()))
    loads.append(pltpu.make_async_copy(dsh_ref, sh, sems.new()))
    for copy in loads:
        copy.start()

    def block(ref, w):
        return ref.at[pl.ds(pl.multiple_of(shard * w, 64), shard)]

    greet((spot.core, spot.across, spot.corner, spot.column, spot.inner), (spot.mid, spot.outer))
    grad_second = grad_second_ref[...]
    ga[...] = grad_second.astype(BF)
    grads_w = Spread(spot, lambda w: ga, lambda w: ga4.at[w], sems)
    loads[-1].wait()
    shared = Reduce(spot, sh, None, sh_zo, sh_zi, sem_sh, folded=True)
    for number in (3, 2, 1):
        shared.launch(number)
    mixed = mixed_ref[...]
    n_t[...] = normed_ref[...].T
    m_t[...] = mixed.astype(BF).T

    def columns(ref):
        return lambda w: ref.at[:, pl.ds(pl.multiple_of(rows * w, 128), rows)]

    normed_w = Spread(spot, lambda w: block(n_t, w), columns(n_all), sems)
    mixed_w = Spread(spot, lambda w: block(m_t, w), columns(m_all), sems)
    across = []
    for a in range(2):
        across.append(
            remote(give_ref.at[a], other_out.at[a], sems.new(), sems.new(), spot.across)
        )
        across[-1].start()
    loads[0].wait()
    grad_mixed = nt(ga[...], wbuf[3]).astype(BF)
    product = grad_mixed.astype(F32) * mixed
    for j in range(pairs):
        lanes = slice(PAIR * j, PAIR * (j + 1))
        gst[j] = stack_pair(grad_mixed[:, lanes])
        delta_s[j] = jnp.broadcast_to(
            jnp.sum(stack_pair(product[:, lanes]), axis=1, keepdims=True), (2 * rows, PAIR)
        )
    dq[...] = jnp.zeros_like(dq)
    loads[1].wait()
    q_block = qb[...]

    def chunk(number):
        plane = spot.plane(number)
        k_block = kb[:, pl.ds(pl.multiple_of(2 * rows * plane, 2 * rows), 2 * rows)]
        allowed = k_block <= q_block

        def one_pair(j, carry):
            lane = pl.multiple_of(PAIR * j, PAIR)
            both = pl.ds(2 * plane, 2)
            key = kv[both, :, pl.ds(lane, PAIR)].reshape(2 * rows, PAIR)
            value = kv[both, :, pl.ds(width + lane, PAIR)].reshape(2 * rows, PAIR)
            query, grad = q_ref[j], gst[j]
            scores = nt(query, key)
            probs = jnp.where(allowed, jnp.exp(scores - lse_ref[j][:, 0:1]), 0.0)
            inner = nt(grad, value) - delta_s[j][:, 0:1]
            grad_scores = (probs * inner * HD**-0.5).astype(BF)
            dq[j] += nn(grad_scores, key)
            grad_key = tn(grad_scores, query) * HD**0.5
            grad_value = tn(probs.astype(BF), grad)
            kvb[both, :, pl.ds(lane, PAIR)] = grad_key.astype(BF).reshape(2, rows, PAIR)
            kvb[both, :, pl.ds(width + lane, PAIR)] = grad_value.astype(BF).reshape(2, rows, PAIR)
            return carry

        lax.fori_loop(0, pairs, one_pair, 0)

    kv_grad = Reduce(spot, kvb, kv_x, kv_zo, kv_zi, sem_kv, parts=2)
    chunk(3)
    kv_grad.side(3)
    chunk(2)
    kv_grad.side(2)
    shared.relay(3)
    chunk(1)
    kv_grad.side(1)
    kv_grad.meet(3)
    shared.relay(2)
    chunk(0)
    kv_grad.side(0)
    cosine, sine = cosr[...], sinr[...]
    gq[...] = turn(
        jnp.concatenate([unstack_pair(dq[j]) for j in range(pairs)], axis=1), cosine, -sine
    ).astype(BF)
    query_w = Spread(spot, lambda w: gq, lambda w: gq4.at[w], sems)
    for part_w in (grads_w, normed_w, mixed_w):
        part_w.finish()
    out_grad = nn(m_all[...], ga4[...].reshape(4 * rows, width))
    kv_grad.meet(2)
    kv_grad.relay(3)
    shared.relay(1)
    shared.last(sh_sum)
    sh_chunk[...] = sh_sum[...].astype(BF)
    part = 2 * shard // 2

    def piece(w):
        return sh_chunk.at[pl.ds(pl.multiple_of(part * w, 64), part)]

    def place(w):
        return r3.at[spot.k, pl.ds(pl.multiple_of(part * w, 64), part)]

    shared_w = Spread(spot, piece, place, sems)
    rest = sh_chunk.shape[0] - 4 * part
    r3[spot.k, pl.ds(4 * part, rest)] = sh_chunk[pl.ds(4 * part, rest)]
    kv_grad.meet(1)
    kv_grad.relay(2)
    kv_grad.relay(1)
    query_w.finish()
    query_grad = nn(n_all[...], gq4[...].reshape(4 * rows, width))
    half = jnp.concatenate([out_grad, query_grad], axis=0).astype(BF)
    a1[...] = half.reshape(a1.shape)
    first = Reduce(spot, a1, a1_x, a1_zo, a1_zi, sem_a1)
    for number in (3, 2, 1, 0):
        first.side(number)
    kv_grad.meet(0)
    kv_grad.last(kv_sum)
    gkv[:, 0:width] = turn(kv_sum[:, 0:width], cosine, -sine).astype(BF)
    gkv[:, width : 2 * width] = kv_sum[:, width : 2 * width].astype(BF)
    kv_w = Spread(spot, lambda w: gkv, lambda w: gkv4.at[w], sems)
    shared_w.finish()
    ring3 = Ring(spot, r3, ring_recv.at[2], ring_send.at[2], parts=2)
    ring3.start()
    for copy in loads[2:5]:
        copy.wait()
    grad_normed = nt(gq[...], wbuf[0]) + nt(gkv[:, 0:width], wbuf[1])
    grad_normed = grad_normed + nt(gkv[:, width : 2 * width], wbuf[2])
    inputs = tok[...].astype(F32)
    scale = lax.rsqrt(jnp.mean(inputs * inputs, axis=-1, keepdims=True) + EPS)
    weighted = grad_normed * pack_ref[0:1]
    mean = jnp.mean(weighted * inputs, axis=-1, keepdims=True)
    grad_input_out[...] = (
        grad_second + scale * weighted - inputs * (scale * scale * scale * mean)
    )
    gain_grad = jnp.sum(grad_normed * inputs * scale, axis=0, keepdims=True)
    pk[...] = jnp.concatenate([gain_grad, pack_grad_ref[1:16]], axis=0)
    pack_w = Spread(spot, lambda w: pk, lambda w: pk4.at[w], sems)
    for number in (3, 2, 1, 0):
        first.meet(number)
    first.relay(3)
    first.relay(2)
    kv_w.finish()
    pack_w.finish()
    grad_kv = gkv4[...].reshape(4 * rows, 2 * width)
    both = nn(n_all[...], grad_kv)
    both = jnp.concatenate([both[:, 0:width], both[:, width : 2 * width]], axis=0).astype(BF)
    size = both.shape[0] // 8
    extra = (pk4[0] + pk4[1] + pk4[2] + pk4[3]).astype(BF)
    for r in range(8):
        a2[r, 0:size] = both[size * r : size * (r + 1)]
        a2[r, size : size + 16] = extra
    second = Reduce(spot, a2, a2_x, a2_zo, a2_zi, sem_a2)
    for number in (3, 2, 1, 0):
        second.side(number)
    first.relay(1)
    ring3.step(1)
    first.last(a1_sum)
    r1[spot.k] = a1_sum[...].astype(BF)
    ring1 = Ring(spot, r1, ring_recv.at[0], ring_send.at[0])
    ring1.start()
    ring3.step(2)
    for number in (3, 2, 1, 0):
        second.meet(number)
    ring1.step(1)
    ring3.step(3)
    second.relay(3)
    second.relay(2)
    second.relay(1)
    ring1.step(2)
    second.last(a2_sum)
    r2[spot.k] = a2_sum[0:size].astype(BF)
    ring2 = Ring(spot, r2, ring_recv.at[1], ring_send.at[1])
    ring2.start()
    pack_out[...] = a2_sum[size : size + 16]
    ring1.step(3)
    for number in (1, 2, 3):
        ring2.step(number)
    saves = []
    for ring, src, dst in ((ring3, r3, sh_out), (ring1, r1, att1_out), (ring2, r2, att2_out)):
        for number in range(4):
            ring.other(number)
        saves.append(pltpu.make_async_copy(src, dst, sems.new()))
        saves[-1].start()
    for copy in across:
        copy.wait_recv()
        copy.wait_send()
    for part_w in (grads_w, normed_w, mixed_w, query_w, shared_w, kv_w, pack_w):
        part_w.drain()
    for part_w in (shared, kv_grad, first, second, ring1, ring2, ring3):
        part_w.drain()
    for copy in saves:
        copy.wait()


def run_backward(
    grad_second, tok, pack, pack_grad, normed, mixed, q, lse, cosr, sinr, kb, qb, dsh, kv, wfull,
    give,
):
    rows, width = tok.shape
    pairs = width // PAIR
    ranks = 8
    shard, hidden = width // 4, give.shape[2]
    size = 2 * shard // ranks
    tall = dsh.shape[1]
    any_, vm = pl.BlockSpec(memory_space=pl.ANY), pl.BlockSpec(memory_space=VMEM)
    shape = jax.ShapeDtypeStruct

    def low(*dims):
        return VMEM(dims, BF)

    def full(*dims):
        return VMEM(dims, F32)

    dma = pltpu.SemaphoreType.DMA
    return pl.pallas_call(
        backward_kernel,
        out_shape=(
            shape((rows, width), F32),
            shape(pack.shape, F32),
            shape((ranks, size, width), BF),
            shape((ranks, size, width), BF),
            shape((ranks, tall, 128), BF),
            shape((2, shard, hidden), BF),
        ),
        in_specs=[vm] * 12 + [any_] * 4,
        out_specs=(vm, vm, any_, any_, any_, any_),
        scratch_shapes=[
            low(4, width, width),
            low(ranks, rows, 2 * width),
            low(ranks, rows, 2 * width),
            low(4, rows, 2 * width),
            low(4, rows, 2 * width),
            low(4, rows, 2 * width),
            full(rows, 2 * width),
            low(pairs, 2 * rows, PAIR),
            full(pairs, 2 * rows, PAIR),
            full(pairs, 2 * rows, PAIR),
            low(rows, width),
            low(4, rows, width),
            low(rows, width),
            low(4, rows, width),
            low(rows, 2 * width),
            low(4, rows, 2 * width),
            low(width, rows),
            low(width, rows),
            low(shard, 4 * rows),
            low(shard, 4 * rows),
            full(16, width),
            full(4, 16, width),
            low(ranks, size, width),
            low(4, size, width),
            low(4, size, width),
            low(4, size, width),
            full(size, width),
            low(ranks, size + 16, width),
            low(4, size + 16, width),
            low(4, size + 16, width),
            low(4, size + 16, width),
            full(size + 16, width),
            low(ranks, size, width),
            low(ranks, size, width),
            low(4, tall, 128),
            low(4, tall, 128),
            low(4, tall, 128),
            full(tall, 128),
            low(tall, 128),
            low(ranks, tall, 128),
            dma((112,)),
            dma((5, 8)),
            dma((5, 8)),
            dma((5, 8)),
            dma((5, 8)),
            dma((3, 2 * ranks)),
            dma((3, 32)),
        ],
        compiler_params=pltpu.CompilerParams(
            collective_id=3, has_side_effects=True, vmem_limit_bytes=VMEM_BYTES
        ),
    )(
        grad_second, tok, pack, pack_grad, normed, mixed, q, lse, cosr, sinr, kb, qb, dsh, kv,
        wfull, give,
    )


def unpack_kernel(
    result, grad_input, pack, att1, att2, sh, keep, other0, other,
    result_out, grad_input_out, gain_one, gain_two, router,
    query, key, value, output, gate, up, down, eg, eu, ed,
):
    i = pl.program_id(0)
    result_out[...] = result[...]
    grad_input_out[...] = grad_input[...]
    output[...] = att1[0, 0].astype(F32)
    query[...] = att1[1, 0].astype(F32)
    key[...] = att2[0, 0].astype(F32)
    value[...] = att2[1, 0].astype(F32)
    eg[...] = keep[0].astype(F32) + other0[...].astype(F32)
    eu[...] = keep[1].astype(F32) + other[0].astype(F32)
    ed[...] = keep[2].astype(F32) + other[1].astype(F32)
    size = gate.shape[0]
    shard = 4 * size
    width = 4 * shard
    row, within = lax.div(i, 2), lax.rem(i, 2) * size
    for c in range(4):
        for w in range(4):
            lanes = slice(512 * w + 128 * c, 512 * w + 128 * (c + 1))
            start = pl.multiple_of(shard * w + within, 16)
            gate[:, lanes] = sh[4 * row + c, pl.ds(start, size)].astype(F32)
            start = pl.multiple_of(shard * w + shard // 2 + within, 16)
            up[:, lanes] = sh[4 * row + c, pl.ds(start, size)].astype(F32)
    deep = down.shape[0] // 2
    for r in range(2):
        for t in range(width // 128):
            at = slice(width + deep * t, width + deep * (t + 1))
            down[deep * r : deep * (r + 1), 128 * t : 128 * (t + 1)] = sh[2 * i + r, at].astype(F32)

    @pl.when(i == 0)
    def _():
        back = lax.rem(4 - lax.axis_index("wt"), 4) * shard
        mine = pltpu.roll(pack[...], back, 1)[:, 0:256]
        gain_one[...] = mine[0:1, 0:shard]
        gain_two[...] = mine[1:2, 0:shard]
        router[...] = mine.T[0:shard, 2 : 2 + router.shape[1]]


def run_unpack(result, grad_input, pack, att1, att2, sh, keep, other0, other, experts):
    rows, width = result.shape
    shard, hidden = other0.shape
    steps = 4
    shape = jax.ShapeDtypeStruct
    size = shard // steps
    att1 = att1.reshape(2, 4, size, width)
    att2 = att2.reshape(2, 4, size, width)
    shared_hidden = sh.shape[0] * (sh.shape[1] - width) * 128 // width
    shared = 4 * shared_hidden
    by_rows = lambda r, c: pl.BlockSpec((r, c), lambda i: (i, 0))
    whole = lambda *dims: pl.BlockSpec(dims, lambda i: (0,) * len(dims))
    stack = lambda n, r, c: pl.BlockSpec((n, r, c), lambda i: (0, i, 0))
    att = pl.BlockSpec((2, 1, size, width), lambda i: (0, i, 0, 0))
    return pl.pallas_call(
        unpack_kernel,
        grid=(steps,),
        out_shape=(
            shape((rows, width), BF),
            shape((rows, width), F32),
            shape((1, shard), F32),
            shape((1, shard), F32),
            shape((shard, experts), F32),
            *[shape((shard, width), F32)] * 4,
            *[shape((shard, shared), F32)] * 2,
            shape((shared_hidden, width), F32),
            *[shape((shard, hidden), F32)] * 3,
        ),
        in_specs=[
            by_rows(rows // steps, width),
            by_rows(rows // steps, width),
            whole(*pack.shape),
            att,
            att,
            whole(*sh.shape),
            stack(3, size, hidden),
            by_rows(size, hidden),
            stack(2, size, hidden),
        ],
        out_specs=(
            by_rows(rows // steps, width),
            by_rows(rows // steps, width),
            whole(1, shard),
            whole(1, shard),
            whole(shard, experts),
            *[by_rows(size, width)] * 4,
            *[by_rows(size, shared)] * 2,
            by_rows(shared_hidden // steps, width),
            *[by_rows(size, hidden)] * 3,
        ),
        compiler_params=pltpu.CompilerParams(vmem_limit_bytes=VMEM_BYTES),
    )(result, grad_input, pack, att1, att2, sh, keep, other0, other)


def angles_of(block_deal, rows_dev):
    here = places(lax.axis_index("ctx") * rows_dev, rows_dev, block_deal, rows_dev)
    half_size = HD // 2
    frequency = 10000.0 ** (-jnp.arange(half_size, dtype=F32) / half_size)
    angles = here.astype(F32)[:, None] * frequency[None, :]
    cosine, sine = jnp.cos(angles), jnp.sin(angles)
    cosr = jnp.concatenate([cosine] * 4, axis=1)
    sinr = jnp.concatenate([-sine, sine, -sine, sine], axis=1)
    return here, cosr, sinr


def pack_params(gain_one, gain_two, router):
    width = 4 * gain_one.shape[0]
    shard = jnp.concatenate(
        [gain_one[None], gain_two[None], router.T, jnp.zeros((6, gain_one.shape[0]), BF)], axis=0
    ).astype(F32)
    start = lax.axis_index("wt") * gain_one.shape[0]
    return lax.dynamic_update_slice(jnp.zeros((16, width), F32), shard, (0, start))


def contract_product(left, right, left_dim, right_dim):
    return lax.dot_general(
        left, right, (((left_dim,), (right_dim,)), ((), ())), preferred_element_type=jnp.float32
    )


def contract_exact(left, right, left_dim, right_dim):
    return lax.dot_general(
        left,
        right,
        (((left_dim,), (right_dim,)), ((), ())),
        precision=HIGH,
        preferred_element_type=jnp.float32,
    )


def rms_norm(values, gain):
    norm_scale = lax.rsqrt(jnp.mean(values * values, axis=-1, keepdims=True) + EPS)
    return (values * norm_scale * gain, norm_scale)


def rms_back(values, norm_scale, gain, upstream):
    weighted = upstream * gain
    inner_mean = jnp.mean(weighted * values, axis=-1, keepdims=True)
    through = norm_scale * weighted - values * norm_scale * norm_scale * norm_scale * inner_mean
    return (through, jnp.sum(upstream * values * norm_scale, axis=0))


def silu_parts(gate_part):
    sigmoid = jax.nn.sigmoid(gate_part)
    return (gate_part * sigmoid, sigmoid * (1.0 + gate_part * (1.0 - sigmoid)))


def rotate(values, place, sign):
    half_size = HD // 2
    frequency = 10000.0 ** (-jnp.arange(half_size, dtype=jnp.float32) / half_size)
    angles = place.astype(jnp.float32)[:, None] * frequency[None, :]
    cosine = jnp.cos(angles)[:, None, :]
    sine_part = sign * jnp.sin(angles)[:, None, :]
    shaped = values.reshape(values.shape[0], values.shape[1] // HD, 2, half_size)
    first_half = shaped[:, :, 0, :]
    second_half = shaped[:, :, 1, :]
    turned = jnp.stack(
        [
            first_half * cosine - second_half * sine_part,
            second_half * cosine + first_half * sine_part,
        ],
        axis=2,
    )
    return turned.reshape(values.shape)


def places(first_row, row_count, block_deal, rows_dev):
    row_index = first_row + jnp.arange(row_count, dtype=jnp.int32)
    owner_rank = row_index // rows_dev
    inner_row = row_index % rows_dev
    ranks = block_deal.shape[0]
    matches = owner_rank[:, None] == jnp.arange(ranks, dtype=jnp.int32)[None, :]
    paired = jnp.sum(jnp.where(matches, block_deal[None, :], 0), axis=1)
    piece_size = rows_dev // 2
    unit_index = jnp.where(inner_row < piece_size, paired, 2 * ranks - 1 - paired)
    return unit_index * piece_size + inner_row % piece_size


def score_block(query_side, key_rows, key_place):
    query3, query_block = query_side
    key3 = key_rows.reshape(key_rows.shape[0], -1, HD)
    raw_scores = jnp.einsum("qhd,khd->hqk", query3, key3, preferred_element_type=jnp.float32)
    allowed = (key_place // BLK)[None, None, :] <= query_block[None, :, None]
    return (jnp.where(allowed, raw_scores * HD ** (-0.5), MASKED), allowed)


def absorb(running, key_rows, value_rows, key_place, query_side):
    largest, denom, accum = running
    scores, allowed = score_block(query_side, key_rows, key_place)
    new_largest = jnp.maximum(largest, jnp.max(scores, axis=2))
    factor = jnp.exp(largest - new_largest)
    raised = jnp.where(allowed, jnp.exp(scores - new_largest[:, :, None]), 0.0)
    denom = denom * factor + jnp.sum(raised, axis=2)
    value3 = value_rows.reshape(value_rows.shape[0], -1, HD)
    accum = accum * factor.T[:, :, None] + jnp.einsum(
        "hqk,khd->qhd", raised.astype(jnp.bfloat16), value3, preferred_element_type=jnp.float32
    )
    return (new_largest, denom, accum)


def fold_keys(running, key_piece, query_side, block_deal, rows_dev):
    key_all, value_all = key_piece
    row_count = key_all.shape[0]
    block_size = KEY_ROWS

    def key_step(current, offset):
        key_rows = lax.dynamic_slice_in_dim(key_all, offset, block_size, 0)
        value_rows = lax.dynamic_slice_in_dim(value_all, offset, block_size, 0)
        key_place = places(offset, block_size, block_deal, rows_dev)
        return (absorb(current, key_rows, value_rows, key_place, query_side), None)

    offsets = jnp.arange(row_count // block_size, dtype=jnp.int32) * block_size
    running, unused = lax.scan(key_step, running, offsets)
    return running


def differentiate(query_side, log_total, delta, grad_out3, key_rows, value_rows, key_place):
    scores, allowed = score_block(query_side, key_rows, key_place)
    probs_full = jnp.where(allowed, jnp.exp(scores - log_total[:, :, None]), 0.0)
    value3 = value_rows.reshape(value_rows.shape[0], -1, HD)
    grad_probs = jnp.einsum("qhd,khd->hqk", grad_out3, value3, preferred_element_type=jnp.float32)
    grad_scores = (probs_full * (grad_probs - delta[:, :, None]) * HD ** (-0.5)).astype(
        jnp.bfloat16
    )
    return (probs_full, grad_scores)


def assign_slots(route, order, experts, capacity):
    pair_count = order.shape[0]
    expert_ids = route.reshape(pair_count)
    ordered = expert_ids[order]
    onehot = (ordered[:, None] == jnp.arange(experts, dtype=jnp.int32)[None, :]).astype(jnp.int32)
    before = jnp.cumsum(onehot, axis=0) - onehot
    slot_turn = jnp.sum(before * onehot, axis=1)
    slot_index = jnp.zeros((pair_count,), jnp.int32).at[order].set(slot_turn)
    kept_pairs = slot_index < capacity
    target = jnp.where(kept_pairs, expert_ids * capacity + slot_index, experts * capacity)
    slot_table = (
        jnp.full((experts * capacity,), pair_count, jnp.int32)
        .at[target]
        .set(jnp.arange(pair_count, dtype=jnp.int32), mode="drop")
    )
    return (target, kept_pairs, slot_table)


def body(
    tokens,
    cotangent,
    gain_attention,
    query_weight,
    key_weight,
    value_weight,
    output_weight,
    gain_mixer,
    router_weight,
    shared_gate,
    shared_up,
    shared_down,
    expert_gate,
    expert_up,
    expert_down,
    routes,
    slot_order,
    block_deal,
):
    rows_dev = tokens.shape[1]
    width = tokens.shape[2]
    ranks = lax.axis_size("ctx")
    (
        gain_one,
        query_full,
        key_full,
        value_full,
        output_full,
        gain_two,
        router_full,
        sgate_full,
        sup_full,
        sdown_full,
        expert_gate_whole,
        expert_up_whole,
        edown_full,
    ) = (
        lax.all_gather(gain_attention, "wt", axis=0, tiled=True),
        lax.all_gather(query_weight, "wt", axis=0, tiled=True),
        lax.all_gather(key_weight, "wt", axis=0, tiled=True),
        lax.all_gather(value_weight, "wt", axis=0, tiled=True),
        lax.all_gather(output_weight, "wt", axis=0, tiled=True),
        lax.all_gather(gain_mixer, "wt", axis=0, tiled=True),
        lax.all_gather(router_weight, "wt", axis=0, tiled=True),
        lax.all_gather(shared_gate, "wt", axis=0, tiled=True),
        lax.all_gather(shared_up, "wt", axis=0, tiled=True),
        lax.all_gather(shared_down, "wt", axis=0, tiled=True),
        lax.all_gather(expert_gate, "wt", axis=0, tiled=True),
        lax.all_gather(expert_up, "wt", axis=0, tiled=True),
        lax.all_gather(expert_down, "wt", axis=0, tiled=True),
    )
    gain_first = gain_one.astype(jnp.float32)
    gain_second = gain_two.astype(jnp.float32)
    heads = width // HD
    inputs = tokens[0].astype(jnp.float32)
    here = places(lax.axis_index("ctx") * rows_dev, rows_dev, block_deal, rows_dev)
    query_side_block = here // BLK
    normed_f, scale_one = rms_norm(inputs, gain_first)
    normed = normed_f.astype(jnp.bfloat16)
    query_rot = rotate(
        jnp.dot(normed, query_full, preferred_element_type=jnp.float32), here, 1.0
    ).astype(jnp.bfloat16)
    key_rot = rotate(
        jnp.dot(normed, key_full, preferred_element_type=jnp.float32), here, 1.0
    ).astype(jnp.bfloat16)
    value_low = jnp.dot(normed, value_full, preferred_element_type=jnp.float32).astype(jnp.bfloat16)
    query3 = query_rot.reshape(rows_dev, heads, HD)
    query_side = (query3, query_side_block)
    start_state = (
        jnp.full((heads, rows_dev), MASKED, jnp.float32),
        jnp.zeros((heads, rows_dev), jnp.float32),
        jnp.zeros((rows_dev, heads, HD), jnp.float32),
    )
    largest, denom, accum = fold_keys(
        start_state,
        (
            lax.all_gather(key_rot, "ctx", axis=0, tiled=True),
            lax.all_gather(value_low, "ctx", axis=0, tiled=True),
        ),
        query_side,
        block_deal,
        rows_dev,
    )
    mixed3 = accum / denom.T[:, :, None]
    log_total = largest + jnp.log(denom)
    mixed_low = mixed3.reshape(rows_dev, width).astype(jnp.bfloat16)
    second = inputs + jnp.dot(mixed_low, output_full, preferred_element_type=jnp.float32)
    mixer_f, scale_two = rms_norm(second, gain_second)
    mixer = mixer_f.astype(jnp.bfloat16)
    experts = router_full.shape[1]
    logits = jnp.dot(mixer, router_full, preferred_element_type=jnp.float32)
    route = routes[0]
    top_count = route.shape[1]
    pair_count = rows_dev * top_count
    capacity = (5 * pair_count + 4 * experts - 1) // (4 * experts)
    split_count = ranks // experts
    expert_match = route[:, :, None] == jnp.arange(experts, dtype=jnp.int32)[None, None, :]
    chosen = jnp.sum(jnp.where(expert_match, logits[:, None, :], 0.0), axis=2)
    gates = jax.nn.softmax(chosen, axis=1)
    target, kept_pairs, slot_table = assign_slots(route, slot_order[0, 0], experts, capacity)
    valid = slot_table < pair_count
    pair_pick = jnp.minimum(slot_table, pair_count - 1)
    target_pick = jnp.minimum(target, experts * capacity - 1)
    send_rows = jnp.where(
        valid[:, None], mixer[pair_pick // top_count], jnp.zeros((), jnp.bfloat16)
    )
    send_rows = jnp.broadcast_to(
        send_rows.reshape(experts, 1, capacity, width), (experts, split_count, capacity, width)
    ).reshape(ranks, capacity, width)
    received = lax.all_to_all(send_rows, "ctx", split_axis=0, concat_axis=0, tiled=True)
    slot_count = received.shape[1]
    flattened_input = received.reshape(ranks * slot_count, width)
    gate_part = jnp.dot(flattened_input, expert_gate_whole, preferred_element_type=jnp.float32)
    up_projection_part = jnp.dot(
        flattened_input, expert_up_whole, preferred_element_type=jnp.float32
    )
    activated, unused = silu_parts(gate_part)
    hidden = (activated * up_projection_part).astype(jnp.bfloat16)
    partial_value = contract_product(hidden, edown_full, 1, 1).reshape(ranks, slot_count, width)
    back = lax.all_to_all(
        partial_value.astype(jnp.bfloat16), "ctx", split_axis=0, concat_axis=0, tiled=True
    ).astype(partial_value.dtype)
    expert_gate_part = gate_part.reshape(ranks, slot_count, -1)
    expert_up_part = up_projection_part.reshape(ranks, slot_count, -1)
    combined = jnp.sum(back.reshape(experts, split_count, capacity, width), axis=1).reshape(
        experts * capacity, width
    )
    pair_out = jnp.where(kept_pairs[:, None], combined[target_pick], 0.0).reshape(
        rows_dev, top_count, width
    )
    mixture = jnp.sum(gates[:, :, None] * pair_out, axis=1)
    sgate_part = jnp.dot(mixer, sgate_full, preferred_element_type=jnp.float32)
    sup_part = jnp.dot(mixer, sup_full, preferred_element_type=jnp.float32)
    shared_act, shared_slope = silu_parts(sgate_part)
    shared_hidden = (shared_act * sup_part).astype(jnp.bfloat16)
    shared_out = jnp.dot(shared_hidden, sdown_full, preferred_element_type=jnp.float32)
    result = (second + mixture + shared_out).astype(jnp.bfloat16)
    grad_final = cotangent[0].astype(jnp.float32)
    grad_low = grad_final.astype(jnp.bfloat16)
    sdown_grad = contract_product(shared_hidden, grad_low, 0, 0)
    grad_shared_hidden = contract_product(grad_low, sdown_full, 1, 1)
    grad_sgate = (grad_shared_hidden * sup_part * shared_slope).astype(jnp.bfloat16)
    grad_sup = (grad_shared_hidden * shared_act).astype(jnp.bfloat16)
    sgate_grad = contract_product(mixer, grad_sgate, 0, 0)
    sup_grad = contract_product(mixer, grad_sup, 0, 0)
    grad_mixer = contract_product(grad_sgate, sgate_full, 1, 1) + contract_product(
        grad_sup, sup_full, 1, 1
    )
    pair_grad = (
        (gates[:, :, None] * grad_final[:, None, :]).reshape(pair_count, width).astype(jnp.bfloat16)
    )
    grad_gates = jnp.sum(grad_final[:, None, :] * pair_out, axis=2)
    send_grad = jnp.where(valid[:, None], pair_grad[pair_pick], jnp.zeros((), jnp.bfloat16))
    send_grad = jnp.broadcast_to(
        send_grad.reshape(experts, 1, capacity, width), (experts, split_count, capacity, width)
    ).reshape(ranks, capacity, width)
    recv_grad = lax.all_to_all(send_grad, "ctx", split_axis=0, concat_axis=0, tiled=True)
    flattened_input = received.reshape(ranks * capacity, width)
    flat_grad = recv_grad.reshape(ranks * capacity, width)
    gate_flat = expert_gate_part.reshape(ranks * capacity, -1)
    up_flat = expert_up_part.reshape(ranks * capacity, -1)
    expert_activation, expert_slope = silu_parts(gate_flat)
    expert_hidden = (expert_activation * up_flat).astype(jnp.bfloat16)
    edown_grad = contract_product(flat_grad, expert_hidden, 0, 0)
    expert_hidden_grad = jnp.dot(flat_grad, edown_full, preferred_element_type=jnp.float32)
    expert_gate_grad_rows = (expert_hidden_grad * up_flat * expert_slope).astype(jnp.bfloat16)
    expert_up_grad_rows = (expert_hidden_grad * expert_activation).astype(jnp.bfloat16)
    egate_grad = contract_product(flattened_input, expert_gate_grad_rows, 0, 0)
    expert_up_weight_grad = contract_product(flattened_input, expert_up_grad_rows, 0, 0)
    input_back = (
        contract_product(expert_gate_grad_rows, expert_gate_whole, 1, 1)
        + contract_product(expert_up_grad_rows, expert_up_whole, 1, 1)
    ).reshape(ranks, capacity, width)
    back_grad = lax.all_to_all(
        input_back.astype(jnp.bfloat16), "ctx", split_axis=0, concat_axis=0, tiled=True
    ).astype(input_back.dtype)
    merged = jnp.sum(back_grad.reshape(experts, split_count, capacity, width), axis=1).reshape(
        experts * capacity, width
    )
    pair_back = jnp.where(kept_pairs[:, None], merged[target_pick], 0.0).reshape(
        rows_dev, top_count, width
    )
    grad_mixer = grad_mixer + jnp.sum(pair_back, axis=1)
    grad_chosen = gates * (grad_gates - jnp.sum(gates * grad_gates, axis=1, keepdims=True))
    grad_logits = jnp.sum(jnp.where(expert_match, grad_chosen[:, :, None], 0.0), axis=1)
    router_grad = contract_exact(mixer.astype(jnp.float32), grad_logits, 0, 0)
    grad_mixer = grad_mixer + contract_exact(grad_logits, router_full.astype(jnp.float32), 1, 1)
    through_two, gain_two_grad = rms_back(second, scale_two, gain_second, grad_mixer)
    grad_second = grad_final + through_two
    grad_attention = grad_second.astype(jnp.bfloat16)
    output_grad = contract_product(mixed_low, grad_attention, 0, 0)
    grad_mixed = contract_product(grad_attention, output_full, 1, 1).astype(jnp.bfloat16)
    grad_out3 = grad_mixed.reshape(rows_dev, heads, HD)
    delta = jnp.sum(grad_out3.astype(jnp.float32) * mixed3, axis=2).T
    all_keys, all_values = (
        lax.all_gather(key_rot, "ctx", axis=0, tiled=True),
        lax.all_gather(value_low, "ctx", axis=0, tiled=True),
    )
    total_rows = all_keys.shape[0]
    block_size = KEY_ROWS

    def query_step(grad_sum, offset):
        key_rows = lax.dynamic_slice_in_dim(all_keys, offset, block_size, 0)
        value_rows = lax.dynamic_slice_in_dim(all_values, offset, block_size, 0)
        key_place = places(offset, block_size, block_deal, rows_dev)
        unused, grad_scores = differentiate(
            query_side, log_total, delta, grad_out3, key_rows, value_rows, key_place
        )
        key3 = key_rows.reshape(block_size, heads, HD)
        return (
            grad_sum
            + jnp.einsum("hqk,khd->qhd", grad_scores, key3, preferred_element_type=jnp.float32),
            None,
        )

    offsets = jnp.arange(total_rows // block_size, dtype=jnp.int32) * block_size
    grad_query3, unused = lax.scan(
        query_step, jnp.zeros((rows_dev, heads, HD), jnp.float32), offsets
    )
    inner_size = KEY_ROWS

    def one_part(offset):
        key_rows = lax.dynamic_slice_in_dim(all_keys, offset, inner_size, 0)
        value_rows = lax.dynamic_slice_in_dim(all_values, offset, inner_size, 0)
        key_place = places(offset, inner_size, block_deal, rows_dev)
        probs_full, grad_scores = differentiate(
            query_side, log_total, delta, grad_out3, key_rows, value_rows, key_place
        )
        grad_value_rows = jnp.einsum(
            "hqk,qhd->khd",
            probs_full.astype(jnp.bfloat16),
            grad_out3,
            preferred_element_type=jnp.float32,
        )
        grad_key_rows = jnp.einsum(
            "hqk,qhd->khd", grad_scores, query3, preferred_element_type=jnp.float32
        )
        return jnp.concatenate(
            [grad_key_rows.reshape(inner_size, width), grad_value_rows.reshape(inner_size, width)],
            axis=1,
        )

    parts = lax.map(
        one_part,
        jnp.arange(lax.axis_size("ctx") * rows_dev // inner_size, dtype=jnp.int32) * inner_size,
    )
    key_value_grad = lax.psum_scatter(
        parts.reshape(lax.axis_size("ctx") * rows_dev, 2 * width),
        "ctx",
        scatter_dimension=0,
        tiled=True,
    )
    grad_key_pre = rotate(key_value_grad[:, :width], here, -1.0).astype(jnp.bfloat16)
    grad_value_low = key_value_grad[:, width:].astype(jnp.bfloat16)
    grad_query_pre = rotate(grad_query3.reshape(rows_dev, width), here, -1.0).astype(jnp.bfloat16)
    query_grad = contract_product(normed, grad_query_pre, 0, 0)
    key_grad = contract_product(normed, grad_key_pre, 0, 0)
    value_grad = contract_product(normed, grad_value_low, 0, 0)
    grad_normed = (
        contract_product(grad_query_pre, query_full, 1, 1)
        + contract_product(grad_key_pre, key_full, 1, 1)
        + contract_product(grad_value_low, value_full, 1, 1)
    )
    through_one, gain_one_grad = rms_back(inputs, scale_one, gain_first, grad_normed)
    grad_input = grad_second + through_one
    (
        gain_one_share,
        query_share,
        key_share,
        value_share,
        output_share,
        gain_two_share,
        router_share,
        sgate_share,
        sup_share,
        sdown_share,
        egate_share,
        expert_up_portion,
        edown_share,
    ) = (
        lax.psum_scatter(
            gain_one_grad.astype(jnp.bfloat16), "wt", scatter_dimension=0, tiled=True
        ).astype(jnp.float32),
        lax.psum_scatter(
            query_grad.astype(jnp.bfloat16), "wt", scatter_dimension=0, tiled=True
        ).astype(jnp.float32),
        lax.psum_scatter(
            key_grad.astype(jnp.bfloat16), "wt", scatter_dimension=0, tiled=True
        ).astype(jnp.float32),
        lax.psum_scatter(
            value_grad.astype(jnp.bfloat16), "wt", scatter_dimension=0, tiled=True
        ).astype(jnp.float32),
        lax.psum_scatter(
            output_grad.astype(jnp.bfloat16), "wt", scatter_dimension=0, tiled=True
        ).astype(jnp.float32),
        lax.psum_scatter(
            gain_two_grad.astype(jnp.bfloat16), "wt", scatter_dimension=0, tiled=True
        ).astype(jnp.float32),
        lax.psum_scatter(
            router_grad.astype(jnp.bfloat16), "wt", scatter_dimension=0, tiled=True
        ).astype(jnp.float32),
        lax.psum_scatter(
            sgate_grad.astype(jnp.bfloat16), "wt", scatter_dimension=0, tiled=True
        ).astype(jnp.float32),
        lax.psum_scatter(
            sup_grad.astype(jnp.bfloat16), "wt", scatter_dimension=0, tiled=True
        ).astype(jnp.float32),
        lax.psum_scatter(
            sdown_grad.astype(jnp.bfloat16), "wt", scatter_dimension=0, tiled=True
        ).astype(jnp.float32),
        lax.psum_scatter(
            egate_grad.astype(jnp.bfloat16), "wt", scatter_dimension=0, tiled=True
        ).astype(jnp.float32),
        lax.psum_scatter(
            expert_up_weight_grad.astype(jnp.bfloat16), "wt", scatter_dimension=0, tiled=True
        ).astype(jnp.float32),
        lax.psum_scatter(
            edown_grad.astype(jnp.bfloat16), "wt", scatter_dimension=0, tiled=True
        ).astype(jnp.float32),
    )
    (
        gain_one_sum,
        query_sum,
        key_sum,
        value_sum,
        output_sum,
        gain_two_sum,
        router_sum,
        sgate_sum,
        sup_sum,
        sdown_sum,
    ) = lax.psum(
        (
            gain_one_share,
            query_share,
            key_share,
            value_share,
            output_share,
            gain_two_share,
            router_share,
            sgate_share,
            sup_share,
            sdown_share,
        ),
        "ctx",
    )
    return (
        result[None],
        grad_input[None],
        gain_one_sum,
        query_sum,
        key_sum,
        value_sum,
        output_sum,
        gain_two_sum,
        router_sum,
        sgate_sum,
        sup_sum,
        sdown_sum,
        egate_share,
        expert_up_portion,
        edown_share,
    )


def fast_body(
    tokens,
    cotangent,
    gain_attention,
    query_weight,
    key_weight,
    value_weight,
    output_weight,
    gain_mixer,
    router_weight,
    shared_gate,
    shared_up,
    shared_down,
    expert_gate,
    expert_up,
    expert_down,
    routes,
    slot_order,
    block_deal,
):
    rows_dev = tokens.shape[1]
    ranks = lax.axis_size("ctx")
    here, cosr, sinr = angles_of(block_deal, rows_dev)
    kb = (places(0, ranks * rows_dev, block_deal, rows_dev) // BLK)[None, :]
    qb = jnp.concatenate([here // BLK] * 2)[:, None]
    pack = pack_params(gain_attention, gain_mixer, router_weight)
    (
        q_st, mixed, lse, normed, pack_all, result, grad_second, pack_grad, dsh, kv_all, wfull,
        keep, give, other0,
    ) = run_forward(
        tokens[0], pack, cosr, sinr, kb, qb, cotangent[0], routes[0], slot_order[0], shared_down,
        query_weight, key_weight, value_weight, output_weight, shared_gate, shared_up,
        expert_gate, expert_up, expert_down,
    )
    grad_input, pack_sum, att1, att2, sh, other = run_backward(
        grad_second, tokens[0], pack_all, pack_grad, normed, mixed, q_st, lse, cosr, sinr, kb, qb,
        dsh, kv_all, wfull, give,
    )
    (
        result, grad_input, gain_one, gain_two, router, query, key, value, output, gate, up, down,
        eg, eu, ed,
    ) = run_unpack(
        result, grad_input, pack_sum, att1, att2, sh, keep, other0, other, router_weight.shape[1]
    )
    return (
        result[None], grad_input[None], gain_one.reshape(-1), query, key, value, output,
        gain_two.reshape(-1), router, gate, up, down, eg, eu, ed,
    )


def solution(mesh):
    in_specs = (
        P("wt", "ctx", None),
        P("wt", "ctx", None),
        P("wt"),
        P("wt", None),
        P("wt", None),
        P("wt", None),
        P("wt", None),
        P("wt"),
        P("wt", None),
        P("wt", None),
        P("wt", None),
        P("wt", None),
        P("wt", "ctx"),
        P("wt", "ctx"),
        P("wt", "ctx"),
        P("wt", "ctx", None),
        P("wt", "ctx", None),
        P(),
    )
    out_specs = (
        P("wt", "ctx", None),
        P("wt", "ctx", None),
        P("wt"),
        P("wt", None),
        P("wt", None),
        P("wt", None),
        P("wt", None),
        P("wt"),
        P("wt", None),
        P("wt", None),
        P("wt", None),
        P("wt", None),
        P("wt", "ctx"),
        P("wt", "ctx"),
        P("wt", "ctx"),
    )
    chosen = fast_body if (mesh.shape["ctx"], mesh.shape["wt"]) == (8, 4) else body
    return jax.shard_map(chosen, mesh=mesh, in_specs=in_specs, out_specs=out_specs, check_vma=False)
```

```python
import jax
import jax.numpy as jnp
from jax import lax
from jax.experimental import pallas as pl
from jax.experimental.pallas import tpu as pltpu
from jax.sharding import PartitionSpec as P

HD = 64
BLK = 256


EPS = 1e-06
KEY_ROWS = 512
HIGH = lax.Precision.HIGHEST
MASKED = -1e30


MESH = pl.DeviceIdType.MESH
VMEM = pltpu.VMEM
BF = jnp.bfloat16
F32 = jnp.float32
PAIR = 2 * HD
VMEM_BYTES = 63 * 2**20


class Spot:
    def __init__(self, line_size):
        self.k = lax.axis_index("ctx")
        self.w = lax.axis_index("wt")
        self.z, self.x = lax.div(self.k, 2), lax.rem(self.k, 2)
        self.y, self.c = lax.div(self.w, 2), lax.rem(self.w, 2)
        self.far = lax.div(self.z, 2)
        self.mid = self.z + self.far * (3 - 2 * self.z)
        step = 1 - 2 * self.far
        self.core = (self.k, 2 * self.y + 1 - self.c)
        self.across = (self.k, 2 * (1 - self.y) + self.c)
        self.corner = (self.k, 2 * (1 - self.y) + 1 - self.c)
        self.column = (2 * self.z + 1 - self.x, self.w)
        self.odd = lax.rem(self.z, 2)
        self.line = (2 * (self.z + 1 - 2 * self.odd) + self.x, self.w)
        self.inner = (2 * (self.z + step) + self.x, self.w)
        self.outer = (2 * (self.z - step) + self.x, self.w)

    def plane(self, step):
        mirrored = (self.mid, 1 - self.mid, 2, 3)[step]
        return mirrored + self.far * (3 - 2 * mirrored)


class Sems:
    def __init__(self, ref):
        self.ref, self.used = ref, 0

    def new(self):
        self.used += 1
        return self.ref.at[self.used - 1]


def remote(src, dst, send, recv, to):
    return pltpu.make_async_remote_copy(
        src_ref=src, dst_ref=dst, send_sem=send, recv_sem=recv, device_id=to, device_id_type=MESH
    )


def greet(devices, middle=None):
    barrier = pltpu.get_barrier_semaphore()
    for to in devices:
        pl.semaphore_signal(barrier, inc=1, device_id=to, device_id_type=MESH)
    if middle is None:
        pl.semaphore_wait(barrier, len(devices))
        return

    @pl.when(middle[0] == 1)
    def _():
        pl.semaphore_signal(barrier, inc=1, device_id=middle[1], device_id_type=MESH)

    pl.semaphore_wait(barrier, len(devices) + middle[0])


class Gather:
    def __init__(self, spot, src, place, sems, local=True):
        self.spot, self.place, self.sems = spot, place, sems
        here = place(spot.w)
        self.local = pltpu.make_async_copy(src, here, sems.new()) if local else None
        self.to_core = remote(src, here, sems.new(), sems.new(), spot.core)
        self.to_across = remote(src, here, sems.new(), sems.new(), spot.across)
        self.to_across.start()
        self.to_core.start()
        if local:
            self.local.start()

    def forward(self):
        self.to_across.wait_recv()
        part = self.place(self.spot.across[1])
        self.onward = remote(part, part, self.sems.new(), self.sems.new(), self.spot.core)
        self.onward.start()

    def finish(self):
        if self.local is not None:
            self.local.wait()
        self.to_core.wait_recv()
        self.onward.wait_recv()

    def drain(self):
        for copy in (self.to_core, self.to_across, self.onward):
            copy.wait_send()


class Share:
    def __init__(self, spot, src, dst, sems, mate, bit):
        self.spot, self.dst, self.sems, self.mate, self.bit = spot, dst, sems, mate, bit
        self.rows = src.shape[0]
        self.half = self.rows // 2
        here = dst.at[pl.ds(pl.multiple_of(self.rows * spot.w, 64), self.rows)]
        half = pl.ds(pl.multiple_of(self.half * bit, 32), self.half)
        self.local = pltpu.make_async_copy(src, here, sems.new())
        self.to_core = remote(src, here, sems.new(), sems.new(), spot.core)
        self.to_across = remote(
            src.at[half], self.part(spot.w, bit), sems.new(), sems.new(), spot.across
        )
        for copy in (self.to_across, self.to_core, self.local):
            copy.start()

    def part(self, w, bit):
        return self.dst.at[pl.ds(pl.multiple_of(self.rows * w + self.half * bit, 32), self.half)]

    def forward(self):
        spot = self.spot
        self.to_across.wait_recv()
        part = self.part(spot.across[1], self.bit)
        self.aside = remote(part, part, self.sems.new(), self.sems.new(), self.mate)
        self.onward = remote(part, part, self.sems.new(), self.sems.new(), spot.core)
        self.aside.start()
        self.onward.start()

    def second(self):
        self.aside.wait_recv()
        part = self.part(self.spot.across[1], 1 - self.bit)
        self.rest = remote(part, part, self.sems.new(), self.sems.new(), self.spot.core)
        self.rest.start()

    def finish(self):
        self.local.wait()
        self.to_core.wait_recv()
        self.onward.wait_recv()
        self.rest.wait_recv()

    def drain(self):
        for copy in (self.to_core, self.to_across, self.aside, self.onward, self.rest):
            copy.wait_send()


class ShareColumns:
    def __init__(self, spot, src, dst, sems, mate, bit):
        self.spot, self.dst, self.sems, self.mate, self.bit = spot, dst, sems, mate, bit
        self.rows, self.part_cols = src.shape[0], dst.shape[1]
        self.half = self.rows // 2
        half = pl.ds(pl.multiple_of(self.half * bit, 32), self.half)

        def columns(to):
            return pl.ds(pl.multiple_of(self.part_cols * to, self.part_cols), self.part_cols)

        here = dst.at[pl.ds(pl.multiple_of(self.rows * spot.w, 64), self.rows)]
        self.halves = [
            remote(
                src.at[half, columns(to[1])],
                self.part(spot.w, bit),
                sems.new(),
                sems.new(),
                to,
            )
            for to in (spot.across, spot.corner)
        ]
        self.to_core = remote(
            src.at[:, columns(spot.core[1])], here, sems.new(), sems.new(), spot.core
        )
        self.local = pltpu.make_async_copy(src.at[:, columns(spot.w)], here, sems.new())
        for copy in self.halves + [self.to_core, self.local]:
            copy.start()

    def part(self, w, bit):
        return self.dst.at[pl.ds(pl.multiple_of(self.rows * w + self.half * bit, 32), self.half)]

    def forward(self):
        self.aside = []
        for copy, source in zip(self.halves, (self.spot.across, self.spot.corner)):
            copy.wait_recv()
            part = self.part(source[1], self.bit)
            self.aside.append(remote(part, part, self.sems.new(), self.sems.new(), self.mate))
            self.aside[-1].start()

    def finish(self):
        self.local.wait()
        self.to_core.wait_recv()
        for copy in self.aside:
            copy.wait_recv()

    def drain(self):
        for copy in self.halves + self.aside + [self.to_core]:
            copy.wait_send()


class Merge:
    def __init__(self, spot, send, land, sems):
        self.spot, self.send, self.land = spot, send, land
        self.far = remote(
            send.at[spot.corner[1]], land.at[0], sems.new(), sems.new(), spot.core
        )
        self.near = remote(send.at[spot.core[1]], land.at[1], sems.new(), sems.new(), spot.core)
        self.over = remote(
            send.at[spot.across[1]], land.at[2], sems.new(), sems.new(), spot.across
        )
        self.far.start()
        self.near.start()

    def forward(self):
        self.far.wait_recv()
        block = self.send.at[self.spot.across[1]]
        block[...] = (block[...].astype(F32) + self.land[0].astype(F32)).astype(BF)
        self.over.start()

    def finish(self):
        self.near.wait_recv()
        self.over.wait_recv()
        own = self.send[self.spot.w].astype(F32)
        return own + self.land[1].astype(F32) + self.land[2].astype(F32)

    def drain(self):
        for copy in (self.far, self.near, self.over):
            copy.wait_send()


class Spread:
    def __init__(self, spot, pick, place, sems):
        self.copies = []
        for to in (spot.across, spot.corner, spot.core):
            self.copies.append(remote(pick(to[1]), place(spot.w), sems.new(), sems.new(), to))
        self.local = pltpu.make_async_copy(pick(spot.w), place(spot.w), sems.new())
        for copy in self.copies:
            copy.start()
        self.local.start()

    def finish(self):
        for copy in self.copies:
            copy.wait_recv()
        self.local.wait()

    def drain(self):
        for copy in self.copies:
            copy.wait_send()


def nt(left, right):
    return lax.dot_general(left, right, (((1,), (1,)), ((), ())), preferred_element_type=F32)


def nn(left, right):
    return jnp.dot(left, right, preferred_element_type=F32)


def tn(left, right):
    return lax.dot_general(left, right, (((0,), (0,)), ((), ())), preferred_element_type=F32)


def turn(values, cosine, sine):
    wide = values.shape[1]
    lane = lax.broadcasted_iota(jnp.int32, values.shape, 1)
    first = lax.rem(lane, HD) < HD // 2
    swapped = jnp.where(
        first, pltpu.roll(values, wide - HD // 2, 1), pltpu.roll(values, HD // 2, 1)
    )
    copies = wide // PAIR
    cosine = jnp.concatenate([cosine] * copies, axis=1)
    sine = jnp.concatenate([sine] * copies, axis=1)
    return values * cosine + swapped * sine


def stack_pair(values):
    lane = lax.broadcasted_iota(jnp.int32, values.shape, 1)
    none = jnp.zeros_like(values)
    return jnp.concatenate(
        [jnp.where(lane < HD, values, none), jnp.where(lane < HD, none, values)], axis=0
    )


def unstack_pair(values):
    rows = values.shape[0] // 2
    lane = lax.broadcasted_iota(jnp.int32, (rows, PAIR), 1)
    return jnp.where(lane < HD, values[:rows], values[rows:])


class Ring:
    def __init__(self, spot, blocks, recv, send, parts=1):
        self.spot, self.blocks, self.recv, self.send, self.parts = spot, blocks, recv, send, parts
        self.ranks = blocks.shape[0]
        self.used = 0
        self.sent, self.sent_mid, self.sent_end = [], [], []

    def piece(self, slot, part):
        rows = self.blocks.shape[1] // self.parts
        return self.blocks.at[slot, pl.ds(rows * part, rows)]

    def copy(self, slot, part, to):
        self.used += 1
        return remote(
            self.piece(slot, part),
            self.piece(slot, part),
            self.send.at[self.used - 1],
            self.recv.at[slot + self.ranks * part],
            to,
        )

    def arrived(self, slot, part):
        remote(
            self.piece(slot, part),
            self.piece(slot, part),
            self.send.at[0],
            self.recv.at[slot + self.ranks * part],
            self.spot.column,
        ).wait_recv()

    def start(self):
        spot = self.spot
        for part in range(self.parts):
            own = self.copy(spot.k, part, spot.inner)
            side = self.copy(spot.k, part, spot.column)
            back = self.copy(spot.k, part, spot.outer)
            own.start()
            self.middle(back)
            side.start()
            self.sent += [own, side]
            self.sent_mid += [back]

    def middle(self, copy):
        @pl.when(self.spot.mid == 1)
        def _():
            copy.start()

    def step(self, number, only=None):
        spot = self.spot
        slot = 2 * spot.plane(number) + spot.x
        onward = spot.inner if number == 1 else spot.outer
        pieces = []
        for part in range(self.parts):
            along = self.copy(slot, part, onward) if only != 0 else None
            pieces.append((along, self.copy(slot, part, spot.column)))
        if only != 0:

            @pl.when(spot.mid == 1)
            def _():
                for part, (along, side) in enumerate(pieces):
                    self.arrived(slot, part)
                    along.start()
                    side.start()

        if only != 1:

            @pl.when(spot.mid == 0)
            def _():
                for part, (along, side) in enumerate(pieces):
                    self.arrived(slot, part)
                    side.start()

        if only != 0:
            self.sent_mid += [along for along, _ in pieces]
            self.sent_mid += [side for _, side in pieces]
        if only != 1:
            self.sent_end += [side for _, side in pieces]

    def other(self, number):
        for part in range(self.parts):
            self.arrived(2 * self.spot.plane(number) + 1 - self.spot.x, part)

    def drain(self):
        for copy in self.sent:
            copy.wait_send()
        for role, copies in ((0, self.sent_end), (1, self.sent_mid)):

            @pl.when(self.spot.mid == role)
            def _(copies=copies):
                for copy in copies:
                    copy.wait_send()


class Reduce:
    def __init__(self, spot, part, sides, zo, zi, sems, folded=False, parts=1):
        self.spot, self.part, self.sides, self.zo, self.zi = spot, part, sides, zo, zi
        self.x_send, self.x_recv, self.z_send, self.zo_recv, self.zi_recv = (
            sems.at[i] for i in range(5)
        )
        self.folded, self.parts = folded, parts
        self.rows = part.shape[1] // parts
        self.sent, self.sent_end, self.sent_mid = [], [], []

    def cut(self, ref, index, h):
        return ref.at[index, pl.ds(self.rows * h, self.rows)]

    def own(self, plane, h):
        return self.cut(self.part, plane if self.folded else 2 * plane + self.spot.x, h)

    def wait(self, land, recv, plane, h):
        piece = self.cut(land, plane, h)
        at = plane + 4 * h
        remote(piece, piece, self.z_send.at[at], recv.at[at], self.spot.column).wait_recv()

    def side(self, number):
        spot = self.spot
        plane = spot.plane(number)
        for h in range(self.parts):
            at = plane + 4 * h
            copy = remote(
                self.cut(self.part, 2 * plane + 1 - spot.x, h),
                self.cut(self.sides, plane, h),
                self.x_send.at[at],
                self.x_recv.at[at],
                spot.column,
            )
            copy.start()
            self.sent.append(copy)

    def add(self, ref, land):
        ref[...] = (ref[...].astype(F32) + land[...].astype(F32)).astype(BF)

    def meet(self, number):
        plane = self.spot.plane(number)
        for h in range(self.parts):
            self.wait(self.sides, self.x_recv, plane, h)
            self.add(self.own(plane, h), self.cut(self.sides, plane, h))
            if number > 0 and self.zo is not None:
                self.launch_part(number, h)

    def launch(self, number):
        for h in range(self.parts):
            self.launch_part(number, h)

    def launch_part(self, number, h):
        plane = self.spot.plane(number)
        at = plane + 4 * h
        copy = remote(
            self.own(plane, h),
            self.cut(self.zo, plane, h),
            self.z_send.at[at],
            self.zo_recv.at[at],
            self.spot.inner,
        )

        @pl.when(self.spot.mid == 0)
        def _():
            copy.start()

        self.sent_end.append(copy)

    def relay(self, number):
        plane = self.spot.plane(number)
        land, recv = (self.zi, self.zi_recv) if number == 1 else (self.zo, self.zo_recv)
        copies = []
        for h in range(self.parts):
            at = plane + 4 * h
            copies.append(
                remote(
                    self.own(plane, h),
                    self.cut(self.zi, plane, h),
                    self.z_send.at[at],
                    self.zi_recv.at[at],
                    self.spot.outer if number == 1 else self.spot.inner,
                )
            )

        @pl.when(self.spot.mid == 1)
        def _():
            for h, copy in enumerate(copies):
                self.wait(land, recv, plane, h)
                self.add(self.own(plane, h), self.cut(land, plane, h))
                copy.start()

        self.sent_mid += copies

    def last(self, result):
        plane = self.spot.plane(0)
        for h in range(self.parts):
            self.wait(self.zi, self.zi_recv, plane, h)
            rows = pl.ds(self.rows * h, self.rows)
            total = self.own(plane, h)[...].astype(F32)
            result[rows] = total + self.cut(self.zi, plane, h)[...].astype(F32)

        @pl.when(self.spot.mid == 1)
        def _():
            for h in range(self.parts):
                self.wait(self.zo, self.zo_recv, plane, h)
                rows = pl.ds(self.rows * h, self.rows)
                result[rows] += self.cut(self.zo, plane, h)[...].astype(F32)

    def drain(self):
        for copy in self.sent:
            copy.wait_send()

        @pl.when(self.spot.mid == 0)
        def _():
            for copy in self.sent_end:
                copy.wait_send()

        @pl.when(self.spot.mid == 1)
        def _():
            for copy in self.sent_mid:
                copy.wait_send()


def swish(values):
    sigmoid = 1.0 / (1.0 + jnp.exp(-values))
    return values * sigmoid, sigmoid * (1.0 + values * (1.0 - sigmoid))


class Exchange:
    def __init__(self, spot, out, back, send, recv):
        self.spot, self.out, self.back = spot, out, back
        self.send, self.recv, self.ranks = send, recv, out.shape[0]
        self.copies = []

    def start(self):
        spot = self.spot
        for offset in range(1, self.ranks):
            peer = lax.rem(spot.k + offset, self.ranks)
            self.copies.append(
                remote(
                    self.out.at[peer],
                    self.back.at[spot.k],
                    self.send.at[offset],
                    self.recv.at[spot.k],
                    (peer, spot.w),
                )
            )
            self.copies[-1].start()
        self.back[spot.k] = self.out[spot.k]

    def finish(self):
        spot = self.spot
        for offset in range(1, self.ranks):
            peer = lax.rem(spot.k + offset, self.ranks)
            remote(
                self.out.at[peer],
                self.back.at[peer],
                self.send.at[offset],
                self.recv.at[peer],
                (peer, spot.w),
            ).wait_recv()

    def drain(self):
        for copy in self.copies:
            copy.wait_send()


def fold_rows(values, ref):
    ranks = ref.shape[0]
    slots = values.shape[0] // ranks
    for e in range(ranks):
        part = values[slots * e : slots * (e + 1)]
        tiles = [part[:, 128 * t : 128 * (t + 1)] for t in range(values.shape[1] // 128)]
        ref[e] = jnp.concatenate(tiles, axis=0).astype(BF)


def unfold_rows(ref, slots):
    parts = []
    for e in range(ref.shape[0]):
        part = ref[e].astype(F32)
        tiles = [part[slots * t : slots * (t + 1)] for t in range(part.shape[0] // slots)]
        parts.append(jnp.concatenate(tiles, axis=1))
    return jnp.concatenate(parts, axis=0).astype(BF)


def split_three(values):
    high = values.astype(BF)
    rest = values - high.astype(F32)
    middle = rest.astype(BF)
    return high, middle, (rest - middle.astype(F32)).astype(BF)


def diagonal(values, axis):
    size = max(values.shape)
    down = lax.broadcasted_iota(jnp.int32, (size, size), 0)
    along = lax.broadcasted_iota(jnp.int32, (size, size), 1)
    return jnp.sum(
        jnp.where(down == along, values.astype(F32), 0.0), axis=axis, keepdims=True
    ).astype(jnp.int32)


def slot_maps(routes, order, slots, experts):
    rows, top = routes.shape
    pairs = rows * top
    columns = [routes[:, j : j + 1] for j in range(top)]
    e_col = jnp.concatenate(columns, axis=0)
    e_row = jnp.concatenate([diagonal(column, 0) for column in columns], axis=1)
    o_row = lax.rem(order, top) * rows + lax.div(order, top)
    o_col = diagonal(o_row, 1)
    down = lax.broadcasted_iota(jnp.int32, (pairs, pairs), 0)
    along = lax.broadcasted_iota(jnp.int32, (pairs, pairs), 1)
    turn_row = jnp.sum(jnp.where(o_col == along, down.astype(F32), 0.0), axis=0, keepdims=True)
    turn_col = jnp.sum(jnp.where(o_row == down, along.astype(F32), 0.0), axis=1, keepdims=True)
    same = e_col == e_row
    slot_row = jnp.sum(
        jnp.where(same & (turn_col < turn_row), 1.0, 0.0), axis=0, keepdims=True
    ).astype(jnp.int32)
    slot_col = jnp.sum(
        jnp.where(same & (turn_row < turn_col), 1.0, 0.0), axis=1, keepdims=True
    ).astype(jnp.int32)
    target_row = jnp.where(slot_row < slots, e_row * slots + slot_row, -1)
    target_col = jnp.where(slot_col < slots, e_col * slots + slot_col, -1)
    total = experts * slots
    place = lax.broadcasted_iota(jnp.int32, (total, pairs), 0)
    to_slots = jnp.where(place == target_row, 1.0, 0.0).astype(BF)
    place = lax.broadcasted_iota(jnp.int32, (pairs, total), 1)
    to_pairs = jnp.where(place == target_col, 1.0, 0.0).astype(BF)
    return to_slots, to_pairs


def forward_kernel(
    tok, gain_one, gain_two, router_ref, freq, deal, cot, routes, order, sd,
    wq, wk, wv, wo, sg, su, eg, eu, ed,
    cosr, sinr, kb, qb, q_out, mixed_out, lse_out, normed_out, pack_out, result_out, grad_second_out, pack_grad_out,
    dsh_out, kv_out, wfull_out, keep_out, give_out, other_out,
    wbuf, kv, pack, packs, top, low, acc, sg_all, su_all, wg, wu, wd, mix, m4, cot4,
    sh_send, sh_recv, gm_send, gm_recv, xs, xr, gs, gr, os, orr, bs, br,
    x_s, g_s, sum_s, gate_s, up_s, hid_s, dgate_s, dup_s, dsh, dsh_x, slot_s, pair_s, cb,
    sem, kv_recv, kv_send, a2a_send, a2a_recv, sem_sh,
):
    spot = Spot(4)
    sems = Sems(sem)
    rows, width = tok.shape
    pairs = width // PAIR
    ranks = xs.shape[0]
    slots = xs.shape[1] * 128 // width
    hidden = wg.shape[1]
    shard = width // 4
    part = sg_all.shape[1]
    peers = [(lax.rem(spot.k + o, ranks), spot.w) for o in range(1, ranks)]
    greet([spot.core, spot.across, spot.corner] + peers)
    column = (spot.column, spot.x)
    key_w = Share(spot, wk, wbuf.at[1], sems, *column)
    value_w = Share(spot, wv, wbuf.at[2], sems, *column)
    shards = jnp.concatenate(
        [
            jnp.concatenate([gain_one[...], gain_two[...]], axis=0).astype(F32),
            router_ref[...].astype(F32).T,
            jnp.zeros((16 - 2 - router_ref.shape[1], shard), F32),
        ],
        axis=0,
    )
    shards = jnp.concatenate([shards, jnp.zeros((16, width - shard), F32)], axis=1)
    pack[...] = pltpu.roll(shards, shard * spot.w, 1).astype(BF)
    params = Gather(spot, pack, lambda w: packs.at[w], sems)
    query_w = Share(spot, wq, wbuf.at[0], sems, *column)
    inputs = tok[...].astype(F32)
    scale = lax.rsqrt(jnp.mean(inputs * inputs, axis=-1, keepdims=True) + EPS)
    scaled = inputs * scale
    piece = rows // 2
    inner = lax.broadcasted_iota(jnp.int32, (rows, 1), 0)
    paired = deal[spot.k]
    unit = jnp.where(inner < piece, paired, 2 * ranks - 1 - paired)
    place = unit * piece + lax.rem(inner, piece)
    qb[...] = jnp.concatenate([lax.div(place, BLK)] * 2, axis=0)
    along = lax.broadcasted_iota(jnp.int32, (1, rows), 1)
    for r in range(ranks):
        unit = jnp.where(along < piece, deal[r], 2 * ranks - 1 - deal[r])
        kb[:, rows * r : rows * (r + 1)] = lax.div(unit * piece + lax.rem(along, piece), BLK)
    angles = place.astype(F32) * freq[...]
    cosr[...] = jnp.cos(angles)
    lane = lax.broadcasted_iota(jnp.int32, angles.shape, 1)
    sinr[...] = jnp.sin(angles) * jnp.where(lax.rem(lane, HD) < HD // 2, -1.0, 1.0)
    params.forward()
    params.finish()
    pack_all = (packs[0].astype(F32) + packs[1].astype(F32)) + (
        packs[2].astype(F32) + packs[3].astype(F32)
    )
    pack_out[...] = pack_all
    normed = (scaled * pack_all[0:1]).astype(BF)
    normed_out[...] = normed
    cosine, sine = cosr[...], sinr[...]
    key_w.forward()
    to_slots, to_pairs = slot_maps(routes[...], order[...], slots, ranks)
    slot_s[...] = to_slots
    pair_s[...] = to_pairs
    value_w.forward()
    key_w.second()
    query_w.forward()
    key_w.finish()
    kv[spot.k, :, 0:width] = turn(nn(normed, wbuf[1]), cosine, sine).astype(BF)
    value_w.second()
    value_w.finish()
    kv[spot.k, :, width : 2 * width] = nn(normed, wbuf[2]).astype(BF)
    ring = Ring(spot, kv, kv_recv, kv_send, parts=2)
    ring.start()
    query_w.second()

    def stripe(ref):
        return lambda w: ref.at[pl.ds(pl.multiple_of(shard * w, 64), shard)]

    line = (spot.line, spot.odd)
    gate_w = Gather(spot, eg, stripe(wg), sems)
    out_w = Share(spot, wo, wbuf.at[3], sems, *line)
    cot_w = Gather(spot, cot, lambda w: cot4.at[w], sems)
    sg_w = ShareColumns(spot, sg, sg_all, sems, *line)
    su_w = ShareColumns(spot, su, su_all, sems, *line)
    up_w = Gather(spot, eu, stripe(wu), sems)
    query_w.finish()
    query = turn(nn(normed, wbuf[0]), cosine, sine).astype(BF) * jnp.asarray(HD**-0.5, BF)
    for j in range(pairs):
        q_out[j] = stack_pair(query[:, PAIR * j : PAIR * (j + 1)])
    top[...] = jnp.full_like(top, MASKED)
    low[...] = jnp.zeros_like(low)
    acc[...] = jnp.zeros_like(acc)
    q_block = qb[...]

    def chunk(plane):
        k_block = kb[:, pl.ds(pl.multiple_of(2 * rows * plane, 2 * rows), 2 * rows)]
        allowed = k_block <= q_block

        def one_pair(j, carry):
            lane = pl.multiple_of(PAIR * j, PAIR)
            key = kv[pl.ds(2 * plane, 2), :, pl.ds(lane, PAIR)].reshape(2 * rows, PAIR)
            value = kv[pl.ds(2 * plane, 2), :, pl.ds(width + lane, PAIR)].reshape(2 * rows, PAIR)
            scores = jnp.where(allowed, nt(q_out[j], key), MASKED)
            old = top[j]
            new = jnp.maximum(old, jnp.max(scores, axis=1, keepdims=True))
            raised = jnp.where(allowed, jnp.exp(scores - new[:, 0:1]), 0.0)
            factor = jnp.exp(old - new)
            top[j] = new
            low[j] = low[j] * factor + jnp.sum(raised, axis=1, keepdims=True)
            acc[j] = acc[j] * factor + nn(raised.astype(BF), value)
            return carry

        lax.fori_loop(0, pairs, one_pair, 0)

    ring.step(1)
    ring.step(2, only=1)
    ring.other(0)
    chunk(spot.plane(0))
    ring.step(2, only=0)
    ring.step(3, only=1)
    ring.other(1)
    chunk(spot.plane(1))
    ring.step(3, only=0)
    out_w.forward()
    ring.other(2)
    chunk(spot.plane(2))
    out_w.second()
    cot_w.forward()
    ring.other(3)
    chunk(spot.plane(3))
    saves = [pltpu.make_async_copy(kv, kv_out, sems.new())]
    saves[0].start()
    for j in range(pairs):
        mixed_out[:, PAIR * j : PAIR * (j + 1)] = unstack_pair(acc[j] / low[j])
        lse_out[j] = top[j] + jnp.log(low[j])
    out_w.finish()
    saves.append(pltpu.make_async_copy(wbuf, wfull_out, sems.new()))
    saves[1].start()
    second = inputs + nn(mixed_out[...].astype(BF), wbuf[3])
    scale = lax.rsqrt(jnp.mean(second * second, axis=-1, keepdims=True) + EPS)
    mixer = (second * scale * pack_all[1:2]).astype(BF)
    mix[...] = mixer

    mixers = Gather(spot, mix, lambda w: m4.at[w], sems)
    down_w = Gather(spot, ed, stripe(wd), sems)
    fold_rows(nn(slot_s[:, :rows] + slot_s[:, rows:], mixer), xs)
    rows_out = Exchange(spot, xs, xr, a2a_send.at[0], a2a_recv.at[0])
    rows_out.start()
    router = pack_all[2:16].astype(BF)
    router = jnp.concatenate([router, jnp.zeros((2, width), BF)], axis=0)
    logits = nt(mixer, router)
    lane = lax.broadcasted_iota(jnp.int32, logits.shape, 1)
    matches = [lane == routes[:, j : j + 1] for j in range(2)]
    chosen = [jnp.sum(jnp.where(m, logits, 0.0), axis=1, keepdims=True) for m in matches]
    largest = jnp.maximum(chosen[0], chosen[1])
    raised = [jnp.exp(c - largest) for c in chosen]
    gates = [r / (raised[0] + raised[1]) for r in raised]
    grad = cot[...].astype(F32)
    pair_grad = jnp.concatenate([(g * grad).astype(BF) for g in gates], axis=0)
    fold_rows(nn(slot_s[...], pair_grad), gs)
    grads_out = Exchange(spot, gs, gr, a2a_send.at[1], a2a_recv.at[1])
    grads_out.start()
    sg_w.forward()
    su_w.forward()
    gate_w.forward()
    up_w.forward()
    mixers.forward()

    for part_w in (sg_w, su_w, cot_w, mixers):
        part_w.finish()
    rows_all = m4[...].reshape(4 * rows, width)
    grad_all = cot4[...].reshape(4 * rows, width)
    gate_part, up_part = nn(rows_all, sg_all[...]), nn(rows_all, su_all[...])
    act, slope = swish(gate_part)
    shared_hidden = (act * up_part).astype(BF)
    sh_send[...] = nn(shared_hidden, sd[...]).astype(BF).reshape(4, rows, width)
    shared_out = Merge(spot, sh_send, sh_recv, sems)
    hid_grad = nt(grad_all, sd[...])
    grad_gate = (hid_grad * up_part * slope).astype(BF)
    grad_up = (hid_grad * act).astype(BF)
    back = nt(grad_gate, sg_all[...]) + nt(grad_up, su_all[...])
    gm_send[...] = back.astype(BF).reshape(4, rows, width)
    shared_out.forward()
    shared_back = Merge(spot, gm_send, gm_recv, sems)
    half = shard // 2
    for at, values in ((0, tn(rows_all, grad_gate)), (half, tn(rows_all, grad_up))):
        values = values.astype(BF)
        for r in range(ranks):
            down, left = half * (r // 4), 128 * (r % 4)
            for w in range(4):
                dsh[r, shard * w + at : shard * w + at + half] = values[
                    shard * w + down : shard * w + down + half, left : left + 128
                ]
    values = tn(shared_hidden, grad_all).astype(BF)
    deep = values.shape[0] // ranks
    for r in range(ranks):
        for t in range(width // 128):
            dsh[r, width + deep * t : width + deep * (t + 1)] = values[
                deep * r : deep * (r + 1), 128 * t : 128 * (t + 1)
            ]
    shared_back.forward()
    shared_grad = Reduce(spot, dsh, dsh_x, None, None, sem_sh)
    for number in (3, 2, 1, 0):
        shared_grad.side(number)

    for part_w in (gate_w, up_w):
        part_w.finish()
    rows_out.finish()
    x_s[...] = unfold_rows(xr, slots)
    block = 512

    def parts(i):
        return pl.ds(pl.multiple_of(block * i, block), block)

    def up_step(i, carry):
        at = parts(i)
        gate = nn(x_s[...], wg[:, at])
        up = nn(x_s[...], wu[:, at])
        act, slope = swish(gate)
        hid_s[:, at] = (act * up).astype(BF)
        gate_s[:, at] = up * slope
        up_s[:, at] = act
        return carry

    lax.fori_loop(0, hidden // block, up_step, 0)
    grads_out.finish()
    g_s[...] = unfold_rows(gr, slots)
    down_w.forward()
    down_w.finish()

    def down_step(i, carry):
        at = parts(i)
        grad_hidden = nn(g_s[...], wd[:, at])
        dgate_s[:, at] = (grad_hidden * gate_s[:, at]).astype(BF)
        dup_s[:, at] = (grad_hidden * up_s[:, at]).astype(BF)
        return carry

    lax.fori_loop(0, hidden // block, down_step, 0)
    sum_s[...] = nt(dgate_s[...], wg[...]) + nt(dup_s[...], wu[...])
    fold_rows(sum_s[...], bs)
    backs = Exchange(spot, bs, br, a2a_send.at[3], a2a_recv.at[3])
    backs.start()
    sum_s[...] = nt(hid_s[...], wd[...])
    fold_rows(sum_s[...], os)
    outs = Exchange(spot, os, orr, a2a_send.at[2], a2a_recv.at[2])
    outs.start()

    for part_w in (gate_w, up_w, down_w):
        part_w.drain()
    swaps, across = [], []
    first = 2 * shard // 3
    sources = ((wg, x_s, dgate_s), (wu, x_s, dup_s), (wd, g_s, hid_s))

    def grads_of(a):
        ref, left, right = sources[a]

        def grad_step(i, carry):
            at = parts(i)
            ref[:, at] = tn(left[...], right[:, at]).astype(BF)
            return carry

        lax.fori_loop(0, hidden // block, grad_step, 0)
        for row in range(2):
            src = ref.at[pl.ds(pl.multiple_of(shard * (2 * row + 1 - spot.c), 64), shard)]
            swaps.append(remote(src, cb.at[a, row], sems.new(), sems.new(), spot.core))
            swaps[-1].start()

    def add_mate(a):
        ref = sources[a][0]
        for row in range(2):
            swaps[2 * a + row].wait_recv()

        def add(i, carry):
            for row in range(2):
                at = pl.ds(pl.multiple_of(shard * (2 * row + spot.c) + 16 * i, 16), 16)
                mate = cb[a, row, pl.ds(pl.multiple_of(16 * i, 16), 16)].astype(F32)
                ref[at] = (ref[at].astype(F32) + mate).astype(BF)
            return carry

        lax.fori_loop(0, shard // 16, add, 0)
        start = pl.multiple_of(shard * spot.across[1], 64)
        keep = ref.at[pl.ds(pl.multiple_of(shard * spot.w, 64), shard)]
        saves.append(pltpu.make_async_copy(keep, keep_out.at[a], sems.new()))
        if a == 0:
            across.append(
                remote(ref.at[pl.ds(start, first)], other_out, sems.new(), sems.new(), spot.across)
            )
            across[-1].start()
            give = ref.at[pl.ds(pl.multiple_of(start + first, 64), shard - first)]
            saves.append(
                pltpu.make_async_copy(give, give_out.at[0, pl.ds(first, shard - first)], sems.new())
            )
        else:
            give = ref.at[pl.ds(start, shard)]
            saves.append(pltpu.make_async_copy(give, give_out.at[a], sems.new()))
        for copy in saves[-2:]:
            copy.start()

    grads_of(0)
    grads_of(1)
    add_mate(0)
    grads_of(2)
    add_mate(1)
    add_mate(2)
    for number in (3, 2, 1, 0):
        shared_grad.meet(number)
        plane = spot.plane(number)
        dsh_out[plane] = dsh[2 * plane + spot.x]

    total = second + shared_out.finish()
    grad_mixer = shared_back.finish()
    outs.finish()
    pair_out = nn(pair_s[...], unfold_rows(orr, slots))
    pair_out = [pair_out[:rows], pair_out[rows:]]
    result_out[...] = (total + gates[0] * pair_out[0] + gates[1] * pair_out[1]).astype(BF)
    grad_gates = [jnp.sum(grad * p, axis=1, keepdims=True) for p in pair_out]
    inner = gates[0] * grad_gates[0] + gates[1] * grad_gates[1]
    grad_logits = jnp.zeros_like(logits)
    for j in range(2):
        grad_logits += jnp.where(matches[j], gates[j] * (grad_gates[j] - inner), 0.0)
    pieces = split_three(grad_logits)
    router_grad = sum(tn(piece, mixer) for piece in pieces)
    grad_mixer = grad_mixer + sum(nn(piece, router) for piece in pieces)
    backs.finish()
    grad_mixer = grad_mixer + nn(pair_s[:rows] + pair_s[rows:], unfold_rows(br, slots))
    weighted = grad_mixer * pack_all[1:2]
    mean = jnp.mean(weighted * second, axis=-1, keepdims=True)
    grad_second_out[...] = grad + scale * weighted - second * (scale * scale * scale * mean)
    gain_grad = jnp.sum(grad_mixer * second * scale, axis=0, keepdims=True)
    pack_grad_out[...] = jnp.concatenate(
        [jnp.zeros_like(gain_grad), gain_grad, router_grad[:14]], axis=0
    )
    for copy in across:
        copy.wait_recv()
    for part_w in (params, key_w, value_w, query_w, out_w, sg_w, su_w, cot_w, ring, mixers):
        part_w.drain()
    for part_w in (rows_out, grads_out, outs, backs, shared_out, shared_back):
        part_w.drain()
    for copy in shared_grad.sent + swaps + across:
        copy.wait_send()
    for copy in saves:
        copy.wait()


def run_forward(
    tok, gain_one, gain_two, router, freq, deal, cot, routes, order, sd,
    wq, wk, wv, wo, sg, su, eg, eu, ed,
):
    rows, width = tok.shape
    pairs = width // PAIR
    ranks, slots = 8, 40
    hidden = eg.shape[1]
    part = sg.shape[1] // 4
    shard = width // 4
    total = ranks * slots
    tall = width + part * width // (128 * ranks)
    any_, vm = pl.BlockSpec(memory_space=pl.ANY), pl.BlockSpec(memory_space=VMEM)
    shape = jax.ShapeDtypeStruct

    def low(*dims):
        return VMEM(dims, BF)

    def full(*dims):
        return VMEM(dims, F32)

    dma = pltpu.SemaphoreType.DMA
    folded = low(ranks, slots * width // 128, 128)
    return pl.pallas_call(
        forward_kernel,
        out_shape=(
            shape((rows, PAIR), F32),
            shape((rows, PAIR), F32),
            shape((1, ranks * rows), jnp.int32),
            shape((2 * rows, 1), jnp.int32),
            shape((pairs, 2 * rows, PAIR), BF),
            shape((rows, width), F32),
            shape((pairs, 2 * rows, PAIR), F32),
            shape((rows, width), BF),
            shape((16, width), F32),
            shape((rows, width), BF),
            shape((rows, width), F32),
            shape((16, width), F32),
            shape((4, tall, 128), BF),
            shape((ranks, rows, 2 * width), BF),
            shape((4, width, width), BF),
            shape((3, shard, hidden), BF),
            shape((3, shard, hidden), BF),
            shape((2 * shard // 3, hidden), BF),
        ),
        in_specs=[vm] * 5 + [pl.BlockSpec(memory_space=pltpu.SMEM)] + [vm] * 4 + [any_] * 9,
        out_specs=tuple([vm] * 13 + [any_] * 5),
        scratch_shapes=[
            low(4, width, width),
            low(ranks, rows, 2 * width),
            low(16, width),
            low(4, 16, width),
            full(pairs, 2 * rows, PAIR),
            full(pairs, 2 * rows, PAIR),
            full(pairs, 2 * rows, PAIR),
            low(width, part),
            low(width, part),
            low(width, hidden),
            low(width, hidden),
            low(width, hidden),
            low(rows, width),
            low(4, rows, width),
            low(4, rows, width),
            low(4, rows, width),
            low(3, rows, width),
            low(4, rows, width),
            low(3, rows, width),
            *[folded] * 8,
            low(total, width),
            low(total, width),
            full(total, width),
            full(total, hidden),
            full(total, hidden),
            low(total, hidden),
            low(total, hidden),
            low(total, hidden),
            low(ranks, tall, 128),
            low(4, tall, 128),
            low(total, 2 * rows),
            low(2 * rows, total),
            low(3, 2, shard, hidden),
            dma((144,)),
            dma((2 * ranks,)),
            dma((32,)),
            dma((4, ranks)),
            dma((4, ranks)),
            dma((5, 8)),
        ],
        compiler_params=pltpu.CompilerParams(
            collective_id=1, has_side_effects=True, vmem_limit_bytes=VMEM_BYTES
        ),
    )(
        tok, gain_one, gain_two, router, freq, deal, cot, routes, order, sd,
        wq, wk, wv, wo, sg, su, eg, eu, ed,
    )


def backward_kernel(
    grad_second_ref, tok, pack_ref, pack_grad_ref, normed_ref, mixed_ref, q_ref, lse_ref,
    cosr, sinr, kb, qb, dsh_ref, kv_ref, wfull_ref, give_ref, other_ref,
    grad_input_out, pack_out, att1_out, att2_out, sh_out, other_out,
    wbuf, kv, kvb, kv_x, kv_zo, kv_zi, kv_sum, gst, delta_s, dq,
    ga, ga4, gq, gq4, gkv, gkv4, n_t, m_t, n_all, m_all, pk, pk4,
    a1, a1_x, a1_zo, a1_zi, a1_sum, a2, a2_x, a2_zo, a2_zi, a2_sum, r1, r2,
    sh, sh_zo, sh_zi, sh_sum, sh_chunk, r3,
    sem, sem_kv, sem_a1, sem_a2, sem_sh, ring_recv, ring_send,
):
    spot = Spot(4)
    sems = Sems(sem)
    rows, width = tok.shape
    pairs = width // PAIR
    shard = width // 4
    loads = [pltpu.make_async_copy(wfull_ref.at[i], wbuf.at[i], sems.new()) for i in (3, 0, 1, 2)]
    loads.insert(1, pltpu.make_async_copy(kv_ref, kv, sems.new()))
    loads.append(pltpu.make_async_copy(dsh_ref, sh, sems.new()))
    for copy in loads:
        copy.start()

    def block(ref, w):
        return ref.at[pl.ds(pl.multiple_of(shard * w, 64), shard)]

    greet((spot.core, spot.across, spot.corner, spot.column, spot.inner), (spot.mid, spot.outer))
    grad_second = grad_second_ref[...]
    ga[...] = grad_second.astype(BF)
    grads_w = Gather(spot, ga, lambda w: ga4.at[w], sems)
    loads[-1].wait()
    shared = Reduce(spot, sh, None, sh_zo, sh_zi, sem_sh, folded=True)
    for number in (3, 2, 1):
        shared.launch(number)
    mixed = mixed_ref[...]
    n_t[...] = normed_ref[...].T
    m_t[...] = mixed.astype(BF).T

    def columns(ref):
        return lambda w: ref.at[:, pl.ds(pl.multiple_of(rows * w, 128), rows)]

    normed_w = Spread(spot, lambda w: block(n_t, w), columns(n_all), sems)
    mixed_w = Spread(spot, lambda w: block(m_t, w), columns(m_all), sems)
    across = []

    def send_across(src, dst):
        across.append(remote(src, dst, sems.new(), sems.new(), spot.across))
        across[-1].start()

    done = other_ref.shape[0]
    loads.append(pltpu.make_async_copy(other_ref, other_out.at[0, pl.ds(0, done)], sems.new()))
    loads[-1].start()
    left = pl.ds(done, shard - done)
    send_across(give_ref.at[0, left], other_out.at[0, left])
    send_across(give_ref.at[1], other_out.at[1])
    loads[0].wait()
    grad_mixed = nt(ga[...], wbuf[3]).astype(BF)
    product = grad_mixed.astype(F32) * mixed
    for j in range(pairs):
        lanes = slice(PAIR * j, PAIR * (j + 1))
        gst[j] = stack_pair(grad_mixed[:, lanes])
        delta_s[j] = jnp.broadcast_to(
            jnp.sum(stack_pair(product[:, lanes]), axis=1, keepdims=True), (2 * rows, PAIR)
        )
    dq[...] = jnp.zeros_like(dq)
    loads[1].wait()
    q_block = qb[...]

    def chunk(number):
        plane = spot.plane(number)
        k_block = kb[:, pl.ds(pl.multiple_of(2 * rows * plane, 2 * rows), 2 * rows)]
        allowed = k_block <= q_block

        def one_pair(j, carry):
            lane = pl.multiple_of(PAIR * j, PAIR)
            both = pl.ds(2 * plane, 2)
            key = kv[both, :, pl.ds(lane, PAIR)].reshape(2 * rows, PAIR)
            value = kv[both, :, pl.ds(width + lane, PAIR)].reshape(2 * rows, PAIR)
            query, grad = q_ref[j], gst[j]
            scores = nt(query, key)
            probs = jnp.where(allowed, jnp.exp(scores - lse_ref[j][:, 0:1]), 0.0)
            inner = nt(grad, value) - delta_s[j][:, 0:1]
            grad_scores = (probs * inner * HD**-0.5).astype(BF)
            dq[j] += nn(grad_scores, key)
            grad_key = tn(grad_scores, query) * HD**0.5
            grad_value = tn(probs.astype(BF), grad)
            kvb[both, :, pl.ds(lane, PAIR)] = grad_key.astype(BF).reshape(2, rows, PAIR)
            kvb[both, :, pl.ds(width + lane, PAIR)] = grad_value.astype(BF).reshape(2, rows, PAIR)
            return carry

        lax.fori_loop(0, pairs, one_pair, 0)

    kv_grad = Reduce(spot, kvb, kv_x, kv_zo, kv_zi, sem_kv, parts=2)
    chunk(3)
    kv_grad.side(3)
    chunk(2)
    kv_grad.side(2)
    shared.relay(3)
    chunk(1)
    kv_grad.side(1)
    shared.relay(2)
    kv_grad.meet(3)
    chunk(0)
    kv_grad.side(0)
    cosine, sine = cosr[...], sinr[...]
    gq[...] = turn(
        jnp.concatenate([unstack_pair(dq[j]) for j in range(pairs)], axis=1), cosine, -sine
    ).astype(BF)
    query_w = Gather(spot, gq, lambda w: gq4.at[w], sems)
    shared.relay(1)
    kv_grad.meet(2)
    kv_grad.relay(3)
    grads_w.forward()
    for part_w in (grads_w, normed_w, mixed_w):
        part_w.finish()
    out_grad = nn(m_all[...], ga4[...].reshape(4 * rows, width))
    shared.last(sh_sum)
    sh_chunk[...] = sh_sum[...].astype(BF)
    part = 2 * shard // 2

    def piece(w):
        return sh_chunk.at[pl.ds(pl.multiple_of(part * w, 64), part)]

    def place(w):
        return r3.at[spot.k, pl.ds(pl.multiple_of(part * w, 64), part)]

    shared_w = Spread(spot, piece, place, sems)
    rest = sh_chunk.shape[0] - 4 * part
    r3[spot.k, pl.ds(4 * part, rest)] = sh_chunk[pl.ds(4 * part, rest)]
    kv_grad.meet(1)
    kv_grad.relay(2)
    kv_grad.relay(1)
    query_w.forward()
    query_w.finish()
    query_grad = nn(n_all[...], gq4[...].reshape(4 * rows, width))
    half = jnp.concatenate([out_grad, query_grad], axis=0).astype(BF)
    a1[...] = half.reshape(a1.shape)
    first = Reduce(spot, a1, a1_x, a1_zo, a1_zi, sem_a1)
    for number in (3, 2, 1, 0):
        first.side(number)
    kv_grad.meet(0)
    kv_grad.last(kv_sum)
    gkv[:, 0:width] = turn(kv_sum[:, 0:width], cosine, -sine).astype(BF)
    gkv[:, width : 2 * width] = kv_sum[:, width : 2 * width].astype(BF)
    kv_w = Gather(spot, gkv, lambda w: gkv4.at[w], sems)
    shared_w.finish()
    ring3 = Ring(spot, r3, ring_recv.at[2], ring_send.at[2], parts=2)
    ring3.start()
    for copy in loads[2:5]:
        copy.wait()
    grad_normed = nt(gq[...], wbuf[0]) + nt(gkv[:, 0:width], wbuf[1])
    grad_normed = grad_normed + nt(gkv[:, width : 2 * width], wbuf[2])
    inputs = tok[...].astype(F32)
    scale = lax.rsqrt(jnp.mean(inputs * inputs, axis=-1, keepdims=True) + EPS)
    weighted = grad_normed * pack_ref[0:1]
    mean = jnp.mean(weighted * inputs, axis=-1, keepdims=True)
    grad_input_out[...] = (
        grad_second + scale * weighted - inputs * (scale * scale * scale * mean)
    )
    gain_grad = jnp.sum(grad_normed * inputs * scale, axis=0, keepdims=True)
    pk[...] = jnp.concatenate([gain_grad, pack_grad_ref[1:16]], axis=0).astype(BF)
    pack_w = Gather(spot, pk, lambda w: pk4.at[w], sems)
    send_across(give_ref.at[2], other_out.at[2])
    for number in (3, 2, 1, 0):
        first.meet(number)
    first.relay(3)
    first.relay(2)
    kv_w.forward()
    pack_w.forward()
    kv_w.finish()
    pack_w.finish()
    grad_kv = gkv4[...].reshape(4 * rows, 2 * width)
    both = nn(n_all[...], grad_kv)
    both = jnp.concatenate([both[:, 0:width], both[:, width : 2 * width]], axis=0).astype(BF)
    size = both.shape[0] // 8
    extra = sum(pk4[w].astype(F32) for w in range(4)).astype(BF)
    for r in range(8):
        a2[r, 0:size] = both[size * r : size * (r + 1)]
        a2[r, size : size + 16] = extra
    second = Reduce(spot, a2, a2_x, a2_zo, a2_zi, sem_a2)
    for number in (3, 2, 1, 0):
        second.side(number)
    first.relay(1)
    ring3.step(1)
    first.last(a1_sum)
    r1[spot.k] = a1_sum[...].astype(BF)
    ring1 = Ring(spot, r1, ring_recv.at[0], ring_send.at[0])
    ring1.start()
    ring3.step(2)
    for number in (3, 2, 1, 0):
        second.meet(number)
    ring1.step(1)
    ring3.step(3)
    second.relay(3)
    second.relay(2)
    second.relay(1)
    ring1.step(2)
    second.last(a2_sum)
    r2[spot.k] = a2_sum[0:size].astype(BF)
    ring2 = Ring(spot, r2, ring_recv.at[1], ring_send.at[1])
    ring2.start()
    pack_out[...] = a2_sum[size : size + 16]
    ring1.step(3)
    for number in (1, 2, 3):
        ring2.step(number)
    saves = []
    for ring, src, dst in ((ring3, r3, sh_out), (ring1, r1, att1_out), (ring2, r2, att2_out)):
        for number in range(4):
            ring.other(number)
        saves.append(pltpu.make_async_copy(src, dst, sems.new()))
        saves[-1].start()
    for copy in across:
        copy.wait_recv()
        copy.wait_send()
    for part_w in (grads_w, normed_w, mixed_w, query_w, shared_w, kv_w, pack_w):
        part_w.drain()
    for part_w in (shared, kv_grad, first, second, ring1, ring2, ring3):
        part_w.drain()
    for copy in saves + loads[6:]:
        copy.wait()


def run_backward(
    grad_second, tok, pack, pack_grad, normed, mixed, q, lse, cosr, sinr, kb, qb, dsh, kv, wfull,
    give, other,
):
    rows, width = tok.shape
    pairs = width // PAIR
    ranks = 8
    shard, hidden = width // 4, give.shape[2]
    size = 2 * shard // ranks
    tall = dsh.shape[1]
    any_, vm = pl.BlockSpec(memory_space=pl.ANY), pl.BlockSpec(memory_space=VMEM)
    shape = jax.ShapeDtypeStruct

    def low(*dims):
        return VMEM(dims, BF)

    def full(*dims):
        return VMEM(dims, F32)

    dma = pltpu.SemaphoreType.DMA
    return pl.pallas_call(
        backward_kernel,
        out_shape=(
            shape((rows, width), F32),
            shape(pack.shape, F32),
            shape((ranks, size, width), BF),
            shape((ranks, size, width), BF),
            shape((ranks, tall, 128), BF),
            shape((3, shard, hidden), BF),
        ),
        in_specs=[vm] * 12 + [any_] * 5,
        out_specs=(vm, vm, any_, any_, any_, any_),
        scratch_shapes=[
            low(4, width, width),
            low(ranks, rows, 2 * width),
            low(ranks, rows, 2 * width),
            low(4, rows, 2 * width),
            low(4, rows, 2 * width),
            low(4, rows, 2 * width),
            full(rows, 2 * width),
            low(pairs, 2 * rows, PAIR),
            full(pairs, 2 * rows, PAIR),
            full(pairs, 2 * rows, PAIR),
            low(rows, width),
            low(4, rows, width),
            low(rows, width),
            low(4, rows, width),
            low(rows, 2 * width),
            low(4, rows, 2 * width),
            low(width, rows),
            low(width, rows),
            low(shard, 4 * rows),
            low(shard, 4 * rows),
            low(16, width),
            low(4, 16, width),
            low(ranks, size, width),
            low(4, size, width),
            low(4, size, width),
            low(4, size, width),
            full(size, width),
            low(ranks, size + 16, width),
            low(4, size + 16, width),
            low(4, size + 16, width),
            low(4, size + 16, width),
            full(size + 16, width),
            low(ranks, size, width),
            low(ranks, size, width),
            low(4, tall, 128),
            low(4, tall, 128),
            low(4, tall, 128),
            full(tall, 128),
            low(tall, 128),
            low(ranks, tall, 128),
            dma((112,)),
            dma((5, 8)),
            dma((5, 8)),
            dma((5, 8)),
            dma((5, 8)),
            dma((3, 2 * ranks)),
            dma((3, 32)),
        ],
        compiler_params=pltpu.CompilerParams(
            collective_id=3, has_side_effects=True, vmem_limit_bytes=VMEM_BYTES
        ),
    )(
        grad_second, tok, pack, pack_grad, normed, mixed, q, lse, cosr, sinr, kb, qb, dsh, kv,
        wfull, give, other,
    )


def unpack_kernel(
    result, grad_input, pack, att1, att2, sh, keep, other,
    result_out, grad_input_out, gain_one, gain_two, router,
    query, key, value, output, gate, up, down, eg, eu, ed,
):
    i = pl.program_id(0)
    result_out[...] = result[...]
    grad_input_out[...] = grad_input[...]
    output[...] = att1[0, 0].astype(F32)
    query[...] = att1[1, 0].astype(F32)
    key[...] = att2[0, 0].astype(F32)
    value[...] = att2[1, 0].astype(F32)
    for a, ref in enumerate((eg, eu, ed)):
        ref[...] = keep[a].astype(F32) + other[a].astype(F32)
    size = gate.shape[0]
    shard = 4 * size
    width = 4 * shard
    row, within = lax.div(i, 2), lax.rem(i, 2) * size
    for c in range(4):
        for w in range(4):
            lanes = slice(512 * w + 128 * c, 512 * w + 128 * (c + 1))
            start = pl.multiple_of(shard * w + within, 16)
            gate[:, lanes] = sh[4 * row + c, pl.ds(start, size)].astype(F32)
            start = pl.multiple_of(shard * w + shard // 2 + within, 16)
            up[:, lanes] = sh[4 * row + c, pl.ds(start, size)].astype(F32)
    deep = down.shape[0] // 2
    for r in range(2):
        for t in range(width // 128):
            at = slice(width + deep * t, width + deep * (t + 1))
            down[deep * r : deep * (r + 1), 128 * t : 128 * (t + 1)] = sh[2 * i + r, at].astype(F32)

    @pl.when(i == 0)
    def _():
        back = lax.rem(4 - lax.axis_index("wt"), 4) * shard
        mine = pltpu.roll(pack[...], back, 1)[:, 0:256]
        gain_one[...] = mine[0:1, 0:shard]
        gain_two[...] = mine[1:2, 0:shard]
        router[...] = mine.T[0:shard, 2 : 2 + router.shape[1]]


def run_unpack(result, grad_input, pack, att1, att2, sh, keep, other, experts):
    rows, width = result.shape
    shard, hidden = keep.shape[1:]
    steps = 4
    shape = jax.ShapeDtypeStruct
    size = shard // steps
    att1 = att1.reshape(2, 4, size, width)
    att2 = att2.reshape(2, 4, size, width)
    shared_hidden = sh.shape[0] * (sh.shape[1] - width) * 128 // width
    shared = 4 * shared_hidden
    by_rows = lambda r, c: pl.BlockSpec((r, c), lambda i: (i, 0))
    whole = lambda *dims: pl.BlockSpec(dims, lambda i: (0,) * len(dims))
    stack = lambda n, r, c: pl.BlockSpec((n, r, c), lambda i: (0, i, 0))
    att = pl.BlockSpec((2, 1, size, width), lambda i: (0, i, 0, 0))
    return pl.pallas_call(
        unpack_kernel,
        grid=(steps,),
        out_shape=(
            shape((rows, width), BF),
            shape((rows, width), F32),
            shape((1, shard), F32),
            shape((1, shard), F32),
            shape((shard, experts), F32),
            *[shape((shard, width), F32)] * 4,
            *[shape((shard, shared), F32)] * 2,
            shape((shared_hidden, width), F32),
            *[shape((shard, hidden), F32)] * 3,
        ),
        in_specs=[
            by_rows(rows // steps, width),
            by_rows(rows // steps, width),
            whole(*pack.shape),
            att,
            att,
            whole(*sh.shape),
            stack(3, size, hidden),
            stack(3, size, hidden),
        ],
        out_specs=(
            by_rows(rows // steps, width),
            by_rows(rows // steps, width),
            whole(1, shard),
            whole(1, shard),
            whole(shard, experts),
            *[by_rows(size, width)] * 4,
            *[by_rows(size, shared)] * 2,
            by_rows(shared_hidden // steps, width),
            *[by_rows(size, hidden)] * 3,
        ),
        compiler_params=pltpu.CompilerParams(vmem_limit_bytes=VMEM_BYTES),
    )(result, grad_input, pack, att1, att2, sh, keep, other)


def contract_product(left, right, left_dim, right_dim):
    return lax.dot_general(
        left, right, (((left_dim,), (right_dim,)), ((), ())), preferred_element_type=jnp.float32
    )


def contract_exact(left, right, left_dim, right_dim):
    return lax.dot_general(
        left,
        right,
        (((left_dim,), (right_dim,)), ((), ())),
        precision=HIGH,
        preferred_element_type=jnp.float32,
    )


def rms_norm(values, gain):
    norm_scale = lax.rsqrt(jnp.mean(values * values, axis=-1, keepdims=True) + EPS)
    return (values * norm_scale * gain, norm_scale)


def rms_back(values, norm_scale, gain, upstream):
    weighted = upstream * gain
    inner_mean = jnp.mean(weighted * values, axis=-1, keepdims=True)
    through = norm_scale * weighted - values * norm_scale * norm_scale * norm_scale * inner_mean
    return (through, jnp.sum(upstream * values * norm_scale, axis=0))


def silu_parts(gate_part):
    sigmoid = jax.nn.sigmoid(gate_part)
    return (gate_part * sigmoid, sigmoid * (1.0 + gate_part * (1.0 - sigmoid)))


def rotate(values, place, sign):
    half_size = HD // 2
    frequency = 10000.0 ** (-jnp.arange(half_size, dtype=jnp.float32) / half_size)
    angles = place.astype(jnp.float32)[:, None] * frequency[None, :]
    cosine = jnp.cos(angles)[:, None, :]
    sine_part = sign * jnp.sin(angles)[:, None, :]
    shaped = values.reshape(values.shape[0], values.shape[1] // HD, 2, half_size)
    first_half = shaped[:, :, 0, :]
    second_half = shaped[:, :, 1, :]
    turned = jnp.stack(
        [
            first_half * cosine - second_half * sine_part,
            second_half * cosine + first_half * sine_part,
        ],
        axis=2,
    )
    return turned.reshape(values.shape)


def places(first_row, row_count, block_deal, rows_dev):
    row_index = first_row + jnp.arange(row_count, dtype=jnp.int32)
    owner_rank = row_index // rows_dev
    inner_row = row_index % rows_dev
    ranks = block_deal.shape[0]
    matches = owner_rank[:, None] == jnp.arange(ranks, dtype=jnp.int32)[None, :]
    paired = jnp.sum(jnp.where(matches, block_deal[None, :], 0), axis=1)
    piece_size = rows_dev // 2
    unit_index = jnp.where(inner_row < piece_size, paired, 2 * ranks - 1 - paired)
    return unit_index * piece_size + inner_row % piece_size


def score_block(query_side, key_rows, key_place):
    query3, query_block = query_side
    key3 = key_rows.reshape(key_rows.shape[0], -1, HD)
    raw_scores = jnp.einsum("qhd,khd->hqk", query3, key3, preferred_element_type=jnp.float32)
    allowed = (key_place // BLK)[None, None, :] <= query_block[None, :, None]
    return (jnp.where(allowed, raw_scores * HD ** (-0.5), MASKED), allowed)


def absorb(running, key_rows, value_rows, key_place, query_side):
    largest, denom, accum = running
    scores, allowed = score_block(query_side, key_rows, key_place)
    new_largest = jnp.maximum(largest, jnp.max(scores, axis=2))
    factor = jnp.exp(largest - new_largest)
    raised = jnp.where(allowed, jnp.exp(scores - new_largest[:, :, None]), 0.0)
    denom = denom * factor + jnp.sum(raised, axis=2)
    value3 = value_rows.reshape(value_rows.shape[0], -1, HD)
    accum = accum * factor.T[:, :, None] + jnp.einsum(
        "hqk,khd->qhd", raised.astype(jnp.bfloat16), value3, preferred_element_type=jnp.float32
    )
    return (new_largest, denom, accum)


def fold_keys(running, key_piece, query_side, block_deal, rows_dev):
    key_all, value_all = key_piece
    row_count = key_all.shape[0]
    block_size = KEY_ROWS

    def key_step(current, offset):
        key_rows = lax.dynamic_slice_in_dim(key_all, offset, block_size, 0)
        value_rows = lax.dynamic_slice_in_dim(value_all, offset, block_size, 0)
        key_place = places(offset, block_size, block_deal, rows_dev)
        return (absorb(current, key_rows, value_rows, key_place, query_side), None)

    offsets = jnp.arange(row_count // block_size, dtype=jnp.int32) * block_size
    running, unused = lax.scan(key_step, running, offsets)
    return running


def differentiate(query_side, log_total, delta, grad_out3, key_rows, value_rows, key_place):
    scores, allowed = score_block(query_side, key_rows, key_place)
    probs_full = jnp.where(allowed, jnp.exp(scores - log_total[:, :, None]), 0.0)
    value3 = value_rows.reshape(value_rows.shape[0], -1, HD)
    grad_probs = jnp.einsum("qhd,khd->hqk", grad_out3, value3, preferred_element_type=jnp.float32)
    grad_scores = (probs_full * (grad_probs - delta[:, :, None]) * HD ** (-0.5)).astype(
        jnp.bfloat16
    )
    return (probs_full, grad_scores)


def assign_slots(route, order, experts, capacity):
    pair_count = order.shape[0]
    expert_ids = route.reshape(pair_count)
    ordered = expert_ids[order]
    onehot = (ordered[:, None] == jnp.arange(experts, dtype=jnp.int32)[None, :]).astype(jnp.int32)
    before = jnp.cumsum(onehot, axis=0) - onehot
    slot_turn = jnp.sum(before * onehot, axis=1)
    slot_index = jnp.zeros((pair_count,), jnp.int32).at[order].set(slot_turn)
    kept_pairs = slot_index < capacity
    target = jnp.where(kept_pairs, expert_ids * capacity + slot_index, experts * capacity)
    slot_table = (
        jnp.full((experts * capacity,), pair_count, jnp.int32)
        .at[target]
        .set(jnp.arange(pair_count, dtype=jnp.int32), mode="drop")
    )
    return (target, kept_pairs, slot_table)


def body(
    tokens,
    cotangent,
    gain_attention,
    query_weight,
    key_weight,
    value_weight,
    output_weight,
    gain_mixer,
    router_weight,
    shared_gate,
    shared_up,
    shared_down,
    expert_gate,
    expert_up,
    expert_down,
    routes,
    slot_order,
    block_deal,
):
    rows_dev = tokens.shape[1]
    width = tokens.shape[2]
    ranks = lax.axis_size("ctx")
    (
        gain_one,
        query_full,
        key_full,
        value_full,
        output_full,
        gain_two,
        router_full,
        sgate_full,
        sup_full,
        sdown_full,
        expert_gate_whole,
        expert_up_whole,
        edown_full,
    ) = (
        lax.all_gather(gain_attention, "wt", axis=0, tiled=True),
        lax.all_gather(query_weight, "wt", axis=0, tiled=True),
        lax.all_gather(key_weight, "wt", axis=0, tiled=True),
        lax.all_gather(value_weight, "wt", axis=0, tiled=True),
        lax.all_gather(output_weight, "wt", axis=0, tiled=True),
        lax.all_gather(gain_mixer, "wt", axis=0, tiled=True),
        lax.all_gather(router_weight, "wt", axis=0, tiled=True),
        lax.all_gather(shared_gate, "wt", axis=0, tiled=True),
        lax.all_gather(shared_up, "wt", axis=0, tiled=True),
        lax.all_gather(shared_down, "wt", axis=0, tiled=True),
        lax.all_gather(expert_gate, "wt", axis=0, tiled=True),
        lax.all_gather(expert_up, "wt", axis=0, tiled=True),
        lax.all_gather(expert_down, "wt", axis=0, tiled=True),
    )
    gain_first = gain_one.astype(jnp.float32)
    gain_second = gain_two.astype(jnp.float32)
    heads = width // HD
    inputs = tokens[0].astype(jnp.float32)
    here = places(lax.axis_index("ctx") * rows_dev, rows_dev, block_deal, rows_dev)
    query_side_block = here // BLK
    normed_f, scale_one = rms_norm(inputs, gain_first)
    normed = normed_f.astype(jnp.bfloat16)
    query_rot = rotate(
        jnp.dot(normed, query_full, preferred_element_type=jnp.float32), here, 1.0
    ).astype(jnp.bfloat16)
    key_rot = rotate(
        jnp.dot(normed, key_full, preferred_element_type=jnp.float32), here, 1.0
    ).astype(jnp.bfloat16)
    value_low = jnp.dot(normed, value_full, preferred_element_type=jnp.float32).astype(jnp.bfloat16)
    query3 = query_rot.reshape(rows_dev, heads, HD)
    query_side = (query3, query_side_block)
    start_state = (
        jnp.full((heads, rows_dev), MASKED, jnp.float32),
        jnp.zeros((heads, rows_dev), jnp.float32),
        jnp.zeros((rows_dev, heads, HD), jnp.float32),
    )
    largest, denom, accum = fold_keys(
        start_state,
        (
            lax.all_gather(key_rot, "ctx", axis=0, tiled=True),
            lax.all_gather(value_low, "ctx", axis=0, tiled=True),
        ),
        query_side,
        block_deal,
        rows_dev,
    )
    mixed3 = accum / denom.T[:, :, None]
    log_total = largest + jnp.log(denom)
    mixed_low = mixed3.reshape(rows_dev, width).astype(jnp.bfloat16)
    second = inputs + jnp.dot(mixed_low, output_full, preferred_element_type=jnp.float32)
    mixer_f, scale_two = rms_norm(second, gain_second)
    mixer = mixer_f.astype(jnp.bfloat16)
    experts = router_full.shape[1]
    logits = jnp.dot(mixer, router_full, preferred_element_type=jnp.float32)
    route = routes[0]
    top_count = route.shape[1]
    pair_count = rows_dev * top_count
    capacity = (5 * pair_count + 4 * experts - 1) // (4 * experts)
    split_count = ranks // experts
    expert_match = route[:, :, None] == jnp.arange(experts, dtype=jnp.int32)[None, None, :]
    chosen = jnp.sum(jnp.where(expert_match, logits[:, None, :], 0.0), axis=2)
    gates = jax.nn.softmax(chosen, axis=1)
    target, kept_pairs, slot_table = assign_slots(route, slot_order[0, 0], experts, capacity)
    valid = slot_table < pair_count
    pair_pick = jnp.minimum(slot_table, pair_count - 1)
    target_pick = jnp.minimum(target, experts * capacity - 1)
    send_rows = jnp.where(
        valid[:, None], mixer[pair_pick // top_count], jnp.zeros((), jnp.bfloat16)
    )
    send_rows = jnp.broadcast_to(
        send_rows.reshape(experts, 1, capacity, width), (experts, split_count, capacity, width)
    ).reshape(ranks, capacity, width)
    received = lax.all_to_all(send_rows, "ctx", split_axis=0, concat_axis=0, tiled=True)
    slot_count = received.shape[1]
    flattened_input = received.reshape(ranks * slot_count, width)
    gate_part = jnp.dot(flattened_input, expert_gate_whole, preferred_element_type=jnp.float32)
    up_projection_part = jnp.dot(
        flattened_input, expert_up_whole, preferred_element_type=jnp.float32
    )
    activated, unused = silu_parts(gate_part)
    hidden = (activated * up_projection_part).astype(jnp.bfloat16)
    partial_value = contract_product(hidden, edown_full, 1, 1).reshape(ranks, slot_count, width)
    back = lax.all_to_all(
        partial_value.astype(jnp.bfloat16), "ctx", split_axis=0, concat_axis=0, tiled=True
    ).astype(partial_value.dtype)
    expert_gate_part = gate_part.reshape(ranks, slot_count, -1)
    expert_up_part = up_projection_part.reshape(ranks, slot_count, -1)
    combined = jnp.sum(back.reshape(experts, split_count, capacity, width), axis=1).reshape(
        experts * capacity, width
    )
    pair_out = jnp.where(kept_pairs[:, None], combined[target_pick], 0.0).reshape(
        rows_dev, top_count, width
    )
    mixture = jnp.sum(gates[:, :, None] * pair_out, axis=1)
    sgate_part = jnp.dot(mixer, sgate_full, preferred_element_type=jnp.float32)
    sup_part = jnp.dot(mixer, sup_full, preferred_element_type=jnp.float32)
    shared_act, shared_slope = silu_parts(sgate_part)
    shared_hidden = (shared_act * sup_part).astype(jnp.bfloat16)
    shared_out = jnp.dot(shared_hidden, sdown_full, preferred_element_type=jnp.float32)
    result = (second + mixture + shared_out).astype(jnp.bfloat16)
    grad_final = cotangent[0].astype(jnp.float32)
    grad_low = grad_final.astype(jnp.bfloat16)
    sdown_grad = contract_product(shared_hidden, grad_low, 0, 0)
    grad_shared_hidden = contract_product(grad_low, sdown_full, 1, 1)
    grad_sgate = (grad_shared_hidden * sup_part * shared_slope).astype(jnp.bfloat16)
    grad_sup = (grad_shared_hidden * shared_act).astype(jnp.bfloat16)
    sgate_grad = contract_product(mixer, grad_sgate, 0, 0)
    sup_grad = contract_product(mixer, grad_sup, 0, 0)
    grad_mixer = contract_product(grad_sgate, sgate_full, 1, 1) + contract_product(
        grad_sup, sup_full, 1, 1
    )
    pair_grad = (
        (gates[:, :, None] * grad_final[:, None, :]).reshape(pair_count, width).astype(jnp.bfloat16)
    )
    grad_gates = jnp.sum(grad_final[:, None, :] * pair_out, axis=2)
    send_grad = jnp.where(valid[:, None], pair_grad[pair_pick], jnp.zeros((), jnp.bfloat16))
    send_grad = jnp.broadcast_to(
        send_grad.reshape(experts, 1, capacity, width), (experts, split_count, capacity, width)
    ).reshape(ranks, capacity, width)
    recv_grad = lax.all_to_all(send_grad, "ctx", split_axis=0, concat_axis=0, tiled=True)
    flattened_input = received.reshape(ranks * capacity, width)
    flat_grad = recv_grad.reshape(ranks * capacity, width)
    gate_flat = expert_gate_part.reshape(ranks * capacity, -1)
    up_flat = expert_up_part.reshape(ranks * capacity, -1)
    expert_activation, expert_slope = silu_parts(gate_flat)
    expert_hidden = (expert_activation * up_flat).astype(jnp.bfloat16)
    edown_grad = contract_product(flat_grad, expert_hidden, 0, 0)
    expert_hidden_grad = jnp.dot(flat_grad, edown_full, preferred_element_type=jnp.float32)
    expert_gate_grad_rows = (expert_hidden_grad * up_flat * expert_slope).astype(jnp.bfloat16)
    expert_up_grad_rows = (expert_hidden_grad * expert_activation).astype(jnp.bfloat16)
    egate_grad = contract_product(flattened_input, expert_gate_grad_rows, 0, 0)
    expert_up_weight_grad = contract_product(flattened_input, expert_up_grad_rows, 0, 0)
    input_back = (
        contract_product(expert_gate_grad_rows, expert_gate_whole, 1, 1)
        + contract_product(expert_up_grad_rows, expert_up_whole, 1, 1)
    ).reshape(ranks, capacity, width)
    back_grad = lax.all_to_all(
        input_back.astype(jnp.bfloat16), "ctx", split_axis=0, concat_axis=0, tiled=True
    ).astype(input_back.dtype)
    merged = jnp.sum(back_grad.reshape(experts, split_count, capacity, width), axis=1).reshape(
        experts * capacity, width
    )
    pair_back = jnp.where(kept_pairs[:, None], merged[target_pick], 0.0).reshape(
        rows_dev, top_count, width
    )
    grad_mixer = grad_mixer + jnp.sum(pair_back, axis=1)
    grad_chosen = gates * (grad_gates - jnp.sum(gates * grad_gates, axis=1, keepdims=True))
    grad_logits = jnp.sum(jnp.where(expert_match, grad_chosen[:, :, None], 0.0), axis=1)
    router_grad = contract_exact(mixer.astype(jnp.float32), grad_logits, 0, 0)
    grad_mixer = grad_mixer + contract_exact(grad_logits, router_full.astype(jnp.float32), 1, 1)
    through_two, gain_two_grad = rms_back(second, scale_two, gain_second, grad_mixer)
    grad_second = grad_final + through_two
    grad_attention = grad_second.astype(jnp.bfloat16)
    output_grad = contract_product(mixed_low, grad_attention, 0, 0)
    grad_mixed = contract_product(grad_attention, output_full, 1, 1).astype(jnp.bfloat16)
    grad_out3 = grad_mixed.reshape(rows_dev, heads, HD)
    delta = jnp.sum(grad_out3.astype(jnp.float32) * mixed3, axis=2).T
    all_keys, all_values = (
        lax.all_gather(key_rot, "ctx", axis=0, tiled=True),
        lax.all_gather(value_low, "ctx", axis=0, tiled=True),
    )
    total_rows = all_keys.shape[0]
    block_size = KEY_ROWS

    def query_step(grad_sum, offset):
        key_rows = lax.dynamic_slice_in_dim(all_keys, offset, block_size, 0)
        value_rows = lax.dynamic_slice_in_dim(all_values, offset, block_size, 0)
        key_place = places(offset, block_size, block_deal, rows_dev)
        unused, grad_scores = differentiate(
            query_side, log_total, delta, grad_out3, key_rows, value_rows, key_place
        )
        key3 = key_rows.reshape(block_size, heads, HD)
        return (
            grad_sum
            + jnp.einsum("hqk,khd->qhd", grad_scores, key3, preferred_element_type=jnp.float32),
            None,
        )

    offsets = jnp.arange(total_rows // block_size, dtype=jnp.int32) * block_size
    grad_query3, unused = lax.scan(
        query_step, jnp.zeros((rows_dev, heads, HD), jnp.float32), offsets
    )
    inner_size = KEY_ROWS

    def one_part(offset):
        key_rows = lax.dynamic_slice_in_dim(all_keys, offset, inner_size, 0)
        value_rows = lax.dynamic_slice_in_dim(all_values, offset, inner_size, 0)
        key_place = places(offset, inner_size, block_deal, rows_dev)
        probs_full, grad_scores = differentiate(
            query_side, log_total, delta, grad_out3, key_rows, value_rows, key_place
        )
        grad_value_rows = jnp.einsum(
            "hqk,qhd->khd",
            probs_full.astype(jnp.bfloat16),
            grad_out3,
            preferred_element_type=jnp.float32,
        )
        grad_key_rows = jnp.einsum(
            "hqk,qhd->khd", grad_scores, query3, preferred_element_type=jnp.float32
        )
        return jnp.concatenate(
            [grad_key_rows.reshape(inner_size, width), grad_value_rows.reshape(inner_size, width)],
            axis=1,
        )

    parts = lax.map(
        one_part,
        jnp.arange(lax.axis_size("ctx") * rows_dev // inner_size, dtype=jnp.int32) * inner_size,
    )
    key_value_grad = lax.psum_scatter(
        parts.reshape(lax.axis_size("ctx") * rows_dev, 2 * width),
        "ctx",
        scatter_dimension=0,
        tiled=True,
    )
    grad_key_pre = rotate(key_value_grad[:, :width], here, -1.0).astype(jnp.bfloat16)
    grad_value_low = key_value_grad[:, width:].astype(jnp.bfloat16)
    grad_query_pre = rotate(grad_query3.reshape(rows_dev, width), here, -1.0).astype(jnp.bfloat16)
    query_grad = contract_product(normed, grad_query_pre, 0, 0)
    key_grad = contract_product(normed, grad_key_pre, 0, 0)
    value_grad = contract_product(normed, grad_value_low, 0, 0)
    grad_normed = (
        contract_product(grad_query_pre, query_full, 1, 1)
        + contract_product(grad_key_pre, key_full, 1, 1)
        + contract_product(grad_value_low, value_full, 1, 1)
    )
    through_one, gain_one_grad = rms_back(inputs, scale_one, gain_first, grad_normed)
    grad_input = grad_second + through_one
    (
        gain_one_share,
        query_share,
        key_share,
        value_share,
        output_share,
        gain_two_share,
        router_share,
        sgate_share,
        sup_share,
        sdown_share,
        egate_share,
        expert_up_portion,
        edown_share,
    ) = (
        lax.psum_scatter(
            gain_one_grad.astype(jnp.bfloat16), "wt", scatter_dimension=0, tiled=True
        ).astype(jnp.float32),
        lax.psum_scatter(
            query_grad.astype(jnp.bfloat16), "wt", scatter_dimension=0, tiled=True
        ).astype(jnp.float32),
        lax.psum_scatter(
            key_grad.astype(jnp.bfloat16), "wt", scatter_dimension=0, tiled=True
        ).astype(jnp.float32),
        lax.psum_scatter(
            value_grad.astype(jnp.bfloat16), "wt", scatter_dimension=0, tiled=True
        ).astype(jnp.float32),
        lax.psum_scatter(
            output_grad.astype(jnp.bfloat16), "wt", scatter_dimension=0, tiled=True
        ).astype(jnp.float32),
        lax.psum_scatter(
            gain_two_grad.astype(jnp.bfloat16), "wt", scatter_dimension=0, tiled=True
        ).astype(jnp.float32),
        lax.psum_scatter(
            router_grad.astype(jnp.bfloat16), "wt", scatter_dimension=0, tiled=True
        ).astype(jnp.float32),
        lax.psum_scatter(
            sgate_grad.astype(jnp.bfloat16), "wt", scatter_dimension=0, tiled=True
        ).astype(jnp.float32),
        lax.psum_scatter(
            sup_grad.astype(jnp.bfloat16), "wt", scatter_dimension=0, tiled=True
        ).astype(jnp.float32),
        lax.psum_scatter(
            sdown_grad.astype(jnp.bfloat16), "wt", scatter_dimension=0, tiled=True
        ).astype(jnp.float32),
        lax.psum_scatter(
            egate_grad.astype(jnp.bfloat16), "wt", scatter_dimension=0, tiled=True
        ).astype(jnp.float32),
        lax.psum_scatter(
            expert_up_weight_grad.astype(jnp.bfloat16), "wt", scatter_dimension=0, tiled=True
        ).astype(jnp.float32),
        lax.psum_scatter(
            edown_grad.astype(jnp.bfloat16), "wt", scatter_dimension=0, tiled=True
        ).astype(jnp.float32),
    )
    (
        gain_one_sum,
        query_sum,
        key_sum,
        value_sum,
        output_sum,
        gain_two_sum,
        router_sum,
        sgate_sum,
        sup_sum,
        sdown_sum,
    ) = lax.psum(
        (
            gain_one_share,
            query_share,
            key_share,
            value_share,
            output_share,
            gain_two_share,
            router_share,
            sgate_share,
            sup_share,
            sdown_share,
        ),
        "ctx",
    )
    return (
        result[None],
        grad_input[None],
        gain_one_sum,
        query_sum,
        key_sum,
        value_sum,
        output_sum,
        gain_two_sum,
        router_sum,
        sgate_sum,
        sup_sum,
        sdown_sum,
        egate_share,
        expert_up_portion,
        edown_share,
    )


def fast_body(
    tokens,
    cotangent,
    gain_attention,
    query_weight,
    key_weight,
    value_weight,
    output_weight,
    gain_mixer,
    router_weight,
    shared_gate,
    shared_up,
    shared_down,
    expert_gate,
    expert_up,
    expert_down,
    routes,
    slot_order,
    block_deal,
):
    half_size = HD // 2
    frequency = 10000.0 ** (-jnp.arange(half_size, dtype=F32) / half_size)
    (
        cosr, sinr, kb, qb, q_st, mixed, lse, normed, pack_all, result, grad_second, pack_grad, dsh,
        kv_all, wfull, keep, give, other,
    ) = run_forward(
        tokens[0], gain_attention[None], gain_mixer[None], router_weight,
        jnp.concatenate([frequency] * 4)[None], block_deal, cotangent[0], routes[0], slot_order[0],
        shared_down, query_weight, key_weight, value_weight, output_weight, shared_gate, shared_up,
        expert_gate, expert_up, expert_down,
    )
    grad_input, pack_sum, att1, att2, sh, other = run_backward(
        grad_second, tokens[0], pack_all, pack_grad, normed, mixed, q_st, lse, cosr, sinr, kb, qb,
        dsh, kv_all, wfull, give, other,
    )
    (
        result, grad_input, gain_one, gain_two, router, query, key, value, output, gate, up, down,
        eg, eu, ed,
    ) = run_unpack(
        result, grad_input, pack_sum, att1, att2, sh, keep, other, router_weight.shape[1]
    )
    return (
        result[None], grad_input[None], gain_one.reshape(-1), query, key, value, output,
        gain_two.reshape(-1), router, gate, up, down, eg, eu, ed,
    )


def solution(mesh):
    in_specs = (
        P("wt", "ctx", None),
        P("wt", "ctx", None),
        P("wt"),
        P("wt", None),
        P("wt", None),
        P("wt", None),
        P("wt", None),
        P("wt"),
        P("wt", None),
        P("wt", None),
        P("wt", None),
        P("wt", None),
        P("wt", "ctx"),
        P("wt", "ctx"),
        P("wt", "ctx"),
        P("wt", "ctx", None),
        P("wt", "ctx", None),
        P(),
    )
    out_specs = (
        P("wt", "ctx", None),
        P("wt", "ctx", None),
        P("wt"),
        P("wt", None),
        P("wt", None),
        P("wt", None),
        P("wt", None),
        P("wt"),
        P("wt", None),
        P("wt", None),
        P("wt", None),
        P("wt", None),
        P("wt", "ctx"),
        P("wt", "ctx"),
        P("wt", "ctx"),
    )
    chosen = fast_body if (mesh.shape["ctx"], mesh.shape["wt"]) == (8, 4) else body
    return jax.shard_map(chosen, mesh=mesh, in_specs=in_specs, out_specs=out_specs, check_vma=False)
```

```python
import jax
import jax.numpy as jnp
import numpy as np
from jax import lax
from jax.experimental import pallas as pl
from jax.experimental.pallas import tpu as pltpu
from jax.sharding import PartitionSpec as P

HD = 64
BLK = 256


EPS = 1e-06
KEY_ROWS = 512
HIGH = lax.Precision.HIGHEST
MASKED = -1e30


MESH = pl.DeviceIdType.MESH
VMEM = pltpu.VMEM
BF = jnp.bfloat16
F32 = jnp.float32
PAIR = 2 * HD
VMEM_BYTES = 63 * 2**20


class Spot:
    def __init__(self, line_size):
        self.k = lax.axis_index("ctx")
        self.w = lax.axis_index("wt")
        self.z, self.x = lax.div(self.k, 2), lax.rem(self.k, 2)
        self.y, self.c = lax.div(self.w, 2), lax.rem(self.w, 2)
        self.far = lax.div(self.z, 2)
        self.mid = self.z + self.far * (3 - 2 * self.z)
        step = 1 - 2 * self.far
        self.core = (self.k, 2 * self.y + 1 - self.c)
        self.across = (self.k, 2 * (1 - self.y) + self.c)
        self.corner = (self.k, 2 * (1 - self.y) + 1 - self.c)
        self.column = (2 * self.z + 1 - self.x, self.w)
        self.odd = lax.rem(self.z, 2)
        self.line = (2 * (self.z + 1 - 2 * self.odd) + self.x, self.w)
        self.inner = (2 * (self.z + step) + self.x, self.w)
        self.outer = (2 * (self.z - step) + self.x, self.w)

    def plane(self, step):
        mirrored = (self.mid, 1 - self.mid, 2, 3)[step]
        return mirrored + self.far * (3 - 2 * mirrored)


class Sems:
    def __init__(self, ref):
        self.ref, self.used = ref, 0

    def new(self):
        self.used += 1
        return self.ref.at[self.used - 1]


def remote(src, dst, send, recv, to):
    return pltpu.make_async_remote_copy(
        src_ref=src, dst_ref=dst, send_sem=send, recv_sem=recv, device_id=to, device_id_type=MESH
    )


def greet(devices, middle=None):
    barrier = pltpu.get_barrier_semaphore()
    for to in devices:
        pl.semaphore_signal(barrier, inc=1, device_id=to, device_id_type=MESH)
    if middle is None:
        pl.semaphore_wait(barrier, len(devices))
        return

    @pl.when(middle[0] == 1)
    def _():
        pl.semaphore_signal(barrier, inc=1, device_id=middle[1], device_id_type=MESH)

    pl.semaphore_wait(barrier, len(devices) + middle[0])


class Gather:
    def __init__(self, spot, src, place, sems, local=True):
        self.spot, self.place, self.sems = spot, place, sems
        here = place(spot.w)
        self.local = pltpu.make_async_copy(src, here, sems.new()) if local else None
        self.to_core = remote(src, here, sems.new(), sems.new(), spot.core)
        self.to_across = remote(src, here, sems.new(), sems.new(), spot.across)
        self.to_across.start()
        self.to_core.start()
        if local:
            self.local.start()

    def forward(self):
        self.to_across.wait_recv()
        part = self.place(self.spot.across[1])
        self.onward = remote(part, part, self.sems.new(), self.sems.new(), self.spot.core)
        self.onward.start()

    def finish(self):
        if self.local is not None:
            self.local.wait()
        self.to_core.wait_recv()
        self.onward.wait_recv()

    def drain(self):
        for copy in (self.to_core, self.to_across, self.onward):
            copy.wait_send()


class Share:
    def __init__(self, spot, src, dst, sems, mate, bit):
        self.spot, self.dst, self.sems, self.mate, self.bit = spot, dst, sems, mate, bit
        self.rows = src.shape[0]
        self.half = self.rows // 2
        here = dst.at[pl.ds(pl.multiple_of(self.rows * spot.w, 64), self.rows)]
        half = pl.ds(pl.multiple_of(self.half * bit, 32), self.half)
        self.local = pltpu.make_async_copy(src, here, sems.new())
        self.to_core = remote(src, here, sems.new(), sems.new(), spot.core)
        self.to_across = remote(
            src.at[half], self.part(spot.w, bit), sems.new(), sems.new(), spot.across
        )
        for copy in (self.to_across, self.to_core, self.local):
            copy.start()

    def part(self, w, bit):
        return self.dst.at[pl.ds(pl.multiple_of(self.rows * w + self.half * bit, 32), self.half)]

    def forward(self):
        spot = self.spot
        self.to_across.wait_recv()
        part = self.part(spot.across[1], self.bit)
        self.aside = remote(part, part, self.sems.new(), self.sems.new(), self.mate)
        self.onward = remote(part, part, self.sems.new(), self.sems.new(), spot.core)
        self.aside.start()
        self.onward.start()

    def second(self):
        self.aside.wait_recv()
        part = self.part(self.spot.across[1], 1 - self.bit)
        self.rest = remote(part, part, self.sems.new(), self.sems.new(), self.spot.core)
        self.rest.start()

    def finish(self):
        self.local.wait()
        self.to_core.wait_recv()
        self.onward.wait_recv()
        self.rest.wait_recv()

    def drain(self):
        for copy in (self.to_core, self.to_across, self.aside, self.onward, self.rest):
            copy.wait_send()


class ShareColumns:
    def __init__(self, spot, src, dst, sems, mate, bit):
        self.spot, self.dst, self.sems, self.mate, self.bit = spot, dst, sems, mate, bit
        self.rows, self.part_cols = src.shape[0], dst.shape[1]
        self.half = self.rows // 2
        half = pl.ds(pl.multiple_of(self.half * bit, 32), self.half)

        def columns(to):
            return pl.ds(pl.multiple_of(self.part_cols * to, self.part_cols), self.part_cols)

        here = dst.at[pl.ds(pl.multiple_of(self.rows * spot.w, 64), self.rows)]
        self.halves = [
            remote(
                src.at[half, columns(to[1])],
                self.part(spot.w, bit),
                sems.new(),
                sems.new(),
                to,
            )
            for to in (spot.across, spot.corner)
        ]
        self.to_core = remote(
            src.at[:, columns(spot.core[1])], here, sems.new(), sems.new(), spot.core
        )
        self.local = pltpu.make_async_copy(src.at[:, columns(spot.w)], here, sems.new())
        for copy in self.halves + [self.to_core, self.local]:
            copy.start()

    def part(self, w, bit):
        return self.dst.at[pl.ds(pl.multiple_of(self.rows * w + self.half * bit, 32), self.half)]

    def forward(self):
        self.aside = []
        for copy, source in zip(self.halves, (self.spot.across, self.spot.corner)):
            copy.wait_recv()
            part = self.part(source[1], self.bit)
            self.aside.append(remote(part, part, self.sems.new(), self.sems.new(), self.mate))
            self.aside[-1].start()

    def finish(self):
        self.local.wait()
        self.to_core.wait_recv()
        for copy in self.aside:
            copy.wait_recv()

    def drain(self):
        for copy in self.halves + self.aside + [self.to_core]:
            copy.wait_send()


class Merge:
    def __init__(self, spot, send, land, sems):
        self.spot, self.send, self.land = spot, send, land
        self.far = remote(
            send.at[spot.corner[1]], land.at[0], sems.new(), sems.new(), spot.core
        )
        self.near = remote(send.at[spot.core[1]], land.at[1], sems.new(), sems.new(), spot.core)
        self.over = remote(
            send.at[spot.across[1]], land.at[2], sems.new(), sems.new(), spot.across
        )
        self.far.start()
        self.near.start()

    def forward(self):
        self.far.wait_recv()
        block = self.send.at[self.spot.across[1]]
        block[...] = (block[...].astype(F32) + self.land[0].astype(F32)).astype(BF)
        self.over.start()

    def finish(self):
        self.near.wait_recv()
        self.over.wait_recv()
        own = self.send[self.spot.w].astype(F32)
        return own + self.land[1].astype(F32) + self.land[2].astype(F32)

    def drain(self):
        for copy in (self.far, self.near, self.over):
            copy.wait_send()


class Spread:
    def __init__(self, spot, pick, place, sems):
        self.copies = []
        for to in (spot.across, spot.corner, spot.core):
            self.copies.append(remote(pick(to[1]), place(spot.w), sems.new(), sems.new(), to))
        self.local = pltpu.make_async_copy(pick(spot.w), place(spot.w), sems.new())
        for copy in self.copies:
            copy.start()
        self.local.start()

    def finish(self):
        for copy in self.copies:
            copy.wait_recv()
        self.local.wait()

    def drain(self):
        for copy in self.copies:
            copy.wait_send()


def nt(left, right):
    return lax.dot_general(left, right, (((1,), (1,)), ((), ())), preferred_element_type=F32)


def nn(left, right):
    return jnp.dot(left, right, preferred_element_type=F32)


def tn(left, right):
    return lax.dot_general(left, right, (((0,), (0,)), ((), ())), preferred_element_type=F32)


def turn(values, cosine, sine):
    wide = values.shape[1]
    lane = lax.broadcasted_iota(jnp.int32, values.shape, 1)
    first = lax.rem(lane, HD) < HD // 2
    swapped = jnp.where(
        first, pltpu.roll(values, wide - HD // 2, 1), pltpu.roll(values, HD // 2, 1)
    )
    copies = wide // PAIR
    cosine = jnp.concatenate([cosine] * copies, axis=1)
    sine = jnp.concatenate([sine] * copies, axis=1)
    return values * cosine + swapped * sine


def stack_pair(values):
    lane = lax.broadcasted_iota(jnp.int32, values.shape, 1)
    none = jnp.zeros_like(values)
    return jnp.concatenate(
        [jnp.where(lane < HD, values, none), jnp.where(lane < HD, none, values)], axis=0
    )


def unstack_pair(values):
    rows = values.shape[0] // 2
    lane = lax.broadcasted_iota(jnp.int32, (rows, PAIR), 1)
    return jnp.where(lane < HD, values[:rows], values[rows:])


class Ring:
    def __init__(self, spot, blocks, recv, send, parts=1):
        self.spot, self.blocks, self.recv, self.send, self.parts = spot, blocks, recv, send, parts
        self.ranks = blocks.shape[0]
        self.used = 0
        self.sent, self.sent_mid, self.sent_end = [], [], []

    def piece(self, slot, part):
        rows = self.blocks.shape[1] // self.parts
        return self.blocks.at[slot, pl.ds(rows * part, rows)]

    def copy(self, slot, part, to):
        self.used += 1
        return remote(
            self.piece(slot, part),
            self.piece(slot, part),
            self.send.at[self.used - 1],
            self.recv.at[slot + self.ranks * part],
            to,
        )

    def arrived(self, slot, part):
        remote(
            self.piece(slot, part),
            self.piece(slot, part),
            self.send.at[0],
            self.recv.at[slot + self.ranks * part],
            self.spot.column,
        ).wait_recv()

    def start(self):
        spot = self.spot
        for part in range(self.parts):
            own = self.copy(spot.k, part, spot.inner)
            side = self.copy(spot.k, part, spot.column)
            back = self.copy(spot.k, part, spot.outer)
            own.start()
            self.middle(back)
            side.start()
            self.sent += [own, side]
            self.sent_mid += [back]

    def middle(self, copy):
        @pl.when(self.spot.mid == 1)
        def _():
            copy.start()

    def step(self, number, only=None):
        spot = self.spot
        slot = 2 * spot.plane(number) + spot.x
        onward = spot.inner if number == 1 else spot.outer
        pieces = []
        for part in range(self.parts):
            along = self.copy(slot, part, onward) if only != 0 else None
            pieces.append((along, self.copy(slot, part, spot.column)))
        if only != 0:

            @pl.when(spot.mid == 1)
            def _():
                for part, (along, side) in enumerate(pieces):
                    self.arrived(slot, part)
                    along.start()
                    side.start()

        if only != 1:

            @pl.when(spot.mid == 0)
            def _():
                for part, (along, side) in enumerate(pieces):
                    self.arrived(slot, part)
                    side.start()

        if only != 0:
            self.sent_mid += [along for along, _ in pieces]
            self.sent_mid += [side for _, side in pieces]
        if only != 1:
            self.sent_end += [side for _, side in pieces]

    def other(self, number):
        for part in range(self.parts):
            self.arrived(2 * self.spot.plane(number) + 1 - self.spot.x, part)

    def drain(self):
        for copy in self.sent:
            copy.wait_send()
        for role, copies in ((0, self.sent_end), (1, self.sent_mid)):

            @pl.when(self.spot.mid == role)
            def _(copies=copies):
                for copy in copies:
                    copy.wait_send()


class Reduce:
    def __init__(self, spot, part, sides, zo, zi, sems, folded=False, parts=1):
        self.spot, self.part, self.sides, self.zo, self.zi = spot, part, sides, zo, zi
        self.x_send, self.x_recv, self.z_send, self.zo_recv, self.zi_recv = (
            sems.at[i] for i in range(5)
        )
        self.folded, self.parts = folded, parts
        self.rows = part.shape[1] // parts
        self.sent, self.sent_end, self.sent_mid = [], [], []

    def cut(self, ref, index, h):
        return ref.at[index, pl.ds(self.rows * h, self.rows)]

    def own(self, plane, h):
        return self.cut(self.part, plane if self.folded else 2 * plane + self.spot.x, h)

    def wait(self, land, recv, plane, h):
        piece = self.cut(land, plane, h)
        at = plane + 4 * h
        remote(piece, piece, self.z_send.at[at], recv.at[at], self.spot.column).wait_recv()

    def side(self, number):
        spot = self.spot
        plane = spot.plane(number)
        for h in range(self.parts):
            at = plane + 4 * h
            copy = remote(
                self.cut(self.part, 2 * plane + 1 - spot.x, h),
                self.cut(self.sides, plane, h),
                self.x_send.at[at],
                self.x_recv.at[at],
                spot.column,
            )
            copy.start()
            self.sent.append(copy)

    def add(self, ref, land):
        ref[...] = (ref[...].astype(F32) + land[...].astype(F32)).astype(BF)

    def meet(self, number):
        plane = self.spot.plane(number)
        for h in range(self.parts):
            self.wait(self.sides, self.x_recv, plane, h)
            self.add(self.own(plane, h), self.cut(self.sides, plane, h))
            if number > 0 and self.zo is not None:
                self.launch_part(number, h)

    def launch(self, number):
        for h in range(self.parts):
            self.launch_part(number, h)

    def launch_part(self, number, h):
        plane = self.spot.plane(number)
        at = plane + 4 * h
        copy = remote(
            self.own(plane, h),
            self.cut(self.zo, plane, h),
            self.z_send.at[at],
            self.zo_recv.at[at],
            self.spot.inner,
        )

        @pl.when(self.spot.mid == 0)
        def _():
            copy.start()

        self.sent_end.append(copy)

    def absorb(self, number):
        plane = self.spot.plane(number)

        @pl.when(self.spot.mid == 1)
        def _():
            for h in range(self.parts):
                self.wait(self.zo, self.zo_recv, plane, h)
                self.add(self.own(plane, h), self.cut(self.zo, plane, h))

    def relay(self, number):
        plane = self.spot.plane(number)
        land, recv = (self.zi, self.zi_recv) if number == 1 else (self.zo, self.zo_recv)
        copies = []
        for h in range(self.parts):
            at = plane + 4 * h
            copies.append(
                remote(
                    self.own(plane, h),
                    self.cut(self.zi, plane, h),
                    self.z_send.at[at],
                    self.zi_recv.at[at],
                    self.spot.outer if number == 1 else self.spot.inner,
                )
            )

        @pl.when(self.spot.mid == 1)
        def _():
            for h, copy in enumerate(copies):
                if land is not None:
                    self.wait(land, recv, plane, h)
                    self.add(self.own(plane, h), self.cut(land, plane, h))
                copy.start()

        self.sent_mid += copies

    def last(self, result):
        plane = self.spot.plane(0)
        for h in range(self.parts):
            self.wait(self.zi, self.zi_recv, plane, h)
            rows = pl.ds(self.rows * h, self.rows)
            total = self.own(plane, h)[...].astype(F32)
            result[rows] = total + self.cut(self.zi, plane, h)[...].astype(F32)

        if self.zo is None:
            return

        @pl.when(self.spot.mid == 1)
        def _():
            for h in range(self.parts):
                self.wait(self.zo, self.zo_recv, plane, h)
                rows = pl.ds(self.rows * h, self.rows)
                result[rows] += self.cut(self.zo, plane, h)[...].astype(F32)

    def drain(self):
        for copy in self.sent:
            copy.wait_send()

        @pl.when(self.spot.mid == 0)
        def _():
            for copy in self.sent_end:
                copy.wait_send()

        @pl.when(self.spot.mid == 1)
        def _():
            for copy in self.sent_mid:
                copy.wait_send()


def swish(values):
    sigmoid = 1.0 / (1.0 + jnp.exp(-values))
    return values * sigmoid, sigmoid * (1.0 + values * (1.0 - sigmoid))


class Exchange:
    def __init__(self, spot, out, back, send, recv):
        self.spot, self.out, self.back = spot, out, back
        self.send, self.recv, self.ranks = send, recv, out.shape[0]
        self.copies = []

    def start(self):
        spot = self.spot
        for offset in range(1, self.ranks):
            peer = lax.rem(spot.k + offset, self.ranks)
            self.copies.append(
                remote(
                    self.out.at[peer],
                    self.back.at[spot.k],
                    self.send.at[offset],
                    self.recv.at[spot.k],
                    (peer, spot.w),
                )
            )
            self.copies[-1].start()
        self.back[spot.k] = self.out[spot.k]

    def finish(self):
        spot = self.spot
        for offset in range(1, self.ranks):
            peer = lax.rem(spot.k + offset, self.ranks)
            remote(
                self.out.at[peer],
                self.back.at[peer],
                self.send.at[offset],
                self.recv.at[peer],
                (peer, spot.w),
            ).wait_recv()

    def drain(self):
        for copy in self.copies:
            copy.wait_send()


def fold_rows(values, ref):
    ranks = ref.shape[0]
    slots = values.shape[0] // ranks
    for e in range(ranks):
        part = values[slots * e : slots * (e + 1)]
        tiles = [part[:, 128 * t : 128 * (t + 1)] for t in range(values.shape[1] // 128)]
        ref[e] = jnp.concatenate(tiles, axis=0).astype(BF)


def unfold_rows(ref, slots):
    parts = []
    for e in range(ref.shape[0]):
        part = ref[e].astype(F32)
        tiles = [part[slots * t : slots * (t + 1)] for t in range(part.shape[0] // slots)]
        parts.append(jnp.concatenate(tiles, axis=1))
    return jnp.concatenate(parts, axis=0).astype(BF)


def split_three(values):
    high = values.astype(BF)
    rest = values - high.astype(F32)
    middle = rest.astype(BF)
    return high, middle, (rest - middle.astype(F32)).astype(BF)


def diagonal(values, axis):
    size = max(values.shape)
    down = lax.broadcasted_iota(jnp.int32, (size, size), 0)
    along = lax.broadcasted_iota(jnp.int32, (size, size), 1)
    return jnp.sum(
        jnp.where(down == along, values.astype(F32), 0.0), axis=axis, keepdims=True
    ).astype(jnp.int32)


def slot_maps(routes, order, slots, experts):
    top, rows = routes.shape
    pairs = rows * top
    lines = [routes[j : j + 1] for j in range(top)]
    e_row = jnp.concatenate(lines, axis=1)
    e_col = jnp.concatenate([diagonal(line, 1) for line in lines], axis=0)
    o_row = lax.rem(order, top) * rows + lax.div(order, top)
    o_col = diagonal(o_row, 1)
    down = lax.broadcasted_iota(jnp.int32, (pairs, pairs), 0)
    along = lax.broadcasted_iota(jnp.int32, (pairs, pairs), 1)
    turn_row = jnp.sum(jnp.where(o_col == along, down.astype(F32), 0.0), axis=0, keepdims=True)
    turn_col = jnp.sum(jnp.where(o_row == down, along.astype(F32), 0.0), axis=1, keepdims=True)
    same = e_col == e_row
    slot_row = jnp.sum(
        jnp.where(same & (turn_col < turn_row), 1.0, 0.0), axis=0, keepdims=True
    ).astype(jnp.int32)
    slot_col = jnp.sum(
        jnp.where(same & (turn_row < turn_col), 1.0, 0.0), axis=1, keepdims=True
    ).astype(jnp.int32)
    target_row = jnp.where(slot_row < slots, e_row * slots + slot_row, -1)
    target_col = jnp.where(slot_col < slots, e_col * slots + slot_col, -1)
    total = experts * slots
    place = lax.broadcasted_iota(jnp.int32, (total, pairs), 0)
    to_slots = jnp.where(place == target_row, 1.0, 0.0).astype(BF)
    place = lax.broadcasted_iota(jnp.int32, (pairs, total), 1)
    to_pairs = jnp.where(place == target_col, 1.0, 0.0).astype(BF)
    return to_slots, to_pairs


def forward_kernel(
    tok, gains, router_ref, freq, deal, cot, routes, order, sd,
    wq, wk, wv, wo, sg, su, eg, eu, ed,
    cosr, sinr, kb, qb, q_out, mixed_out, lse_out, normed_out, pack_out, result_out, grad_second_out, pack_grad_out,
    dsh_out, kv_out, wfull_out, keep_out, give_out, other_out,
    wbuf, kv, q_s, pack, packs, top, low, acc, sg_all, su_all, wg, wu, wd, mix, m4, cot4,
    sh_send, sh_recv, gm_send, gm_recv, xs, xr, gs, gr, os, orr, bs, br,
    x_s, g_s, sum_s, gate_s, up_s, hid_s, dgate_s, dup_s, dsh, dsh_x, dsh_z, slot_s, pair_s, cb,
    sem, kv_recv, kv_send, a2a_send, a2a_recv, sem_sh,
):
    spot = Spot(4)
    sems = Sems(sem)
    rows, width = tok.shape
    pairs = width // PAIR
    ranks = xs.shape[0]
    slots = xs.shape[1] * 128 // width
    hidden = wg.shape[1]
    shard = width // 4
    part = sg_all.shape[1]
    peers = [(lax.rem(spot.k + o, ranks), spot.w) for o in range(1, ranks)]
    greet([spot.core, spot.across, spot.corner] + peers)
    column, line = (spot.column, spot.x), (spot.line, spot.odd)
    key_w = Share(spot, wk, wbuf.at[1], sems, *column)
    shards = jnp.concatenate(
        [gains[...], router_ref[...], jnp.zeros((16 - 2 - router_ref.shape[0], shard), BF)], axis=0
    ).astype(F32)
    shards = jnp.concatenate([shards, jnp.zeros((16, width - shard), F32)], axis=1)
    pack[...] = pltpu.roll(shards, shard * spot.w, 1).astype(BF)
    params = Gather(spot, pack, lambda w: packs.at[w], sems)
    value_w = Share(spot, wv, wbuf.at[2], sems, *column)
    query_w = Share(spot, wq, wbuf.at[0], sems, *column)

    def stripe(ref):
        return lambda w: ref.at[pl.ds(pl.multiple_of(shard * w, 64), shard)]

    out_w = Share(spot, wo, wbuf.at[3], sems, *line)
    sg_w = ShareColumns(spot, sg, sg_all, sems, *line)
    su_w = ShareColumns(spot, su, su_all, sems, *line)
    cot_w = Gather(spot, cot, lambda w: cot4.at[w], sems)
    gate_w = Gather(spot, eg, stripe(wg), sems)
    up_w = Gather(spot, eu, stripe(wu), sems)
    inputs = tok[...].astype(F32)
    scale = lax.rsqrt(jnp.mean(inputs * inputs, axis=-1, keepdims=True) + EPS)
    scaled = inputs * scale
    piece = rows // 2
    inner = lax.broadcasted_iota(jnp.int32, (rows, 1), 0)
    lane = lax.broadcasted_iota(jnp.int32, (rows, PAIR), 1)
    sign = jnp.where(lax.rem(lane, HD) < HD // 2, -1.0, 1.0)
    for r in range(2):
        paired = deal[2 * spot.z + r]
        unit = jnp.where(inner < piece, paired, 2 * ranks - 1 - paired)
        place = unit * piece + lax.rem(inner, piece)
        qb[r] = jnp.concatenate([lax.div(place, BLK)] * 2, axis=0)
        angles = place.astype(F32) * freq[...]
        cosr[r] = jnp.cos(angles)
        sinr[r] = jnp.sin(angles) * sign
    along = lax.broadcasted_iota(jnp.int32, (1, rows), 1)
    for r in range(ranks):
        unit = jnp.where(along < piece, deal[r], 2 * ranks - 1 - deal[r])
        kb[:, rows * r : rows * (r + 1)] = lax.div(unit * piece + lax.rem(along, piece), BLK)
    key_w.forward()
    params.forward()
    params.finish()
    pack_all = (packs[0].astype(F32) + packs[1].astype(F32)) + (
        packs[2].astype(F32) + packs[3].astype(F32)
    )
    pack_out[...] = pack_all
    normed = (scaled * pack_all[0:1]).astype(BF)
    normed_out[...] = normed
    cosine, sine = cosr[spot.x], sinr[spot.x]
    to_slots, to_pairs = slot_maps(routes[...], order[...], slots, ranks)
    route = [diagonal(routes[j : j + 1], 1) for j in range(2)]
    slot_s[...] = to_slots
    pair_s[...] = to_pairs
    value_w.forward()
    key_w.second()
    query_w.forward()
    key_w.finish()
    kv[spot.k, :, 0:width] = turn(nn(normed, wbuf[1]), cosine, sine).astype(BF)
    value_w.second()
    value_w.finish()
    kv[spot.k, :, width : 2 * width] = nn(normed, wbuf[2]).astype(BF)
    ring = Ring(spot, kv, kv_recv, kv_send, parts=2)
    ring.start()
    query_w.second()

    query_w.finish()
    query = turn(nn(normed, wbuf[0]), cosine, sine).astype(BF) * jnp.asarray(HD**-0.5, BF)
    for j in range(pairs):
        q_s[j] = stack_pair(query[:, PAIR * j : PAIR * (j + 1)])
    for x in range(2):
        q_out[x] = query[:, width // 2 * x : width // 2 * (x + 1)]
    top[...] = jnp.full_like(top, MASKED)
    low[...] = jnp.zeros_like(low)
    acc[...] = jnp.zeros_like(acc)
    q_block = qb[spot.x]

    def chunk(plane):
        k_block = kb[:, pl.ds(pl.multiple_of(2 * rows * plane, 2 * rows), 2 * rows)]
        allowed = k_block <= q_block

        def one_pair(j, carry):
            lane = pl.multiple_of(PAIR * j, PAIR)
            key = kv[pl.ds(2 * plane, 2), :, pl.ds(lane, PAIR)].reshape(2 * rows, PAIR)
            value = kv[pl.ds(2 * plane, 2), :, pl.ds(width + lane, PAIR)].reshape(2 * rows, PAIR)
            scores = jnp.where(allowed, nt(q_s[j], key), MASKED)
            old = top[j]
            new = jnp.maximum(old, jnp.max(scores, axis=1, keepdims=True))
            raised = jnp.where(allowed, jnp.exp(scores - new[:, 0:1]), 0.0)
            factor = jnp.exp(old - new)
            top[j] = new
            low[j] = low[j] * factor + jnp.sum(raised, axis=1, keepdims=True)
            acc[j] = acc[j] * factor + nn(raised.astype(BF), value)
            return carry

        lax.fori_loop(0, pairs, one_pair, 0)

    ring.step(1)
    ring.step(2, only=1)
    ring.other(0)
    chunk(spot.plane(0))
    ring.step(2, only=0)
    ring.step(3, only=1)
    ring.other(1)
    chunk(spot.plane(1))
    ring.step(3, only=0)
    out_w.forward()
    sg_w.forward()
    su_w.forward()
    ring.other(2)
    chunk(spot.plane(2))
    out_w.second()
    cot_w.forward()
    ring.other(3)
    chunk(spot.plane(3))
    saves = [pltpu.make_async_copy(kv, kv_out, sems.new())]
    saves[0].start()
    for j in range(pairs):
        mixed_out[:, PAIR * j : PAIR * (j + 1)] = unstack_pair(acc[j] / low[j])
        lse_out[j] = top[j] + jnp.log(low[j])
    out_w.finish()
    saves.append(pltpu.make_async_copy(wbuf, wfull_out, sems.new()))
    saves[1].start()
    second = inputs + nn(mixed_out[...].astype(BF), wbuf[3])
    scale = lax.rsqrt(jnp.mean(second * second, axis=-1, keepdims=True) + EPS)
    mixer = (second * scale * pack_all[1:2]).astype(BF)
    mix[...] = mixer

    mixers = Gather(spot, mix, lambda w: m4.at[w], sems)
    down_w = Gather(spot, ed, stripe(wd), sems)
    fold_rows(nn(slot_s[:, :rows] + slot_s[:, rows:], mixer), xs)
    rows_out = Exchange(spot, xs, xr, a2a_send.at[0], a2a_recv.at[0])
    rows_out.start()
    router = pack_all[2:16].astype(BF)
    router = jnp.concatenate([router, jnp.zeros((2, width), BF)], axis=0)
    logits = nt(mixer, router)
    lane = lax.broadcasted_iota(jnp.int32, logits.shape, 1)
    matches = [lane == route[j] for j in range(2)]
    chosen = [jnp.sum(jnp.where(m, logits, 0.0), axis=1, keepdims=True) for m in matches]
    largest = jnp.maximum(chosen[0], chosen[1])
    raised = [jnp.exp(c - largest) for c in chosen]
    gates = [r / (raised[0] + raised[1]) for r in raised]
    grad = cot[...].astype(F32)
    pair_grad = jnp.concatenate([(g * grad).astype(BF) for g in gates], axis=0)
    fold_rows(nn(slot_s[...], pair_grad), gs)
    grads_out = Exchange(spot, gs, gr, a2a_send.at[1], a2a_recv.at[1])
    grads_out.start()
    gate_w.forward()
    up_w.forward()
    mixers.forward()

    for part_w in (sg_w, su_w, cot_w, mixers):
        part_w.finish()
    rows_all = m4[...].reshape(4 * rows, width)
    grad_all = cot4[...].reshape(4 * rows, width)
    gate_part, up_part = nn(rows_all, sg_all[...]), nn(rows_all, su_all[...])
    act, slope = swish(gate_part)
    shared_hidden = (act * up_part).astype(BF)
    sh_send[...] = nn(shared_hidden, sd[...]).astype(BF).reshape(4, rows, width)
    shared_out = Merge(spot, sh_send, sh_recv, sems)
    hid_grad = nt(grad_all, sd[...])
    grad_gate = (hid_grad * up_part * slope).astype(BF)
    grad_up = (hid_grad * act).astype(BF)
    back = nt(grad_gate, sg_all[...]) + nt(grad_up, su_all[...])
    gm_send[...] = back.astype(BF).reshape(4, rows, width)
    shared_out.forward()
    shared_back = Merge(spot, gm_send, gm_recv, sems)
    half = shard // 2
    for at, values in ((0, tn(rows_all, grad_gate)), (half, tn(rows_all, grad_up))):
        values = values.astype(BF)
        for r in range(ranks):
            down, left = half * (r // 4), 128 * (r % 4)
            for w in range(4):
                dsh[r, shard * w + at : shard * w + at + half] = values[
                    shard * w + down : shard * w + down + half, left : left + 128
                ]
    values = tn(shared_hidden, grad_all).astype(BF)
    deep = values.shape[0] // ranks
    for r in range(ranks):
        for t in range(width // 128):
            dsh[r, width + deep * t : width + deep * (t + 1)] = values[
                deep * r : deep * (r + 1), 128 * t : 128 * (t + 1)
            ]
    shared_back.forward()
    shared_grad = Reduce(spot, dsh, dsh_x, dsh_z, None, sem_sh)
    for number in (3, 2, 1, 0):
        shared_grad.side(number)

    for part_w in (gate_w, up_w):
        part_w.finish()
    rows_out.finish()
    x_s[...] = unfold_rows(xr, slots)
    block = 512

    def parts(i):
        return pl.ds(pl.multiple_of(block * i, block), block)

    def up_step(i, carry):
        at = parts(i)
        gate = nn(x_s[...], wg[:, at])
        up = nn(x_s[...], wu[:, at])
        act, slope = swish(gate)
        hid_s[:, at] = (act * up).astype(BF)
        gate_s[:, at] = up * slope
        up_s[:, at] = act
        return carry

    lax.fori_loop(0, hidden // block, up_step, 0)
    down_w.forward()
    down_w.finish()
    shared_grad.meet(3)
    sum_s[...] = nt(hid_s[...], wd[...])
    fold_rows(sum_s[...], os)
    outs = Exchange(spot, os, orr, a2a_send.at[2], a2a_recv.at[2])
    outs.start()
    grads_out.finish()
    g_s[...] = unfold_rows(gr, slots)

    def down_step(i, carry):
        at = parts(i)
        grad_hidden = nn(g_s[...], wd[:, at])
        dgate_s[:, at] = (grad_hidden * gate_s[:, at]).astype(BF)
        dup_s[:, at] = (grad_hidden * up_s[:, at]).astype(BF)
        return carry

    lax.fori_loop(0, hidden // block, down_step, 0)
    sum_s[...] = nt(dgate_s[...], wg[...]) + nt(dup_s[...], wu[...])
    fold_rows(sum_s[...], bs)
    backs = Exchange(spot, bs, br, a2a_send.at[3], a2a_recv.at[3])
    backs.start()

    for part_w in (gate_w, up_w, down_w):
        part_w.drain()
    swaps, across = [], []
    first = 2 * shard // 3
    sources = ((wg, x_s, dgate_s), (wu, x_s, dup_s), (wd, g_s, hid_s))

    def grads_of(a):
        ref, left, right = sources[a]

        def grad_step(i, carry):
            at = parts(i)
            ref[:, at] = tn(left[...], right[:, at]).astype(BF)
            return carry

        lax.fori_loop(0, hidden // block, grad_step, 0)
        for row in range(2):
            src = ref.at[pl.ds(pl.multiple_of(shard * (2 * row + 1 - spot.c), 64), shard)]
            swaps.append(remote(src, cb.at[a, row], sems.new(), sems.new(), spot.core))
            swaps[-1].start()

    def add_mate(a):
        ref = sources[a][0]
        for row in range(2):
            swaps[2 * a + row].wait_recv()

        def add(i, carry):
            for row in range(2):
                at = pl.ds(pl.multiple_of(shard * (2 * row + spot.c) + 16 * i, 16), 16)
                mate = cb[a, row, pl.ds(pl.multiple_of(16 * i, 16), 16)].astype(F32)
                ref[at] = (ref[at].astype(F32) + mate).astype(BF)
            return carry

        lax.fori_loop(0, shard // 16, add, 0)
        start = pl.multiple_of(shard * spot.across[1], 64)
        keep = ref.at[pl.ds(pl.multiple_of(shard * spot.w, 64), shard)]
        saves.append(pltpu.make_async_copy(keep, keep_out.at[a], sems.new()))
        if a == 0:
            across.append(
                remote(ref.at[pl.ds(start, first)], other_out, sems.new(), sems.new(), spot.across)
            )
            across[-1].start()
            give = ref.at[pl.ds(pl.multiple_of(start + first, 64), shard - first)]
            saves.append(
                pltpu.make_async_copy(give, give_out.at[0, pl.ds(first, shard - first)], sems.new())
            )
        else:
            give = ref.at[pl.ds(start, shard)]
            saves.append(pltpu.make_async_copy(give, give_out.at[a], sems.new()))
        for copy in saves[-2:]:
            copy.start()

    shared_grad.meet(2)
    grads_of(0)
    grads_of(1)
    add_mate(0)
    shared_grad.meet(1)
    grads_of(2)
    add_mate(1)
    add_mate(2)
    shared_grad.meet(0)
    total = second + shared_out.finish()
    grad_mixer = shared_back.finish()
    outs.finish()
    pair_out = nn(pair_s[...], unfold_rows(orr, slots))
    pair_out = [pair_out[:rows], pair_out[rows:]]
    result_out[...] = (total + gates[0] * pair_out[0] + gates[1] * pair_out[1]).astype(BF)
    grad_gates = [jnp.sum(grad * p, axis=1, keepdims=True) for p in pair_out]
    inner = gates[0] * grad_gates[0] + gates[1] * grad_gates[1]
    grad_logits = jnp.zeros_like(logits)
    for j in range(2):
        grad_logits += jnp.where(matches[j], gates[j] * (grad_gates[j] - inner), 0.0)
    pieces = split_three(grad_logits)
    router_grad = sum(tn(piece, mixer) for piece in pieces)
    grad_mixer = grad_mixer + sum(nn(piece, router) for piece in pieces)
    backs.finish()
    grad_mixer = grad_mixer + nn(pair_s[:rows] + pair_s[rows:], unfold_rows(br, slots))
    weighted = grad_mixer * pack_all[1:2]
    mean = jnp.mean(weighted * second, axis=-1, keepdims=True)
    grad_second_out[...] = grad + scale * weighted - second * (scale * scale * scale * mean)
    gain_grad = jnp.sum(grad_mixer * second * scale, axis=0, keepdims=True)
    pack_grad_out[...] = jnp.concatenate(
        [jnp.zeros_like(gain_grad), gain_grad, router_grad[:14]], axis=0
    )
    for number in (3, 2, 0):
        shared_grad.absorb(number)
    for plane in range(4):
        dsh_out[plane] = dsh[2 * plane + spot.x]
    for copy in across:
        copy.wait_recv()
    for part_w in (params, key_w, value_w, query_w, out_w, sg_w, su_w, cot_w, ring, mixers):
        part_w.drain()
    for part_w in (rows_out, grads_out, outs, backs, shared_out, shared_back, shared_grad):
        part_w.drain()
    for copy in swaps + across:
        copy.wait_send()
    for copy in saves:
        copy.wait()


def run_forward(
    tok, gains, router, freq, deal, cot, routes, order, sd,
    wq, wk, wv, wo, sg, su, eg, eu, ed,
):
    rows, width = tok.shape
    pairs = width // PAIR
    ranks, slots = 8, 40
    hidden = eg.shape[1]
    part = sg.shape[1] // 4
    shard = width // 4
    total = ranks * slots
    tall = width + part * width // (128 * ranks)
    any_, vm = pl.BlockSpec(memory_space=pl.ANY), pl.BlockSpec(memory_space=VMEM)
    shape = jax.ShapeDtypeStruct

    def low(*dims):
        return VMEM(dims, BF)

    def full(*dims):
        return VMEM(dims, F32)

    dma = pltpu.SemaphoreType.DMA
    folded = low(ranks, slots * width // 128, 128)
    return pl.pallas_call(
        forward_kernel,
        out_shape=(
            shape((2, rows, PAIR), F32),
            shape((2, rows, PAIR), F32),
            shape((1, ranks * rows), jnp.int32),
            shape((2, 2 * rows, 1), jnp.int32),
            shape((2, rows, width // 2), BF),
            shape((rows, width), F32),
            shape((pairs, 2 * rows, PAIR), F32),
            shape((rows, width), BF),
            shape((16, width), F32),
            shape((rows, width), BF),
            shape((rows, width), F32),
            shape((16, width), F32),
            shape((4, tall, 128), BF),
            shape((ranks, rows, 2 * width), BF),
            shape((4, width, width), BF),
            shape((3, shard, hidden), BF),
            shape((3, shard, hidden), BF),
            shape((2 * shard // 3, hidden), BF),
        ),
        in_specs=[vm] * 4 + [pl.BlockSpec(memory_space=pltpu.SMEM)] + [vm] * 4 + [any_] * 9,
        out_specs=tuple([vm] * 13 + [any_] * 5),
        scratch_shapes=[
            low(4, width, width),
            low(ranks, rows, 2 * width),
            low(pairs, 2 * rows, PAIR),
            low(16, width),
            low(4, 16, width),
            full(pairs, 2 * rows, PAIR),
            full(pairs, 2 * rows, PAIR),
            full(pairs, 2 * rows, PAIR),
            low(width, part),
            low(width, part),
            low(width, hidden),
            low(width, hidden),
            low(width, hidden),
            low(rows, width),
            low(4, rows, width),
            low(4, rows, width),
            low(4, rows, width),
            low(3, rows, width),
            low(4, rows, width),
            low(3, rows, width),
            *[folded] * 8,
            low(total, width),
            low(total, width),
            full(total, width),
            full(total, hidden),
            full(total, hidden),
            low(total, hidden),
            low(total, hidden),
            low(total, hidden),
            low(ranks, tall, 128),
            low(4, tall, 128),
            low(4, tall, 128),
            low(total, 2 * rows),
            low(2 * rows, total),
            low(3, 2, shard, hidden),
            dma((144,)),
            dma((2 * ranks,)),
            dma((32,)),
            dma((4, ranks)),
            dma((4, ranks)),
            dma((5, 8)),
        ],
        compiler_params=pltpu.CompilerParams(
            collective_id=1, has_side_effects=True, vmem_limit_bytes=VMEM_BYTES
        ),
    )(
        tok, gains, router, freq, deal, cot, routes, order, sd,
        wq, wk, wv, wo, sg, su, eg, eu, ed,
    )


def backward_kernel(
    grad_second_ref, tok, pack_ref, pack_grad_ref, normed_ref, mixed_ref, qc_ref, lse_ref,
    cosr, sinr, kb, qb, dsh_ref, kv_ref, wfull_ref, give_ref, other_ref,
    grad_input_out, pack_out, att1_out, att2_out, sh_out, other_out,
    wo, w_half, kv, kvb, kv_zo, kv_zi, kv_sum, q_land, gm, gm_land, qx, gx, lse_x, delta_s, delta_x,
    stat, stat_land, dq, ga, ga4, gq, gq4, gkv, gkv4, n_t, m_t, n_all, m_all, pk, pk4, pk_sum, pk_land,
    o_send, o_land, gn_send, gn_land, a1, a1_zo, a1_zi, a1_sum, a2, a2_zo, a2_zi, a2_sum, r1, r2,
    sh, sh_zi, sh_sum, sh_chunk, r3,
    sem, sem_kv, sem_a1, sem_a2, sem_sh, ring_recv, ring_send,
):
    spot = Spot(4)
    sems = Sems(sem)
    rows, width = tok.shape
    half = width // 2
    group = half // PAIR
    shard = width // 4
    mine = pl.ds(pl.multiple_of(half * spot.x, half), half)
    values = pl.ds(pl.multiple_of(width + half * spot.x, half), half)
    ranks = kv.shape[0]
    dsh_load = pltpu.make_async_copy(dsh_ref, sh, sems.new())
    dsh_load.start()
    loads = [
        pltpu.make_async_copy(wfull_ref.at[3], wo, sems.new()),
        pltpu.make_async_copy(kv_ref.at[:, :, mine], kv.at[:, :, pl.ds(0, half)], sems.new()),
        pltpu.make_async_copy(kv_ref.at[:, :, values], kv.at[:, :, pl.ds(half, half)], sems.new()),
        *[
            pltpu.make_async_copy(wfull_ref.at[i, :, mine], w_half.at[i], sems.new())
            for i in range(3)
        ],
    ]
    done = other_ref.shape[0]
    loads.append(pltpu.make_async_copy(other_ref, other_out.at[0, pl.ds(0, done)], sems.new()))
    for copy in loads:
        copy.start()

    def block(ref, w):
        return ref.at[pl.ds(pl.multiple_of(shard * w, 64), shard)]

    greet((spot.core, spot.across, spot.corner, spot.column, spot.inner), (spot.mid, spot.outer))
    asides = []

    def aside(src, dst):
        asides.append(remote(src, dst, sems.new(), sems.new(), spot.column))
        asides[-1].start()
        return asides[-1]

    query_x = aside(qc_ref.at[1 - spot.x], q_land)
    grad_second = grad_second_ref[...]
    ga[...] = grad_second.astype(BF)
    grads_w = Gather(spot, ga, lambda w: ga4.at[w], sems)
    mixed = mixed_ref[...]
    dsh_load.wait()
    shared = Reduce(spot, sh, None, None, sh_zi, sem_sh, folded=True, parts=2)
    shared.relay(3)
    shared.relay(2)

    loads[0].wait()
    grad_mixed = nt(ga[...], wo[...]).astype(BF)
    for x in range(2):
        gm[x] = grad_mixed[:, half * x : half * (x + 1)]
    grads_x = aside(gm.at[1 - spot.x], gm_land)
    product = grad_mixed.astype(F32) * mixed
    for j in range(2 * group):
        delta_s[j] = jnp.broadcast_to(
            jnp.sum(stack_pair(product[:, PAIR * j : PAIR * (j + 1)]), axis=1, keepdims=True),
            (2 * rows, PAIR),
        )
    lane = lax.broadcasted_iota(jnp.int32, (2 * rows, PAIR), 1)
    table = jnp.zeros((2 * rows, PAIR), F32)
    for i in range(group):
        theirs = group * (1 - spot.x) + i
        table = jnp.where(lane == i, lse_ref[theirs], table)
        table = jnp.where(lane == group + i, delta_s[theirs], table)
    stat[...] = table.T[0:8]
    stat_x = aside(stat, stat_land)
    for i in range(group):
        qx[i] = stack_pair(qc_ref[spot.x, :, PAIR * i : PAIR * (i + 1)])
        gx[i] = stack_pair(gm[spot.x, :, PAIR * i : PAIR * (i + 1)])
        lse_x[i] = lse_ref[group * spot.x + i]
        delta_x[i] = delta_s[group * spot.x + i]
    n_t[...] = normed_ref[...].T
    m_t[...] = mixed.astype(BF).T

    def columns(ref):
        return lambda w: ref.at[:, pl.ds(pl.multiple_of(rows * w, 128), rows)]

    normed_w = Spread(spot, lambda w: block(n_t, w), columns(n_all.at[spot.x]), sems)
    mixed_w = Spread(spot, lambda w: block(m_t, w), columns(m_all), sems)
    across = []

    def send_across(src, dst):
        across.append(remote(src, dst, sems.new(), sems.new(), spot.across))
        across[-1].start()

    left = pl.ds(done, shard - done)
    send_across(give_ref.at[0, left], other_out.at[0, left])
    dq[...] = jnp.zeros_like(dq)
    query_x.wait_recv()
    grads_x.wait_recv()
    for i in range(group):
        qx[group + i] = stack_pair(q_land[:, PAIR * i : PAIR * (i + 1)])
        gx[group + i] = stack_pair(gm_land[:, PAIR * i : PAIR * (i + 1)])
    stat_x.wait_recv()
    table = jnp.concatenate([stat_land[...], jnp.zeros((PAIR - 8, 2 * rows), F32)], axis=0).T
    for i in range(group):
        lse_x[group + i] = jnp.broadcast_to(table[:, i : i + 1], (2 * rows, PAIR))
        delta_x[group + i] = jnp.broadcast_to(
            table[:, group + i : group + i + 1], (2 * rows, PAIR)
        )
    loads[1].wait()
    loads[2].wait()

    def chunk(number):
        plane = spot.plane(number)
        k_block = kb[:, pl.ds(pl.multiple_of(2 * rows * plane, 2 * rows), 2 * rows)]
        allowed = [k_block <= qb[spot.x], k_block <= qb[1 - spot.x]]

        def one_pair(i, carry):
            lane = pl.multiple_of(PAIR * i, PAIR)
            both = pl.ds(2 * plane, 2)
            key = kv[both, :, pl.ds(lane, PAIR)].reshape(2 * rows, PAIR)
            value = kv[both, :, pl.ds(half + lane, PAIR)].reshape(2 * rows, PAIR)
            grad_key = jnp.zeros((2 * rows, PAIR), F32)
            grad_value = jnp.zeros((2 * rows, PAIR), F32)
            for owner in range(2):
                j = group * owner + i
                query, grad = qx[j], gx[j]
                raised = jnp.exp(nt(query, key) - lse_x[j][:, 0:1])
                probs = jnp.where(allowed[owner], raised, 0.0)
                inner = nt(grad, value) - delta_x[j][:, 0:1]
                grad_scores = (probs * inner * HD**-0.5).astype(BF)
                dq[j] += nn(grad_scores, key)
                grad_key += tn(grad_scores, query)
                grad_value += tn(probs.astype(BF), grad)
            kvb[plane, :, pl.ds(lane, PAIR)] = (grad_key * HD**0.5).astype(BF)
            kvb[plane, :, pl.ds(half + lane, PAIR)] = grad_value.astype(BF)
            return carry

        lax.fori_loop(0, group, one_pair, 0)

    kv_grad = Reduce(spot, kvb, None, kv_zo, kv_zi, sem_kv, folded=True, parts=2)
    chunk(3)
    kv_grad.launch(3)
    chunk(2)
    kv_grad.launch(2)
    shared.relay(1)
    chunk(1)
    kv_grad.launch(1)
    shared.last(sh_sum)
    sh_chunk[...] = sh_sum[...].astype(BF)
    part = 2 * shard // 2

    def piece(w):
        return sh_chunk.at[pl.ds(pl.multiple_of(part * w, 64), part)]

    def place(w):
        return r3.at[spot.k, pl.ds(pl.multiple_of(part * w, 64), part)]

    shared_w = Spread(spot, piece, place, sems)
    rest = sh_chunk.shape[0] - 4 * part
    r3[spot.k, pl.ds(4 * part, rest)] = sh_chunk[pl.ds(4 * part, rest)]
    kv_grad.relay(3)
    chunk(0)
    cosine, sine = cosr[...].reshape(2 * rows, PAIR), sinr[...].reshape(2 * rows, PAIR)
    for owner in range(2):
        at = spot.x if owner == 0 else 1 - spot.x
        parts = [unstack_pair(dq[group * owner + i]) for i in range(group)]
        gq[at] = turn(jnp.concatenate(parts, axis=1), cosr[at], -sinr[at]).astype(BF)
    query_w = Gather(spot, gq, lambda w: gq4.at[w], sems)
    send_across(give_ref.at[1], other_out.at[1])
    shared_w.finish()
    ring3 = Ring(spot, r3, ring_recv.at[2], ring_send.at[2], parts=2)
    ring3.start()
    normed_w.finish()
    normed_x = aside(n_all.at[spot.x], n_all.at[spot.x])
    grads_w.forward()
    mixed_w.finish()
    grads_w.finish()
    kv_grad.relay(2)
    out_grad = nn(m_all[...], ga4[...].reshape(4 * rows, width)).astype(BF)
    for x in range(2):
        o_send[x] = out_grad[:, half * x : half * (x + 1)]
    out_x = aside(o_send.at[1 - spot.x], o_land)
    kv_grad.relay(1)
    ring3.step(1)
    ring3.step(2, only=1)
    for copy in loads[3:6]:
        copy.wait()
    flat = gq[...].reshape(2 * rows, half)
    grad_normed = nt(flat, w_half[0])
    query_w.forward()
    query_w.finish()
    normed_x.wait_recv()

    def weight_grad(grads4):
        total = nn(n_all[0], grads4[:, 0].reshape(4 * rows, grads4.shape[3]))
        return total + nn(n_all[1], grads4[:, 1].reshape(4 * rows, grads4.shape[3]))

    query_grad = weight_grad(gq4).astype(BF)
    out_x.wait_recv()
    out_half = (o_send[spot.x].astype(F32) + o_land[...].astype(F32)).astype(BF)
    size = shard // 4
    for plane in range(4):
        at = slice(size * plane, size * (plane + 1))
        a1[plane, :, 0:half] = out_half[at]
        a1[plane, :, half:width] = query_grad[at]
    first = Reduce(spot, a1, None, a1_zo, a1_zi, sem_a1, folded=True)
    for number in (3, 2, 1):
        first.launch(number)
    kv_grad.last(kv_sum)
    gkv[:, :, 0:half] = (
        turn(kv_sum[:, 0:half], cosine, -sine).astype(BF).reshape(2, rows, half)
    )
    gkv[:, :, half:width] = kv_sum[:, half:width].astype(BF).reshape(2, rows, half)
    kv_w = Gather(spot, gkv, lambda w: gkv4.at[w], sems)
    flat = gkv[...].reshape(2 * rows, width)
    grad_normed = grad_normed + nt(flat[:, 0:half], w_half[1]) + nt(flat[:, half:width], w_half[2])
    gn_send[...] = grad_normed.astype(BF).reshape(2, rows, width)
    normed_grad_x = aside(gn_send.at[1 - spot.x], gn_land)
    ring3.step(3, only=1)
    first.relay(3)
    first.relay(2)
    first.relay(1)
    ring3.step(2, only=0)
    normed_grad_x.wait_recv()
    grad_normed = gn_send[spot.x].astype(F32) + gn_land[...].astype(F32)
    inputs = tok[...].astype(F32)
    scale = lax.rsqrt(jnp.mean(inputs * inputs, axis=-1, keepdims=True) + EPS)
    weighted = grad_normed * pack_ref[0:1]
    mean = jnp.mean(weighted * inputs, axis=-1, keepdims=True)
    grad_input_out[...] = (
        grad_second + scale * weighted - inputs * (scale * scale * scale * mean)
    )
    gain_grad = jnp.sum(grad_normed * inputs * scale, axis=0, keepdims=True)
    pk[...] = jnp.concatenate([gain_grad, pack_grad_ref[1:16]], axis=0).astype(BF)
    pack_w = Gather(spot, pk, lambda w: pk4.at[w], sems)
    send_across(give_ref.at[2], other_out.at[2])
    first.last(a1_sum)
    r1[spot.k] = a1_sum[...].astype(BF)
    ring1 = Ring(spot, r1, ring_recv.at[0], ring_send.at[0])
    ring1.start()
    kv_w.forward()
    pack_w.forward()
    pack_w.finish()
    pk_sum[...] = sum(pk4[w].astype(F32) for w in range(4)).astype(BF)
    pack_x = aside(pk_sum, pk_land)
    kv_w.finish()
    both = weight_grad(gkv4).astype(BF)
    pack_x.wait_recv()
    extra = (pk_sum[...].astype(F32) + pk_land[...].astype(F32)).astype(BF)
    for plane in range(4):
        a2[plane, 0:size] = both[size * plane : size * (plane + 1)]
        a2[plane, size : size + 16] = extra
    second = Reduce(spot, a2, None, a2_zo, a2_zi, sem_a2, folded=True)
    for number in (3, 2, 1):
        second.launch(number)
    ring3.step(3, only=0)
    ring1.step(1)
    ring1.step(2, only=1)
    second.relay(3)
    second.relay(2)
    second.relay(1)
    ring1.step(3, only=1)
    ring1.step(2, only=0)
    second.last(a2_sum)
    r2[spot.k] = a2_sum[0:size].astype(BF)
    ring2 = Ring(spot, r2, ring_recv.at[1], ring_send.at[1])
    ring2.start()
    pack_out[...] = a2_sum[size : size + 16]
    ring1.step(3, only=0)
    for number in (1, 2, 3):
        ring2.step(number)
    saves = []
    for ring, src, dst in ((ring3, r3, sh_out), (ring1, r1, att1_out), (ring2, r2, att2_out)):
        for number in range(4):
            ring.other(number)
        saves.append(pltpu.make_async_copy(src, dst, sems.new()))
        saves[-1].start()
    for copy in across:
        copy.wait_recv()
    for copy in across + asides:
        copy.wait_send()
    for part_w in (grads_w, normed_w, mixed_w, query_w, shared_w, kv_w, pack_w):
        part_w.drain()
    for part_w in (shared, kv_grad, first, second, ring1, ring2, ring3):
        part_w.drain()
    for copy in saves + loads[6:]:
        copy.wait()


def run_backward(
    grad_second, tok, pack, pack_grad, normed, mixed, qc, lse, cosr, sinr, kb, qb, dsh, kv, wfull,
    give, other,
):
    rows, width = tok.shape
    pairs = width // PAIR
    half = width // 2
    ranks = 8
    shard, hidden = width // 4, give.shape[2]
    size = shard // 4
    tall = dsh.shape[1]
    any_, vm = pl.BlockSpec(memory_space=pl.ANY), pl.BlockSpec(memory_space=VMEM)
    shape = jax.ShapeDtypeStruct

    def low(*dims):
        return VMEM(dims, BF)

    def full(*dims):
        return VMEM(dims, F32)

    dma = pltpu.SemaphoreType.DMA
    return pl.pallas_call(
        backward_kernel,
        out_shape=(
            shape((rows, width), F32),
            shape(pack.shape, F32),
            shape((ranks, size, width), BF),
            shape((ranks, size, width), BF),
            shape((ranks, tall, 128), BF),
            shape((3, shard, hidden), BF),
        ),
        in_specs=[vm] * 12 + [any_] * 5,
        out_specs=(vm, vm, any_, any_, any_, any_),
        scratch_shapes=[
            low(width, width),
            low(3, width, half),
            low(ranks, rows, width),
            low(4, 2 * rows, width),
            low(4, 2 * rows, width),
            low(4, 2 * rows, width),
            full(2 * rows, width),
            low(rows, half),
            low(2, rows, half),
            low(rows, half),
            low(pairs, 2 * rows, PAIR),
            low(pairs, 2 * rows, PAIR),
            full(pairs, 2 * rows, PAIR),
            full(pairs, 2 * rows, PAIR),
            full(pairs, 2 * rows, PAIR),
            full(8, 2 * rows),
            full(8, 2 * rows),
            full(pairs, 2 * rows, PAIR),
            low(rows, width),
            low(4, rows, width),
            low(2, rows, half),
            low(4, 2, rows, half),
            low(2, rows, width),
            low(4, 2, rows, width),
            low(width, rows),
            low(width, rows),
            low(2, shard, 4 * rows),
            low(shard, 4 * rows),
            low(16, width),
            low(4, 16, width),
            low(16, width),
            low(16, width),
            low(2, shard, half),
            low(shard, half),
            low(2, rows, width),
            low(rows, width),
            low(4, size, width),
            low(4, size, width),
            low(4, size, width),
            full(size, width),
            low(4, size + 16, width),
            low(4, size + 16, width),
            low(4, size + 16, width),
            full(size + 16, width),
            low(ranks, size, width),
            low(ranks, size, width),
            low(4, tall, 128),
            low(4, tall, 128),
            full(tall, 128),
            low(tall, 128),
            low(ranks, tall, 128),
            dma((128,)),
            dma((5, 8)),
            dma((5, 8)),
            dma((5, 8)),
            dma((5, 8)),
            dma((3, 2 * ranks)),
            dma((3, 32)),
        ],
        compiler_params=pltpu.CompilerParams(
            collective_id=3, has_side_effects=True, vmem_limit_bytes=VMEM_BYTES
        ),
    )(
        grad_second, tok, pack, pack_grad, normed, mixed, qc, lse, cosr, sinr, kb, qb, dsh, kv,
        wfull, give, other,
    )


def unpack_kernel(
    result, grad_input, pack, att1, att2, sh, keep, other,
    result_out, grad_input_out, gain_one, gain_two, router,
    query, key, value, output, gate, up, down, eg, eu, ed,
):
    i = pl.program_id(0)
    result_out[...] = result[...]
    grad_input_out[...] = grad_input[...]
    half = query.shape[1] // 2
    for x in range(2):
        lanes = slice(half * x, half * (x + 1))
        for ref, src, low in ((output, att1, 0), (query, att1, 1), (key, att2, 0), (value, att2, 1)):
            ref[:, lanes] = src[0, x, :, half * low : half * (low + 1)].astype(F32)
    for a, ref in enumerate((eg, eu, ed)):
        ref[...] = keep[a].astype(F32) + other[a].astype(F32)
    size = gate.shape[0]
    shard = 4 * size
    width = 4 * shard
    row, within = lax.div(i, 2), lax.rem(i, 2) * size
    for c in range(4):
        for w in range(4):
            lanes = slice(512 * w + 128 * c, 512 * w + 128 * (c + 1))
            start = pl.multiple_of(shard * w + within, 16)
            gate[:, lanes] = sh[4 * row + c, pl.ds(start, size)].astype(F32)
            start = pl.multiple_of(shard * w + shard // 2 + within, 16)
            up[:, lanes] = sh[4 * row + c, pl.ds(start, size)].astype(F32)
    deep = down.shape[0] // 2
    for r in range(2):
        for t in range(width // 128):
            at = slice(width + deep * t, width + deep * (t + 1))
            down[deep * r : deep * (r + 1), 128 * t : 128 * (t + 1)] = sh[2 * i + r, at].astype(F32)

    @pl.when(i == 0)
    def _():
        back = lax.rem(4 - lax.axis_index("wt"), 4) * shard
        mine = pltpu.roll(pack[...], back, 1)[:, 0:256]
        gain_one[...] = mine[0:1, 0:shard]
        gain_two[...] = mine[1:2, 0:shard]
        router[...] = mine[2 : 2 + router.shape[0], 0:shard]


def run_unpack(result, grad_input, pack, att1, att2, sh, keep, other, experts):
    rows, width = result.shape
    shard, hidden = keep.shape[1:]
    steps = 4
    shape = jax.ShapeDtypeStruct
    size = shard // steps
    att1 = att1.reshape(4, 2, size, width)
    att2 = att2.reshape(4, 2, size, width)
    shared_hidden = sh.shape[0] * (sh.shape[1] - width) * 128 // width
    shared = 4 * shared_hidden
    by_rows = lambda r, c: pl.BlockSpec((r, c), lambda i: (i, 0))
    whole = lambda *dims: pl.BlockSpec(dims, lambda i: (0,) * len(dims))
    stack = lambda n, r, c: pl.BlockSpec((n, r, c), lambda i: (0, i, 0))
    att = pl.BlockSpec((1, 2, size, width), lambda i: (i, 0, 0, 0))
    return pl.pallas_call(
        unpack_kernel,
        grid=(steps,),
        out_shape=(
            shape((rows, width), BF),
            shape((rows, width), F32),
            shape((1, shard), F32),
            shape((1, shard), F32),
            shape((experts, shard), F32),
            *[shape((shard, width), F32)] * 4,
            *[shape((shard, shared), F32)] * 2,
            shape((shared_hidden, width), F32),
            *[shape((shard, hidden), F32)] * 3,
        ),
        in_specs=[
            by_rows(rows // steps, width),
            by_rows(rows // steps, width),
            whole(*pack.shape),
            att,
            att,
            whole(*sh.shape),
            stack(3, size, hidden),
            stack(3, size, hidden),
        ],
        out_specs=(
            by_rows(rows // steps, width),
            by_rows(rows // steps, width),
            whole(1, shard),
            whole(1, shard),
            whole(experts, shard),
            *[by_rows(size, width)] * 4,
            *[by_rows(size, shared)] * 2,
            by_rows(shared_hidden // steps, width),
            *[by_rows(size, hidden)] * 3,
        ),
        compiler_params=pltpu.CompilerParams(vmem_limit_bytes=VMEM_BYTES),
    )(result, grad_input, pack, att1, att2, sh, keep, other)


def contract_product(left, right, left_dim, right_dim):
    return lax.dot_general(
        left, right, (((left_dim,), (right_dim,)), ((), ())), preferred_element_type=jnp.float32
    )


def contract_exact(left, right, left_dim, right_dim):
    return lax.dot_general(
        left,
        right,
        (((left_dim,), (right_dim,)), ((), ())),
        precision=HIGH,
        preferred_element_type=jnp.float32,
    )


def rms_norm(values, gain):
    norm_scale = lax.rsqrt(jnp.mean(values * values, axis=-1, keepdims=True) + EPS)
    return (values * norm_scale * gain, norm_scale)


def rms_back(values, norm_scale, gain, upstream):
    weighted = upstream * gain
    inner_mean = jnp.mean(weighted * values, axis=-1, keepdims=True)
    through = norm_scale * weighted - values * norm_scale * norm_scale * norm_scale * inner_mean
    return (through, jnp.sum(upstream * values * norm_scale, axis=0))


def silu_parts(gate_part):
    sigmoid = jax.nn.sigmoid(gate_part)
    return (gate_part * sigmoid, sigmoid * (1.0 + gate_part * (1.0 - sigmoid)))


def rotate(values, place, sign):
    half_size = HD // 2
    frequency = 10000.0 ** (-jnp.arange(half_size, dtype=jnp.float32) / half_size)
    angles = place.astype(jnp.float32)[:, None] * frequency[None, :]
    cosine = jnp.cos(angles)[:, None, :]
    sine_part = sign * jnp.sin(angles)[:, None, :]
    shaped = values.reshape(values.shape[0], values.shape[1] // HD, 2, half_size)
    first_half = shaped[:, :, 0, :]
    second_half = shaped[:, :, 1, :]
    turned = jnp.stack(
        [
            first_half * cosine - second_half * sine_part,
            second_half * cosine + first_half * sine_part,
        ],
        axis=2,
    )
    return turned.reshape(values.shape)


def places(first_row, row_count, block_deal, rows_dev):
    row_index = first_row + jnp.arange(row_count, dtype=jnp.int32)
    owner_rank = row_index // rows_dev
    inner_row = row_index % rows_dev
    ranks = block_deal.shape[0]
    matches = owner_rank[:, None] == jnp.arange(ranks, dtype=jnp.int32)[None, :]
    paired = jnp.sum(jnp.where(matches, block_deal[None, :], 0), axis=1)
    piece_size = rows_dev // 2
    unit_index = jnp.where(inner_row < piece_size, paired, 2 * ranks - 1 - paired)
    return unit_index * piece_size + inner_row % piece_size


def score_block(query_side, key_rows, key_place):
    query3, query_block = query_side
    key3 = key_rows.reshape(key_rows.shape[0], -1, HD)
    raw_scores = jnp.einsum("qhd,khd->hqk", query3, key3, preferred_element_type=jnp.float32)
    allowed = (key_place // BLK)[None, None, :] <= query_block[None, :, None]
    return (jnp.where(allowed, raw_scores * HD ** (-0.5), MASKED), allowed)


def absorb(running, key_rows, value_rows, key_place, query_side):
    largest, denom, accum = running
    scores, allowed = score_block(query_side, key_rows, key_place)
    new_largest = jnp.maximum(largest, jnp.max(scores, axis=2))
    factor = jnp.exp(largest - new_largest)
    raised = jnp.where(allowed, jnp.exp(scores - new_largest[:, :, None]), 0.0)
    denom = denom * factor + jnp.sum(raised, axis=2)
    value3 = value_rows.reshape(value_rows.shape[0], -1, HD)
    accum = accum * factor.T[:, :, None] + jnp.einsum(
        "hqk,khd->qhd", raised.astype(jnp.bfloat16), value3, preferred_element_type=jnp.float32
    )
    return (new_largest, denom, accum)


def fold_keys(running, key_piece, query_side, block_deal, rows_dev):
    key_all, value_all = key_piece
    row_count = key_all.shape[0]
    block_size = KEY_ROWS

    def key_step(current, offset):
        key_rows = lax.dynamic_slice_in_dim(key_all, offset, block_size, 0)
        value_rows = lax.dynamic_slice_in_dim(value_all, offset, block_size, 0)
        key_place = places(offset, block_size, block_deal, rows_dev)
        return (absorb(current, key_rows, value_rows, key_place, query_side), None)

    offsets = jnp.arange(row_count // block_size, dtype=jnp.int32) * block_size
    running, unused = lax.scan(key_step, running, offsets)
    return running


def differentiate(query_side, log_total, delta, grad_out3, key_rows, value_rows, key_place):
    scores, allowed = score_block(query_side, key_rows, key_place)
    probs_full = jnp.where(allowed, jnp.exp(scores - log_total[:, :, None]), 0.0)
    value3 = value_rows.reshape(value_rows.shape[0], -1, HD)
    grad_probs = jnp.einsum("qhd,khd->hqk", grad_out3, value3, preferred_element_type=jnp.float32)
    grad_scores = (probs_full * (grad_probs - delta[:, :, None]) * HD ** (-0.5)).astype(
        jnp.bfloat16
    )
    return (probs_full, grad_scores)


def assign_slots(route, order, experts, capacity):
    pair_count = order.shape[0]
    expert_ids = route.reshape(pair_count)
    ordered = expert_ids[order]
    onehot = (ordered[:, None] == jnp.arange(experts, dtype=jnp.int32)[None, :]).astype(jnp.int32)
    before = jnp.cumsum(onehot, axis=0) - onehot
    slot_turn = jnp.sum(before * onehot, axis=1)
    slot_index = jnp.zeros((pair_count,), jnp.int32).at[order].set(slot_turn)
    kept_pairs = slot_index < capacity
    target = jnp.where(kept_pairs, expert_ids * capacity + slot_index, experts * capacity)
    slot_table = (
        jnp.full((experts * capacity,), pair_count, jnp.int32)
        .at[target]
        .set(jnp.arange(pair_count, dtype=jnp.int32), mode="drop")
    )
    return (target, kept_pairs, slot_table)


def body(
    tokens,
    cotangent,
    gain_attention,
    query_weight,
    key_weight,
    value_weight,
    output_weight,
    gain_mixer,
    router_weight,
    shared_gate,
    shared_up,
    shared_down,
    expert_gate,
    expert_up,
    expert_down,
    routes,
    slot_order,
    block_deal,
):
    rows_dev = tokens.shape[1]
    width = tokens.shape[2]
    ranks = lax.axis_size("ctx")
    (
        gain_one,
        query_full,
        key_full,
        value_full,
        output_full,
        gain_two,
        router_full,
        sgate_full,
        sup_full,
        sdown_full,
        expert_gate_whole,
        expert_up_whole,
        edown_full,
    ) = (
        lax.all_gather(gain_attention, "wt", axis=0, tiled=True),
        lax.all_gather(query_weight, "wt", axis=0, tiled=True),
        lax.all_gather(key_weight, "wt", axis=0, tiled=True),
        lax.all_gather(value_weight, "wt", axis=0, tiled=True),
        lax.all_gather(output_weight, "wt", axis=0, tiled=True),
        lax.all_gather(gain_mixer, "wt", axis=0, tiled=True),
        lax.all_gather(router_weight, "wt", axis=0, tiled=True),
        lax.all_gather(shared_gate, "wt", axis=0, tiled=True),
        lax.all_gather(shared_up, "wt", axis=0, tiled=True),
        lax.all_gather(shared_down, "wt", axis=0, tiled=True),
        lax.all_gather(expert_gate, "wt", axis=0, tiled=True),
        lax.all_gather(expert_up, "wt", axis=0, tiled=True),
        lax.all_gather(expert_down, "wt", axis=0, tiled=True),
    )
    gain_first = gain_one.astype(jnp.float32)
    gain_second = gain_two.astype(jnp.float32)
    heads = width // HD
    inputs = tokens[0].astype(jnp.float32)
    here = places(lax.axis_index("ctx") * rows_dev, rows_dev, block_deal, rows_dev)
    query_side_block = here // BLK
    normed_f, scale_one = rms_norm(inputs, gain_first)
    normed = normed_f.astype(jnp.bfloat16)
    query_rot = rotate(
        jnp.dot(normed, query_full, preferred_element_type=jnp.float32), here, 1.0
    ).astype(jnp.bfloat16)
    key_rot = rotate(
        jnp.dot(normed, key_full, preferred_element_type=jnp.float32), here, 1.0
    ).astype(jnp.bfloat16)
    value_low = jnp.dot(normed, value_full, preferred_element_type=jnp.float32).astype(jnp.bfloat16)
    query3 = query_rot.reshape(rows_dev, heads, HD)
    query_side = (query3, query_side_block)
    start_state = (
        jnp.full((heads, rows_dev), MASKED, jnp.float32),
        jnp.zeros((heads, rows_dev), jnp.float32),
        jnp.zeros((rows_dev, heads, HD), jnp.float32),
    )
    largest, denom, accum = fold_keys(
        start_state,
        (
            lax.all_gather(key_rot, "ctx", axis=0, tiled=True),
            lax.all_gather(value_low, "ctx", axis=0, tiled=True),
        ),
        query_side,
        block_deal,
        rows_dev,
    )
    mixed3 = accum / denom.T[:, :, None]
    log_total = largest + jnp.log(denom)
    mixed_low = mixed3.reshape(rows_dev, width).astype(jnp.bfloat16)
    second = inputs + jnp.dot(mixed_low, output_full, preferred_element_type=jnp.float32)
    mixer_f, scale_two = rms_norm(second, gain_second)
    mixer = mixer_f.astype(jnp.bfloat16)
    experts = router_full.shape[1]
    logits = jnp.dot(mixer, router_full, preferred_element_type=jnp.float32)
    route = routes[0]
    top_count = route.shape[1]
    pair_count = rows_dev * top_count
    capacity = (5 * pair_count + 4 * experts - 1) // (4 * experts)
    split_count = ranks // experts
    expert_match = route[:, :, None] == jnp.arange(experts, dtype=jnp.int32)[None, None, :]
    chosen = jnp.sum(jnp.where(expert_match, logits[:, None, :], 0.0), axis=2)
    gates = jax.nn.softmax(chosen, axis=1)
    target, kept_pairs, slot_table = assign_slots(route, slot_order[0, 0], experts, capacity)
    valid = slot_table < pair_count
    pair_pick = jnp.minimum(slot_table, pair_count - 1)
    target_pick = jnp.minimum(target, experts * capacity - 1)
    send_rows = jnp.where(
        valid[:, None], mixer[pair_pick // top_count], jnp.zeros((), jnp.bfloat16)
    )
    send_rows = jnp.broadcast_to(
        send_rows.reshape(experts, 1, capacity, width), (experts, split_count, capacity, width)
    ).reshape(ranks, capacity, width)
    received = lax.all_to_all(send_rows, "ctx", split_axis=0, concat_axis=0, tiled=True)
    slot_count = received.shape[1]
    flattened_input = received.reshape(ranks * slot_count, width)
    gate_part = jnp.dot(flattened_input, expert_gate_whole, preferred_element_type=jnp.float32)
    up_projection_part = jnp.dot(
        flattened_input, expert_up_whole, preferred_element_type=jnp.float32
    )
    activated, unused = silu_parts(gate_part)
    hidden = (activated * up_projection_part).astype(jnp.bfloat16)
    partial_value = contract_product(hidden, edown_full, 1, 1).reshape(ranks, slot_count, width)
    back = lax.all_to_all(
        partial_value.astype(jnp.bfloat16), "ctx", split_axis=0, concat_axis=0, tiled=True
    ).astype(partial_value.dtype)
    expert_gate_part = gate_part.reshape(ranks, slot_count, -1)
    expert_up_part = up_projection_part.reshape(ranks, slot_count, -1)
    combined = jnp.sum(back.reshape(experts, split_count, capacity, width), axis=1).reshape(
        experts * capacity, width
    )
    pair_out = jnp.where(kept_pairs[:, None], combined[target_pick], 0.0).reshape(
        rows_dev, top_count, width
    )
    mixture = jnp.sum(gates[:, :, None] * pair_out, axis=1)
    sgate_part = jnp.dot(mixer, sgate_full, preferred_element_type=jnp.float32)
    sup_part = jnp.dot(mixer, sup_full, preferred_element_type=jnp.float32)
    shared_act, shared_slope = silu_parts(sgate_part)
    shared_hidden = (shared_act * sup_part).astype(jnp.bfloat16)
    shared_out = jnp.dot(shared_hidden, sdown_full, preferred_element_type=jnp.float32)
    result = (second + mixture + shared_out).astype(jnp.bfloat16)
    grad_final = cotangent[0].astype(jnp.float32)
    grad_low = grad_final.astype(jnp.bfloat16)
    sdown_grad = contract_product(shared_hidden, grad_low, 0, 0)
    grad_shared_hidden = contract_product(grad_low, sdown_full, 1, 1)
    grad_sgate = (grad_shared_hidden * sup_part * shared_slope).astype(jnp.bfloat16)
    grad_sup = (grad_shared_hidden * shared_act).astype(jnp.bfloat16)
    sgate_grad = contract_product(mixer, grad_sgate, 0, 0)
    sup_grad = contract_product(mixer, grad_sup, 0, 0)
    grad_mixer = contract_product(grad_sgate, sgate_full, 1, 1) + contract_product(
        grad_sup, sup_full, 1, 1
    )
    pair_grad = (
        (gates[:, :, None] * grad_final[:, None, :]).reshape(pair_count, width).astype(jnp.bfloat16)
    )
    grad_gates = jnp.sum(grad_final[:, None, :] * pair_out, axis=2)
    send_grad = jnp.where(valid[:, None], pair_grad[pair_pick], jnp.zeros((), jnp.bfloat16))
    send_grad = jnp.broadcast_to(
        send_grad.reshape(experts, 1, capacity, width), (experts, split_count, capacity, width)
    ).reshape(ranks, capacity, width)
    recv_grad = lax.all_to_all(send_grad, "ctx", split_axis=0, concat_axis=0, tiled=True)
    flattened_input = received.reshape(ranks * capacity, width)
    flat_grad = recv_grad.reshape(ranks * capacity, width)
    gate_flat = expert_gate_part.reshape(ranks * capacity, -1)
    up_flat = expert_up_part.reshape(ranks * capacity, -1)
    expert_activation, expert_slope = silu_parts(gate_flat)
    expert_hidden = (expert_activation * up_flat).astype(jnp.bfloat16)
    edown_grad = contract_product(flat_grad, expert_hidden, 0, 0)
    expert_hidden_grad = jnp.dot(flat_grad, edown_full, preferred_element_type=jnp.float32)
    expert_gate_grad_rows = (expert_hidden_grad * up_flat * expert_slope).astype(jnp.bfloat16)
    expert_up_grad_rows = (expert_hidden_grad * expert_activation).astype(jnp.bfloat16)
    egate_grad = contract_product(flattened_input, expert_gate_grad_rows, 0, 0)
    expert_up_weight_grad = contract_product(flattened_input, expert_up_grad_rows, 0, 0)
    input_back = (
        contract_product(expert_gate_grad_rows, expert_gate_whole, 1, 1)
        + contract_product(expert_up_grad_rows, expert_up_whole, 1, 1)
    ).reshape(ranks, capacity, width)
    back_grad = lax.all_to_all(
        input_back.astype(jnp.bfloat16), "ctx", split_axis=0, concat_axis=0, tiled=True
    ).astype(input_back.dtype)
    merged = jnp.sum(back_grad.reshape(experts, split_count, capacity, width), axis=1).reshape(
        experts * capacity, width
    )
    pair_back = jnp.where(kept_pairs[:, None], merged[target_pick], 0.0).reshape(
        rows_dev, top_count, width
    )
    grad_mixer = grad_mixer + jnp.sum(pair_back, axis=1)
    grad_chosen = gates * (grad_gates - jnp.sum(gates * grad_gates, axis=1, keepdims=True))
    grad_logits = jnp.sum(jnp.where(expert_match, grad_chosen[:, :, None], 0.0), axis=1)
    router_grad = contract_exact(mixer.astype(jnp.float32), grad_logits, 0, 0)
    grad_mixer = grad_mixer + contract_exact(grad_logits, router_full.astype(jnp.float32), 1, 1)
    through_two, gain_two_grad = rms_back(second, scale_two, gain_second, grad_mixer)
    grad_second = grad_final + through_two
    grad_attention = grad_second.astype(jnp.bfloat16)
    output_grad = contract_product(mixed_low, grad_attention, 0, 0)
    grad_mixed = contract_product(grad_attention, output_full, 1, 1).astype(jnp.bfloat16)
    grad_out3 = grad_mixed.reshape(rows_dev, heads, HD)
    delta = jnp.sum(grad_out3.astype(jnp.float32) * mixed3, axis=2).T
    all_keys, all_values = (
        lax.all_gather(key_rot, "ctx", axis=0, tiled=True),
        lax.all_gather(value_low, "ctx", axis=0, tiled=True),
    )
    total_rows = all_keys.shape[0]
    block_size = KEY_ROWS

    def query_step(grad_sum, offset):
        key_rows = lax.dynamic_slice_in_dim(all_keys, offset, block_size, 0)
        value_rows = lax.dynamic_slice_in_dim(all_values, offset, block_size, 0)
        key_place = places(offset, block_size, block_deal, rows_dev)
        unused, grad_scores = differentiate(
            query_side, log_total, delta, grad_out3, key_rows, value_rows, key_place
        )
        key3 = key_rows.reshape(block_size, heads, HD)
        return (
            grad_sum
            + jnp.einsum("hqk,khd->qhd", grad_scores, key3, preferred_element_type=jnp.float32),
            None,
        )

    offsets = jnp.arange(total_rows // block_size, dtype=jnp.int32) * block_size
    grad_query3, unused = lax.scan(
        query_step, jnp.zeros((rows_dev, heads, HD), jnp.float32), offsets
    )
    inner_size = KEY_ROWS

    def one_part(offset):
        key_rows = lax.dynamic_slice_in_dim(all_keys, offset, inner_size, 0)
        value_rows = lax.dynamic_slice_in_dim(all_values, offset, inner_size, 0)
        key_place = places(offset, inner_size, block_deal, rows_dev)
        probs_full, grad_scores = differentiate(
            query_side, log_total, delta, grad_out3, key_rows, value_rows, key_place
        )
        grad_value_rows = jnp.einsum(
            "hqk,qhd->khd",
            probs_full.astype(jnp.bfloat16),
            grad_out3,
            preferred_element_type=jnp.float32,
        )
        grad_key_rows = jnp.einsum(
            "hqk,qhd->khd", grad_scores, query3, preferred_element_type=jnp.float32
        )
        return jnp.concatenate(
            [grad_key_rows.reshape(inner_size, width), grad_value_rows.reshape(inner_size, width)],
            axis=1,
        )

    parts = lax.map(
        one_part,
        jnp.arange(lax.axis_size("ctx") * rows_dev // inner_size, dtype=jnp.int32) * inner_size,
    )
    key_value_grad = lax.psum_scatter(
        parts.reshape(lax.axis_size("ctx") * rows_dev, 2 * width),
        "ctx",
        scatter_dimension=0,
        tiled=True,
    )
    grad_key_pre = rotate(key_value_grad[:, :width], here, -1.0).astype(jnp.bfloat16)
    grad_value_low = key_value_grad[:, width:].astype(jnp.bfloat16)
    grad_query_pre = rotate(grad_query3.reshape(rows_dev, width), here, -1.0).astype(jnp.bfloat16)
    query_grad = contract_product(normed, grad_query_pre, 0, 0)
    key_grad = contract_product(normed, grad_key_pre, 0, 0)
    value_grad = contract_product(normed, grad_value_low, 0, 0)
    grad_normed = (
        contract_product(grad_query_pre, query_full, 1, 1)
        + contract_product(grad_key_pre, key_full, 1, 1)
        + contract_product(grad_value_low, value_full, 1, 1)
    )
    through_one, gain_one_grad = rms_back(inputs, scale_one, gain_first, grad_normed)
    grad_input = grad_second + through_one
    (
        gain_one_share,
        query_share,
        key_share,
        value_share,
        output_share,
        gain_two_share,
        router_share,
        sgate_share,
        sup_share,
        sdown_share,
        egate_share,
        expert_up_portion,
        edown_share,
    ) = (
        lax.psum_scatter(
            gain_one_grad.astype(jnp.bfloat16), "wt", scatter_dimension=0, tiled=True
        ).astype(jnp.float32),
        lax.psum_scatter(
            query_grad.astype(jnp.bfloat16), "wt", scatter_dimension=0, tiled=True
        ).astype(jnp.float32),
        lax.psum_scatter(
            key_grad.astype(jnp.bfloat16), "wt", scatter_dimension=0, tiled=True
        ).astype(jnp.float32),
        lax.psum_scatter(
            value_grad.astype(jnp.bfloat16), "wt", scatter_dimension=0, tiled=True
        ).astype(jnp.float32),
        lax.psum_scatter(
            output_grad.astype(jnp.bfloat16), "wt", scatter_dimension=0, tiled=True
        ).astype(jnp.float32),
        lax.psum_scatter(
            gain_two_grad.astype(jnp.bfloat16), "wt", scatter_dimension=0, tiled=True
        ).astype(jnp.float32),
        lax.psum_scatter(
            router_grad.astype(jnp.bfloat16), "wt", scatter_dimension=0, tiled=True
        ).astype(jnp.float32),
        lax.psum_scatter(
            sgate_grad.astype(jnp.bfloat16), "wt", scatter_dimension=0, tiled=True
        ).astype(jnp.float32),
        lax.psum_scatter(
            sup_grad.astype(jnp.bfloat16), "wt", scatter_dimension=0, tiled=True
        ).astype(jnp.float32),
        lax.psum_scatter(
            sdown_grad.astype(jnp.bfloat16), "wt", scatter_dimension=0, tiled=True
        ).astype(jnp.float32),
        lax.psum_scatter(
            egate_grad.astype(jnp.bfloat16), "wt", scatter_dimension=0, tiled=True
        ).astype(jnp.float32),
        lax.psum_scatter(
            expert_up_weight_grad.astype(jnp.bfloat16), "wt", scatter_dimension=0, tiled=True
        ).astype(jnp.float32),
        lax.psum_scatter(
            edown_grad.astype(jnp.bfloat16), "wt", scatter_dimension=0, tiled=True
        ).astype(jnp.float32),
    )
    (
        gain_one_sum,
        query_sum,
        key_sum,
        value_sum,
        output_sum,
        gain_two_sum,
        router_sum,
        sgate_sum,
        sup_sum,
        sdown_sum,
    ) = lax.psum(
        (
            gain_one_share,
            query_share,
            key_share,
            value_share,
            output_share,
            gain_two_share,
            router_share,
            sgate_share,
            sup_share,
            sdown_share,
        ),
        "ctx",
    )
    return (
        result[None],
        grad_input[None],
        gain_one_sum,
        query_sum,
        key_sum,
        value_sum,
        output_sum,
        gain_two_sum,
        router_sum,
        sgate_sum,
        sup_sum,
        sdown_sum,
        egate_share,
        expert_up_portion,
        edown_share,
    )


def fast_body(
    tokens,
    cotangent,
    gain_attention,
    query_weight,
    key_weight,
    value_weight,
    output_weight,
    gain_mixer,
    router_weight,
    shared_gate,
    shared_up,
    shared_down,
    expert_gate,
    expert_up,
    expert_down,
    routes,
    slot_order,
    block_deal,
):
    half_size = HD // 2
    frequency = 10000.0 ** (-np.arange(half_size) / half_size)
    frequency = jnp.asarray(np.tile(frequency, 4)[None].astype(np.float32))
    (
        cosr, sinr, kb, qb, q_st, mixed, lse, normed, pack_all, result, grad_second, pack_grad, dsh,
        kv_all, wfull, keep, give, other,
    ) = run_forward(
        tokens[0], jnp.stack([gain_attention, gain_mixer]), router_weight.T, frequency, block_deal,
        cotangent[0], routes[0].T, slot_order[0],
        shared_down, query_weight, key_weight, value_weight, output_weight, shared_gate, shared_up,
        expert_gate, expert_up, expert_down,
    )
    grad_input, pack_sum, att1, att2, sh, other = run_backward(
        grad_second, tokens[0], pack_all, pack_grad, normed, mixed, q_st, lse, cosr, sinr, kb, qb,
        dsh, kv_all, wfull, give, other,
    )
    (
        result, grad_input, gain_one, gain_two, router, query, key, value, output, gate, up, down,
        eg, eu, ed,
    ) = run_unpack(
        result, grad_input, pack_sum, att1, att2, sh, keep, other, router_weight.shape[1]
    )
    return (
        result[None], grad_input[None], gain_one.reshape(-1), query, key, value, output,
        gain_two.reshape(-1), router.T, gate, up, down, eg, eu, ed,
    )


def solution(mesh):
    in_specs = (
        P("wt", "ctx", None),
        P("wt", "ctx", None),
        P("wt"),
        P("wt", None),
        P("wt", None),
        P("wt", None),
        P("wt", None),
        P("wt"),
        P("wt", None),
        P("wt", None),
        P("wt", None),
        P("wt", None),
        P("wt", "ctx"),
        P("wt", "ctx"),
        P("wt", "ctx"),
        P("wt", "ctx", None),
        P("wt", "ctx", None),
        P(),
    )
    out_specs = (
        P("wt", "ctx", None),
        P("wt", "ctx", None),
        P("wt"),
        P("wt", None),
        P("wt", None),
        P("wt", None),
        P("wt", None),
        P("wt"),
        P("wt", None),
        P("wt", None),
        P("wt", None),
        P("wt", None),
        P("wt", "ctx"),
        P("wt", "ctx"),
        P("wt", "ctx"),
    )
    chosen = fast_body if (mesh.shape["ctx"], mesh.shape["wt"]) == (8, 4) else body
    return jax.shard_map(chosen, mesh=mesh, in_specs=in_specs, out_specs=out_specs, check_vma=False)
```

```python
import jax
import jax.numpy as jnp
import numpy as np
from jax import lax
from jax.experimental import pallas as pl
from jax.experimental.pallas import tpu as pltpu
from jax.sharding import PartitionSpec as P

HD = 64
BLK = 256


EPS = 1e-06
KEY_ROWS = 512
HIGH = lax.Precision.HIGHEST
MASKED = -1e30


MESH = pl.DeviceIdType.MESH
VMEM = pltpu.VMEM
BF = jnp.bfloat16
F32 = jnp.float32
PAIR = 2 * HD
VMEM_BYTES = 127 * 2**19
SEMS_FORWARD = 148
SEMS_BACKWARD = 73


class Spot:
    def __init__(self, line_size):
        self.k = lax.axis_index("ctx")
        self.w = lax.axis_index("wt")
        self.z, self.x = lax.div(self.k, 2), lax.rem(self.k, 2)
        self.y, self.c = lax.div(self.w, 2), lax.rem(self.w, 2)
        self.far = lax.div(self.z, 2)
        self.mid = self.z + self.far * (3 - 2 * self.z)
        step = 1 - 2 * self.far
        self.core = (self.k, 2 * self.y + 1 - self.c)
        self.across = (self.k, 2 * (1 - self.y) + self.c)
        self.corner = (self.k, 2 * (1 - self.y) + 1 - self.c)
        self.column = (2 * self.z + 1 - self.x, self.w)
        self.odd = lax.rem(self.z, 2)
        self.line = (2 * (self.z + 1 - 2 * self.odd) + self.x, self.w)
        self.inner = (2 * (self.z + step) + self.x, self.w)
        self.outer = (2 * (self.z - step) + self.x, self.w)

    def plane(self, step):
        mirrored = (self.mid, 1 - self.mid, 2, 3)[step]
        return mirrored + self.far * (3 - 2 * mirrored)


class Sems:
    def __init__(self, ref):
        self.ref, self.used = ref, 0

    def new(self):
        self.used += 1
        return self.ref.at[self.used - 1]


def remote(src, dst, send, recv, to):
    return pltpu.make_async_remote_copy(
        src_ref=src, dst_ref=dst, send_sem=send, recv_sem=recv, device_id=to, device_id_type=MESH
    )


def greet(devices, middle=None):
    barrier = pltpu.get_barrier_semaphore()
    for to in devices:
        pl.semaphore_signal(barrier, inc=1, device_id=to, device_id_type=MESH)
    if middle is None:
        pl.semaphore_wait(barrier, len(devices))
        return

    @pl.when(middle[0] == 1)
    def _():
        pl.semaphore_signal(barrier, inc=1, device_id=middle[1], device_id_type=MESH)

    pl.semaphore_wait(barrier, len(devices) + middle[0])


class Gather:
    def __init__(self, spot, src, place, sems, local=True):
        self.spot, self.place, self.sems = spot, place, sems
        here = place(spot.w)
        self.local = pltpu.make_async_copy(src, here, sems.new()) if local else None
        self.to_core = remote(src, here, sems.new(), sems.new(), spot.core)
        self.to_across = remote(src, here, sems.new(), sems.new(), spot.across)
        self.to_across.start()
        self.to_core.start()
        if local:
            self.local.start()

    def forward(self):
        self.to_across.wait_recv()
        part = self.place(self.spot.across[1])
        self.onward = remote(part, part, self.sems.new(), self.sems.new(), self.spot.core)
        self.onward.start()

    def finish(self):
        if self.local is not None:
            self.local.wait()
        self.to_core.wait_recv()
        self.onward.wait_recv()

    def drain(self):
        for copy in (self.to_core, self.to_across, self.onward):
            copy.wait_send()


class Share:
    def __init__(self, spot, src, dst, sems, mate, bit):
        self.spot, self.dst, self.sems, self.mate, self.bit = spot, dst, sems, mate, bit
        self.rows = src.shape[0]
        self.half = self.rows // 2
        here = dst.at[pl.ds(pl.multiple_of(self.rows * spot.w, 64), self.rows)]
        half = pl.ds(pl.multiple_of(self.half * bit, 32), self.half)
        self.local = pltpu.make_async_copy(src, here, sems.new())
        self.to_core = remote(src, here, sems.new(), sems.new(), spot.core)
        self.to_across = remote(
            src.at[half], self.part(spot.w, bit), sems.new(), sems.new(), spot.across
        )
        for copy in (self.to_across, self.to_core, self.local):
            copy.start()

    def part(self, w, bit):
        return self.dst.at[pl.ds(pl.multiple_of(self.rows * w + self.half * bit, 32), self.half)]

    def forward(self):
        spot = self.spot
        self.to_across.wait_recv()
        part = self.part(spot.across[1], self.bit)
        self.aside = remote(part, part, self.sems.new(), self.sems.new(), self.mate)
        self.onward = remote(part, part, self.sems.new(), self.sems.new(), spot.core)
        self.aside.start()
        self.onward.start()

    def second(self):
        self.aside.wait_recv()
        part = self.part(self.spot.across[1], 1 - self.bit)
        self.rest = remote(part, part, self.sems.new(), self.sems.new(), self.spot.core)
        self.rest.start()

    def finish(self):
        self.local.wait()
        self.to_core.wait_recv()
        self.onward.wait_recv()
        self.rest.wait_recv()

    def drain(self):
        for copy in (self.to_core, self.to_across, self.aside, self.onward, self.rest):
            copy.wait_send()


class ShareColumns:
    def __init__(self, spot, src, dst, sems, mate, bit):
        self.spot, self.dst, self.sems, self.mate, self.bit = spot, dst, sems, mate, bit
        self.rows, self.part_cols = src.shape[0], dst.shape[1]
        self.half = self.rows // 2
        half = pl.ds(pl.multiple_of(self.half * bit, 32), self.half)

        def columns(to):
            return pl.ds(pl.multiple_of(self.part_cols * to, self.part_cols), self.part_cols)

        here = dst.at[pl.ds(pl.multiple_of(self.rows * spot.w, 64), self.rows)]
        self.halves = [
            remote(
                src.at[half, columns(to[1])],
                self.part(spot.w, bit),
                sems.new(),
                sems.new(),
                to,
            )
            for to in (spot.across, spot.corner)
        ]
        self.to_core = remote(
            src.at[:, columns(spot.core[1])], here, sems.new(), sems.new(), spot.core
        )
        self.local = pltpu.make_async_copy(src.at[:, columns(spot.w)], here, sems.new())
        for copy in self.halves + [self.to_core, self.local]:
            copy.start()

    def part(self, w, bit):
        return self.dst.at[pl.ds(pl.multiple_of(self.rows * w + self.half * bit, 32), self.half)]

    def forward(self):
        self.aside = []
        for copy, source in zip(self.halves, (self.spot.across, self.spot.corner)):
            copy.wait_recv()
            part = self.part(source[1], self.bit)
            self.aside.append(remote(part, part, self.sems.new(), self.sems.new(), self.mate))
            self.aside[-1].start()

    def finish(self):
        self.local.wait()
        self.to_core.wait_recv()
        for copy in self.aside:
            copy.wait_recv()

    def drain(self):
        for copy in self.halves + self.aside + [self.to_core]:
            copy.wait_send()


class Merge:
    def __init__(self, spot, send, land, sems):
        self.spot, self.send, self.land = spot, send, land
        self.far = remote(
            send.at[spot.corner[1]], land.at[0], sems.new(), sems.new(), spot.core
        )
        self.near = remote(send.at[spot.core[1]], land.at[1], sems.new(), sems.new(), spot.core)
        self.over = remote(
            send.at[spot.across[1]], land.at[2], sems.new(), sems.new(), spot.across
        )
        self.far.start()
        self.near.start()

    def forward(self):
        self.far.wait_recv()
        block = self.send.at[self.spot.across[1]]
        block[...] = (block[...].astype(F32) + self.land[0].astype(F32)).astype(BF)
        self.over.start()

    def finish(self):
        self.near.wait_recv()
        self.over.wait_recv()
        own = self.send[self.spot.w].astype(F32)
        return own + self.land[1].astype(F32) + self.land[2].astype(F32)

    def drain(self):
        for copy in (self.far, self.near, self.over):
            copy.wait_send()


class Spread:
    def __init__(self, spot, pick, place, sems):
        self.copies = []
        for to in (spot.across, spot.corner, spot.core):
            self.copies.append(remote(pick(to[1]), place(spot.w), sems.new(), sems.new(), to))
        self.local = pltpu.make_async_copy(pick(spot.w), place(spot.w), sems.new())
        for copy in self.copies:
            copy.start()
        self.local.start()

    def finish(self):
        for copy in self.copies:
            copy.wait_recv()
        self.local.wait()

    def drain(self):
        for copy in self.copies:
            copy.wait_send()


def nt(left, right):
    return lax.dot_general(left, right, (((1,), (1,)), ((), ())), preferred_element_type=F32)


def nn(left, right):
    return jnp.dot(left, right, preferred_element_type=F32)


def tn(left, right):
    return lax.dot_general(left, right, (((0,), (0,)), ((), ())), preferred_element_type=F32)


def turn(values, cosine, sine):
    wide = values.shape[1]
    lane = lax.broadcasted_iota(jnp.int32, values.shape, 1)
    first = lax.rem(lane, HD) < HD // 2
    swapped = jnp.where(
        first, pltpu.roll(values, wide - HD // 2, 1), pltpu.roll(values, HD // 2, 1)
    )
    copies = wide // PAIR
    cosine = jnp.concatenate([cosine] * copies, axis=1)
    sine = jnp.concatenate([sine] * copies, axis=1)
    return values * cosine + swapped * sine


def stack_pair(values):
    lane = lax.broadcasted_iota(jnp.int32, values.shape, 1)
    none = jnp.zeros_like(values)
    return jnp.concatenate(
        [jnp.where(lane < HD, values, none), jnp.where(lane < HD, none, values)], axis=0
    )


def unstack_pair(values):
    rows = values.shape[0] // 2
    lane = lax.broadcasted_iota(jnp.int32, (rows, PAIR), 1)
    return jnp.where(lane < HD, values[:rows], values[rows:])


class Ring:
    def __init__(self, spot, blocks, recv, send, parts=1, first=(0, 0)):
        self.spot, self.blocks, self.recv, self.send, self.parts = spot, blocks, recv, send, parts
        self.ranks = blocks.shape[0]
        self.first, self.used = first[0], first[1]
        self.sent, self.sent_mid, self.sent_end = [], [], []

    def piece(self, slot, part):
        rows = self.blocks.shape[1] // self.parts
        return self.blocks.at[slot, pl.ds(rows * part, rows)]

    def copy(self, slot, part, to):
        self.used += 1
        return remote(
            self.piece(slot, part),
            self.piece(slot, part),
            self.send.at[self.used - 1],
            self.recv.at[self.first + slot + self.ranks * part],
            to,
        )

    def arrived(self, slot, part):
        remote(
            self.piece(slot, part),
            self.piece(slot, part),
            self.send.at[0],
            self.recv.at[self.first + slot + self.ranks * part],
            self.spot.column,
        ).wait_recv()

    def start(self):
        spot = self.spot
        for part in range(self.parts):
            own = self.copy(spot.k, part, spot.inner)
            side = self.copy(spot.k, part, spot.column)
            back = self.copy(spot.k, part, spot.outer)
            own.start()
            self.middle(back)
            side.start()
            self.sent += [own, side]
            self.sent_mid += [back]

    def middle(self, copy):
        @pl.when(self.spot.mid == 1)
        def _():
            copy.start()

    def step(self, number, only=None):
        spot = self.spot
        slot = 2 * spot.plane(number) + spot.x
        onward = spot.inner if number == 1 else spot.outer
        pieces = []
        for part in range(self.parts):
            along = self.copy(slot, part, onward) if only != 0 else None
            pieces.append((along, self.copy(slot, part, spot.column)))
        if only != 0:

            @pl.when(spot.mid == 1)
            def _():
                for part, (along, side) in enumerate(pieces):
                    self.arrived(slot, part)
                    along.start()
                    side.start()

        if only != 1:

            @pl.when(spot.mid == 0)
            def _():
                for part, (along, side) in enumerate(pieces):
                    self.arrived(slot, part)
                    side.start()

        if only != 0:
            self.sent_mid += [along for along, _ in pieces]
            self.sent_mid += [side for _, side in pieces]
        if only != 1:
            self.sent_end += [side for _, side in pieces]

    def other(self, number):
        for part in range(self.parts):
            self.arrived(2 * self.spot.plane(number) + 1 - self.spot.x, part)

    def drain(self):
        for copy in self.sent:
            copy.wait_send()
        for role, copies in ((0, self.sent_end), (1, self.sent_mid)):

            @pl.when(self.spot.mid == role)
            def _(copies=copies):
                for copy in copies:
                    copy.wait_send()


class Reduce:
    def __init__(self, spot, part, sides, zo, zi, sems, folded=False, parts=1):
        self.spot, self.part, self.sides, self.zo, self.zi = spot, part, sides, zo, zi
        self.z_send, self.zo_recv = sems.at[0], sems.at[1]
        if folded:
            self.zi_recv = sems.at[2]
        else:
            self.x_send, self.x_recv = sems.at[2], sems.at[3]
        self.folded, self.parts = folded, parts
        self.rows = part.shape[1] // parts
        self.sent, self.sent_end, self.sent_mid = [], [], []

    def cut(self, ref, index, h):
        return ref.at[index, pl.ds(self.rows * h, self.rows)]

    def own(self, plane, h):
        return self.cut(self.part, plane if self.folded else 2 * plane + self.spot.x, h)

    def wait(self, land, recv, plane, h):
        piece = self.cut(land, plane, h)
        at = plane + 4 * h
        remote(piece, piece, self.z_send.at[at], recv.at[at], self.spot.column).wait_recv()

    def side(self, number):
        spot = self.spot
        plane = spot.plane(number)
        for h in range(self.parts):
            at = plane + 4 * h
            copy = remote(
                self.cut(self.part, 2 * plane + 1 - spot.x, h),
                self.cut(self.sides, plane, h),
                self.x_send.at[at],
                self.x_recv.at[at],
                spot.column,
            )
            copy.start()
            self.sent.append(copy)

    def add(self, ref, land):
        ref[...] = (ref[...].astype(F32) + land[...].astype(F32)).astype(BF)

    def meet(self, number, launch):
        plane = self.spot.plane(number)
        for h in range(self.parts):
            self.wait(self.sides, self.x_recv, plane, h)
            self.add(self.own(plane, h), self.cut(self.sides, plane, h))
            if launch:
                self.launch_part(number, h)

    def launch(self, number):
        for h in range(self.parts):
            self.launch_part(number, h)

    def launch_part(self, number, h):
        plane = self.spot.plane(number)
        at = plane + 4 * h
        copy = remote(
            self.own(plane, h),
            self.cut(self.zo, plane, h),
            self.z_send.at[at],
            self.zo_recv.at[at],
            self.spot.inner,
        )

        @pl.when(self.spot.mid == 0)
        def _():
            copy.start()

        self.sent_end.append(copy)

    def absorb(self, number):
        plane = self.spot.plane(number)

        @pl.when(self.spot.mid == 1)
        def _():
            for h in range(self.parts):
                self.wait(self.zo, self.zo_recv, plane, h)
                self.add(self.own(plane, h), self.cut(self.zo, plane, h))

    def relay(self, number, settled=False):
        plane = self.spot.plane(number)
        land, recv = (self.zi, self.zi_recv) if number == 1 else (self.zo, self.zo_recv)
        copies = []
        for h in range(self.parts):
            at = plane + 4 * h
            copies.append(
                remote(
                    self.own(plane, h),
                    self.cut(self.zi, plane, h),
                    self.z_send.at[at],
                    self.zi_recv.at[at],
                    self.spot.outer if number == 1 else self.spot.inner,
                )
            )

        @pl.when(self.spot.mid == 1)
        def _():
            for h, copy in enumerate(copies):
                if not settled:
                    self.wait(land, recv, plane, h)
                    self.add(self.own(plane, h), self.cut(land, plane, h))
                copy.start()

        self.sent_mid += copies

    def last(self, result):
        plane = self.spot.plane(0)
        for h in range(self.parts):
            self.wait(self.zi, self.zi_recv, plane, h)
            rows = pl.ds(self.rows * h, self.rows)
            total = self.own(plane, h)[...].astype(F32)
            result[rows] = total + self.cut(self.zi, plane, h)[...].astype(F32)

        @pl.when(self.spot.mid == 1)
        def _():
            for h in range(self.parts):
                self.wait(self.zo, self.zo_recv, plane, h)
                rows = pl.ds(self.rows * h, self.rows)
                result[rows] += self.cut(self.zo, plane, h)[...].astype(F32)

    def drain(self):
        for copy in self.sent:
            copy.wait_send()

        @pl.when(self.spot.mid == 0)
        def _():
            for copy in self.sent_end:
                copy.wait_send()

        @pl.when(self.spot.mid == 1)
        def _():
            for copy in self.sent_mid:
                copy.wait_send()


def swish(values):
    sigmoid = 1.0 / (1.0 + jnp.exp(-values))
    return values * sigmoid, sigmoid * (1.0 + values * (1.0 - sigmoid))


class Exchange:
    def __init__(self, spot, out, back, send, recv):
        self.spot, self.out, self.back = spot, out, back
        self.send, self.recv, self.ranks = send, recv, out.shape[0]
        self.copies = []

    def start(self):
        spot = self.spot
        for offset in range(1, self.ranks):
            peer = lax.rem(spot.k + offset, self.ranks)
            self.copies.append(
                remote(
                    self.out.at[peer],
                    self.back.at[spot.k],
                    self.send.at[offset],
                    self.recv.at[spot.k],
                    (peer, spot.w),
                )
            )
            self.copies[-1].start()
        self.back[spot.k] = self.out[spot.k]

    def finish(self):
        spot = self.spot
        for offset in range(1, self.ranks):
            peer = lax.rem(spot.k + offset, self.ranks)
            remote(
                self.out.at[peer],
                self.back.at[peer],
                self.send.at[offset],
                self.recv.at[peer],
                (peer, spot.w),
            ).wait_recv()

    def drain(self):
        for copy in self.copies:
            copy.wait_send()


def fold_rows(values, ref):
    ranks = ref.shape[0]
    slots = values.shape[0] // ranks
    for e in range(ranks):
        part = values[slots * e : slots * (e + 1)]
        tiles = [part[:, 128 * t : 128 * (t + 1)] for t in range(values.shape[1] // 128)]
        ref[e] = jnp.concatenate(tiles, axis=0).astype(BF)


def unfold_rows(ref, slots):
    parts = []
    for e in range(ref.shape[0]):
        part = ref[e].astype(F32)
        tiles = [part[slots * t : slots * (t + 1)] for t in range(part.shape[0] // slots)]
        parts.append(jnp.concatenate(tiles, axis=1))
    return jnp.concatenate(parts, axis=0).astype(BF)


def split_three(values):
    high = values.astype(BF)
    rest = values - high.astype(F32)
    middle = rest.astype(BF)
    return high, middle, (rest - middle.astype(F32)).astype(BF)


def diagonal(values, axis):
    size = max(values.shape)
    down = lax.broadcasted_iota(jnp.int32, (size, size), 0)
    along = lax.broadcasted_iota(jnp.int32, (size, size), 1)
    return jnp.sum(
        jnp.where(down == along, values.astype(F32), 0.0), axis=axis, keepdims=True
    ).astype(jnp.int32)


def slot_maps(routes, order, slots, experts):
    top, rows = routes.shape
    pairs = rows * top
    lines = [routes[j : j + 1] for j in range(top)]
    e_row = jnp.concatenate(lines, axis=1)
    e_col = jnp.concatenate([diagonal(line, 1) for line in lines], axis=0)
    o_row = lax.rem(order, top) * rows + lax.div(order, top)
    o_col = diagonal(o_row, 1)
    down = lax.broadcasted_iota(jnp.int32, (pairs, pairs), 0)
    along = lax.broadcasted_iota(jnp.int32, (pairs, pairs), 1)
    turn_row = jnp.sum(jnp.where(o_col == along, down.astype(F32), 0.0), axis=0, keepdims=True)
    turn_col = jnp.sum(jnp.where(o_row == down, along.astype(F32), 0.0), axis=1, keepdims=True)
    same = e_col == e_row
    slot_row = jnp.sum(
        jnp.where(same & (turn_col < turn_row), 1.0, 0.0), axis=0, keepdims=True
    ).astype(jnp.int32)
    slot_col = jnp.sum(
        jnp.where(same & (turn_row < turn_col), 1.0, 0.0), axis=1, keepdims=True
    ).astype(jnp.int32)
    target_row = jnp.where(slot_row < slots, e_row * slots + slot_row, -1)
    target_col = jnp.where(slot_col < slots, e_col * slots + slot_col, -1)
    total = experts * slots
    place = lax.broadcasted_iota(jnp.int32, (total, pairs), 0)
    to_slots = jnp.where(place == target_row, 1.0, 0.0).astype(BF)
    place = lax.broadcasted_iota(jnp.int32, (pairs, total), 1)
    to_pairs = jnp.where(place == target_col, 1.0, 0.0).astype(BF)
    return to_slots, to_pairs


def forward_kernel(
    tok, gains, router_ref, freq, deal, cot, routes, order, sd,
    wq, wk, wv, wo, sg, su, eg, eu, ed,
    cosr, sinr, kb, qb, qx, gx, stats_out, normed_out, mixed_out, pack_out, result_out, grad_second_out, pack_grad_out,
    dsh_out, kv_out, wfull_out, keep_out, give_out, other_out,
    wbuf, kv, q_s, qc, q_land, gm, gm_land, stat, stat_land, mixed, pack, packs, top, low, acc, sg_all, su_all, wg, wu, wd, mix, m4, cot4,
    sh_send, sh_recv, gm_send, gm_recv, xs, xr, gs, gr, orr, br,
    x_s, g_s, sum_s, gate_s, up_s, hid_s, dgate_s, dup_s, dsh, dsh_x, dsh_z, slot_s, pair_s, cb,
    sem, kv_recv, kv_send, a2a_send, a2a_recv, sem_sh,
):
    spot = Spot(4)
    sems = Sems(sem)
    rows, width = tok.shape
    pairs = width // PAIR
    ranks = xs.shape[0]
    slots = xs.shape[1] * 128 // width
    hidden = wg.shape[1]
    shard = width // 4
    part = sg_all.shape[1]
    peers = [(lax.rem(spot.k + o, ranks), spot.w) for o in range(1, ranks)]
    greet([spot.core, spot.across, spot.corner] + peers)
    column, line = (spot.column, spot.x), (spot.line, spot.odd)
    key_w = Share(spot, wk, wbuf.at[1], sems, *column)
    shards = jnp.concatenate(
        [gains[...], router_ref[...], jnp.zeros((16 - 2 - router_ref.shape[0], shard), BF)], axis=0
    ).astype(F32)
    shards = jnp.concatenate([shards, jnp.zeros((16, width - shard), F32)], axis=1)
    pack[...] = pltpu.roll(shards, shard * spot.w, 1).astype(BF)
    params = Gather(spot, pack, lambda w: packs.at[w], sems)
    value_w = Share(spot, wv, wbuf.at[2], sems, *column)
    query_w = Share(spot, wq, wbuf.at[0], sems, *column)

    def stripe(ref):
        return lambda w: ref.at[pl.ds(pl.multiple_of(shard * w, 64), shard)]

    out_w = Share(spot, wo, wbuf.at[3], sems, *line)
    sg_w = ShareColumns(spot, sg, sg_all, sems, *line)
    su_w = ShareColumns(spot, su, su_all, sems, *line)
    cot_w = Gather(spot, cot, lambda w: cot4.at[w], sems)
    gate_w = Gather(spot, eg, stripe(wg), sems)
    up_w = Gather(spot, eu, stripe(wu), sems)
    inputs = tok[...].astype(F32)
    scale = lax.rsqrt(jnp.mean(inputs * inputs, axis=-1, keepdims=True) + EPS)
    scaled = inputs * scale
    piece = rows // 2
    inner = lax.broadcasted_iota(jnp.int32, (rows, 1), 0)
    lane = lax.broadcasted_iota(jnp.int32, (rows, PAIR), 1)
    sign = jnp.where(lax.rem(lane, HD) < HD // 2, -1.0, 1.0)
    for r in range(2):
        paired = deal[2 * spot.z + r]
        unit = jnp.where(inner < piece, paired, 2 * ranks - 1 - paired)
        place = unit * piece + lax.rem(inner, piece)
        qb[r] = jnp.concatenate([lax.div(place, BLK)] * 2, axis=0)
        angles = place.astype(F32) * freq[...]
        cosr[r] = jnp.cos(angles)
        sinr[r] = jnp.sin(angles) * sign
    along = lax.broadcasted_iota(jnp.int32, (1, rows), 1)
    for r in range(ranks):
        unit = jnp.where(along < piece, deal[r], 2 * ranks - 1 - deal[r])
        kb[:, rows * r : rows * (r + 1)] = lax.div(unit * piece + lax.rem(along, piece), BLK)
    key_w.forward()
    params.forward()
    params.finish()
    pack_all = (packs[0].astype(F32) + packs[1].astype(F32)) + (
        packs[2].astype(F32) + packs[3].astype(F32)
    )
    pack_out[...] = pack_all
    normed = (scaled * pack_all[0:1]).astype(BF)
    normed_out[...] = normed.T
    cosine, sine = cosr[spot.x], sinr[spot.x]
    to_slots, to_pairs = slot_maps(routes[...], order[...], slots, ranks)
    route = [diagonal(routes[j : j + 1], 1) for j in range(2)]
    slot_s[...] = to_slots
    pair_s[...] = to_pairs
    value_w.forward()
    key_w.second()
    query_w.forward()
    key_w.finish()
    kv[spot.k, :, 0:width] = turn(nn(normed, wbuf[1]), cosine, sine).astype(BF)
    value_w.second()
    value_w.finish()
    kv[spot.k, :, width : 2 * width] = nn(normed, wbuf[2]).astype(BF)
    ring = Ring(spot, kv, kv_recv, kv_send, parts=2)
    ring.start()
    query_w.second()

    query_w.finish()
    query = turn(nn(normed, wbuf[0]), cosine, sine).astype(BF) * jnp.asarray(HD**-0.5, BF)
    for j in range(pairs):
        q_s[j] = stack_pair(query[:, PAIR * j : PAIR * (j + 1)])
    for x in range(2):
        qc[x] = query[:, width // 2 * x : width // 2 * (x + 1)]
    top[...] = jnp.full_like(top, MASKED)
    low[...] = jnp.zeros_like(low)
    acc[...] = jnp.zeros_like(acc)
    q_block = qb[spot.x]

    def chunk(plane):
        k_block = kb[:, pl.ds(pl.multiple_of(2 * rows * plane, 2 * rows), 2 * rows)]
        allowed = k_block <= q_block

        def one_pair(j, carry):
            lane = pl.multiple_of(PAIR * j, PAIR)
            key = kv[pl.ds(2 * plane, 2), :, pl.ds(lane, PAIR)].reshape(2 * rows, PAIR)
            value = kv[pl.ds(2 * plane, 2), :, pl.ds(width + lane, PAIR)].reshape(2 * rows, PAIR)
            scores = jnp.where(allowed, nt(q_s[j], key), MASKED)
            old = top[j]
            new = jnp.maximum(old, jnp.max(scores, axis=1, keepdims=True))
            raised = jnp.where(allowed, jnp.exp(scores - new[:, 0:1]), 0.0)
            factor = jnp.exp(old - new)
            top[j] = new
            low[j] = low[j] * factor + jnp.sum(raised, axis=1, keepdims=True)
            acc[j] = acc[j] * factor + nn(raised.astype(BF), value)
            return carry

        lax.fori_loop(0, pairs, one_pair, 0, unroll=3)

    ring.step(1)
    ring.step(2, only=1)
    ring.other(0)
    chunk(spot.plane(0))
    ring.step(2, only=0)
    ring.step(3, only=1)
    ring.other(1)
    chunk(spot.plane(1))
    ring.step(3, only=0)
    out_w.forward()
    sg_w.forward()
    su_w.forward()
    ring.other(2)
    chunk(spot.plane(2))
    out_w.second()
    cot_w.forward()
    ring.other(3)
    chunk(spot.plane(3))
    saves = [pltpu.make_async_copy(kv, kv_out, sems.new())]
    saves[0].start()
    for j in range(pairs):
        mixed[:, PAIR * j : PAIR * (j + 1)] = unstack_pair(acc[j] / low[j])
        top[j] = top[j] + jnp.log(low[j])
    asides = []

    def aside(src, dst):
        asides.append(remote(src, dst, sems.new(), sems.new(), spot.column))
        asides[-1].start()
        return asides[-1]

    out_w.finish()
    saves.append(pltpu.make_async_copy(wbuf, wfull_out, sems.new()))
    saves[1].start()
    second = inputs + nn(mixed[...].astype(BF), wbuf[3])
    scale = lax.rsqrt(jnp.mean(second * second, axis=-1, keepdims=True) + EPS)
    mixer = (second * scale * pack_all[1:2]).astype(BF)
    mix[...] = mixer

    mixers = Gather(spot, mix, lambda w: m4.at[w], sems)
    down_w = Gather(spot, ed, stripe(wd), sems)
    fold_rows(nn(slot_s[:, :rows] + slot_s[:, rows:], mixer), xs)
    rows_out = Exchange(spot, xs, xr, a2a_send.at[0], a2a_recv.at[0])
    rows_out.start()
    router = pack_all[2:16].astype(BF)
    router = jnp.concatenate([router, jnp.zeros((2, width), BF)], axis=0)
    logits = nt(mixer, router)
    lane = lax.broadcasted_iota(jnp.int32, logits.shape, 1)
    matches = [lane == route[j] for j in range(2)]
    chosen = [jnp.sum(jnp.where(m, logits, 0.0), axis=1, keepdims=True) for m in matches]
    largest = jnp.maximum(chosen[0], chosen[1])
    raised = [jnp.exp(c - largest) for c in chosen]
    gates = [r / (raised[0] + raised[1]) for r in raised]
    grad = cot[...].astype(F32)
    pair_grad = jnp.concatenate([(g * grad).astype(BF) for g in gates], axis=0)
    fold_rows(nn(slot_s[...], pair_grad), gs)
    grads_out = Exchange(spot, gs, gr, a2a_send.at[1], a2a_recv.at[1])
    grads_out.start()
    gate_w.forward()
    up_w.forward()
    mixers.forward()

    for part_w in (sg_w, su_w, cot_w, mixers):
        part_w.finish()
    rows_all = m4[...].reshape(4 * rows, width)
    grad_all = cot4[...].reshape(4 * rows, width)
    gate_part, up_part = nn(rows_all, sg_all[...]), nn(rows_all, su_all[...])
    act, slope = swish(gate_part)
    shared_hidden = (act * up_part).astype(BF)
    sh_send[...] = nn(shared_hidden, sd[...]).astype(BF).reshape(4, rows, width)
    mixed_out[...] = mixed[...].astype(BF).T
    query_x = aside(qc.at[1 - spot.x], q_land)
    shared_out = Merge(spot, sh_send, sh_recv, sems)
    hid_grad = nt(grad_all, sd[...])
    grad_gate = (hid_grad * up_part * slope).astype(BF)
    grad_up = (hid_grad * act).astype(BF)
    back = nt(grad_gate, sg_all[...]) + nt(grad_up, su_all[...])
    gm_send[...] = back.astype(BF).reshape(4, rows, width)
    shared_out.forward()
    shared_back = Merge(spot, gm_send, gm_recv, sems)
    half = shard // 2
    for at, values in ((0, tn(rows_all, grad_gate)), (half, tn(rows_all, grad_up))):
        values = values.astype(BF)
        for r in range(ranks):
            down, left = half * (r // 4), 128 * (r % 4)
            for w in range(4):
                dsh[r, shard * w + at : shard * w + at + half] = values[
                    shard * w + down : shard * w + down + half, left : left + 128
                ]
    values = tn(shared_hidden, grad_all).astype(BF)
    deep = values.shape[0] // ranks
    for r in range(ranks):
        for t in range(width // 128):
            dsh[r, width + deep * t : width + deep * (t + 1)] = values[
                deep * r : deep * (r + 1), 128 * t : 128 * (t + 1)
            ]
    shared_back.forward()
    shared_grad = Reduce(spot, dsh, dsh_x, dsh_z, None, sem_sh)
    for number in (3, 2, 1, 0):
        shared_grad.side(number)

    for part_w in (gate_w, up_w):
        part_w.finish()
    rows_out.finish()
    x_s[...] = unfold_rows(xr, slots)
    block = 512

    def parts(i):
        return pl.ds(pl.multiple_of(block * i, block), block)

    def up_step(i, carry):
        at = parts(i)
        gate = nn(x_s[...], wg[:, at])
        up = nn(x_s[...], wu[:, at])
        act, slope = swish(gate)
        hid_s[:, at] = (act * up).astype(BF)
        gate_s[:, at] = up * slope
        up_s[:, at] = act
        return carry

    lax.fori_loop(0, hidden // block, up_step, 0)
    down_w.forward()
    down_w.finish()
    shared_grad.meet(3, True)
    sum_s[...] = nt(hid_s[...], wd[...])
    rows_out.drain()
    fold_rows(sum_s[...], xs)
    outs = Exchange(spot, xs, orr, a2a_send.at[2], a2a_recv.at[2])
    outs.start()
    grads_out.finish()
    g_s[...] = unfold_rows(gr, slots)

    def down_step(i, carry):
        at = parts(i)
        grad_hidden = nn(g_s[...], wd[:, at])
        dgate_s[:, at] = (grad_hidden * gate_s[:, at]).astype(BF)
        dup_s[:, at] = (grad_hidden * up_s[:, at]).astype(BF)
        return carry

    lax.fori_loop(0, hidden // block, down_step, 0)
    sum_s[...] = nt(dgate_s[...], wg[...]) + nt(dup_s[...], wu[...])
    grads_out.drain()
    fold_rows(sum_s[...], gs)
    backs = Exchange(spot, gs, br, a2a_send.at[3], a2a_recv.at[3])
    backs.start()

    for part_w in (gate_w, up_w, down_w):
        part_w.drain()
    swaps, across = [], []
    first = 2 * shard // 3
    sources = ((wg, x_s, dgate_s), (wu, x_s, dup_s), (wd, g_s, hid_s))

    def grads_of(a):
        ref, left, right = sources[a]

        def grad_step(i, carry):
            at = parts(i)
            ref[:, at] = tn(left[...], right[:, at]).astype(BF)
            return carry

        lax.fori_loop(0, hidden // block, grad_step, 0)
        for row in range(2):
            src = ref.at[pl.ds(pl.multiple_of(shard * (2 * row + 1 - spot.c), 64), shard)]
            swaps.append(remote(src, cb.at[a, row], sems.new(), sems.new(), spot.core))
            swaps[-1].start()

    def add_mate(a):
        ref = sources[a][0]
        for row in range(2):
            swaps[2 * a + row].wait_recv()

        def add(i, carry):
            for row in range(2):
                at = pl.ds(pl.multiple_of(shard * (2 * row + spot.c) + 16 * i, 16), 16)
                mate = cb[a, row, pl.ds(pl.multiple_of(16 * i, 16), 16)].astype(F32)
                ref[at] = (ref[at].astype(F32) + mate).astype(BF)
            return carry

        lax.fori_loop(0, shard // 16, add, 0)
        start = pl.multiple_of(shard * spot.across[1], 64)
        keep = ref.at[pl.ds(pl.multiple_of(shard * spot.w, 64), shard)]
        saves.append(pltpu.make_async_copy(keep, keep_out.at[a], sems.new()))
        if a == 0:
            across.append(
                remote(ref.at[pl.ds(start, first)], other_out, sems.new(), sems.new(), spot.across)
            )
            across[-1].start()
            give = ref.at[pl.ds(pl.multiple_of(start + first, 64), shard - first)]
            saves.append(
                pltpu.make_async_copy(give, give_out.at[0, pl.ds(first, shard - first)], sems.new())
            )
        else:
            give = ref.at[pl.ds(start, shard)]
            saves.append(pltpu.make_async_copy(give, give_out.at[a], sems.new()))
        for copy in saves[-2:]:
            copy.start()

    shared_grad.meet(2, True)
    grads_of(0)
    grads_of(1)
    add_mate(0)
    shared_grad.meet(1, False)
    grads_of(2)
    add_mate(1)
    add_mate(2)
    shared_grad.meet(0, False)
    total = second + shared_out.finish()
    grad_mixer = shared_back.finish()
    outs.finish()
    pair_out = nn(pair_s[...], unfold_rows(orr, slots))
    pair_out = [pair_out[:rows], pair_out[rows:]]
    result_out[...] = (total + gates[0] * pair_out[0] + gates[1] * pair_out[1]).astype(BF)
    grad_gates = [jnp.sum(grad * p, axis=1, keepdims=True) for p in pair_out]
    inner = gates[0] * grad_gates[0] + gates[1] * grad_gates[1]
    grad_logits = jnp.zeros_like(logits)
    for j in range(2):
        grad_logits += jnp.where(matches[j], gates[j] * (grad_gates[j] - inner), 0.0)
    pieces = split_three(grad_logits)
    router_grad = sum(tn(piece, mixer) for piece in pieces)
    grad_mixer = grad_mixer + sum(nn(piece, router) for piece in pieces)
    backs.finish()
    grad_mixer = grad_mixer + nn(pair_s[:rows] + pair_s[rows:], unfold_rows(br, slots))
    weighted = grad_mixer * pack_all[1:2]
    mean = jnp.mean(weighted * second, axis=-1, keepdims=True)
    grad_second = grad + scale * weighted - second * (scale * scale * scale * mean)
    grad_second_out[...] = grad_second

    grad_mixed = nt(grad_second.astype(BF), wbuf[3]).astype(BF)
    half = width // 2
    group = half // PAIR
    for x in range(2):
        gm[x] = grad_mixed[:, half * x : half * (x + 1)]
    grads_x = aside(gm.at[1 - spot.x], gm_land)
    product = grad_mixed.astype(F32) * mixed[...]
    lane = lax.broadcasted_iota(jnp.int32, (2 * rows, PAIR), 1)
    mine = jnp.zeros((2 * rows, PAIR), F32)
    theirs = jnp.zeros((2 * rows, PAIR), F32)
    for i in range(group):
        delta = [
            jnp.sum(stack_pair(product[:, PAIR * j : PAIR * (j + 1)]), axis=1, keepdims=True)
            for j in (i, group + i)
        ]
        swap = spot.x == 1
        mine = jnp.where(lane == i, top[group * spot.x + i], mine)
        theirs = jnp.where(lane == i, top[group * (1 - spot.x) + i], theirs)
        mine = jnp.where(lane == group + i, jnp.where(swap, delta[1], delta[0]), mine)
        theirs = jnp.where(lane == group + i, jnp.where(swap, delta[0], delta[1]), theirs)
        qx[i] = stack_pair(qc[spot.x, :, PAIR * i : PAIR * (i + 1)])
        gx[i] = stack_pair(gm[spot.x, :, PAIR * i : PAIR * (i + 1)])
    stat[...] = theirs.T[0:8]
    stat_x = aside(stat, stat_land)
    stats_out[0] = mine
    gain_grad = jnp.sum(grad_mixer * second * scale, axis=0, keepdims=True)
    pack_grad_out[...] = jnp.concatenate(
        [jnp.zeros_like(gain_grad), gain_grad, router_grad[:14]], axis=0
    )
    query_x.wait_recv()
    grads_x.wait_recv()
    for i in range(group):
        qx[group + i] = stack_pair(q_land[:, PAIR * i : PAIR * (i + 1)])
        gx[group + i] = stack_pair(gm_land[:, PAIR * i : PAIR * (i + 1)])
    stat_x.wait_recv()
    stats_out[1] = jnp.concatenate(
        [stat_land[...], jnp.zeros((PAIR - 8, 2 * rows), F32)], axis=0
    ).T
    for number in (3, 2):
        shared_grad.absorb(number)
    for plane in range(4):
        dsh_out[plane] = dsh[2 * plane + spot.x]
    for copy in across:
        copy.wait_recv()
    for part_w in (params, key_w, value_w, query_w, out_w, sg_w, su_w, cot_w, ring, mixers):
        part_w.drain()
    for part_w in (outs, backs, shared_out, shared_back, shared_grad):
        part_w.drain()
    for copy in swaps + across + asides:
        copy.wait_send()
    for copy in saves:
        copy.wait()


def run_forward(
    tok, gains, router, freq, deal, cot, routes, order, sd,
    wq, wk, wv, wo, sg, su, eg, eu, ed,
):
    rows, width = tok.shape
    pairs = width // PAIR
    ranks, slots = 8, 40
    hidden = eg.shape[1]
    part = sg.shape[1] // 4
    shard = width // 4
    total = ranks * slots
    tall = width + part * width // (128 * ranks)
    any_, vm = pl.BlockSpec(memory_space=pl.ANY), pl.BlockSpec(memory_space=VMEM)
    shape = jax.ShapeDtypeStruct

    def low(*dims):
        return VMEM(dims, BF)

    def full(*dims):
        return VMEM(dims, F32)

    dma = pltpu.SemaphoreType.DMA
    folded = low(ranks, slots * width // 128, 128)
    return pl.pallas_call(
        forward_kernel,
        out_shape=(
            shape((2, rows, PAIR), F32),
            shape((2, rows, PAIR), F32),
            shape((1, ranks * rows), jnp.int32),
            shape((2, 2 * rows, 1), jnp.int32),
            shape((pairs, 2 * rows, PAIR), BF),
            shape((pairs, 2 * rows, PAIR), BF),
            shape((2, 2 * rows, PAIR), F32),
            shape((width, rows), BF),
            shape((width, rows), BF),
            shape((16, width), F32),
            shape((rows, width), BF),
            shape((rows, width), F32),
            shape((16, width), F32),
            shape((4, tall, 128), BF),
            shape((ranks, rows, 2 * width), BF),
            shape((4, width, width), BF),
            shape((3, shard, hidden), BF),
            shape((3, shard, hidden), BF),
            shape((2 * shard // 3, hidden), BF),
        ),
        in_specs=[vm] * 4 + [pl.BlockSpec(memory_space=pltpu.SMEM)] + [vm] * 4 + [any_] * 9,
        out_specs=tuple([vm] * 14 + [any_] * 5),
        scratch_shapes=[
            low(4, width, width),
            low(ranks, rows, 2 * width),
            low(pairs, 2 * rows, PAIR),
            low(2, rows, width // 2),
            low(rows, width // 2),
            low(2, rows, width // 2),
            low(rows, width // 2),
            full(8, 2 * rows),
            full(8, 2 * rows),
            full(rows, width),
            low(16, width),
            low(4, 16, width),
            full(pairs, 2 * rows, PAIR),
            full(pairs, 2 * rows, PAIR),
            full(pairs, 2 * rows, PAIR),
            low(width, part),
            low(width, part),
            low(width, hidden),
            low(width, hidden),
            low(width, hidden),
            low(rows, width),
            low(4, rows, width),
            low(4, rows, width),
            low(4, rows, width),
            low(3, rows, width),
            low(4, rows, width),
            low(3, rows, width),
            *[folded] * 6,
            low(total, width),
            low(total, width),
            full(total, width),
            full(total, hidden),
            full(total, hidden),
            low(total, hidden),
            low(total, hidden),
            low(total, hidden),
            low(ranks, tall, 128),
            low(4, tall, 128),
            low(4, tall, 128),
            low(total, 2 * rows),
            low(2 * rows, total),
            low(3, 2, shard, hidden),
            dma((SEMS_FORWARD,)),
            dma((2 * ranks,)),
            dma((22,)),
            dma((4, ranks)),
            dma((4, ranks)),
            dma((4, 4)),
        ],
        compiler_params=pltpu.CompilerParams(
            collective_id=1, has_side_effects=True, vmem_limit_bytes=VMEM_BYTES
        ),
    )(
        tok, gains, router, freq, deal, cot, routes, order, sd,
        wq, wk, wv, wo, sg, su, eg, eu, ed,
    )


def backward_kernel(
    grad_second_ref, tok, pack_ref, pack_grad_ref, n_t, m_t, qx, gx, stats,
    cosr, sinr, kb, qb, dsh_ref, kv_ref, wfull_ref, give_ref, other_ref,
    grad_input_out, pack_out, att1_out, att2_out, sh_out, other_out,
    w_half, kv, kvb, kv_zo, kv_zi, kv_sum, dq, ga, ga4, gq, gq4, gkv, gkv4, n_all, m_all, pk, pk4,
    o_send, o_land, gn_send, gn_land, a1, a1_zo, a1_zi, a1_sum, a2, a2_zo, a2_zi, a2_sum, r1, r2,
    sh, sh_zo, sh_zi, sh_sum, sh_chunk, r3,
    sem, sem_kv, sem_a1, sem_a2, sem_sh, ring_recv, ring_send,
):
    spot = Spot(4)
    sems = Sems(sem)
    rows, width = tok.shape
    half = width // 2
    group = half // PAIR
    shard = width // 4
    mine = pl.ds(pl.multiple_of(half * spot.x, half), half)
    values = pl.ds(pl.multiple_of(width + half * spot.x, half), half)
    ranks = kv.shape[0]
    dsh_load = pltpu.make_async_copy(dsh_ref, sh, sems.new())
    dsh_load.start()
    loads = [
        pltpu.make_async_copy(kv_ref.at[:, :, mine], kv.at[:, :, pl.ds(0, half)], sems.new()),
        pltpu.make_async_copy(kv_ref.at[:, :, values], kv.at[:, :, pl.ds(half, half)], sems.new()),
        *[
            pltpu.make_async_copy(wfull_ref.at[i, :, mine], w_half.at[i], sems.new())
            for i in range(3)
        ],
    ]
    done = other_ref.shape[0]
    loads.append(pltpu.make_async_copy(other_ref, other_out.at[0, pl.ds(0, done)], sems.new()))
    for copy in loads:
        copy.start()

    def block(ref, w):
        return ref.at[pl.ds(pl.multiple_of(shard * w, 64), shard)]

    greet((spot.core, spot.across, spot.corner, spot.column, spot.inner), (spot.mid, spot.outer))
    asides = []

    def aside(src, dst):
        asides.append(remote(src, dst, sems.new(), sems.new(), spot.column))
        asides[-1].start()
        return asides[-1]

    grad_second = grad_second_ref[...]
    ga[...] = grad_second.astype(BF)
    grads_w = Gather(spot, ga, lambda w: ga4.at[w], sems)
    dsh_load.wait()
    shared = Reduce(spot, sh, None, sh_zo, sh_zi, sem_sh, folded=True, parts=2)
    shared.launch(1)
    shared.relay(3, settled=True)
    shared.relay(2, settled=True)

    def columns(ref):
        return lambda w: ref.at[:, pl.ds(pl.multiple_of(rows * w, 128), rows)]

    normed_w = Spread(spot, lambda w: block(n_t, w), columns(n_all.at[spot.x]), sems)
    mixed_w = Spread(spot, lambda w: block(m_t, w), columns(m_all), sems)
    across = []

    def send_across(src, dst):
        across.append(remote(src, dst, sems.new(), sems.new(), spot.across))
        across[-1].start()

    left = pl.ds(done, shard - done)
    send_across(give_ref.at[0, left], other_out.at[0, left])
    dq[...] = jnp.zeros_like(dq)
    loads[0].wait()
    loads[1].wait()

    def chunk(number):
        plane = spot.plane(number)
        k_block = kb[:, pl.ds(pl.multiple_of(2 * rows * plane, 2 * rows), 2 * rows)]
        allowed = [k_block <= qb[spot.x], k_block <= qb[1 - spot.x]]

        for i in range(group):
            lane = PAIR * i
            both = pl.ds(2 * plane, 2)
            key = kv[both, :, pl.ds(lane, PAIR)].reshape(2 * rows, PAIR)
            value = kv[both, :, pl.ds(half + lane, PAIR)].reshape(2 * rows, PAIR)
            grad_key = jnp.zeros((2 * rows, PAIR), F32)
            grad_value = jnp.zeros((2 * rows, PAIR), F32)
            for owner in range(2):
                j = group * owner + i
                stat = stats[owner]
                query, grad = qx[j], gx[j]
                raised = jnp.exp(nt(query, key) - stat[:, i : i + 1])
                probs = jnp.where(allowed[owner], raised, 0.0)
                inner = nt(grad, value) - stat[:, group + i : group + i + 1]
                grad_scores = (probs * inner * HD**-0.5).astype(BF)
                dq[j] += nn(grad_scores, key)
                grad_key += tn(grad_scores, query)
                grad_value += tn(probs.astype(BF), grad)
            kvb[plane, :, pl.ds(lane, PAIR)] = (grad_key * HD**0.5).astype(BF)
            kvb[plane, :, pl.ds(half + lane, PAIR)] = grad_value.astype(BF)

    kv_grad = Reduce(spot, kvb, None, kv_zo, kv_zi, sem_kv, folded=True, parts=2)
    chunk(3)
    kv_grad.launch(3)
    chunk(2)
    kv_grad.launch(2)
    shared.relay(1)
    chunk(1)
    kv_grad.launch(1)
    chunk(0)
    cosine, sine = cosr[...].reshape(2 * rows, PAIR), sinr[...].reshape(2 * rows, PAIR)
    for owner in range(2):
        at = spot.x if owner == 0 else 1 - spot.x
        parts = [unstack_pair(dq[group * owner + i]) for i in range(group)]
        gq[at] = turn(jnp.concatenate(parts, axis=1), cosr[at], -sinr[at]).astype(BF)
    query_w = Gather(spot, gq, lambda w: gq4.at[w], sems)
    shared.last(sh_sum)
    sh_chunk[...] = sh_sum[...].astype(BF)
    part = 2 * shard // 2

    def piece(w):
        return sh_chunk.at[pl.ds(pl.multiple_of(part * w, 64), part)]

    def place(w):
        return r3.at[spot.k, pl.ds(pl.multiple_of(part * w, 64), part)]

    shared_w = Spread(spot, piece, place, sems)
    rest = sh_chunk.shape[0] - 4 * part
    r3[spot.k, pl.ds(4 * part, rest)] = sh_chunk[pl.ds(4 * part, rest)]
    send_across(give_ref.at[1], other_out.at[1])
    kv_grad.relay(3)
    shared_w.finish()
    ring3 = Ring(spot, r3, ring_recv, ring_send, parts=2)
    ring3.start()
    normed_w.finish()
    normed_x = aside(n_all.at[spot.x], n_all.at[spot.x])
    grads_w.forward()
    mixed_w.finish()
    grads_w.finish()
    kv_grad.relay(2)
    out_grad = nn(m_all[...], ga4[...].reshape(4 * rows, width)).astype(BF)
    for x in range(2):
        o_send[x] = out_grad[:, half * x : half * (x + 1)]
    out_x = aside(o_send.at[1 - spot.x], o_land)
    kv_grad.relay(1)
    ring3.step(1, only=0)
    ring3.step(2, only=1)
    for copy in loads[2:5]:
        copy.wait()
    flat = gq[...].reshape(2 * rows, half)
    grad_normed = nt(flat, w_half[0])
    query_w.forward()
    query_w.finish()
    normed_x.wait_recv()

    def weight_grad(grads4):
        total = nn(n_all[0], grads4[:, 0].reshape(4 * rows, grads4.shape[3]))
        return total + nn(n_all[1], grads4[:, 1].reshape(4 * rows, grads4.shape[3]))

    query_grad = weight_grad(gq4).astype(BF)
    out_x.wait_recv()
    out_half = (o_send[spot.x].astype(F32) + o_land[...].astype(F32)).astype(BF)
    size = shard // 4
    for plane in range(4):
        at = slice(size * plane, size * (plane + 1))
        a1[plane, :, 0:half] = out_half[at]
        a1[plane, :, half:width] = query_grad[at]
    first = Reduce(spot, a1, None, a1_zo, a1_zi, sem_a1, folded=True)
    for number in (3, 2, 1):
        first.launch(number)
    kv_grad.last(kv_sum)
    gkv[:, :, 0:half] = (
        turn(kv_sum[:, 0:half], cosine, -sine).astype(BF).reshape(2, rows, half)
    )
    gkv[:, :, half:width] = kv_sum[:, half:width].astype(BF).reshape(2, rows, half)
    kv_w = Gather(spot, gkv, lambda w: gkv4.at[w], sems)
    flat = gkv[...].reshape(2 * rows, width)
    grad_normed = grad_normed + nt(flat[:, 0:half], w_half[1]) + nt(flat[:, half:width], w_half[2])
    gn_send[...] = grad_normed.astype(BF).reshape(2, rows, width)
    normed_grad_x = aside(gn_send.at[1 - spot.x], gn_land)
    ring3.step(1, only=1)
    ring3.step(2, only=0)
    first.relay(3)
    first.relay(2)
    first.relay(1)
    ring3.step(3, only=1)
    kv_w.forward()
    kv_w.finish()
    both = weight_grad(gkv4).astype(BF)
    for plane in range(4):
        a2[plane] = both[size * plane : size * (plane + 1)]
    second = Reduce(spot, a2, None, a2_zo, a2_zi, sem_a2, folded=True)
    for number in (3, 2, 1):
        second.launch(number)
    normed_grad_x.wait_recv()
    grad_normed = gn_send[spot.x].astype(F32) + gn_land[...].astype(F32)
    inputs = tok[...].astype(F32)
    scale = lax.rsqrt(jnp.mean(inputs * inputs, axis=-1, keepdims=True) + EPS)
    weighted = grad_normed * pack_ref[0:1]
    mean = jnp.mean(weighted * inputs, axis=-1, keepdims=True)
    grad_input_out[...] = (
        grad_second + scale * weighted - inputs * (scale * scale * scale * mean)
    )
    gain_grad = jnp.sum(grad_normed * inputs * scale, axis=0, keepdims=True)
    pk[...] = jnp.concatenate([gain_grad, pack_grad_ref[1:16]], axis=0).astype(BF)
    pack_w = Gather(spot, pk, lambda w: pk4.at[w], sems)
    send_across(give_ref.at[2], other_out.at[2])
    second.relay(3)
    first.last(a1_sum)
    r1[spot.k] = a1_sum[...].astype(BF)
    ring1 = Ring(spot, r1, ring_recv, ring_send, first=(16, 22))
    ring1.start()
    second.relay(2)
    second.relay(1)
    ring3.step(3, only=0)
    pack_w.forward()
    pack_w.finish()
    extra = sum(pk4[w].astype(F32) for w in range(4)).astype(BF)
    ring1.step(1)
    ring1.step(2, only=1)
    second.last(a2_sum)
    r2[spot.k, 0:size] = a2_sum[...].astype(BF)
    r2[spot.k, size : size + 16] = extra
    ring2 = Ring(spot, r2, ring_recv, ring_send, first=(24, 33))
    ring2.start()
    ring1.step(3, only=1)
    ring1.step(2, only=0)
    ring1.step(3, only=0)
    ring2.step(1)
    ring2.step(2)
    ring2.step(3)
    saves = []
    for ring, src, dst in ((ring3, r3, sh_out), (ring1, r1, att1_out), (ring2, r2, att2_out)):
        for number in range(4):
            ring.other(number)
        saves.append(pltpu.make_async_copy(src, dst, sems.new()))
        saves[-1].start()
    total = jnp.zeros(pk.shape, F32)
    for r in range(ranks):
        total = total + r2[r, size : size + 16].astype(F32)
    pack_out[...] = total
    for copy in across:
        copy.wait_recv()
    for copy in across + asides:
        copy.wait_send()
    for part_w in (grads_w, normed_w, mixed_w, query_w, shared_w, kv_w, pack_w):
        part_w.drain()
    for part_w in (shared, kv_grad, first, second, ring1, ring2, ring3):
        part_w.drain()
    for copy in saves + loads[5:]:
        copy.wait()


def run_backward(
    grad_second, tok, pack, pack_grad, n_t, m_t, qx, gx, stats, cosr, sinr, kb, qb, dsh, kv, wfull,
    give, other,
):
    rows, width = tok.shape
    pairs = width // PAIR
    half = width // 2
    ranks = 8
    shard, hidden = width // 4, give.shape[2]
    size = shard // 4
    tall = dsh.shape[1]
    any_, vm = pl.BlockSpec(memory_space=pl.ANY), pl.BlockSpec(memory_space=VMEM)
    shape = jax.ShapeDtypeStruct

    def low(*dims):
        return VMEM(dims, BF)

    def full(*dims):
        return VMEM(dims, F32)

    dma = pltpu.SemaphoreType.DMA
    return pl.pallas_call(
        backward_kernel,
        out_shape=(
            shape((rows, width), F32),
            shape(pack.shape, F32),
            shape((ranks, size, width), BF),
            shape((ranks, size + 16, width), BF),
            shape((ranks, tall, 128), BF),
            shape((3, shard, hidden), BF),
        ),
        in_specs=[vm] * 13 + [any_] * 5,
        out_specs=(vm, vm, any_, any_, any_, any_),
        scratch_shapes=[
            low(3, width, half),
            low(ranks, rows, width),
            low(4, 2 * rows, width),
            low(4, 2 * rows, width),
            low(4, 2 * rows, width),
            full(2 * rows, width),
            full(pairs, 2 * rows, PAIR),
            low(rows, width),
            low(4, rows, width),
            low(2, rows, half),
            low(4, 2, rows, half),
            low(2, rows, width),
            low(4, 2, rows, width),
            low(2, shard, 4 * rows),
            low(shard, 4 * rows),
            low(16, width),
            low(4, 16, width),
            low(2, shard, half),
            low(shard, half),
            low(2, rows, width),
            low(rows, width),
            low(4, size, width),
            low(4, size, width),
            low(4, size, width),
            full(size, width),
            low(4, size, width),
            low(4, size, width),
            low(4, size, width),
            full(size, width),
            low(ranks, size, width),
            low(ranks, size + 16, width),
            low(4, tall, 128),
            low(4, tall, 128),
            low(4, tall, 128),
            full(tall, 128),
            low(tall, 128),
            low(ranks, tall, 128),
            dma((SEMS_BACKWARD,)),
            dma((3, 8)),
            dma((3, 4)),
            dma((3, 4)),
            dma((3, 8)),
            dma((4 * ranks,)),
            dma((44,)),
        ],
        compiler_params=pltpu.CompilerParams(
            collective_id=3, has_side_effects=True, vmem_limit_bytes=VMEM_BYTES
        ),
    )(
        grad_second, tok, pack, pack_grad, n_t, m_t, qx, gx, stats, cosr, sinr, kb, qb, dsh, kv,
        wfull, give, other,
    )


def unpack_kernel(
    result, grad_input, pack, att1, att2, sh, keep, other,
    result_out, grad_input_out, gain_one, gain_two, router,
    query, key, value, output, gate, up, down, eg, eu, ed,
):
    i = pl.program_id(0)
    result_out[...] = result[...]
    grad_input_out[...] = grad_input[...]
    half = query.shape[1] // 2
    size = query.shape[0]
    for x in range(2):
        lanes = slice(half * x, half * (x + 1))
        for ref, src, low in ((output, att1, 0), (query, att1, 1), (key, att2, 0), (value, att2, 1)):
            ref[:, lanes] = src[0, x, 0:size, half * low : half * (low + 1)].astype(F32)
    for a, ref in enumerate((eg, eu, ed)):
        ref[...] = keep[a].astype(F32) + other[a].astype(F32)
    size = gate.shape[0]
    shard = 4 * size
    width = 4 * shard
    row, within = lax.div(i, 2), lax.rem(i, 2) * size
    for c in range(4):
        for w in range(4):
            lanes = slice(512 * w + 128 * c, 512 * w + 128 * (c + 1))
            start = pl.multiple_of(shard * w + within, 16)
            gate[:, lanes] = sh[4 * row + c, pl.ds(start, size)].astype(F32)
            start = pl.multiple_of(shard * w + shard // 2 + within, 16)
            up[:, lanes] = sh[4 * row + c, pl.ds(start, size)].astype(F32)
    deep = down.shape[0] // 2
    for r in range(2):
        for t in range(width // 128):
            at = slice(width + deep * t, width + deep * (t + 1))
            down[deep * r : deep * (r + 1), 128 * t : 128 * (t + 1)] = sh[2 * i + r, at].astype(F32)

    @pl.when(i == 0)
    def _():
        back = lax.rem(4 - lax.axis_index("wt"), 4) * shard
        mine = pltpu.roll(pack[...], back, 1)[:, 0:256]
        gain_one[...] = mine[0:1, 0:shard]
        gain_two[...] = mine[1:2, 0:shard]
        router[...] = mine[2 : 2 + router.shape[0], 0:shard]


def run_unpack(result, grad_input, pack, att1, att2, sh, keep, other, experts):
    rows, width = result.shape
    shard, hidden = keep.shape[1:]
    steps = 4
    shape = jax.ShapeDtypeStruct
    size = shard // steps
    att1 = att1.reshape(4, 2, size, width)
    att2 = att2.reshape(4, 2, size + 16, width)
    shared_hidden = sh.shape[0] * (sh.shape[1] - width) * 128 // width
    shared = 4 * shared_hidden
    by_rows = lambda r, c: pl.BlockSpec((r, c), lambda i: (i, 0))
    whole = lambda *dims: pl.BlockSpec(dims, lambda i: (0,) * len(dims))
    stack = lambda n, r, c: pl.BlockSpec((n, r, c), lambda i: (0, i, 0))
    att = lambda r: pl.BlockSpec((1, 2, r, width), lambda i: (i, 0, 0, 0))
    return pl.pallas_call(
        unpack_kernel,
        grid=(steps,),
        out_shape=(
            shape((rows, width), BF),
            shape((rows, width), F32),
            shape((1, shard), F32),
            shape((1, shard), F32),
            shape((experts, shard), F32),
            *[shape((shard, width), F32)] * 4,
            *[shape((shard, shared), F32)] * 2,
            shape((shared_hidden, width), F32),
            *[shape((shard, hidden), F32)] * 3,
        ),
        in_specs=[
            by_rows(rows // steps, width),
            by_rows(rows // steps, width),
            whole(*pack.shape),
            att(size),
            att(size + 16),
            whole(*sh.shape),
            stack(3, size, hidden),
            stack(3, size, hidden),
        ],
        out_specs=(
            by_rows(rows // steps, width),
            by_rows(rows // steps, width),
            whole(1, shard),
            whole(1, shard),
            whole(experts, shard),
            *[by_rows(size, width)] * 4,
            *[by_rows(size, shared)] * 2,
            by_rows(shared_hidden // steps, width),
            *[by_rows(size, hidden)] * 3,
        ),
        compiler_params=pltpu.CompilerParams(vmem_limit_bytes=VMEM_BYTES),
    )(result, grad_input, pack, att1, att2, sh, keep, other)


def contract_product(left, right, left_dim, right_dim):
    return lax.dot_general(
        left, right, (((left_dim,), (right_dim,)), ((), ())), preferred_element_type=jnp.float32
    )


def contract_exact(left, right, left_dim, right_dim):
    return lax.dot_general(
        left,
        right,
        (((left_dim,), (right_dim,)), ((), ())),
        precision=HIGH,
        preferred_element_type=jnp.float32,
    )


def rms_norm(values, gain):
    norm_scale = lax.rsqrt(jnp.mean(values * values, axis=-1, keepdims=True) + EPS)
    return (values * norm_scale * gain, norm_scale)


def rms_back(values, norm_scale, gain, upstream):
    weighted = upstream * gain
    inner_mean = jnp.mean(weighted * values, axis=-1, keepdims=True)
    through = norm_scale * weighted - values * norm_scale * norm_scale * norm_scale * inner_mean
    return (through, jnp.sum(upstream * values * norm_scale, axis=0))


def silu_parts(gate_part):
    sigmoid = jax.nn.sigmoid(gate_part)
    return (gate_part * sigmoid, sigmoid * (1.0 + gate_part * (1.0 - sigmoid)))


def rotate(values, place, sign):
    half_size = HD // 2
    frequency = 10000.0 ** (-jnp.arange(half_size, dtype=jnp.float32) / half_size)
    angles = place.astype(jnp.float32)[:, None] * frequency[None, :]
    cosine = jnp.cos(angles)[:, None, :]
    sine_part = sign * jnp.sin(angles)[:, None, :]
    shaped = values.reshape(values.shape[0], values.shape[1] // HD, 2, half_size)
    first_half = shaped[:, :, 0, :]
    second_half = shaped[:, :, 1, :]
    turned = jnp.stack(
        [
            first_half * cosine - second_half * sine_part,
            second_half * cosine + first_half * sine_part,
        ],
        axis=2,
    )
    return turned.reshape(values.shape)


def places(first_row, row_count, block_deal, rows_dev):
    row_index = first_row + jnp.arange(row_count, dtype=jnp.int32)
    owner_rank = row_index // rows_dev
    inner_row = row_index % rows_dev
    ranks = block_deal.shape[0]
    matches = owner_rank[:, None] == jnp.arange(ranks, dtype=jnp.int32)[None, :]
    paired = jnp.sum(jnp.where(matches, block_deal[None, :], 0), axis=1)
    piece_size = rows_dev // 2
    unit_index = jnp.where(inner_row < piece_size, paired, 2 * ranks - 1 - paired)
    return unit_index * piece_size + inner_row % piece_size


def score_block(query_side, key_rows, key_place):
    query3, query_block = query_side
    key3 = key_rows.reshape(key_rows.shape[0], -1, HD)
    raw_scores = jnp.einsum("qhd,khd->hqk", query3, key3, preferred_element_type=jnp.float32)
    allowed = (key_place // BLK)[None, None, :] <= query_block[None, :, None]
    return (jnp.where(allowed, raw_scores * HD ** (-0.5), MASKED), allowed)


def absorb(running, key_rows, value_rows, key_place, query_side):
    largest, denom, accum = running
    scores, allowed = score_block(query_side, key_rows, key_place)
    new_largest = jnp.maximum(largest, jnp.max(scores, axis=2))
    factor = jnp.exp(largest - new_largest)
    raised = jnp.where(allowed, jnp.exp(scores - new_largest[:, :, None]), 0.0)
    denom = denom * factor + jnp.sum(raised, axis=2)
    value3 = value_rows.reshape(value_rows.shape[0], -1, HD)
    accum = accum * factor.T[:, :, None] + jnp.einsum(
        "hqk,khd->qhd", raised.astype(jnp.bfloat16), value3, preferred_element_type=jnp.float32
    )
    return (new_largest, denom, accum)


def fold_keys(running, key_piece, query_side, block_deal, rows_dev):
    key_all, value_all = key_piece
    row_count = key_all.shape[0]
    block_size = KEY_ROWS

    def key_step(current, offset):
        key_rows = lax.dynamic_slice_in_dim(key_all, offset, block_size, 0)
        value_rows = lax.dynamic_slice_in_dim(value_all, offset, block_size, 0)
        key_place = places(offset, block_size, block_deal, rows_dev)
        return (absorb(current, key_rows, value_rows, key_place, query_side), None)

    offsets = jnp.arange(row_count // block_size, dtype=jnp.int32) * block_size
    running, unused = lax.scan(key_step, running, offsets)
    return running


def differentiate(query_side, log_total, delta, grad_out3, key_rows, value_rows, key_place):
    scores, allowed = score_block(query_side, key_rows, key_place)
    probs_full = jnp.where(allowed, jnp.exp(scores - log_total[:, :, None]), 0.0)
    value3 = value_rows.reshape(value_rows.shape[0], -1, HD)
    grad_probs = jnp.einsum("qhd,khd->hqk", grad_out3, value3, preferred_element_type=jnp.float32)
    grad_scores = (probs_full * (grad_probs - delta[:, :, None]) * HD ** (-0.5)).astype(
        jnp.bfloat16
    )
    return (probs_full, grad_scores)


def assign_slots(route, order, experts, capacity):
    pair_count = order.shape[0]
    expert_ids = route.reshape(pair_count)
    ordered = expert_ids[order]
    onehot = (ordered[:, None] == jnp.arange(experts, dtype=jnp.int32)[None, :]).astype(jnp.int32)
    before = jnp.cumsum(onehot, axis=0) - onehot
    slot_turn = jnp.sum(before * onehot, axis=1)
    slot_index = jnp.zeros((pair_count,), jnp.int32).at[order].set(slot_turn)
    kept_pairs = slot_index < capacity
    target = jnp.where(kept_pairs, expert_ids * capacity + slot_index, experts * capacity)
    slot_table = (
        jnp.full((experts * capacity,), pair_count, jnp.int32)
        .at[target]
        .set(jnp.arange(pair_count, dtype=jnp.int32), mode="drop")
    )
    return (target, kept_pairs, slot_table)


def body(
    tokens,
    cotangent,
    gain_attention,
    query_weight,
    key_weight,
    value_weight,
    output_weight,
    gain_mixer,
    router_weight,
    shared_gate,
    shared_up,
    shared_down,
    expert_gate,
    expert_up,
    expert_down,
    routes,
    slot_order,
    block_deal,
):
    rows_dev = tokens.shape[1]
    width = tokens.shape[2]
    ranks = lax.axis_size("ctx")
    (
        gain_one,
        query_full,
        key_full,
        value_full,
        output_full,
        gain_two,
        router_full,
        sgate_full,
        sup_full,
        sdown_full,
        expert_gate_whole,
        expert_up_whole,
        edown_full,
    ) = (
        lax.all_gather(gain_attention, "wt", axis=0, tiled=True),
        lax.all_gather(query_weight, "wt", axis=0, tiled=True),
        lax.all_gather(key_weight, "wt", axis=0, tiled=True),
        lax.all_gather(value_weight, "wt", axis=0, tiled=True),
        lax.all_gather(output_weight, "wt", axis=0, tiled=True),
        lax.all_gather(gain_mixer, "wt", axis=0, tiled=True),
        lax.all_gather(router_weight, "wt", axis=0, tiled=True),
        lax.all_gather(shared_gate, "wt", axis=0, tiled=True),
        lax.all_gather(shared_up, "wt", axis=0, tiled=True),
        lax.all_gather(shared_down, "wt", axis=0, tiled=True),
        lax.all_gather(expert_gate, "wt", axis=0, tiled=True),
        lax.all_gather(expert_up, "wt", axis=0, tiled=True),
        lax.all_gather(expert_down, "wt", axis=0, tiled=True),
    )
    gain_first = gain_one.astype(jnp.float32)
    gain_second = gain_two.astype(jnp.float32)
    heads = width // HD
    inputs = tokens[0].astype(jnp.float32)
    here = places(lax.axis_index("ctx") * rows_dev, rows_dev, block_deal, rows_dev)
    query_side_block = here // BLK
    normed_f, scale_one = rms_norm(inputs, gain_first)
    normed = normed_f.astype(jnp.bfloat16)
    query_rot = rotate(
        jnp.dot(normed, query_full, preferred_element_type=jnp.float32), here, 1.0
    ).astype(jnp.bfloat16)
    key_rot = rotate(
        jnp.dot(normed, key_full, preferred_element_type=jnp.float32), here, 1.0
    ).astype(jnp.bfloat16)
    value_low = jnp.dot(normed, value_full, preferred_element_type=jnp.float32).astype(jnp.bfloat16)
    query3 = query_rot.reshape(rows_dev, heads, HD)
    query_side = (query3, query_side_block)
    start_state = (
        jnp.full((heads, rows_dev), MASKED, jnp.float32),
        jnp.zeros((heads, rows_dev), jnp.float32),
        jnp.zeros((rows_dev, heads, HD), jnp.float32),
    )
    largest, denom, accum = fold_keys(
        start_state,
        (
            lax.all_gather(key_rot, "ctx", axis=0, tiled=True),
            lax.all_gather(value_low, "ctx", axis=0, tiled=True),
        ),
        query_side,
        block_deal,
        rows_dev,
    )
    mixed3 = accum / denom.T[:, :, None]
    log_total = largest + jnp.log(denom)
    mixed_low = mixed3.reshape(rows_dev, width).astype(jnp.bfloat16)
    second = inputs + jnp.dot(mixed_low, output_full, preferred_element_type=jnp.float32)
    mixer_f, scale_two = rms_norm(second, gain_second)
    mixer = mixer_f.astype(jnp.bfloat16)
    experts = router_full.shape[1]
    logits = jnp.dot(mixer, router_full, preferred_element_type=jnp.float32)
    route = routes[0]
    top_count = route.shape[1]
    pair_count = rows_dev * top_count
    capacity = (5 * pair_count + 4 * experts - 1) // (4 * experts)
    split_count = ranks // experts
    expert_match = route[:, :, None] == jnp.arange(experts, dtype=jnp.int32)[None, None, :]
    chosen = jnp.sum(jnp.where(expert_match, logits[:, None, :], 0.0), axis=2)
    gates = jax.nn.softmax(chosen, axis=1)
    target, kept_pairs, slot_table = assign_slots(route, slot_order[0, 0], experts, capacity)
    valid = slot_table < pair_count
    pair_pick = jnp.minimum(slot_table, pair_count - 1)
    target_pick = jnp.minimum(target, experts * capacity - 1)
    send_rows = jnp.where(
        valid[:, None], mixer[pair_pick // top_count], jnp.zeros((), jnp.bfloat16)
    )
    send_rows = jnp.broadcast_to(
        send_rows.reshape(experts, 1, capacity, width), (experts, split_count, capacity, width)
    ).reshape(ranks, capacity, width)
    received = lax.all_to_all(send_rows, "ctx", split_axis=0, concat_axis=0, tiled=True)
    slot_count = received.shape[1]
    flattened_input = received.reshape(ranks * slot_count, width)
    gate_part = jnp.dot(flattened_input, expert_gate_whole, preferred_element_type=jnp.float32)
    up_projection_part = jnp.dot(
        flattened_input, expert_up_whole, preferred_element_type=jnp.float32
    )
    activated, unused = silu_parts(gate_part)
    hidden = (activated * up_projection_part).astype(jnp.bfloat16)
    partial_value = contract_product(hidden, edown_full, 1, 1).reshape(ranks, slot_count, width)
    back = lax.all_to_all(
        partial_value.astype(jnp.bfloat16), "ctx", split_axis=0, concat_axis=0, tiled=True
    ).astype(partial_value.dtype)
    expert_gate_part = gate_part.reshape(ranks, slot_count, -1)
    expert_up_part = up_projection_part.reshape(ranks, slot_count, -1)
    combined = jnp.sum(back.reshape(experts, split_count, capacity, width), axis=1).reshape(
        experts * capacity, width
    )
    pair_out = jnp.where(kept_pairs[:, None], combined[target_pick], 0.0).reshape(
        rows_dev, top_count, width
    )
    mixture = jnp.sum(gates[:, :, None] * pair_out, axis=1)
    sgate_part = jnp.dot(mixer, sgate_full, preferred_element_type=jnp.float32)
    sup_part = jnp.dot(mixer, sup_full, preferred_element_type=jnp.float32)
    shared_act, shared_slope = silu_parts(sgate_part)
    shared_hidden = (shared_act * sup_part).astype(jnp.bfloat16)
    shared_out = jnp.dot(shared_hidden, sdown_full, preferred_element_type=jnp.float32)
    result = (second + mixture + shared_out).astype(jnp.bfloat16)
    grad_final = cotangent[0].astype(jnp.float32)
    grad_low = grad_final.astype(jnp.bfloat16)
    sdown_grad = contract_product(shared_hidden, grad_low, 0, 0)
    grad_shared_hidden = contract_product(grad_low, sdown_full, 1, 1)
    grad_sgate = (grad_shared_hidden * sup_part * shared_slope).astype(jnp.bfloat16)
    grad_sup = (grad_shared_hidden * shared_act).astype(jnp.bfloat16)
    sgate_grad = contract_product(mixer, grad_sgate, 0, 0)
    sup_grad = contract_product(mixer, grad_sup, 0, 0)
    grad_mixer = contract_product(grad_sgate, sgate_full, 1, 1) + contract_product(
        grad_sup, sup_full, 1, 1
    )
    pair_grad = (
        (gates[:, :, None] * grad_final[:, None, :]).reshape(pair_count, width).astype(jnp.bfloat16)
    )
    grad_gates = jnp.sum(grad_final[:, None, :] * pair_out, axis=2)
    send_grad = jnp.where(valid[:, None], pair_grad[pair_pick], jnp.zeros((), jnp.bfloat16))
    send_grad = jnp.broadcast_to(
        send_grad.reshape(experts, 1, capacity, width), (experts, split_count, capacity, width)
    ).reshape(ranks, capacity, width)
    recv_grad = lax.all_to_all(send_grad, "ctx", split_axis=0, concat_axis=0, tiled=True)
    flattened_input = received.reshape(ranks * capacity, width)
    flat_grad = recv_grad.reshape(ranks * capacity, width)
    gate_flat = expert_gate_part.reshape(ranks * capacity, -1)
    up_flat = expert_up_part.reshape(ranks * capacity, -1)
    expert_activation, expert_slope = silu_parts(gate_flat)
    expert_hidden = (expert_activation * up_flat).astype(jnp.bfloat16)
    edown_grad = contract_product(flat_grad, expert_hidden, 0, 0)
    expert_hidden_grad = jnp.dot(flat_grad, edown_full, preferred_element_type=jnp.float32)
    expert_gate_grad_rows = (expert_hidden_grad * up_flat * expert_slope).astype(jnp.bfloat16)
    expert_up_grad_rows = (expert_hidden_grad * expert_activation).astype(jnp.bfloat16)
    egate_grad = contract_product(flattened_input, expert_gate_grad_rows, 0, 0)
    expert_up_weight_grad = contract_product(flattened_input, expert_up_grad_rows, 0, 0)
    input_back = (
        contract_product(expert_gate_grad_rows, expert_gate_whole, 1, 1)
        + contract_product(expert_up_grad_rows, expert_up_whole, 1, 1)
    ).reshape(ranks, capacity, width)
    back_grad = lax.all_to_all(
        input_back.astype(jnp.bfloat16), "ctx", split_axis=0, concat_axis=0, tiled=True
    ).astype(input_back.dtype)
    merged = jnp.sum(back_grad.reshape(experts, split_count, capacity, width), axis=1).reshape(
        experts * capacity, width
    )
    pair_back = jnp.where(kept_pairs[:, None], merged[target_pick], 0.0).reshape(
        rows_dev, top_count, width
    )
    grad_mixer = grad_mixer + jnp.sum(pair_back, axis=1)
    grad_chosen = gates * (grad_gates - jnp.sum(gates * grad_gates, axis=1, keepdims=True))
    grad_logits = jnp.sum(jnp.where(expert_match, grad_chosen[:, :, None], 0.0), axis=1)
    router_grad = contract_exact(mixer.astype(jnp.float32), grad_logits, 0, 0)
    grad_mixer = grad_mixer + contract_exact(grad_logits, router_full.astype(jnp.float32), 1, 1)
    through_two, gain_two_grad = rms_back(second, scale_two, gain_second, grad_mixer)
    grad_second = grad_final + through_two
    grad_attention = grad_second.astype(jnp.bfloat16)
    output_grad = contract_product(mixed_low, grad_attention, 0, 0)
    grad_mixed = contract_product(grad_attention, output_full, 1, 1).astype(jnp.bfloat16)
    grad_out3 = grad_mixed.reshape(rows_dev, heads, HD)
    delta = jnp.sum(grad_out3.astype(jnp.float32) * mixed3, axis=2).T
    all_keys, all_values = (
        lax.all_gather(key_rot, "ctx", axis=0, tiled=True),
        lax.all_gather(value_low, "ctx", axis=0, tiled=True),
    )
    total_rows = all_keys.shape[0]
    block_size = KEY_ROWS

    def query_step(grad_sum, offset):
        key_rows = lax.dynamic_slice_in_dim(all_keys, offset, block_size, 0)
        value_rows = lax.dynamic_slice_in_dim(all_values, offset, block_size, 0)
        key_place = places(offset, block_size, block_deal, rows_dev)
        unused, grad_scores = differentiate(
            query_side, log_total, delta, grad_out3, key_rows, value_rows, key_place
        )
        key3 = key_rows.reshape(block_size, heads, HD)
        return (
            grad_sum
            + jnp.einsum("hqk,khd->qhd", grad_scores, key3, preferred_element_type=jnp.float32),
            None,
        )

    offsets = jnp.arange(total_rows // block_size, dtype=jnp.int32) * block_size
    grad_query3, unused = lax.scan(
        query_step, jnp.zeros((rows_dev, heads, HD), jnp.float32), offsets
    )
    inner_size = KEY_ROWS

    def one_part(offset):
        key_rows = lax.dynamic_slice_in_dim(all_keys, offset, inner_size, 0)
        value_rows = lax.dynamic_slice_in_dim(all_values, offset, inner_size, 0)
        key_place = places(offset, inner_size, block_deal, rows_dev)
        probs_full, grad_scores = differentiate(
            query_side, log_total, delta, grad_out3, key_rows, value_rows, key_place
        )
        grad_value_rows = jnp.einsum(
            "hqk,qhd->khd",
            probs_full.astype(jnp.bfloat16),
            grad_out3,
            preferred_element_type=jnp.float32,
        )
        grad_key_rows = jnp.einsum(
            "hqk,qhd->khd", grad_scores, query3, preferred_element_type=jnp.float32
        )
        return jnp.concatenate(
            [grad_key_rows.reshape(inner_size, width), grad_value_rows.reshape(inner_size, width)],
            axis=1,
        )

    parts = lax.map(
        one_part,
        jnp.arange(lax.axis_size("ctx") * rows_dev // inner_size, dtype=jnp.int32) * inner_size,
    )
    key_value_grad = lax.psum_scatter(
        parts.reshape(lax.axis_size("ctx") * rows_dev, 2 * width),
        "ctx",
        scatter_dimension=0,
        tiled=True,
    )
    grad_key_pre = rotate(key_value_grad[:, :width], here, -1.0).astype(jnp.bfloat16)
    grad_value_low = key_value_grad[:, width:].astype(jnp.bfloat16)
    grad_query_pre = rotate(grad_query3.reshape(rows_dev, width), here, -1.0).astype(jnp.bfloat16)
    query_grad = contract_product(normed, grad_query_pre, 0, 0)
    key_grad = contract_product(normed, grad_key_pre, 0, 0)
    value_grad = contract_product(normed, grad_value_low, 0, 0)
    grad_normed = (
        contract_product(grad_query_pre, query_full, 1, 1)
        + contract_product(grad_key_pre, key_full, 1, 1)
        + contract_product(grad_value_low, value_full, 1, 1)
    )
    through_one, gain_one_grad = rms_back(inputs, scale_one, gain_first, grad_normed)
    grad_input = grad_second + through_one
    (
        gain_one_share,
        query_share,
        key_share,
        value_share,
        output_share,
        gain_two_share,
        router_share,
        sgate_share,
        sup_share,
        sdown_share,
        egate_share,
        expert_up_portion,
        edown_share,
    ) = (
        lax.psum_scatter(
            gain_one_grad.astype(jnp.bfloat16), "wt", scatter_dimension=0, tiled=True
        ).astype(jnp.float32),
        lax.psum_scatter(
            query_grad.astype(jnp.bfloat16), "wt", scatter_dimension=0, tiled=True
        ).astype(jnp.float32),
        lax.psum_scatter(
            key_grad.astype(jnp.bfloat16), "wt", scatter_dimension=0, tiled=True
        ).astype(jnp.float32),
        lax.psum_scatter(
            value_grad.astype(jnp.bfloat16), "wt", scatter_dimension=0, tiled=True
        ).astype(jnp.float32),
        lax.psum_scatter(
            output_grad.astype(jnp.bfloat16), "wt", scatter_dimension=0, tiled=True
        ).astype(jnp.float32),
        lax.psum_scatter(
            gain_two_grad.astype(jnp.bfloat16), "wt", scatter_dimension=0, tiled=True
        ).astype(jnp.float32),
        lax.psum_scatter(
            router_grad.astype(jnp.bfloat16), "wt", scatter_dimension=0, tiled=True
        ).astype(jnp.float32),
        lax.psum_scatter(
            sgate_grad.astype(jnp.bfloat16), "wt", scatter_dimension=0, tiled=True
        ).astype(jnp.float32),
        lax.psum_scatter(
            sup_grad.astype(jnp.bfloat16), "wt", scatter_dimension=0, tiled=True
        ).astype(jnp.float32),
        lax.psum_scatter(
            sdown_grad.astype(jnp.bfloat16), "wt", scatter_dimension=0, tiled=True
        ).astype(jnp.float32),
        lax.psum_scatter(
            egate_grad.astype(jnp.bfloat16), "wt", scatter_dimension=0, tiled=True
        ).astype(jnp.float32),
        lax.psum_scatter(
            expert_up_weight_grad.astype(jnp.bfloat16), "wt", scatter_dimension=0, tiled=True
        ).astype(jnp.float32),
        lax.psum_scatter(
            edown_grad.astype(jnp.bfloat16), "wt", scatter_dimension=0, tiled=True
        ).astype(jnp.float32),
    )
    (
        gain_one_sum,
        query_sum,
        key_sum,
        value_sum,
        output_sum,
        gain_two_sum,
        router_sum,
        sgate_sum,
        sup_sum,
        sdown_sum,
    ) = lax.psum(
        (
            gain_one_share,
            query_share,
            key_share,
            value_share,
            output_share,
            gain_two_share,
            router_share,
            sgate_share,
            sup_share,
            sdown_share,
        ),
        "ctx",
    )
    return (
        result[None],
        grad_input[None],
        gain_one_sum,
        query_sum,
        key_sum,
        value_sum,
        output_sum,
        gain_two_sum,
        router_sum,
        sgate_sum,
        sup_sum,
        sdown_sum,
        egate_share,
        expert_up_portion,
        edown_share,
    )


def fast_body(
    tokens,
    cotangent,
    gain_attention,
    query_weight,
    key_weight,
    value_weight,
    output_weight,
    gain_mixer,
    router_weight,
    shared_gate,
    shared_up,
    shared_down,
    expert_gate,
    expert_up,
    expert_down,
    routes,
    slot_order,
    block_deal,
):
    half_size = HD // 2
    frequency = 10000.0 ** (-np.arange(half_size) / half_size)
    frequency = jnp.asarray(np.tile(frequency, 4)[None].astype(np.float32))
    (
        cosr, sinr, kb, qb, qx, gx, stats, n_t, m_t, pack_all, result, grad_second, pack_grad, dsh,
        kv_all, wfull, keep, give, other,
    ) = run_forward(
        tokens[0], jnp.stack([gain_attention, gain_mixer]), router_weight.T, frequency, block_deal,
        cotangent[0], routes[0].T, slot_order[0],
        shared_down, query_weight, key_weight, value_weight, output_weight, shared_gate, shared_up,
        expert_gate, expert_up, expert_down,
    )
    grad_input, pack_sum, att1, att2, sh, other = run_backward(
        grad_second, tokens[0], pack_all, pack_grad, n_t, m_t, qx, gx, stats, cosr, sinr, kb, qb,
        dsh, kv_all, wfull, give, other,
    )
    (
        result, grad_input, gain_one, gain_two, router, query, key, value, output, gate, up, down,
        eg, eu, ed,
    ) = run_unpack(
        result, grad_input, pack_sum, att1, att2, sh, keep, other, router_weight.shape[1]
    )
    return (
        result[None], grad_input[None], gain_one.reshape(-1), query, key, value, output,
        gain_two.reshape(-1), router.T, gate, up, down, eg, eu, ed,
    )


def solution(mesh):
    in_specs = (
        P("wt", "ctx", None),
        P("wt", "ctx", None),
        P("wt"),
        P("wt", None),
        P("wt", None),
        P("wt", None),
        P("wt", None),
        P("wt"),
        P("wt", None),
        P("wt", None),
        P("wt", None),
        P("wt", None),
        P("wt", "ctx"),
        P("wt", "ctx"),
        P("wt", "ctx"),
        P("wt", "ctx", None),
        P("wt", "ctx", None),
        P(),
    )
    out_specs = (
        P("wt", "ctx", None),
        P("wt", "ctx", None),
        P("wt"),
        P("wt", None),
        P("wt", None),
        P("wt", None),
        P("wt", None),
        P("wt"),
        P("wt", None),
        P("wt", None),
        P("wt", None),
        P("wt", None),
        P("wt", "ctx"),
        P("wt", "ctx"),
        P("wt", "ctx"),
    )
    chosen = fast_body if (mesh.shape["ctx"], mesh.shape["wt"]) == (8, 4) else body
    return jax.shard_map(chosen, mesh=mesh, in_specs=in_specs, out_specs=out_specs, check_vma=False)
```

```python
import jax
import jax.numpy as jnp
import numpy as np
from jax import lax
from jax.experimental import pallas as pl
from jax.experimental.pallas import tpu as pltpu
from jax.sharding import PartitionSpec as P

HD = 64
BLK = 256


EPS = 1e-06
KEY_ROWS = 512
HIGH = lax.Precision.HIGHEST
MASKED = -1e30


MESH = pl.DeviceIdType.MESH
VMEM = pltpu.VMEM
BF = jnp.bfloat16
F32 = jnp.float32
PAIR = 2 * HD
VMEM_BYTES = 127 * 2**19
SEMS_FORWARD = 207
SEMS_BACKWARD = 95
SEMS_RINGS = 48


class Spot:
    def __init__(self, line_size):
        self.k = lax.axis_index("ctx")
        self.w = lax.axis_index("wt")
        self.z, self.x = lax.div(self.k, 2), lax.rem(self.k, 2)
        self.y, self.c = lax.div(self.w, 2), lax.rem(self.w, 2)
        self.far = lax.div(self.z, 2)
        self.mid = self.z + self.far * (3 - 2 * self.z)
        step = 1 - 2 * self.far
        self.core = (self.k, 2 * self.y + 1 - self.c)
        self.across = (self.k, 2 * (1 - self.y) + self.c)
        self.corner = (self.k, 2 * (1 - self.y) + 1 - self.c)
        self.column = (2 * self.z + 1 - self.x, self.w)
        self.odd = lax.rem(self.z, 2)
        self.line = (2 * (self.z + 1 - 2 * self.odd) + self.x, self.w)
        self.inner = (2 * (self.z + step) + self.x, self.w)
        self.outer = (2 * (self.z - step) + self.x, self.w)

    def plane(self, step):
        mirrored = (self.mid, 1 - self.mid, 2, 3)[step]
        return mirrored + self.far * (3 - 2 * mirrored)


class Sems:
    def __init__(self, ref):
        self.ref, self.used = ref, 0

    def new(self):
        self.used += 1
        return self.ref.at[self.used - 1]


def remote(src, dst, send, recv, to):
    return pltpu.make_async_remote_copy(
        src_ref=src, dst_ref=dst, send_sem=send, recv_sem=recv, device_id=to, device_id_type=MESH
    )


def greet(devices, middle=None):
    barrier = pltpu.get_barrier_semaphore()
    for to in devices:
        pl.semaphore_signal(barrier, inc=1, device_id=to, device_id_type=MESH)
    if middle is None:
        pl.semaphore_wait(barrier, len(devices))
        return

    @pl.when(middle[0] == 1)
    def _():
        pl.semaphore_signal(barrier, inc=1, device_id=middle[1], device_id_type=MESH)

    pl.semaphore_wait(barrier, len(devices) + middle[0])


class Gather:
    def __init__(self, spot, src, place, sems, local=True):
        self.spot, self.place, self.sems = spot, place, sems
        here = place(spot.w)
        self.local = pltpu.make_async_copy(src, here, sems.new()) if local else None
        self.to_core = remote(src, here, sems.new(), sems.new(), spot.core)
        self.to_across = remote(src, here, sems.new(), sems.new(), spot.across)
        self.to_across.start()
        self.to_core.start()
        if local:
            self.local.start()

    def forward(self):
        self.to_across.wait_recv()
        part = self.place(self.spot.across[1])
        self.onward = remote(part, part, self.sems.new(), self.sems.new(), self.spot.core)
        self.onward.start()

    def finish(self):
        if self.local is not None:
            self.local.wait()
        self.to_core.wait_recv()
        self.onward.wait_recv()

    def drain(self):
        for copy in (self.to_core, self.to_across, self.onward):
            copy.wait_send()


class Share:
    def __init__(self, spot, src, dst, sems, mate, bit):
        self.spot, self.dst, self.sems, self.mate, self.bit = spot, dst, sems, mate, bit
        self.rows = src.shape[0]
        self.half = self.rows // 2
        here = dst.at[pl.ds(pl.multiple_of(self.rows * spot.w, 64), self.rows)]
        half = pl.ds(pl.multiple_of(self.half * bit, 32), self.half)
        self.local = pltpu.make_async_copy(src, here, sems.new())
        self.to_core = remote(src, here, sems.new(), sems.new(), spot.core)
        self.to_across = remote(
            src.at[half], self.part(spot.w, bit), sems.new(), sems.new(), spot.across
        )
        for copy in (self.to_across, self.to_core, self.local):
            copy.start()

    def part(self, w, bit):
        return self.dst.at[pl.ds(pl.multiple_of(self.rows * w + self.half * bit, 32), self.half)]

    def forward(self):
        spot = self.spot
        self.to_across.wait_recv()
        part = self.part(spot.across[1], self.bit)
        self.aside = remote(part, part, self.sems.new(), self.sems.new(), self.mate)
        self.onward = remote(part, part, self.sems.new(), self.sems.new(), spot.core)
        self.aside.start()
        self.onward.start()

    def second(self):
        self.aside.wait_recv()
        part = self.part(self.spot.across[1], 1 - self.bit)
        self.rest = remote(part, part, self.sems.new(), self.sems.new(), self.spot.core)
        self.rest.start()

    def finish(self):
        self.local.wait()
        self.to_core.wait_recv()
        self.onward.wait_recv()
        self.rest.wait_recv()

    def drain(self):
        for copy in (self.to_core, self.to_across, self.aside, self.onward, self.rest):
            copy.wait_send()


class Quarters:
    def __init__(self, spot, src, dst, sems, columns=False):
        self.spot, self.dst, self.sems, self.columns = spot, dst, sems, columns
        self.rows = src.shape[0]
        self.size = self.rows // 4
        self.q = 2 * spot.x + spot.odd
        self.sources = (spot.across, spot.corner) if columns else (spot.across,)
        cols = dst.shape[1]

        def take(to, quarter):
            at = pl.ds(pl.multiple_of(self.size * self.q, 16), self.size)
            if not columns:
                return src.at[at] if quarter else src
            lanes = pl.ds(pl.multiple_of(cols * to, cols), cols)
            return src.at[at, lanes] if quarter else src.at[:, lanes]

        here = dst.at[pl.ds(pl.multiple_of(self.rows * spot.w, 64), self.rows)]
        self.far = [
            remote(take(to[1], True), self.part(spot.w, self.q), sems.new(), sems.new(), to)
            for to in self.sources
        ]
        self.to_core = remote(take(spot.core[1], False), here, sems.new(), sems.new(), spot.core)
        self.local = pltpu.make_async_copy(take(spot.w, False), here, sems.new())
        for copy in self.far + [self.to_core, self.local]:
            copy.start()
        self.lines, self.sides, self.cores = [], [], []

    def part(self, w, q, count=1):
        start = pl.multiple_of(self.rows * w + self.size * q, 16)
        return self.dst.at[pl.ds(start, self.size * count)]

    def send(self, copies, part, to):
        copies.append(remote(part, part, self.sems.new(), self.sems.new(), to))
        copies[-1].start()

    def forward(self):
        for copy, source in zip(self.far, self.sources):
            copy.wait_recv()
            part = self.part(source[1], self.q)
            self.send(self.lines, part, self.spot.line)
            self.send(self.sides, part, self.spot.column)
            if not self.columns:
                self.send(self.cores, part, self.spot.core)

    def second(self):
        for copy, source in zip(self.lines, self.sources):
            copy.wait_recv()
            part = self.part(source[1], 2 * self.spot.x + 1 - self.spot.odd)
            self.send(self.sides, part, self.spot.column)
            if not self.columns:
                self.send(self.cores, part, self.spot.core)

    def third(self):
        for copy in self.sides:
            copy.wait_recv()
        if not self.columns:
            part = self.part(self.spot.across[1], 2 * (1 - self.spot.x), 2)
            self.send(self.cores, part, self.spot.core)

    def finish(self):
        self.local.wait()
        self.to_core.wait_recv()
        for copy in self.cores:
            copy.wait_recv()

    def drain(self):
        for copy in self.far + self.lines + self.sides + self.cores + [self.to_core]:
            copy.wait_send()


class Merge:
    def __init__(self, spot, send, land, sems):
        self.spot, self.send, self.land = spot, send, land
        self.far = remote(
            send.at[spot.corner[1]], land.at[0], sems.new(), sems.new(), spot.core
        )
        self.near = remote(send.at[spot.core[1]], land.at[1], sems.new(), sems.new(), spot.core)
        self.over = remote(
            send.at[spot.across[1]], land.at[2], sems.new(), sems.new(), spot.across
        )
        self.far.start()
        self.near.start()

    def forward(self):
        self.far.wait_recv()
        block = self.send.at[self.spot.across[1]]
        block[...] = (block[...].astype(F32) + self.land[0].astype(F32)).astype(BF)
        self.over.start()

    def finish(self):
        self.near.wait_recv()
        self.over.wait_recv()
        own = self.send[self.spot.w].astype(F32)
        return own + self.land[1].astype(F32) + self.land[2].astype(F32)

    def drain(self):
        for copy in (self.far, self.near, self.over):
            copy.wait_send()


class Spread:
    def __init__(self, spot, pick, place, sems):
        self.copies = []
        for to in (spot.across, spot.corner, spot.core):
            self.copies.append(remote(pick(to[1]), place(spot.w), sems.new(), sems.new(), to))
        self.local = pltpu.make_async_copy(pick(spot.w), place(spot.w), sems.new())
        for copy in self.copies:
            copy.start()
        self.local.start()

    def finish(self):
        for copy in self.copies:
            copy.wait_recv()
        self.local.wait()

    def drain(self):
        for copy in self.copies:
            copy.wait_send()


def nt(left, right):
    return lax.dot_general(left, right, (((1,), (1,)), ((), ())), preferred_element_type=F32)


def nn(left, right):
    return jnp.dot(left, right, preferred_element_type=F32)


def tn(left, right):
    return lax.dot_general(left, right, (((0,), (0,)), ((), ())), preferred_element_type=F32)


def turn(values, cosine, sine):
    wide = values.shape[1]
    lane = lax.broadcasted_iota(jnp.int32, values.shape, 1)
    first = lax.rem(lane, HD) < HD // 2
    swapped = jnp.where(
        first, pltpu.roll(values, wide - HD // 2, 1), pltpu.roll(values, HD // 2, 1)
    )
    copies = wide // PAIR
    cosine = jnp.concatenate([cosine] * copies, axis=1)
    sine = jnp.concatenate([sine] * copies, axis=1)
    return values * cosine + swapped * sine


def stack_pair(values):
    lane = lax.broadcasted_iota(jnp.int32, values.shape, 1)
    none = jnp.zeros_like(values)
    return jnp.concatenate(
        [jnp.where(lane < HD, values, none), jnp.where(lane < HD, none, values)], axis=0
    )


def unstack_pair(values):
    rows = values.shape[0] // 2
    lane = lax.broadcasted_iota(jnp.int32, (rows, PAIR), 1)
    return jnp.where(lane < HD, values[:rows], values[rows:])


class Ring:
    def __init__(self, spot, blocks, recv, send, parts=1, sides=1, first=(0, 0)):
        self.spot, self.blocks, self.recv, self.send, self.parts = spot, blocks, recv, send, parts
        self.sides = sides
        self.ranks = blocks.shape[0]
        self.first, self.used = first[0], first[1]
        self.sent, self.sent_mid, self.sent_end = [], [], []

    def piece(self, slot, part):
        if self.sides == 1:
            rows = self.blocks.shape[1] // self.parts
            return self.blocks.at[slot, pl.ds(rows * part, rows)]
        high = self.parts // self.sides
        rows, lanes = self.blocks.shape[1] // high, self.blocks.shape[2] // self.sides
        return self.blocks.at[
            slot, pl.ds(rows * (part % high), rows), pl.ds(lanes * (part // high), lanes)
        ]

    def copy(self, slot, part, to):
        self.used += 1
        return remote(
            self.piece(slot, part),
            self.piece(slot, part),
            self.send.at[self.used - 1],
            self.recv.at[self.first + slot + self.ranks * part],
            to,
        )

    def arrived(self, slot, part):
        remote(
            self.piece(slot, part),
            self.piece(slot, part),
            self.send.at[0],
            self.recv.at[self.first + slot + self.ranks * part],
            self.spot.column,
        ).wait_recv()

    def start(self, parts=None, only=None):
        spot = self.spot
        for part in range(self.parts) if parts is None else parts:
            own = self.copy(spot.k, part, spot.inner)
            side = self.copy(spot.k, part, spot.column)
            back = self.copy(spot.k, part, spot.outer) if only != 0 else None
            if only is None:
                own.start()
                self.middle(back)
                side.start()
                self.sent += [own, side]
                self.sent_mid += [back]
                continue

            @pl.when(spot.mid == only)
            def _(copies=(own, back, side)):
                for copy in copies:
                    if copy is not None:
                        copy.start()

            if only == 1:
                self.sent_mid += [own, back, side]
            else:
                self.sent_end += [own, side]

    def middle(self, copy):
        @pl.when(self.spot.mid == 1)
        def _():
            copy.start()

    def step(self, number, only=None):
        spot = self.spot
        slot = 2 * spot.plane(number) + spot.x
        onward = spot.inner if number == 1 else spot.outer
        pieces = []
        for part in range(self.parts):
            along = self.copy(slot, part, onward) if only != 0 else None
            pieces.append((along, self.copy(slot, part, spot.column)))
        if only != 0:

            @pl.when(spot.mid == 1)
            def _():
                for part, (along, side) in enumerate(pieces):
                    self.arrived(slot, part)
                    along.start()
                    side.start()

        if only != 1:

            @pl.when(spot.mid == 0)
            def _():
                for part, (along, side) in enumerate(pieces):
                    self.arrived(slot, part)
                    side.start()

        if only != 0:
            self.sent_mid += [along for along, _ in pieces]
            self.sent_mid += [side for _, side in pieces]
        if only != 1:
            self.sent_end += [side for _, side in pieces]

    def other(self, number):
        for part in range(self.parts):
            self.arrived(2 * self.spot.plane(number) + 1 - self.spot.x, part)

    def drain(self):
        for copy in self.sent:
            copy.wait_send()
        for role, copies in ((0, self.sent_end), (1, self.sent_mid)):

            @pl.when(self.spot.mid == role)
            def _(copies=copies):
                for copy in copies:
                    copy.wait_send()


class Reduce:
    def __init__(self, spot, part, sides, zo, zi, sems, folded=False, parts=1):
        self.spot, self.part, self.sides, self.zo, self.zi = spot, part, sides, zo, zi
        self.z_send, self.zo_recv = sems.at[0], sems.at[1]
        if folded:
            self.zi_recv = sems.at[2]
        else:
            self.x_send, self.x_recv = sems.at[2], sems.at[3]
        self.folded, self.parts = folded, parts
        self.rows = part.shape[1] // parts
        self.sent, self.sent_end, self.sent_mid = [], [], []

    def cut(self, ref, index, h):
        return ref.at[index, pl.ds(self.rows * h, self.rows)]

    def own(self, plane, h):
        return self.cut(self.part, plane if self.folded else 2 * plane + self.spot.x, h)

    def wait(self, land, recv, plane, h):
        piece = self.cut(land, plane, h)
        at = plane + 4 * h
        remote(piece, piece, self.z_send.at[at], recv.at[at], self.spot.column).wait_recv()

    def side(self, number):
        spot = self.spot
        plane = spot.plane(number)
        for h in range(self.parts):
            at = plane + 4 * h
            copy = remote(
                self.cut(self.part, 2 * plane + 1 - spot.x, h),
                self.cut(self.sides, plane, h),
                self.x_send.at[at],
                self.x_recv.at[at],
                spot.column,
            )
            copy.start()
            self.sent.append(copy)

    def add(self, ref, land):
        ref[...] = (ref[...].astype(F32) + land[...].astype(F32)).astype(BF)

    def meet(self, number, launch):
        plane = self.spot.plane(number)
        for h in range(self.parts):
            self.wait(self.sides, self.x_recv, plane, h)
            self.add(self.own(plane, h), self.cut(self.sides, plane, h))
            if launch:
                self.launch_part(number, h)

    def launch(self, number):
        for h in range(self.parts):
            self.launch_part(number, h)

    def launch_part(self, number, h):
        plane = self.spot.plane(number)
        at = plane + 4 * h
        copy = remote(
            self.own(plane, h),
            self.cut(self.zo, plane, h),
            self.z_send.at[at],
            self.zo_recv.at[at],
            self.spot.inner,
        )

        @pl.when(self.spot.mid == 0)
        def _():
            copy.start()

        self.sent_end.append(copy)

    def absorb(self, number):
        plane = self.spot.plane(number)

        @pl.when(self.spot.mid == 1)
        def _():
            for h in range(self.parts):
                self.wait(self.zo, self.zo_recv, plane, h)
                self.add(self.own(plane, h), self.cut(self.zo, plane, h))

    def relay(self, number, settled=False, parts=None):
        plane = self.spot.plane(number)
        land, recv = (self.zi, self.zi_recv) if number == 1 else (self.zo, self.zo_recv)
        copies = []
        for h in range(self.parts) if parts is None else parts:
            at = plane + 4 * h
            copy = remote(
                self.own(plane, h),
                self.cut(self.zi, plane, h),
                self.z_send.at[at],
                self.zi_recv.at[at],
                self.spot.outer if number == 1 else self.spot.inner,
            )
            copies.append((h, copy))

        @pl.when(self.spot.mid == 1)
        def _():
            for h, copy in copies:
                if not settled:
                    self.wait(land, recv, plane, h)
                    self.add(self.own(plane, h), self.cut(land, plane, h))
                copy.start()

        self.sent_mid += [copy for _, copy in copies]

    def last(self, result, parts=None):
        plane = self.spot.plane(0)
        parts = range(self.parts) if parts is None else parts
        for h in parts:
            self.wait(self.zi, self.zi_recv, plane, h)
            rows = pl.ds(self.rows * h, self.rows)
            total = self.own(plane, h)[...].astype(F32)
            result[rows] = total + self.cut(self.zi, plane, h)[...].astype(F32)

        @pl.when(self.spot.mid == 1)
        def _():
            for h in parts:
                self.wait(self.zo, self.zo_recv, plane, h)
                rows = pl.ds(self.rows * h, self.rows)
                result[rows] += self.cut(self.zo, plane, h)[...].astype(F32)

    def drain(self):
        for copy in self.sent:
            copy.wait_send()

        @pl.when(self.spot.mid == 0)
        def _():
            for copy in self.sent_end:
                copy.wait_send()

        @pl.when(self.spot.mid == 1)
        def _():
            for copy in self.sent_mid:
                copy.wait_send()


def swish(values):
    sigmoid = 1.0 / (1.0 + jnp.exp(-values))
    return values * sigmoid, sigmoid * (1.0 + values * (1.0 - sigmoid))


class Exchange:
    def __init__(self, spot, out, back, send, recv):
        self.spot, self.out, self.back = spot, out, back
        self.send, self.recv, self.ranks = send, recv, out.shape[0]
        self.copies = []

    def start(self):
        spot = self.spot
        for offset in range(1, self.ranks):
            peer = lax.rem(spot.k + offset, self.ranks)
            self.copies.append(
                remote(
                    self.out.at[peer],
                    self.back.at[spot.k],
                    self.send.at[offset],
                    self.recv.at[spot.k],
                    (peer, spot.w),
                )
            )
            self.copies[-1].start()
        self.back[spot.k] = self.out[spot.k]

    def finish(self):
        spot = self.spot
        for offset in range(1, self.ranks):
            peer = lax.rem(spot.k + offset, self.ranks)
            remote(
                self.out.at[peer],
                self.back.at[peer],
                self.send.at[offset],
                self.recv.at[peer],
                (peer, spot.w),
            ).wait_recv()

    def drain(self):
        for copy in self.copies:
            copy.wait_send()


def fold_rows(values, ref):
    ranks = ref.shape[0]
    slots = values.shape[0] // ranks
    for e in range(ranks):
        part = values[slots * e : slots * (e + 1)]
        tiles = [part[:, 128 * t : 128 * (t + 1)] for t in range(values.shape[1] // 128)]
        ref[e] = jnp.concatenate(tiles, axis=0).astype(BF)


def unfold_rows(ref, slots):
    parts = []
    for e in range(ref.shape[0]):
        part = ref[e].astype(F32)
        tiles = [part[slots * t : slots * (t + 1)] for t in range(part.shape[0] // slots)]
        parts.append(jnp.concatenate(tiles, axis=1))
    return jnp.concatenate(parts, axis=0).astype(BF)


def split_three(values):
    high = values.astype(BF)
    rest = values - high.astype(F32)
    middle = rest.astype(BF)
    return high, middle, (rest - middle.astype(F32)).astype(BF)


def diagonal(values, axis):
    size = max(values.shape)
    down = lax.broadcasted_iota(jnp.int32, (size, size), 0)
    along = lax.broadcasted_iota(jnp.int32, (size, size), 1)
    return jnp.sum(
        jnp.where(down == along, values.astype(F32), 0.0), axis=axis, keepdims=True
    ).astype(jnp.int32)


def slot_maps(routes, order, slots, experts):
    top, rows = routes.shape
    pairs = rows * top
    lines = [routes[j : j + 1] for j in range(top)]
    e_row = jnp.concatenate(lines, axis=1)
    e_col = jnp.concatenate([diagonal(line, 1) for line in lines], axis=0)
    o_row = lax.rem(order, top) * rows + lax.div(order, top)
    o_col = diagonal(o_row, 1)
    down = lax.broadcasted_iota(jnp.int32, (pairs, pairs), 0)
    along = lax.broadcasted_iota(jnp.int32, (pairs, pairs), 1)
    turn_row = jnp.sum(jnp.where(o_col == along, down.astype(F32), 0.0), axis=0, keepdims=True)
    turn_col = jnp.sum(jnp.where(o_row == down, along.astype(F32), 0.0), axis=1, keepdims=True)
    same = e_col == e_row
    slot_row = jnp.sum(
        jnp.where(same & (turn_col < turn_row), 1.0, 0.0), axis=0, keepdims=True
    ).astype(jnp.int32)
    slot_col = jnp.sum(
        jnp.where(same & (turn_row < turn_col), 1.0, 0.0), axis=1, keepdims=True
    ).astype(jnp.int32)
    target_row = jnp.where(slot_row < slots, e_row * slots + slot_row, -1)
    target_col = jnp.where(slot_col < slots, e_col * slots + slot_col, -1)
    total = experts * slots
    place = lax.broadcasted_iota(jnp.int32, (total, pairs), 0)
    to_slots = jnp.where(place == target_row, 1.0, 0.0).astype(BF)
    place = lax.broadcasted_iota(jnp.int32, (pairs, total), 1)
    to_pairs = jnp.where(place == target_col, 1.0, 0.0).astype(BF)
    return to_slots, to_pairs


def forward_kernel(
    tok, gain_one, gain_two, router_ref, freq, deal, cot, routes, order, sd,
    wq, wk, wv, wo, sg, su, eg, eu, ed,
    cosr_out, sinr_out, kb_out, qb_out, qx_out, gx_out, stats_hbm, normed_hbm, mixed_hbm, pack_hbm,
    result_hbm, grad_second_hbm, pack_grad_hbm, dsh_out, side_out, kv_out, wfull_out, keep_out, give_out, other_out,
    cosr, sinr, kb, qb, qx, gx, stats_out, normed_out, mixed_out, pack_out, result_out,
    grad_second_out, pack_grad_out, wbuf, kv, q_s, qc, q_land, gm, gm_land, stat, stat_land, mixed, pack, packs, top, low, acc, sg_all, su_all, wg, wu, wd, mix, m4, cot4,
    sh_send, sh_recv, gm_send, gm_recv, xs, xr, gs, gr, orr, br,
    x_s, g_s, sum_s, gate_s, up_s, hid_s, dgate_s, dup_s, dsh, dsh_x, dsh_z, slot_s, pair_s, cb,
    sem, kv_recv, kv_send, a2a_send, a2a_recv, sem_sh,
):
    spot = Spot(4)
    sems = Sems(sem)
    rows, width = tok.shape
    pairs = width // PAIR
    ranks = xs.shape[0]
    slots = xs.shape[1] * 128 // width
    hidden = wg.shape[1]
    shard = width // 4
    part = sg_all.shape[1]
    peers = [(lax.rem(spot.k + o, ranks), spot.w) for o in range(1, ranks)]
    greet([spot.core, spot.across, spot.corner] + peers)
    line = (spot.line, spot.odd)
    key_w = Quarters(spot, wk, wbuf.at[1], sems)
    shards = jnp.concatenate(
        [
            gain_one[...].astype(F32).reshape(1, shard),
            gain_two[...].astype(F32).reshape(1, shard),
            router_ref[...].astype(F32),
            jnp.zeros((16 - 2 - router_ref.shape[0], shard), F32),
        ],
        axis=0,
    )
    shards = jnp.concatenate([shards, jnp.zeros((16, width - shard), F32)], axis=1)
    pack[...] = pltpu.roll(shards, shard * spot.w, 1).astype(BF)
    params = Gather(spot, pack, lambda w: packs.at[w], sems)
    value_w = Quarters(spot, wv, wbuf.at[2], sems)
    query_w = Quarters(spot, wq, wbuf.at[0], sems)

    def stripe(ref):
        return lambda w: ref.at[pl.ds(pl.multiple_of(shard * w, 64), shard)]

    out_w = Share(spot, wo, wbuf.at[3], sems, *line)
    sg_w = Quarters(spot, sg, sg_all, sems, columns=True)
    su_w = Quarters(spot, su, su_all, sems, columns=True)
    cot_w = Gather(spot, cot, lambda w: cot4.at[w], sems)
    gate_w = Gather(spot, eg, stripe(wg), sems)
    up_w = Gather(spot, eu, stripe(wu), sems)
    early = shard // 3

    def down_part(start, count):
        at = pl.ds(start, count)
        place = lambda w: wd.at[pl.ds(pl.multiple_of(shard * w + start, 64), count)]
        return Gather(spot, ed.at[at], place, sems)

    down_w = [down_part(0, early)]
    inputs = tok[...].astype(F32)
    scale = lax.rsqrt(jnp.mean(inputs * inputs, axis=-1, keepdims=True) + EPS)
    scaled = inputs * scale
    piece = rows // 2
    inner = lax.broadcasted_iota(jnp.int32, (rows, 1), 0)
    lane = lax.broadcasted_iota(jnp.int32, (rows, PAIR), 1)
    sign = jnp.where(lax.rem(lane, HD) < HD // 2, -1.0, 1.0)
    for r in range(2):
        paired = deal[2 * spot.z + r]
        unit = jnp.where(inner < piece, paired, 2 * ranks - 1 - paired)
        place = unit * piece + lax.rem(inner, piece)
        qb[r] = jnp.concatenate([lax.div(place, BLK)] * 2, axis=0)
        angles = place.astype(F32) * freq[...]
        cosr[r] = jnp.cos(angles)
        sinr[r] = jnp.sin(angles) * sign
    along = lax.broadcasted_iota(jnp.int32, (1, rows), 1)
    for r in range(ranks):
        unit = jnp.where(along < piece, deal[r], 2 * ranks - 1 - deal[r])
        kb[:, rows * r : rows * (r + 1)] = lax.div(unit * piece + lax.rem(along, piece), BLK)
    key_w.forward()
    params.forward()
    params.finish()
    pack_all = (packs[0].astype(F32) + packs[1].astype(F32)) + (
        packs[2].astype(F32) + packs[3].astype(F32)
    )
    pack_out[...] = pack_all
    normed = (scaled * pack_all[0:1]).astype(BF)
    normed_out[...] = normed.T
    cosine, sine = cosr[spot.x], sinr[spot.x]
    value_w.forward()
    to_slots, to_pairs = slot_maps(routes[...], order[...], slots, ranks)
    route = [diagonal(routes[j : j + 1], 1) for j in range(2)]
    slot_s[...] = to_slots
    pair_s[...] = to_pairs
    key_w.second()
    query_w.forward()
    value_w.second()
    key_w.third()
    key_w.finish()
    kv[spot.k, :, 0:width] = turn(nn(normed, wbuf[1]), cosine, sine).astype(BF)
    ring = Ring(spot, kv, kv_recv, kv_send, parts=4, sides=2)
    ring.start(parts=(0, 1))
    query_w.second()
    value_w.third()
    value_w.finish()
    kv[spot.k, :, width : 2 * width] = nn(normed, wbuf[2]).astype(BF)
    ring.start(parts=(2, 3))
    query_w.third()
    query_w.finish()
    query = turn(nn(normed, wbuf[0]), cosine, sine).astype(BF) * jnp.asarray(HD**-0.5, BF)
    for j in range(pairs):
        q_s[j] = stack_pair(query[:, PAIR * j : PAIR * (j + 1)])
    for x in range(2):
        qc[x] = query[:, width // 2 * x : width // 2 * (x + 1)]
    top[...] = jnp.full_like(top, MASKED)
    low[...] = jnp.zeros_like(low)
    acc[...] = jnp.zeros_like(acc)
    q_block = qb[spot.x]

    def chunk(plane):
        k_block = kb[:, pl.ds(pl.multiple_of(2 * rows * plane, 2 * rows), 2 * rows)]
        allowed = k_block <= q_block

        def one_pair(j, carry):
            lane = pl.multiple_of(PAIR * j, PAIR)
            key = kv[pl.ds(2 * plane, 2), :, pl.ds(lane, PAIR)].reshape(2 * rows, PAIR)
            value = kv[pl.ds(2 * plane, 2), :, pl.ds(width + lane, PAIR)].reshape(2 * rows, PAIR)
            scores = jnp.where(allowed, nt(q_s[j], key), MASKED)
            old = top[j]
            new = jnp.maximum(old, jnp.max(scores, axis=1, keepdims=True))
            raised = jnp.where(allowed, jnp.exp(scores - new[:, 0:1]), 0.0)
            factor = jnp.exp(old - new)
            top[j] = new
            low[j] = low[j] * factor + jnp.sum(raised, axis=1, keepdims=True)
            acc[j] = acc[j] * factor + nn(raised.astype(BF), value)
            return carry

        lax.fori_loop(0, pairs, one_pair, 0, unroll=3)

    ring.step(1)
    ring.step(2, only=1)
    ring.other(0)
    chunk(spot.plane(0))
    ring.step(2, only=0)
    ring.step(3, only=1)
    ring.other(1)
    chunk(spot.plane(1))
    ring.step(3, only=0)
    out_w.forward()
    sg_w.forward()
    su_w.forward()
    ring.other(2)
    chunk(spot.plane(2))
    out_w.second()
    cot_w.forward()
    ring.other(3)
    chunk(spot.plane(3))
    sg_w.second()
    su_w.second()
    saves = []

    def save(src, dst):
        saves.append(pltpu.make_async_copy(src, dst, sems.new()))
        saves[-1].start()

    save(kv, kv_out)
    for src, dst in ((cosr, cosr_out), (sinr, sinr_out), (kb, kb_out), (qb, qb_out)):
        save(src, dst)
    save(normed_out, normed_hbm)
    save(pack_out, pack_hbm)
    for j in range(pairs):
        mixed[:, PAIR * j : PAIR * (j + 1)] = unstack_pair(acc[j] / low[j])
        top[j] = top[j] + jnp.log(low[j])
    asides = []

    def aside(src, dst):
        asides.append(remote(src, dst, sems.new(), sems.new(), spot.column))
        asides[-1].start()
        return asides[-1]

    out_w.finish()
    save(wbuf, wfull_out)
    second = inputs + nn(mixed[...].astype(BF), wbuf[3])
    scale = lax.rsqrt(jnp.mean(second * second, axis=-1, keepdims=True) + EPS)
    mixer = (second * scale * pack_all[1:2]).astype(BF)
    mix[...] = mixer

    mixers = Gather(spot, mix, lambda w: m4.at[w], sems)
    down_w.append(down_part(early, shard - early))
    fold_rows(nn(slot_s[:, :rows] + slot_s[:, rows:], mixer), xs)
    rows_out = Exchange(spot, xs, xr, a2a_send.at[0], a2a_recv.at[0])
    rows_out.start()
    router = pack_all[2:16].astype(BF)
    router = jnp.concatenate([router, jnp.zeros((2, width), BF)], axis=0)
    logits = nt(mixer, router)
    lane = lax.broadcasted_iota(jnp.int32, logits.shape, 1)
    matches = [lane == route[j] for j in range(2)]
    chosen = [jnp.sum(jnp.where(m, logits, 0.0), axis=1, keepdims=True) for m in matches]
    largest = jnp.maximum(chosen[0], chosen[1])
    raised = [jnp.exp(c - largest) for c in chosen]
    gates = [r / (raised[0] + raised[1]) for r in raised]
    grad = cot[...].astype(F32)
    pair_grad = jnp.concatenate([(g * grad).astype(BF) for g in gates], axis=0)
    fold_rows(nn(slot_s[...], pair_grad), gs)
    grads_out = Exchange(spot, gs, gr, a2a_send.at[1], a2a_recv.at[1])
    grads_out.start()
    gate_w.forward()
    up_w.forward()
    mixers.forward()

    for part_w in (sg_w, su_w):
        part_w.third()
    for part_w in (sg_w, su_w, cot_w, mixers):
        part_w.finish()
    rows_all = m4[...].reshape(4 * rows, width)
    grad_all = cot4[...].reshape(4 * rows, width)
    gate_part, up_part = nn(rows_all, sg_all[...]), nn(rows_all, su_all[...])
    act, slope = swish(gate_part)
    shared_hidden = (act * up_part).astype(BF)
    sh_send[...] = nn(shared_hidden, sd[...]).astype(BF).reshape(4, rows, width)
    mixed_out[...] = mixed[...].astype(BF).T
    save(mixed_out, mixed_hbm)
    query_x = aside(qc.at[1 - spot.x], q_land)
    shared_out = Merge(spot, sh_send, sh_recv, sems)
    hid_grad = nt(grad_all, sd[...])
    grad_gate = (hid_grad * up_part * slope).astype(BF)
    grad_up = (hid_grad * act).astype(BF)
    back = nt(grad_gate, sg_all[...]) + nt(grad_up, su_all[...])
    gm_send[...] = back.astype(BF).reshape(4, rows, width)
    shared_out.forward()
    shared_back = Merge(spot, gm_send, gm_recv, sems)
    half = shard // 2
    for at, values in ((0, tn(rows_all, grad_gate)), (half, tn(rows_all, grad_up))):
        values = values.astype(BF)
        for r in range(ranks):
            down, left = half * (r // 4), 128 * (r % 4)
            for w in range(4):
                dsh[r, shard * w + at : shard * w + at + half] = values[
                    shard * w + down : shard * w + down + half, left : left + 128
                ]
    values = tn(shared_hidden, grad_all).astype(BF)
    deep = values.shape[0] // ranks
    for r in range(ranks):
        for t in range(width // 128):
            dsh[r, width + deep * t : width + deep * (t + 1)] = values[
                deep * r : deep * (r + 1), 128 * t : 128 * (t + 1)
            ]
    shared_back.forward()
    shared_grad = Reduce(spot, dsh, dsh_x, dsh_z, None, sem_sh)
    for number in (3, 2):
        shared_grad.side(number)

    for part_w in (gate_w, up_w):
        part_w.finish()
    rows_out.finish()
    x_s[...] = unfold_rows(xr, slots)
    block = 512

    def parts(i):
        return pl.ds(pl.multiple_of(block * i, block), block)

    def up_step(i, carry):
        at = parts(i)
        gate = nn(x_s[...], wg[:, at])
        up = nn(x_s[...], wu[:, at])
        act, slope = swish(gate)
        hid_s[:, at] = (act * up).astype(BF)
        gate_s[:, at] = up * slope
        up_s[:, at] = act
        return carry

    lax.fori_loop(0, hidden // block, up_step, 0)
    for part_w in down_w:
        part_w.forward()
    for part_w in down_w:
        part_w.finish()
    sum_s[...] = nt(hid_s[...], wd[...])
    rows_out.drain()
    fold_rows(sum_s[...], xs)
    outs = Exchange(spot, xs, orr, a2a_send.at[2], a2a_recv.at[2])
    outs.start()
    grads_out.finish()
    g_s[...] = unfold_rows(gr, slots)

    def down_step(i, carry):
        at = parts(i)
        grad_hidden = nn(g_s[...], wd[:, at])
        dgate_s[:, at] = (grad_hidden * gate_s[:, at]).astype(BF)
        dup_s[:, at] = (grad_hidden * up_s[:, at]).astype(BF)
        return carry

    lax.fori_loop(0, hidden // block, down_step, 0)
    sum_s[...] = nt(dgate_s[...], wg[...]) + nt(dup_s[...], wu[...])
    grads_out.drain()
    fold_rows(sum_s[...], gs)
    backs = Exchange(spot, gs, br, a2a_send.at[3], a2a_recv.at[3])
    backs.start()
    shared_grad.side(1)

    for part_w in [gate_w, up_w] + down_w:
        part_w.drain()
    swaps, across = [], []
    first = 2 * shard // 3
    sources = ((wg, x_s, dgate_s), (wu, x_s, dup_s), (wd, g_s, hid_s))

    def grads_of(a):
        ref, left, right = sources[a]

        def grad_step(i, carry):
            at = parts(i)
            ref[:, at] = tn(left[...], right[:, at]).astype(BF)
            return carry

        lax.fori_loop(0, hidden // block, grad_step, 0)
        for row in range(2):
            src = ref.at[pl.ds(pl.multiple_of(shard * (2 * row + 1 - spot.c), 64), shard)]
            swaps.append(remote(src, cb.at[a, row], sems.new(), sems.new(), spot.core))
            swaps[-1].start()

    def add_mate(a):
        ref = sources[a][0]
        for row in range(2):
            swaps[2 * a + row].wait_recv()

        def add(i, carry):
            for row in range(2):
                at = pl.ds(pl.multiple_of(shard * (2 * row + spot.c) + 16 * i, 16), 16)
                mate = cb[a, row, pl.ds(pl.multiple_of(16 * i, 16), 16)].astype(F32)
                ref[at] = (ref[at].astype(F32) + mate).astype(BF)
            return carry

        lax.fori_loop(0, shard // 16, add, 0)
        start = pl.multiple_of(shard * spot.across[1], 64)
        keep = ref.at[pl.ds(pl.multiple_of(shard * spot.w, 64), shard)]
        saves.append(pltpu.make_async_copy(keep, keep_out.at[a], sems.new()))
        saves[-1].start()
        if a == 0:
            across.append(
                remote(ref.at[pl.ds(start, first)], other_out, sems.new(), sems.new(), spot.across)
            )
            across[-1].start()
            give = ref.at[pl.ds(pl.multiple_of(start + first, 64), shard - first)]
            there = give_out.at[0, pl.ds(first, shard - first)]
        else:
            give, there = ref.at[pl.ds(start, shard)], give_out.at[a]
        saves.append(pltpu.make_async_copy(give, there, sems.new()))
        saves[-1].start()

    shared_grad.meet(3, True)
    grads_of(0)
    grads_of(1)
    add_mate(0)
    shared_grad.meet(2, True)
    grads_of(2)
    add_mate(1)
    add_mate(2)
    total = second + shared_out.finish()
    grad_mixer = shared_back.finish()
    outs.finish()
    pair_out = nn(pair_s[...], unfold_rows(orr, slots))
    pair_out = [pair_out[:rows], pair_out[rows:]]
    result_out[...] = (total + gates[0] * pair_out[0] + gates[1] * pair_out[1]).astype(BF)
    save(result_out, result_hbm)
    grad_gates = [jnp.sum(grad * p, axis=1, keepdims=True) for p in pair_out]
    inner = gates[0] * grad_gates[0] + gates[1] * grad_gates[1]
    grad_logits = jnp.zeros_like(logits)
    for j in range(2):
        grad_logits += jnp.where(matches[j], gates[j] * (grad_gates[j] - inner), 0.0)
    pieces = split_three(grad_logits)
    router_grad = sum(tn(piece, mixer) for piece in pieces)
    grad_mixer = grad_mixer + sum(nn(piece, router) for piece in pieces)
    shared_grad.meet(1, False)
    backs.finish()
    grad_mixer = grad_mixer + nn(pair_s[:rows] + pair_s[rows:], unfold_rows(br, slots))
    weighted = grad_mixer * pack_all[1:2]
    mean = jnp.mean(weighted * second, axis=-1, keepdims=True)
    grad_second = grad + scale * weighted - second * (scale * scale * scale * mean)
    grad_second_out[...] = grad_second
    save(grad_second_out, grad_second_hbm)

    grad_mixed = nt(grad_second.astype(BF), wbuf[3]).astype(BF)
    half = width // 2
    group = half // PAIR
    for x in range(2):
        gm[x] = grad_mixed[:, half * x : half * (x + 1)]
    grads_x = aside(gm.at[1 - spot.x], gm_land)
    product = grad_mixed.astype(F32) * mixed[...]
    lane = lax.broadcasted_iota(jnp.int32, (2 * rows, PAIR), 1)
    mine = jnp.zeros((2 * rows, PAIR), F32)
    theirs = jnp.zeros((2 * rows, PAIR), F32)
    for i in range(group):
        delta = [
            jnp.sum(stack_pair(product[:, PAIR * j : PAIR * (j + 1)]), axis=1, keepdims=True)
            for j in (i, group + i)
        ]
        swap = spot.x == 1
        mine = jnp.where(lane == i, top[group * spot.x + i], mine)
        theirs = jnp.where(lane == i, top[group * (1 - spot.x) + i], theirs)
        mine = jnp.where(lane == group + i, jnp.where(swap, delta[1], delta[0]), mine)
        theirs = jnp.where(lane == group + i, jnp.where(swap, delta[0], delta[1]), theirs)
        qx[i] = stack_pair(qc[spot.x, :, PAIR * i : PAIR * (i + 1)])
        gx[i] = stack_pair(gm[spot.x, :, PAIR * i : PAIR * (i + 1)])
    stat[...] = theirs.T[0:8]
    stat_x = aside(stat, stat_land)
    stats_out[0] = mine
    gain_grad = jnp.sum(grad_mixer * second * scale, axis=0, keepdims=True)
    pack_grad_out[...] = jnp.concatenate(
        [jnp.zeros_like(gain_grad), gain_grad, router_grad[:14]], axis=0
    )
    query_x.wait_recv()
    grads_x.wait_recv()
    for i in range(group):
        qx[group + i] = stack_pair(q_land[:, PAIR * i : PAIR * (i + 1)])
        gx[group + i] = stack_pair(gm_land[:, PAIR * i : PAIR * (i + 1)])
    stat_x.wait_recv()
    stats_out[1] = jnp.concatenate(
        [stat_land[...], jnp.zeros((PAIR - 8, 2 * rows), F32)], axis=0
    ).T
    for number in (3, 2):
        shared_grad.absorb(number)
    for plane in range(4):
        save(dsh.at[2 * plane + spot.x], dsh_out.at[plane])
    save(dsh.at[2 * spot.z + 1 - spot.x], side_out)
    for src, dst in (
        (qx, qx_out),
        (gx, gx_out),
        (stats_out, stats_hbm),
        (pack_grad_out, pack_grad_hbm),
    ):
        save(src, dst)
    for copy in across:
        copy.wait_recv()
    for part_w in (params, key_w, value_w, query_w, out_w, sg_w, su_w, cot_w, ring, mixers):
        part_w.drain()
    for part_w in (outs, backs, shared_out, shared_back, shared_grad):
        part_w.drain()
    for copy in swaps + across + asides:
        copy.wait_send()
    for copy in saves:
        copy.wait()


def run_forward(
    tok, gain_one, gain_two, router, freq, deal, cot, routes, order, sd,
    wq, wk, wv, wo, sg, su, eg, eu, ed,
):
    rows, width = tok.shape
    pairs = width // PAIR
    ranks, slots = 8, 40
    hidden = eg.shape[1]
    part = sg.shape[1] // 4
    shard = width // 4
    total = ranks * slots
    tall = width + part * width // (128 * ranks)
    any_, vm = pl.BlockSpec(memory_space=pl.ANY), pl.BlockSpec(memory_space=VMEM)
    shape = jax.ShapeDtypeStruct

    def low(*dims):
        return VMEM(dims, BF)

    def full(*dims):
        return VMEM(dims, F32)

    dma = pltpu.SemaphoreType.DMA
    folded = low(ranks, slots * width // 128, 128)
    return pl.pallas_call(
        forward_kernel,
        out_shape=(
            shape((2, rows, PAIR), F32),
            shape((2, rows, PAIR), F32),
            shape((1, ranks * rows), jnp.int32),
            shape((2, 2 * rows, 1), jnp.int32),
            shape((pairs, 2 * rows, PAIR), BF),
            shape((pairs, 2 * rows, PAIR), BF),
            shape((2, 2 * rows, PAIR), F32),
            shape((width, rows), BF),
            shape((width, rows), BF),
            shape((16, width), F32),
            shape((rows, width), BF),
            shape((rows, width), F32),
            shape((16, width), F32),
            shape((4, tall, 128), BF),
            shape((tall, 128), BF),
            shape((ranks, rows, 2 * width), BF),
            shape((4, width, width), BF),
            shape((3, shard, hidden), BF),
            shape((3, shard, hidden), BF),
            shape((2 * shard // 3, hidden), BF),
        ),
        in_specs=[vm] * 5 + [pl.BlockSpec(memory_space=pltpu.SMEM)] + [vm] * 4 + [any_] * 9,
        out_specs=tuple([any_] * 20),
        scratch_shapes=[
            full(2, rows, PAIR),
            full(2, rows, PAIR),
            VMEM((1, ranks * rows), jnp.int32),
            VMEM((2, 2 * rows, 1), jnp.int32),
            low(pairs, 2 * rows, PAIR),
            low(pairs, 2 * rows, PAIR),
            full(2, 2 * rows, PAIR),
            low(width, rows),
            low(width, rows),
            full(16, width),
            low(rows, width),
            full(rows, width),
            full(16, width),
            low(4, width, width),
            low(ranks, rows, 2 * width),
            low(pairs, 2 * rows, PAIR),
            low(2, rows, width // 2),
            low(rows, width // 2),
            low(2, rows, width // 2),
            low(rows, width // 2),
            full(8, 2 * rows),
            full(8, 2 * rows),
            full(rows, width),
            low(16, width),
            low(4, 16, width),
            full(pairs, 2 * rows, PAIR),
            full(pairs, 2 * rows, PAIR),
            full(pairs, 2 * rows, PAIR),
            low(width, part),
            low(width, part),
            low(width, hidden),
            low(width, hidden),
            low(width, hidden),
            low(rows, width),
            low(4, rows, width),
            low(4, rows, width),
            low(4, rows, width),
            low(3, rows, width),
            low(4, rows, width),
            low(3, rows, width),
            *[folded] * 6,
            low(total, width),
            low(total, width),
            full(total, width),
            full(total, hidden),
            full(total, hidden),
            low(total, hidden),
            low(total, hidden),
            low(total, hidden),
            low(ranks, tall, 128),
            low(4, tall, 128),
            low(4, tall, 128),
            low(total, 2 * rows),
            low(2 * rows, total),
            low(3, 2, shard, hidden),
            dma((SEMS_FORWARD,)),
            dma((4 * ranks,)),
            dma((44,)),
            dma((4, ranks)),
            dma((4, ranks)),
            dma((4, 4)),
        ],
        compiler_params=pltpu.CompilerParams(
            collective_id=1, has_side_effects=True, vmem_limit_bytes=VMEM_BYTES
        ),
    )(
        tok, gain_one, gain_two, router, freq, deal, cot, routes, order, sd,
        wq, wk, wv, wo, sg, su, eg, eu, ed,
    )


def backward_kernel(
    grad_second_hbm, tok_hbm, pack_hbm, pack_grad_hbm, n_t_hbm, m_t_hbm, qx_hbm, gx_hbm, stats_hbm,
    cosr_hbm, sinr_hbm, kb_hbm, qb_hbm, side_ref, dsh_ref, kv_ref, wfull_ref, give_ref, other_ref,
    grad_input_out, pack_out, att1_out, att2_out, sh_out, other_out,
    grad_second_ref, tok, pack_ref, pack_grad_ref, n_t, m_t, qx, gx, stats, cosr, sinr, kb, qb,
    w_half, kv, kvb, kv_zo, kv_zi, kv_sum, dq, ga, ga4, gq, gq4, gkv, gkv4, n_all, m_all, pk, pk4,
    o_send, o_land, gn_send, gn_land, a1, a1_zo, a1_zi, a1_sum, a2, a2_zo, a2_zi, a2_sum, r1, r2,
    sh, sh_land, sh_zo, sh_zi, sh_sum, sh_chunk, r3,
    sem, sem_kv, sem_a1, sem_a2, sem_sh, ring_recv, ring_send,
):
    spot = Spot(4)
    sems = Sems(sem)
    rows, width = tok.shape
    half = width // 2
    group = half // PAIR
    shard = width // 4
    mine = pl.ds(pl.multiple_of(half * spot.x, half), half)
    values = pl.ds(pl.multiple_of(width + half * spot.x, half), half)
    ranks = kv.shape[0]
    inputs = []
    for src, dst in (
        (grad_second_hbm, grad_second_ref),
        (dsh_ref, sh),
        (qx_hbm, qx),
        (gx_hbm, gx),
        (stats_hbm, stats),
        (kb_hbm, kb),
        (qb_hbm, qb),
        (n_t_hbm, n_t),
        (m_t_hbm, m_t),
        (cosr_hbm, cosr),
        (sinr_hbm, sinr),
        (tok_hbm, tok),
        (pack_hbm, pack_ref),
        (pack_grad_hbm, pack_grad_ref),
    ):
        inputs.append(pltpu.make_async_copy(src, dst, sems.new()))
        inputs[-1].start()
    loads = [
        pltpu.make_async_copy(kv_ref.at[:, :, mine], kv.at[:, :, pl.ds(0, half)], sems.new()),
        pltpu.make_async_copy(kv_ref.at[:, :, values], kv.at[:, :, pl.ds(half, half)], sems.new()),
        *[
            pltpu.make_async_copy(wfull_ref.at[i, :, mine], w_half.at[i], sems.new())
            for i in range(3)
        ],
    ]
    done = other_ref.shape[0]
    loads.append(pltpu.make_async_copy(other_ref, other_out.at[0, pl.ds(0, done)], sems.new()))
    for copy in loads:
        copy.start()

    def block(ref, w):
        return ref.at[pl.ds(pl.multiple_of(shard * w, 64), shard)]

    greet((spot.core, spot.across, spot.corner, spot.column, spot.inner), (spot.mid, spot.outer))
    asides = []

    def aside(src, dst):
        asides.append(remote(src, dst, sems.new(), sems.new(), spot.column))
        asides[-1].start()
        return asides[-1]

    shared_x = aside(side_ref, sh_land)
    inputs[0].wait()
    grad_second = grad_second_ref[...]
    ga[...] = grad_second.astype(BF)
    grads_w = Gather(spot, ga, lambda w: ga4.at[w], sems)
    for copy in inputs[1:]:
        copy.wait()
    shared = Reduce(spot, sh, None, sh_zo, sh_zi, sem_sh, folded=True, parts=2)
    shared.launch(1)
    shared.relay(3, settled=True)
    shared.relay(2, settled=True)

    def columns(ref):
        return lambda w: ref.at[:, pl.ds(pl.multiple_of(rows * w, 128), rows)]

    normed_w = Spread(spot, lambda w: block(n_t, w), columns(n_all.at[spot.x]), sems)
    mixed_w = Spread(spot, lambda w: block(m_t, w), columns(m_all), sems)
    across = []

    def send_across(src, dst):
        across.append(remote(src, dst, sems.new(), sems.new(), spot.across))
        across[-1].start()

    def send_give(a, start, count):
        at = pl.ds(start, count)
        send_across(give_ref.at[a, at], other_out.at[a, at])

    third = shard // 3
    send_give(1, 0, third)
    dq[...] = jnp.zeros_like(dq)
    loads[0].wait()
    loads[1].wait()

    def chunk(number):
        plane = spot.plane(number)
        k_block = kb[:, pl.ds(pl.multiple_of(2 * rows * plane, 2 * rows), 2 * rows)]
        allowed = [k_block <= qb[spot.x], k_block <= qb[1 - spot.x]]

        for i in range(group):
            lane = PAIR * i
            both = pl.ds(2 * plane, 2)
            key = kv[both, :, pl.ds(lane, PAIR)].reshape(2 * rows, PAIR)
            value = kv[both, :, pl.ds(half + lane, PAIR)].reshape(2 * rows, PAIR)
            grad_key = jnp.zeros((2 * rows, PAIR), F32)
            grad_value = jnp.zeros((2 * rows, PAIR), F32)
            for owner in range(2):
                j = group * owner + i
                stat = stats[owner]
                query, grad = qx[j], gx[j]
                raised = jnp.exp(nt(query, key) - stat[:, i : i + 1])
                probs = jnp.where(allowed[owner], raised, 0.0)
                inner = nt(grad, value) - stat[:, group + i : group + i + 1]
                grad_scores = (probs * inner * HD**-0.5).astype(BF)
                dq[j] += nn(grad_scores, key)
                grad_key += tn(grad_scores, query)
                grad_value += tn(probs.astype(BF), grad)
            kvb[plane, :, pl.ds(lane, PAIR)] = (grad_key * HD**0.5).astype(BF)
            kvb[plane, :, pl.ds(half + lane, PAIR)] = grad_value.astype(BF)

    kv_grad = Reduce(spot, kvb, None, kv_zo, kv_zi, sem_kv, folded=True, parts=2)
    chunk(3)
    kv_grad.launch(3)
    chunk(2)
    kv_grad.launch(2)
    chunk(1)
    kv_grad.launch(1)
    normed_w.finish()
    normed_x = aside(n_all.at[spot.x], n_all.at[spot.x])
    shared.relay(1)
    kv_grad.relay(3, parts=(0,))
    chunk(0)
    for owner in range(2):
        at = spot.x if owner == 0 else 1 - spot.x
        parts = [unstack_pair(dq[group * owner + i]) for i in range(group)]
        gq[at] = turn(jnp.concatenate(parts, axis=1), cosr[at], -sinr[at]).astype(BF)
    query_w = Gather(spot, gq, lambda w: gq4.at[w], sems)
    grads_w.forward()
    mixed_w.finish()
    grads_w.finish()
    out_grad = nn(m_all[...], ga4[...].reshape(4 * rows, width)).astype(BF)
    for x in range(2):
        o_send[x] = out_grad[:, half * x : half * (x + 1)]
    out_x = aside(o_send.at[1 - spot.x], o_land)
    shared_x.wait_recv()
    sh[spot.z] = (sh[spot.z].astype(F32) + sh_land[...].astype(F32)).astype(BF)
    shared.last(sh_sum)
    kv_grad.relay(3, parts=(1,))
    sh_chunk[...] = sh_sum[...].astype(BF)
    part = 2 * shard // 2

    def piece(w):
        return sh_chunk.at[pl.ds(pl.multiple_of(part * w, 64), part)]

    def place(w):
        return r3.at[spot.k, pl.ds(pl.multiple_of(part * w, 64), part)]

    shared_w = Spread(spot, piece, place, sems)
    rest = sh_chunk.shape[0] - 4 * part
    r3[spot.k, pl.ds(4 * part, rest)] = sh_chunk[pl.ds(4 * part, rest)]
    send_give(1, third, shard - third)
    kv_grad.relay(2, parts=(0,))
    kv_grad.relay(1, parts=(0,))
    shared_w.finish()
    ring3 = Ring(spot, r3, ring_recv, ring_send, parts=2)
    ring3.start(only=0)
    kv_grad.relay(2, parts=(1,))
    kv_grad.relay(1, parts=(1,))
    ring3.start(only=1)
    for copy in loads[2:5]:
        copy.wait()
    flat = gq[...].reshape(2 * rows, half)
    grad_normed = nt(flat, w_half[0])
    query_w.forward()
    query_w.finish()
    normed_x.wait_recv()

    def weight_grad(grads4):
        total = nn(n_all[0], grads4[:, 0].reshape(4 * rows, grads4.shape[3]))
        return total + nn(n_all[1], grads4[:, 1].reshape(4 * rows, grads4.shape[3]))

    query_grad = weight_grad(gq4).astype(BF)
    out_x.wait_recv()
    out_half = (o_send[spot.x].astype(F32) + o_land[...].astype(F32)).astype(BF)
    size = shard // 4
    for plane in range(4):
        at = slice(size * plane, size * (plane + 1))
        a1[plane, :, 0:half] = out_half[at]
        a1[plane, :, half:width] = query_grad[at]
    first = Reduce(spot, a1, None, a1_zo, a1_zi, sem_a1, folded=True)
    for number in (3, 2, 1):
        first.launch(number)
    kv_w = []
    for r in range(2):
        at = slice(rows * r, rows * (r + 1))
        kv_grad.last(kv_sum, parts=(r,))
        gkv[r, :, 0:half] = turn(kv_sum[at, 0:half], cosr[r], -sinr[r]).astype(BF)
        gkv[r, :, half:width] = kv_sum[at, half:width].astype(BF)
        kv_w.append(Gather(spot, gkv.at[r], lambda w, r=r: gkv4.at[w, r], sems))
    flat = gkv[...].reshape(2 * rows, width)
    grad_normed = grad_normed + nt(flat[:, 0:half], w_half[1]) + nt(flat[:, half:width], w_half[2])
    gn_send[...] = grad_normed.astype(BF).reshape(2, rows, width)
    normed_grad_x = aside(gn_send.at[1 - spot.x], gn_land)
    ring3.step(1, only=0)
    ring3.step(2, only=1)
    ring3.step(1, only=1)
    first.relay(3)
    first.relay(2)
    for part_w in kv_w:
        part_w.forward()
    for part_w in kv_w:
        part_w.finish()
    both = weight_grad(gkv4).astype(BF)
    for plane in range(4):
        a2[plane] = both[size * plane : size * (plane + 1)]
    second = Reduce(spot, a2, None, a2_zo, a2_zi, sem_a2, folded=True)
    for number in (3, 2, 1):
        second.launch(number)
    first.relay(1)
    ring3.step(2, only=0)
    second.relay(3)
    second.relay(2)
    second.relay(1)
    ring3.step(3, only=1)
    normed_grad_x.wait_recv()
    grad_normed = gn_send[spot.x].astype(F32) + gn_land[...].astype(F32)
    inputs = tok[...].astype(F32)
    scale = lax.rsqrt(jnp.mean(inputs * inputs, axis=-1, keepdims=True) + EPS)
    weighted = grad_normed * pack_ref[0:1]
    mean = jnp.mean(weighted * inputs, axis=-1, keepdims=True)
    grad_input_out[...] = (
        grad_second + scale * weighted - inputs * (scale * scale * scale * mean)
    )
    gain_grad = jnp.sum(grad_normed * inputs * scale, axis=0, keepdims=True)
    pk[...] = jnp.concatenate([gain_grad, pack_grad_ref[1:16]], axis=0).astype(BF)
    pack_w = Gather(spot, pk, lambda w: pk4.at[w], sems)
    send_give(0, done, shard - done)
    send_give(2, 0, shard)
    first.last(a1_sum)
    r1[spot.k] = a1_sum[...].astype(BF)
    ring1 = Ring(spot, r1, ring_recv, ring_send, first=(16, 28))
    ring1.start()
    pack_w.forward()
    pack_w.finish()
    extra = sum(pk4[w].astype(F32) for w in range(4)).astype(BF)
    second.last(a2_sum)
    r2[spot.k, 0:size] = a2_sum[...].astype(BF)
    r2[spot.k, size : size + 16] = extra
    ring2 = Ring(spot, r2, ring_recv, ring_send, first=(24, 39))
    ring2.start()
    ring3.step(3, only=0)
    ring1.step(1)
    ring1.step(2, only=1)
    ring1.step(3, only=1)
    ring1.step(2, only=0)
    ring1.step(3, only=0)
    ring2.step(1)
    ring2.step(2)
    ring2.step(3)
    saves = []
    for ring, src, dst in ((ring3, r3, sh_out), (ring1, r1, att1_out), (ring2, r2, att2_out)):
        for number in range(4):
            ring.other(number)
        saves.append(pltpu.make_async_copy(src, dst, sems.new()))
        saves[-1].start()
    total = jnp.zeros(pk.shape, F32)
    for r in range(ranks):
        total = total + r2[r, size : size + 16].astype(F32)
    pack_out[...] = total
    for copy in across:
        copy.wait_recv()
    for copy in across + asides:
        copy.wait_send()
    for part_w in [grads_w, normed_w, mixed_w, query_w, shared_w, pack_w] + kv_w:
        part_w.drain()
    for part_w in (shared, kv_grad, first, second, ring1, ring2, ring3):
        part_w.drain()
    for copy in saves + loads[5:]:
        copy.wait()


def run_backward(
    grad_second, tok, pack, pack_grad, n_t, m_t, qx, gx, stats, cosr, sinr, kb, qb, side, dsh, kv,
    wfull,
    give, other,
):
    rows, width = tok.shape
    pairs = width // PAIR
    half = width // 2
    ranks = 8
    shard, hidden = width // 4, give.shape[2]
    size = shard // 4
    tall = dsh.shape[1]
    any_, vm = pl.BlockSpec(memory_space=pl.ANY), pl.BlockSpec(memory_space=VMEM)
    shape = jax.ShapeDtypeStruct

    def low(*dims):
        return VMEM(dims, BF)

    def full(*dims):
        return VMEM(dims, F32)

    dma = pltpu.SemaphoreType.DMA
    return pl.pallas_call(
        backward_kernel,
        out_shape=(
            shape((rows, width), F32),
            shape(pack.shape, F32),
            shape((ranks, size, width), BF),
            shape((ranks, size + 16, width), BF),
            shape((ranks, tall, 128), BF),
            shape((3, shard, hidden), BF),
        ),
        in_specs=[any_] * 19,
        out_specs=(vm, vm, any_, any_, any_, any_),
        scratch_shapes=[
            full(rows, width),
            low(rows, width),
            full(16, width),
            full(16, width),
            low(width, rows),
            low(width, rows),
            low(pairs, 2 * rows, PAIR),
            low(pairs, 2 * rows, PAIR),
            full(2, 2 * rows, PAIR),
            full(2, rows, PAIR),
            full(2, rows, PAIR),
            VMEM((1, ranks * rows), jnp.int32),
            VMEM((2, 2 * rows, 1), jnp.int32),
            low(3, width, half),
            low(ranks, rows, width),
            low(4, 2 * rows, width),
            low(4, 2 * rows, width),
            low(4, 2 * rows, width),
            full(2 * rows, width),
            full(pairs, 2 * rows, PAIR),
            low(rows, width),
            low(4, rows, width),
            low(2, rows, half),
            low(4, 2, rows, half),
            low(2, rows, width),
            low(4, 2, rows, width),
            low(2, shard, 4 * rows),
            low(shard, 4 * rows),
            low(16, width),
            low(4, 16, width),
            low(2, shard, half),
            low(shard, half),
            low(2, rows, width),
            low(rows, width),
            low(4, size, width),
            low(4, size, width),
            low(4, size, width),
            full(size, width),
            low(4, size, width),
            low(4, size, width),
            low(4, size, width),
            full(size, width),
            low(ranks, size, width),
            low(ranks, size + 16, width),
            low(4, tall, 128),
            low(tall, 128),
            low(4, tall, 128),
            low(4, tall, 128),
            full(tall, 128),
            low(tall, 128),
            low(ranks, tall, 128),
            dma((SEMS_BACKWARD,)),
            dma((3, 8)),
            dma((3, 4)),
            dma((3, 4)),
            dma((3, 8)),
            dma((4 * ranks,)),
            dma((SEMS_RINGS,)),
        ],
        compiler_params=pltpu.CompilerParams(
            collective_id=3, has_side_effects=True, vmem_limit_bytes=VMEM_BYTES
        ),
    )(
        grad_second, tok, pack, pack_grad, n_t, m_t, qx, gx, stats, cosr, sinr, kb, qb, side, dsh, kv,
        wfull, give, other,
    )


def unpack_kernel(
    result, grad_input, pack, att1, att2, sh, keep, other,
    result_out, grad_input_out, gain_one, gain_two, router,
    query, key, value, output, gate, up, down, eg, eu, ed,
):
    i = pl.program_id(0)
    result_out[...] = result[...]
    grad_input_out[...] = grad_input[...]
    half = query.shape[1] // 2
    size = query.shape[0]
    for x in range(2):
        lanes = slice(half * x, half * (x + 1))
        for ref, src, low in ((output, att1, 0), (query, att1, 1), (key, att2, 0), (value, att2, 1)):
            ref[:, lanes] = src[0, x, 0:size, half * low : half * (low + 1)].astype(F32)
    for a, ref in enumerate((eg, eu, ed)):
        ref[...] = keep[a].astype(F32) + other[a].astype(F32)
    size = gate.shape[0]
    shard = 4 * size
    width = 4 * shard
    within = lax.rem(i, 2) * size
    for c in range(4):
        for w in range(4):
            lanes = slice(512 * w + 128 * c, 512 * w + 128 * (c + 1))
            start = pl.multiple_of(shard * w + within, 16)
            gate[:, lanes] = sh[c, pl.ds(start, size)].astype(F32)
            start = pl.multiple_of(shard * w + shard // 2 + within, 16)
            up[:, lanes] = sh[c, pl.ds(start, size)].astype(F32)
    deep = down.shape[0] // 2
    for r in range(2):
        for t in range(width // 128):
            at = slice(width + deep * t, width + deep * (t + 1))
            down[deep * r : deep * (r + 1), 128 * t : 128 * (t + 1)] = sh[2 * lax.rem(i, 2) + r, at].astype(F32)

    @pl.when(i == 0)
    def _():
        back = lax.rem(4 - lax.axis_index("wt"), 4) * shard
        mine = pltpu.roll(pack[...], back, 1)[:, 0:256]
        gain_one[...] = mine[0:1, 0:shard]
        gain_two[...] = mine[1:2, 0:shard]
        router[...] = mine[2 : 2 + router.shape[0], 0:shard]


def run_unpack(result, grad_input, pack, att1, att2, sh, keep, other, experts):
    rows, width = result.shape
    shard, hidden = keep.shape[1:]
    steps = 4
    shape = jax.ShapeDtypeStruct
    size = shard // steps
    att1 = att1.reshape(4, 2, size, width)
    att2 = att2.reshape(4, 2, size + 16, width)
    shared_hidden = sh.shape[0] * (sh.shape[1] - width) * 128 // width
    shared = 4 * shared_hidden
    by_rows = lambda r, c: pl.BlockSpec((r, c), lambda i: (i, 0))
    whole = lambda *dims: pl.BlockSpec(dims, lambda i: (0,) * len(dims))
    stack = lambda n, r, c: pl.BlockSpec((n, r, c), lambda i: (0, i, 0))
    att = lambda r: pl.BlockSpec((1, 2, r, width), lambda i: (i, 0, 0, 0))
    return pl.pallas_call(
        unpack_kernel,
        grid=(steps,),
        out_shape=(
            shape((rows, width), BF),
            shape((rows, width), F32),
            shape((1, shard), F32),
            shape((1, shard), F32),
            shape((experts, shard), F32),
            *[shape((shard, width), F32)] * 4,
            *[shape((shard, shared), F32)] * 2,
            shape((shared_hidden, width), F32),
            *[shape((shard, hidden), F32)] * 3,
        ),
        in_specs=[
            by_rows(rows // steps, width),
            by_rows(rows // steps, width),
            whole(*pack.shape),
            att(size),
            att(size + 16),
            pl.BlockSpec((4,) + sh.shape[1:], lambda i: (i // 2, 0, 0)),
            stack(3, size, hidden),
            stack(3, size, hidden),
        ],
        out_specs=(
            by_rows(rows // steps, width),
            by_rows(rows // steps, width),
            whole(1, shard),
            whole(1, shard),
            whole(experts, shard),
            *[by_rows(size, width)] * 4,
            *[by_rows(size, shared)] * 2,
            by_rows(shared_hidden // steps, width),
            *[by_rows(size, hidden)] * 3,
        ),
        compiler_params=pltpu.CompilerParams(vmem_limit_bytes=VMEM_BYTES),
    )(result, grad_input, pack, att1, att2, sh, keep, other)


def contract_product(left, right, left_dim, right_dim):
    return lax.dot_general(
        left, right, (((left_dim,), (right_dim,)), ((), ())), preferred_element_type=jnp.float32
    )


def contract_exact(left, right, left_dim, right_dim):
    return lax.dot_general(
        left,
        right,
        (((left_dim,), (right_dim,)), ((), ())),
        precision=HIGH,
        preferred_element_type=jnp.float32,
    )


def rms_norm(values, gain):
    norm_scale = lax.rsqrt(jnp.mean(values * values, axis=-1, keepdims=True) + EPS)
    return (values * norm_scale * gain, norm_scale)


def rms_back(values, norm_scale, gain, upstream):
    weighted = upstream * gain
    inner_mean = jnp.mean(weighted * values, axis=-1, keepdims=True)
    through = norm_scale * weighted - values * norm_scale * norm_scale * norm_scale * inner_mean
    return (through, jnp.sum(upstream * values * norm_scale, axis=0))


def silu_parts(gate_part):
    sigmoid = jax.nn.sigmoid(gate_part)
    return (gate_part * sigmoid, sigmoid * (1.0 + gate_part * (1.0 - sigmoid)))


def rotate(values, place, sign):
    half_size = HD // 2
    frequency = 10000.0 ** (-jnp.arange(half_size, dtype=jnp.float32) / half_size)
    angles = place.astype(jnp.float32)[:, None] * frequency[None, :]
    cosine = jnp.cos(angles)[:, None, :]
    sine_part = sign * jnp.sin(angles)[:, None, :]
    shaped = values.reshape(values.shape[0], values.shape[1] // HD, 2, half_size)
    first_half = shaped[:, :, 0, :]
    second_half = shaped[:, :, 1, :]
    turned = jnp.stack(
        [
            first_half * cosine - second_half * sine_part,
            second_half * cosine + first_half * sine_part,
        ],
        axis=2,
    )
    return turned.reshape(values.shape)


def places(first_row, row_count, block_deal, rows_dev):
    row_index = first_row + jnp.arange(row_count, dtype=jnp.int32)
    owner_rank = row_index // rows_dev
    inner_row = row_index % rows_dev
    ranks = block_deal.shape[0]
    matches = owner_rank[:, None] == jnp.arange(ranks, dtype=jnp.int32)[None, :]
    paired = jnp.sum(jnp.where(matches, block_deal[None, :], 0), axis=1)
    piece_size = rows_dev // 2
    unit_index = jnp.where(inner_row < piece_size, paired, 2 * ranks - 1 - paired)
    return unit_index * piece_size + inner_row % piece_size


def score_block(query_side, key_rows, key_place):
    query3, query_block = query_side
    key3 = key_rows.reshape(key_rows.shape[0], -1, HD)
    raw_scores = jnp.einsum("qhd,khd->hqk", query3, key3, preferred_element_type=jnp.float32)
    allowed = (key_place // BLK)[None, None, :] <= query_block[None, :, None]
    return (jnp.where(allowed, raw_scores * HD ** (-0.5), MASKED), allowed)


def absorb(running, key_rows, value_rows, key_place, query_side):
    largest, denom, accum = running
    scores, allowed = score_block(query_side, key_rows, key_place)
    new_largest = jnp.maximum(largest, jnp.max(scores, axis=2))
    factor = jnp.exp(largest - new_largest)
    raised = jnp.where(allowed, jnp.exp(scores - new_largest[:, :, None]), 0.0)
    denom = denom * factor + jnp.sum(raised, axis=2)
    value3 = value_rows.reshape(value_rows.shape[0], -1, HD)
    accum = accum * factor.T[:, :, None] + jnp.einsum(
        "hqk,khd->qhd", raised.astype(jnp.bfloat16), value3, preferred_element_type=jnp.float32
    )
    return (new_largest, denom, accum)


def fold_keys(running, key_piece, query_side, block_deal, rows_dev):
    key_all, value_all = key_piece
    row_count = key_all.shape[0]
    block_size = KEY_ROWS

    def key_step(current, offset):
        key_rows = lax.dynamic_slice_in_dim(key_all, offset, block_size, 0)
        value_rows = lax.dynamic_slice_in_dim(value_all, offset, block_size, 0)
        key_place = places(offset, block_size, block_deal, rows_dev)
        return (absorb(current, key_rows, value_rows, key_place, query_side), None)

    offsets = jnp.arange(row_count // block_size, dtype=jnp.int32) * block_size
    running, unused = lax.scan(key_step, running, offsets)
    return running


def differentiate(query_side, log_total, delta, grad_out3, key_rows, value_rows, key_place):
    scores, allowed = score_block(query_side, key_rows, key_place)
    probs_full = jnp.where(allowed, jnp.exp(scores - log_total[:, :, None]), 0.0)
    value3 = value_rows.reshape(value_rows.shape[0], -1, HD)
    grad_probs = jnp.einsum("qhd,khd->hqk", grad_out3, value3, preferred_element_type=jnp.float32)
    grad_scores = (probs_full * (grad_probs - delta[:, :, None]) * HD ** (-0.5)).astype(
        jnp.bfloat16
    )
    return (probs_full, grad_scores)


def assign_slots(route, order, experts, capacity):
    pair_count = order.shape[0]
    expert_ids = route.reshape(pair_count)
    ordered = expert_ids[order]
    onehot = (ordered[:, None] == jnp.arange(experts, dtype=jnp.int32)[None, :]).astype(jnp.int32)
    before = jnp.cumsum(onehot, axis=0) - onehot
    slot_turn = jnp.sum(before * onehot, axis=1)
    slot_index = jnp.zeros((pair_count,), jnp.int32).at[order].set(slot_turn)
    kept_pairs = slot_index < capacity
    target = jnp.where(kept_pairs, expert_ids * capacity + slot_index, experts * capacity)
    slot_table = (
        jnp.full((experts * capacity,), pair_count, jnp.int32)
        .at[target]
        .set(jnp.arange(pair_count, dtype=jnp.int32), mode="drop")
    )
    return (target, kept_pairs, slot_table)


def body(
    tokens,
    cotangent,
    gain_attention,
    query_weight,
    key_weight,
    value_weight,
    output_weight,
    gain_mixer,
    router_weight,
    shared_gate,
    shared_up,
    shared_down,
    expert_gate,
    expert_up,
    expert_down,
    routes,
    slot_order,
    block_deal,
):
    rows_dev = tokens.shape[1]
    width = tokens.shape[2]
    ranks = lax.axis_size("ctx")
    (
        gain_one,
        query_full,
        key_full,
        value_full,
        output_full,
        gain_two,
        router_full,
        sgate_full,
        sup_full,
        sdown_full,
        expert_gate_whole,
        expert_up_whole,
        edown_full,
    ) = (
        lax.all_gather(gain_attention, "wt", axis=0, tiled=True),
        lax.all_gather(query_weight, "wt", axis=0, tiled=True),
        lax.all_gather(key_weight, "wt", axis=0, tiled=True),
        lax.all_gather(value_weight, "wt", axis=0, tiled=True),
        lax.all_gather(output_weight, "wt", axis=0, tiled=True),
        lax.all_gather(gain_mixer, "wt", axis=0, tiled=True),
        lax.all_gather(router_weight, "wt", axis=0, tiled=True),
        lax.all_gather(shared_gate, "wt", axis=0, tiled=True),
        lax.all_gather(shared_up, "wt", axis=0, tiled=True),
        lax.all_gather(shared_down, "wt", axis=0, tiled=True),
        lax.all_gather(expert_gate, "wt", axis=0, tiled=True),
        lax.all_gather(expert_up, "wt", axis=0, tiled=True),
        lax.all_gather(expert_down, "wt", axis=0, tiled=True),
    )
    gain_first = gain_one.astype(jnp.float32)
    gain_second = gain_two.astype(jnp.float32)
    heads = width // HD
    inputs = tokens[0].astype(jnp.float32)
    here = places(lax.axis_index("ctx") * rows_dev, rows_dev, block_deal, rows_dev)
    query_side_block = here // BLK
    normed_f, scale_one = rms_norm(inputs, gain_first)
    normed = normed_f.astype(jnp.bfloat16)
    query_rot = rotate(
        jnp.dot(normed, query_full, preferred_element_type=jnp.float32), here, 1.0
    ).astype(jnp.bfloat16)
    key_rot = rotate(
        jnp.dot(normed, key_full, preferred_element_type=jnp.float32), here, 1.0
    ).astype(jnp.bfloat16)
    value_low = jnp.dot(normed, value_full, preferred_element_type=jnp.float32).astype(jnp.bfloat16)
    query3 = query_rot.reshape(rows_dev, heads, HD)
    query_side = (query3, query_side_block)
    start_state = (
        jnp.full((heads, rows_dev), MASKED, jnp.float32),
        jnp.zeros((heads, rows_dev), jnp.float32),
        jnp.zeros((rows_dev, heads, HD), jnp.float32),
    )
    largest, denom, accum = fold_keys(
        start_state,
        (
            lax.all_gather(key_rot, "ctx", axis=0, tiled=True),
            lax.all_gather(value_low, "ctx", axis=0, tiled=True),
        ),
        query_side,
        block_deal,
        rows_dev,
    )
    mixed3 = accum / denom.T[:, :, None]
    log_total = largest + jnp.log(denom)
    mixed_low = mixed3.reshape(rows_dev, width).astype(jnp.bfloat16)
    second = inputs + jnp.dot(mixed_low, output_full, preferred_element_type=jnp.float32)
    mixer_f, scale_two = rms_norm(second, gain_second)
    mixer = mixer_f.astype(jnp.bfloat16)
    experts = router_full.shape[1]
    logits = jnp.dot(mixer, router_full, preferred_element_type=jnp.float32)
    route = routes[0]
    top_count = route.shape[1]
    pair_count = rows_dev * top_count
    capacity = (5 * pair_count + 4 * experts - 1) // (4 * experts)
    split_count = ranks // experts
    expert_match = route[:, :, None] == jnp.arange(experts, dtype=jnp.int32)[None, None, :]
    chosen = jnp.sum(jnp.where(expert_match, logits[:, None, :], 0.0), axis=2)
    gates = jax.nn.softmax(chosen, axis=1)
    target, kept_pairs, slot_table = assign_slots(route, slot_order[0, 0], experts, capacity)
    valid = slot_table < pair_count
    pair_pick = jnp.minimum(slot_table, pair_count - 1)
    target_pick = jnp.minimum(target, experts * capacity - 1)
    send_rows = jnp.where(
        valid[:, None], mixer[pair_pick // top_count], jnp.zeros((), jnp.bfloat16)
    )
    send_rows = jnp.broadcast_to(
        send_rows.reshape(experts, 1, capacity, width), (experts, split_count, capacity, width)
    ).reshape(ranks, capacity, width)
    received = lax.all_to_all(send_rows, "ctx", split_axis=0, concat_axis=0, tiled=True)
    slot_count = received.shape[1]
    flattened_input = received.reshape(ranks * slot_count, width)
    gate_part = jnp.dot(flattened_input, expert_gate_whole, preferred_element_type=jnp.float32)
    up_projection_part = jnp.dot(
        flattened_input, expert_up_whole, preferred_element_type=jnp.float32
    )
    activated, unused = silu_parts(gate_part)
    hidden = (activated * up_projection_part).astype(jnp.bfloat16)
    partial_value = contract_product(hidden, edown_full, 1, 1).reshape(ranks, slot_count, width)
    back = lax.all_to_all(
        partial_value.astype(jnp.bfloat16), "ctx", split_axis=0, concat_axis=0, tiled=True
    ).astype(partial_value.dtype)
    expert_gate_part = gate_part.reshape(ranks, slot_count, -1)
    expert_up_part = up_projection_part.reshape(ranks, slot_count, -1)
    combined = jnp.sum(back.reshape(experts, split_count, capacity, width), axis=1).reshape(
        experts * capacity, width
    )
    pair_out = jnp.where(kept_pairs[:, None], combined[target_pick], 0.0).reshape(
        rows_dev, top_count, width
    )
    mixture = jnp.sum(gates[:, :, None] * pair_out, axis=1)
    sgate_part = jnp.dot(mixer, sgate_full, preferred_element_type=jnp.float32)
    sup_part = jnp.dot(mixer, sup_full, preferred_element_type=jnp.float32)
    shared_act, shared_slope = silu_parts(sgate_part)
    shared_hidden = (shared_act * sup_part).astype(jnp.bfloat16)
    shared_out = jnp.dot(shared_hidden, sdown_full, preferred_element_type=jnp.float32)
    result = (second + mixture + shared_out).astype(jnp.bfloat16)
    grad_final = cotangent[0].astype(jnp.float32)
    grad_low = grad_final.astype(jnp.bfloat16)
    sdown_grad = contract_product(shared_hidden, grad_low, 0, 0)
    grad_shared_hidden = contract_product(grad_low, sdown_full, 1, 1)
    grad_sgate = (grad_shared_hidden * sup_part * shared_slope).astype(jnp.bfloat16)
    grad_sup = (grad_shared_hidden * shared_act).astype(jnp.bfloat16)
    sgate_grad = contract_product(mixer, grad_sgate, 0, 0)
    sup_grad = contract_product(mixer, grad_sup, 0, 0)
    grad_mixer = contract_product(grad_sgate, sgate_full, 1, 1) + contract_product(
        grad_sup, sup_full, 1, 1
    )
    pair_grad = (
        (gates[:, :, None] * grad_final[:, None, :]).reshape(pair_count, width).astype(jnp.bfloat16)
    )
    grad_gates = jnp.sum(grad_final[:, None, :] * pair_out, axis=2)
    send_grad = jnp.where(valid[:, None], pair_grad[pair_pick], jnp.zeros((), jnp.bfloat16))
    send_grad = jnp.broadcast_to(
        send_grad.reshape(experts, 1, capacity, width), (experts, split_count, capacity, width)
    ).reshape(ranks, capacity, width)
    recv_grad = lax.all_to_all(send_grad, "ctx", split_axis=0, concat_axis=0, tiled=True)
    flattened_input = received.reshape(ranks * capacity, width)
    flat_grad = recv_grad.reshape(ranks * capacity, width)
    gate_flat = expert_gate_part.reshape(ranks * capacity, -1)
    up_flat = expert_up_part.reshape(ranks * capacity, -1)
    expert_activation, expert_slope = silu_parts(gate_flat)
    expert_hidden = (expert_activation * up_flat).astype(jnp.bfloat16)
    edown_grad = contract_product(flat_grad, expert_hidden, 0, 0)
    expert_hidden_grad = jnp.dot(flat_grad, edown_full, preferred_element_type=jnp.float32)
    expert_gate_grad_rows = (expert_hidden_grad * up_flat * expert_slope).astype(jnp.bfloat16)
    expert_up_grad_rows = (expert_hidden_grad * expert_activation).astype(jnp.bfloat16)
    egate_grad = contract_product(flattened_input, expert_gate_grad_rows, 0, 0)
    expert_up_weight_grad = contract_product(flattened_input, expert_up_grad_rows, 0, 0)
    input_back = (
        contract_product(expert_gate_grad_rows, expert_gate_whole, 1, 1)
        + contract_product(expert_up_grad_rows, expert_up_whole, 1, 1)
    ).reshape(ranks, capacity, width)
    back_grad = lax.all_to_all(
        input_back.astype(jnp.bfloat16), "ctx", split_axis=0, concat_axis=0, tiled=True
    ).astype(input_back.dtype)
    merged = jnp.sum(back_grad.reshape(experts, split_count, capacity, width), axis=1).reshape(
        experts * capacity, width
    )
    pair_back = jnp.where(kept_pairs[:, None], merged[target_pick], 0.0).reshape(
        rows_dev, top_count, width
    )
    grad_mixer = grad_mixer + jnp.sum(pair_back, axis=1)
    grad_chosen = gates * (grad_gates - jnp.sum(gates * grad_gates, axis=1, keepdims=True))
    grad_logits = jnp.sum(jnp.where(expert_match, grad_chosen[:, :, None], 0.0), axis=1)
    router_grad = contract_exact(mixer.astype(jnp.float32), grad_logits, 0, 0)
    grad_mixer = grad_mixer + contract_exact(grad_logits, router_full.astype(jnp.float32), 1, 1)
    through_two, gain_two_grad = rms_back(second, scale_two, gain_second, grad_mixer)
    grad_second = grad_final + through_two
    grad_attention = grad_second.astype(jnp.bfloat16)
    output_grad = contract_product(mixed_low, grad_attention, 0, 0)
    grad_mixed = contract_product(grad_attention, output_full, 1, 1).astype(jnp.bfloat16)
    grad_out3 = grad_mixed.reshape(rows_dev, heads, HD)
    delta = jnp.sum(grad_out3.astype(jnp.float32) * mixed3, axis=2).T
    all_keys, all_values = (
        lax.all_gather(key_rot, "ctx", axis=0, tiled=True),
        lax.all_gather(value_low, "ctx", axis=0, tiled=True),
    )
    total_rows = all_keys.shape[0]
    block_size = KEY_ROWS

    def query_step(grad_sum, offset):
        key_rows = lax.dynamic_slice_in_dim(all_keys, offset, block_size, 0)
        value_rows = lax.dynamic_slice_in_dim(all_values, offset, block_size, 0)
        key_place = places(offset, block_size, block_deal, rows_dev)
        unused, grad_scores = differentiate(
            query_side, log_total, delta, grad_out3, key_rows, value_rows, key_place
        )
        key3 = key_rows.reshape(block_size, heads, HD)
        return (
            grad_sum
            + jnp.einsum("hqk,khd->qhd", grad_scores, key3, preferred_element_type=jnp.float32),
            None,
        )

    offsets = jnp.arange(total_rows // block_size, dtype=jnp.int32) * block_size
    grad_query3, unused = lax.scan(
        query_step, jnp.zeros((rows_dev, heads, HD), jnp.float32), offsets
    )
    inner_size = KEY_ROWS

    def one_part(offset):
        key_rows = lax.dynamic_slice_in_dim(all_keys, offset, inner_size, 0)
        value_rows = lax.dynamic_slice_in_dim(all_values, offset, inner_size, 0)
        key_place = places(offset, inner_size, block_deal, rows_dev)
        probs_full, grad_scores = differentiate(
            query_side, log_total, delta, grad_out3, key_rows, value_rows, key_place
        )
        grad_value_rows = jnp.einsum(
            "hqk,qhd->khd",
            probs_full.astype(jnp.bfloat16),
            grad_out3,
            preferred_element_type=jnp.float32,
        )
        grad_key_rows = jnp.einsum(
            "hqk,qhd->khd", grad_scores, query3, preferred_element_type=jnp.float32
        )
        return jnp.concatenate(
            [grad_key_rows.reshape(inner_size, width), grad_value_rows.reshape(inner_size, width)],
            axis=1,
        )

    parts = lax.map(
        one_part,
        jnp.arange(lax.axis_size("ctx") * rows_dev // inner_size, dtype=jnp.int32) * inner_size,
    )
    key_value_grad = lax.psum_scatter(
        parts.reshape(lax.axis_size("ctx") * rows_dev, 2 * width),
        "ctx",
        scatter_dimension=0,
        tiled=True,
    )
    grad_key_pre = rotate(key_value_grad[:, :width], here, -1.0).astype(jnp.bfloat16)
    grad_value_low = key_value_grad[:, width:].astype(jnp.bfloat16)
    grad_query_pre = rotate(grad_query3.reshape(rows_dev, width), here, -1.0).astype(jnp.bfloat16)
    query_grad = contract_product(normed, grad_query_pre, 0, 0)
    key_grad = contract_product(normed, grad_key_pre, 0, 0)
    value_grad = contract_product(normed, grad_value_low, 0, 0)
    grad_normed = (
        contract_product(grad_query_pre, query_full, 1, 1)
        + contract_product(grad_key_pre, key_full, 1, 1)
        + contract_product(grad_value_low, value_full, 1, 1)
    )
    through_one, gain_one_grad = rms_back(inputs, scale_one, gain_first, grad_normed)
    grad_input = grad_second + through_one
    (
        gain_one_share,
        query_share,
        key_share,
        value_share,
        output_share,
        gain_two_share,
        router_share,
        sgate_share,
        sup_share,
        sdown_share,
        egate_share,
        expert_up_portion,
        edown_share,
    ) = (
        lax.psum_scatter(
            gain_one_grad.astype(jnp.bfloat16), "wt", scatter_dimension=0, tiled=True
        ).astype(jnp.float32),
        lax.psum_scatter(
            query_grad.astype(jnp.bfloat16), "wt", scatter_dimension=0, tiled=True
        ).astype(jnp.float32),
        lax.psum_scatter(
            key_grad.astype(jnp.bfloat16), "wt", scatter_dimension=0, tiled=True
        ).astype(jnp.float32),
        lax.psum_scatter(
            value_grad.astype(jnp.bfloat16), "wt", scatter_dimension=0, tiled=True
        ).astype(jnp.float32),
        lax.psum_scatter(
            output_grad.astype(jnp.bfloat16), "wt", scatter_dimension=0, tiled=True
        ).astype(jnp.float32),
        lax.psum_scatter(
            gain_two_grad.astype(jnp.bfloat16), "wt", scatter_dimension=0, tiled=True
        ).astype(jnp.float32),
        lax.psum_scatter(
            router_grad.astype(jnp.bfloat16), "wt", scatter_dimension=0, tiled=True
        ).astype(jnp.float32),
        lax.psum_scatter(
            sgate_grad.astype(jnp.bfloat16), "wt", scatter_dimension=0, tiled=True
        ).astype(jnp.float32),
        lax.psum_scatter(
            sup_grad.astype(jnp.bfloat16), "wt", scatter_dimension=0, tiled=True
        ).astype(jnp.float32),
        lax.psum_scatter(
            sdown_grad.astype(jnp.bfloat16), "wt", scatter_dimension=0, tiled=True
        ).astype(jnp.float32),
        lax.psum_scatter(
            egate_grad.astype(jnp.bfloat16), "wt", scatter_dimension=0, tiled=True
        ).astype(jnp.float32),
        lax.psum_scatter(
            expert_up_weight_grad.astype(jnp.bfloat16), "wt", scatter_dimension=0, tiled=True
        ).astype(jnp.float32),
        lax.psum_scatter(
            edown_grad.astype(jnp.bfloat16), "wt", scatter_dimension=0, tiled=True
        ).astype(jnp.float32),
    )
    (
        gain_one_sum,
        query_sum,
        key_sum,
        value_sum,
        output_sum,
        gain_two_sum,
        router_sum,
        sgate_sum,
        sup_sum,
        sdown_sum,
    ) = lax.psum(
        (
            gain_one_share,
            query_share,
            key_share,
            value_share,
            output_share,
            gain_two_share,
            router_share,
            sgate_share,
            sup_share,
            sdown_share,
        ),
        "ctx",
    )
    return (
        result[None],
        grad_input[None],
        gain_one_sum,
        query_sum,
        key_sum,
        value_sum,
        output_sum,
        gain_two_sum,
        router_sum,
        sgate_sum,
        sup_sum,
        sdown_sum,
        egate_share,
        expert_up_portion,
        edown_share,
    )


def fast_body(
    tokens,
    cotangent,
    gain_attention,
    query_weight,
    key_weight,
    value_weight,
    output_weight,
    gain_mixer,
    router_weight,
    shared_gate,
    shared_up,
    shared_down,
    expert_gate,
    expert_up,
    expert_down,
    routes,
    slot_order,
    block_deal,
):
    half_size = HD // 2
    frequency = 10000.0 ** (-np.arange(half_size) / half_size)
    frequency = jnp.asarray(np.tile(frequency, 4)[None].astype(np.float32))
    (
        cosr, sinr, kb, qb, qx, gx, stats, n_t, m_t, pack_all, result, grad_second, pack_grad, dsh,
        side, kv_all, wfull, keep, give, other,
    ) = run_forward(
        tokens[0], gain_attention, gain_mixer, router_weight.T, frequency, block_deal,
        cotangent[0], routes[0].T, slot_order[0],
        shared_down, query_weight, key_weight, value_weight, output_weight, shared_gate, shared_up,
        expert_gate, expert_up, expert_down,
    )
    grad_input, pack_sum, att1, att2, sh, other = run_backward(
        grad_second, tokens[0], pack_all, pack_grad, n_t, m_t, qx, gx, stats, cosr, sinr, kb, qb,
        side, dsh, kv_all, wfull, give, other,
    )
    (
        result, grad_input, gain_one, gain_two, router, query, key, value, output, gate, up, down,
        eg, eu, ed,
    ) = run_unpack(
        result, grad_input, pack_sum, att1, att2, sh, keep, other, router_weight.shape[1]
    )
    return (
        result[None], grad_input[None], gain_one.reshape(-1), query, key, value, output,
        gain_two.reshape(-1), router.T, gate, up, down, eg, eu, ed,
    )


def solution(mesh):
    in_specs = (
        P("wt", "ctx", None),
        P("wt", "ctx", None),
        P("wt"),
        P("wt", None),
        P("wt", None),
        P("wt", None),
        P("wt", None),
        P("wt"),
        P("wt", None),
        P("wt", None),
        P("wt", None),
        P("wt", None),
        P("wt", "ctx"),
        P("wt", "ctx"),
        P("wt", "ctx"),
        P("wt", "ctx", None),
        P("wt", "ctx", None),
        P(),
    )
    out_specs = (
        P("wt", "ctx", None),
        P("wt", "ctx", None),
        P("wt"),
        P("wt", None),
        P("wt", None),
        P("wt", None),
        P("wt", None),
        P("wt"),
        P("wt", None),
        P("wt", None),
        P("wt", None),
        P("wt", None),
        P("wt", "ctx"),
        P("wt", "ctx"),
        P("wt", "ctx"),
    )
    chosen = fast_body if (mesh.shape["ctx"], mesh.shape["wt"]) == (8, 4) else body
    return jax.shard_map(chosen, mesh=mesh, in_specs=in_specs, out_specs=out_specs, check_vma=False)
```

```python
import jax
import jax.numpy as jnp
import numpy as np
from jax import lax
from jax.experimental import pallas as pl
from jax.experimental.pallas import tpu as pltpu
from jax.sharding import PartitionSpec as P

HD = 64
BLK = 256


EPS = 1e-06
KEY_ROWS = 512
HIGH = lax.Precision.HIGHEST
MASKED = -1e30


MESH = pl.DeviceIdType.MESH
VMEM = pltpu.VMEM
BF = jnp.bfloat16
F32 = jnp.float32
PAIR = 2 * HD
VMEM_BYTES = 127 * 2**19
SEMS_FORWARD = 204
SEMS_BACKWARD = 102
SEMS_RINGS = 48
SEMS_LAYOUT = 34


class Spot:
    def __init__(self, line_size):
        self.k = lax.axis_index("ctx")
        self.w = lax.axis_index("wt")
        self.z, self.x = lax.div(self.k, 2), lax.rem(self.k, 2)
        self.y, self.c = lax.div(self.w, 2), lax.rem(self.w, 2)
        self.far = lax.div(self.z, 2)
        self.mid = self.z + self.far * (3 - 2 * self.z)
        step = 1 - 2 * self.far
        self.core = (self.k, 2 * self.y + 1 - self.c)
        self.across = (self.k, 2 * (1 - self.y) + self.c)
        self.corner = (self.k, 2 * (1 - self.y) + 1 - self.c)
        self.column = (2 * self.z + 1 - self.x, self.w)
        self.odd = lax.rem(self.z, 2)
        self.line = (2 * (self.z + 1 - 2 * self.odd) + self.x, self.w)
        self.inner = (2 * (self.z + step) + self.x, self.w)
        self.outer = (2 * (self.z - step) + self.x, self.w)

    def plane(self, step):
        mirrored = (self.mid, 1 - self.mid, 2, 3)[step]
        return mirrored + self.far * (3 - 2 * mirrored)


class Sems:
    def __init__(self, ref):
        self.ref, self.used = ref, 0

    def new(self):
        self.used += 1
        return self.ref.at[self.used - 1]


def remote(src, dst, send, recv, to):
    return pltpu.make_async_remote_copy(
        src_ref=src, dst_ref=dst, send_sem=send, recv_sem=recv, device_id=to, device_id_type=MESH
    )


def greet(devices, middle=None):
    barrier = pltpu.get_barrier_semaphore()
    for to in devices:
        pl.semaphore_signal(barrier, inc=1, device_id=to, device_id_type=MESH)
    if middle is None:
        pl.semaphore_wait(barrier, len(devices))
        return

    @pl.when(middle[0] == 1)
    def _():
        pl.semaphore_signal(barrier, inc=1, device_id=middle[1], device_id_type=MESH)

    pl.semaphore_wait(barrier, len(devices) + middle[0])


class Gather:
    def __init__(self, spot, src, place, sems, local=True):
        self.spot, self.place, self.sems = spot, place, sems
        here = place(spot.w)
        self.local = pltpu.make_async_copy(src, here, sems.new()) if local else None
        self.to_core = remote(src, here, sems.new(), sems.new(), spot.core)
        self.to_across = remote(src, here, sems.new(), sems.new(), spot.across)
        self.to_across.start()
        self.to_core.start()
        if local:
            self.local.start()

    def forward(self):
        self.to_across.wait_recv()
        part = self.place(self.spot.across[1])
        self.onward = remote(part, part, self.sems.new(), self.sems.new(), self.spot.core)
        self.onward.start()

    def finish(self):
        if self.local is not None:
            self.local.wait()
        self.to_core.wait_recv()
        self.onward.wait_recv()

    def drain(self):
        for copy in (self.to_core, self.to_across, self.onward):
            copy.wait_send()


class Share:
    def __init__(self, spot, src, dst, sems, mate, bit):
        self.spot, self.dst, self.sems, self.mate, self.bit = spot, dst, sems, mate, bit
        self.rows = src.shape[0]
        self.half = self.rows // 2
        here = dst.at[pl.ds(pl.multiple_of(self.rows * spot.w, 64), self.rows)]
        half = pl.ds(pl.multiple_of(self.half * bit, 32), self.half)
        self.local = pltpu.make_async_copy(src, here, sems.new())
        self.to_core = remote(src, here, sems.new(), sems.new(), spot.core)
        self.to_across = remote(
            src.at[half], self.part(spot.w, bit), sems.new(), sems.new(), spot.across
        )
        for copy in (self.to_across, self.to_core, self.local):
            copy.start()

    def part(self, w, bit):
        return self.dst.at[pl.ds(pl.multiple_of(self.rows * w + self.half * bit, 32), self.half)]

    def forward(self):
        spot = self.spot
        self.to_across.wait_recv()
        part = self.part(spot.across[1], self.bit)
        self.aside = remote(part, part, self.sems.new(), self.sems.new(), self.mate)
        self.onward = remote(part, part, self.sems.new(), self.sems.new(), spot.core)
        self.aside.start()
        self.onward.start()

    def second(self):
        self.aside.wait_recv()
        part = self.part(self.spot.across[1], 1 - self.bit)
        self.rest = remote(part, part, self.sems.new(), self.sems.new(), self.spot.core)
        self.rest.start()

    def finish(self):
        self.local.wait()
        self.to_core.wait_recv()
        self.onward.wait_recv()
        self.rest.wait_recv()

    def drain(self):
        for copy in (self.to_core, self.to_across, self.aside, self.onward, self.rest):
            copy.wait_send()


class Quarters:
    def __init__(self, spot, src, dst, sems, columns=False):
        self.spot, self.dst, self.sems, self.columns = spot, dst, sems, columns
        self.rows = src.shape[0]
        self.size = self.rows // 4
        self.q = 2 * spot.x + spot.odd
        self.sources = (spot.across, spot.corner) if columns else (spot.across,)
        cols = dst.shape[1]

        def take(to, quarter):
            at = pl.ds(pl.multiple_of(self.size * self.q, 16), self.size)
            if not columns:
                return src.at[at] if quarter else src
            lanes = pl.ds(pl.multiple_of(cols * to, cols), cols)
            return src.at[at, lanes] if quarter else src.at[:, lanes]

        here = dst.at[pl.ds(pl.multiple_of(self.rows * spot.w, 64), self.rows)]
        self.far = [
            remote(take(to[1], True), self.part(spot.w, self.q), sems.new(), sems.new(), to)
            for to in self.sources
        ]
        self.to_core = remote(take(spot.core[1], False), here, sems.new(), sems.new(), spot.core)
        self.local = pltpu.make_async_copy(take(spot.w, False), here, sems.new())
        for copy in self.far + [self.to_core, self.local]:
            copy.start()
        self.lines, self.sides, self.cores = [], [], []

    def part(self, w, q, count=1):
        start = pl.multiple_of(self.rows * w + self.size * q, 16)
        return self.dst.at[pl.ds(start, self.size * count)]

    def send(self, copies, part, to):
        copies.append(remote(part, part, self.sems.new(), self.sems.new(), to))
        copies[-1].start()

    def forward(self):
        for copy, source in zip(self.far, self.sources):
            copy.wait_recv()
            part = self.part(source[1], self.q)
            self.send(self.lines, part, self.spot.line)
            self.send(self.sides, part, self.spot.column)
            if not self.columns:
                self.send(self.cores, part, self.spot.core)

    def second(self):
        for copy, source in zip(self.lines, self.sources):
            copy.wait_recv()
            part = self.part(source[1], 2 * self.spot.x + 1 - self.spot.odd)
            self.send(self.sides, part, self.spot.column)
            if not self.columns:
                self.send(self.cores, part, self.spot.core)

    def third(self):
        for copy in self.sides:
            copy.wait_recv()
        if not self.columns:
            part = self.part(self.spot.across[1], 2 * (1 - self.spot.x), 2)
            self.send(self.cores, part, self.spot.core)

    def finish(self):
        self.local.wait()
        self.to_core.wait_recv()
        for copy in self.cores:
            copy.wait_recv()

    def drain(self):
        for copy in self.far + self.lines + self.sides + self.cores + [self.to_core]:
            copy.wait_send()


class Merge:
    def __init__(self, spot, send, land, sems):
        self.spot, self.send, self.land = spot, send, land
        self.far = remote(
            send.at[spot.corner[1]], land.at[0], sems.new(), sems.new(), spot.core
        )
        self.near = remote(send.at[spot.core[1]], land.at[1], sems.new(), sems.new(), spot.core)
        self.over = remote(
            send.at[spot.across[1]], land.at[2], sems.new(), sems.new(), spot.across
        )
        self.far.start()
        self.near.start()

    def forward(self):
        self.far.wait_recv()
        block = self.send.at[self.spot.across[1]]
        block[...] = (block[...].astype(F32) + self.land[0].astype(F32)).astype(BF)
        self.over.start()

    def finish(self):
        self.near.wait_recv()
        self.over.wait_recv()
        own = self.send[self.spot.w].astype(F32)
        return own + self.land[1].astype(F32) + self.land[2].astype(F32)

    def drain(self):
        for copy in (self.far, self.near, self.over):
            copy.wait_send()


class Spread:
    def __init__(self, spot, pick, place, sems):
        self.copies = []
        for to in (spot.across, spot.corner, spot.core):
            self.copies.append(remote(pick(to[1]), place(spot.w), sems.new(), sems.new(), to))
        self.local = pltpu.make_async_copy(pick(spot.w), place(spot.w), sems.new())
        for copy in self.copies:
            copy.start()
        self.local.start()

    def finish(self):
        for copy in self.copies:
            copy.wait_recv()
        self.local.wait()

    def drain(self):
        for copy in self.copies:
            copy.wait_send()


def nt(left, right):
    return lax.dot_general(left, right, (((1,), (1,)), ((), ())), preferred_element_type=F32)


def nn(left, right):
    return jnp.dot(left, right, preferred_element_type=F32)


def tn(left, right):
    return lax.dot_general(left, right, (((0,), (0,)), ((), ())), preferred_element_type=F32)


def turn(values, cosine, sine):
    wide = values.shape[1]
    lane = lax.broadcasted_iota(jnp.int32, values.shape, 1)
    first = lax.rem(lane, HD) < HD // 2
    swapped = jnp.where(
        first, pltpu.roll(values, wide - HD // 2, 1), pltpu.roll(values, HD // 2, 1)
    )
    copies = wide // PAIR
    cosine = jnp.concatenate([cosine] * copies, axis=1)
    sine = jnp.concatenate([sine] * copies, axis=1)
    return values * cosine + swapped * sine


def stack_pair(values):
    lane = lax.broadcasted_iota(jnp.int32, values.shape, 1)
    none = jnp.zeros_like(values)
    return jnp.concatenate(
        [jnp.where(lane < HD, values, none), jnp.where(lane < HD, none, values)], axis=0
    )


def unstack_pair(values):
    rows = values.shape[0] // 2
    lane = lax.broadcasted_iota(jnp.int32, (rows, PAIR), 1)
    return jnp.where(lane < HD, values[:rows], values[rows:])


class Ring:
    def __init__(self, spot, blocks, recv, send, parts=1, sides=1, first=(0, 0)):
        self.spot, self.blocks, self.recv, self.send, self.parts = spot, blocks, recv, send, parts
        self.sides = sides
        self.ranks = blocks.shape[0]
        self.first, self.used = first[0], first[1]
        self.sent, self.sent_mid, self.sent_end = [], [], []

    def piece(self, slot, part):
        if self.sides == 1:
            rows = self.blocks.shape[1] // self.parts
            return self.blocks.at[slot, pl.ds(rows * part, rows)]
        high = self.parts // self.sides
        rows, lanes = self.blocks.shape[1] // high, self.blocks.shape[2] // self.sides
        return self.blocks.at[
            slot, pl.ds(rows * (part % high), rows), pl.ds(lanes * (part // high), lanes)
        ]

    def copy(self, slot, part, to):
        self.used += 1
        return remote(
            self.piece(slot, part),
            self.piece(slot, part),
            self.send.at[self.used - 1],
            self.recv.at[self.first + slot + self.ranks * part],
            to,
        )

    def arrived(self, slot, part):
        remote(
            self.piece(slot, part),
            self.piece(slot, part),
            self.send.at[0],
            self.recv.at[self.first + slot + self.ranks * part],
            self.spot.column,
        ).wait_recv()

    def start(self, parts=None, only=None):
        spot = self.spot
        for part in range(self.parts) if parts is None else parts:
            own = self.copy(spot.k, part, spot.inner)
            side = self.copy(spot.k, part, spot.column)
            back = self.copy(spot.k, part, spot.outer) if only != 0 else None
            if only is None:
                own.start()
                self.middle(back)
                side.start()
                self.sent += [own, side]
                self.sent_mid += [back]
                continue

            @pl.when(spot.mid == only)
            def _(copies=(own, back, side)):
                for copy in copies:
                    if copy is not None:
                        copy.start()

            if only == 1:
                self.sent_mid += [own, back, side]
            else:
                self.sent_end += [own, side]

    def middle(self, copy):
        @pl.when(self.spot.mid == 1)
        def _():
            copy.start()

    def step(self, number, only=None):
        spot = self.spot
        slot = 2 * spot.plane(number) + spot.x
        onward = spot.inner if number == 1 else spot.outer
        pieces = []
        for part in range(self.parts):
            along = self.copy(slot, part, onward) if only != 0 else None
            pieces.append((along, self.copy(slot, part, spot.column)))
        if only != 0:

            @pl.when(spot.mid == 1)
            def _():
                for part, (along, side) in enumerate(pieces):
                    self.arrived(slot, part)
                    along.start()
                    side.start()

        if only != 1:

            @pl.when(spot.mid == 0)
            def _():
                for part, (along, side) in enumerate(pieces):
                    self.arrived(slot, part)
                    side.start()

        if only != 0:
            self.sent_mid += [along for along, _ in pieces]
            self.sent_mid += [side for _, side in pieces]
        if only != 1:
            self.sent_end += [side for _, side in pieces]

    def other(self, number):
        for part in range(self.parts):
            self.arrived(2 * self.spot.plane(number) + 1 - self.spot.x, part)

    def drain(self):
        for copy in self.sent:
            copy.wait_send()
        for role, copies in ((0, self.sent_end), (1, self.sent_mid)):

            @pl.when(self.spot.mid == role)
            def _(copies=copies):
                for copy in copies:
                    copy.wait_send()


class Reduce:
    def __init__(self, spot, part, sides, zo, zi, sems, folded=False, parts=1):
        self.spot, self.part, self.sides, self.zo, self.zi = spot, part, sides, zo, zi
        self.z_send, self.zo_recv = sems.at[0], sems.at[1]
        if folded:
            self.zi_recv = sems.at[2]
        else:
            self.x_send, self.x_recv = sems.at[2], sems.at[3]
        self.folded, self.parts = folded, parts
        self.rows = part.shape[1] // parts
        self.sent, self.sent_end, self.sent_mid = [], [], []

    def cut(self, ref, index, h):
        return ref.at[index, pl.ds(self.rows * h, self.rows)]

    def own(self, plane, h):
        return self.cut(self.part, plane if self.folded else 2 * plane + self.spot.x, h)

    def wait(self, land, recv, plane, h):
        piece = self.cut(land, plane, h)
        at = plane + 4 * h
        remote(piece, piece, self.z_send.at[at], recv.at[at], self.spot.column).wait_recv()

    def side(self, number):
        spot = self.spot
        plane = spot.plane(number)
        for h in range(self.parts):
            at = plane + 4 * h
            copy = remote(
                self.cut(self.part, 2 * plane + 1 - spot.x, h),
                self.cut(self.sides, plane, h),
                self.x_send.at[at],
                self.x_recv.at[at],
                spot.column,
            )
            copy.start()
            self.sent.append(copy)

    def add(self, ref, land):
        ref[...] = (ref[...].astype(F32) + land[...].astype(F32)).astype(BF)

    def meet(self, number, launch):
        plane = self.spot.plane(number)
        for h in range(self.parts):
            self.wait(self.sides, self.x_recv, plane, h)
            self.add(self.own(plane, h), self.cut(self.sides, plane, h))
            if launch:
                self.launch_part(number, h)

    def launch(self, number):
        for h in range(self.parts):
            self.launch_part(number, h)

    def launch_part(self, number, h):
        plane = self.spot.plane(number)
        at = plane + 4 * h
        copy = remote(
            self.own(plane, h),
            self.cut(self.zo, plane, h),
            self.z_send.at[at],
            self.zo_recv.at[at],
            self.spot.inner,
        )

        @pl.when(self.spot.mid == 0)
        def _():
            copy.start()

        self.sent_end.append(copy)

    def absorb(self, number):
        plane = self.spot.plane(number)

        @pl.when(self.spot.mid == 1)
        def _():
            for h in range(self.parts):
                self.wait(self.zo, self.zo_recv, plane, h)
                self.add(self.own(plane, h), self.cut(self.zo, plane, h))

    def relay(self, number, settled=False, parts=None):
        plane = self.spot.plane(number)
        land, recv = (self.zi, self.zi_recv) if number == 1 else (self.zo, self.zo_recv)
        copies = []
        for h in range(self.parts) if parts is None else parts:
            at = plane + 4 * h
            copy = remote(
                self.own(plane, h),
                self.cut(self.zi, plane, h),
                self.z_send.at[at],
                self.zi_recv.at[at],
                self.spot.outer if number == 1 else self.spot.inner,
            )
            copies.append((h, copy))

        @pl.when(self.spot.mid == 1)
        def _():
            for h, copy in copies:
                if not settled:
                    self.wait(land, recv, plane, h)
                    self.add(self.own(plane, h), self.cut(land, plane, h))
                copy.start()

        self.sent_mid += [copy for _, copy in copies]

    def last(self, result, parts=None):
        plane = self.spot.plane(0)
        parts = range(self.parts) if parts is None else parts
        for h in parts:
            self.wait(self.zi, self.zi_recv, plane, h)
            rows = pl.ds(self.rows * h, self.rows)
            total = self.own(plane, h)[...].astype(F32)
            result[rows] = total + self.cut(self.zi, plane, h)[...].astype(F32)

        @pl.when(self.spot.mid == 1)
        def _():
            for h in parts:
                self.wait(self.zo, self.zo_recv, plane, h)
                rows = pl.ds(self.rows * h, self.rows)
                result[rows] += self.cut(self.zo, plane, h)[...].astype(F32)

    def drain(self):
        for copy in self.sent:
            copy.wait_send()

        @pl.when(self.spot.mid == 0)
        def _():
            for copy in self.sent_end:
                copy.wait_send()

        @pl.when(self.spot.mid == 1)
        def _():
            for copy in self.sent_mid:
                copy.wait_send()


def swish(values):
    sigmoid = 1.0 / (1.0 + jnp.exp(-values))
    return values * sigmoid, sigmoid * (1.0 + values * (1.0 - sigmoid))


class Exchange:
    def __init__(self, spot, out, back, send, recv):
        self.spot, self.out, self.back = spot, out, back
        self.send, self.recv, self.ranks = send, recv, out.shape[0]
        self.copies = []

    def start(self):
        spot = self.spot
        for offset in range(1, self.ranks):
            peer = lax.rem(spot.k + offset, self.ranks)
            self.copies.append(
                remote(
                    self.out.at[peer],
                    self.back.at[spot.k],
                    self.send.at[offset],
                    self.recv.at[spot.k],
                    (peer, spot.w),
                )
            )
            self.copies[-1].start()
        self.back[spot.k] = self.out[spot.k]

    def finish(self):
        spot = self.spot
        for offset in range(1, self.ranks):
            peer = lax.rem(spot.k + offset, self.ranks)
            remote(
                self.out.at[peer],
                self.back.at[peer],
                self.send.at[offset],
                self.recv.at[peer],
                (peer, spot.w),
            ).wait_recv()

    def drain(self):
        for copy in self.copies:
            copy.wait_send()


def fold_rows(values, ref):
    ranks = ref.shape[0]
    slots = values.shape[0] // ranks
    for e in range(ranks):
        part = values[slots * e : slots * (e + 1)]
        tiles = [part[:, 128 * t : 128 * (t + 1)] for t in range(values.shape[1] // 128)]
        ref[e] = jnp.concatenate(tiles, axis=0).astype(BF)


def unfold_rows(ref, slots):
    parts = []
    for e in range(ref.shape[0]):
        part = ref[e].astype(F32)
        tiles = [part[slots * t : slots * (t + 1)] for t in range(part.shape[0] // slots)]
        parts.append(jnp.concatenate(tiles, axis=1))
    return jnp.concatenate(parts, axis=0).astype(BF)


def split_three(values):
    high = values.astype(BF)
    rest = values - high.astype(F32)
    middle = rest.astype(BF)
    return high, middle, (rest - middle.astype(F32)).astype(BF)


def diagonal(values, axis):
    size = max(values.shape)
    down = lax.broadcasted_iota(jnp.int32, (size, size), 0)
    along = lax.broadcasted_iota(jnp.int32, (size, size), 1)
    return jnp.sum(
        jnp.where(down == along, values.astype(F32), 0.0), axis=axis, keepdims=True
    ).astype(jnp.int32)


def slot_maps(routes, order, slots, experts):
    top, rows = routes.shape
    pairs = rows * top
    lines = [routes[j : j + 1] for j in range(top)]
    e_row = jnp.concatenate(lines, axis=1)
    e_col = jnp.concatenate([diagonal(line, 1) for line in lines], axis=0)
    o_row = lax.rem(order, top) * rows + lax.div(order, top)
    o_col = diagonal(o_row, 1)
    down = lax.broadcasted_iota(jnp.int32, (pairs, pairs), 0)
    along = lax.broadcasted_iota(jnp.int32, (pairs, pairs), 1)
    turn_row = jnp.sum(jnp.where(o_col == along, down.astype(F32), 0.0), axis=0, keepdims=True)
    turn_col = jnp.sum(jnp.where(o_row == down, along.astype(F32), 0.0), axis=1, keepdims=True)
    same = e_col == e_row
    slot_row = jnp.sum(
        jnp.where(same & (turn_col < turn_row), 1.0, 0.0), axis=0, keepdims=True
    ).astype(jnp.int32)
    slot_col = jnp.sum(
        jnp.where(same & (turn_row < turn_col), 1.0, 0.0), axis=1, keepdims=True
    ).astype(jnp.int32)
    target_row = jnp.where(slot_row < slots, e_row * slots + slot_row, -1)
    target_col = jnp.where(slot_col < slots, e_col * slots + slot_col, -1)
    total = experts * slots
    place = lax.broadcasted_iota(jnp.int32, (total, pairs), 0)
    to_slots = jnp.where(place == target_row, 1.0, 0.0).astype(BF)
    place = lax.broadcasted_iota(jnp.int32, (pairs, total), 1)
    to_pairs = jnp.where(place == target_col, 1.0, 0.0).astype(BF)
    return to_slots, to_pairs


def forward_kernel(
    tok, gain_one, gain_two, router_ref, freq, deal, cot, routes, order, sd,
    wq, wk, wv, wo, sg, su, eg, eu, ed,
    cosr_out, sinr_out, kb_out, qb_out, qx_out, gm_out, stats_hbm, stat_out, normed_hbm, mixed_hbm, pack_hbm,
    result_hbm, grad_second_hbm, pack_grad_hbm, dsh_out, side_out, kv_out, wfull_out, keep_out, give_out, other_out,
    cosr, sinr, kb, qb, qx, stats_out, normed_out, mixed_out, pack_out, result_out,
    grad_second_out, pack_grad_out, wbuf, kv, q_s, qc, q_land, gm, stat, mixed, pack, packs, top, low, acc, sg_all, su_all, wg, wu, wd, mix, m4, cot4,
    sh_send, sh_recv, gm_send, gm_recv, xs, xr, gs, gr, orr, br,
    x_s, g_s, sum_s, gate_s, up_s, hid_s, dgate_s, dup_s, dsh, dsh_x, dsh_z, slot_s, pair_s, cb,
    sem, kv_recv, kv_send, a2a_send, a2a_recv, sem_sh,
):
    spot = Spot(4)
    sems = Sems(sem)
    rows, width = tok.shape
    pairs = width // PAIR
    ranks = xs.shape[0]
    slots = xs.shape[1] * 128 // width
    hidden = wg.shape[1]
    shard = width // 4
    part = sg_all.shape[1]
    peers = [(lax.rem(spot.k + o, ranks), spot.w) for o in range(1, ranks)]
    greet([spot.core, spot.across, spot.corner] + peers)
    line = (spot.line, spot.odd)
    key_w = Quarters(spot, wk, wbuf.at[1], sems)
    shards = jnp.concatenate(
        [
            gain_one[...].astype(F32).reshape(1, shard),
            gain_two[...].astype(F32).reshape(1, shard),
            router_ref[...].astype(F32),
            jnp.zeros((16 - 2 - router_ref.shape[0], shard), F32),
        ],
        axis=0,
    )
    shards = jnp.concatenate([shards, jnp.zeros((16, width - shard), F32)], axis=1)
    pack[...] = pltpu.roll(shards, shard * spot.w, 1).astype(BF)
    params = Gather(spot, pack, lambda w: packs.at[w], sems)
    value_w = Quarters(spot, wv, wbuf.at[2], sems)
    query_w = Quarters(spot, wq, wbuf.at[0], sems)

    def stripe(ref):
        return lambda w: ref.at[pl.ds(pl.multiple_of(shard * w, 64), shard)]

    out_w = Share(spot, wo, wbuf.at[3], sems, *line)
    sg_w = Quarters(spot, sg, sg_all, sems, columns=True)
    su_w = Quarters(spot, su, su_all, sems, columns=True)
    cot_w = Gather(spot, cot, lambda w: cot4.at[w], sems)
    gate_w = Gather(spot, eg, stripe(wg), sems)
    up_w = Gather(spot, eu, stripe(wu), sems)
    early = shard // 3

    def down_part(start, count):
        at = pl.ds(start, count)
        place = lambda w: wd.at[pl.ds(pl.multiple_of(shard * w + start, 64), count)]
        return Gather(spot, ed.at[at], place, sems)

    down_w = [down_part(0, early)]
    inputs = tok[...].astype(F32)
    scale = lax.rsqrt(jnp.mean(inputs * inputs, axis=-1, keepdims=True) + EPS)
    scaled = inputs * scale
    piece = rows // 2
    inner = lax.broadcasted_iota(jnp.int32, (rows, 1), 0)
    lane = lax.broadcasted_iota(jnp.int32, (rows, PAIR), 1)
    sign = jnp.where(lax.rem(lane, HD) < HD // 2, -1.0, 1.0)
    for r in range(2):
        paired = deal[2 * spot.z + r]
        unit = jnp.where(inner < piece, paired, 2 * ranks - 1 - paired)
        place = unit * piece + lax.rem(inner, piece)
        qb[r] = jnp.concatenate([lax.div(place, BLK)] * 2, axis=0)
        angles = place.astype(F32) * freq[...]
        cosr[r] = jnp.cos(angles)
        sinr[r] = jnp.sin(angles) * sign
    along = lax.broadcasted_iota(jnp.int32, (1, rows), 1)
    for r in range(ranks):
        unit = jnp.where(along < piece, deal[r], 2 * ranks - 1 - deal[r])
        kb[:, rows * r : rows * (r + 1)] = lax.div(unit * piece + lax.rem(along, piece), BLK)
    key_w.forward()
    params.forward()
    params.finish()
    pack_all = (packs[0].astype(F32) + packs[1].astype(F32)) + (
        packs[2].astype(F32) + packs[3].astype(F32)
    )
    pack_out[...] = pack_all
    normed = (scaled * pack_all[0:1]).astype(BF)
    normed_out[...] = normed.T
    cosine, sine = cosr[spot.x], sinr[spot.x]
    value_w.forward()
    to_slots, to_pairs = slot_maps(routes[...], order[...], slots, ranks)
    route = [diagonal(routes[j : j + 1], 1) for j in range(2)]
    slot_s[...] = to_slots
    pair_s[...] = to_pairs
    key_w.second()
    query_w.forward()
    value_w.second()
    key_w.third()
    key_w.finish()
    kv[spot.k, :, 0:width] = turn(nn(normed, wbuf[1]), cosine, sine).astype(BF)
    ring = Ring(spot, kv, kv_recv, kv_send, parts=4, sides=2)
    ring.start(parts=(0, 1))
    query_w.second()
    value_w.third()
    value_w.finish()
    kv[spot.k, :, width : 2 * width] = nn(normed, wbuf[2]).astype(BF)
    ring.start(parts=(2, 3))
    query_w.third()
    query_w.finish()
    query = turn(nn(normed, wbuf[0]), cosine, sine).astype(BF) * jnp.asarray(HD**-0.5, BF)
    for j in range(pairs):
        q_s[j] = stack_pair(query[:, PAIR * j : PAIR * (j + 1)])
    for x in range(2):
        qc[x] = query[:, width // 2 * x : width // 2 * (x + 1)]
    top[...] = jnp.full_like(top, MASKED)
    low[...] = jnp.zeros_like(low)
    acc[...] = jnp.zeros_like(acc)
    q_block = qb[spot.x]

    def chunk(slot, count):
        keys = count * rows
        k_block = kb[:, pl.ds(pl.multiple_of(rows * slot, rows), keys)]
        allowed = k_block <= q_block

        def one_pair(j, carry):
            lane = pl.multiple_of(PAIR * j, PAIR)
            key = kv[pl.ds(slot, count), :, pl.ds(lane, PAIR)].reshape(keys, PAIR)
            value = kv[pl.ds(slot, count), :, pl.ds(width + lane, PAIR)].reshape(keys, PAIR)
            scores = jnp.where(allowed, nt(q_s[j], key), MASKED)
            old = top[j]
            new = jnp.maximum(old, jnp.max(scores, axis=1, keepdims=True))
            raised = jnp.where(allowed, jnp.exp(scores - new[:, 0:1]), 0.0)
            factor = jnp.exp(old - new)
            top[j] = new
            low[j] = low[j] * factor + jnp.sum(raised, axis=1, keepdims=True)
            acc[j] = acc[j] * factor + nn(raised.astype(BF), value)
            return carry

        lax.fori_loop(0, pairs, one_pair, 0, unroll=3)

    ring.step(1)
    ring.step(2, only=1)
    ring.other(0)
    chunk(2 * spot.plane(0), 2)
    ring.step(2, only=0)
    ring.step(3, only=1)
    ring.other(1)
    chunk(2 * spot.plane(1), 2)
    ring.step(3, only=0)
    out_w.forward()
    sg_w.forward()
    su_w.forward()
    ring.other(2)
    chunk(2 * spot.plane(2), 2)
    out_w.second()
    cot_w.forward()
    chunk(2 * spot.plane(3) + spot.x, 1)
    ring.other(3)
    chunk(2 * spot.plane(3) + 1 - spot.x, 1)
    sg_w.second()
    su_w.second()
    saves = []

    def save(src, dst):
        saves.append(pltpu.make_async_copy(src, dst, sems.new()))
        saves[-1].start()

    save(kv, kv_out)
    for src, dst in ((cosr, cosr_out), (sinr, sinr_out), (kb, kb_out), (qb, qb_out)):
        save(src, dst)
    save(normed_out, normed_hbm)
    save(pack_out, pack_hbm)
    for j in range(pairs):
        mixed[:, PAIR * j : PAIR * (j + 1)] = unstack_pair(acc[j] / low[j])
        top[j] = top[j] + jnp.log(low[j])
    asides = []

    def aside(src, dst):
        asides.append(remote(src, dst, sems.new(), sems.new(), spot.column))
        asides[-1].start()
        return asides[-1]

    out_w.finish()
    save(wbuf, wfull_out)
    second = inputs + nn(mixed[...].astype(BF), wbuf[3])
    scale = lax.rsqrt(jnp.mean(second * second, axis=-1, keepdims=True) + EPS)
    mixer = (second * scale * pack_all[1:2]).astype(BF)
    mix[...] = mixer

    mixers = Gather(spot, mix, lambda w: m4.at[w], sems)
    down_w.append(down_part(early, shard - early))
    fold_rows(nn(slot_s[:, :rows] + slot_s[:, rows:], mixer), xs)
    rows_out = Exchange(spot, xs, xr, a2a_send.at[0], a2a_recv.at[0])
    rows_out.start()
    router = pack_all[2:16].astype(BF)
    router = jnp.concatenate([router, jnp.zeros((2, width), BF)], axis=0)
    logits = nt(mixer, router)
    lane = lax.broadcasted_iota(jnp.int32, logits.shape, 1)
    matches = [lane == route[j] for j in range(2)]
    chosen = [jnp.sum(jnp.where(m, logits, 0.0), axis=1, keepdims=True) for m in matches]
    largest = jnp.maximum(chosen[0], chosen[1])
    raised = [jnp.exp(c - largest) for c in chosen]
    gates = [r / (raised[0] + raised[1]) for r in raised]
    grad = cot[...].astype(F32)
    pair_grad = jnp.concatenate([(g * grad).astype(BF) for g in gates], axis=0)
    fold_rows(nn(slot_s[...], pair_grad), gs)
    grads_out = Exchange(spot, gs, gr, a2a_send.at[1], a2a_recv.at[1])
    grads_out.start()
    gate_w.forward()
    up_w.forward()
    mixers.forward()

    for part_w in (sg_w, su_w):
        part_w.third()
    for part_w in (sg_w, su_w, cot_w, mixers):
        part_w.finish()
    rows_all = m4[...].reshape(4 * rows, width)
    grad_all = cot4[...].reshape(4 * rows, width)
    gate_part, up_part = nn(rows_all, sg_all[...]), nn(rows_all, su_all[...])
    act, slope = swish(gate_part)
    shared_hidden = (act * up_part).astype(BF)
    sh_send[...] = nn(shared_hidden, sd[...]).astype(BF).reshape(4, rows, width)
    mixed_out[...] = mixed[...].astype(BF).T
    save(mixed_out, mixed_hbm)
    query_x = aside(qc.at[1 - spot.x], q_land)
    shared_out = Merge(spot, sh_send, sh_recv, sems)
    hid_grad = nt(grad_all, sd[...])
    grad_gate = (hid_grad * up_part * slope).astype(BF)
    grad_up = (hid_grad * act).astype(BF)
    back = nt(grad_gate, sg_all[...]) + nt(grad_up, su_all[...])
    gm_send[...] = back.astype(BF).reshape(4, rows, width)
    shared_out.forward()
    shared_back = Merge(spot, gm_send, gm_recv, sems)
    half = shard // 2
    for at, values in ((0, tn(rows_all, grad_gate)), (half, tn(rows_all, grad_up))):
        values = values.astype(BF)
        for r in range(ranks):
            down, left = half * (r // 4), 128 * (r % 4)
            for w in range(4):
                dsh[r, shard * w + at : shard * w + at + half] = values[
                    shard * w + down : shard * w + down + half, left : left + 128
                ]
    values = tn(shared_hidden, grad_all).astype(BF)
    deep = values.shape[0] // ranks
    for r in range(ranks):
        for t in range(width // 128):
            dsh[r, width + deep * t : width + deep * (t + 1)] = values[
                deep * r : deep * (r + 1), 128 * t : 128 * (t + 1)
            ]
    shared_back.forward()
    shared_grad = Reduce(spot, dsh, dsh_x, dsh_z, None, sem_sh)
    for number in (3, 2):
        shared_grad.side(number)

    for part_w in (gate_w, up_w):
        part_w.finish()
    rows_out.finish()
    x_s[...] = unfold_rows(xr, slots)
    block = 512

    def parts(i):
        return pl.ds(pl.multiple_of(block * i, block), block)

    def up_step(i, carry):
        at = parts(i)
        gate = nn(x_s[...], wg[:, at])
        up = nn(x_s[...], wu[:, at])
        act, slope = swish(gate)
        hid_s[:, at] = (act * up).astype(BF)
        gate_s[:, at] = up * slope
        up_s[:, at] = act
        return carry

    lax.fori_loop(0, hidden // block, up_step, 0)
    for part_w in down_w:
        part_w.forward()
    for part_w in down_w:
        part_w.finish()
    sum_s[...] = nt(hid_s[...], wd[...])
    rows_out.drain()
    fold_rows(sum_s[...], xs)
    outs = Exchange(spot, xs, orr, a2a_send.at[2], a2a_recv.at[2])
    outs.start()
    grads_out.finish()
    g_s[...] = unfold_rows(gr, slots)

    def down_step(i, carry):
        at = parts(i)
        grad_hidden = nn(g_s[...], wd[:, at])
        dgate_s[:, at] = (grad_hidden * gate_s[:, at]).astype(BF)
        dup_s[:, at] = (grad_hidden * up_s[:, at]).astype(BF)
        return carry

    lax.fori_loop(0, hidden // block, down_step, 0)
    sum_s[...] = nt(dgate_s[...], wg[...]) + nt(dup_s[...], wu[...])
    grads_out.drain()
    fold_rows(sum_s[...], gs)
    backs = Exchange(spot, gs, br, a2a_send.at[3], a2a_recv.at[3])
    backs.start()
    shared_grad.side(1)

    for part_w in [gate_w, up_w] + down_w:
        part_w.drain()
    swaps, across = [], []
    first = 2 * shard // 3
    sources = ((wg, x_s, dgate_s), (wu, x_s, dup_s), (wd, g_s, hid_s))

    def grads_of(a):
        ref, left, right = sources[a]

        def grad_step(i, carry):
            at = parts(i)
            ref[:, at] = tn(left[...], right[:, at]).astype(BF)
            return carry

        lax.fori_loop(0, hidden // block, grad_step, 0)
        for row in range(2):
            src = ref.at[pl.ds(pl.multiple_of(shard * (2 * row + 1 - spot.c), 64), shard)]
            swaps.append(remote(src, cb.at[a, row], sems.new(), sems.new(), spot.core))
            swaps[-1].start()

    def add_mate(a):
        ref = sources[a][0]
        for row in range(2):
            swaps[2 * a + row].wait_recv()

        def add(i, carry):
            for row in range(2):
                at = pl.ds(pl.multiple_of(shard * (2 * row + spot.c) + 16 * i, 16), 16)
                mate = cb[a, row, pl.ds(pl.multiple_of(16 * i, 16), 16)].astype(F32)
                ref[at] = (ref[at].astype(F32) + mate).astype(BF)
            return carry

        lax.fori_loop(0, shard // 16, add, 0)
        start = pl.multiple_of(shard * spot.across[1], 64)
        keep = ref.at[pl.ds(pl.multiple_of(shard * spot.w, 64), shard)]
        saves.append(pltpu.make_async_copy(keep, keep_out.at[a], sems.new()))
        saves[-1].start()
        if a == 0:
            across.append(
                remote(ref.at[pl.ds(start, first)], other_out, sems.new(), sems.new(), spot.across)
            )
            across[-1].start()
            give = ref.at[pl.ds(pl.multiple_of(start + first, 64), shard - first)]
            there = give_out.at[0, pl.ds(first, shard - first)]
        else:
            give, there = ref.at[pl.ds(start, shard)], give_out.at[a]
        saves.append(pltpu.make_async_copy(give, there, sems.new()))
        saves[-1].start()

    shared_grad.meet(3, True)
    grads_of(0)
    grads_of(1)
    add_mate(0)
    shared_grad.meet(2, True)
    grads_of(2)
    add_mate(1)
    add_mate(2)
    total = second + shared_out.finish()
    grad_mixer = shared_back.finish()
    outs.finish()
    pair_out = nn(pair_s[...], unfold_rows(orr, slots))
    pair_out = [pair_out[:rows], pair_out[rows:]]
    result_out[...] = (total + gates[0] * pair_out[0] + gates[1] * pair_out[1]).astype(BF)
    save(result_out, result_hbm)
    grad_gates = [jnp.sum(grad * p, axis=1, keepdims=True) for p in pair_out]
    inner = gates[0] * grad_gates[0] + gates[1] * grad_gates[1]
    grad_logits = jnp.zeros_like(logits)
    for j in range(2):
        grad_logits += jnp.where(matches[j], gates[j] * (grad_gates[j] - inner), 0.0)
    pieces = split_three(grad_logits)
    router_grad = sum(tn(piece, mixer) for piece in pieces)
    grad_mixer = grad_mixer + sum(nn(piece, router) for piece in pieces)
    shared_grad.meet(1, False)
    backs.finish()
    grad_mixer = grad_mixer + nn(pair_s[:rows] + pair_s[rows:], unfold_rows(br, slots))
    weighted = grad_mixer * pack_all[1:2]
    mean = jnp.mean(weighted * second, axis=-1, keepdims=True)
    grad_second = grad + scale * weighted - second * (scale * scale * scale * mean)
    grad_second_out[...] = grad_second
    save(grad_second_out, grad_second_hbm)

    grad_mixed = nt(grad_second.astype(BF), wbuf[3]).astype(BF)
    half = width // 2
    group = half // PAIR
    for x in range(2):
        gm[x] = grad_mixed[:, half * x : half * (x + 1)]
    product = grad_mixed.astype(F32) * mixed[...]
    lane = lax.broadcasted_iota(jnp.int32, (2 * rows, PAIR), 1)
    mine = jnp.zeros((2 * rows, PAIR), F32)
    theirs = jnp.zeros((2 * rows, PAIR), F32)
    for i in range(group):
        delta = [
            jnp.sum(stack_pair(product[:, PAIR * j : PAIR * (j + 1)]), axis=1, keepdims=True)
            for j in (i, group + i)
        ]
        swap = spot.x == 1
        mine = jnp.where(lane == i, top[group * spot.x + i], mine)
        theirs = jnp.where(lane == i, top[group * (1 - spot.x) + i], theirs)
        mine = jnp.where(lane == group + i, jnp.where(swap, delta[1], delta[0]), mine)
        theirs = jnp.where(lane == group + i, jnp.where(swap, delta[0], delta[1]), theirs)
        qx[i] = stack_pair(qc[spot.x, :, PAIR * i : PAIR * (i + 1)])
    stat[...] = theirs.T[0:8]
    stats_out[...] = mine
    gain_grad = jnp.sum(grad_mixer * second * scale, axis=0, keepdims=True)
    pack_grad_out[...] = jnp.concatenate(
        [jnp.zeros_like(gain_grad), gain_grad, router_grad[:14]], axis=0
    )
    query_x.wait_recv()
    for i in range(group):
        qx[group + i] = stack_pair(q_land[:, PAIR * i : PAIR * (i + 1)])
    for number in (3, 2):
        shared_grad.absorb(number)
    for plane in range(4):
        save(dsh.at[2 * plane + spot.x], dsh_out.at[plane])
    save(dsh.at[2 * spot.z + 1 - spot.x], side_out)
    for src, dst in (
        (qx, qx_out),
        (gm, gm_out),
        (stats_out, stats_hbm),
        (stat, stat_out),
        (pack_grad_out, pack_grad_hbm),
    ):
        save(src, dst)
    for copy in across:
        copy.wait_recv()
    for part_w in (params, key_w, value_w, query_w, out_w, sg_w, su_w, cot_w, ring, mixers):
        part_w.drain()
    for part_w in (outs, backs, shared_out, shared_back, shared_grad):
        part_w.drain()
    for copy in swaps + across + asides:
        copy.wait_send()
    for copy in saves:
        copy.wait()


def run_forward(
    tok, gain_one, gain_two, router, freq, deal, cot, routes, order, sd,
    wq, wk, wv, wo, sg, su, eg, eu, ed,
):
    rows, width = tok.shape
    pairs = width // PAIR
    ranks, slots = 8, 40
    hidden = eg.shape[1]
    part = sg.shape[1] // 4
    shard = width // 4
    total = ranks * slots
    tall = width + part * width // (128 * ranks)
    any_, vm = pl.BlockSpec(memory_space=pl.ANY), pl.BlockSpec(memory_space=VMEM)
    shape = jax.ShapeDtypeStruct

    def low(*dims):
        return VMEM(dims, BF)

    def full(*dims):
        return VMEM(dims, F32)

    dma = pltpu.SemaphoreType.DMA
    folded = low(ranks, slots * width // 128, 128)
    return pl.pallas_call(
        forward_kernel,
        out_shape=(
            shape((2, rows, PAIR), F32),
            shape((2, rows, PAIR), F32),
            shape((1, ranks * rows), jnp.int32),
            shape((2, 2 * rows, 1), jnp.int32),
            shape((pairs, 2 * rows, PAIR), BF),
            shape((2, rows, width // 2), BF),
            shape((2 * rows, PAIR), F32),
            shape((8, 2 * rows), F32),
            shape((width, rows), BF),
            shape((width, rows), BF),
            shape((16, width), F32),
            shape((rows, width), BF),
            shape((rows, width), F32),
            shape((16, width), F32),
            shape((4, tall, 128), BF),
            shape((tall, 128), BF),
            shape((ranks, rows, 2 * width), BF),
            shape((4, width, width), BF),
            shape((3, shard, hidden), BF),
            shape((3, shard, hidden), BF),
            shape((2 * shard // 3, hidden), BF),
        ),
        in_specs=[vm] * 5 + [pl.BlockSpec(memory_space=pltpu.SMEM)] + [vm] * 4 + [any_] * 9,
        out_specs=tuple([any_] * 21),
        scratch_shapes=[
            full(2, rows, PAIR),
            full(2, rows, PAIR),
            VMEM((1, ranks * rows), jnp.int32),
            VMEM((2, 2 * rows, 1), jnp.int32),
            low(pairs, 2 * rows, PAIR),
            full(2 * rows, PAIR),
            low(width, rows),
            low(width, rows),
            full(16, width),
            low(rows, width),
            full(rows, width),
            full(16, width),
            low(4, width, width),
            low(ranks, rows, 2 * width),
            low(pairs, 2 * rows, PAIR),
            low(2, rows, width // 2),
            low(rows, width // 2),
            low(2, rows, width // 2),
            full(8, 2 * rows),
            full(rows, width),
            low(16, width),
            low(4, 16, width),
            full(pairs, 2 * rows, PAIR),
            full(pairs, 2 * rows, PAIR),
            full(pairs, 2 * rows, PAIR),
            low(width, part),
            low(width, part),
            low(width, hidden),
            low(width, hidden),
            low(width, hidden),
            low(rows, width),
            low(4, rows, width),
            low(4, rows, width),
            low(4, rows, width),
            low(3, rows, width),
            low(4, rows, width),
            low(3, rows, width),
            *[folded] * 6,
            low(total, width),
            low(total, width),
            full(total, width),
            full(total, hidden),
            full(total, hidden),
            low(total, hidden),
            low(total, hidden),
            low(total, hidden),
            low(ranks, tall, 128),
            low(4, tall, 128),
            low(4, tall, 128),
            low(total, 2 * rows),
            low(2 * rows, total),
            low(3, 2, shard, hidden),
            dma((SEMS_FORWARD,)),
            dma((4 * ranks,)),
            dma((44,)),
            dma((4, ranks)),
            dma((4, ranks)),
            dma((4, 4)),
        ],
        compiler_params=pltpu.CompilerParams(
            collective_id=1, has_side_effects=True, vmem_limit_bytes=VMEM_BYTES
        ),
    )(
        tok, gain_one, gain_two, router, freq, deal, cot, routes, order, sd,
        wq, wk, wv, wo, sg, su, eg, eu, ed,
    )


def backward_kernel(
    grad_second_hbm, tok_hbm, pack_hbm, pack_grad_hbm, n_t_hbm, m_t_hbm, qx_hbm, gm_hbm, stats_hbm, stat_hbm,
    cosr_hbm, sinr_hbm, kb_hbm, qb_hbm, side_ref, dsh_ref, kv_ref, wfull_ref, give_ref, other_ref,
    grad_input_out, pack_out, att1_out, att2_out, sh_out, other_out,
    grad_second_ref, tok, pack_ref, pack_grad_ref, n_t, m_t, qx, gm, stats, stat, cosr, sinr, kb, qb,
    gx, gm_land, stat_land, w_half, kv, kvb, kv_zo, kv_zi, kv_sum, dq, ga, ga4, gq, gq4, gkv, gkv4, n_all, m_all, pk, pk4,
    o_send, o_land, gn_send, gn_land, a1, a1_zo, a1_zi, a1_sum, a2, a2_zo, a2_zi, a2_sum, r1, r2,
    sh, sh_land, sh_zo, sh_zi, sh_sum, sh_chunk, r3,
    sem, sem_kv, sem_a1, sem_a2, sem_sh, ring_recv, ring_send,
):
    spot = Spot(4)
    sems = Sems(sem)
    rows, width = tok.shape
    half = width // 2
    group = half // PAIR
    shard = width // 4
    mine = pl.ds(pl.multiple_of(half * spot.x, half), half)
    values = pl.ds(pl.multiple_of(width + half * spot.x, half), half)
    ranks = kv.shape[0]
    sources = dict(
        gm=(gm_hbm, gm),
        stat=(stat_hbm, stat),
        dsh=(dsh_ref, sh),
        second=(grad_second_hbm, grad_second_ref),
        n_t=(n_t_hbm, n_t),
        m_t=(m_t_hbm, m_t),
        qx=(qx_hbm, qx),
        stats=(stats_hbm, stats.at[0]),
        kb=(kb_hbm, kb),
        qb=(qb_hbm, qb),
        cosr=(cosr_hbm, cosr),
        sinr=(sinr_hbm, sinr),
        tok=(tok_hbm, tok),
        pack=(pack_hbm, pack_ref),
        pack_grad=(pack_grad_hbm, pack_grad_ref),
    )
    inputs = {
        name: pltpu.make_async_copy(src, dst, sems.new()) for name, (src, dst) in sources.items()
    }
    for copy in inputs.values():
        copy.start()
    loads = [
        pltpu.make_async_copy(kv_ref.at[:, :, mine], kv.at[:, :, pl.ds(0, half)], sems.new()),
        pltpu.make_async_copy(kv_ref.at[:, :, values], kv.at[:, :, pl.ds(half, half)], sems.new()),
        *[
            pltpu.make_async_copy(wfull_ref.at[i, :, mine], w_half.at[i], sems.new())
            for i in range(3)
        ],
    ]
    done = other_ref.shape[0]
    loads.append(pltpu.make_async_copy(other_ref, other_out.at[0, pl.ds(0, done)], sems.new()))
    for copy in loads:
        copy.start()

    def block(ref, w):
        return ref.at[pl.ds(pl.multiple_of(shard * w, 64), shard)]

    greet((spot.core, spot.across, spot.corner, spot.column, spot.inner), (spot.mid, spot.outer))
    asides = []

    def aside(src, dst):
        asides.append(remote(src, dst, sems.new(), sems.new(), spot.column))
        asides[-1].start()
        return asides[-1]

    inputs["gm"].wait()
    inputs["stat"].wait()
    grads_x = aside(gm.at[1 - spot.x], gm_land)
    stat_x = aside(stat, stat_land)
    shared_x = aside(side_ref, sh_land)
    inputs["dsh"].wait()
    shared = Reduce(spot, sh, None, sh_zo, sh_zi, sem_sh, folded=True, parts=2)
    shared.launch(1)
    shared.relay(3, settled=True)
    shared.relay(2, settled=True)
    inputs["second"].wait()
    grad_second = grad_second_ref[...]
    ga[...] = grad_second.astype(BF)
    grads_w = Gather(spot, ga, lambda w: ga4.at[w], sems)
    inputs["n_t"].wait()
    inputs["m_t"].wait()

    def columns(ref):
        return lambda w: ref.at[:, pl.ds(pl.multiple_of(rows * w, 128), rows)]

    normed_w = Spread(spot, lambda w: block(n_t, w), columns(n_all.at[spot.x]), sems)
    mixed_w = Spread(spot, lambda w: block(m_t, w), columns(m_all), sems)
    across = []

    def send_across(src, dst):
        across.append(remote(src, dst, sems.new(), sems.new(), spot.across))
        across[-1].start()

    def send_give(a, start, count):
        at = pl.ds(start, count)
        send_across(give_ref.at[a, at], other_out.at[a, at])

    third = shard // 3
    send_give(1, 0, third)
    dq[...] = jnp.zeros_like(dq)
    for name in ("qx", "stats", "kb", "qb", "cosr", "sinr", "tok", "pack", "pack_grad"):
        inputs[name].wait()
    loads[0].wait()
    loads[1].wait()
    for i in range(group):
        gx[i] = stack_pair(gm[spot.x, :, PAIR * i : PAIR * (i + 1)])
    grads_x.wait_recv()
    for i in range(group):
        gx[group + i] = stack_pair(gm_land[:, PAIR * i : PAIR * (i + 1)])
    stat_x.wait_recv()
    stats[1] = jnp.concatenate([stat_land[...], jnp.zeros((PAIR - 8, 2 * rows), F32)], axis=0).T

    def chunk(number):
        plane = spot.plane(number)
        k_block = kb[:, pl.ds(pl.multiple_of(2 * rows * plane, 2 * rows), 2 * rows)]
        allowed = [k_block <= qb[spot.x], k_block <= qb[1 - spot.x]]

        for i in range(group):
            lane = PAIR * i
            both = pl.ds(2 * plane, 2)
            key = kv[both, :, pl.ds(lane, PAIR)].reshape(2 * rows, PAIR)
            value = kv[both, :, pl.ds(half + lane, PAIR)].reshape(2 * rows, PAIR)
            grad_key = jnp.zeros((2 * rows, PAIR), F32)
            grad_value = jnp.zeros((2 * rows, PAIR), F32)
            for owner in range(2):
                j = group * owner + i
                stat = stats[owner]
                query, grad = qx[j], gx[j]
                raised = jnp.exp(nt(query, key) - stat[:, i : i + 1])
                probs = jnp.where(allowed[owner], raised, 0.0)
                inner = nt(grad, value) - stat[:, group + i : group + i + 1]
                grad_scores = (probs * inner * HD**-0.5).astype(BF)
                dq[j] += nn(grad_scores, key)
                grad_key += tn(grad_scores, query)
                grad_value += tn(probs.astype(BF), grad)
            kvb[plane, :, pl.ds(lane, PAIR)] = (grad_key * HD**0.5).astype(BF)
            kvb[plane, :, pl.ds(half + lane, PAIR)] = grad_value.astype(BF)

    kv_grad = Reduce(spot, kvb, None, kv_zo, kv_zi, sem_kv, folded=True, parts=2)
    chunk(3)
    kv_grad.launch(3)
    chunk(2)
    kv_grad.launch(2)
    chunk(1)
    kv_grad.launch(1)
    normed_w.finish()
    normed_x = aside(n_all.at[spot.x], n_all.at[spot.x])
    shared.relay(1)
    kv_grad.relay(3, parts=(0,))
    chunk(0)
    for owner in range(2):
        at = spot.x if owner == 0 else 1 - spot.x
        parts = [unstack_pair(dq[group * owner + i]) for i in range(group)]
        gq[at] = turn(jnp.concatenate(parts, axis=1), cosr[at], -sinr[at]).astype(BF)
    grads_w.forward()
    mixed_w.finish()
    grads_w.finish()
    out_grad = nn(m_all[...], ga4[...].reshape(4 * rows, width)).astype(BF)
    for x in range(2):
        o_send[x] = out_grad[:, half * x : half * (x + 1)]
    out_x = aside(o_send.at[1 - spot.x], o_land)
    shared_x.wait_recv()
    sh[spot.z] = (sh[spot.z].astype(F32) + sh_land[...].astype(F32)).astype(BF)
    shared.last(sh_sum)
    kv_grad.relay(3, parts=(1,))
    sh_chunk[...] = sh_sum[...].astype(BF)
    part = 2 * shard // 2

    def piece(w):
        return sh_chunk.at[pl.ds(pl.multiple_of(part * w, 64), part)]

    def place(w):
        return r3.at[spot.k, pl.ds(pl.multiple_of(part * w, 64), part)]

    shared_w = Spread(spot, piece, place, sems)
    rest = sh_chunk.shape[0] - 4 * part
    r3[spot.k, pl.ds(4 * part, rest)] = sh_chunk[pl.ds(4 * part, rest)]
    query_w = Gather(spot, gq, lambda w: gq4.at[w], sems)
    send_give(1, third, third)
    kv_grad.relay(2, parts=(0,))
    kv_grad.relay(1, parts=(0,))
    shared_w.finish()
    ring3 = Ring(spot, r3, ring_recv, ring_send, parts=2)
    ring3.start(only=0)
    kv_grad.relay(2, parts=(1,))
    kv_grad.relay(1, parts=(1,))
    ring3.start(only=1)
    for copy in loads[2:5]:
        copy.wait()
    flat = gq[...].reshape(2 * rows, half)
    grad_normed = nt(flat, w_half[0])
    query_w.forward()
    query_w.finish()
    normed_x.wait_recv()

    def weight_grad(grads4):
        total = nn(n_all[0], grads4[:, 0].reshape(4 * rows, grads4.shape[3]))
        return total + nn(n_all[1], grads4[:, 1].reshape(4 * rows, grads4.shape[3]))

    query_grad = weight_grad(gq4).astype(BF)
    out_x.wait_recv()
    out_half = (o_send[spot.x].astype(F32) + o_land[...].astype(F32)).astype(BF)
    size = shard // 4
    for plane in range(4):
        at = slice(size * plane, size * (plane + 1))
        a1[plane, :, 0:half] = out_half[at]
        a1[plane, :, half:width] = query_grad[at]
    first = Reduce(spot, a1, None, a1_zo, a1_zi, sem_a1, folded=True)
    for number in (3, 2, 1):
        first.launch(number)
    kv_w = []
    for r in range(2):
        at = slice(rows * r, rows * (r + 1))
        kv_grad.last(kv_sum, parts=(r,))
        gkv[r, :, 0:half] = turn(kv_sum[at, 0:half], cosr[r], -sinr[r]).astype(BF)
        gkv[r, :, half:width] = kv_sum[at, half:width].astype(BF)
        kv_w.append(Gather(spot, gkv.at[r], lambda w, r=r: gkv4.at[w, r], sems))
    send_give(1, 2 * third, third)
    send_give(0, done, shard - done)
    flat = gkv[...].reshape(2 * rows, width)
    grad_normed = grad_normed + nt(flat[:, 0:half], w_half[1]) + nt(flat[:, half:width], w_half[2])
    gn_send[...] = grad_normed.astype(BF).reshape(2, rows, width)
    normed_grad_x = aside(gn_send.at[1 - spot.x], gn_land)
    ring3.step(1, only=0)
    ring3.step(2, only=1)
    ring3.step(1, only=1)
    first.relay(3)
    first.relay(2)
    for part_w in kv_w:
        part_w.forward()
    for part_w in kv_w:
        part_w.finish()
    both = weight_grad(gkv4).astype(BF)
    for plane in range(4):
        a2[plane] = both[size * plane : size * (plane + 1)]
    second = Reduce(spot, a2, None, a2_zo, a2_zi, sem_a2, folded=True)
    for number in (3, 2, 1):
        second.launch(number)
    first.relay(1)
    ring3.step(2, only=0)
    second.relay(3)
    second.relay(2)
    second.relay(1)
    ring3.step(3, only=1)
    normed_grad_x.wait_recv()
    grad_normed = gn_send[spot.x].astype(F32) + gn_land[...].astype(F32)
    inputs = tok[...].astype(F32)
    scale = lax.rsqrt(jnp.mean(inputs * inputs, axis=-1, keepdims=True) + EPS)
    weighted = grad_normed * pack_ref[0:1]
    mean = jnp.mean(weighted * inputs, axis=-1, keepdims=True)
    grad_input_out[...] = (
        grad_second + scale * weighted - inputs * (scale * scale * scale * mean)
    )
    gain_grad = jnp.sum(grad_normed * inputs * scale, axis=0, keepdims=True)
    pk[...] = jnp.concatenate([gain_grad, pack_grad_ref[1:16]], axis=0).astype(BF)
    pack_w = Gather(spot, pk, lambda w: pk4.at[w], sems)
    send_give(2, 0, shard)
    first.last(a1_sum)
    r1[spot.k] = a1_sum[...].astype(BF)
    ring1 = Ring(spot, r1, ring_recv, ring_send, first=(16, 28))
    ring1.start()
    pack_w.forward()
    pack_w.finish()
    extra = sum(pk4[w].astype(F32) for w in range(4)).astype(BF)
    second.last(a2_sum)
    r2[spot.k, 0:size] = a2_sum[...].astype(BF)
    r2[spot.k, size : size + 16] = extra
    ring2 = Ring(spot, r2, ring_recv, ring_send, first=(24, 39))
    ring2.start()
    ring3.step(3, only=0)
    ring1.step(1)
    ring1.step(2, only=1)
    ring1.step(3, only=1)
    ring1.step(2, only=0)
    ring1.step(3, only=0)
    ring2.step(1)
    ring2.step(2)
    ring2.step(3)
    saves = []
    for ring, src, dst in ((ring3, r3, sh_out), (ring1, r1, att1_out), (ring2, r2, att2_out)):
        for number in range(4):
            ring.other(number)
        saves.append(pltpu.make_async_copy(src, dst, sems.new()))
        saves[-1].start()
    total = jnp.zeros(pk.shape, F32)
    for r in range(ranks):
        total = total + r2[r, size : size + 16].astype(F32)
    pack_out[...] = total
    for copy in across:
        copy.wait_recv()
    for copy in across + asides:
        copy.wait_send()
    for part_w in [grads_w, normed_w, mixed_w, query_w, shared_w, pack_w] + kv_w:
        part_w.drain()
    for part_w in (shared, kv_grad, first, second, ring1, ring2, ring3):
        part_w.drain()
    for copy in saves + loads[5:]:
        copy.wait()


def run_backward(
    grad_second, tok, pack, pack_grad, n_t, m_t, qx, gm, stats, stat, cosr, sinr, kb, qb, side, dsh, kv,
    wfull,
    give, other,
):
    rows, width = tok.shape
    pairs = width // PAIR
    half = width // 2
    ranks = 8
    shard, hidden = width // 4, give.shape[2]
    size = shard // 4
    tall = dsh.shape[1]
    any_, vm = pl.BlockSpec(memory_space=pl.ANY), pl.BlockSpec(memory_space=VMEM)
    shape = jax.ShapeDtypeStruct

    def low(*dims):
        return VMEM(dims, BF)

    def full(*dims):
        return VMEM(dims, F32)

    dma = pltpu.SemaphoreType.DMA
    return pl.pallas_call(
        backward_kernel,
        out_shape=(
            shape((rows, width), F32),
            shape(pack.shape, F32),
            shape((ranks, size, width), BF),
            shape((ranks, size + 16, width), BF),
            shape((ranks, tall, 128), BF),
            shape((3, shard, hidden), BF),
        ),
        in_specs=[any_] * 20,
        out_specs=(vm, vm, any_, any_, any_, any_),
        scratch_shapes=[
            full(rows, width),
            low(rows, width),
            full(16, width),
            full(16, width),
            low(width, rows),
            low(width, rows),
            low(pairs, 2 * rows, PAIR),
            low(2, rows, half),
            full(2, 2 * rows, PAIR),
            full(8, 2 * rows),
            full(2, rows, PAIR),
            full(2, rows, PAIR),
            VMEM((1, ranks * rows), jnp.int32),
            VMEM((2, 2 * rows, 1), jnp.int32),
            low(pairs, 2 * rows, PAIR),
            low(rows, half),
            full(8, 2 * rows),
            low(3, width, half),
            low(ranks, rows, width),
            low(4, 2 * rows, width),
            low(4, 2 * rows, width),
            low(4, 2 * rows, width),
            full(2 * rows, width),
            full(pairs, 2 * rows, PAIR),
            low(rows, width),
            low(4, rows, width),
            low(2, rows, half),
            low(4, 2, rows, half),
            low(2, rows, width),
            low(4, 2, rows, width),
            low(2, shard, 4 * rows),
            low(shard, 4 * rows),
            low(16, width),
            low(4, 16, width),
            low(2, shard, half),
            low(shard, half),
            low(2, rows, width),
            low(rows, width),
            low(4, size, width),
            low(4, size, width),
            low(4, size, width),
            full(size, width),
            low(4, size, width),
            low(4, size, width),
            low(4, size, width),
            full(size, width),
            low(ranks, size, width),
            low(ranks, size + 16, width),
            low(4, tall, 128),
            low(tall, 128),
            low(4, tall, 128),
            low(4, tall, 128),
            full(tall, 128),
            low(tall, 128),
            low(ranks, tall, 128),
            dma((SEMS_BACKWARD,)),
            dma((3, 8)),
            dma((3, 4)),
            dma((3, 4)),
            dma((3, 8)),
            dma((4 * ranks,)),
            dma((SEMS_RINGS,)),
        ],
        compiler_params=pltpu.CompilerParams(
            collective_id=3, has_side_effects=True, vmem_limit_bytes=VMEM_BYTES
        ),
    )(
        grad_second, tok, pack, pack_grad, n_t, m_t, qx, gm, stats, stat, cosr, sinr, kb, qb, side, dsh, kv,
        wfull, give, other,
    )


def unpack_kernel(
    result_hbm, grad_input_hbm, pack_hbm, att1_hbm, att2_hbm, sh_hbm, keep_hbm, other_hbm,
    result_out, grad_input_out, gain_one_out, gain_two_out, router_out,
    query_out, key_out, value_out, output_out, gate_out, up_out, down_out, eg_out, eu_out, ed_out,
    result, grad_input, pack, att1, att2, sh, keep, other, experts_f, both_f, down, att_f,
    gains, router, sem,
):
    sems = Sems(sem)

    def copy(src, dst):
        made = pltpu.make_async_copy(src, dst, sems.new())
        made.start()
        return made

    shard, hidden = keep.shape[1:]
    width = 4 * shard
    half = width // 2
    loads = []
    for a in range(3):
        loads.append([copy(keep_hbm.at[a], keep.at[a]), copy(other_hbm.at[a], other.at[a])])
    shared_loads = [copy(sh_hbm.at[pl.ds(4 * r, 4)], sh.at[pl.ds(4 * r, 4)]) for r in range(2)]
    att_loads = [copy(att1_hbm, att1), copy(att2_hbm, att2)]
    small = [copy(pack_hbm, pack), copy(result_hbm, result), copy(grad_input_hbm, grad_input)]
    saves = []
    for a, out in enumerate((eg_out, eu_out, ed_out)):
        for made in loads[a]:
            made.wait()
        for part in range(2):
            at = slice(shard // 2 * part, shard // 2 * (part + 1))
            experts_f[a, at] = keep[a, at].astype(F32) + other[a, at].astype(F32)
            saves.append(copy(experts_f.at[a, at], out.at[at]))
    size = shard // 2
    deep = down.shape[0] // 8
    for row in range(2):
        shared_loads[row].wait()
        rows = slice(size * row, size * (row + 1))
        for c in range(4):
            for w in range(4):
                lanes = slice(512 * w + 128 * c, 512 * w + 128 * (c + 1))
                for a in range(2):
                    start = shard * w + size * a
                    both_f[a, rows, lanes] = sh[4 * row + c, start : start + size].astype(F32)
        for a, out in enumerate((gate_out, up_out)):
            saves.append(copy(both_f.at[a, rows], out.at[rows]))
        for r in range(4 * row, 4 * row + 4):
            for t in range(width // 128):
                at = slice(width + deep * t, width + deep * (t + 1))
                lanes = slice(128 * t, 128 * (t + 1))
                down[deep * r : deep * (r + 1), lanes] = sh[r, at].astype(F32)
        rows = slice(4 * deep * row, 4 * deep * (row + 1))
        saves.append(copy(down.at[rows], down_out.at[rows]))
    for made in att_loads:
        made.wait()
    slots = att1.shape[1]
    parts = ((output_out, att1, 0), (query_out, att1, 1), (key_out, att2, 0), (value_out, att2, 1))
    for n, (out, src, low) in enumerate(parts):
        for r in range(8):
            plane, x = r // 2, r % 2
            rows, lanes = slice(slots * plane, slots * (plane + 1)), slice(half * x, half * (x + 1))
            att_f[n, rows, lanes] = src[r, 0:slots, half * low : half * (low + 1)].astype(F32)
        saves.append(copy(att_f.at[n], out))
    for made in small:
        made.wait()
    saves += [copy(result, result_out), copy(grad_input, grad_input_out)]
    back = lax.rem(4 - lax.axis_index("wt"), 4) * shard
    mine = pltpu.roll(pack[...], back, 1)
    gains[0] = mine[0:1, 0:shard]
    gains[1] = mine[1:2, 0:shard]
    router[...] = mine[2 : 2 + router.shape[0], 0:shard]
    saves += [copy(gains.at[0], gain_one_out), copy(gains.at[1], gain_two_out)]
    saves.append(copy(router, router_out))
    for made in saves:
        made.wait()


def run_unpack(result, grad_input, pack, att1, att2, sh, keep, other, experts):
    rows, width = result.shape
    shard, hidden = keep.shape[1:]
    shape = jax.ShapeDtypeStruct
    shared_hidden = sh.shape[0] * (sh.shape[1] - width) * 128 // width
    shared = 4 * shared_hidden
    any_ = pl.BlockSpec(memory_space=pl.ANY)
    return pl.pallas_call(
        unpack_kernel,
        out_shape=(
            shape((rows, width), BF),
            shape((rows, width), F32),
            shape((1, shard), F32),
            shape((1, shard), F32),
            shape((experts, shard), F32),
            *[shape((shard, width), F32)] * 4,
            *[shape((shard, shared), F32)] * 2,
            shape((shared_hidden, width), F32),
            *[shape((shard, hidden), F32)] * 3,
        ),
        in_specs=[any_] * 8,
        out_specs=tuple([any_] * 15),
        scratch_shapes=[
            VMEM((rows, width), BF),
            VMEM((rows, width), F32),
            VMEM(pack.shape, F32),
            VMEM(att1.shape, BF),
            VMEM(att2.shape, BF),
            VMEM(sh.shape, BF),
            VMEM(keep.shape, BF),
            VMEM(other.shape, BF),
            VMEM((3, shard, hidden), F32),
            VMEM((2, shard, shared), F32),
            VMEM((shared_hidden, width), F32),
            VMEM((4, shard, width), F32),
            VMEM((2, 1, shard), F32),
            VMEM((experts, shard), F32),
            pltpu.SemaphoreType.DMA((SEMS_LAYOUT,)),
        ],
        compiler_params=pltpu.CompilerParams(vmem_limit_bytes=VMEM_BYTES),
    )(result, grad_input, pack, att1, att2, sh, keep, other)


def contract_product(left, right, left_dim, right_dim):
    return lax.dot_general(
        left, right, (((left_dim,), (right_dim,)), ((), ())), preferred_element_type=jnp.float32
    )


def contract_exact(left, right, left_dim, right_dim):
    return lax.dot_general(
        left,
        right,
        (((left_dim,), (right_dim,)), ((), ())),
        precision=HIGH,
        preferred_element_type=jnp.float32,
    )


def rms_norm(values, gain):
    norm_scale = lax.rsqrt(jnp.mean(values * values, axis=-1, keepdims=True) + EPS)
    return (values * norm_scale * gain, norm_scale)


def rms_back(values, norm_scale, gain, upstream):
    weighted = upstream * gain
    inner_mean = jnp.mean(weighted * values, axis=-1, keepdims=True)
    through = norm_scale * weighted - values * norm_scale * norm_scale * norm_scale * inner_mean
    return (through, jnp.sum(upstream * values * norm_scale, axis=0))


def silu_parts(gate_part):
    sigmoid = jax.nn.sigmoid(gate_part)
    return (gate_part * sigmoid, sigmoid * (1.0 + gate_part * (1.0 - sigmoid)))


def rotate(values, place, sign):
    half_size = HD // 2
    frequency = 10000.0 ** (-jnp.arange(half_size, dtype=jnp.float32) / half_size)
    angles = place.astype(jnp.float32)[:, None] * frequency[None, :]
    cosine = jnp.cos(angles)[:, None, :]
    sine_part = sign * jnp.sin(angles)[:, None, :]
    shaped = values.reshape(values.shape[0], values.shape[1] // HD, 2, half_size)
    first_half = shaped[:, :, 0, :]
    second_half = shaped[:, :, 1, :]
    turned = jnp.stack(
        [
            first_half * cosine - second_half * sine_part,
            second_half * cosine + first_half * sine_part,
        ],
        axis=2,
    )
    return turned.reshape(values.shape)


def places(first_row, row_count, block_deal, rows_dev):
    row_index = first_row + jnp.arange(row_count, dtype=jnp.int32)
    owner_rank = row_index // rows_dev
    inner_row = row_index % rows_dev
    ranks = block_deal.shape[0]
    matches = owner_rank[:, None] == jnp.arange(ranks, dtype=jnp.int32)[None, :]
    paired = jnp.sum(jnp.where(matches, block_deal[None, :], 0), axis=1)
    piece_size = rows_dev // 2
    unit_index = jnp.where(inner_row < piece_size, paired, 2 * ranks - 1 - paired)
    return unit_index * piece_size + inner_row % piece_size


def score_block(query_side, key_rows, key_place):
    query3, query_block = query_side
    key3 = key_rows.reshape(key_rows.shape[0], -1, HD)
    raw_scores = jnp.einsum("qhd,khd->hqk", query3, key3, preferred_element_type=jnp.float32)
    allowed = (key_place // BLK)[None, None, :] <= query_block[None, :, None]
    return (jnp.where(allowed, raw_scores * HD ** (-0.5), MASKED), allowed)


def absorb(running, key_rows, value_rows, key_place, query_side):
    largest, denom, accum = running
    scores, allowed = score_block(query_side, key_rows, key_place)
    new_largest = jnp.maximum(largest, jnp.max(scores, axis=2))
    factor = jnp.exp(largest - new_largest)
    raised = jnp.where(allowed, jnp.exp(scores - new_largest[:, :, None]), 0.0)
    denom = denom * factor + jnp.sum(raised, axis=2)
    value3 = value_rows.reshape(value_rows.shape[0], -1, HD)
    accum = accum * factor.T[:, :, None] + jnp.einsum(
        "hqk,khd->qhd", raised.astype(jnp.bfloat16), value3, preferred_element_type=jnp.float32
    )
    return (new_largest, denom, accum)


def fold_keys(running, key_piece, query_side, block_deal, rows_dev):
    key_all, value_all = key_piece
    row_count = key_all.shape[0]
    block_size = KEY_ROWS

    def key_step(current, offset):
        key_rows = lax.dynamic_slice_in_dim(key_all, offset, block_size, 0)
        value_rows = lax.dynamic_slice_in_dim(value_all, offset, block_size, 0)
        key_place = places(offset, block_size, block_deal, rows_dev)
        return (absorb(current, key_rows, value_rows, key_place, query_side), None)

    offsets = jnp.arange(row_count // block_size, dtype=jnp.int32) * block_size
    running, unused = lax.scan(key_step, running, offsets)
    return running


def differentiate(query_side, log_total, delta, grad_out3, key_rows, value_rows, key_place):
    scores, allowed = score_block(query_side, key_rows, key_place)
    probs_full = jnp.where(allowed, jnp.exp(scores - log_total[:, :, None]), 0.0)
    value3 = value_rows.reshape(value_rows.shape[0], -1, HD)
    grad_probs = jnp.einsum("qhd,khd->hqk", grad_out3, value3, preferred_element_type=jnp.float32)
    grad_scores = (probs_full * (grad_probs - delta[:, :, None]) * HD ** (-0.5)).astype(
        jnp.bfloat16
    )
    return (probs_full, grad_scores)


def assign_slots(route, order, experts, capacity):
    pair_count = order.shape[0]
    expert_ids = route.reshape(pair_count)
    ordered = expert_ids[order]
    onehot = (ordered[:, None] == jnp.arange(experts, dtype=jnp.int32)[None, :]).astype(jnp.int32)
    before = jnp.cumsum(onehot, axis=0) - onehot
    slot_turn = jnp.sum(before * onehot, axis=1)
    slot_index = jnp.zeros((pair_count,), jnp.int32).at[order].set(slot_turn)
    kept_pairs = slot_index < capacity
    target = jnp.where(kept_pairs, expert_ids * capacity + slot_index, experts * capacity)
    slot_table = (
        jnp.full((experts * capacity,), pair_count, jnp.int32)
        .at[target]
        .set(jnp.arange(pair_count, dtype=jnp.int32), mode="drop")
    )
    return (target, kept_pairs, slot_table)


def body(
    tokens,
    cotangent,
    gain_attention,
    query_weight,
    key_weight,
    value_weight,
    output_weight,
    gain_mixer,
    router_weight,
    shared_gate,
    shared_up,
    shared_down,
    expert_gate,
    expert_up,
    expert_down,
    routes,
    slot_order,
    block_deal,
):
    rows_dev = tokens.shape[1]
    width = tokens.shape[2]
    ranks = lax.axis_size("ctx")
    (
        gain_one,
        query_full,
        key_full,
        value_full,
        output_full,
        gain_two,
        router_full,
        sgate_full,
        sup_full,
        sdown_full,
        expert_gate_whole,
        expert_up_whole,
        edown_full,
    ) = (
        lax.all_gather(gain_attention, "wt", axis=0, tiled=True),
        lax.all_gather(query_weight, "wt", axis=0, tiled=True),
        lax.all_gather(key_weight, "wt", axis=0, tiled=True),
        lax.all_gather(value_weight, "wt", axis=0, tiled=True),
        lax.all_gather(output_weight, "wt", axis=0, tiled=True),
        lax.all_gather(gain_mixer, "wt", axis=0, tiled=True),
        lax.all_gather(router_weight, "wt", axis=0, tiled=True),
        lax.all_gather(shared_gate, "wt", axis=0, tiled=True),
        lax.all_gather(shared_up, "wt", axis=0, tiled=True),
        lax.all_gather(shared_down, "wt", axis=0, tiled=True),
        lax.all_gather(expert_gate, "wt", axis=0, tiled=True),
        lax.all_gather(expert_up, "wt", axis=0, tiled=True),
        lax.all_gather(expert_down, "wt", axis=0, tiled=True),
    )
    gain_first = gain_one.astype(jnp.float32)
    gain_second = gain_two.astype(jnp.float32)
    heads = width // HD
    inputs = tokens[0].astype(jnp.float32)
    here = places(lax.axis_index("ctx") * rows_dev, rows_dev, block_deal, rows_dev)
    query_side_block = here // BLK
    normed_f, scale_one = rms_norm(inputs, gain_first)
    normed = normed_f.astype(jnp.bfloat16)
    query_rot = rotate(
        jnp.dot(normed, query_full, preferred_element_type=jnp.float32), here, 1.0
    ).astype(jnp.bfloat16)
    key_rot = rotate(
        jnp.dot(normed, key_full, preferred_element_type=jnp.float32), here, 1.0
    ).astype(jnp.bfloat16)
    value_low = jnp.dot(normed, value_full, preferred_element_type=jnp.float32).astype(jnp.bfloat16)
    query3 = query_rot.reshape(rows_dev, heads, HD)
    query_side = (query3, query_side_block)
    start_state = (
        jnp.full((heads, rows_dev), MASKED, jnp.float32),
        jnp.zeros((heads, rows_dev), jnp.float32),
        jnp.zeros((rows_dev, heads, HD), jnp.float32),
    )
    largest, denom, accum = fold_keys(
        start_state,
        (
            lax.all_gather(key_rot, "ctx", axis=0, tiled=True),
            lax.all_gather(value_low, "ctx", axis=0, tiled=True),
        ),
        query_side,
        block_deal,
        rows_dev,
    )
    mixed3 = accum / denom.T[:, :, None]
    log_total = largest + jnp.log(denom)
    mixed_low = mixed3.reshape(rows_dev, width).astype(jnp.bfloat16)
    second = inputs + jnp.dot(mixed_low, output_full, preferred_element_type=jnp.float32)
    mixer_f, scale_two = rms_norm(second, gain_second)
    mixer = mixer_f.astype(jnp.bfloat16)
    experts = router_full.shape[1]
    logits = jnp.dot(mixer, router_full, preferred_element_type=jnp.float32)
    route = routes[0]
    top_count = route.shape[1]
    pair_count = rows_dev * top_count
    capacity = (5 * pair_count + 4 * experts - 1) // (4 * experts)
    split_count = ranks // experts
    expert_match = route[:, :, None] == jnp.arange(experts, dtype=jnp.int32)[None, None, :]
    chosen = jnp.sum(jnp.where(expert_match, logits[:, None, :], 0.0), axis=2)
    gates = jax.nn.softmax(chosen, axis=1)
    target, kept_pairs, slot_table = assign_slots(route, slot_order[0, 0], experts, capacity)
    valid = slot_table < pair_count
    pair_pick = jnp.minimum(slot_table, pair_count - 1)
    target_pick = jnp.minimum(target, experts * capacity - 1)
    send_rows = jnp.where(
        valid[:, None], mixer[pair_pick // top_count], jnp.zeros((), jnp.bfloat16)
    )
    send_rows = jnp.broadcast_to(
        send_rows.reshape(experts, 1, capacity, width), (experts, split_count, capacity, width)
    ).reshape(ranks, capacity, width)
    received = lax.all_to_all(send_rows, "ctx", split_axis=0, concat_axis=0, tiled=True)
    slot_count = received.shape[1]
    flattened_input = received.reshape(ranks * slot_count, width)
    gate_part = jnp.dot(flattened_input, expert_gate_whole, preferred_element_type=jnp.float32)
    up_projection_part = jnp.dot(
        flattened_input, expert_up_whole, preferred_element_type=jnp.float32
    )
    activated, unused = silu_parts(gate_part)
    hidden = (activated * up_projection_part).astype(jnp.bfloat16)
    partial_value = contract_product(hidden, edown_full, 1, 1).reshape(ranks, slot_count, width)
    back = lax.all_to_all(
        partial_value.astype(jnp.bfloat16), "ctx", split_axis=0, concat_axis=0, tiled=True
    ).astype(partial_value.dtype)
    expert_gate_part = gate_part.reshape(ranks, slot_count, -1)
    expert_up_part = up_projection_part.reshape(ranks, slot_count, -1)
    combined = jnp.sum(back.reshape(experts, split_count, capacity, width), axis=1).reshape(
        experts * capacity, width
    )
    pair_out = jnp.where(kept_pairs[:, None], combined[target_pick], 0.0).reshape(
        rows_dev, top_count, width
    )
    mixture = jnp.sum(gates[:, :, None] * pair_out, axis=1)
    sgate_part = jnp.dot(mixer, sgate_full, preferred_element_type=jnp.float32)
    sup_part = jnp.dot(mixer, sup_full, preferred_element_type=jnp.float32)
    shared_act, shared_slope = silu_parts(sgate_part)
    shared_hidden = (shared_act * sup_part).astype(jnp.bfloat16)
    shared_out = jnp.dot(shared_hidden, sdown_full, preferred_element_type=jnp.float32)
    result = (second + mixture + shared_out).astype(jnp.bfloat16)
    grad_final = cotangent[0].astype(jnp.float32)
    grad_low = grad_final.astype(jnp.bfloat16)
    sdown_grad = contract_product(shared_hidden, grad_low, 0, 0)
    grad_shared_hidden = contract_product(grad_low, sdown_full, 1, 1)
    grad_sgate = (grad_shared_hidden * sup_part * shared_slope).astype(jnp.bfloat16)
    grad_sup = (grad_shared_hidden * shared_act).astype(jnp.bfloat16)
    sgate_grad = contract_product(mixer, grad_sgate, 0, 0)
    sup_grad = contract_product(mixer, grad_sup, 0, 0)
    grad_mixer = contract_product(grad_sgate, sgate_full, 1, 1) + contract_product(
        grad_sup, sup_full, 1, 1
    )
    pair_grad = (
        (gates[:, :, None] * grad_final[:, None, :]).reshape(pair_count, width).astype(jnp.bfloat16)
    )
    grad_gates = jnp.sum(grad_final[:, None, :] * pair_out, axis=2)
    send_grad = jnp.where(valid[:, None], pair_grad[pair_pick], jnp.zeros((), jnp.bfloat16))
    send_grad = jnp.broadcast_to(
        send_grad.reshape(experts, 1, capacity, width), (experts, split_count, capacity, width)
    ).reshape(ranks, capacity, width)
    recv_grad = lax.all_to_all(send_grad, "ctx", split_axis=0, concat_axis=0, tiled=True)
    flattened_input = received.reshape(ranks * capacity, width)
    flat_grad = recv_grad.reshape(ranks * capacity, width)
    gate_flat = expert_gate_part.reshape(ranks * capacity, -1)
    up_flat = expert_up_part.reshape(ranks * capacity, -1)
    expert_activation, expert_slope = silu_parts(gate_flat)
    expert_hidden = (expert_activation * up_flat).astype(jnp.bfloat16)
    edown_grad = contract_product(flat_grad, expert_hidden, 0, 0)
    expert_hidden_grad = jnp.dot(flat_grad, edown_full, preferred_element_type=jnp.float32)
    expert_gate_grad_rows = (expert_hidden_grad * up_flat * expert_slope).astype(jnp.bfloat16)
    expert_up_grad_rows = (expert_hidden_grad * expert_activation).astype(jnp.bfloat16)
    egate_grad = contract_product(flattened_input, expert_gate_grad_rows, 0, 0)
    expert_up_weight_grad = contract_product(flattened_input, expert_up_grad_rows, 0, 0)
    input_back = (
        contract_product(expert_gate_grad_rows, expert_gate_whole, 1, 1)
        + contract_product(expert_up_grad_rows, expert_up_whole, 1, 1)
    ).reshape(ranks, capacity, width)
    back_grad = lax.all_to_all(
        input_back.astype(jnp.bfloat16), "ctx", split_axis=0, concat_axis=0, tiled=True
    ).astype(input_back.dtype)
    merged = jnp.sum(back_grad.reshape(experts, split_count, capacity, width), axis=1).reshape(
        experts * capacity, width
    )
    pair_back = jnp.where(kept_pairs[:, None], merged[target_pick], 0.0).reshape(
        rows_dev, top_count, width
    )
    grad_mixer = grad_mixer + jnp.sum(pair_back, axis=1)
    grad_chosen = gates * (grad_gates - jnp.sum(gates * grad_gates, axis=1, keepdims=True))
    grad_logits = jnp.sum(jnp.where(expert_match, grad_chosen[:, :, None], 0.0), axis=1)
    router_grad = contract_exact(mixer.astype(jnp.float32), grad_logits, 0, 0)
    grad_mixer = grad_mixer + contract_exact(grad_logits, router_full.astype(jnp.float32), 1, 1)
    through_two, gain_two_grad = rms_back(second, scale_two, gain_second, grad_mixer)
    grad_second = grad_final + through_two
    grad_attention = grad_second.astype(jnp.bfloat16)
    output_grad = contract_product(mixed_low, grad_attention, 0, 0)
    grad_mixed = contract_product(grad_attention, output_full, 1, 1).astype(jnp.bfloat16)
    grad_out3 = grad_mixed.reshape(rows_dev, heads, HD)
    delta = jnp.sum(grad_out3.astype(jnp.float32) * mixed3, axis=2).T
    all_keys, all_values = (
        lax.all_gather(key_rot, "ctx", axis=0, tiled=True),
        lax.all_gather(value_low, "ctx", axis=0, tiled=True),
    )
    total_rows = all_keys.shape[0]
    block_size = KEY_ROWS

    def query_step(grad_sum, offset):
        key_rows = lax.dynamic_slice_in_dim(all_keys, offset, block_size, 0)
        value_rows = lax.dynamic_slice_in_dim(all_values, offset, block_size, 0)
        key_place = places(offset, block_size, block_deal, rows_dev)
        unused, grad_scores = differentiate(
            query_side, log_total, delta, grad_out3, key_rows, value_rows, key_place
        )
        key3 = key_rows.reshape(block_size, heads, HD)
        return (
            grad_sum
            + jnp.einsum("hqk,khd->qhd", grad_scores, key3, preferred_element_type=jnp.float32),
            None,
        )

    offsets = jnp.arange(total_rows // block_size, dtype=jnp.int32) * block_size
    grad_query3, unused = lax.scan(
        query_step, jnp.zeros((rows_dev, heads, HD), jnp.float32), offsets
    )
    inner_size = KEY_ROWS

    def one_part(offset):
        key_rows = lax.dynamic_slice_in_dim(all_keys, offset, inner_size, 0)
        value_rows = lax.dynamic_slice_in_dim(all_values, offset, inner_size, 0)
        key_place = places(offset, inner_size, block_deal, rows_dev)
        probs_full, grad_scores = differentiate(
            query_side, log_total, delta, grad_out3, key_rows, value_rows, key_place
        )
        grad_value_rows = jnp.einsum(
            "hqk,qhd->khd",
            probs_full.astype(jnp.bfloat16),
            grad_out3,
            preferred_element_type=jnp.float32,
        )
        grad_key_rows = jnp.einsum(
            "hqk,qhd->khd", grad_scores, query3, preferred_element_type=jnp.float32
        )
        return jnp.concatenate(
            [grad_key_rows.reshape(inner_size, width), grad_value_rows.reshape(inner_size, width)],
            axis=1,
        )

    parts = lax.map(
        one_part,
        jnp.arange(lax.axis_size("ctx") * rows_dev // inner_size, dtype=jnp.int32) * inner_size,
    )
    key_value_grad = lax.psum_scatter(
        parts.reshape(lax.axis_size("ctx") * rows_dev, 2 * width),
        "ctx",
        scatter_dimension=0,
        tiled=True,
    )
    grad_key_pre = rotate(key_value_grad[:, :width], here, -1.0).astype(jnp.bfloat16)
    grad_value_low = key_value_grad[:, width:].astype(jnp.bfloat16)
    grad_query_pre = rotate(grad_query3.reshape(rows_dev, width), here, -1.0).astype(jnp.bfloat16)
    query_grad = contract_product(normed, grad_query_pre, 0, 0)
    key_grad = contract_product(normed, grad_key_pre, 0, 0)
    value_grad = contract_product(normed, grad_value_low, 0, 0)
    grad_normed = (
        contract_product(grad_query_pre, query_full, 1, 1)
        + contract_product(grad_key_pre, key_full, 1, 1)
        + contract_product(grad_value_low, value_full, 1, 1)
    )
    through_one, gain_one_grad = rms_back(inputs, scale_one, gain_first, grad_normed)
    grad_input = grad_second + through_one
    (
        gain_one_share,
        query_share,
        key_share,
        value_share,
        output_share,
        gain_two_share,
        router_share,
        sgate_share,
        sup_share,
        sdown_share,
        egate_share,
        expert_up_portion,
        edown_share,
    ) = (
        lax.psum_scatter(
            gain_one_grad.astype(jnp.bfloat16), "wt", scatter_dimension=0, tiled=True
        ).astype(jnp.float32),
        lax.psum_scatter(
            query_grad.astype(jnp.bfloat16), "wt", scatter_dimension=0, tiled=True
        ).astype(jnp.float32),
        lax.psum_scatter(
            key_grad.astype(jnp.bfloat16), "wt", scatter_dimension=0, tiled=True
        ).astype(jnp.float32),
        lax.psum_scatter(
            value_grad.astype(jnp.bfloat16), "wt", scatter_dimension=0, tiled=True
        ).astype(jnp.float32),
        lax.psum_scatter(
            output_grad.astype(jnp.bfloat16), "wt", scatter_dimension=0, tiled=True
        ).astype(jnp.float32),
        lax.psum_scatter(
            gain_two_grad.astype(jnp.bfloat16), "wt", scatter_dimension=0, tiled=True
        ).astype(jnp.float32),
        lax.psum_scatter(
            router_grad.astype(jnp.bfloat16), "wt", scatter_dimension=0, tiled=True
        ).astype(jnp.float32),
        lax.psum_scatter(
            sgate_grad.astype(jnp.bfloat16), "wt", scatter_dimension=0, tiled=True
        ).astype(jnp.float32),
        lax.psum_scatter(
            sup_grad.astype(jnp.bfloat16), "wt", scatter_dimension=0, tiled=True
        ).astype(jnp.float32),
        lax.psum_scatter(
            sdown_grad.astype(jnp.bfloat16), "wt", scatter_dimension=0, tiled=True
        ).astype(jnp.float32),
        lax.psum_scatter(
            egate_grad.astype(jnp.bfloat16), "wt", scatter_dimension=0, tiled=True
        ).astype(jnp.float32),
        lax.psum_scatter(
            expert_up_weight_grad.astype(jnp.bfloat16), "wt", scatter_dimension=0, tiled=True
        ).astype(jnp.float32),
        lax.psum_scatter(
            edown_grad.astype(jnp.bfloat16), "wt", scatter_dimension=0, tiled=True
        ).astype(jnp.float32),
    )
    (
        gain_one_sum,
        query_sum,
        key_sum,
        value_sum,
        output_sum,
        gain_two_sum,
        router_sum,
        sgate_sum,
        sup_sum,
        sdown_sum,
    ) = lax.psum(
        (
            gain_one_share,
            query_share,
            key_share,
            value_share,
            output_share,
            gain_two_share,
            router_share,
            sgate_share,
            sup_share,
            sdown_share,
        ),
        "ctx",
    )
    return (
        result[None],
        grad_input[None],
        gain_one_sum,
        query_sum,
        key_sum,
        value_sum,
        output_sum,
        gain_two_sum,
        router_sum,
        sgate_sum,
        sup_sum,
        sdown_sum,
        egate_share,
        expert_up_portion,
        edown_share,
    )


def fast_body(
    tokens,
    cotangent,
    gain_attention,
    query_weight,
    key_weight,
    value_weight,
    output_weight,
    gain_mixer,
    router_weight,
    shared_gate,
    shared_up,
    shared_down,
    expert_gate,
    expert_up,
    expert_down,
    routes,
    slot_order,
    block_deal,
):
    half_size = HD // 2
    frequency = 10000.0 ** (-np.arange(half_size) / half_size)
    frequency = jnp.asarray(np.tile(frequency, 4)[None].astype(np.float32))
    (
        cosr, sinr, kb, qb, qx, gm, stats, stat, n_t, m_t, pack_all, result, grad_second, pack_grad, dsh,
        side, kv_all, wfull, keep, give, other,
    ) = run_forward(
        tokens[0], gain_attention, gain_mixer, router_weight.T, frequency, block_deal,
        cotangent[0], routes[0].T, slot_order[0],
        shared_down, query_weight, key_weight, value_weight, output_weight, shared_gate, shared_up,
        expert_gate, expert_up, expert_down,
    )
    grad_input, pack_sum, att1, att2, sh, other = run_backward(
        grad_second, tokens[0], pack_all, pack_grad, n_t, m_t, qx, gm, stats, stat, cosr, sinr, kb, qb,
        side, dsh, kv_all, wfull, give, other,
    )
    (
        result, grad_input, gain_one, gain_two, router, query, key, value, output, gate, up, down,
        eg, eu, ed,
    ) = run_unpack(
        result, grad_input, pack_sum, att1, att2, sh, keep, other, router_weight.shape[1]
    )
    return (
        result[None], grad_input[None], gain_one.reshape(-1), query, key, value, output,
        gain_two.reshape(-1), router.T, gate, up, down, eg, eu, ed,
    )


def solution(mesh):
    in_specs = (
        P("wt", "ctx", None),
        P("wt", "ctx", None),
        P("wt"),
        P("wt", None),
        P("wt", None),
        P("wt", None),
        P("wt", None),
        P("wt"),
        P("wt", None),
        P("wt", None),
        P("wt", None),
        P("wt", None),
        P("wt", "ctx"),
        P("wt", "ctx"),
        P("wt", "ctx"),
        P("wt", "ctx", None),
        P("wt", "ctx", None),
        P(),
    )
    out_specs = (
        P("wt", "ctx", None),
        P("wt", "ctx", None),
        P("wt"),
        P("wt", None),
        P("wt", None),
        P("wt", None),
        P("wt", None),
        P("wt"),
        P("wt", None),
        P("wt", None),
        P("wt", None),
        P("wt", None),
        P("wt", "ctx"),
        P("wt", "ctx"),
        P("wt", "ctx"),
    )
    chosen = fast_body if (mesh.shape["ctx"], mesh.shape["wt"]) == (8, 4) else body
    return jax.shard_map(chosen, mesh=mesh, in_specs=in_specs, out_specs=out_specs, check_vma=False)
```

```python
import jax
import jax.numpy as jnp
import numpy as np
from jax import lax
from jax.experimental import pallas as pl
from jax.experimental.pallas import tpu as pltpu
from jax.sharding import PartitionSpec as P

HD = 64
BLK = 256


EPS = 1e-06
KEY_ROWS = 512
HIGH = lax.Precision.HIGHEST
MASKED = -1e30


MESH = pl.DeviceIdType.MESH
VMEM = pltpu.VMEM
BF = jnp.bfloat16
F32 = jnp.float32
PAIR = 2 * HD
VMEM_BYTES = 127 * 2**19
SEMS_FORWARD = 204
SEMS_BACKWARD = 102
SEMS_RINGS = 48
SEMS_LAYOUT = 40


class Spot:
    def __init__(self, line_size):
        self.k = lax.axis_index("ctx")
        self.w = lax.axis_index("wt")
        self.z, self.x = lax.div(self.k, 2), lax.rem(self.k, 2)
        self.y, self.c = lax.div(self.w, 2), lax.rem(self.w, 2)
        self.far = lax.div(self.z, 2)
        self.mid = self.z + self.far * (3 - 2 * self.z)
        step = 1 - 2 * self.far
        self.core = (self.k, 2 * self.y + 1 - self.c)
        self.across = (self.k, 2 * (1 - self.y) + self.c)
        self.corner = (self.k, 2 * (1 - self.y) + 1 - self.c)
        self.column = (2 * self.z + 1 - self.x, self.w)
        self.odd = lax.rem(self.z, 2)
        self.line = (2 * (self.z + 1 - 2 * self.odd) + self.x, self.w)
        self.inner = (2 * (self.z + step) + self.x, self.w)
        self.outer = (2 * (self.z - step) + self.x, self.w)

    def plane(self, step):
        mirrored = (self.mid, 1 - self.mid, 2, 3)[step]
        return mirrored + self.far * (3 - 2 * mirrored)


class Sems:
    def __init__(self, ref):
        self.ref, self.used = ref, 0

    def new(self):
        self.used += 1
        return self.ref.at[self.used - 1]


def remote(src, dst, send, recv, to):
    return pltpu.make_async_remote_copy(
        src_ref=src, dst_ref=dst, send_sem=send, recv_sem=recv, device_id=to, device_id_type=MESH
    )


def greet(devices, middle=None):
    barrier = pltpu.get_barrier_semaphore()
    for to in devices:
        pl.semaphore_signal(barrier, inc=1, device_id=to, device_id_type=MESH)
    if middle is None:
        pl.semaphore_wait(barrier, len(devices))
        return

    @pl.when(middle[0] == 1)
    def _():
        pl.semaphore_signal(barrier, inc=1, device_id=middle[1], device_id_type=MESH)

    pl.semaphore_wait(barrier, len(devices) + middle[0])


class Gather:
    def __init__(self, spot, src, place, sems, local=True):
        self.spot, self.place, self.sems = spot, place, sems
        here = place(spot.w)
        self.local = pltpu.make_async_copy(src, here, sems.new()) if local else None
        self.to_core = remote(src, here, sems.new(), sems.new(), spot.core)
        self.to_across = remote(src, here, sems.new(), sems.new(), spot.across)
        self.to_across.start()
        self.to_core.start()
        if local:
            self.local.start()

    def forward(self):
        self.to_across.wait_recv()
        part = self.place(self.spot.across[1])
        self.onward = remote(part, part, self.sems.new(), self.sems.new(), self.spot.core)
        self.onward.start()

    def finish(self):
        if self.local is not None:
            self.local.wait()
        self.to_core.wait_recv()
        self.onward.wait_recv()

    def drain(self):
        for copy in (self.to_core, self.to_across, self.onward):
            copy.wait_send()


class Share:
    def __init__(self, spot, src, dst, sems, mate, bit):
        self.spot, self.dst, self.sems, self.mate, self.bit = spot, dst, sems, mate, bit
        self.rows = src.shape[0]
        self.half = self.rows // 2
        here = dst.at[pl.ds(pl.multiple_of(self.rows * spot.w, 64), self.rows)]
        half = pl.ds(pl.multiple_of(self.half * bit, 32), self.half)
        self.local = pltpu.make_async_copy(src, here, sems.new())
        self.to_core = remote(src, here, sems.new(), sems.new(), spot.core)
        self.to_across = remote(
            src.at[half], self.part(spot.w, bit), sems.new(), sems.new(), spot.across
        )
        for copy in (self.to_across, self.to_core, self.local):
            copy.start()

    def part(self, w, bit):
        return self.dst.at[pl.ds(pl.multiple_of(self.rows * w + self.half * bit, 32), self.half)]

    def forward(self):
        spot = self.spot
        self.to_across.wait_recv()
        part = self.part(spot.across[1], self.bit)
        self.aside = remote(part, part, self.sems.new(), self.sems.new(), self.mate)
        self.onward = remote(part, part, self.sems.new(), self.sems.new(), spot.core)
        self.aside.start()
        self.onward.start()

    def second(self):
        self.aside.wait_recv()
        part = self.part(self.spot.across[1], 1 - self.bit)
        self.rest = remote(part, part, self.sems.new(), self.sems.new(), self.spot.core)
        self.rest.start()

    def finish(self):
        self.local.wait()
        self.to_core.wait_recv()
        self.onward.wait_recv()
        self.rest.wait_recv()

    def drain(self):
        for copy in (self.to_core, self.to_across, self.aside, self.onward, self.rest):
            copy.wait_send()


class Quarters:
    def __init__(self, spot, src, dst, sems, columns=False):
        self.spot, self.dst, self.sems, self.columns = spot, dst, sems, columns
        self.rows = src.shape[0]
        self.size = self.rows // 4
        self.q = 2 * spot.x + spot.odd
        self.sources = (spot.across, spot.corner) if columns else (spot.across,)
        cols = dst.shape[1]

        def take(to, quarter):
            at = pl.ds(pl.multiple_of(self.size * self.q, 16), self.size)
            if not columns:
                return src.at[at] if quarter else src
            lanes = pl.ds(pl.multiple_of(cols * to, cols), cols)
            return src.at[at, lanes] if quarter else src.at[:, lanes]

        here = dst.at[pl.ds(pl.multiple_of(self.rows * spot.w, 64), self.rows)]
        self.far = [
            remote(take(to[1], True), self.part(spot.w, self.q), sems.new(), sems.new(), to)
            for to in self.sources
        ]
        self.to_core = remote(take(spot.core[1], False), here, sems.new(), sems.new(), spot.core)
        self.local = pltpu.make_async_copy(take(spot.w, False), here, sems.new())
        for copy in self.far + [self.to_core, self.local]:
            copy.start()
        self.lines, self.sides, self.cores = [], [], []

    def part(self, w, q, count=1):
        start = pl.multiple_of(self.rows * w + self.size * q, 16)
        return self.dst.at[pl.ds(start, self.size * count)]

    def send(self, copies, part, to):
        copies.append(remote(part, part, self.sems.new(), self.sems.new(), to))
        copies[-1].start()

    def forward(self):
        for copy, source in zip(self.far, self.sources):
            copy.wait_recv()
            part = self.part(source[1], self.q)
            self.send(self.lines, part, self.spot.line)
            self.send(self.sides, part, self.spot.column)
            if not self.columns:
                self.send(self.cores, part, self.spot.core)

    def second(self):
        for copy, source in zip(self.lines, self.sources):
            copy.wait_recv()
            part = self.part(source[1], 2 * self.spot.x + 1 - self.spot.odd)
            self.send(self.sides, part, self.spot.column)
            if not self.columns:
                self.send(self.cores, part, self.spot.core)

    def third(self):
        for copy in self.sides:
            copy.wait_recv()
        if not self.columns:
            part = self.part(self.spot.across[1], 2 * (1 - self.spot.x), 2)
            self.send(self.cores, part, self.spot.core)

    def finish(self):
        self.local.wait()
        self.to_core.wait_recv()
        for copy in self.cores:
            copy.wait_recv()

    def drain(self):
        for copy in self.far + self.lines + self.sides + self.cores + [self.to_core]:
            copy.wait_send()


class Merge:
    def __init__(self, spot, send, land, sems):
        self.spot, self.send, self.land = spot, send, land
        self.far = remote(
            send.at[spot.corner[1]], land.at[0], sems.new(), sems.new(), spot.core
        )
        self.near = remote(send.at[spot.core[1]], land.at[1], sems.new(), sems.new(), spot.core)
        self.over = remote(
            send.at[spot.across[1]], land.at[2], sems.new(), sems.new(), spot.across
        )
        self.far.start()
        self.near.start()

    def forward(self):
        self.far.wait_recv()
        block = self.send.at[self.spot.across[1]]
        block[...] = (block[...].astype(F32) + self.land[0].astype(F32)).astype(BF)
        self.over.start()

    def finish(self):
        self.near.wait_recv()
        self.over.wait_recv()
        own = self.send[self.spot.w].astype(F32)
        return own + self.land[1].astype(F32) + self.land[2].astype(F32)

    def drain(self):
        for copy in (self.far, self.near, self.over):
            copy.wait_send()


class Spread:
    def __init__(self, spot, pick, place, sems):
        self.copies = []
        for to in (spot.across, spot.corner, spot.core):
            self.copies.append(remote(pick(to[1]), place(spot.w), sems.new(), sems.new(), to))
        self.local = pltpu.make_async_copy(pick(spot.w), place(spot.w), sems.new())
        for copy in self.copies:
            copy.start()
        self.local.start()

    def finish(self):
        for copy in self.copies:
            copy.wait_recv()
        self.local.wait()

    def drain(self):
        for copy in self.copies:
            copy.wait_send()


def nt(left, right):
    return lax.dot_general(left, right, (((1,), (1,)), ((), ())), preferred_element_type=F32)


def nn(left, right):
    return jnp.dot(left, right, preferred_element_type=F32)


def tn(left, right):
    return lax.dot_general(left, right, (((0,), (0,)), ((), ())), preferred_element_type=F32)


def turn(values, cosine, sine):
    wide = values.shape[1]
    lane = lax.broadcasted_iota(jnp.int32, values.shape, 1)
    first = lax.rem(lane, HD) < HD // 2
    swapped = jnp.where(
        first, pltpu.roll(values, wide - HD // 2, 1), pltpu.roll(values, HD // 2, 1)
    )
    copies = wide // PAIR
    cosine = jnp.concatenate([cosine] * copies, axis=1)
    sine = jnp.concatenate([sine] * copies, axis=1)
    return values * cosine + swapped * sine


def stack_pair(values):
    lane = lax.broadcasted_iota(jnp.int32, values.shape, 1)
    none = jnp.zeros_like(values)
    return jnp.concatenate(
        [jnp.where(lane < HD, values, none), jnp.where(lane < HD, none, values)], axis=0
    )


def unstack_pair(values):
    rows = values.shape[0] // 2
    lane = lax.broadcasted_iota(jnp.int32, (rows, PAIR), 1)
    return jnp.where(lane < HD, values[:rows], values[rows:])


class Ring:
    def __init__(self, spot, blocks, recv, send, parts=1, sides=1, first=(0, 0)):
        self.spot, self.blocks, self.recv, self.send, self.parts = spot, blocks, recv, send, parts
        self.sides = sides
        self.ranks = blocks.shape[0]
        self.first, self.used = first[0], first[1]
        self.sent, self.sent_mid, self.sent_end = [], [], []

    def piece(self, slot, part):
        if self.sides == 1:
            rows = self.blocks.shape[1] // self.parts
            return self.blocks.at[slot, pl.ds(rows * part, rows)]
        high = self.parts // self.sides
        rows, lanes = self.blocks.shape[1] // high, self.blocks.shape[2] // self.sides
        return self.blocks.at[
            slot, pl.ds(rows * (part % high), rows), pl.ds(lanes * (part // high), lanes)
        ]

    def copy(self, slot, part, to):
        self.used += 1
        return remote(
            self.piece(slot, part),
            self.piece(slot, part),
            self.send.at[self.used - 1],
            self.recv.at[self.first + slot + self.ranks * part],
            to,
        )

    def arrived(self, slot, part):
        remote(
            self.piece(slot, part),
            self.piece(slot, part),
            self.send.at[0],
            self.recv.at[self.first + slot + self.ranks * part],
            self.spot.column,
        ).wait_recv()

    def start(self, parts=None, only=None):
        spot = self.spot
        for part in range(self.parts) if parts is None else parts:
            own = self.copy(spot.k, part, spot.inner)
            side = self.copy(spot.k, part, spot.column)
            back = self.copy(spot.k, part, spot.outer) if only != 0 else None
            if only is None:
                own.start()
                self.middle(back)
                side.start()
                self.sent += [own, side]
                self.sent_mid += [back]
                continue

            @pl.when(spot.mid == only)
            def _(copies=(own, back, side)):
                for copy in copies:
                    if copy is not None:
                        copy.start()

            if only == 1:
                self.sent_mid += [own, back, side]
            else:
                self.sent_end += [own, side]

    def middle(self, copy):
        @pl.when(self.spot.mid == 1)
        def _():
            copy.start()

    def step(self, number, only=None):
        spot = self.spot
        slot = 2 * spot.plane(number) + spot.x
        onward = spot.inner if number == 1 else spot.outer
        pieces = []
        for part in range(self.parts):
            along = self.copy(slot, part, onward) if only != 0 else None
            pieces.append((along, self.copy(slot, part, spot.column)))
        if only != 0:

            @pl.when(spot.mid == 1)
            def _():
                for part, (along, side) in enumerate(pieces):
                    self.arrived(slot, part)
                    along.start()
                    side.start()

        if only != 1:

            @pl.when(spot.mid == 0)
            def _():
                for part, (along, side) in enumerate(pieces):
                    self.arrived(slot, part)
                    side.start()

        if only != 0:
            self.sent_mid += [along for along, _ in pieces]
            self.sent_mid += [side for _, side in pieces]
        if only != 1:
            self.sent_end += [side for _, side in pieces]

    def other(self, number):
        for part in range(self.parts):
            self.arrived(2 * self.spot.plane(number) + 1 - self.spot.x, part)

    def drain(self):
        for copy in self.sent:
            copy.wait_send()
        for role, copies in ((0, self.sent_end), (1, self.sent_mid)):

            @pl.when(self.spot.mid == role)
            def _(copies=copies):
                for copy in copies:
                    copy.wait_send()


class Reduce:
    def __init__(self, spot, part, sides, zo, zi, sems, folded=False, parts=1):
        self.spot, self.part, self.sides, self.zo, self.zi = spot, part, sides, zo, zi
        self.z_send, self.zo_recv = sems.at[0], sems.at[1]
        if folded:
            self.zi_recv = sems.at[2]
        else:
            self.x_send, self.x_recv = sems.at[2], sems.at[3]
        self.folded, self.parts = folded, parts
        self.rows = part.shape[1] // parts
        self.sent, self.sent_end, self.sent_mid = [], [], []

    def cut(self, ref, index, h):
        return ref.at[index, pl.ds(self.rows * h, self.rows)]

    def own(self, plane, h):
        return self.cut(self.part, plane if self.folded else 2 * plane + self.spot.x, h)

    def wait(self, land, recv, plane, h):
        piece = self.cut(land, plane, h)
        at = plane + 4 * h
        remote(piece, piece, self.z_send.at[at], recv.at[at], self.spot.column).wait_recv()

    def side(self, number):
        spot = self.spot
        plane = spot.plane(number)
        for h in range(self.parts):
            at = plane + 4 * h
            copy = remote(
                self.cut(self.part, 2 * plane + 1 - spot.x, h),
                self.cut(self.sides, plane, h),
                self.x_send.at[at],
                self.x_recv.at[at],
                spot.column,
            )
            copy.start()
            self.sent.append(copy)

    def add(self, ref, land):
        ref[...] = (ref[...].astype(F32) + land[...].astype(F32)).astype(BF)

    def meet(self, number, launch):
        plane = self.spot.plane(number)
        for h in range(self.parts):
            self.wait(self.sides, self.x_recv, plane, h)
            self.add(self.own(plane, h), self.cut(self.sides, plane, h))
            if launch:
                self.launch_part(number, h)

    def launch(self, number):
        for h in range(self.parts):
            self.launch_part(number, h)

    def launch_part(self, number, h):
        plane = self.spot.plane(number)
        at = plane + 4 * h
        copy = remote(
            self.own(plane, h),
            self.cut(self.zo, plane, h),
            self.z_send.at[at],
            self.zo_recv.at[at],
            self.spot.inner,
        )

        @pl.when(self.spot.mid == 0)
        def _():
            copy.start()

        self.sent_end.append(copy)

    def absorb(self, number):
        plane = self.spot.plane(number)

        @pl.when(self.spot.mid == 1)
        def _():
            for h in range(self.parts):
                self.wait(self.zo, self.zo_recv, plane, h)
                self.add(self.own(plane, h), self.cut(self.zo, plane, h))

    def relay(self, number, settled=False, parts=None):
        plane = self.spot.plane(number)
        land, recv = (self.zi, self.zi_recv) if number == 1 else (self.zo, self.zo_recv)
        copies = []
        for h in range(self.parts) if parts is None else parts:
            at = plane + 4 * h
            copy = remote(
                self.own(plane, h),
                self.cut(self.zi, plane, h),
                self.z_send.at[at],
                self.zi_recv.at[at],
                self.spot.outer if number == 1 else self.spot.inner,
            )
            copies.append((h, copy))

        @pl.when(self.spot.mid == 1)
        def _():
            for h, copy in copies:
                if not settled:
                    self.wait(land, recv, plane, h)
                    self.add(self.own(plane, h), self.cut(land, plane, h))
                copy.start()

        self.sent_mid += [copy for _, copy in copies]

    def last(self, result, parts=None):
        plane = self.spot.plane(0)
        parts = range(self.parts) if parts is None else parts
        for h in parts:
            self.wait(self.zi, self.zi_recv, plane, h)
            rows = pl.ds(self.rows * h, self.rows)
            total = self.own(plane, h)[...].astype(F32)
            result[rows] = total + self.cut(self.zi, plane, h)[...].astype(F32)

        @pl.when(self.spot.mid == 1)
        def _():
            for h in parts:
                self.wait(self.zo, self.zo_recv, plane, h)
                rows = pl.ds(self.rows * h, self.rows)
                result[rows] += self.cut(self.zo, plane, h)[...].astype(F32)

    def drain(self):
        for copy in self.sent:
            copy.wait_send()

        @pl.when(self.spot.mid == 0)
        def _():
            for copy in self.sent_end:
                copy.wait_send()

        @pl.when(self.spot.mid == 1)
        def _():
            for copy in self.sent_mid:
                copy.wait_send()


def swish(values):
    sigmoid = 1.0 / (1.0 + jnp.exp(-values))
    return values * sigmoid, sigmoid * (1.0 + values * (1.0 - sigmoid))


class Exchange:
    def __init__(self, spot, out, back, send, recv):
        self.spot, self.out, self.back = spot, out, back
        self.send, self.recv, self.ranks = send, recv, out.shape[0]
        self.copies = []

    def start(self):
        spot = self.spot
        for offset in range(1, self.ranks):
            peer = lax.rem(spot.k + offset, self.ranks)
            self.copies.append(
                remote(
                    self.out.at[peer],
                    self.back.at[spot.k],
                    self.send.at[offset],
                    self.recv.at[spot.k],
                    (peer, spot.w),
                )
            )
            self.copies[-1].start()
        self.back[spot.k] = self.out[spot.k]

    def finish(self):
        spot = self.spot
        for offset in range(1, self.ranks):
            peer = lax.rem(spot.k + offset, self.ranks)
            remote(
                self.out.at[peer],
                self.back.at[peer],
                self.send.at[offset],
                self.recv.at[peer],
                (peer, spot.w),
            ).wait_recv()

    def drain(self):
        for copy in self.copies:
            copy.wait_send()


def fold_rows(values, ref):
    ranks = ref.shape[0]
    slots = values.shape[0] // ranks
    for e in range(ranks):
        part = values[slots * e : slots * (e + 1)]
        tiles = [part[:, 128 * t : 128 * (t + 1)] for t in range(values.shape[1] // 128)]
        ref[e] = jnp.concatenate(tiles, axis=0).astype(BF)


def unfold_rows(ref, slots):
    parts = []
    for e in range(ref.shape[0]):
        part = ref[e].astype(F32)
        tiles = [part[slots * t : slots * (t + 1)] for t in range(part.shape[0] // slots)]
        parts.append(jnp.concatenate(tiles, axis=1))
    return jnp.concatenate(parts, axis=0).astype(BF)


def split_three(values):
    high = values.astype(BF)
    rest = values - high.astype(F32)
    middle = rest.astype(BF)
    return high, middle, (rest - middle.astype(F32)).astype(BF)


def diagonal(values, axis):
    size = max(values.shape)
    down = lax.broadcasted_iota(jnp.int32, (size, size), 0)
    along = lax.broadcasted_iota(jnp.int32, (size, size), 1)
    return jnp.sum(
        jnp.where(down == along, values.astype(F32), 0.0), axis=axis, keepdims=True
    ).astype(jnp.int32)


def slot_maps(routes, order, slots, experts):
    top, rows = routes.shape
    pairs = rows * top
    lines = [routes[j : j + 1] for j in range(top)]
    e_row = jnp.concatenate(lines, axis=1)
    e_col = jnp.concatenate([diagonal(line, 1) for line in lines], axis=0)
    o_row = lax.rem(order, top) * rows + lax.div(order, top)
    o_col = diagonal(o_row, 1)
    down = lax.broadcasted_iota(jnp.int32, (pairs, pairs), 0)
    along = lax.broadcasted_iota(jnp.int32, (pairs, pairs), 1)
    turn_row = jnp.sum(jnp.where(o_col == along, down.astype(F32), 0.0), axis=0, keepdims=True)
    turn_col = jnp.sum(jnp.where(o_row == down, along.astype(F32), 0.0), axis=1, keepdims=True)
    same = e_col == e_row
    slot_row = jnp.sum(
        jnp.where(same & (turn_col < turn_row), 1.0, 0.0), axis=0, keepdims=True
    ).astype(jnp.int32)
    slot_col = jnp.sum(
        jnp.where(same & (turn_row < turn_col), 1.0, 0.0), axis=1, keepdims=True
    ).astype(jnp.int32)
    target_row = jnp.where(slot_row < slots, e_row * slots + slot_row, -1)
    target_col = jnp.where(slot_col < slots, e_col * slots + slot_col, -1)
    total = experts * slots
    place = lax.broadcasted_iota(jnp.int32, (total, pairs), 0)
    to_slots = jnp.where(place == target_row, 1.0, 0.0).astype(BF)
    place = lax.broadcasted_iota(jnp.int32, (pairs, total), 1)
    to_pairs = jnp.where(place == target_col, 1.0, 0.0).astype(BF)
    return to_slots, to_pairs


def forward_kernel(
    tok, gain_one, gain_two, router_ref, freq, deal, cot, routes, order, sd,
    wq, wk, wv, wo, sg, su, eg, eu, ed,
    cosr_out, sinr_out, kb_out, qb_out, qx_out, gm_out, stats_hbm, stat_out, normed_hbm, mixed_hbm, pack_hbm,
    result_hbm, grad_second_hbm, pack_grad_hbm, dsh_out, side_out, kv_out, wfull_out, keep_out, give_out, other_out,
    cosr, sinr, kb, qb, qx, stats_out, normed_out, mixed_out, pack_out, result_out,
    grad_second_out, pack_grad_out, wbuf, kv, q_s, qc, q_land, gm, stat, mixed, pack, packs, top, low, acc, sg_all, su_all, wg, wu, wd, mix, m4, cot4,
    sh_send, sh_recv, gm_send, gm_recv, xs, xr, gs, gr, orr, br,
    x_s, g_s, sum_s, gate_s, up_s, hid_s, dgate_s, dup_s, dsh, dsh_x, dsh_z, slot_s, pair_s, cb,
    sem, kv_recv, kv_send, a2a_send, a2a_recv, sem_sh,
):
    spot = Spot(4)
    sems = Sems(sem)
    rows, width = tok.shape
    pairs = width // PAIR
    ranks = xs.shape[0]
    slots = xs.shape[1] * 128 // width
    hidden = wg.shape[1]
    shard = width // 4
    part = sg_all.shape[1]
    peers = [(lax.rem(spot.k + o, ranks), spot.w) for o in range(1, ranks)]
    greet([spot.core, spot.across, spot.corner] + peers)
    line = (spot.line, spot.odd)
    key_w = Quarters(spot, wk, wbuf.at[1], sems)
    shards = jnp.concatenate(
        [
            gain_one[...].astype(F32).reshape(1, shard),
            gain_two[...].astype(F32).reshape(1, shard),
            router_ref[...].astype(F32),
            jnp.zeros((16 - 2 - router_ref.shape[0], shard), F32),
        ],
        axis=0,
    )
    shards = jnp.concatenate([shards, jnp.zeros((16, width - shard), F32)], axis=1)
    pack[...] = pltpu.roll(shards, shard * spot.w, 1).astype(BF)
    params = Gather(spot, pack, lambda w: packs.at[w], sems)
    value_w = Quarters(spot, wv, wbuf.at[2], sems)
    query_w = Quarters(spot, wq, wbuf.at[0], sems)

    def stripe(ref):
        return lambda w: ref.at[pl.ds(pl.multiple_of(shard * w, 64), shard)]

    out_w = Share(spot, wo, wbuf.at[3], sems, *line)
    sg_w = Quarters(spot, sg, sg_all, sems, columns=True)
    su_w = Quarters(spot, su, su_all, sems, columns=True)
    cot_w = Gather(spot, cot, lambda w: cot4.at[w], sems)
    gate_w = Gather(spot, eg, stripe(wg), sems)
    up_w = Gather(spot, eu, stripe(wu), sems)
    early = shard // 3

    def down_part(start, count):
        at = pl.ds(start, count)
        place = lambda w: wd.at[pl.ds(pl.multiple_of(shard * w + start, 64), count)]
        return Gather(spot, ed.at[at], place, sems)

    down_w = [down_part(0, early)]
    inputs = tok[...].astype(F32)
    scale = lax.rsqrt(jnp.mean(inputs * inputs, axis=-1, keepdims=True) + EPS)
    scaled = inputs * scale
    piece = rows // 2
    inner = lax.broadcasted_iota(jnp.int32, (rows, 1), 0)
    lane = lax.broadcasted_iota(jnp.int32, (rows, PAIR), 1)
    sign = jnp.where(lax.rem(lane, HD) < HD // 2, -1.0, 1.0)
    for r in range(2):
        paired = deal[2 * spot.z + r]
        unit = jnp.where(inner < piece, paired, 2 * ranks - 1 - paired)
        place = unit * piece + lax.rem(inner, piece)
        qb[r] = jnp.concatenate([lax.div(place, BLK)] * 2, axis=0)
        angles = place.astype(F32) * freq[...]
        cosr[r] = jnp.cos(angles)
        sinr[r] = jnp.sin(angles) * sign
    along = lax.broadcasted_iota(jnp.int32, (1, rows), 1)
    for r in range(ranks):
        unit = jnp.where(along < piece, deal[r], 2 * ranks - 1 - deal[r])
        kb[:, rows * r : rows * (r + 1)] = lax.div(unit * piece + lax.rem(along, piece), BLK)
    key_w.forward()
    params.forward()
    params.finish()
    pack_all = (packs[0].astype(F32) + packs[1].astype(F32)) + (
        packs[2].astype(F32) + packs[3].astype(F32)
    )
    pack_out[...] = pack_all
    normed = (scaled * pack_all[0:1]).astype(BF)
    normed_out[...] = normed.T
    cosine, sine = cosr[spot.x], sinr[spot.x]
    value_w.forward()
    to_slots, to_pairs = slot_maps(routes[...], order[...], slots, ranks)
    route = [diagonal(routes[j : j + 1], 1) for j in range(2)]
    slot_s[...] = to_slots
    pair_s[...] = to_pairs
    key_w.second()
    query_w.forward()
    value_w.second()
    key_w.third()
    key_w.finish()
    kv[spot.k, :, 0:width] = turn(nn(normed, wbuf[1]), cosine, sine).astype(BF)
    ring = Ring(spot, kv, kv_recv, kv_send, parts=4, sides=2)
    ring.start(parts=(0, 1))
    query_w.second()
    value_w.third()
    value_w.finish()
    kv[spot.k, :, width : 2 * width] = nn(normed, wbuf[2]).astype(BF)
    ring.start(parts=(2, 3))
    query_w.third()
    query_w.finish()
    query = turn(nn(normed, wbuf[0]), cosine, sine).astype(BF) * jnp.asarray(HD**-0.5, BF)
    for j in range(pairs):
        q_s[j] = stack_pair(query[:, PAIR * j : PAIR * (j + 1)])
    for x in range(2):
        qc[x] = query[:, width // 2 * x : width // 2 * (x + 1)]
    top[...] = jnp.full_like(top, MASKED)
    low[...] = jnp.zeros_like(low)
    acc[...] = jnp.zeros_like(acc)
    q_block = qb[spot.x]

    def chunk(slot, count):
        keys = count * rows
        k_block = kb[:, pl.ds(pl.multiple_of(rows * slot, rows), keys)]
        allowed = k_block <= q_block

        def one_pair(j, carry):
            lane = pl.multiple_of(PAIR * j, PAIR)
            key = kv[pl.ds(slot, count), :, pl.ds(lane, PAIR)].reshape(keys, PAIR)
            value = kv[pl.ds(slot, count), :, pl.ds(width + lane, PAIR)].reshape(keys, PAIR)
            scores = jnp.where(allowed, nt(q_s[j], key), MASKED)
            old = top[j]
            new = jnp.maximum(old, jnp.max(scores, axis=1, keepdims=True))
            raised = jnp.where(allowed, jnp.exp(scores - new[:, 0:1]), 0.0)
            factor = jnp.exp(old - new)
            top[j] = new
            low[j] = low[j] * factor + jnp.sum(raised, axis=1, keepdims=True)
            acc[j] = acc[j] * factor + nn(raised.astype(BF), value)
            return carry

        lax.fori_loop(0, pairs, one_pair, 0, unroll=3)

    ring.step(1)
    ring.step(2, only=1)
    ring.other(0)
    chunk(2 * spot.plane(0), 2)
    ring.step(2, only=0)
    ring.step(3, only=1)
    ring.other(1)
    chunk(2 * spot.plane(1), 2)
    ring.step(3, only=0)
    out_w.forward()
    sg_w.forward()
    su_w.forward()
    ring.other(2)
    chunk(2 * spot.plane(2), 2)
    out_w.second()
    cot_w.forward()
    chunk(2 * spot.plane(3) + spot.x, 1)
    ring.other(3)
    chunk(2 * spot.plane(3) + 1 - spot.x, 1)
    sg_w.second()
    su_w.second()
    saves = []

    def save(src, dst):
        saves.append(pltpu.make_async_copy(src, dst, sems.new()))
        saves[-1].start()

    save(kv, kv_out)
    for src, dst in ((cosr, cosr_out), (sinr, sinr_out), (kb, kb_out), (qb, qb_out)):
        save(src, dst)
    save(normed_out, normed_hbm)
    save(pack_out, pack_hbm)
    for j in range(pairs):
        mixed[:, PAIR * j : PAIR * (j + 1)] = unstack_pair(acc[j] / low[j])
        top[j] = top[j] + jnp.log(low[j])
    asides = []

    def aside(src, dst):
        asides.append(remote(src, dst, sems.new(), sems.new(), spot.column))
        asides[-1].start()
        return asides[-1]

    out_w.finish()
    save(wbuf, wfull_out)
    second = inputs + nn(mixed[...].astype(BF), wbuf[3])
    scale = lax.rsqrt(jnp.mean(second * second, axis=-1, keepdims=True) + EPS)
    mixer = (second * scale * pack_all[1:2]).astype(BF)
    mix[...] = mixer

    mixers = Gather(spot, mix, lambda w: m4.at[w], sems)
    down_w.append(down_part(early, shard - early))
    fold_rows(nn(slot_s[:, :rows] + slot_s[:, rows:], mixer), xs)
    rows_out = Exchange(spot, xs, xr, a2a_send.at[0], a2a_recv.at[0])
    rows_out.start()
    router = pack_all[2:16].astype(BF)
    router = jnp.concatenate([router, jnp.zeros((2, width), BF)], axis=0)
    logits = nt(mixer, router)
    lane = lax.broadcasted_iota(jnp.int32, logits.shape, 1)
    matches = [lane == route[j] for j in range(2)]
    chosen = [jnp.sum(jnp.where(m, logits, 0.0), axis=1, keepdims=True) for m in matches]
    largest = jnp.maximum(chosen[0], chosen[1])
    raised = [jnp.exp(c - largest) for c in chosen]
    gates = [r / (raised[0] + raised[1]) for r in raised]
    grad = cot[...].astype(F32)
    pair_grad = jnp.concatenate([(g * grad).astype(BF) for g in gates], axis=0)
    fold_rows(nn(slot_s[...], pair_grad), gs)
    grads_out = Exchange(spot, gs, gr, a2a_send.at[1], a2a_recv.at[1])
    grads_out.start()
    gate_w.forward()
    up_w.forward()
    mixers.forward()

    for part_w in (sg_w, su_w):
        part_w.third()
    for part_w in (sg_w, su_w, cot_w, mixers):
        part_w.finish()
    rows_all = m4[...].reshape(4 * rows, width)
    grad_all = cot4[...].reshape(4 * rows, width)
    gate_part, up_part = nn(rows_all, sg_all[...]), nn(rows_all, su_all[...])
    act, slope = swish(gate_part)
    shared_hidden = (act * up_part).astype(BF)
    sh_send[...] = nn(shared_hidden, sd[...]).astype(BF).reshape(4, rows, width)
    mixed_out[...] = mixed[...].astype(BF).T
    save(mixed_out, mixed_hbm)
    query_x = aside(qc.at[1 - spot.x], q_land)
    shared_out = Merge(spot, sh_send, sh_recv, sems)
    hid_grad = nt(grad_all, sd[...])
    grad_gate = (hid_grad * up_part * slope).astype(BF)
    grad_up = (hid_grad * act).astype(BF)
    back = nt(grad_gate, sg_all[...]) + nt(grad_up, su_all[...])
    gm_send[...] = back.astype(BF).reshape(4, rows, width)
    shared_out.forward()
    shared_back = Merge(spot, gm_send, gm_recv, sems)
    half = shard // 2
    for at, values in ((0, tn(rows_all, grad_gate)), (half, tn(rows_all, grad_up))):
        values = values.astype(BF)
        for r in range(ranks):
            down, left = half * (r // 4), 128 * (r % 4)
            for w in range(4):
                dsh[r, shard * w + at : shard * w + at + half] = values[
                    shard * w + down : shard * w + down + half, left : left + 128
                ]
    values = tn(shared_hidden, grad_all).astype(BF)
    deep = values.shape[0] // ranks
    for r in range(ranks):
        for t in range(width // 128):
            dsh[r, width + deep * t : width + deep * (t + 1)] = values[
                deep * r : deep * (r + 1), 128 * t : 128 * (t + 1)
            ]
    shared_back.forward()
    shared_grad = Reduce(spot, dsh, dsh_x, dsh_z, None, sem_sh)
    for number in (3, 2):
        shared_grad.side(number)

    for part_w in (gate_w, up_w):
        part_w.finish()
    rows_out.finish()
    x_s[...] = unfold_rows(xr, slots)
    block = 512

    def parts(i):
        return pl.ds(pl.multiple_of(block * i, block), block)

    def up_step(i, carry):
        at = parts(i)
        gate = nn(x_s[...], wg[:, at])
        up = nn(x_s[...], wu[:, at])
        act, slope = swish(gate)
        hid_s[:, at] = (act * up).astype(BF)
        gate_s[:, at] = up * slope
        up_s[:, at] = act
        return carry

    lax.fori_loop(0, hidden // block, up_step, 0)
    for part_w in down_w:
        part_w.forward()
    for part_w in down_w:
        part_w.finish()
    sum_s[...] = nt(hid_s[...], wd[...])
    rows_out.drain()
    fold_rows(sum_s[...], xs)
    outs = Exchange(spot, xs, orr, a2a_send.at[2], a2a_recv.at[2])
    outs.start()
    grads_out.finish()
    g_s[...] = unfold_rows(gr, slots)

    def down_step(i, carry):
        at = parts(i)
        grad_hidden = nn(g_s[...], wd[:, at])
        dgate_s[:, at] = (grad_hidden * gate_s[:, at]).astype(BF)
        dup_s[:, at] = (grad_hidden * up_s[:, at]).astype(BF)
        return carry

    lax.fori_loop(0, hidden // block, down_step, 0)
    sum_s[...] = nt(dgate_s[...], wg[...]) + nt(dup_s[...], wu[...])
    grads_out.drain()
    fold_rows(sum_s[...], gs)
    backs = Exchange(spot, gs, br, a2a_send.at[3], a2a_recv.at[3])
    backs.start()
    shared_grad.side(1)

    for part_w in [gate_w, up_w] + down_w:
        part_w.drain()
    swaps, across = [], []
    first = 2 * shard // 3
    sources = ((wg, x_s, dgate_s), (wu, x_s, dup_s), (wd, g_s, hid_s))

    def grads_of(a):
        ref, left, right = sources[a]

        def grad_step(i, carry):
            at = parts(i)
            ref[:, at] = tn(left[...], right[:, at]).astype(BF)
            return carry

        lax.fori_loop(0, hidden // block, grad_step, 0)
        for row in range(2):
            src = ref.at[pl.ds(pl.multiple_of(shard * (2 * row + 1 - spot.c), 64), shard)]
            swaps.append(remote(src, cb.at[a, row], sems.new(), sems.new(), spot.core))
            swaps[-1].start()

    def add_mate(a):
        ref = sources[a][0]
        for row in range(2):
            swaps[2 * a + row].wait_recv()

        def add(i, carry):
            for row in range(2):
                at = pl.ds(pl.multiple_of(shard * (2 * row + spot.c) + 16 * i, 16), 16)
                mate = cb[a, row, pl.ds(pl.multiple_of(16 * i, 16), 16)].astype(F32)
                ref[at] = (ref[at].astype(F32) + mate).astype(BF)
            return carry

        lax.fori_loop(0, shard // 16, add, 0)
        start = pl.multiple_of(shard * spot.across[1], 64)
        keep = ref.at[pl.ds(pl.multiple_of(shard * spot.w, 64), shard)]
        saves.append(pltpu.make_async_copy(keep, keep_out.at[a], sems.new()))
        saves[-1].start()
        if a == 0:
            across.append(
                remote(ref.at[pl.ds(start, first)], other_out, sems.new(), sems.new(), spot.across)
            )
            across[-1].start()
            give = ref.at[pl.ds(pl.multiple_of(start + first, 64), shard - first)]
            there = give_out.at[0, pl.ds(first, shard - first)]
        else:
            give, there = ref.at[pl.ds(start, shard)], give_out.at[a]
        saves.append(pltpu.make_async_copy(give, there, sems.new()))
        saves[-1].start()

    shared_grad.meet(3, True)
    grads_of(0)
    grads_of(1)
    add_mate(0)
    shared_grad.meet(2, True)
    grads_of(2)
    add_mate(1)
    add_mate(2)
    total = second + shared_out.finish()
    grad_mixer = shared_back.finish()
    outs.finish()
    pair_out = nn(pair_s[...], unfold_rows(orr, slots))
    pair_out = [pair_out[:rows], pair_out[rows:]]
    result_out[...] = (total + gates[0] * pair_out[0] + gates[1] * pair_out[1]).astype(BF)
    save(result_out, result_hbm)
    grad_gates = [jnp.sum(grad * p, axis=1, keepdims=True) for p in pair_out]
    inner = gates[0] * grad_gates[0] + gates[1] * grad_gates[1]
    grad_logits = jnp.zeros_like(logits)
    for j in range(2):
        grad_logits += jnp.where(matches[j], gates[j] * (grad_gates[j] - inner), 0.0)
    pieces = split_three(grad_logits)
    router_grad = sum(tn(piece, mixer) for piece in pieces)
    grad_mixer = grad_mixer + sum(nn(piece, router) for piece in pieces)
    shared_grad.meet(1, False)
    backs.finish()
    grad_mixer = grad_mixer + nn(pair_s[:rows] + pair_s[rows:], unfold_rows(br, slots))
    weighted = grad_mixer * pack_all[1:2]
    mean = jnp.mean(weighted * second, axis=-1, keepdims=True)
    grad_second = grad + scale * weighted - second * (scale * scale * scale * mean)
    grad_second_out[...] = grad_second
    save(grad_second_out, grad_second_hbm)

    grad_mixed = nt(grad_second.astype(BF), wbuf[3]).astype(BF)
    half = width // 2
    group = half // PAIR
    for x in range(2):
        gm[x] = grad_mixed[:, half * x : half * (x + 1)]
    product = grad_mixed.astype(F32) * mixed[...]
    lane = lax.broadcasted_iota(jnp.int32, (2 * rows, PAIR), 1)
    mine = jnp.zeros((2 * rows, PAIR), F32)
    theirs = jnp.zeros((2 * rows, PAIR), F32)
    for i in range(group):
        delta = [
            jnp.sum(stack_pair(product[:, PAIR * j : PAIR * (j + 1)]), axis=1, keepdims=True)
            for j in (i, group + i)
        ]
        swap = spot.x == 1
        mine = jnp.where(lane == i, top[group * spot.x + i], mine)
        theirs = jnp.where(lane == i, top[group * (1 - spot.x) + i], theirs)
        mine = jnp.where(lane == group + i, jnp.where(swap, delta[1], delta[0]), mine)
        theirs = jnp.where(lane == group + i, jnp.where(swap, delta[0], delta[1]), theirs)
        qx[i] = stack_pair(qc[spot.x, :, PAIR * i : PAIR * (i + 1)])
    stat[...] = theirs.T[0:8]
    stats_out[...] = mine
    gain_grad = jnp.sum(grad_mixer * second * scale, axis=0, keepdims=True)
    pack_grad_out[...] = jnp.concatenate(
        [jnp.zeros_like(gain_grad), gain_grad, router_grad[:14]], axis=0
    )
    query_x.wait_recv()
    for i in range(group):
        qx[group + i] = stack_pair(q_land[:, PAIR * i : PAIR * (i + 1)])
    for number in (3, 2):
        shared_grad.absorb(number)
    for plane in range(4):
        save(dsh.at[2 * plane + spot.x], dsh_out.at[plane])
    save(dsh.at[2 * spot.z + 1 - spot.x], side_out)
    for src, dst in (
        (qx, qx_out),
        (gm, gm_out),
        (stats_out, stats_hbm),
        (stat, stat_out),
        (pack_grad_out, pack_grad_hbm),
    ):
        save(src, dst)
    for copy in across:
        copy.wait_recv()
    for part_w in (params, key_w, value_w, query_w, out_w, sg_w, su_w, cot_w, ring, mixers):
        part_w.drain()
    for part_w in (outs, backs, shared_out, shared_back, shared_grad):
        part_w.drain()
    for copy in swaps + across + asides:
        copy.wait_send()
    for copy in saves:
        copy.wait()


def run_forward(
    tok, gain_one, gain_two, router, freq, deal, cot, routes, order, sd,
    wq, wk, wv, wo, sg, su, eg, eu, ed,
):
    rows, width = tok.shape
    pairs = width // PAIR
    ranks, slots = 8, 40
    hidden = eg.shape[1]
    part = sg.shape[1] // 4
    shard = width // 4
    total = ranks * slots
    tall = width + part * width // (128 * ranks)
    any_, vm = pl.BlockSpec(memory_space=pl.ANY), pl.BlockSpec(memory_space=VMEM)
    shape = jax.ShapeDtypeStruct

    def low(*dims):
        return VMEM(dims, BF)

    def full(*dims):
        return VMEM(dims, F32)

    dma = pltpu.SemaphoreType.DMA
    folded = low(ranks, slots * width // 128, 128)
    return pl.pallas_call(
        forward_kernel,
        out_shape=(
            shape((2, rows, PAIR), F32),
            shape((2, rows, PAIR), F32),
            shape((1, ranks * rows), jnp.int32),
            shape((2, 2 * rows, 1), jnp.int32),
            shape((pairs, 2 * rows, PAIR), BF),
            shape((2, rows, width // 2), BF),
            shape((2 * rows, PAIR), F32),
            shape((8, 2 * rows), F32),
            shape((width, rows), BF),
            shape((width, rows), BF),
            shape((16, width), F32),
            shape((rows, width), BF),
            shape((rows, width), F32),
            shape((16, width), F32),
            shape((4, tall, 128), BF),
            shape((tall, 128), BF),
            shape((ranks, rows, 2 * width), BF),
            shape((4, width, width), BF),
            shape((3, shard, hidden), BF),
            shape((3, shard, hidden), BF),
            shape((2 * shard // 3, hidden), BF),
        ),
        in_specs=[vm] * 5 + [pl.BlockSpec(memory_space=pltpu.SMEM)] + [vm] * 4 + [any_] * 9,
        out_specs=tuple([any_] * 21),
        scratch_shapes=[
            full(2, rows, PAIR),
            full(2, rows, PAIR),
            VMEM((1, ranks * rows), jnp.int32),
            VMEM((2, 2 * rows, 1), jnp.int32),
            low(pairs, 2 * rows, PAIR),
            full(2 * rows, PAIR),
            low(width, rows),
            low(width, rows),
            full(16, width),
            low(rows, width),
            full(rows, width),
            full(16, width),
            low(4, width, width),
            low(ranks, rows, 2 * width),
            low(pairs, 2 * rows, PAIR),
            low(2, rows, width // 2),
            low(rows, width // 2),
            low(2, rows, width // 2),
            full(8, 2 * rows),
            full(rows, width),
            low(16, width),
            low(4, 16, width),
            full(pairs, 2 * rows, PAIR),
            full(pairs, 2 * rows, PAIR),
            full(pairs, 2 * rows, PAIR),
            low(width, part),
            low(width, part),
            low(width, hidden),
            low(width, hidden),
            low(width, hidden),
            low(rows, width),
            low(4, rows, width),
            low(4, rows, width),
            low(4, rows, width),
            low(3, rows, width),
            low(4, rows, width),
            low(3, rows, width),
            *[folded] * 6,
            low(total, width),
            low(total, width),
            full(total, width),
            full(total, hidden),
            full(total, hidden),
            low(total, hidden),
            low(total, hidden),
            low(total, hidden),
            low(ranks, tall, 128),
            low(4, tall, 128),
            low(4, tall, 128),
            low(total, 2 * rows),
            low(2 * rows, total),
            low(3, 2, shard, hidden),
            dma((SEMS_FORWARD,)),
            dma((4 * ranks,)),
            dma((44,)),
            dma((4, ranks)),
            dma((4, ranks)),
            dma((4, 4)),
        ],
        compiler_params=pltpu.CompilerParams(
            collective_id=1, has_side_effects=True, vmem_limit_bytes=VMEM_BYTES
        ),
    )(
        tok, gain_one, gain_two, router, freq, deal, cot, routes, order, sd,
        wq, wk, wv, wo, sg, su, eg, eu, ed,
    )


def backward_kernel(
    grad_second_hbm, tok_hbm, pack_hbm, pack_grad_hbm, n_t_hbm, m_t_hbm, qx_hbm, gm_hbm, stats_hbm, stat_hbm,
    cosr_hbm, sinr_hbm, kb_hbm, qb_hbm, side_ref, dsh_ref, kv_ref, wfull_ref, give_ref, other_ref,
    grad_input_out, pack_out, att1_out, att2_out, sh_out, other_out,
    grad_second_ref, tok, pack_ref, pack_grad_ref, n_t, m_t, qx, gm, stats, stat, cosr, sinr, kb, qb,
    gx, gm_land, stat_land, w_half, kv, kvb, kv_zo, kv_zi, kv_sum, dq, ga, ga4, gq, gq4, gkv, gkv4, n_all, m_all, pk, pk4,
    o_send, o_land, gn_send, gn_land, a1, a1_zo, a1_zi, a1_sum, a2, a2_zo, a2_zi, a2_sum, r1, r2,
    sh, sh_land, sh_zo, sh_zi, sh_sum, sh_chunk, r3,
    sem, sem_kv, sem_a1, sem_a2, sem_sh, ring_recv, ring_send,
):
    spot = Spot(4)
    sems = Sems(sem)
    rows, width = tok.shape
    half = width // 2
    group = half // PAIR
    shard = width // 4
    mine = pl.ds(pl.multiple_of(half * spot.x, half), half)
    values = pl.ds(pl.multiple_of(width + half * spot.x, half), half)
    ranks = kv.shape[0]
    sources = dict(
        gm=(gm_hbm, gm),
        stat=(stat_hbm, stat),
        dsh=(dsh_ref, sh),
        second=(grad_second_hbm, grad_second_ref),
        n_t=(n_t_hbm, n_t),
        m_t=(m_t_hbm, m_t),
        qx=(qx_hbm, qx),
        stats=(stats_hbm, stats.at[0]),
        kb=(kb_hbm, kb),
        qb=(qb_hbm, qb),
        cosr=(cosr_hbm, cosr),
        sinr=(sinr_hbm, sinr),
        tok=(tok_hbm, tok),
        pack=(pack_hbm, pack_ref),
        pack_grad=(pack_grad_hbm, pack_grad_ref),
    )
    inputs = {
        name: pltpu.make_async_copy(src, dst, sems.new()) for name, (src, dst) in sources.items()
    }
    for copy in inputs.values():
        copy.start()
    loads = [
        pltpu.make_async_copy(kv_ref.at[:, :, mine], kv.at[:, :, pl.ds(0, half)], sems.new()),
        pltpu.make_async_copy(kv_ref.at[:, :, values], kv.at[:, :, pl.ds(half, half)], sems.new()),
        *[
            pltpu.make_async_copy(wfull_ref.at[i, :, mine], w_half.at[i], sems.new())
            for i in range(3)
        ],
    ]
    done = other_ref.shape[0]
    loads.append(pltpu.make_async_copy(other_ref, other_out.at[0, pl.ds(0, done)], sems.new()))
    for copy in loads:
        copy.start()

    def block(ref, w):
        return ref.at[pl.ds(pl.multiple_of(shard * w, 64), shard)]

    greet((spot.core, spot.across, spot.corner, spot.column, spot.inner), (spot.mid, spot.outer))
    asides = []

    def aside(src, dst):
        asides.append(remote(src, dst, sems.new(), sems.new(), spot.column))
        asides[-1].start()
        return asides[-1]

    inputs["gm"].wait()
    inputs["stat"].wait()
    grads_x = aside(gm.at[1 - spot.x], gm_land)
    stat_x = aside(stat, stat_land)
    shared_x = aside(side_ref, sh_land)
    inputs["dsh"].wait()
    shared = Reduce(spot, sh, None, sh_zo, sh_zi, sem_sh, folded=True, parts=2)
    shared.launch(1)
    shared.relay(3, settled=True)
    shared.relay(2, settled=True)
    inputs["second"].wait()
    grad_second = grad_second_ref[...]
    ga[...] = grad_second.astype(BF)
    grads_w = Gather(spot, ga, lambda w: ga4.at[w], sems)
    inputs["n_t"].wait()
    inputs["m_t"].wait()

    def columns(ref):
        return lambda w: ref.at[:, pl.ds(pl.multiple_of(rows * w, 128), rows)]

    normed_w = Spread(spot, lambda w: block(n_t, w), columns(n_all.at[spot.x]), sems)
    mixed_w = Spread(spot, lambda w: block(m_t, w), columns(m_all), sems)
    across = []

    def send_across(src, dst):
        across.append(remote(src, dst, sems.new(), sems.new(), spot.across))
        across[-1].start()

    def send_give(a, start, count):
        at = pl.ds(start, count)
        send_across(give_ref.at[a, at], other_out.at[a, at])

    third = shard // 3
    send_give(1, 0, third)
    dq[...] = jnp.zeros_like(dq)
    for name in ("qx", "stats", "kb", "qb", "cosr", "sinr", "tok", "pack", "pack_grad"):
        inputs[name].wait()
    loads[0].wait()
    loads[1].wait()
    for i in range(group):
        gx[i] = stack_pair(gm[spot.x, :, PAIR * i : PAIR * (i + 1)])
    grads_x.wait_recv()
    for i in range(group):
        gx[group + i] = stack_pair(gm_land[:, PAIR * i : PAIR * (i + 1)])
    stat_x.wait_recv()
    stats[1] = jnp.concatenate([stat_land[...], jnp.zeros((PAIR - 8, 2 * rows), F32)], axis=0).T

    def chunk(number):
        plane = spot.plane(number)
        k_block = kb[:, pl.ds(pl.multiple_of(2 * rows * plane, 2 * rows), 2 * rows)]
        allowed = [k_block <= qb[spot.x], k_block <= qb[1 - spot.x]]

        for i in range(group):
            lane = PAIR * i
            both = pl.ds(2 * plane, 2)
            key = kv[both, :, pl.ds(lane, PAIR)].reshape(2 * rows, PAIR)
            value = kv[both, :, pl.ds(half + lane, PAIR)].reshape(2 * rows, PAIR)
            grad_key = jnp.zeros((2 * rows, PAIR), F32)
            grad_value = jnp.zeros((2 * rows, PAIR), F32)
            for owner in range(2):
                j = group * owner + i
                stat = stats[owner]
                query, grad = qx[j], gx[j]
                raised = jnp.exp(nt(query, key) - stat[:, i : i + 1])
                probs = jnp.where(allowed[owner], raised, 0.0)
                inner = nt(grad, value) - stat[:, group + i : group + i + 1]
                grad_scores = (probs * inner * HD**-0.5).astype(BF)
                dq[j] += nn(grad_scores, key)
                grad_key += tn(grad_scores, query)
                grad_value += tn(probs.astype(BF), grad)
            kvb[plane, :, pl.ds(lane, PAIR)] = (grad_key * HD**0.5).astype(BF)
            kvb[plane, :, pl.ds(half + lane, PAIR)] = grad_value.astype(BF)

    kv_grad = Reduce(spot, kvb, None, kv_zo, kv_zi, sem_kv, folded=True, parts=2)
    chunk(3)
    kv_grad.launch(3)
    chunk(2)
    kv_grad.launch(2)
    chunk(1)
    kv_grad.launch(1)
    normed_w.finish()
    normed_x = aside(n_all.at[spot.x], n_all.at[spot.x])
    shared.relay(1)
    kv_grad.relay(3, parts=(0,))
    chunk(0)
    for owner in range(2):
        at = spot.x if owner == 0 else 1 - spot.x
        parts = [unstack_pair(dq[group * owner + i]) for i in range(group)]
        gq[at] = turn(jnp.concatenate(parts, axis=1), cosr[at], -sinr[at]).astype(BF)
    grads_w.forward()
    mixed_w.finish()
    grads_w.finish()
    out_grad = nn(m_all[...], ga4[...].reshape(4 * rows, width)).astype(BF)
    for x in range(2):
        o_send[x] = out_grad[:, half * x : half * (x + 1)]
    out_x = aside(o_send.at[1 - spot.x], o_land)
    shared_x.wait_recv()
    sh[spot.z] = (sh[spot.z].astype(F32) + sh_land[...].astype(F32)).astype(BF)
    shared.last(sh_sum)
    kv_grad.relay(3, parts=(1,))
    sh_chunk[...] = sh_sum[...].astype(BF)
    part = 2 * shard // 2

    def piece(w):
        return sh_chunk.at[pl.ds(pl.multiple_of(part * w, 64), part)]

    def place(w):
        return r3.at[spot.k, pl.ds(pl.multiple_of(part * w, 64), part)]

    shared_w = Spread(spot, piece, place, sems)
    rest = sh_chunk.shape[0] - 4 * part
    r3[spot.k, pl.ds(4 * part, rest)] = sh_chunk[pl.ds(4 * part, rest)]
    query_w = Gather(spot, gq, lambda w: gq4.at[w], sems)
    send_give(1, third, third)
    kv_grad.relay(2, parts=(0,))
    kv_grad.relay(1, parts=(0,))
    shared_w.finish()
    ring3 = Ring(spot, r3, ring_recv, ring_send, parts=2)
    ring3.start(only=0)
    kv_grad.relay(2, parts=(1,))
    kv_grad.relay(1, parts=(1,))
    ring3.start(only=1)
    for copy in loads[2:5]:
        copy.wait()
    flat = gq[...].reshape(2 * rows, half)
    grad_normed = nt(flat, w_half[0])
    query_w.forward()
    query_w.finish()
    normed_x.wait_recv()

    def weight_grad(grads4):
        total = nn(n_all[0], grads4[:, 0].reshape(4 * rows, grads4.shape[3]))
        return total + nn(n_all[1], grads4[:, 1].reshape(4 * rows, grads4.shape[3]))

    query_grad = weight_grad(gq4).astype(BF)
    out_x.wait_recv()
    out_half = (o_send[spot.x].astype(F32) + o_land[...].astype(F32)).astype(BF)
    size = shard // 4
    for plane in range(4):
        at = slice(size * plane, size * (plane + 1))
        a1[plane, :, 0:half] = out_half[at]
        a1[plane, :, half:width] = query_grad[at]
    first = Reduce(spot, a1, None, a1_zo, a1_zi, sem_a1, folded=True)
    for number in (3, 2, 1):
        first.launch(number)
    kv_w = []
    for r in range(2):
        at = slice(rows * r, rows * (r + 1))
        kv_grad.last(kv_sum, parts=(r,))
        gkv[r, :, 0:half] = turn(kv_sum[at, 0:half], cosr[r], -sinr[r]).astype(BF)
        gkv[r, :, half:width] = kv_sum[at, half:width].astype(BF)
        kv_w.append(Gather(spot, gkv.at[r], lambda w, r=r: gkv4.at[w, r], sems))
    ring3.step(1, only=0)
    send_give(1, 2 * third, third)
    send_give(0, done, shard - done)
    flat = gkv[...].reshape(2 * rows, width)
    grad_normed = grad_normed + nt(flat[:, 0:half], w_half[1]) + nt(flat[:, half:width], w_half[2])
    gn_send[...] = grad_normed.astype(BF).reshape(2, rows, width)
    normed_grad_x = aside(gn_send.at[1 - spot.x], gn_land)
    ring3.step(2, only=1)
    ring3.step(1, only=1)
    first.relay(3)
    first.relay(2)
    for part_w in kv_w:
        part_w.forward()
    for part_w in kv_w:
        part_w.finish()
    both = weight_grad(gkv4).astype(BF)
    for plane in range(4):
        a2[plane] = both[size * plane : size * (plane + 1)]
    second = Reduce(spot, a2, None, a2_zo, a2_zi, sem_a2, folded=True)
    for number in (3, 2, 1):
        second.launch(number)
    first.relay(1)
    ring3.step(2, only=0)
    second.relay(3)
    second.relay(2)
    second.relay(1)
    ring3.step(3, only=1)
    normed_grad_x.wait_recv()
    grad_normed = gn_send[spot.x].astype(F32) + gn_land[...].astype(F32)
    inputs = tok[...].astype(F32)
    scale = lax.rsqrt(jnp.mean(inputs * inputs, axis=-1, keepdims=True) + EPS)
    weighted = grad_normed * pack_ref[0:1]
    mean = jnp.mean(weighted * inputs, axis=-1, keepdims=True)
    grad_input_out[...] = (
        grad_second + scale * weighted - inputs * (scale * scale * scale * mean)
    )
    gain_grad = jnp.sum(grad_normed * inputs * scale, axis=0, keepdims=True)
    pk[...] = jnp.concatenate([gain_grad, pack_grad_ref[1:16]], axis=0).astype(BF)
    pack_w = Gather(spot, pk, lambda w: pk4.at[w], sems)
    send_give(2, 0, shard)
    first.last(a1_sum)
    r1[spot.k] = a1_sum[...].astype(BF)
    ring1 = Ring(spot, r1, ring_recv, ring_send, first=(16, 28))
    ring1.start()
    pack_w.forward()
    pack_w.finish()
    extra = sum(pk4[w].astype(F32) for w in range(4)).astype(BF)
    second.last(a2_sum)
    r2[spot.k, 0:size] = a2_sum[...].astype(BF)
    r2[spot.k, size : size + 16] = extra
    ring2 = Ring(spot, r2, ring_recv, ring_send, first=(24, 39))
    ring2.start()
    ring3.step(3, only=0)
    ring1.step(1)
    ring1.step(2, only=1)
    ring1.step(3, only=1)
    ring1.step(2, only=0)
    ring1.step(3, only=0)
    ring2.step(1)
    ring2.step(2)
    ring2.step(3)
    saves = []
    for ring, src, dst in ((ring3, r3, sh_out), (ring1, r1, att1_out), (ring2, r2, att2_out)):
        for number in range(4):
            ring.other(number)
        saves.append(pltpu.make_async_copy(src, dst, sems.new()))
        saves[-1].start()
    total = jnp.zeros(pk.shape, F32)
    for r in range(ranks):
        total = total + r2[r, size : size + 16].astype(F32)
    pack_out[...] = total
    for copy in across:
        copy.wait_recv()
    for copy in across + asides:
        copy.wait_send()
    for part_w in [grads_w, normed_w, mixed_w, query_w, shared_w, pack_w] + kv_w:
        part_w.drain()
    for part_w in (shared, kv_grad, first, second, ring1, ring2, ring3):
        part_w.drain()
    for copy in saves + loads[5:]:
        copy.wait()


def run_backward(
    grad_second, tok, pack, pack_grad, n_t, m_t, qx, gm, stats, stat, cosr, sinr, kb, qb, side, dsh, kv,
    wfull,
    give, other,
):
    rows, width = tok.shape
    pairs = width // PAIR
    half = width // 2
    ranks = 8
    shard, hidden = width // 4, give.shape[2]
    size = shard // 4
    tall = dsh.shape[1]
    any_, vm = pl.BlockSpec(memory_space=pl.ANY), pl.BlockSpec(memory_space=VMEM)
    shape = jax.ShapeDtypeStruct

    def low(*dims):
        return VMEM(dims, BF)

    def full(*dims):
        return VMEM(dims, F32)

    dma = pltpu.SemaphoreType.DMA
    return pl.pallas_call(
        backward_kernel,
        out_shape=(
            shape((rows, width), F32),
            shape(pack.shape, F32),
            shape((ranks, size, width), BF),
            shape((ranks, size + 16, width), BF),
            shape((ranks, tall, 128), BF),
            shape((3, shard, hidden), BF),
        ),
        in_specs=[any_] * 20,
        out_specs=(vm, vm, any_, any_, any_, any_),
        scratch_shapes=[
            full(rows, width),
            low(rows, width),
            full(16, width),
            full(16, width),
            low(width, rows),
            low(width, rows),
            low(pairs, 2 * rows, PAIR),
            low(2, rows, half),
            full(2, 2 * rows, PAIR),
            full(8, 2 * rows),
            full(2, rows, PAIR),
            full(2, rows, PAIR),
            VMEM((1, ranks * rows), jnp.int32),
            VMEM((2, 2 * rows, 1), jnp.int32),
            low(pairs, 2 * rows, PAIR),
            low(rows, half),
            full(8, 2 * rows),
            low(3, width, half),
            low(ranks, rows, width),
            low(4, 2 * rows, width),
            low(4, 2 * rows, width),
            low(4, 2 * rows, width),
            full(2 * rows, width),
            full(pairs, 2 * rows, PAIR),
            low(rows, width),
            low(4, rows, width),
            low(2, rows, half),
            low(4, 2, rows, half),
            low(2, rows, width),
            low(4, 2, rows, width),
            low(2, shard, 4 * rows),
            low(shard, 4 * rows),
            low(16, width),
            low(4, 16, width),
            low(2, shard, half),
            low(shard, half),
            low(2, rows, width),
            low(rows, width),
            low(4, size, width),
            low(4, size, width),
            low(4, size, width),
            full(size, width),
            low(4, size, width),
            low(4, size, width),
            low(4, size, width),
            full(size, width),
            low(ranks, size, width),
            low(ranks, size + 16, width),
            low(4, tall, 128),
            low(tall, 128),
            low(4, tall, 128),
            low(4, tall, 128),
            full(tall, 128),
            low(tall, 128),
            low(ranks, tall, 128),
            dma((SEMS_BACKWARD,)),
            dma((3, 8)),
            dma((3, 4)),
            dma((3, 4)),
            dma((3, 8)),
            dma((4 * ranks,)),
            dma((SEMS_RINGS,)),
        ],
        compiler_params=pltpu.CompilerParams(
            collective_id=3, has_side_effects=True, vmem_limit_bytes=VMEM_BYTES
        ),
    )(
        grad_second, tok, pack, pack_grad, n_t, m_t, qx, gm, stats, stat, cosr, sinr, kb, qb, side, dsh, kv,
        wfull, give, other,
    )


def unpack_kernel(
    result_hbm, grad_input_hbm, pack_hbm, att1_hbm, att2_hbm, sh_hbm, keep_hbm, other_hbm,
    result_out, grad_input_out, gain_one_out, gain_two_out, router_out,
    query_out, key_out, value_out, output_out, gate_out, up_out, down_out, eg_out, eu_out, ed_out,
    result, grad_input, pack, att1, att2, sh, keep, other, experts_f, both_f, down, att_f,
    gains, router, sem,
):
    sems = Sems(sem)

    def copy(src, dst):
        made = pltpu.make_async_copy(src, dst, sems.new())
        made.start()
        return made

    shard, hidden = keep.shape[1:]
    width = 4 * shard
    half = width // 2
    loads = []
    for a in range(3):
        loads.append([copy(keep_hbm.at[a], keep.at[a]), copy(other_hbm.at[a], other.at[a])])
    shared_loads = [copy(sh_hbm.at[pl.ds(4 * r, 4)], sh.at[pl.ds(4 * r, 4)]) for r in range(2)]
    att_loads = [copy(att1_hbm, att1), copy(att2_hbm, att2)]
    small = [copy(pack_hbm, pack), copy(result_hbm, result), copy(grad_input_hbm, grad_input)]
    saves = []
    for a, out in enumerate((eg_out, eu_out, ed_out)):
        for made in loads[a]:
            made.wait()
        for part in range(4):
            at = slice(shard // 4 * part, shard // 4 * (part + 1))
            experts_f[a, at] = keep[a, at].astype(F32) + other[a, at].astype(F32)
            saves.append(copy(experts_f.at[a, at], out.at[at]))
    size = shard // 2
    deep = down.shape[0] // 8
    for row in range(2):
        shared_loads[row].wait()
        rows = slice(size * row, size * (row + 1))
        for c in range(4):
            for w in range(4):
                lanes = slice(512 * w + 128 * c, 512 * w + 128 * (c + 1))
                for a in range(2):
                    start = shard * w + size * a
                    both_f[a, rows, lanes] = sh[4 * row + c, start : start + size].astype(F32)
        for a, out in enumerate((gate_out, up_out)):
            saves.append(copy(both_f.at[a, rows], out.at[rows]))
        for r in range(4 * row, 4 * row + 4):
            for t in range(width // 128):
                at = slice(width + deep * t, width + deep * (t + 1))
                lanes = slice(128 * t, 128 * (t + 1))
                down[deep * r : deep * (r + 1), lanes] = sh[r, at].astype(F32)
        rows = slice(4 * deep * row, 4 * deep * (row + 1))
        saves.append(copy(down.at[rows], down_out.at[rows]))
    for made in att_loads:
        made.wait()
    slots = att1.shape[1]
    parts = ((output_out, att1, 0), (query_out, att1, 1), (key_out, att2, 0), (value_out, att2, 1))
    for n, (out, src, low) in enumerate(parts):
        for r in range(8):
            plane, x = r // 2, r % 2
            rows, lanes = slice(slots * plane, slots * (plane + 1)), slice(half * x, half * (x + 1))
            att_f[n, rows, lanes] = src[r, 0:slots, half * low : half * (low + 1)].astype(F32)
        saves.append(copy(att_f.at[n], out))
    for made in small:
        made.wait()
    saves += [copy(result, result_out), copy(grad_input, grad_input_out)]
    back = lax.rem(4 - lax.axis_index("wt"), 4) * shard
    mine = pltpu.roll(pack[...], back, 1)
    gains[0] = mine[0:1, 0:shard]
    gains[1] = mine[1:2, 0:shard]
    router[...] = mine[2 : 2 + router.shape[0], 0:shard]
    saves += [copy(gains.at[0], gain_one_out), copy(gains.at[1], gain_two_out)]
    saves.append(copy(router, router_out))
    for made in saves:
        made.wait()


def run_unpack(result, grad_input, pack, att1, att2, sh, keep, other, experts):
    rows, width = result.shape
    shard, hidden = keep.shape[1:]
    shape = jax.ShapeDtypeStruct
    shared_hidden = sh.shape[0] * (sh.shape[1] - width) * 128 // width
    shared = 4 * shared_hidden
    any_ = pl.BlockSpec(memory_space=pl.ANY)
    return pl.pallas_call(
        unpack_kernel,
        out_shape=(
            shape((rows, width), BF),
            shape((rows, width), F32),
            shape((1, shard), F32),
            shape((1, shard), F32),
            shape((experts, shard), F32),
            *[shape((shard, width), F32)] * 4,
            *[shape((shard, shared), F32)] * 2,
            shape((shared_hidden, width), F32),
            *[shape((shard, hidden), F32)] * 3,
        ),
        in_specs=[any_] * 8,
        out_specs=tuple([any_] * 15),
        scratch_shapes=[
            VMEM((rows, width), BF),
            VMEM((rows, width), F32),
            VMEM(pack.shape, F32),
            VMEM(att1.shape, BF),
            VMEM(att2.shape, BF),
            VMEM(sh.shape, BF),
            VMEM(keep.shape, BF),
            VMEM(other.shape, BF),
            VMEM((3, shard, hidden), F32),
            VMEM((2, shard, shared), F32),
            VMEM((shared_hidden, width), F32),
            VMEM((4, shard, width), F32),
            VMEM((2, 1, shard), F32),
            VMEM((experts, shard), F32),
            pltpu.SemaphoreType.DMA((SEMS_LAYOUT,)),
        ],
        compiler_params=pltpu.CompilerParams(vmem_limit_bytes=VMEM_BYTES),
    )(result, grad_input, pack, att1, att2, sh, keep, other)


def contract_product(left, right, left_dim, right_dim):
    return lax.dot_general(
        left, right, (((left_dim,), (right_dim,)), ((), ())), preferred_element_type=jnp.float32
    )


def contract_exact(left, right, left_dim, right_dim):
    return lax.dot_general(
        left,
        right,
        (((left_dim,), (right_dim,)), ((), ())),
        precision=HIGH,
        preferred_element_type=jnp.float32,
    )


def rms_norm(values, gain):
    norm_scale = lax.rsqrt(jnp.mean(values * values, axis=-1, keepdims=True) + EPS)
    return (values * norm_scale * gain, norm_scale)


def rms_back(values, norm_scale, gain, upstream):
    weighted = upstream * gain
    inner_mean = jnp.mean(weighted * values, axis=-1, keepdims=True)
    through = norm_scale * weighted - values * norm_scale * norm_scale * norm_scale * inner_mean
    return (through, jnp.sum(upstream * values * norm_scale, axis=0))


def silu_parts(gate_part):
    sigmoid = jax.nn.sigmoid(gate_part)
    return (gate_part * sigmoid, sigmoid * (1.0 + gate_part * (1.0 - sigmoid)))


def rotate(values, place, sign):
    half_size = HD // 2
    frequency = 10000.0 ** (-jnp.arange(half_size, dtype=jnp.float32) / half_size)
    angles = place.astype(jnp.float32)[:, None] * frequency[None, :]
    cosine = jnp.cos(angles)[:, None, :]
    sine_part = sign * jnp.sin(angles)[:, None, :]
    shaped = values.reshape(values.shape[0], values.shape[1] // HD, 2, half_size)
    first_half = shaped[:, :, 0, :]
    second_half = shaped[:, :, 1, :]
    turned = jnp.stack(
        [
            first_half * cosine - second_half * sine_part,
            second_half * cosine + first_half * sine_part,
        ],
        axis=2,
    )
    return turned.reshape(values.shape)


def places(first_row, row_count, block_deal, rows_dev):
    row_index = first_row + jnp.arange(row_count, dtype=jnp.int32)
    owner_rank = row_index // rows_dev
    inner_row = row_index % rows_dev
    ranks = block_deal.shape[0]
    matches = owner_rank[:, None] == jnp.arange(ranks, dtype=jnp.int32)[None, :]
    paired = jnp.sum(jnp.where(matches, block_deal[None, :], 0), axis=1)
    piece_size = rows_dev // 2
    unit_index = jnp.where(inner_row < piece_size, paired, 2 * ranks - 1 - paired)
    return unit_index * piece_size + inner_row % piece_size


def score_block(query_side, key_rows, key_place):
    query3, query_block = query_side
    key3 = key_rows.reshape(key_rows.shape[0], -1, HD)
    raw_scores = jnp.einsum("qhd,khd->hqk", query3, key3, preferred_element_type=jnp.float32)
    allowed = (key_place // BLK)[None, None, :] <= query_block[None, :, None]
    return (jnp.where(allowed, raw_scores * HD ** (-0.5), MASKED), allowed)


def absorb(running, key_rows, value_rows, key_place, query_side):
    largest, denom, accum = running
    scores, allowed = score_block(query_side, key_rows, key_place)
    new_largest = jnp.maximum(largest, jnp.max(scores, axis=2))
    factor = jnp.exp(largest - new_largest)
    raised = jnp.where(allowed, jnp.exp(scores - new_largest[:, :, None]), 0.0)
    denom = denom * factor + jnp.sum(raised, axis=2)
    value3 = value_rows.reshape(value_rows.shape[0], -1, HD)
    accum = accum * factor.T[:, :, None] + jnp.einsum(
        "hqk,khd->qhd", raised.astype(jnp.bfloat16), value3, preferred_element_type=jnp.float32
    )
    return (new_largest, denom, accum)


def fold_keys(running, key_piece, query_side, block_deal, rows_dev):
    key_all, value_all = key_piece
    row_count = key_all.shape[0]
    block_size = KEY_ROWS

    def key_step(current, offset):
        key_rows = lax.dynamic_slice_in_dim(key_all, offset, block_size, 0)
        value_rows = lax.dynamic_slice_in_dim(value_all, offset, block_size, 0)
        key_place = places(offset, block_size, block_deal, rows_dev)
        return (absorb(current, key_rows, value_rows, key_place, query_side), None)

    offsets = jnp.arange(row_count // block_size, dtype=jnp.int32) * block_size
    running, unused = lax.scan(key_step, running, offsets)
    return running


def differentiate(query_side, log_total, delta, grad_out3, key_rows, value_rows, key_place):
    scores, allowed = score_block(query_side, key_rows, key_place)
    probs_full = jnp.where(allowed, jnp.exp(scores - log_total[:, :, None]), 0.0)
    value3 = value_rows.reshape(value_rows.shape[0], -1, HD)
    grad_probs = jnp.einsum("qhd,khd->hqk", grad_out3, value3, preferred_element_type=jnp.float32)
    grad_scores = (probs_full * (grad_probs - delta[:, :, None]) * HD ** (-0.5)).astype(
        jnp.bfloat16
    )
    return (probs_full, grad_scores)


def assign_slots(route, order, experts, capacity):
    pair_count = order.shape[0]
    expert_ids = route.reshape(pair_count)
    ordered = expert_ids[order]
    onehot = (ordered[:, None] == jnp.arange(experts, dtype=jnp.int32)[None, :]).astype(jnp.int32)
    before = jnp.cumsum(onehot, axis=0) - onehot
    slot_turn = jnp.sum(before * onehot, axis=1)
    slot_index = jnp.zeros((pair_count,), jnp.int32).at[order].set(slot_turn)
    kept_pairs = slot_index < capacity
    target = jnp.where(kept_pairs, expert_ids * capacity + slot_index, experts * capacity)
    slot_table = (
        jnp.full((experts * capacity,), pair_count, jnp.int32)
        .at[target]
        .set(jnp.arange(pair_count, dtype=jnp.int32), mode="drop")
    )
    return (target, kept_pairs, slot_table)


def body(
    tokens,
    cotangent,
    gain_attention,
    query_weight,
    key_weight,
    value_weight,
    output_weight,
    gain_mixer,
    router_weight,
    shared_gate,
    shared_up,
    shared_down,
    expert_gate,
    expert_up,
    expert_down,
    routes,
    slot_order,
    block_deal,
):
    rows_dev = tokens.shape[1]
    width = tokens.shape[2]
    ranks = lax.axis_size("ctx")
    (
        gain_one,
        query_full,
        key_full,
        value_full,
        output_full,
        gain_two,
        router_full,
        sgate_full,
        sup_full,
        sdown_full,
        expert_gate_whole,
        expert_up_whole,
        edown_full,
    ) = (
        lax.all_gather(gain_attention, "wt", axis=0, tiled=True),
        lax.all_gather(query_weight, "wt", axis=0, tiled=True),
        lax.all_gather(key_weight, "wt", axis=0, tiled=True),
        lax.all_gather(value_weight, "wt", axis=0, tiled=True),
        lax.all_gather(output_weight, "wt", axis=0, tiled=True),
        lax.all_gather(gain_mixer, "wt", axis=0, tiled=True),
        lax.all_gather(router_weight, "wt", axis=0, tiled=True),
        lax.all_gather(shared_gate, "wt", axis=0, tiled=True),
        lax.all_gather(shared_up, "wt", axis=0, tiled=True),
        lax.all_gather(shared_down, "wt", axis=0, tiled=True),
        lax.all_gather(expert_gate, "wt", axis=0, tiled=True),
        lax.all_gather(expert_up, "wt", axis=0, tiled=True),
        lax.all_gather(expert_down, "wt", axis=0, tiled=True),
    )
    gain_first = gain_one.astype(jnp.float32)
    gain_second = gain_two.astype(jnp.float32)
    heads = width // HD
    inputs = tokens[0].astype(jnp.float32)
    here = places(lax.axis_index("ctx") * rows_dev, rows_dev, block_deal, rows_dev)
    query_side_block = here // BLK
    normed_f, scale_one = rms_norm(inputs, gain_first)
    normed = normed_f.astype(jnp.bfloat16)
    query_rot = rotate(
        jnp.dot(normed, query_full, preferred_element_type=jnp.float32), here, 1.0
    ).astype(jnp.bfloat16)
    key_rot = rotate(
        jnp.dot(normed, key_full, preferred_element_type=jnp.float32), here, 1.0
    ).astype(jnp.bfloat16)
    value_low = jnp.dot(normed, value_full, preferred_element_type=jnp.float32).astype(jnp.bfloat16)
    query3 = query_rot.reshape(rows_dev, heads, HD)
    query_side = (query3, query_side_block)
    start_state = (
        jnp.full((heads, rows_dev), MASKED, jnp.float32),
        jnp.zeros((heads, rows_dev), jnp.float32),
        jnp.zeros((rows_dev, heads, HD), jnp.float32),
    )
    largest, denom, accum = fold_keys(
        start_state,
        (
            lax.all_gather(key_rot, "ctx", axis=0, tiled=True),
            lax.all_gather(value_low, "ctx", axis=0, tiled=True),
        ),
        query_side,
        block_deal,
        rows_dev,
    )
    mixed3 = accum / denom.T[:, :, None]
    log_total = largest + jnp.log(denom)
    mixed_low = mixed3.reshape(rows_dev, width).astype(jnp.bfloat16)
    second = inputs + jnp.dot(mixed_low, output_full, preferred_element_type=jnp.float32)
    mixer_f, scale_two = rms_norm(second, gain_second)
    mixer = mixer_f.astype(jnp.bfloat16)
    experts = router_full.shape[1]
    logits = jnp.dot(mixer, router_full, preferred_element_type=jnp.float32)
    route = routes[0]
    top_count = route.shape[1]
    pair_count = rows_dev * top_count
    capacity = (5 * pair_count + 4 * experts - 1) // (4 * experts)
    split_count = ranks // experts
    expert_match = route[:, :, None] == jnp.arange(experts, dtype=jnp.int32)[None, None, :]
    chosen = jnp.sum(jnp.where(expert_match, logits[:, None, :], 0.0), axis=2)
    gates = jax.nn.softmax(chosen, axis=1)
    target, kept_pairs, slot_table = assign_slots(route, slot_order[0, 0], experts, capacity)
    valid = slot_table < pair_count
    pair_pick = jnp.minimum(slot_table, pair_count - 1)
    target_pick = jnp.minimum(target, experts * capacity - 1)
    send_rows = jnp.where(
        valid[:, None], mixer[pair_pick // top_count], jnp.zeros((), jnp.bfloat16)
    )
    send_rows = jnp.broadcast_to(
        send_rows.reshape(experts, 1, capacity, width), (experts, split_count, capacity, width)
    ).reshape(ranks, capacity, width)
    received = lax.all_to_all(send_rows, "ctx", split_axis=0, concat_axis=0, tiled=True)
    slot_count = received.shape[1]
    flattened_input = received.reshape(ranks * slot_count, width)
    gate_part = jnp.dot(flattened_input, expert_gate_whole, preferred_element_type=jnp.float32)
    up_projection_part = jnp.dot(
        flattened_input, expert_up_whole, preferred_element_type=jnp.float32
    )
    activated, unused = silu_parts(gate_part)
    hidden = (activated * up_projection_part).astype(jnp.bfloat16)
    partial_value = contract_product(hidden, edown_full, 1, 1).reshape(ranks, slot_count, width)
    back = lax.all_to_all(
        partial_value.astype(jnp.bfloat16), "ctx", split_axis=0, concat_axis=0, tiled=True
    ).astype(partial_value.dtype)
    expert_gate_part = gate_part.reshape(ranks, slot_count, -1)
    expert_up_part = up_projection_part.reshape(ranks, slot_count, -1)
    combined = jnp.sum(back.reshape(experts, split_count, capacity, width), axis=1).reshape(
        experts * capacity, width
    )
    pair_out = jnp.where(kept_pairs[:, None], combined[target_pick], 0.0).reshape(
        rows_dev, top_count, width
    )
    mixture = jnp.sum(gates[:, :, None] * pair_out, axis=1)
    sgate_part = jnp.dot(mixer, sgate_full, preferred_element_type=jnp.float32)
    sup_part = jnp.dot(mixer, sup_full, preferred_element_type=jnp.float32)
    shared_act, shared_slope = silu_parts(sgate_part)
    shared_hidden = (shared_act * sup_part).astype(jnp.bfloat16)
    shared_out = jnp.dot(shared_hidden, sdown_full, preferred_element_type=jnp.float32)
    result = (second + mixture + shared_out).astype(jnp.bfloat16)
    grad_final = cotangent[0].astype(jnp.float32)
    grad_low = grad_final.astype(jnp.bfloat16)
    sdown_grad = contract_product(shared_hidden, grad_low, 0, 0)
    grad_shared_hidden = contract_product(grad_low, sdown_full, 1, 1)
    grad_sgate = (grad_shared_hidden * sup_part * shared_slope).astype(jnp.bfloat16)
    grad_sup = (grad_shared_hidden * shared_act).astype(jnp.bfloat16)
    sgate_grad = contract_product(mixer, grad_sgate, 0, 0)
    sup_grad = contract_product(mixer, grad_sup, 0, 0)
    grad_mixer = contract_product(grad_sgate, sgate_full, 1, 1) + contract_product(
        grad_sup, sup_full, 1, 1
    )
    pair_grad = (
        (gates[:, :, None] * grad_final[:, None, :]).reshape(pair_count, width).astype(jnp.bfloat16)
    )
    grad_gates = jnp.sum(grad_final[:, None, :] * pair_out, axis=2)
    send_grad = jnp.where(valid[:, None], pair_grad[pair_pick], jnp.zeros((), jnp.bfloat16))
    send_grad = jnp.broadcast_to(
        send_grad.reshape(experts, 1, capacity, width), (experts, split_count, capacity, width)
    ).reshape(ranks, capacity, width)
    recv_grad = lax.all_to_all(send_grad, "ctx", split_axis=0, concat_axis=0, tiled=True)
    flattened_input = received.reshape(ranks * capacity, width)
    flat_grad = recv_grad.reshape(ranks * capacity, width)
    gate_flat = expert_gate_part.reshape(ranks * capacity, -1)
    up_flat = expert_up_part.reshape(ranks * capacity, -1)
    expert_activation, expert_slope = silu_parts(gate_flat)
    expert_hidden = (expert_activation * up_flat).astype(jnp.bfloat16)
    edown_grad = contract_product(flat_grad, expert_hidden, 0, 0)
    expert_hidden_grad = jnp.dot(flat_grad, edown_full, preferred_element_type=jnp.float32)
    expert_gate_grad_rows = (expert_hidden_grad * up_flat * expert_slope).astype(jnp.bfloat16)
    expert_up_grad_rows = (expert_hidden_grad * expert_activation).astype(jnp.bfloat16)
    egate_grad = contract_product(flattened_input, expert_gate_grad_rows, 0, 0)
    expert_up_weight_grad = contract_product(flattened_input, expert_up_grad_rows, 0, 0)
    input_back = (
        contract_product(expert_gate_grad_rows, expert_gate_whole, 1, 1)
        + contract_product(expert_up_grad_rows, expert_up_whole, 1, 1)
    ).reshape(ranks, capacity, width)
    back_grad = lax.all_to_all(
        input_back.astype(jnp.bfloat16), "ctx", split_axis=0, concat_axis=0, tiled=True
    ).astype(input_back.dtype)
    merged = jnp.sum(back_grad.reshape(experts, split_count, capacity, width), axis=1).reshape(
        experts * capacity, width
    )
    pair_back = jnp.where(kept_pairs[:, None], merged[target_pick], 0.0).reshape(
        rows_dev, top_count, width
    )
    grad_mixer = grad_mixer + jnp.sum(pair_back, axis=1)
    grad_chosen = gates * (grad_gates - jnp.sum(gates * grad_gates, axis=1, keepdims=True))
    grad_logits = jnp.sum(jnp.where(expert_match, grad_chosen[:, :, None], 0.0), axis=1)
    router_grad = contract_exact(mixer.astype(jnp.float32), grad_logits, 0, 0)
    grad_mixer = grad_mixer + contract_exact(grad_logits, router_full.astype(jnp.float32), 1, 1)
    through_two, gain_two_grad = rms_back(second, scale_two, gain_second, grad_mixer)
    grad_second = grad_final + through_two
    grad_attention = grad_second.astype(jnp.bfloat16)
    output_grad = contract_product(mixed_low, grad_attention, 0, 0)
    grad_mixed = contract_product(grad_attention, output_full, 1, 1).astype(jnp.bfloat16)
    grad_out3 = grad_mixed.reshape(rows_dev, heads, HD)
    delta = jnp.sum(grad_out3.astype(jnp.float32) * mixed3, axis=2).T
    all_keys, all_values = (
        lax.all_gather(key_rot, "ctx", axis=0, tiled=True),
        lax.all_gather(value_low, "ctx", axis=0, tiled=True),
    )
    total_rows = all_keys.shape[0]
    block_size = KEY_ROWS

    def query_step(grad_sum, offset):
        key_rows = lax.dynamic_slice_in_dim(all_keys, offset, block_size, 0)
        value_rows = lax.dynamic_slice_in_dim(all_values, offset, block_size, 0)
        key_place = places(offset, block_size, block_deal, rows_dev)
        unused, grad_scores = differentiate(
            query_side, log_total, delta, grad_out3, key_rows, value_rows, key_place
        )
        key3 = key_rows.reshape(block_size, heads, HD)
        return (
            grad_sum
            + jnp.einsum("hqk,khd->qhd", grad_scores, key3, preferred_element_type=jnp.float32),
            None,
        )

    offsets = jnp.arange(total_rows // block_size, dtype=jnp.int32) * block_size
    grad_query3, unused = lax.scan(
        query_step, jnp.zeros((rows_dev, heads, HD), jnp.float32), offsets
    )
    inner_size = KEY_ROWS

    def one_part(offset):
        key_rows = lax.dynamic_slice_in_dim(all_keys, offset, inner_size, 0)
        value_rows = lax.dynamic_slice_in_dim(all_values, offset, inner_size, 0)
        key_place = places(offset, inner_size, block_deal, rows_dev)
        probs_full, grad_scores = differentiate(
            query_side, log_total, delta, grad_out3, key_rows, value_rows, key_place
        )
        grad_value_rows = jnp.einsum(
            "hqk,qhd->khd",
            probs_full.astype(jnp.bfloat16),
            grad_out3,
            preferred_element_type=jnp.float32,
        )
        grad_key_rows = jnp.einsum(
            "hqk,qhd->khd", grad_scores, query3, preferred_element_type=jnp.float32
        )
        return jnp.concatenate(
            [grad_key_rows.reshape(inner_size, width), grad_value_rows.reshape(inner_size, width)],
            axis=1,
        )

    parts = lax.map(
        one_part,
        jnp.arange(lax.axis_size("ctx") * rows_dev // inner_size, dtype=jnp.int32) * inner_size,
    )
    key_value_grad = lax.psum_scatter(
        parts.reshape(lax.axis_size("ctx") * rows_dev, 2 * width),
        "ctx",
        scatter_dimension=0,
        tiled=True,
    )
    grad_key_pre = rotate(key_value_grad[:, :width], here, -1.0).astype(jnp.bfloat16)
    grad_value_low = key_value_grad[:, width:].astype(jnp.bfloat16)
    grad_query_pre = rotate(grad_query3.reshape(rows_dev, width), here, -1.0).astype(jnp.bfloat16)
    query_grad = contract_product(normed, grad_query_pre, 0, 0)
    key_grad = contract_product(normed, grad_key_pre, 0, 0)
    value_grad = contract_product(normed, grad_value_low, 0, 0)
    grad_normed = (
        contract_product(grad_query_pre, query_full, 1, 1)
        + contract_product(grad_key_pre, key_full, 1, 1)
        + contract_product(grad_value_low, value_full, 1, 1)
    )
    through_one, gain_one_grad = rms_back(inputs, scale_one, gain_first, grad_normed)
    grad_input = grad_second + through_one
    (
        gain_one_share,
        query_share,
        key_share,
        value_share,
        output_share,
        gain_two_share,
        router_share,
        sgate_share,
        sup_share,
        sdown_share,
        egate_share,
        expert_up_portion,
        edown_share,
    ) = (
        lax.psum_scatter(
            gain_one_grad.astype(jnp.bfloat16), "wt", scatter_dimension=0, tiled=True
        ).astype(jnp.float32),
        lax.psum_scatter(
            query_grad.astype(jnp.bfloat16), "wt", scatter_dimension=0, tiled=True
        ).astype(jnp.float32),
        lax.psum_scatter(
            key_grad.astype(jnp.bfloat16), "wt", scatter_dimension=0, tiled=True
        ).astype(jnp.float32),
        lax.psum_scatter(
            value_grad.astype(jnp.bfloat16), "wt", scatter_dimension=0, tiled=True
        ).astype(jnp.float32),
        lax.psum_scatter(
            output_grad.astype(jnp.bfloat16), "wt", scatter_dimension=0, tiled=True
        ).astype(jnp.float32),
        lax.psum_scatter(
            gain_two_grad.astype(jnp.bfloat16), "wt", scatter_dimension=0, tiled=True
        ).astype(jnp.float32),
        lax.psum_scatter(
            router_grad.astype(jnp.bfloat16), "wt", scatter_dimension=0, tiled=True
        ).astype(jnp.float32),
        lax.psum_scatter(
            sgate_grad.astype(jnp.bfloat16), "wt", scatter_dimension=0, tiled=True
        ).astype(jnp.float32),
        lax.psum_scatter(
            sup_grad.astype(jnp.bfloat16), "wt", scatter_dimension=0, tiled=True
        ).astype(jnp.float32),
        lax.psum_scatter(
            sdown_grad.astype(jnp.bfloat16), "wt", scatter_dimension=0, tiled=True
        ).astype(jnp.float32),
        lax.psum_scatter(
            egate_grad.astype(jnp.bfloat16), "wt", scatter_dimension=0, tiled=True
        ).astype(jnp.float32),
        lax.psum_scatter(
            expert_up_weight_grad.astype(jnp.bfloat16), "wt", scatter_dimension=0, tiled=True
        ).astype(jnp.float32),
        lax.psum_scatter(
            edown_grad.astype(jnp.bfloat16), "wt", scatter_dimension=0, tiled=True
        ).astype(jnp.float32),
    )
    (
        gain_one_sum,
        query_sum,
        key_sum,
        value_sum,
        output_sum,
        gain_two_sum,
        router_sum,
        sgate_sum,
        sup_sum,
        sdown_sum,
    ) = lax.psum(
        (
            gain_one_share,
            query_share,
            key_share,
            value_share,
            output_share,
            gain_two_share,
            router_share,
            sgate_share,
            sup_share,
            sdown_share,
        ),
        "ctx",
    )
    return (
        result[None],
        grad_input[None],
        gain_one_sum,
        query_sum,
        key_sum,
        value_sum,
        output_sum,
        gain_two_sum,
        router_sum,
        sgate_sum,
        sup_sum,
        sdown_sum,
        egate_share,
        expert_up_portion,
        edown_share,
    )


def fast_body(
    tokens,
    cotangent,
    gain_attention,
    query_weight,
    key_weight,
    value_weight,
    output_weight,
    gain_mixer,
    router_weight,
    shared_gate,
    shared_up,
    shared_down,
    expert_gate,
    expert_up,
    expert_down,
    routes,
    slot_order,
    block_deal,
):
    half_size = HD // 2
    frequency = 10000.0 ** (-np.arange(half_size) / half_size)
    frequency = jnp.asarray(np.tile(frequency, 4)[None].astype(np.float32))
    (
        cosr, sinr, kb, qb, qx, gm, stats, stat, n_t, m_t, pack_all, result, grad_second, pack_grad, dsh,
        side, kv_all, wfull, keep, give, other,
    ) = run_forward(
        tokens[0], gain_attention, gain_mixer, router_weight.T, frequency, block_deal,
        cotangent[0], routes[0].T, slot_order[0],
        shared_down, query_weight, key_weight, value_weight, output_weight, shared_gate, shared_up,
        expert_gate, expert_up, expert_down,
    )
    grad_input, pack_sum, att1, att2, sh, other = run_backward(
        grad_second, tokens[0], pack_all, pack_grad, n_t, m_t, qx, gm, stats, stat, cosr, sinr, kb, qb,
        side, dsh, kv_all, wfull, give, other,
    )
    (
        result, grad_input, gain_one, gain_two, router, query, key, value, output, gate, up, down,
        eg, eu, ed,
    ) = run_unpack(
        result, grad_input, pack_sum, att1, att2, sh, keep, other, router_weight.shape[1]
    )
    return (
        result[None], grad_input[None], gain_one.reshape(-1), query, key, value, output,
        gain_two.reshape(-1), router.T, gate, up, down, eg, eu, ed,
    )


def solution(mesh):
    in_specs = (
        P("wt", "ctx", None),
        P("wt", "ctx", None),
        P("wt"),
        P("wt", None),
        P("wt", None),
        P("wt", None),
        P("wt", None),
        P("wt"),
        P("wt", None),
        P("wt", None),
        P("wt", None),
        P("wt", None),
        P("wt", "ctx"),
        P("wt", "ctx"),
        P("wt", "ctx"),
        P("wt", "ctx", None),
        P("wt", "ctx", None),
        P(),
    )
    out_specs = (
        P("wt", "ctx", None),
        P("wt", "ctx", None),
        P("wt"),
        P("wt", None),
        P("wt", None),
        P("wt", None),
        P("wt", None),
        P("wt"),
        P("wt", None),
        P("wt", None),
        P("wt", None),
        P("wt", None),
        P("wt", "ctx"),
        P("wt", "ctx"),
        P("wt", "ctx"),
    )
    chosen = fast_body if (mesh.shape["ctx"], mesh.shape["wt"]) == (8, 4) else body
    return jax.shard_map(chosen, mesh=mesh, in_specs=in_specs, out_specs=out_specs, check_vma=False)
```
